32 devices in a mesh: seq: 16 (over z, y, x), tp: 2 (over core).
Axes of the slice: x: 2, y: 2, z: 4, core: 2. Of those that a mesh axis runs over, the one named last changes fastest.
Arguments:
- tokens: bfloat16 [1024, 2, 1024], P('seq'), may hold values from -6 to 6
- d_out: float32 [1024, 2, 1024], P('seq'), may hold values from -6 to 6
- norm1_gain: float32 [2, 1024], replicated, may hold values from 0.1 to 1.9
- norm1_shift: float32 [2, 1024], replicated, may hold values from -3 to 3
- w_qkv: bfloat16 [2, 1024, 3, 1024], P(None, None, None, 'tp'), may hold values from -0.1875 to 0.1875
- b_qkv: float32 [2, 3, 1024], P(None, None, 'tp'), may hold values from -3 to 3
- w_out: bfloat16 [2, 1024, 1024], P(None, 'tp'), may hold values from -1.5 to 1.5
- b_out: float32 [2, 1024], replicated, may hold values from -3 to 3
- norm2_gain: float32 [2, 1024], replicated, may hold values from 0.1 to 1.9
- norm2_shift: float32 [2, 1024], replicated, may hold values from -3 to 3
- w_up: bfloat16 [2, 1024, 4096], P(None, None, 'tp'), may hold values from -0.1875 to 0.1875
- b_up: float32 [2, 4096], P(None, 'tp'), may hold values from -3 to 3
- w_down: bfloat16 [2, 4096, 1024], P(None, 'tp'), may hold values from -0.09375 to 0.09375
- b_down: float32 [2, 1024], replicated, may hold values from -3 to 3
- episode_frames: int32 [2, 4], replicated, may hold values from 0 to 4, as said below
- live: int32 [1024, 2], P('seq'), may hold values from 0 to 1, as said below
Outputs:
- out: float32 [1024, 2, 1024], P('seq')
- d_x: float32 [1024, 2, 1024], P('seq')
- g_norm1_gain: float32 [2, 1024], P(None, 'seq')
- g_norm1_shift: float32 [2, 1024], P(None, 'seq')
- g_w_qkv: float32 [2, 1024, 3, 1024], P(None, 'seq', None, 'tp')
- g_b_qkv: float32 [2, 3, 1024], P(None, None, 'tp')
- g_w_out: float32 [2, 1024, 1024], P(None, 'tp', 'seq')
- g_b_out: float32 [2, 1024], P(None, 'seq')
- g_norm2_gain: float32 [2, 1024], P(None, 'seq')
- g_norm2_shift: float32 [2, 1024], P(None, 'seq')
- g_w_up: float32 [2, 1024, 4096], P(None, 'seq', 'tp')
- g_b_up: float32 [2, 4096], P(None, 'tp')
- g_w_down: float32 [2, 4096, 1024], P(None, 'tp', 'seq')
- g_b_down: float32 [2, 1024], P(None, 'seq')
The draws below stay inside these ranges and needn't reach their ends.
Inputs may be any that keep to these rules, and one draw needn't show every extreme that they name: `episode_frames`: each row sums to 4. In every draw one lane, drawn from the seed, is a single episode of all 4 frames followed by empty slots; every other lane holds 4 episodes of one frame or more. Padding only at the end of an episode, at most half of 256 tokens of its last frame; the first token of every episode is live.
All inputs are finite; a program needn't handle non-finite values.
Results may differ from the reference program's by a relative error of at most 0.024.
Values may be sent and summed in bfloat16 or wider, within the bound.
A program may use at most 256 MiB of HBM per device.

```python
import math
import jax
import jax.numpy as jnp
from jax import lax

D = 1024
FF = 4096
HEAD_DIM = 64
HEADS = 16
GRID = 16
FRAME = 256
LAYERS = 2
EPISODES = 4
LANES = 2
LEN = 1024
LANE_FRAMES = 4


def episode_draw(base_key):
    base_key = jax.random.fold_in(base_key, 11)
    long_key, weight_key, padding_key = jax.random.split(base_key, 3)
    longest = jax.random.randint(long_key, (), 0, LANES)
    powers = jax.random.randint(weight_key, (LANES, EPISODES), 0, 5)
    weights = jnp.left_shift(jnp.ones((LANES, EPISODES), jnp.int32), powers)
    spare = LANE_FRAMES - EPISODES
    shares = spare * weights // jnp.sum(weights, axis=1, keepdims=True)
    frames = 1 + shares
    remains = LANE_FRAMES - jnp.sum(frames, axis=1)
    frames = frames.at[:, 0].add(remains)
    single = jnp.zeros((LANES, EPISODES), jnp.int32).at[:, 0].set(LANE_FRAMES)
    frames = jnp.where((jnp.arange(LANES) == longest)[:, None], single, frames).astype(jnp.int32)
    paddings = jax.random.randint(padding_key, (LANES, EPISODES), 0, FRAME // 2 + 1)
    endings = jnp.cumsum(frames, axis=1) * FRAME
    positions = jnp.arange(LEN, dtype=jnp.int32)
    inside = (positions[:, None, None] >= (endings - paddings)[None]) & (positions[:, None, None] < endings[None]) & (frames[None] > 0)
    alive = 1 - jnp.sum(inside.astype(jnp.int32), axis=2)
    return (frames, alive.astype(jnp.int32))


def draw_episode_frames(key, part):
    return episode_draw(key)[0]


def draw_live(key, part):
    return episode_draw(key)[1]


def spiked(drawn, key, source, target, parts, factor):
    def block_of(position):
        return (jnp.arange(drawn.shape[position]) // (drawn.shape[position] // parts)).reshape((-1,) + (1,) * (drawn.ndim - 1 - position))

    first = jax.random.permutation(key, parts)[block_of(target)]
    far = (block_of(target) + parts // 2) % parts
    return jnp.where((block_of(source) == first) | (block_of(source) == far), factor * drawn, drawn)


def level_of(key, shape, cuts, low, largest):
    loudness, own = 1.0, jax.random.fold_in(key, 6)
    for axis_at, parts in cuts:
        steps = jnp.exp(jax.random.uniform(jax.random.fold_in(own, axis_at), (parts,), jnp.float32, low / len(cuts), largest / len(cuts)))
        loudness = loudness * jnp.repeat(steps, shape[axis_at] // parts).reshape([-1 if axis == axis_at else 1 for axis in range(len(shape))])
    return loudness


def noise(own_key, extent, width, bound, cuts=(), kind=jnp.bfloat16):
    entries = jax.random.normal(own_key, extent, jnp.float32) * width
    if len(cuts) > 0:
        entries = level_of(own_key, extent, cuts, -0.22, 0.18) * entries
    return jnp.clip(entries, min=-bound, max=bound).astype(kind)


def noise_with(rng, extent, scale, bound, cuts, heavy, kind=jnp.bfloat16):
    drawn = scale * jax.random.normal(rng, extent, jnp.float32)
    if cuts:
        drawn = drawn * level_of(rng, extent, cuts, -0.22, 0.18)
    return jnp.clip(spiked(drawn, jax.random.fold_in(rng, 3), *heavy), -bound, bound).astype(kind)


def setup_inputs(seed: int = 0) -> dict:
    key_of = jax.random.split(jax.random.key(seed), 17)
    return {
        "tokens": noise_with(key_of[0], (LEN, LANES, D), 1.0, 6.0, ((0, 16),), (0, 2, 16, 2.0)),
        "d_out": noise_with(key_of[1], (LEN, LANES, D), 1.0, 6.0, ((0, 16),), (0, 2, 16, 2.0), jnp.float32),
        "norm1_gain": jnp.clip(1.0 + 0.18 * jax.random.normal(key_of[2], (LAYERS, D), jnp.float32), 0.1, 1.9),
        "norm1_shift": noise(key_of[3], (LAYERS, D), 0.5, 3.0, (), jnp.float32),
        "w_qkv": noise(key_of[4], (LAYERS, D, 3, D), D ** -0.5, 0.1875, ((3, 2),)),
        "b_qkv": noise(key_of[5], (LAYERS, 3, D), 0.5, 3.0, ((2, 2),), jnp.float32),
        "w_out": noise(key_of[6], (LAYERS, D, D), (D // 64) ** -0.5, 1.5, ((1, 2),)),
        "b_out": noise(key_of[7], (LAYERS, D), 0.5, 3.0, (), jnp.float32),
        "norm2_gain": jnp.clip(1.0 + 0.18 * jax.random.normal(key_of[8], (LAYERS, D), jnp.float32), 0.1, 1.9),
        "norm2_shift": noise(key_of[9], (LAYERS, D), 0.5, 3.0, (), jnp.float32),
        "w_up": noise(key_of[10], (LAYERS, D, FF), D ** -0.5, 0.1875, ((2, 2),)),
        "b_up": noise(key_of[11], (LAYERS, FF), 0.5, 3.0, ((1, 2),), jnp.float32),
        "w_down": noise(key_of[12], (LAYERS, FF, D), FF ** -0.5, 0.09375, ((1, 2),)),
        "b_down": noise(key_of[13], (LAYERS, D), 0.5, 3.0, (), jnp.float32),
        "episode_frames": draw_episode_frames(jax.random.fold_in(key_of[16], 71), 0),
        "live": draw_live(jax.random.fold_in(key_of[16], 71), 0),
    }


@jax.custom_vjp
def low(v):
    return lax.optimization_barrier(v.astype(jnp.bfloat16)).astype(jnp.float32)

@jax.custom_vjp
def low_back(v):
    return v

def low_keep(v):
    return (low(v), None)

def low_pass(kept, grad):
    return (grad,)

def back_keep(v):
    return (v, None)

def back_low(kept, grad):
    return (low(grad),)
low.defvjp(low_keep, low_pass)
low_back.defvjp(back_keep, back_low)
EPSILON = 1e-06
MASKED = -1e+30
SCORE_SCALE = 0.125
HIGHEST = lax.Precision.HIGHEST

def layer_norm(stream, norm_gain, norm_shift):
    center = stream - lax.optimization_barrier(jnp.mean(stream, axis=-1, keepdims=True))
    spread = lax.optimization_barrier(jnp.mean(center * center, axis=-1, keepdims=True))
    return center * lax.rsqrt(spread + EPSILON) * norm_gain + norm_shift

def rotate(values, frame_place, row_place, column_place):
    frequency = jnp.exp(jnp.arange(10, dtype=jnp.float32) * (-math.log(10000.0) / 10.0))
    pieces = []
    for section, place in enumerate((frame_place, row_place, column_place)):
        lower = values[..., 20 * section:20 * section + 10]
        upper = values[..., 20 * section + 10:20 * section + 20]
        angles = place.astype(jnp.float32)[..., None, None] * frequency
        cosine = jnp.cos(angles)
        sine_part = jnp.sin(angles)
        pieces.append(lower * cosine - upper * sine_part)
        pieces.append(lower * sine_part + upper * cosine)
    pieces.append(values[..., 60:])
    return jnp.concatenate(pieces, axis=-1)

def episode_tags(frame_counts, positions):
    endings = (jnp.cumsum(frame_counts) * FRAME).astype(jnp.int32)
    passed = (positions[:, None] >= endings[None, :]).astype(jnp.int32)
    episode = lax.optimization_barrier(jnp.sum(passed, axis=1)).astype(jnp.int32)
    opening = lax.optimization_barrier(jnp.sum(passed * frame_counts[None, :], axis=1)).astype(jnp.int32)
    frame_index = (positions // FRAME - opening).astype(jnp.int32)
    within = positions % FRAME
    return (episode, frame_index, (within // GRID).astype(jnp.int32), (within % GRID).astype(jnp.int32))

def lane_forward(weights, stream, allowed, frame_index, patch_row, patch_column):
    length = stream.shape[0]
    for layer_index in range(LAYERS):
        gain_one, shift_one, mat_qkv, bias_qkv, mat_out, bias_out, gain_two, shift_two, mat_up, bias_up, mat_down, bias_down = [item[layer_index] for item in weights]
        first = low(layer_norm(stream, gain_one, shift_one))
        projected = low_back(jnp.einsum('td,dcf->tcf', first, mat_qkv, precision=HIGHEST) + bias_qkv)
        split = projected.reshape(length, 3, HEADS, HEAD_DIM)
        query = low(rotate(split[:, 0], frame_index, patch_row, patch_column))
        keys = low(rotate(split[:, 1], frame_index, patch_row, patch_column))
        values = low(split[:, 2])
        scores = low_back(jnp.einsum('qhd,khd->hqk', query, keys, precision=HIGHEST) * SCORE_SCALE)
        scores = jnp.where(allowed[None], scores, MASKED)
        attention = low(jax.nn.softmax(scores, axis=-1))
        mixed = jnp.einsum('hqk,khd->qhd', attention, values, precision=HIGHEST).reshape(length, D)
        mixed = low(low_back(mixed))
        stream = stream + low_back(jnp.dot(mixed, mat_out, precision=HIGHEST)) + bias_out
        second = low(layer_norm(stream, gain_two, shift_two))
        hidden = low_back(jnp.dot(second, mat_up, precision=HIGHEST) + bias_up)
        activation = low(jax.nn.gelu(hidden, approximate=False))
        stream = stream + low_back(jnp.dot(activation, mat_down, precision=HIGHEST)) + bias_down
    return stream

def reference(tokens, d_out, norm1_gain, norm1_shift, w_qkv, b_qkv, w_out, b_out, norm2_gain, norm2_shift, w_up, b_up, w_down, b_down, episode_frames, live):
    params = tuple((item.astype(jnp.float32) for item in (norm1_gain, norm1_shift, w_qkv, b_qkv, w_out, b_out, norm2_gain, norm2_shift, w_up, b_up, w_down, b_down)))
    positions = jnp.arange(LEN, dtype=jnp.int32)

    def one_lane(totals, lane_index):
        stream = jnp.take(tokens, lane_index, axis=1).astype(jnp.float32)
        cotangent = jnp.take(d_out, lane_index, axis=1).astype(jnp.float32)
        episode, frame_index, patch_row, patch_column = episode_tags(jnp.take(episode_frames, lane_index, axis=0), positions)
        alive = jnp.take(live, lane_index, axis=1)
        allowed = (episode[:, None] == episode[None, :]) & (frame_index[None, :] <= frame_index[:, None]) & (alive[None, :] > 0)

        def forward(weights, values):
            return lane_forward(weights, values, allowed, frame_index, patch_row, patch_column)
        result, pullback = jax.vjp(forward, params, stream)
        grads, grad_stream = pullback(cotangent)
        totals = jax.tree.map(jnp.add, totals, grads)
        return (totals, (result, grad_stream))
    zeros = tuple((jnp.zeros_like(item) for item in params))
    totals, (results, grad_streams) = lax.scan(one_lane, zeros, jnp.arange(LANES, dtype=jnp.int32))
    out = jnp.transpose(results, (1, 0, 2))
    grad_tokens = jnp.transpose(grad_streams, (1, 0, 2))
    return (out, grad_tokens, totals[0], totals[1], totals[2], totals[3], totals[4], totals[5], totals[6], totals[7], totals[8], totals[9], totals[10], totals[11])
```

```python
import math

import jax
import jax.numpy as jnp
import numpy as np
from jax import lax
from jax.experimental import pallas as pl
from jax.experimental.pallas import tpu as pltpu
from jax.sharding import PartitionSpec as P

HEAD_DIM = 64
GRID = 16
FRAME = 256
LAYERS = 2
MICRO = 2


EPSILON = 1e-06
MASKED = -1e30
SCORE_SCALE = 0.125


def layer_norm(stream, norm_gain, norm_shift):
    center = stream - jnp.mean(stream, axis=-1, keepdims=True)
    spread = jnp.mean(center * center, axis=-1, keepdims=True)
    return center * lax.rsqrt(spread + EPSILON) * norm_gain + norm_shift


def rotate(values, frame_place, row_place, column_place):
    frequency = jnp.exp(jnp.arange(10, dtype=jnp.float32) * (-math.log(10000.0) / 10.0))
    pieces = []
    for section, place in enumerate((frame_place, row_place, column_place)):
        lower = values[..., 20 * section : 20 * section + 10]
        upper = values[..., 20 * section + 10 : 20 * section + 20]
        angles = place.astype(jnp.float32)[..., None, None] * frequency
        cosine = jnp.cos(angles)
        sine_part = jnp.sin(angles)
        pieces.append(lower * cosine - upper * sine_part)
        pieces.append(lower * sine_part + upper * cosine)
    pieces.append(values[..., 60:])
    return jnp.concatenate(pieces, axis=-1)


def episode_tags(frame_counts, positions):
    endings = jnp.cumsum(frame_counts) * FRAME
    passed = (positions[:, None] >= endings[None, :]).astype(jnp.int32)
    episode = jnp.sum(passed, axis=1)
    opening = jnp.sum(passed * frame_counts[None, :], axis=1)
    frame_index = positions // FRAME - opening
    within = positions % FRAME
    return (episode, frame_index, within // GRID, within % GRID)


def gelu_exact(values):
    return jax.nn.gelu(values, approximate=False)


def sum_heads(partial_sum):
    return lax.psum(partial_sum.astype(jnp.bfloat16), "tp").astype(jnp.float32)


def sum_inputs(partial_sum):
    return lax.psum(partial_sum.astype(jnp.bfloat16), "tp").astype(jnp.float32)


def lane_scores(query, keys_all, lane_index, query_tags, key_tags):
    head_count = query.shape[2] // HEAD_DIM
    query_lane = lax.dynamic_index_in_dim(query, lane_index, 1, False).reshape(
        query.shape[0], head_count, HEAD_DIM
    )
    keys_lane = lax.dynamic_index_in_dim(keys_all, lane_index, 1, False).reshape(
        keys_all.shape[0], head_count, HEAD_DIM
    )
    query_episode, query_frame = [
        lax.dynamic_index_in_dim(item, lane_index, 1, False) for item in query_tags
    ]
    key_episode, key_frame, key_live = [
        lax.dynamic_index_in_dim(item, lane_index, 1, False) for item in key_tags
    ]
    allowed = (
        (query_episode[:, None] == key_episode[None, :])
        & (key_frame[None, :] <= query_frame[:, None])
        & (key_live[None, :] > 0)
    )
    scores = (
        jnp.einsum("qhd,khd->hqk", query_lane, keys_lane, preferred_element_type=jnp.float32)
        * SCORE_SCALE
    )
    return (jnp.where(allowed[None], scores, MASKED), query_lane, keys_lane)


def attend_forward(query, keys_all, values_all, query_tags, key_tags):
    rows_dev, lane_count, features = query.shape
    head_count = features // HEAD_DIM

    def one_lane(lane_index, carry):
        scores, query_lane, keys_lane = lane_scores(
            query, keys_all, lane_index, query_tags, key_tags
        )
        highest = jnp.max(scores, axis=-1, keepdims=True)
        shifted = jnp.exp(scores - highest)
        summed = jnp.sum(shifted, axis=-1, keepdims=True)
        attention = (shifted / summed).astype(jnp.bfloat16)
        values_lane = lax.dynamic_index_in_dim(values_all, lane_index, 1, False).reshape(
            values_all.shape[0], head_count, HEAD_DIM
        )
        result = jnp.einsum(
            "hqk,khd->qhd", attention, values_lane, preferred_element_type=jnp.float32
        ).reshape(rows_dev, 1, features)
        log_total = (highest + jnp.log(summed))[None, :, :, 0]
        return (result, log_total)

    initial = (
        jnp.zeros((rows_dev, lane_count, features), jnp.float32),
        jnp.zeros((lane_count, head_count, rows_dev), jnp.float32),
    )
    return lax.fori_loop(0, lane_count, one_lane, initial)


def attend_backward(query, keys_all, values_all, log_total, grad_mixed, query_tags, key_tags):
    rows_dev, lane_count, features = query.shape
    head_count = features // HEAD_DIM
    key_rows = keys_all.shape[0]

    def one_lane(lane_index, carry):
        scores, query_lane, keys_lane = lane_scores(
            query, keys_all, lane_index, query_tags, key_tags
        )
        values_lane = lax.dynamic_index_in_dim(values_all, lane_index, 1, False).reshape(
            key_rows, head_count, HEAD_DIM
        )
        grad_lane = lax.dynamic_index_in_dim(grad_mixed, lane_index, 1, False).reshape(
            rows_dev, head_count, HEAD_DIM
        )
        attention = jnp.exp(
            scores - lax.dynamic_index_in_dim(log_total, lane_index, 0, False)[:, :, None]
        )
        grad_attention = jnp.einsum(
            "qhd,khd->hqk", grad_lane, values_lane, preferred_element_type=jnp.float32
        )
        inner = jnp.sum(attention * grad_attention, axis=-1, keepdims=True)
        grad_scores = (attention * (grad_attention - inner)).astype(jnp.bfloat16)
        query_part = (
            jnp.einsum("hqk,khd->qhd", grad_scores, keys_lane, preferred_element_type=jnp.float32)
            * SCORE_SCALE
        )
        key_part = (
            jnp.einsum("hqk,qhd->khd", grad_scores, query_lane, preferred_element_type=jnp.float32)
            * SCORE_SCALE
        )
        value_part = jnp.einsum(
            "hqk,qhd->khd",
            attention.astype(jnp.bfloat16),
            grad_lane,
            preferred_element_type=jnp.float32,
        )
        stacked = jnp.stack(
            [key_part.reshape(key_rows, features), value_part.reshape(key_rows, features)], axis=1
        )
        key_terms = stacked[:, None]
        grad_query = query_part.reshape(rows_dev, 1, features)
        return (grad_query, key_terms)

    initial = (
        jnp.zeros((rows_dev, lane_count, features), jnp.float32),
        jnp.zeros((key_rows, lane_count, 2, features), jnp.float32),
    )
    return lax.fori_loop(0, lane_count, one_lane, initial)


def front(stream, layer_index, params, query_tags, key_tags, positions):
    (
        gain_one,
        shift_one,
        mat_qkv,
        bias_qkv,
        mat_out,
        bias_out,
        gain_two,
        shift_two,
        mat_up,
        bias_up,
        mat_down,
        bias_down,
    ) = [item[layer_index] for item in params]
    rows_dev, lane_count, width = stream.shape
    features = mat_qkv.shape[2]
    head_count = features // HEAD_DIM
    frame_place, row_place, column_place = positions
    first = layer_norm(stream, gain_one, shift_one).astype(jnp.bfloat16)
    projected = (
        jnp.einsum("tbd,dcf->tbcf", first, mat_qkv, preferred_element_type=jnp.float32) + bias_qkv
    )
    split = projected.reshape(rows_dev, lane_count, 3, head_count, HEAD_DIM)
    query = (
        rotate(split[:, :, 0], frame_place, row_place, column_place)
        .reshape(rows_dev, lane_count, features)
        .astype(jnp.bfloat16)
    )
    keys = (
        rotate(split[:, :, 1], frame_place, row_place, column_place)
        .reshape(rows_dev, lane_count, features)
        .astype(jnp.bfloat16)
    )
    values = projected[:, :, 2].astype(jnp.bfloat16)
    keys_all, values_all = (
        lax.all_gather(keys, "seq", axis=0, tiled=True),
        lax.all_gather(values, "seq", axis=0, tiled=True),
    )
    mixed_full, log_total = attend_forward(query, keys_all, values_all, query_tags, key_tags)
    mixed = mixed_full.astype(jnp.bfloat16)
    middle = (
        stream
        + sum_heads(jnp.einsum("tbf,fd->tbd", mixed, mat_out, preferred_element_type=jnp.float32))
        + bias_out
    )
    second = layer_norm(middle, gain_two, shift_two).astype(jnp.bfloat16)
    hidden = jnp.einsum("tbd,df->tbf", second, mat_up, preferred_element_type=jnp.float32) + bias_up
    activation = gelu_exact(hidden).astype(jnp.bfloat16)
    return (
        first,
        query,
        keys_all,
        values_all,
        log_total,
        mixed,
        middle,
        second,
        hidden,
        activation,
        mixed_full,
    )


def layer_backward(stream, gradient, layer_index, params, query_tags, key_tags, positions):
    (
        gain_one,
        shift_one,
        mat_qkv,
        bias_qkv,
        mat_out,
        bias_out,
        gain_two,
        shift_two,
        mat_up,
        bias_up,
        mat_down,
        bias_down,
    ) = [item[layer_index] for item in params]
    (
        first,
        query,
        keys_all,
        values_all,
        log_total,
        mixed,
        middle,
        second,
        hidden,
        activation,
        mixed_full,
    ) = front(stream, layer_index, params, query_tags, key_tags, positions)
    frame_place, row_place, column_place = positions
    rows_dev, lane_count, width = stream.shape
    features = query.shape[2]
    head_count = features // HEAD_DIM
    grad_low = gradient.astype(jnp.bfloat16)
    grad_w_down = jnp.einsum(
        "tbf,tbd->fd", activation, grad_low, preferred_element_type=jnp.float32
    )
    grad_b_down = jnp.sum(gradient, axis=(0, 1))
    grad_activation = jnp.einsum(
        "tbd,fd->tbf", grad_low, mat_down, preferred_element_type=jnp.float32
    )
    grad_hidden = jax.vjp(gelu_exact, hidden)[1](grad_activation)[0].astype(jnp.bfloat16)
    grad_b_up = jnp.sum(grad_hidden.astype(jnp.float32), axis=(0, 1))
    grad_w_up = jnp.einsum("tbd,tbf->df", second, grad_hidden, preferred_element_type=jnp.float32)
    grad_second = sum_inputs(
        jnp.einsum("tbf,df->tbd", grad_hidden, mat_up, preferred_element_type=jnp.float32)
    )
    middle_pull = jax.vjp(layer_norm, middle, gain_two, shift_two)[1]
    grad_inner, grad_gain_two, grad_shift_two = middle_pull(grad_second)
    grad_middle = gradient + grad_inner
    grad_b_out = jnp.sum(grad_middle, axis=(0, 1))
    middle_low = grad_middle.astype(jnp.bfloat16)
    grad_w_out = jnp.einsum("tbf,tbd->fd", mixed, middle_low, preferred_element_type=jnp.float32)
    grad_mixed = jnp.einsum(
        "tbd,fd->tbf", middle_low, mat_out, preferred_element_type=jnp.float32
    ).astype(jnp.bfloat16)
    grad_query, key_terms = attend_backward(
        query, keys_all, values_all, log_total, grad_mixed, query_tags, key_tags
    )
    returned = lax.psum_scatter(key_terms, "seq", scatter_dimension=0, tiled=True)
    turned_query = rotate(
        grad_query.reshape(rows_dev, lane_count, head_count, HEAD_DIM),
        -frame_place,
        -row_place,
        -column_place,
    )
    turned_keys = rotate(
        returned[:, :, 0].reshape(rows_dev, lane_count, head_count, HEAD_DIM),
        -frame_place,
        -row_place,
        -column_place,
    )
    grad_projected = jnp.stack(
        [
            turned_query.reshape(rows_dev, lane_count, features),
            turned_keys.reshape(rows_dev, lane_count, features),
            returned[:, :, 1],
        ],
        axis=2,
    ).astype(jnp.bfloat16)
    grad_b_qkv = jnp.sum(grad_projected.astype(jnp.float32), axis=(0, 1))
    grad_w_qkv = jnp.einsum(
        "tbd,tbcf->dcf", first, grad_projected, preferred_element_type=jnp.float32
    )
    grad_first = sum_inputs(
        jnp.einsum("tbcf,dcf->tbd", grad_projected, mat_qkv, preferred_element_type=jnp.float32)
    )
    first_pull = jax.vjp(layer_norm, stream, gain_one, shift_one)[1]
    grad_entry, grad_gain_one, grad_shift_one = first_pull(grad_first)
    grads = (
        grad_gain_one,
        grad_shift_one,
        grad_w_qkv,
        grad_b_qkv,
        grad_w_out,
        grad_b_out,
        grad_gain_two,
        grad_shift_two,
        grad_w_up,
        grad_b_up,
        grad_w_down,
        grad_b_down,
    )
    return (grad_middle + grad_entry, grads)


def per_device(
    tokens,
    d_out,
    norm1_gain,
    norm1_shift,
    w_qkv,
    b_qkv,
    w_out,
    b_out,
    norm2_gain,
    norm2_shift,
    w_up,
    b_up,
    w_down,
    b_down,
    episode_frames,
    live,
):
    rows_dev = tokens.shape[0]
    lane_count = tokens.shape[1] // MICRO
    total_rows = rows_dev * lax.axis_size("seq")
    local_positions = lax.axis_index("seq") * rows_dev + jnp.arange(rows_dev, dtype=jnp.int32)
    key_positions = jnp.arange(total_rows, dtype=jnp.int32)
    tagger = jax.vmap(episode_tags, in_axes=(0, None), out_axes=1)
    query_episode, query_frame, query_row, query_column = tagger(episode_frames, local_positions)
    key_episode, key_frame, key_row, key_column = tagger(episode_frames, key_positions)
    live_keys = lax.all_gather(live, "seq", axis=0, tiled=True)
    params = (
        norm1_gain,
        norm1_shift,
        w_qkv,
        b_qkv,
        w_out,
        b_out,
        norm2_gain,
        norm2_shift,
        w_up,
        b_up,
        w_down,
        b_down,
    )
    layer_grads = [None] * LAYERS
    outputs = []
    grad_tokens = []
    for micro_index in range(MICRO):
        first_lane = micro_index * lane_count
        last_lane = first_lane + lane_count
        query_tags = (query_episode[:, first_lane:last_lane], query_frame[:, first_lane:last_lane])
        key_tags = (
            key_episode[:, first_lane:last_lane],
            key_frame[:, first_lane:last_lane],
            live_keys[:, first_lane:last_lane],
        )
        positions = (
            query_frame[:, first_lane:last_lane],
            query_row[:, first_lane:last_lane],
            query_column[:, first_lane:last_lane],
        )
        stream = tokens[:, first_lane:last_lane].astype(jnp.float32)
        inputs = []
        gathered = []
        for layer_index in range(LAYERS):
            inputs.append(stream)
            layer_state = front(stream, layer_index, params, query_tags, key_tags, positions)
            gathered.append((layer_state[2], layer_state[3]))
            branch = jnp.einsum(
                "tbf,fd->tbd",
                layer_state[9],
                w_down[layer_index],
                preferred_element_type=jnp.float32,
            )
            stream = layer_state[6] + sum_heads(branch) + b_down[layer_index]
        outputs.append(stream)
        gradient = d_out[:, first_lane:last_lane]
        for layer_index in reversed(range(LAYERS)):
            gradient, grads = layer_backward(
                inputs[layer_index], gradient, layer_index, params, query_tags, key_tags, positions
            )
            if layer_grads[layer_index] is None:
                layer_grads[layer_index] = grads
            else:
                layer_grads[layer_index] = jax.tree.map(jnp.add, layer_grads[layer_index], grads)
        grad_tokens.append(gradient)
    stacked = [
        jnp.stack([layer_grads[layer_index][entry] for layer_index in range(LAYERS)])
        for entry in range(12)
    ]
    (
        grad_gain_one,
        grad_shift_one,
        grad_w_qkv,
        grad_b_qkv,
        grad_w_out,
        grad_b_out,
        grad_gain_two,
        grad_shift_two,
        grad_w_up,
        grad_b_up,
        grad_w_down,
        grad_b_down,
    ) = stacked
    in_sums = (
        lax.psum_scatter(grad_w_qkv, "seq", scatter_dimension=1, tiled=True),
        lax.psum_scatter(grad_w_up, "seq", scatter_dimension=1, tiled=True),
        lax.psum_scatter(grad_gain_one, "seq", scatter_dimension=1, tiled=True),
        lax.psum_scatter(grad_shift_one, "seq", scatter_dimension=1, tiled=True),
        lax.psum_scatter(grad_gain_two, "seq", scatter_dimension=1, tiled=True),
        lax.psum_scatter(grad_shift_two, "seq", scatter_dimension=1, tiled=True),
        lax.psum_scatter(grad_b_out, "seq", scatter_dimension=1, tiled=True),
        lax.psum_scatter(grad_b_down, "seq", scatter_dimension=1, tiled=True),
    )
    out_sums = (
        lax.psum_scatter(grad_w_out, "seq", scatter_dimension=2, tiled=True),
        lax.psum_scatter(grad_w_down, "seq", scatter_dimension=2, tiled=True),
    )
    bias_total = lax.psum((grad_b_qkv, grad_b_up), "seq")
    return (
        jnp.concatenate(outputs, axis=1),
        jnp.concatenate(grad_tokens, axis=1),
        in_sums[2],
        in_sums[3],
        in_sums[0],
        bias_total[0],
        out_sums[0],
        in_sums[6],
        in_sums[4],
        in_sums[5],
        in_sums[1],
        bias_total[1],
        out_sums[1],
        in_sums[7],
    )


MESH = pl.DeviceIdType.MESH
BF16 = jnp.bfloat16
F32 = jnp.float32
VMEM_BYTES = 60 * 1024 * 1024
PAIR = 128
VEC = 2048


def nn(left, right):
    return lax.dot_general(left, right, (((1,), (0,)), ((), ())), preferred_element_type=F32)


def nt(left, right):
    return lax.dot_general(left, right, (((1,), (1,)), ((), ())), preferred_element_type=F32)


def tn(left, right):
    return lax.dot_general(left, right, (((0,), (0,)), ((), ())), preferred_element_type=F32)


def at(start, size):
    return pl.ds(pl.multiple_of(start, size), size)


def remote(src, dst, send, recv, seq, tp):
    return pltpu.make_async_remote_copy(
        src_ref=src,
        dst_ref=dst,
        send_sem=send,
        recv_sem=recv,
        device_id=(seq, tp),
        device_id_type=MESH,
    )


def greet(partners):
    barrier = pltpu.get_barrier_semaphore()
    for seq, tp in partners:
        pl.semaphore_signal(barrier, inc=1, device_id=(seq, tp), device_id_type=MESH)
    pl.semaphore_wait(barrier, len(partners))


def whole(array):
    zeros = (0,) * array.ndim
    return pl.BlockSpec(array.shape, lambda s: zeros, pipeline_mode=pl.Buffered(1))


def whole_out(shape):
    zeros = (0,) * len(shape)
    return pl.BlockSpec(shape, lambda s: zeros)


ANYWHERE = pl.BlockSpec(memory_space=pl.ANY)


def turn_constants():
    frequency = np.exp(np.arange(10, dtype=np.float32) * np.float32(-math.log(10000.0) / 10.0))
    within = np.arange(FRAME)
    table = np.zeros((3, FRAME, PAIR), np.float32)
    for head in range(2):
        base = head * HEAD_DIM
        for section, place in ((1, within // GRID), (2, within % GRID)):
            angle = place.astype(np.float32)[:, None] * frequency.astype(np.float32)
            lower = slice(base + 20 * section, base + 20 * section + 10)
            upper = slice(base + 20 * section + 10, base + 20 * section + 20)
            table[0, :, lower] = np.cos(angle)
            table[0, :, upper] = np.cos(angle)
            table[1, :, lower] = -np.sin(angle)
            table[2, :, upper] = np.sin(angle)
        table[0, :, base + 60 : base + 64] = 1.0
    return jnp.asarray(table)


def turn_frames(frame_index):
    frequency = jnp.exp(jnp.arange(10, dtype=F32) * (-math.log(10000.0) / 10.0))
    angle = frame_index.astype(F32)[:, None] * frequency
    cosine, sine = jnp.cos(angle), jnp.sin(angle)
    none, rest = jnp.zeros_like(sine), jnp.zeros((frame_index.shape[0], 44), F32)

    def row(first, second):
        return jnp.concatenate([first, second, rest, first, second, rest], axis=1)

    table = jnp.stack([row(cosine, cosine), row(-sine, none), row(none, sine)])
    return jnp.pad(table, ((0, 0), (0, 8 - frame_index.shape[0]), (0, 0)))


def turn(values, tables, back=False):
    cosine, lower, upper = tables
    pieces = []
    for start in range(0, values.shape[1], PAIR):
        slab = values[:, start : start + PAIR]
        moved = pltpu.roll(slab, PAIR - 10, 1) * lower + pltpu.roll(slab, 10, 1) * upper
        pieces.append(slab * cosine - moved if back else slab * cosine + moved)
    return jnp.concatenate(pieces, axis=1)


def tables_of(fixed_ref, frames_ref, chunk):
    return [fixed_ref[i] + frames_ref[i, pl.ds(chunk, 1), :] for i in range(3)]


def normed(stream):
    center = stream - jnp.mean(stream, axis=-1, keepdims=True)
    spread = jnp.mean(center * center, axis=-1, keepdims=True)
    scale = lax.rsqrt(spread + EPSILON)
    return center * scale, scale


def norm_pull(grad, gain, unit, scale):
    scaled = grad * gain
    return scale * (
        scaled
        - jnp.mean(scaled, axis=-1, keepdims=True)
        - unit * jnp.mean(scaled * unit, axis=-1, keepdims=True)
    )


def column_sum(values):
    return jnp.sum(values, axis=0, keepdims=True)


def gelu_both(hidden):
    normal = 0.5 + 0.5 * lax.erf(hidden * math.sqrt(0.5))
    density = jnp.exp(hidden * hidden * -0.5) * (1.0 / math.sqrt(2.0 * math.pi))
    return hidden * normal, normal + hidden * density


def project(stream, chunk, pair, refs, outs, first_full):
    gain, shift, weight, bias, fixed, frames = refs
    query_ref, key_ref, value_ref, first_ref = outs
    unit, _ = normed(stream)
    first = (unit * gain[...] + shift[...]).astype(BF16)
    first_full[...] = first
    first_ref[...] = first_full[:, at(pair * PAIR, PAIR)]
    tables = tables_of(fixed, frames, chunk)
    half = query_ref.shape[1]
    query = nn(first, weight[:, :half]) + bias[:, :half]
    query_ref[...] = (turn(query, tables) * SCORE_SCALE).astype(BF16)
    key = nn(first, weight[:, half : 2 * half]) + bias[:, half : 2 * half]
    key_ref[...] = turn(key, tables).astype(BF16)
    value = nn(first, weight[:, 2 * half :]) + bias[:, 2 * half :]
    value_ref[...] = value.astype(BF16)


def gather_lane(mine, live_tiles, allow, n):
    _, kinds, _, rows, half = mine.shape
    planes = n // 4
    total = n * rows
    chunks = total // FRAME
    per_frame = FRAME // rows

    def kernel(
        mine_ref,
        live_ref,
        allow_ref,
        all_ref,
        lives_ref,
        bias_ref,
        x_send,
        x_recv,
        own_sem,
        up_send,
        down_send,
        z_recv,
        y_send,
        y_recv,
        c_send,
        c_recv,
    ):
        me, core = lax.axis_index("seq"), lax.axis_index("tp")
        x, y, z = lax.rem(me, 2), lax.rem(me // 2, 2), me // 4
        beside, across = me + 1 - 2 * x, me + 2 - 4 * y

        barrier = pltpu.get_barrier_semaphore()
        for seq, tp in ((beside, core), (across, core), (me, 1 - core)):
            pl.semaphore_signal(barrier, inc=1, device_id=(seq, tp), device_id_type=MESH)

        @pl.when(z > 0)
        def _():
            pl.semaphore_signal(barrier, inc=1, device_id=(me - 4, core), device_id_type=MESH)

        @pl.when(z < planes - 1)
        def _():
            pl.semaphore_signal(barrier, inc=1, device_id=(me + 4, core), device_id_type=MESH)

        inner = (z > 0).astype(jnp.int32) + (z < planes - 1).astype(jnp.int32)
        pl.semaphore_wait(barrier, 3 + inner)

        def block(side, pair):
            return all_ref.at[:, side, at(pair * 2 * rows, 2 * rows), :]

        def lives(pair):
            return lives_ref.at[at(pair * 2, 2)]

        def x_copies():
            return [
                remote(
                    mine_ref.at[1 - x, :, core],
                    all_ref.at[:, core, at(me * rows, rows), :],
                    x_send.at[0],
                    x_recv.at[0],
                    beside,
                    core,
                ),
                remote(
                    live_ref.at[1 - x],
                    lives_ref.at[me],
                    x_send.at[1],
                    x_recv.at[1],
                    beside,
                    core,
                ),
            ]

        def own_copies():
            return [
                pltpu.make_async_copy(
                    mine_ref.at[x, :, core],
                    all_ref.at[:, core, at(me * rows, rows), :],
                    own_sem.at[0],
                ),
                pltpu.make_async_copy(live_ref.at[x], lives_ref.at[me], own_sem.at[1]),
            ]

        def z_copies(plane, step, sends):
            pair = plane * 2 + y
            return [
                remote(
                    block(core, pair),
                    block(core, pair),
                    sends.at[plane, 0],
                    z_recv.at[plane, 0],
                    me + step,
                    core,
                ),
                remote(
                    lives(pair), lives(pair), sends.at[plane, 1], z_recv.at[plane, 1], me + step, core
                ),
            ]

        def y_copies(plane, row):
            pair = plane * 2 + row
            return [
                remote(
                    block(core, pair),
                    block(core, pair),
                    y_send.at[plane, 0],
                    y_recv.at[plane, 0],
                    across,
                    core,
                ),
                remote(
                    lives(pair), lives(pair), y_send.at[plane, 1], y_recv.at[plane, 1], across, core
                ),
            ]

        def c_copy(pair, side):
            return remote(
                block(side, pair), block(side, pair), c_send.at[pair], c_recv.at[pair], me, 1 - core
            )

        def start(copies):
            for copy in copies:
                copy.start()

        start(x_copies())
        start(own_copies())
        for copy in own_copies():
            copy.wait()
        for copy in x_copies():
            copy.wait_recv()

        def pass_on(plane, up, down):
            @pl.when(up)
            def _():
                start(z_copies(plane, 4, up_send))

            @pl.when(down)
            def _():
                start(z_copies(plane, -4, down_send))

            start(y_copies(plane, y))
            c_copy(plane * 2 + y, core).start()

        pass_on(z, z < planes - 1, z > 0)
        for step in range(1, planes):

            @pl.when(z - step >= 0)
            def _():
                for copy in z_copies(z - step, 4, up_send):
                    copy.wait_recv()
                pass_on(z - step, z < planes - 1, z < 0)

            @pl.when(z + step < planes)
            def _():
                for copy in z_copies(z + step, -4, down_send):
                    copy.wait_recv()
                pass_on(z + step, z < 0, z > 0)

        for plane in range(planes):
            for copy in y_copies(plane, 1 - y):
                copy.wait_recv()
            c_copy(plane * 2 + 1 - y, core).start()
        for pair in range(2 * planes):
            c_copy(pair, 1 - core).wait_recv()

        for copy in x_copies():
            copy.wait_send()
        for plane in range(planes):

            @pl.when((plane <= z) & (z < planes - 1))
            def _():
                for copy in z_copies(plane, 4, up_send):
                    copy.wait_send()

            @pl.when((plane >= z) & (z > 0))
            def _():
                for copy in z_copies(plane, -4, down_send):
                    copy.wait_send()

            for copy in y_copies(plane, y):
                copy.wait_send()
        for pair in range(2 * planes):
            c_copy(pair, core).wait_send()

        for key_frame in range(chunks):
            alive = lives_ref[key_frame * per_frame, 0:1, :]
            for part in range(1, per_frame):
                alive = alive + lives_ref[key_frame * per_frame + part, 0:1, :]
            closed = (alive - 1.0) * -MASKED
            for query_frame in range(chunks):
                place = query_frame * chunks + key_frame
                bias_ref[query_frame : query_frame + 1, key_frame * FRAME : (key_frame + 1) * FRAME] = (
                    allow_ref[place : place + 1, :] + closed
                )

    dma = pltpu.SemaphoreType.DMA
    in_vmem = pl.BlockSpec(memory_space=pltpu.VMEM)
    return pl.pallas_call(
        kernel,
        out_shape=(
            jax.ShapeDtypeStruct((kinds, 2, total, half), BF16),
            jax.ShapeDtypeStruct((n, 8, FRAME), F32),
            jax.ShapeDtypeStruct((8, total), F32),
        ),
        in_specs=[in_vmem] * 3,
        out_specs=(in_vmem,) * 3,
        scratch_shapes=[
            dma((2,)),
            dma((2,)),
            dma((2,)),
            dma((planes, 2)),
            dma((planes, 2)),
            dma((planes, 2)),
            dma((planes, 2)),
            dma((planes, 2)),
            dma((2 * planes,)),
            dma((2 * planes,)),
        ],
        compiler_params=pltpu.CompilerParams(
            collective_id=0, has_side_effects=True, vmem_limit_bytes=VMEM_BYTES
        ),
        name="gather_lane",
    )(mine, live_tiles, allow)


def first_projection(gathered, gain, shift, weight, bias, fixed, frames):
    _, _, total, half = gathered.shape
    chunks = total // FRAME
    width = 2 * half
    features = weight.shape[1] // 3

    def kernel(x_ref, gain, shift, weight, bias, fixed, frames, x_out, q_ref, k_ref, v_ref, f_ref, full):
        stream = jnp.concatenate([x_ref[0, 0], x_ref[0, 1]], axis=1).astype(F32)
        x_out[...] = stream
        project(
            stream,
            pl.program_id(0),
            lax.axis_index("seq") // 2,
            (gain, shift, weight, bias, fixed, frames),
            (q_ref, k_ref, v_ref, f_ref),
            full,
        )

    def rows(columns):
        return pl.BlockSpec((FRAME, columns), lambda s: (s, 0))

    return pl.pallas_call(
        kernel,
        grid=(chunks,),
        out_shape=(
            jax.ShapeDtypeStruct((total, width), F32),
            jax.ShapeDtypeStruct((total, features), BF16),
            jax.ShapeDtypeStruct((total, features), BF16),
            jax.ShapeDtypeStruct((total, features), BF16),
            jax.ShapeDtypeStruct((total, PAIR), BF16),
        ),
        in_specs=[pl.BlockSpec((1, 2, FRAME, half), lambda s: (0, 0, s, 0))]
        + [whole(item) for item in (gain, shift, weight, bias, fixed, frames)],
        out_specs=(rows(width), rows(features), rows(features), rows(features), rows(PAIR)),
        scratch_shapes=[pltpu.VMEM((FRAME, width), BF16)],
        compiler_params=pltpu.CompilerParams(vmem_limit_bytes=VMEM_BYTES),
        name="first_projection",
    )(gathered, gain, shift, weight, bias, fixed, frames)


def layer_forward(layer, query, key, value, key_bias, stream, mats, rows_of, next_refs, identity):
    total, features = query.shape
    width = stream.shape[1]
    hidden_units = mats[1].shape[2]
    chunks = total // FRAME
    heads = features // HEAD_DIM
    slabs = features // PAIR
    columns = 512
    last = next_refs is None
    b_out, gain, shift, b_up, b_down = rows_of
    mat_out, mat_up, mat_down = mats

    def kernel(*refs):
        refs = list(refs)

        def take(count):
            taken = refs[:count]
            del refs[:count]
            return taken

        q_ref, k_ref, v_ref, kb_ref, x_ref = take(5)
        wo_any, wu_any, wd_any = take(3)
        bo_ref, gain_ref, shift_ref, bu_ref, bd_ref = take(5)
        if not last:
            wq_any, ngain, nshift, nbias, fixed, frames = take(6)
        p_ref, mixed_ref, middle_ref, second_ref, act_ref, gp_ref, x_out = take(7)
        if not last:
            nq_ref, nk_ref, nv_ref, nf_ref = take(4)
        wo, wu, wd, mid, full, low = take(6)
        if not last:
            (wq,) = take(1)
        a_send, a_recv, b_send, b_recv, w_sem, send_sem, recv_sem = take(7)

        step = pl.program_id(0)
        me, core = lax.axis_index("seq"), lax.axis_index("tp")

        items = [(wo_any, wo), (wu_any, wu), (wd_any, wd)]
        if not last:
            items.append((wq_any, wq))

        def load(index):
            source, target = items[index]
            return pltpu.make_async_copy(
                source.at[layer] if index < 3 else source, target, w_sem.at[index]
            )

        def exchange(kind, chunk):
            source, target = ((a_send, a_recv), (b_send, b_recv))[kind]
            return remote(
                source.at[chunk],
                target.at[chunk],
                send_sem.at[kind, chunk],
                recv_sem.at[kind, chunk],
                me,
                1 - core,
            )

        @pl.when(step == 0)
        def _():
            for index in range(len(items)):
                load(index).start()
            greet([(me, 1 - core)])

        lane = lax.broadcasted_iota(jnp.int32, (1, PAIR), 1)
        sides = [(lane < HEAD_DIM).astype(F32).astype(BF16), (lane >= HEAD_DIM).astype(F32).astype(BF16)]
        for frame in range(chunks):

            @pl.when(step == frame)
            def _():
                keys = FRAME * (frame + 1)
                bias = kb_ref[frame : frame + 1, :keys]

                def one_slab(slab, carry):
                    lanes = at(slab * PAIR, PAIR)
                    q2, k2, v2 = q_ref[:, lanes], k_ref[:keys, lanes], v_ref[:keys, lanes]
                    results = []
                    for side in range(2):
                        scores = nt(q2 * sides[side], k2) + bias
                        highest = jnp.max(scores, axis=-1, keepdims=True)
                        shifted = jnp.exp(scores - highest)
                        summed = jnp.sum(shifted, axis=-1, keepdims=True)
                        attention = (shifted * (1.0 / summed)).astype(BF16)
                        p_ref[0, slab * 2 + side, :, :keys] = attention
                        results.append(nn(attention, v2))
                    mixed = jnp.where(lane < HEAD_DIM, results[0], results[1])
                    mixed_ref[:, lanes] = mixed.astype(BF16)
                    return carry

                lax.fori_loop(0, slabs, one_slab, 0)

        @pl.when(step == 0)
        def _():
            load(0).wait()

        @pl.when(step < chunks)
        def _():
            a_send[step] = nn(mixed_ref[...], wo[...]).astype(BF16)
            exchange(0, step).start()

        @pl.when(step == 1)
        def _():
            load(1).wait()
            load(2).wait()

        @pl.when((step >= 1) & (step <= chunks))
        def _():
            chunk = step - 1
            exchange(0, chunk).wait_recv()
            middle = x_ref[...] + (a_send[chunk].astype(F32) + a_recv[chunk].astype(F32)) + bo_ref[...]
            middle_ref[...] = middle
            mid[lax.rem(chunk, 2)] = middle
            unit, _ = normed(middle)
            second = (unit * gain_ref[...] + shift_ref[...]).astype(BF16)
            full[...] = second
            second_ref[...] = full[:, at((me // 2) * PAIR, PAIR)]
            for start in range(0, hidden_units, columns):
                part = slice(start, start + columns)
                hidden = nn(second, wu[:, part]) + bu_ref[:, part]
                act, slope = gelu_both(hidden)
                act = act.astype(BF16)
                act_ref[:, part] = act
                gp_ref[:, part] = slope.astype(BF16)
                down = nn(act, wd[part, :])
                if start == 0:
                    low[...] = down
                else:
                    low[...] += down
            b_send[chunk] = low[...].astype(BF16)
            exchange(1, chunk).start()

        if not last:

            @pl.when(step == 2)
            def _():
                load(3).wait()

        @pl.when(step >= 2)
        def _():
            chunk = step - 2
            exchange(1, chunk).wait_recv()
            result = (
                mid[lax.rem(chunk, 2)]
                + (b_send[chunk].astype(F32) + b_recv[chunk].astype(F32))
                + bd_ref[...]
            )
            x_out[...] = result
            if not last:
                project(
                    result,
                    chunk,
                    me // 2,
                    (ngain, nshift, wq, nbias, fixed, frames),
                    (nq_ref, nk_ref, nv_ref, nf_ref),
                    full,
                )

        @pl.when(step == chunks + 1)
        def _():
            for kind in range(2):
                for chunk in range(chunks):
                    exchange(kind, chunk).wait_send()

    def rows(columns, behind):
        return pl.BlockSpec(
            (FRAME, columns), lambda s: (jnp.clip(s - behind, 0, chunks - 1), 0)
        )

    in_specs = [rows(features, 0), whole(key), whole(value), whole(key_bias), rows(width, 1)]
    in_specs += [ANYWHERE] * 3 + [whole(item) for item in rows_of]
    operands = [query, key, value, key_bias, stream, *mats, *rows_of]
    if not last:
        in_specs += [ANYWHERE] + [whole(item) for item in next_refs[1:]]
        operands += list(next_refs)
    out_shape = [
        jax.ShapeDtypeStruct((chunks, heads, FRAME, total), BF16),
        jax.ShapeDtypeStruct((total, features), BF16),
        jax.ShapeDtypeStruct((total, width), F32),
        jax.ShapeDtypeStruct((total, PAIR), BF16),
        jax.ShapeDtypeStruct((total, hidden_units), BF16),
        jax.ShapeDtypeStruct((total, hidden_units), BF16),
        jax.ShapeDtypeStruct((total, width), F32),
    ]
    out_specs = [
        pl.BlockSpec((1, heads, FRAME, total), lambda s: (jnp.minimum(s, chunks - 1), 0, 0, 0)),
        rows(features, 0),
        rows(width, 1),
        rows(PAIR, 1),
        rows(hidden_units, 1),
        rows(hidden_units, 1),
        rows(width, 2),
    ]
    scratch = [
        pltpu.VMEM(mat_out.shape[1:], BF16),
        pltpu.VMEM(mat_up.shape[1:], BF16),
        pltpu.VMEM(mat_down.shape[1:], BF16),
        pltpu.VMEM((2, FRAME, width), F32),
        pltpu.VMEM((FRAME, width), BF16),
        pltpu.VMEM((FRAME, width), F32),
    ]
    if not last:
        out_shape += [jax.ShapeDtypeStruct((total, features), BF16)] * 3
        out_shape += [jax.ShapeDtypeStruct((total, PAIR), BF16)]
        out_specs += [rows(features, 2)] * 3 + [rows(PAIR, 2)]
        scratch += [pltpu.VMEM(next_refs[0].shape, BF16)]
    scratch += [pltpu.VMEM((chunks, FRAME, width), BF16)] * 4
    scratch += [
        pltpu.SemaphoreType.DMA((4,)),
        pltpu.SemaphoreType.DMA((2, chunks)),
        pltpu.SemaphoreType.DMA((2, chunks)),
    ]
    return pl.pallas_call(
        kernel,
        grid=(chunks + 2,),
        out_shape=out_shape,
        in_specs=in_specs,
        out_specs=out_specs,
        scratch_shapes=scratch,
        compiler_params=pltpu.CompilerParams(
            collective_id=identity, has_side_effects=True, vmem_limit_bytes=VMEM_BYTES
        ),
        name=f"layer_forward_{layer}",
    )(*operands)


def attention_backward(probs, query, key, value, grad_mixed, fixed, frames, ships, lane_rows, identity):
    total, features = query.shape
    chunks = total // FRAME
    slabs = features // PAIR
    half = PAIR // 2
    ship_count, row_count = len(ships), len(lane_rows)

    def kernel(*refs):
        refs = list(refs)

        def take(count):
            taken = refs[:count]
            del refs[:count]
            return taken

        p_ref, q_ref, k_ref, v_ref, g_ref, fixed_ref, frames_ref = take(7)
        ship_refs, row_refs = take(ship_count), take(row_count)
        dq_ref, dk_ref, dv_ref = take(3)
        ship_outs, row_outs = take(ship_count), take(row_count)
        dk_sum, dv_sum = take(2)
        ship_sends, ship_recvs = take(ship_count), take(ship_count)
        send_sem, recv_sem = take(2)

        step = pl.program_id(0)
        me, core = lax.axis_index("seq"), lax.axis_index("tp")
        x = lax.rem(me, 2)
        beside = me + 1 - 2 * x

        def copies():
            items = [
                (send, recv) for send, recv in zip(ship_sends, ship_recvs)
            ]
            for (_, count), ref, out in zip(lane_rows, row_refs, row_outs):
                items.append((ref.at[at(beside * count, count), :] if count else ref, out))
            return [
                remote(source, target, send_sem.at[i], recv_sem.at[i], beside, core)
                for i, (source, target) in enumerate(items)
            ]

        @pl.when(step == 0)
        def _():
            greet([(beside, core)])
            for ref, send in zip(ship_refs, ship_sends):
                send[...] = ref[at((1 - x) * half, half), :].astype(BF16)
            for copy in copies():
                copy.start()

        lane = lax.broadcasted_iota(jnp.int32, (1, PAIR), 1)
        sides = [(lane < HEAD_DIM).astype(F32).astype(BF16), (lane >= HEAD_DIM).astype(F32).astype(BF16)]
        for frame in reversed(range(chunks)):
            keys = FRAME * (frame + 1)
            own = slice(frame * FRAME, keys)
            tables = tables_of(fixed_ref, frames_ref, frame)
            grad_query = None
            key_parts, value_parts = None, None
            for side in range(2):
                g2 = g_ref[own, :] * sides[side]
                q2 = q_ref[own, :] * sides[side]
                attention = p_ref[frame, side, :, :keys]
                grad = nt(g2, v_ref[:keys, :])
                wide = attention.astype(F32)
                inner = jnp.sum(wide * grad, axis=-1, keepdims=True)
                grad_scores = (wide * (grad - inner)).astype(BF16)
                term = nn(grad_scores, k_ref[:keys, :] * sides[side])
                grad_query = term if grad_query is None else grad_query + term
                key_term, value_term = tn(grad_scores, q2), tn(attention, g2)
                key_parts = key_term if key_parts is None else key_parts + key_term
                value_parts = value_term if value_parts is None else value_parts + value_term
            dq_ref[own, :] = (turn(grad_query, tables, True) * SCORE_SCALE).astype(BF16)
            if frame == chunks - 1:
                dk_sum[...] = key_parts
                dv_sum[...] = value_parts
            else:
                dk_sum[:keys, :] += key_parts
                dv_sum[:keys, :] += value_parts
            dk_ref[own, :] = turn(dk_sum[own, :], tables, True).astype(BF16)
            dv_ref[own, :] = dv_sum[own, :].astype(BF16)

        @pl.when(step == slabs - 1)
        def _():
            for copy in copies():
                copy.wait_recv()
            for ref, recv, out in zip(ship_refs, ship_recvs, ship_outs):
                out[...] = ref[at(x * half, half), :] + recv[...].astype(F32)
            for copy in copies():
                copy.wait_send()

    slab = pl.BlockSpec((total, PAIR), lambda s: (0, s))
    in_specs = [pl.BlockSpec((chunks, 2, FRAME, total), lambda s: (0, s, 0, 0))]
    in_specs += [slab] * 4 + [whole(fixed), whole(frames)]
    in_specs += [whole(item) for item in ships] + [ANYWHERE] * row_count
    out_shape = [jax.ShapeDtypeStruct((total, features), BF16)] * 3
    out_specs = [slab] * 3
    for item in ships:
        out_shape.append(jax.ShapeDtypeStruct((half, item.shape[1]), F32))
        out_specs.append(whole_out((half, item.shape[1])))
    for item, count in lane_rows:
        shape = (count or item.shape[0], item.shape[1])
        out_shape.append(jax.ShapeDtypeStruct(shape, item.dtype))
        out_specs.append(ANYWHERE)
    scratch = [pltpu.VMEM((total, PAIR), F32)] * 2
    scratch += [pltpu.VMEM((half, item.shape[1]), BF16) for item in ships] * 2
    scratch += [pltpu.SemaphoreType.DMA((ship_count + row_count,))] * 2
    return pl.pallas_call(
        kernel,
        grid=(slabs,),
        out_shape=out_shape,
        in_specs=in_specs,
        out_specs=out_specs,
        scratch_shapes=scratch,
        compiler_params=pltpu.CompilerParams(
            collective_id=identity, has_side_effects=True, vmem_limit_bytes=VMEM_BYTES
        ),
        name=f"attention_backward_{identity}",
    )(probs, query, key, value, grad_mixed, fixed, frames, *ships, *[item for item, _ in lane_rows])


def rows_backward(entry, upper, identity):
    top, bottom = len(entry) == 1, upper is None
    total = entry[0].shape[2] if top else entry[0].shape[0]
    chunks = total // FRAME
    columns = 512
    ahead = 0 if top else 1
    if top:
        width = 2 * entry[0].shape[3]
    else:
        features, width = entry[0].shape[1], entry[3].shape[1]
    if not bottom:
        layer = upper[0]
        hidden_units, mixed_features = upper[1].shape[1], upper[5].shape[1]
    half = PAIR // 2
    place_rows = total // lax.axis_size("seq")

    def kernel(*refs):
        refs = list(refs)

        def take(count):
            taken = refs[:count]
            del refs[:count]
            return taken

        if top:
            (d_out_ref,) = take(1)
        else:
            dq_ref, dk_ref, dv_ref, x_ref, dm_ref, first_ref, wq, gain1 = take(8)
        if not bottom:
            act_ref, gp_ref, middle_ref, second_ref, mixed_ref = take(5)
            wo_any, wu_any, wd_any, gain2 = take(4)
        if not top:
            qkv_sum, vec1 = take(2)
        if not bottom:
            dmid_out, dmix_out, out_sum, up_sum, down_sum, vec2 = take(6)
        else:
            dx_out, dx_other = take(2)
        if not top:
            a_send, a_recv = take(2)
        if not bottom:
            b_send, b_recv, grad_keep, part_keep, low_keep, wo, wu, wd, w_sem = take(9)
        else:
            dx_keep, dx_recv, vec_recv, qkv_send, qkv_recv, x_send_sem, x_recv_sem = take(7)
        send_sem, recv_sem = take(2)

        step = pl.program_id(0)
        me, core = lax.axis_index("seq"), lax.axis_index("tp")
        pair = at((me // 2) * PAIR, PAIR)
        x = lax.rem(me, 2)
        beside = me + 1 - 2 * x

        def exchange(kind, chunk):
            source, target = (a_send, a_recv) if kind == 0 else (b_send, b_recv)
            return remote(
                source.at[chunk],
                target.at[chunk],
                send_sem.at[kind, chunk],
                recv_sem.at[kind, chunk],
                me,
                1 - core,
            )

        def load(index):
            source, target = ((wd_any, wd), (wu_any, wu), (wo_any, wo))[index]
            return pltpu.make_async_copy(source.at[layer], target, w_sem.at[index])

        @pl.when(step == 0)
        def _():
            if not bottom:
                for index in range(3):
                    load(index).start()
                out_sum[...] = jnp.zeros_like(out_sum)
                up_sum[...] = jnp.zeros_like(up_sum)
                down_sum[...] = jnp.zeros_like(down_sum)
                vec2[...] = jnp.zeros_like(vec2)
            if not top:
                qkv_sum[...] = jnp.zeros_like(qkv_sum)
                vec1[...] = jnp.zeros_like(vec1)
            greet([(me, 1 - core)] + ([(beside, core)] if bottom else []))

        if not top:

            @pl.when(step < chunks)
            def _():
                first = first_ref[...]
                partial = None
                for part, ref in enumerate((dq_ref, dk_ref, dv_ref)):
                    piece = slice(part * features, (part + 1) * features)
                    grad = ref[...]
                    term = nt(grad, wq[:, piece])
                    partial = term if partial is None else partial + term
                    qkv_sum[:, piece] += tn(first, grad)
                    vec1[0:1, piece] += column_sum(grad.astype(F32))
                a_send[step] = partial.astype(BF16)
                exchange(0, step).start()

        @pl.when((step >= ahead) & (step < chunks + ahead))
        def _():
            chunk = step - ahead
            if top:
                gradient = jnp.concatenate([d_out_ref[0, 0], d_out_ref[0, 1]], axis=1).astype(F32)
            else:
                exchange(0, chunk).wait_recv()
                grad_first = a_send[chunk].astype(F32) + a_recv[chunk].astype(F32)
                unit, scale = normed(x_ref[...])
                vec1[1:2, :width] += column_sum(grad_first * unit)
                vec1[2:3, :width] += column_sum(grad_first)
                gradient = dm_ref[...] + norm_pull(grad_first, gain1[...], unit, scale)
            if bottom:
                dx_keep[at(chunk * FRAME, FRAME), :] = gradient
                return

            @pl.when(chunk == 0)
            def _():
                load(0).wait()
                load(1).wait()

            grad_keep[lax.rem(chunk, 2)] = gradient
            vec2[1:2, :width] += column_sum(gradient)
            low = gradient.astype(BF16)
            low_keep[...] = low
            low_columns = low_keep[:, pair]
            second = second_ref[...]
            for start in range(0, hidden_units, columns):
                part = slice(start, start + columns)
                down_sum[:, part] += tn(low_columns, act_ref[:, part])
                grad_act = nt(low, wd[part, :])
                grad_hidden = (grad_act * gp_ref[:, part].astype(F32)).astype(BF16)
                vec2[0:1, part] += column_sum(grad_hidden.astype(F32))
                up_sum[:, part] += tn(second, grad_hidden)
                term = nt(grad_hidden, wu[:, part])
                if start == 0:
                    part_keep[...] = term
                else:
                    part_keep[...] += term
            b_send[chunk] = part_keep[...].astype(BF16)
            exchange(1, chunk).start()

        if not bottom:

            @pl.when(step == ahead + 1)
            def _():
                load(2).wait()

            @pl.when(step >= ahead + 1)
            def _():
                chunk = step - ahead - 1
                exchange(1, chunk).wait_recv()
                grad_second = b_send[chunk].astype(F32) + b_recv[chunk].astype(F32)
                unit, scale = normed(middle_ref[...])
                vec2[2:3, :width] += column_sum(grad_second * unit)
                vec2[3:4, :width] += column_sum(grad_second)
                grad_middle = grad_keep[lax.rem(chunk, 2)] + norm_pull(
                    grad_second, gain2[...], unit, scale
                )
                dmid_out[...] = grad_middle
                vec2[4:5, :width] += column_sum(grad_middle)
                low = grad_middle.astype(BF16)
                low_keep[...] = low
                out_sum[...] += tn(low_keep[:, pair], mixed_ref[...])
                dmix_out[...] = nt(low, wo[...]).astype(BF16)

        if bottom:

            def x_copy(index):
                source, target = (
                    (qkv_send, qkv_recv),
                    (dx_keep.at[at(beside * place_rows, place_rows), :], dx_recv),
                    (vec1, vec_recv),
                )[index]
                return remote(
                    source, target, x_send_sem.at[index], x_recv_sem.at[index], beside, core
                )

            @pl.when(step == chunks - 1)
            def _():
                qkv_send[...] = qkv_sum[at((1 - x) * half, half), :].astype(BF16)
                x_copy(0).start()

            @pl.when(step == chunks)
            def _():
                x_copy(1).start()
                x_copy(2).start()
                dx_out[...] = dx_keep[at(me * place_rows, place_rows), :]
                for index in range(3):
                    x_copy(index).wait_recv()
                qkv_sum[at(x * half, half), :] += qkv_recv[...].astype(F32)
                dx_other[...] = dx_recv[...]
                for index in range(3):
                    x_copy(index).wait_send()
                vec1[...] += vec_recv[...]

        @pl.when(step == pl.num_programs(0) - 1)
        def _():
            for kind in ([] if top else [0]) + ([] if bottom else [1]):
                for chunk in range(chunks):
                    exchange(kind, chunk).wait_send()

    def rows(columns, behind):
        return pl.BlockSpec(
            (FRAME, columns), lambda s: (jnp.clip(s - behind, 0, chunks - 1), 0)
        )

    vec = jax.ShapeDtypeStruct((8, VEC), F32)
    operands, in_specs, out_shape, out_specs, scratch = [], [], [], [], []
    if top:
        operands += list(entry)
        in_specs += [
            pl.BlockSpec(
                (1, 2, FRAME, width // 2), lambda s: (1, 0, jnp.clip(s, 0, chunks - 1), 0)
            )
        ]
    else:
        operands += list(entry)
        in_specs += [rows(features, 0)] * 3 + [rows(width, 1), rows(width, 1), rows(PAIR, 0)]
        in_specs += [whole(entry[6]), whole(entry[7])]
        out_shape += [jax.ShapeDtypeStruct((PAIR, 3 * features), F32), vec]
        out_specs += [whole_out((PAIR, 3 * features)), whole_out((8, VEC))]
        scratch += [pltpu.VMEM((chunks, FRAME, width), BF16)] * 2
    if not bottom:
        operands += list(upper[1:])
        in_specs += [rows(hidden_units, ahead)] * 2 + [rows(width, ahead + 1), rows(PAIR, ahead)]
        in_specs += [rows(mixed_features, ahead + 1)] + [ANYWHERE] * 3 + [whole(upper[9])]
        sums = [mixed_features, hidden_units, hidden_units]
        out_shape += [
            jax.ShapeDtypeStruct((total, width), F32),
            jax.ShapeDtypeStruct((total, mixed_features), BF16),
        ]
        out_shape += [jax.ShapeDtypeStruct((PAIR, size), F32) for size in sums] + [vec]
        out_specs += [rows(width, ahead + 1), rows(mixed_features, ahead + 1)]
        out_specs += [whole_out((PAIR, size)) for size in sums] + [whole_out((8, VEC))]
        scratch += [pltpu.VMEM((chunks, FRAME, width), BF16)] * 2
        scratch += [
            pltpu.VMEM((2, FRAME, width), F32),
            pltpu.VMEM((FRAME, width), F32),
            pltpu.VMEM((FRAME, width), BF16),
            pltpu.VMEM(upper[6].shape[1:], BF16),
            pltpu.VMEM(upper[7].shape[1:], BF16),
            pltpu.VMEM(upper[8].shape[1:], BF16),
            pltpu.SemaphoreType.DMA((3,)),
        ]
    else:
        out_shape += [
            jax.ShapeDtypeStruct((place_rows, width), F32),
            jax.ShapeDtypeStruct((place_rows, width), F32),
        ]
        out_specs += [whole_out((place_rows, width))] * 2
        scratch += [
            pltpu.VMEM((total, width), F32),
            pltpu.VMEM((place_rows, width), F32),
            pltpu.VMEM((8, VEC), F32),
            pltpu.VMEM((half, 3 * features), BF16),
            pltpu.VMEM((half, 3 * features), BF16),
            pltpu.SemaphoreType.DMA((3,)),
            pltpu.SemaphoreType.DMA((3,)),
        ]
    scratch += [pltpu.SemaphoreType.DMA((2, chunks))] * 2
    return pl.pallas_call(
        kernel,
        grid=(chunks + (1 if top or bottom else 2),),
        out_shape=out_shape,
        in_specs=in_specs,
        out_specs=out_specs,
        scratch_shapes=scratch,
        compiler_params=pltpu.CompilerParams(
            collective_id=identity, has_side_effects=True, vmem_limit_bytes=VMEM_BYTES
        ),
        name=f"rows_backward_{identity}",
    )(*operands)


def per_chip(
    tokens,
    d_out,
    norm1_gain,
    norm1_shift,
    w_qkv,
    b_qkv,
    w_out,
    b_out,
    norm2_gain,
    norm2_shift,
    w_up,
    b_up,
    w_down,
    b_down,
    episode_frames,
    live,
):
    n = lax.axis_size("seq")
    me = lax.axis_index("seq")
    x = me % 2
    rows, lanes, width = tokens.shape
    half = width // 2
    total = rows * n
    chunks = total // FRAME
    features = w_qkv.shape[3]

    mine = jnp.stack([tokens, d_out.astype(BF16)]).reshape(2, rows, lanes, 2, half)
    mine = mine.transpose(2, 0, 3, 1, 4)
    spot = (me * rows) % FRAME
    live_tiles = lax.dynamic_update_slice(
        jnp.zeros((lanes, 8, FRAME), F32),
        jnp.broadcast_to(live.T.astype(F32)[:, None, :], (lanes, 8, rows)),
        (0, 0, spot),
    )
    frame_counts = lax.dynamic_index_in_dim(episode_frames, x, 0, False)
    episode, frame_index, _, _ = episode_tags(
        frame_counts, jnp.arange(chunks, dtype=jnp.int32) * FRAME
    )
    allowed = (episode[:, None] == episode[None, :]) & (frame_index[None, :] <= frame_index[:, None])
    allow = jnp.where(allowed, 0.0, MASKED).astype(F32).reshape(chunks * chunks, 1)
    allow = jnp.broadcast_to(allow, (chunks * chunks, FRAME))
    fixed, frames = turn_constants(), turn_frames(frame_index)

    qkv = w_qkv.reshape(LAYERS, width, 3 * features)
    qkv = [qkv[layer] for layer in range(LAYERS)]
    qkv_bias = b_qkv.reshape(LAYERS, 1, 3 * features)

    def row(item, layer):
        return item[layer][None]

    gathered, _, key_bias = gather_lane(mine, live_tiles, allow, n)
    projections = first_projection(
        gathered, row(norm1_gain, 0), row(norm1_shift, 0), qkv[0], qkv_bias[0], fixed, frames
    )
    streams, kept = [projections[0]], []
    query, key, value, first = projections[1:]
    for layer in range(LAYERS):
        following = None
        if layer + 1 < LAYERS:
            following = (
                qkv[layer + 1],
                row(norm1_gain, layer + 1),
                row(norm1_shift, layer + 1),
                qkv_bias[layer + 1],
                fixed,
                frames,
            )
        results = layer_forward(
            layer,
            query,
            key,
            value,
            key_bias,
            streams[layer],
            (w_out, w_up, w_down),
            (
                row(b_out, layer),
                row(norm2_gain, layer),
                row(norm2_shift, layer),
                row(b_up, layer),
                row(b_down, layer),
            ),
            following,
            1 + layer,
        )
        kept.append((query, key, value, first, *results[:6]))
        streams.append(results[6])
        if following is not None:
            query, key, value, first = results[7:]

    grads = [dict() for _ in range(LAYERS)]
    vecs = [[None, None] for _ in range(LAYERS)]
    entry, pending, pending_rows = (gathered,), [], [(streams[LAYERS], rows)]
    out_other = None
    for layer in reversed(range(LAYERS)):
        query, key, value, first, probs, mixed, middle, second, act, slope = kept[layer]
        upper = (
            layer,
            act,
            slope,
            middle,
            second,
            mixed,
            w_out,
            w_up,
            w_down,
            row(norm2_gain, layer),
        )
        results = rows_backward(entry, upper, 1 + LAYERS + 2 * (LAYERS - 1 - layer))
        if layer + 1 < LAYERS:
            qkv_sum, vec1 = results[:2]
            results = results[2:]
            pending = [("qkv", layer + 1, qkv_sum)]
            pending_rows = [(vec1, 0)]
        grad_middle, grad_mixed, out_sum, up_sum, down_sum, vec2 = results
        pending = pending + [("out", layer, out_sum), ("up", layer, up_sum), ("down", layer, down_sum)]
        pending_rows = pending_rows + [(vec2, 0)]
        results = attention_backward(
            probs,
            query,
            key,
            value,
            grad_mixed,
            fixed,
            frames,
            [item for _, _, item in pending],
            pending_rows,
            2 + LAYERS + 2 * (LAYERS - 1 - layer),
        )
        grad_query, grad_key, grad_value = results[:3]
        swapped = results[3:]
        for (name, owner, _), item in zip(pending, swapped):
            grads[owner][name] = item
        others = swapped[len(pending) :]
        if out_other is None:
            out_other = others[0]
        else:
            vecs[layer + 1][0] = pending_rows[0][0] + others[0]
        vecs[layer][1] = vec2 + others[1]
        entry = (
            grad_query,
            grad_key,
            grad_value,
            streams[layer],
            grad_middle,
            first,
            qkv[layer],
            row(norm1_gain, layer),
        )
    qkv_sum, vec1, dx_own, dx_other = rows_backward(entry, None, 1 + 3 * LAYERS)
    grads[0]["qkv"] = lax.dynamic_slice_in_dim(qkv_sum, x * (PAIR // 2), PAIR // 2, 0)
    vecs[0][0] = vec1

    def both_lanes(own, other):
        return jnp.where(x == 0, jnp.stack([own, other], axis=1), jnp.stack([other, own], axis=1))

    def stacked(name):
        return jnp.stack([grads[layer][name] for layer in range(LAYERS)])

    def vector(part, index, size):
        return jnp.stack([vecs[layer][part][index, :size] for layer in range(LAYERS)])

    def placed(part, index):
        return lax.dynamic_slice_in_dim(vector(part, index, width), me * (width // n), width // n, 1)

    out_own = lax.dynamic_slice_in_dim(streams[LAYERS], me * rows, rows, 0)
    return (
        both_lanes(out_own, out_other),
        both_lanes(dx_own, dx_other),
        placed(0, 1),
        placed(0, 2),
        stacked("qkv").reshape(LAYERS, width // n, 3, features),
        vector(0, 0, 3 * features).reshape(LAYERS, 3, features),
        stacked("out").transpose(0, 2, 1),
        placed(1, 4),
        placed(1, 2),
        placed(1, 3),
        stacked("up"),
        vector(1, 0, w_up.shape[2]),
        stacked("down").transpose(0, 2, 1),
        placed(1, 1),
    )


def lane_fits(mesh, tokens):
    n = mesh.shape["seq"]
    positions, lanes, width = tokens.shape
    rows = positions // n
    return (
        lanes == 2
        and n % 4 == 0
        and positions <= 4 * FRAME
        and positions % FRAME == 0
        and FRAME % rows == 0
        and width // n * 2 == PAIR
        and mesh.shape["tp"] == 2
    )


def solution(mesh):
    placed = (
        P("seq", None, None),
        P("seq", None, None),
        P(),
        P(),
        P(None, None, None, "tp"),
        P(None, None, "tp"),
        P(None, "tp", None),
        P(),
        P(),
        P(),
        P(None, None, "tp"),
        P(None, "tp"),
        P(None, "tp", None),
        P(),
        P(),
        P("seq", None),
    )
    def mapped(body):
        return jax.shard_map(
            body,
            mesh=mesh,
            in_specs=placed,
            out_specs=(
                P("seq", None, None),
                P("seq", None, None),
                P(None, "seq"),
                P(None, "seq"),
                P(None, "seq", None, "tp"),
                P(None, None, "tp"),
                P(None, "tp", "seq"),
                P(None, "seq"),
                P(None, "seq"),
                P(None, "seq"),
                P(None, "seq", "tp"),
                P(None, "tp"),
                P(None, "tp", "seq"),
                P(None, "seq"),
            ),
            check_vma=False,
        )

    def run(tokens, *others):
        if lane_fits(mesh, tokens):
            return mapped(per_chip)(tokens, *others)
        return mapped(per_device)(tokens, *others)

    return run
```

```python
import math

import jax
import jax.numpy as jnp
import numpy as np
from jax import lax
from jax.experimental import pallas as pl
from jax.experimental.pallas import tpu as pltpu
from jax.sharding import PartitionSpec as P

HEAD_DIM = 64
GRID = 16
FRAME = 256
LAYERS = 2
MICRO = 2


EPSILON = 1e-06
MASKED = -1e30
SCORE_SCALE = 0.125


def layer_norm(stream, norm_gain, norm_shift):
    center = stream - jnp.mean(stream, axis=-1, keepdims=True)
    spread = jnp.mean(center * center, axis=-1, keepdims=True)
    return center * lax.rsqrt(spread + EPSILON) * norm_gain + norm_shift


def rotate(values, frame_place, row_place, column_place):
    frequency = jnp.exp(jnp.arange(10, dtype=jnp.float32) * (-math.log(10000.0) / 10.0))
    pieces = []
    for section, place in enumerate((frame_place, row_place, column_place)):
        lower = values[..., 20 * section : 20 * section + 10]
        upper = values[..., 20 * section + 10 : 20 * section + 20]
        angles = place.astype(jnp.float32)[..., None, None] * frequency
        cosine = jnp.cos(angles)
        sine_part = jnp.sin(angles)
        pieces.append(lower * cosine - upper * sine_part)
        pieces.append(lower * sine_part + upper * cosine)
    pieces.append(values[..., 60:])
    return jnp.concatenate(pieces, axis=-1)


def episode_tags(frame_counts, positions):
    endings = jnp.cumsum(frame_counts) * FRAME
    passed = (positions[:, None] >= endings[None, :]).astype(jnp.int32)
    episode = jnp.sum(passed, axis=1)
    opening = jnp.sum(passed * frame_counts[None, :], axis=1)
    frame_index = positions // FRAME - opening
    within = positions % FRAME
    return (episode, frame_index, within // GRID, within % GRID)


def gelu_exact(values):
    return jax.nn.gelu(values, approximate=False)


def sum_heads(partial_sum):
    return lax.psum(partial_sum.astype(jnp.bfloat16), "tp").astype(jnp.float32)


def sum_inputs(partial_sum):
    return lax.psum(partial_sum.astype(jnp.bfloat16), "tp").astype(jnp.float32)


def lane_scores(query, keys_all, lane_index, query_tags, key_tags):
    head_count = query.shape[2] // HEAD_DIM
    query_lane = lax.dynamic_index_in_dim(query, lane_index, 1, False).reshape(
        query.shape[0], head_count, HEAD_DIM
    )
    keys_lane = lax.dynamic_index_in_dim(keys_all, lane_index, 1, False).reshape(
        keys_all.shape[0], head_count, HEAD_DIM
    )
    query_episode, query_frame = [
        lax.dynamic_index_in_dim(item, lane_index, 1, False) for item in query_tags
    ]
    key_episode, key_frame, key_live = [
        lax.dynamic_index_in_dim(item, lane_index, 1, False) for item in key_tags
    ]
    allowed = (
        (query_episode[:, None] == key_episode[None, :])
        & (key_frame[None, :] <= query_frame[:, None])
        & (key_live[None, :] > 0)
    )
    scores = (
        jnp.einsum("qhd,khd->hqk", query_lane, keys_lane, preferred_element_type=jnp.float32)
        * SCORE_SCALE
    )
    return (jnp.where(allowed[None], scores, MASKED), query_lane, keys_lane)


def attend_forward(query, keys_all, values_all, query_tags, key_tags):
    rows_dev, lane_count, features = query.shape
    head_count = features // HEAD_DIM

    def one_lane(lane_index, carry):
        scores, query_lane, keys_lane = lane_scores(
            query, keys_all, lane_index, query_tags, key_tags
        )
        highest = jnp.max(scores, axis=-1, keepdims=True)
        shifted = jnp.exp(scores - highest)
        summed = jnp.sum(shifted, axis=-1, keepdims=True)
        attention = (shifted / summed).astype(jnp.bfloat16)
        values_lane = lax.dynamic_index_in_dim(values_all, lane_index, 1, False).reshape(
            values_all.shape[0], head_count, HEAD_DIM
        )
        result = jnp.einsum(
            "hqk,khd->qhd", attention, values_lane, preferred_element_type=jnp.float32
        ).reshape(rows_dev, 1, features)
        log_total = (highest + jnp.log(summed))[None, :, :, 0]
        return (result, log_total)

    initial = (
        jnp.zeros((rows_dev, lane_count, features), jnp.float32),
        jnp.zeros((lane_count, head_count, rows_dev), jnp.float32),
    )
    return lax.fori_loop(0, lane_count, one_lane, initial)


def attend_backward(query, keys_all, values_all, log_total, grad_mixed, query_tags, key_tags):
    rows_dev, lane_count, features = query.shape
    head_count = features // HEAD_DIM
    key_rows = keys_all.shape[0]

    def one_lane(lane_index, carry):
        scores, query_lane, keys_lane = lane_scores(
            query, keys_all, lane_index, query_tags, key_tags
        )
        values_lane = lax.dynamic_index_in_dim(values_all, lane_index, 1, False).reshape(
            key_rows, head_count, HEAD_DIM
        )
        grad_lane = lax.dynamic_index_in_dim(grad_mixed, lane_index, 1, False).reshape(
            rows_dev, head_count, HEAD_DIM
        )
        attention = jnp.exp(
            scores - lax.dynamic_index_in_dim(log_total, lane_index, 0, False)[:, :, None]
        )
        grad_attention = jnp.einsum(
            "qhd,khd->hqk", grad_lane, values_lane, preferred_element_type=jnp.float32
        )
        inner = jnp.sum(attention * grad_attention, axis=-1, keepdims=True)
        grad_scores = (attention * (grad_attention - inner)).astype(jnp.bfloat16)
        query_part = (
            jnp.einsum("hqk,khd->qhd", grad_scores, keys_lane, preferred_element_type=jnp.float32)
            * SCORE_SCALE
        )
        key_part = (
            jnp.einsum("hqk,qhd->khd", grad_scores, query_lane, preferred_element_type=jnp.float32)
            * SCORE_SCALE
        )
        value_part = jnp.einsum(
            "hqk,qhd->khd",
            attention.astype(jnp.bfloat16),
            grad_lane,
            preferred_element_type=jnp.float32,
        )
        stacked = jnp.stack(
            [key_part.reshape(key_rows, features), value_part.reshape(key_rows, features)], axis=1
        )
        key_terms = stacked[:, None]
        grad_query = query_part.reshape(rows_dev, 1, features)
        return (grad_query, key_terms)

    initial = (
        jnp.zeros((rows_dev, lane_count, features), jnp.float32),
        jnp.zeros((key_rows, lane_count, 2, features), jnp.float32),
    )
    return lax.fori_loop(0, lane_count, one_lane, initial)


def front(stream, layer_index, params, query_tags, key_tags, positions):
    (
        gain_one,
        shift_one,
        mat_qkv,
        bias_qkv,
        mat_out,
        bias_out,
        gain_two,
        shift_two,
        mat_up,
        bias_up,
        mat_down,
        bias_down,
    ) = [item[layer_index] for item in params]
    rows_dev, lane_count, width = stream.shape
    features = mat_qkv.shape[2]
    head_count = features // HEAD_DIM
    frame_place, row_place, column_place = positions
    first = layer_norm(stream, gain_one, shift_one).astype(jnp.bfloat16)
    projected = (
        jnp.einsum("tbd,dcf->tbcf", first, mat_qkv, preferred_element_type=jnp.float32) + bias_qkv
    )
    split = projected.reshape(rows_dev, lane_count, 3, head_count, HEAD_DIM)
    query = (
        rotate(split[:, :, 0], frame_place, row_place, column_place)
        .reshape(rows_dev, lane_count, features)
        .astype(jnp.bfloat16)
    )
    keys = (
        rotate(split[:, :, 1], frame_place, row_place, column_place)
        .reshape(rows_dev, lane_count, features)
        .astype(jnp.bfloat16)
    )
    values = projected[:, :, 2].astype(jnp.bfloat16)
    keys_all, values_all = (
        lax.all_gather(keys, "seq", axis=0, tiled=True),
        lax.all_gather(values, "seq", axis=0, tiled=True),
    )
    mixed_full, log_total = attend_forward(query, keys_all, values_all, query_tags, key_tags)
    mixed = mixed_full.astype(jnp.bfloat16)
    middle = (
        stream
        + sum_heads(jnp.einsum("tbf,fd->tbd", mixed, mat_out, preferred_element_type=jnp.float32))
        + bias_out
    )
    second = layer_norm(middle, gain_two, shift_two).astype(jnp.bfloat16)
    hidden = jnp.einsum("tbd,df->tbf", second, mat_up, preferred_element_type=jnp.float32) + bias_up
    activation = gelu_exact(hidden).astype(jnp.bfloat16)
    return (
        first,
        query,
        keys_all,
        values_all,
        log_total,
        mixed,
        middle,
        second,
        hidden,
        activation,
        mixed_full,
    )


def layer_backward(stream, gradient, layer_index, params, query_tags, key_tags, positions):
    (
        gain_one,
        shift_one,
        mat_qkv,
        bias_qkv,
        mat_out,
        bias_out,
        gain_two,
        shift_two,
        mat_up,
        bias_up,
        mat_down,
        bias_down,
    ) = [item[layer_index] for item in params]
    (
        first,
        query,
        keys_all,
        values_all,
        log_total,
        mixed,
        middle,
        second,
        hidden,
        activation,
        mixed_full,
    ) = front(stream, layer_index, params, query_tags, key_tags, positions)
    frame_place, row_place, column_place = positions
    rows_dev, lane_count, width = stream.shape
    features = query.shape[2]
    head_count = features // HEAD_DIM
    grad_low = gradient.astype(jnp.bfloat16)
    grad_w_down = jnp.einsum(
        "tbf,tbd->fd", activation, grad_low, preferred_element_type=jnp.float32
    )
    grad_b_down = jnp.sum(gradient, axis=(0, 1))
    grad_activation = jnp.einsum(
        "tbd,fd->tbf", grad_low, mat_down, preferred_element_type=jnp.float32
    )
    grad_hidden = jax.vjp(gelu_exact, hidden)[1](grad_activation)[0].astype(jnp.bfloat16)
    grad_b_up = jnp.sum(grad_hidden.astype(jnp.float32), axis=(0, 1))
    grad_w_up = jnp.einsum("tbd,tbf->df", second, grad_hidden, preferred_element_type=jnp.float32)
    grad_second = sum_inputs(
        jnp.einsum("tbf,df->tbd", grad_hidden, mat_up, preferred_element_type=jnp.float32)
    )
    middle_pull = jax.vjp(layer_norm, middle, gain_two, shift_two)[1]
    grad_inner, grad_gain_two, grad_shift_two = middle_pull(grad_second)
    grad_middle = gradient + grad_inner
    grad_b_out = jnp.sum(grad_middle, axis=(0, 1))
    middle_low = grad_middle.astype(jnp.bfloat16)
    grad_w_out = jnp.einsum("tbf,tbd->fd", mixed, middle_low, preferred_element_type=jnp.float32)
    grad_mixed = jnp.einsum(
        "tbd,fd->tbf", middle_low, mat_out, preferred_element_type=jnp.float32
    ).astype(jnp.bfloat16)
    grad_query, key_terms = attend_backward(
        query, keys_all, values_all, log_total, grad_mixed, query_tags, key_tags
    )
    returned = lax.psum_scatter(key_terms, "seq", scatter_dimension=0, tiled=True)
    turned_query = rotate(
        grad_query.reshape(rows_dev, lane_count, head_count, HEAD_DIM),
        -frame_place,
        -row_place,
        -column_place,
    )
    turned_keys = rotate(
        returned[:, :, 0].reshape(rows_dev, lane_count, head_count, HEAD_DIM),
        -frame_place,
        -row_place,
        -column_place,
    )
    grad_projected = jnp.stack(
        [
            turned_query.reshape(rows_dev, lane_count, features),
            turned_keys.reshape(rows_dev, lane_count, features),
            returned[:, :, 1],
        ],
        axis=2,
    ).astype(jnp.bfloat16)
    grad_b_qkv = jnp.sum(grad_projected.astype(jnp.float32), axis=(0, 1))
    grad_w_qkv = jnp.einsum(
        "tbd,tbcf->dcf", first, grad_projected, preferred_element_type=jnp.float32
    )
    grad_first = sum_inputs(
        jnp.einsum("tbcf,dcf->tbd", grad_projected, mat_qkv, preferred_element_type=jnp.float32)
    )
    first_pull = jax.vjp(layer_norm, stream, gain_one, shift_one)[1]
    grad_entry, grad_gain_one, grad_shift_one = first_pull(grad_first)
    grads = (
        grad_gain_one,
        grad_shift_one,
        grad_w_qkv,
        grad_b_qkv,
        grad_w_out,
        grad_b_out,
        grad_gain_two,
        grad_shift_two,
        grad_w_up,
        grad_b_up,
        grad_w_down,
        grad_b_down,
    )
    return (grad_middle + grad_entry, grads)


def per_device(
    tokens,
    d_out,
    norm1_gain,
    norm1_shift,
    w_qkv,
    b_qkv,
    w_out,
    b_out,
    norm2_gain,
    norm2_shift,
    w_up,
    b_up,
    w_down,
    b_down,
    episode_frames,
    live,
):
    rows_dev = tokens.shape[0]
    lane_count = tokens.shape[1] // MICRO
    total_rows = rows_dev * lax.axis_size("seq")
    local_positions = lax.axis_index("seq") * rows_dev + jnp.arange(rows_dev, dtype=jnp.int32)
    key_positions = jnp.arange(total_rows, dtype=jnp.int32)
    tagger = jax.vmap(episode_tags, in_axes=(0, None), out_axes=1)
    query_episode, query_frame, query_row, query_column = tagger(episode_frames, local_positions)
    key_episode, key_frame, key_row, key_column = tagger(episode_frames, key_positions)
    live_keys = lax.all_gather(live, "seq", axis=0, tiled=True)
    params = (
        norm1_gain,
        norm1_shift,
        w_qkv,
        b_qkv,
        w_out,
        b_out,
        norm2_gain,
        norm2_shift,
        w_up,
        b_up,
        w_down,
        b_down,
    )
    layer_grads = [None] * LAYERS
    outputs = []
    grad_tokens = []
    for micro_index in range(MICRO):
        first_lane = micro_index * lane_count
        last_lane = first_lane + lane_count
        query_tags = (query_episode[:, first_lane:last_lane], query_frame[:, first_lane:last_lane])
        key_tags = (
            key_episode[:, first_lane:last_lane],
            key_frame[:, first_lane:last_lane],
            live_keys[:, first_lane:last_lane],
        )
        positions = (
            query_frame[:, first_lane:last_lane],
            query_row[:, first_lane:last_lane],
            query_column[:, first_lane:last_lane],
        )
        stream = tokens[:, first_lane:last_lane].astype(jnp.float32)
        inputs = []
        gathered = []
        for layer_index in range(LAYERS):
            inputs.append(stream)
            layer_state = front(stream, layer_index, params, query_tags, key_tags, positions)
            gathered.append((layer_state[2], layer_state[3]))
            branch = jnp.einsum(
                "tbf,fd->tbd",
                layer_state[9],
                w_down[layer_index],
                preferred_element_type=jnp.float32,
            )
            stream = layer_state[6] + sum_heads(branch) + b_down[layer_index]
        outputs.append(stream)
        gradient = d_out[:, first_lane:last_lane]
        for layer_index in reversed(range(LAYERS)):
            gradient, grads = layer_backward(
                inputs[layer_index], gradient, layer_index, params, query_tags, key_tags, positions
            )
            if layer_grads[layer_index] is None:
                layer_grads[layer_index] = grads
            else:
                layer_grads[layer_index] = jax.tree.map(jnp.add, layer_grads[layer_index], grads)
        grad_tokens.append(gradient)
    stacked = [
        jnp.stack([layer_grads[layer_index][entry] for layer_index in range(LAYERS)])
        for entry in range(12)
    ]
    (
        grad_gain_one,
        grad_shift_one,
        grad_w_qkv,
        grad_b_qkv,
        grad_w_out,
        grad_b_out,
        grad_gain_two,
        grad_shift_two,
        grad_w_up,
        grad_b_up,
        grad_w_down,
        grad_b_down,
    ) = stacked
    in_sums = (
        lax.psum_scatter(grad_w_qkv, "seq", scatter_dimension=1, tiled=True),
        lax.psum_scatter(grad_w_up, "seq", scatter_dimension=1, tiled=True),
        lax.psum_scatter(grad_gain_one, "seq", scatter_dimension=1, tiled=True),
        lax.psum_scatter(grad_shift_one, "seq", scatter_dimension=1, tiled=True),
        lax.psum_scatter(grad_gain_two, "seq", scatter_dimension=1, tiled=True),
        lax.psum_scatter(grad_shift_two, "seq", scatter_dimension=1, tiled=True),
        lax.psum_scatter(grad_b_out, "seq", scatter_dimension=1, tiled=True),
        lax.psum_scatter(grad_b_down, "seq", scatter_dimension=1, tiled=True),
    )
    out_sums = (
        lax.psum_scatter(grad_w_out, "seq", scatter_dimension=2, tiled=True),
        lax.psum_scatter(grad_w_down, "seq", scatter_dimension=2, tiled=True),
    )
    bias_total = lax.psum((grad_b_qkv, grad_b_up), "seq")
    return (
        jnp.concatenate(outputs, axis=1),
        jnp.concatenate(grad_tokens, axis=1),
        in_sums[2],
        in_sums[3],
        in_sums[0],
        bias_total[0],
        out_sums[0],
        in_sums[6],
        in_sums[4],
        in_sums[5],
        in_sums[1],
        bias_total[1],
        out_sums[1],
        in_sums[7],
    )


MESH = pl.DeviceIdType.MESH
BF16 = jnp.bfloat16
F32 = jnp.float32
VMEM_BYTES = 60 * 1024 * 1024
PAIR = 128
VEC = 2048


def nn(left, right):
    return lax.dot_general(left, right, (((1,), (0,)), ((), ())), preferred_element_type=F32)


def nt(left, right):
    return lax.dot_general(left, right, (((1,), (1,)), ((), ())), preferred_element_type=F32)


def tn(left, right):
    return lax.dot_general(left, right, (((0,), (0,)), ((), ())), preferred_element_type=F32)


def at(start, size):
    return pl.ds(pl.multiple_of(start, size), size)


def remote(src, dst, send, recv, seq, tp):
    return pltpu.make_async_remote_copy(
        src_ref=src,
        dst_ref=dst,
        send_sem=send,
        recv_sem=recv,
        device_id=(seq, tp),
        device_id_type=MESH,
    )


def greet(partners):
    barrier = pltpu.get_barrier_semaphore()
    for seq, tp in partners:
        pl.semaphore_signal(barrier, inc=1, device_id=(seq, tp), device_id_type=MESH)
    pl.semaphore_wait(barrier, len(partners))


def whole(array):
    zeros = (0,) * array.ndim
    return pl.BlockSpec(array.shape, lambda s: zeros, pipeline_mode=pl.Buffered(1))


def whole_out(shape):
    zeros = (0,) * len(shape)
    return pl.BlockSpec(shape, lambda s: zeros)


ANYWHERE = pl.BlockSpec(memory_space=pl.ANY)


def turn_row(table, place, section):
    frequency = np.exp(np.arange(10, dtype=np.float32) * np.float32(-math.log(10000.0) / 10.0))
    angle = place.astype(np.float32)[:, None] * frequency
    for base in range(20 * section, PAIR, HEAD_DIM):
        table[0, :, base : base + 10] = np.cos(angle)
        table[0, :, base + 10 : base + 20] = np.cos(angle)
        table[1, :, base : base + 10] = -np.sin(angle)
        table[2, :, base + 10 : base + 20] = np.sin(angle)


def turn_constants(frames):
    within, ahead = np.zeros((3, FRAME, PAIR), np.float32), np.zeros((3, frames, PAIR), np.float32)
    turn_row(within, np.arange(FRAME) // GRID, 1)
    turn_row(within, np.arange(FRAME) % GRID, 2)
    for base in range(60, PAIR, HEAD_DIM):
        within[0, :, base : base + 4] = 1.0
    turn_row(ahead, np.arange(frames), 0)
    return jnp.asarray(within), jnp.asarray(ahead)


def turn(values, tables, back=False):
    cosine, lower, upper = tables
    pieces = []
    for start in range(0, values.shape[1], PAIR):
        slab = values[:, start : start + PAIR]
        moved = pltpu.roll(slab, PAIR - 10, 1) * lower + pltpu.roll(slab, 10, 1) * upper
        pieces.append(slab * cosine - moved if back else slab * cosine + moved)
    return jnp.concatenate(pieces, axis=1)


def tables_of(fixed_ref, frames_ref, chunk):
    return [fixed_ref[i] + frames_ref[i, pl.ds(chunk, 1), :] for i in range(3)]


def normed(stream):
    center = stream - jnp.mean(stream, axis=-1, keepdims=True)
    spread = jnp.mean(center * center, axis=-1, keepdims=True)
    scale = lax.rsqrt(spread + EPSILON)
    return center * scale, scale


def norm_pull(grad, gain, unit, scale):
    scaled = grad * gain
    return scale * (
        scaled
        - jnp.mean(scaled, axis=-1, keepdims=True)
        - unit * jnp.mean(scaled * unit, axis=-1, keepdims=True)
    )


def column_sum(values):
    return jnp.sum(values, axis=0, keepdims=True)


def gelu_both(hidden):
    normal = 0.5 + 0.5 * lax.erf(hidden * math.sqrt(0.5))
    density = jnp.exp(hidden * hidden * -0.5) * (1.0 / math.sqrt(2.0 * math.pi))
    return hidden * normal, normal + hidden * density


def project(stream, chunk, layer, pair, refs, outs, first_full):
    gain, shift, weight, bias, fixed, frames = refs
    query_ref, key_ref, value_ref, first_ref = outs
    unit, _ = normed(stream)
    first = (unit * gain[layer : layer + 1, :] + shift[layer : layer + 1, :]).astype(BF16)
    first_full[...] = first
    first_ref[...] = first_full[:, at(pair * PAIR, PAIR)]
    tables = tables_of(fixed, frames, chunk)
    query = nn(first, weight[0]) + bias[layer, 0:1, :]
    query_ref[...] = (turn(query, tables) * SCORE_SCALE).astype(BF16)
    key = nn(first, weight[1]) + bias[layer, 1:2, :]
    key_ref[...] = turn(key, tables).astype(BF16)
    value = nn(first, weight[2]) + bias[layer, 2:3, :]
    value_ref[...] = value.astype(BF16)


class Relay:
    sems = 9

    def __init__(self, n, rows, buffer, other, sems, lives=None, live_other=None):
        self.n, self.rows, self.buffer, self.other = n, rows, buffer, other
        self.lives, self.live_other = lives, live_other
        (
            self.x_send,
            self.x_recv,
            self.up_send,
            self.down_send,
            self.z_recv,
            self.y_send,
            self.y_recv,
            self.c_send,
            self.c_recv,
        ) = sems
        self.planes = n // 4
        self.me, self.core = lax.axis_index("seq"), lax.axis_index("tp")
        me = self.me
        self.x, self.y, self.z = lax.rem(me, 2), lax.rem(me // 2, 2), me // 4
        self.beside, self.across = me + 1 - 2 * self.x, me + 2 - 4 * self.y

    @staticmethod
    def scratch(n):
        dma, planes = pltpu.SemaphoreType.DMA, n // 4
        shapes = [(2,), (2,)] + [(planes, 2)] * 5 + [(2 * planes,)] * 2
        return [dma(shape) for shape in shapes]

    def hello(self):
        barrier = pltpu.get_barrier_semaphore()
        me, core = self.me, self.core
        for seq, tp in ((self.beside, core), (self.across, core), (me, 1 - core)):
            pl.semaphore_signal(barrier, inc=1, device_id=(seq, tp), device_id_type=MESH)

        @pl.when(self.z > 0)
        def _():
            pl.semaphore_signal(barrier, inc=1, device_id=(me - 4, core), device_id_type=MESH)

        @pl.when(self.z < self.planes - 1)
        def _():
            pl.semaphore_signal(barrier, inc=1, device_id=(me + 4, core), device_id_type=MESH)

    def met(self):
        inner = (self.z > 0).astype(jnp.int32) + (self.z < self.planes - 1).astype(jnp.int32)
        pl.semaphore_wait(pltpu.get_barrier_semaphore(), 3 + inner)

    def block(self, side, pair):
        return self.buffer.at[side, at(pair * 2 * self.rows, 2 * self.rows), :]

    def items(self, pair):
        found = [self.block(self.core, pair)]
        if self.lives is not None:
            found.append(self.lives.at[at(pair * 2, 2)])
        return found

    def each(self, copy, what):
        for index in range(1 if self.lives is None else 2):
            getattr(copy(index), what)()

    def x_copy(self, index):
        if index == 0:
            source = self.other.at[self.core]
            target = self.buffer.at[self.core, at(self.me * self.rows, self.rows), :]
        else:
            source, target = self.live_other, self.lives.at[self.me]
        return remote(
            source, target, self.x_send.at[index], self.x_recv.at[index], self.beside, self.core
        )

    def z_copy(self, plane, step):
        sends = self.up_send if step > 0 else self.down_send

        def copy(index):
            item = self.items(plane * 2 + self.y)[index]
            return remote(
                item,
                item,
                sends.at[plane, index],
                self.z_recv.at[plane, index],
                self.me + step,
                self.core,
            )

        return copy

    def y_copy(self, plane, row):
        def copy(index):
            item = self.items(plane * 2 + row)[index]
            return remote(
                item,
                item,
                self.y_send.at[plane, index],
                self.y_recv.at[plane, index],
                self.across,
                self.core,
            )

        return copy

    def c_copy(self, pair, side):
        item = self.block(side, pair)
        return remote(
            item, item, self.c_send.at[pair], self.c_recv.at[pair], self.me, 1 - self.core
        )

    def pass_on(self, plane, up, down):
        @pl.when(up)
        def _():
            self.each(self.z_copy(plane, 4), "start")

        @pl.when(down)
        def _():
            self.each(self.z_copy(plane, -4), "start")

        self.each(self.y_copy(plane, self.y), "start")
        self.c_copy(plane * 2 + self.y, self.core).start()

    def begin(self):
        self.each(self.x_copy, "start")

    def place(self, event):
        away = (event + 1) // 2
        below = lax.rem(event, 2) == 1
        plane = jnp.where(below, self.z - away, self.z + away)
        return plane, below, (plane >= 0) & (plane < self.planes)

    def arrive(self, event):
        plane, below, valid = self.place(event)

        @pl.when(event == 0)
        def _():
            self.each(self.x_copy, "wait_recv")
            self.pass_on(self.z, self.z < self.planes - 1, self.z > 0)

        @pl.when(valid & (event > 0))
        def _():
            self.each(self.z_copy(plane, 4), "wait_recv")
            self.pass_on(plane, below & (self.z < self.planes - 1), (~below) & (self.z > 0))

    def complete(self, event, then=None):
        plane, _, valid = self.place(event)

        @pl.when(valid)
        def _():
            self.each(self.y_copy(plane, 1 - self.y), "wait_recv")
            self.c_copy(plane * 2 + 1 - self.y, self.core).start()
            self.c_copy(plane * 2, 1 - self.core).wait_recv()
            self.c_copy(plane * 2 + 1, 1 - self.core).wait_recv()
            if then is not None:
                then(plane)

    def finish(self):
        self.each(self.x_copy, "wait_send")
        z, planes = self.z, self.planes
        for plane in range(planes):

            @pl.when((plane <= z) & (z < planes - 1))
            def _():
                self.each(self.z_copy(plane, 4), "wait_send")

            @pl.when((plane >= z) & (z > 0))
            def _():
                self.each(self.z_copy(plane, -4), "wait_send")

            self.each(self.y_copy(plane, self.y), "wait_send")
        for pair in range(2 * planes):
            self.c_copy(pair, self.core).wait_send()

    @property
    def events(self):
        return 2 * self.planes - 1


def split_lanes(values, x, buffer, other, start, rows):
    half = values.shape[2] // 2
    zero, one = values[:, 0, :], values[:, 1, :]
    own, far = jnp.where(x == 0, zero, one), jnp.where(x == 0, one, zero)
    core = lax.axis_index("tp")
    own = jnp.where(core == 0, own[:, :half], own[:, half:]).astype(BF16)
    buffer[core, at(start, rows), :] = own
    for side in range(2):
        other[side] = far[:, side * half : (side + 1) * half].astype(BF16)


def gather_and_project(tokens, live, episode_frames, gain, shift, qkv, bias, fixed, ahead, n):
    rows, lanes, width = tokens.shape
    half = width // 2
    total = n * rows
    chunks = total // FRAME
    per_frame = FRAME // rows
    features = qkv.shape[3]
    slots = episode_frames.shape[1]

    def kernel(*refs):
        refs = list(refs)

        def take(count):
            taken = refs[:count]
            del refs[:count]
            return taken

        tokens_ref, live_ref, counts_ref, gain_ref, shift_ref, w_any, bias_ref = take(7)
        fixed_ref, ahead_ref = take(2)
        all_ref, mask_ref, frames_ref, q_ref, k_ref, v_ref, first_ref = take(7)
        other, lives, live_other, weight, full, w_sem = take(6)
        relay = Relay(n, rows, all_ref, other, take(Relay.sems), lives, live_other)
        load = pltpu.make_async_copy(w_any.at[0], weight, w_sem)
        load.start()
        relay.hello()
        x, me = relay.x, relay.me
        split_lanes(tokens_ref[...].astype(F32), x, all_ref, other, me * rows, rows)
        lane = lax.broadcasted_iota(jnp.int32, (rows, FRAME), 1)
        row = lax.broadcasted_iota(jnp.int32, (rows, FRAME), 0)
        here = lane == row + lax.rem(me, per_frame) * rows
        tiles = []
        for index in range(lanes):
            alive = jnp.where(here, live_ref[:, index : index + 1].astype(F32), 0.0)
            tiles.append(jnp.broadcast_to(column_sum(alive), (8, FRAME)))
        lives[me] = jnp.where(x == 0, tiles[0], tiles[1])
        live_other[...] = jnp.where(x == 0, tiles[1], tiles[0])
        relay.met()
        relay.begin()

        counts = [counts_ref[x, slot] for slot in range(slots)]
        episodes, openings = [], []
        for frame in range(chunks):
            end, episode, opening = 0, 0, 0
            for slot in range(slots):
                end = end + counts[slot]
                passed = frame >= end
                episode = episode + passed.astype(jnp.int32)
                opening = opening + jnp.where(passed, counts[slot], 0)
            episodes.append(episode)
            openings.append(frame - opening)
        for index in range(3):
            table = []
            for frame in range(chunks):
                line = jnp.zeros((1, PAIR), F32)
                for choice in range(chunks):
                    line = jnp.where(
                        openings[frame] == choice, ahead_ref[index, choice : choice + 1, :], line
                    )
                table.append(line)
            frames_ref[index] = jnp.concatenate(
                table + [jnp.zeros((8 - chunks, PAIR), F32)], axis=0
            )
        load.wait()

        def project_frame(frame):
            place = at(frame * FRAME, FRAME)
            stream = jnp.concatenate([all_ref[0, place, :], all_ref[1, place, :]], axis=1)
            project(
                stream.astype(F32),
                frame,
                0,
                me // 2,
                (gain_ref, shift_ref, weight, bias_ref, fixed_ref, frames_ref),
                [ref.at[place, :] for ref in (q_ref, k_ref, v_ref, first_ref)],
                full,
            )

        def one_event(event, carry):
            @pl.when(event < relay.events)
            def _():
                relay.arrive(event)

            @pl.when(event > 0)
            def _():
                relay.complete(event - 1, project_frame)

            return carry

        lax.fori_loop(0, relay.events + 1, one_event, 0)
        relay.finish()

        for key_frame in range(chunks):
            alive = lives[key_frame * per_frame, 0:1, :]
            for part in range(1, per_frame):
                alive = alive + lives[key_frame * per_frame + part, 0:1, :]
            closed = (alive - 1.0) * -MASKED
            for query_frame in range(chunks):
                allowed = (episodes[query_frame] == episodes[key_frame]) & (
                    openings[key_frame] <= openings[query_frame]
                )
                mask_ref[
                    query_frame : query_frame + 1, key_frame * FRAME : (key_frame + 1) * FRAME
                ] = jnp.where(allowed, closed, MASKED)

    in_vmem = pl.BlockSpec(memory_space=pltpu.VMEM)
    in_smem = pl.BlockSpec(memory_space=pltpu.SMEM)
    projected = jax.ShapeDtypeStruct((total, features), BF16)
    return pl.pallas_call(
        kernel,
        out_shape=(
            jax.ShapeDtypeStruct((2, total, half), BF16),
            jax.ShapeDtypeStruct((8, total), F32),
            jax.ShapeDtypeStruct((3, 8, PAIR), F32),
            projected,
            projected,
            projected,
            jax.ShapeDtypeStruct((total, PAIR), BF16),
        ),
        in_specs=[in_vmem, in_vmem, in_smem, in_vmem, in_vmem, ANYWHERE] + [in_vmem] * 3,
        out_specs=(in_vmem,) * 7,
        scratch_shapes=[
            pltpu.VMEM((2, rows, half), BF16),
            pltpu.VMEM((n, 8, FRAME), F32),
            pltpu.VMEM((8, FRAME), F32),
            pltpu.VMEM(qkv.shape[1:], BF16),
            pltpu.VMEM((FRAME, width), BF16),
            pltpu.SemaphoreType.DMA,
        ]
        + Relay.scratch(n),
        compiler_params=pltpu.CompilerParams(
            collective_id=0, has_side_effects=True, vmem_limit_bytes=VMEM_BYTES
        ),
        name="gather_and_project",
    )(tokens, live, episode_frames, gain, shift, qkv, bias, fixed, ahead)


def halves(ref):
    return jnp.concatenate([ref[0], ref[1]], axis=1).astype(F32)


def halves_spec(shape, chunks, behind):
    return pl.BlockSpec(
        (2, FRAME, shape[2]), lambda s: (0, jnp.clip(s - behind, 0, chunks - 1), 0)
    )


def layer_forward(layer, query, key, value, key_bias, stream, mats, rows_of, next_refs, d_out, n, identity):
    total, features = query.shape
    split = stream.ndim == 3
    width = mats[1].shape[1]
    rows_here = total // n
    hidden_units = mats[1].shape[2]
    chunks = total // FRAME
    heads = features // HEAD_DIM
    slabs = features // PAIR
    columns = 512
    last = next_refs is None
    b_out, gain, shift, b_up, b_down = rows_of
    mat_out, mat_up, mat_down = mats

    def kernel(*refs):
        refs = list(refs)

        def take(count):
            taken = refs[:count]
            del refs[:count]
            return taken

        q_ref, k_ref, v_ref, kb_ref, x_ref = take(5)
        wo_any, wu_any, wd_any = take(3)
        bo_ref, gain_ref, shift_ref, bu_ref, bd_ref = take(5)
        if not last:
            wq_any, ngain, nshift, nbias, fixed, frames = take(6)
        if d_out is not None:
            (d_ref,) = take(1)
        p_ref, mixed_ref, middle_ref, second_ref, act_ref, gp_ref, x_out = take(7)
        if not last:
            nq_ref, nk_ref, nv_ref, nf_ref = take(4)
        if d_out is not None:
            (d_all,) = take(1)
        wo, wu, wd, mid, full, low = take(6)
        if not last:
            (wq,) = take(1)
        a_send, a_recv, b_send, b_recv, w_sem, send_sem, recv_sem = take(7)
        relay = None
        if d_out is not None:
            buffer, other, d_sem = take(3)
            relay = Relay(n, rows_here, buffer, other, take(Relay.sems))

        step = pl.program_id(0)
        me, core = lax.axis_index("seq"), lax.axis_index("tp")

        items = [(wo_any, wo), (wu_any, wu), (wd_any, wd)]
        if not last:
            items.append((wq_any, wq))

        def load(index):
            source, target = items[index]
            return pltpu.make_async_copy(
                source.at[layer if index < 3 else layer + 1], target, w_sem.at[index]
            )

        def exchange(kind, chunk):
            source, target = ((a_send, a_recv), (b_send, b_recv))[kind]
            return remote(
                source.at[chunk],
                target.at[chunk],
                send_sem.at[kind, chunk],
                recv_sem.at[kind, chunk],
                me,
                1 - core,
            )

        @pl.when(step == 0)
        def _():
            for index in range(len(items)):
                load(index).start()
            if relay is None:
                greet([(me, 1 - core)])
            else:
                relay.hello()
                split_lanes(d_ref[...], relay.x, buffer, other, me * rows_here, rows_here)
                relay.met()
                relay.begin()

        if relay is not None:
            for event in range(relay.events):

                @pl.when(step == 1 + event // 2)
                def _():
                    relay.arrive(jnp.int32(event))

                @pl.when(step == 2 + event // 2)
                def _():
                    relay.complete(jnp.int32(event))

            @pl.when(step == chunks + 1)
            def _():
                relay.finish()
                pltpu.make_async_copy(buffer, d_all, d_sem).start()

        lane = lax.broadcasted_iota(jnp.int32, (1, PAIR), 1)
        sides = [(lane < HEAD_DIM).astype(F32).astype(BF16), (lane >= HEAD_DIM).astype(F32).astype(BF16)]
        for frame in range(chunks):

            @pl.when(step == frame)
            def _():
                keys = FRAME * (frame + 1)
                bias = kb_ref[frame : frame + 1, :keys]

                def one_slab(slab, carry):
                    lanes = at(slab * PAIR, PAIR)
                    q2, k2, v2 = q_ref[:, lanes], k_ref[:keys, lanes], v_ref[:keys, lanes]
                    results = []
                    for side in range(2):
                        scores = nt(q2 * sides[side], k2) + bias
                        highest = jnp.max(scores, axis=-1, keepdims=True)
                        shifted = jnp.exp(scores - highest)
                        summed = jnp.sum(shifted, axis=-1, keepdims=True)
                        attention = (shifted * (1.0 / summed)).astype(BF16)
                        p_ref[0, slab * 2 + side, :, :keys] = attention
                        results.append(nn(attention, v2))
                    mixed = jnp.where(lane < HEAD_DIM, results[0], results[1])
                    mixed_ref[:, lanes] = mixed.astype(BF16)
                    return carry

                lax.fori_loop(0, slabs, one_slab, 0)

        @pl.when(step == 0)
        def _():
            load(0).wait()

        @pl.when(step < chunks)
        def _():
            a_send[step] = nn(mixed_ref[...], wo[...]).astype(BF16)
            exchange(0, step).start()

        @pl.when(step == 1)
        def _():
            load(1).wait()
            load(2).wait()

        @pl.when((step >= 1) & (step <= chunks))
        def _():
            chunk = step - 1
            exchange(0, chunk).wait_recv()
            middle = (halves(x_ref) if split else x_ref[...]) + (a_send[chunk].astype(F32) + a_recv[chunk].astype(F32))
            middle = middle + bo_ref[layer : layer + 1, :]
            middle_ref[...] = middle
            mid[lax.rem(chunk, 2)] = middle
            unit, _ = normed(middle)
            second = (unit * gain_ref[layer : layer + 1, :] + shift_ref[layer : layer + 1, :]).astype(BF16)
            full[...] = second
            second_ref[...] = full[:, at((me // 2) * PAIR, PAIR)]
            for start in range(0, hidden_units, columns):
                part = slice(start, start + columns)
                hidden = nn(second, wu[:, part]) + bu_ref[layer : layer + 1, part]
                act, slope = gelu_both(hidden)
                act = act.astype(BF16)
                act_ref[:, part] = act
                gp_ref[:, part] = slope.astype(BF16)
                down = nn(act, wd[part, :])
                if start == 0:
                    low[...] = down
                else:
                    low[...] += down
            b_send[chunk] = low[...].astype(BF16)
            exchange(1, chunk).start()

        if not last:

            @pl.when(step == 2)
            def _():
                load(3).wait()

        @pl.when(step >= 2)
        def _():
            chunk = step - 2
            exchange(1, chunk).wait_recv()
            result = (
                mid[lax.rem(chunk, 2)]
                + (b_send[chunk].astype(F32) + b_recv[chunk].astype(F32))
                + bd_ref[layer : layer + 1, :]
            )
            x_out[...] = result
            if not last:
                project(
                    result,
                    chunk,
                    layer + 1,
                    me // 2,
                    (ngain, nshift, wq, nbias, fixed, frames),
                    (nq_ref, nk_ref, nv_ref, nf_ref),
                    full,
                )

        @pl.when(step == chunks + 1)
        def _():
            for kind in range(2):
                for chunk in range(chunks):
                    exchange(kind, chunk).wait_send()
            if relay is not None:
                pltpu.make_async_copy(buffer, d_all, d_sem).wait()

    def rows(columns, behind):
        return pl.BlockSpec(
            (FRAME, columns), lambda s: (jnp.clip(s - behind, 0, chunks - 1), 0)
        )

    in_specs = [rows(features, 0), whole(key), whole(value), whole(key_bias)]
    in_specs += [halves_spec(stream.shape, chunks, 1) if split else rows(width, 1)]
    in_specs += [ANYWHERE] * 3 + [whole(item) for item in rows_of]
    operands = [query, key, value, key_bias, stream, *mats, *rows_of]
    if not last:
        in_specs += [ANYWHERE] + [whole(item) for item in next_refs[1:]]
        operands += list(next_refs)
    if d_out is not None:
        in_specs += [whole(d_out)]
        operands += [d_out]
    out_shape = [
        jax.ShapeDtypeStruct((chunks, heads, FRAME, total), BF16),
        jax.ShapeDtypeStruct((total, features), BF16),
        jax.ShapeDtypeStruct((total, width), F32),
        jax.ShapeDtypeStruct((total, PAIR), BF16),
        jax.ShapeDtypeStruct((total, hidden_units), BF16),
        jax.ShapeDtypeStruct((total, hidden_units), BF16),
        jax.ShapeDtypeStruct((total, width), F32),
    ]
    out_specs = [
        pl.BlockSpec((1, heads, FRAME, total), lambda s: (jnp.minimum(s, chunks - 1), 0, 0, 0)),
        rows(features, 0),
        rows(width, 1),
        rows(PAIR, 1),
        rows(hidden_units, 1),
        rows(hidden_units, 1),
        rows(width, 2),
    ]
    scratch = [
        pltpu.VMEM(mat_out.shape[1:], BF16),
        pltpu.VMEM(mat_up.shape[1:], BF16),
        pltpu.VMEM(mat_down.shape[1:], BF16),
        pltpu.VMEM((2, FRAME, width), F32),
        pltpu.VMEM((FRAME, width), BF16),
        pltpu.VMEM((FRAME, width), F32),
    ]
    if not last:
        out_shape += [jax.ShapeDtypeStruct((total, features), BF16)] * 3
        out_shape += [jax.ShapeDtypeStruct((total, PAIR), BF16)]
        out_specs += [rows(features, 2)] * 3 + [rows(PAIR, 2)]
    if d_out is not None:
        out_shape += [jax.ShapeDtypeStruct((2, total, width // 2), BF16)]
        out_specs += [ANYWHERE]
        scratch += [pltpu.VMEM(next_refs[0].shape[1:], BF16)]
    scratch += [pltpu.VMEM((chunks, FRAME, width), BF16)] * 4
    scratch += [
        pltpu.SemaphoreType.DMA((4,)),
        pltpu.SemaphoreType.DMA((2, chunks)),
        pltpu.SemaphoreType.DMA((2, chunks)),
    ]
    if d_out is not None:
        scratch += [
            pltpu.VMEM((2, total, width // 2), BF16),
            pltpu.VMEM((2, rows_here, width // 2), BF16),
            pltpu.SemaphoreType.DMA,
        ]
        scratch += Relay.scratch(n)
    return pl.pallas_call(
        kernel,
        grid=(chunks + 2,),
        out_shape=out_shape,
        in_specs=in_specs,
        out_specs=out_specs,
        scratch_shapes=scratch,
        compiler_params=pltpu.CompilerParams(
            collective_id=identity, has_side_effects=True, vmem_limit_bytes=VMEM_BYTES
        ),
        name=f"layer_forward_{layer}",
    )(*operands)


def attention_backward(probs, query, key, value, grad_mixed, fixed, frames, ships, lane_rows, identity):
    total, features = query.shape
    chunks = total // FRAME
    slabs = features // PAIR
    half = PAIR // 2
    ship_count, row_count = len(ships), len(lane_rows)

    def kernel(*refs):
        refs = list(refs)

        def take(count):
            taken = refs[:count]
            del refs[:count]
            return taken

        p_ref, q_ref, k_ref, v_ref, g_ref, fixed_ref, frames_ref = take(7)
        ship_refs, row_refs = take(ship_count), take(row_count)
        dq_ref, dk_ref, dv_ref = take(3)
        ship_outs, row_outs = take(ship_count), take(row_count)
        dk_sum, dv_sum = take(2)
        ship_sends, ship_recvs = take(ship_count), take(ship_count)
        send_sem, recv_sem = take(2)

        step = pl.program_id(0)
        me, core = lax.axis_index("seq"), lax.axis_index("tp")
        x = lax.rem(me, 2)
        beside = me + 1 - 2 * x

        def copies():
            items = [
                (send, recv) for send, recv in zip(ship_sends, ship_recvs)
            ]
            for (_, count), ref, out in zip(lane_rows, row_refs, row_outs):
                items.append((ref.at[at(beside * count, count), :] if count else ref, out))
            return [
                remote(source, target, send_sem.at[i], recv_sem.at[i], beside, core)
                for i, (source, target) in enumerate(items)
            ]

        @pl.when(step == 0)
        def _():
            greet([(beside, core)])
            for ref, send in zip(ship_refs, ship_sends):
                send[...] = ref[at((1 - x) * half, half), :].astype(BF16)
            for copy in copies():
                copy.start()

        lane = lax.broadcasted_iota(jnp.int32, (1, PAIR), 1)
        sides = [(lane < HEAD_DIM).astype(F32).astype(BF16), (lane >= HEAD_DIM).astype(F32).astype(BF16)]
        for frame in reversed(range(chunks)):
            keys = FRAME * (frame + 1)
            own = slice(frame * FRAME, keys)
            tables = tables_of(fixed_ref, frames_ref, frame)
            grad_query = None
            key_parts, value_parts = None, None
            for side in range(2):
                g2 = g_ref[own, :] * sides[side]
                q2 = q_ref[own, :] * sides[side]
                attention = p_ref[frame, side, :, :keys]
                grad = nt(g2, v_ref[:keys, :])
                wide = attention.astype(F32)
                inner = jnp.sum(wide * grad, axis=-1, keepdims=True)
                grad_scores = (wide * (grad - inner)).astype(BF16)
                term = nn(grad_scores, k_ref[:keys, :] * sides[side])
                grad_query = term if grad_query is None else grad_query + term
                key_term, value_term = tn(grad_scores, q2), tn(attention, g2)
                key_parts = key_term if key_parts is None else key_parts + key_term
                value_parts = value_term if value_parts is None else value_parts + value_term
            dq_ref[own, :] = (turn(grad_query, tables, True) * SCORE_SCALE).astype(BF16)
            if frame == chunks - 1:
                dk_sum[...] = key_parts
                dv_sum[...] = value_parts
            else:
                dk_sum[:keys, :] += key_parts
                dv_sum[:keys, :] += value_parts
            dk_ref[own, :] = turn(dk_sum[own, :], tables, True).astype(BF16)
            dv_ref[own, :] = dv_sum[own, :].astype(BF16)

        @pl.when(step == slabs - 1)
        def _():
            for copy in copies():
                copy.wait_recv()
            for ref, recv, out in zip(ship_refs, ship_recvs, ship_outs):
                out[...] = ref[at(x * half, half), :] + recv[...].astype(F32)
            for copy in copies():
                copy.wait_send()

    slab = pl.BlockSpec((total, PAIR), lambda s: (0, s))
    in_specs = [pl.BlockSpec((chunks, 2, FRAME, total), lambda s: (0, s, 0, 0))]
    in_specs += [slab] * 4 + [whole(fixed), whole(frames)]
    in_specs += [whole(item) for item in ships] + [ANYWHERE] * row_count
    out_shape = [jax.ShapeDtypeStruct((total, features), BF16)] * 3
    out_specs = [slab] * 3
    for item in ships:
        out_shape.append(jax.ShapeDtypeStruct((half, item.shape[1]), F32))
        out_specs.append(whole_out((half, item.shape[1])))
    for item, count in lane_rows:
        shape = (count or item.shape[0], item.shape[1])
        out_shape.append(jax.ShapeDtypeStruct(shape, item.dtype))
        out_specs.append(ANYWHERE)
    scratch = [pltpu.VMEM((total, PAIR), F32)] * 2
    scratch += [pltpu.VMEM((half, item.shape[1]), BF16) for item in ships] * 2
    scratch += [pltpu.SemaphoreType.DMA((ship_count + row_count,))] * 2
    return pl.pallas_call(
        kernel,
        grid=(slabs,),
        out_shape=out_shape,
        in_specs=in_specs,
        out_specs=out_specs,
        scratch_shapes=scratch,
        compiler_params=pltpu.CompilerParams(
            collective_id=identity, has_side_effects=True, vmem_limit_bytes=VMEM_BYTES
        ),
        name=f"attention_backward_{identity}",
    )(probs, query, key, value, grad_mixed, fixed, frames, *ships, *[item for item, _ in lane_rows])


def rows_backward(entry, upper, identity):
    top, bottom = len(entry) == 1, upper is None
    if not top:
        above, entry = entry[0], entry[1:]
        split = entry[3].ndim == 3
    total = entry[0].shape[1] if top else entry[0].shape[0]
    chunks = total // FRAME
    columns = 512
    ahead = 0 if top else 1
    if top:
        width = 2 * entry[0].shape[2]
    else:
        features, width = entry[0].shape[1], entry[4].shape[1]
    if not bottom:
        layer = upper[0]
        hidden_units, mixed_features = upper[1].shape[1], upper[5].shape[1]
    half = PAIR // 2
    place_rows = total // lax.axis_size("seq")

    def kernel(*refs):
        refs = list(refs)

        def take(count):
            taken = refs[:count]
            del refs[:count]
            return taken

        if top:
            (d_out_ref,) = take(1)
        else:
            dq_ref, dk_ref, dv_ref, x_ref, dm_ref, first_ref, wq, gain1 = take(8)
        if not bottom:
            act_ref, gp_ref, middle_ref, second_ref, mixed_ref = take(5)
            wo_any, wu_any, wd_any, gain2 = take(4)
        if not top:
            qkv_sum, vec1 = take(2)
        if not bottom:
            dmid_out, dmix_out, out_sum, up_sum, down_sum, vec2 = take(6)
        else:
            dx_out, dx_other, vec_other = take(3)
        if not top:
            a_send, a_recv = take(2)
        if not bottom:
            b_send, b_recv, grad_keep, part_keep, low_keep, wo, wu, wd, w_sem = take(9)
        else:
            dx_keep, dx_recv, vec_recv, qkv_send, qkv_recv, x_send_sem, x_recv_sem = take(7)
        send_sem, recv_sem = take(2)

        step = pl.program_id(0)
        me, core = lax.axis_index("seq"), lax.axis_index("tp")
        pair = at((me // 2) * PAIR, PAIR)
        x = lax.rem(me, 2)
        beside = me + 1 - 2 * x

        def exchange(kind, chunk):
            source, target = (a_send, a_recv) if kind == 0 else (b_send, b_recv)
            return remote(
                source.at[chunk],
                target.at[chunk],
                send_sem.at[kind, chunk],
                recv_sem.at[kind, chunk],
                me,
                1 - core,
            )

        def load(index):
            source, target = ((wd_any, wd), (wu_any, wu), (wo_any, wo))[index]
            return pltpu.make_async_copy(source.at[layer], target, w_sem.at[index])

        @pl.when(step == 0)
        def _():
            if not bottom:
                for index in range(3):
                    load(index).start()
                out_sum[...] = jnp.zeros_like(out_sum)
                up_sum[...] = jnp.zeros_like(up_sum)
                down_sum[...] = jnp.zeros_like(down_sum)
                vec2[...] = jnp.zeros_like(vec2)
            if not top:
                qkv_sum[...] = jnp.zeros_like(qkv_sum)
                vec1[...] = jnp.zeros_like(vec1)
            greet([(me, 1 - core)] + ([(beside, core)] if bottom else []))

        if not top:

            @pl.when(step < chunks)
            def _():
                first = first_ref[...]
                partial = None
                for part, ref in enumerate((dq_ref, dk_ref, dv_ref)):
                    piece = slice(part * features, (part + 1) * features)
                    grad = ref[...]
                    term = nt(grad, wq[0, part])
                    partial = term if partial is None else partial + term
                    qkv_sum[:, piece] += tn(first, grad)
                    vec1[0:1, piece] += column_sum(grad.astype(F32))
                a_send[step] = partial.astype(BF16)
                exchange(0, step).start()

        @pl.when((step >= ahead) & (step < chunks + ahead))
        def _():
            chunk = step - ahead
            if top:
                gradient = halves(d_out_ref)
            else:
                exchange(0, chunk).wait_recv()
                grad_first = a_send[chunk].astype(F32) + a_recv[chunk].astype(F32)
                unit, scale = normed(halves(x_ref) if split else x_ref[...])
                vec1[1:2, :width] += column_sum(grad_first * unit)
                vec1[2:3, :width] += column_sum(grad_first)
                gradient = dm_ref[...] + norm_pull(
                    grad_first, gain1[above : above + 1, :], unit, scale
                )
            if bottom:
                dx_keep[at(chunk * FRAME, FRAME), :] = gradient
                return

            @pl.when(chunk == 0)
            def _():
                load(0).wait()
                load(1).wait()

            grad_keep[lax.rem(chunk, 2)] = gradient
            vec2[1:2, :width] += column_sum(gradient)
            low = gradient.astype(BF16)
            low_keep[...] = low
            low_columns = low_keep[:, pair]
            second = second_ref[...]
            for start in range(0, hidden_units, columns):
                part = slice(start, start + columns)
                down_sum[:, part] += tn(low_columns, act_ref[:, part])
                grad_act = nt(low, wd[part, :])
                grad_hidden = (grad_act * gp_ref[:, part].astype(F32)).astype(BF16)
                vec2[0:1, part] += column_sum(grad_hidden.astype(F32))
                up_sum[:, part] += tn(second, grad_hidden)
                term = nt(grad_hidden, wu[:, part])
                if start == 0:
                    part_keep[...] = term
                else:
                    part_keep[...] += term
            b_send[chunk] = part_keep[...].astype(BF16)
            exchange(1, chunk).start()

        if not bottom:

            @pl.when(step == ahead + 1)
            def _():
                load(2).wait()

            @pl.when(step >= ahead + 1)
            def _():
                chunk = step - ahead - 1
                exchange(1, chunk).wait_recv()
                grad_second = b_send[chunk].astype(F32) + b_recv[chunk].astype(F32)
                unit, scale = normed(middle_ref[...])
                vec2[2:3, :width] += column_sum(grad_second * unit)
                vec2[3:4, :width] += column_sum(grad_second)
                grad_middle = grad_keep[lax.rem(chunk, 2)] + norm_pull(
                    grad_second, gain2[layer : layer + 1, :], unit, scale
                )
                dmid_out[...] = grad_middle
                vec2[4:5, :width] += column_sum(grad_middle)
                low = grad_middle.astype(BF16)
                low_keep[...] = low
                out_sum[...] += tn(low_keep[:, pair], mixed_ref[...])
                dmix_out[...] = nt(low, wo[...]).astype(BF16)

        if bottom:

            def x_copy(index):
                source, target = (
                    (qkv_send, qkv_recv),
                    (dx_keep.at[at(beside * place_rows, place_rows), :], dx_recv),
                    (vec1, vec_recv),
                )[index]
                return remote(
                    source, target, x_send_sem.at[index], x_recv_sem.at[index], beside, core
                )

            @pl.when(step == chunks - 1)
            def _():
                qkv_send[...] = qkv_sum[at((1 - x) * half, half), :].astype(BF16)
                x_copy(0).start()

            @pl.when(step == chunks)
            def _():
                x_copy(1).start()
                x_copy(2).start()
                dx_out[...] = dx_keep[at(me * place_rows, place_rows), :]
                for index in range(3):
                    x_copy(index).wait_recv()
                qkv_sum[at(x * half, half), :] += qkv_recv[...].astype(F32)
                dx_other[...] = dx_recv[...]
                for index in range(3):
                    x_copy(index).wait_send()
                vec_other[...] = vec_recv[...]

        @pl.when(step == pl.num_programs(0) - 1)
        def _():
            for kind in ([] if top else [0]) + ([] if bottom else [1]):
                for chunk in range(chunks):
                    exchange(kind, chunk).wait_send()

    def rows(columns, behind):
        return pl.BlockSpec(
            (FRAME, columns), lambda s: (jnp.clip(s - behind, 0, chunks - 1), 0)
        )

    vec = jax.ShapeDtypeStruct((8, VEC), F32)
    operands, in_specs, out_shape, out_specs, scratch = [], [], [], [], []
    if top:
        operands += list(entry)
        in_specs += [halves_spec(entry[0].shape, chunks, 0)]
    else:
        operands += list(entry)
        in_specs += [rows(features, 0)] * 3
        in_specs += [halves_spec(entry[3].shape, chunks, 1) if split else rows(width, 1)]
        in_specs += [rows(width, 1), rows(PAIR, 0)]
        in_specs += [
            pl.BlockSpec(
                (1, *entry[6].shape[1:]),
                lambda s: (above, 0, 0, 0),
                pipeline_mode=pl.Buffered(1),
            ),
            whole(entry[7]),
        ]
        out_shape += [jax.ShapeDtypeStruct((PAIR, 3 * features), F32), vec]
        out_specs += [whole_out((PAIR, 3 * features)), whole_out((8, VEC))]
        scratch += [pltpu.VMEM((chunks, FRAME, width), BF16)] * 2
    if not bottom:
        operands += list(upper[1:])
        in_specs += [rows(hidden_units, ahead)] * 2 + [rows(width, ahead + 1), rows(PAIR, ahead)]
        in_specs += [rows(mixed_features, ahead + 1)] + [ANYWHERE] * 3 + [whole(upper[9])]
        sums = [mixed_features, hidden_units, hidden_units]
        out_shape += [
            jax.ShapeDtypeStruct((total, width), F32),
            jax.ShapeDtypeStruct((total, mixed_features), BF16),
        ]
        out_shape += [jax.ShapeDtypeStruct((PAIR, size), F32) for size in sums] + [vec]
        out_specs += [rows(width, ahead + 1), rows(mixed_features, ahead + 1)]
        out_specs += [whole_out((PAIR, size)) for size in sums] + [whole_out((8, VEC))]
        scratch += [pltpu.VMEM((chunks, FRAME, width), BF16)] * 2
        scratch += [
            pltpu.VMEM((2, FRAME, width), F32),
            pltpu.VMEM((FRAME, width), F32),
            pltpu.VMEM((FRAME, width), BF16),
            pltpu.VMEM(upper[6].shape[1:], BF16),
            pltpu.VMEM(upper[7].shape[1:], BF16),
            pltpu.VMEM(upper[8].shape[1:], BF16),
            pltpu.SemaphoreType.DMA((3,)),
        ]
    else:
        out_shape += [
            jax.ShapeDtypeStruct((place_rows, width), F32),
            jax.ShapeDtypeStruct((place_rows, width), F32),
            vec,
        ]
        out_specs += [whole_out((place_rows, width))] * 2 + [whole_out((8, VEC))]
        scratch += [
            pltpu.VMEM((total, width), F32),
            pltpu.VMEM((place_rows, width), F32),
            pltpu.VMEM((8, VEC), F32),
            pltpu.VMEM((half, 3 * features), BF16),
            pltpu.VMEM((half, 3 * features), BF16),
            pltpu.SemaphoreType.DMA((3,)),
            pltpu.SemaphoreType.DMA((3,)),
        ]
    scratch += [pltpu.SemaphoreType.DMA((2, chunks))] * 2
    return pl.pallas_call(
        kernel,
        grid=(chunks + (1 if top or bottom else 2),),
        out_shape=out_shape,
        in_specs=in_specs,
        out_specs=out_specs,
        scratch_shapes=scratch,
        compiler_params=pltpu.CompilerParams(
            collective_id=identity, has_side_effects=True, vmem_limit_bytes=VMEM_BYTES
        ),
        name=f"rows_backward_{identity}",
    )(*operands)


def assemble(sums, vecs, lanes, qkv_sum, n, features, hidden_units):
    place = lanes[1].shape[0]
    width = lanes[1].shape[1]
    half = PAIR // 2

    def kernel(*refs):
        refs = list(refs)

        def take(count):
            taken = refs[:count]
            del refs[:count]
            return taken

        (qkv_low,) = take(1)
        qkv_high = take(LAYERS - 1)
        outs, ups, downs = take(LAYERS), take(LAYERS), take(LAYERS)
        vec_refs = [take(4) for _ in range(LAYERS)]
        stream_ref, out_other, dx_own, dx_other = take(4)
        out_ref, dx_ref, gain1, shift1, g_qkv, b_qkv, g_out, b_out = take(8)
        gain2, shift2, g_up, b_up, g_down, b_down = take(6)
        own, sems = take(2)
        me = lax.axis_index("seq")
        x = lax.rem(me, 2)
        pair = at((me // 2) * PAIR, PAIR)

        jobs = [(stream_ref.at[at(me * place, place), :], own)]
        for part in range(3):
            piece = pl.ds(part * features, features)
            jobs.append((qkv_low.at[at(x * half, half), piece], g_qkv.at[0, part]))
            for layer, ref in enumerate(qkv_high):
                jobs.append((ref.at[:, piece], g_qkv.at[layer + 1, part]))
        for layer in range(LAYERS):
            for ref, target in ((outs, g_out), (ups, g_up), (downs, g_down)):
                jobs.append((ref[layer], target.at[layer]))

        def copy(index):
            source, target = jobs[index]
            return pltpu.make_async_copy(source, target, sems.at[index])

        for index in range(len(jobs)):
            copy(index).start()

        for layer, (entry_own, entry_other, upper_own, upper_other) in enumerate(vec_refs):
            line = slice(layer, layer + 1)
            for part in range(3):
                piece = slice(part * features, (part + 1) * features)
                b_qkv[layer, part : part + 1, :] = entry_own[0:1, piece] + entry_other[0:1, piece]
            b_up[line, :] = upper_own[0:1, :hidden_units] + upper_other[0:1, :hidden_units]

            def owned(mine, other, row):
                both = mine[row : row + 1, pair] + other[row : row + 1, pair]
                return jnp.where(x == 0, both[:, :half], both[:, half:])

            gain1[line, :] = owned(entry_own, entry_other, 1)
            shift1[line, :] = owned(entry_own, entry_other, 2)
            b_down[line, :] = owned(upper_own, upper_other, 1)
            gain2[line, :] = owned(upper_own, upper_other, 2)
            shift2[line, :] = owned(upper_own, upper_other, 3)
            b_out[line, :] = owned(upper_own, upper_other, 4)

        def both_lanes(target, mine, other):
            target[:, 0, :] = jnp.where(x == 0, mine, other)
            target[:, 1, :] = jnp.where(x == 0, other, mine)

        both_lanes(dx_ref, dx_own[...], dx_other[...])
        copy(0).wait()
        both_lanes(out_ref, own[...], out_other[...])
        for index in range(1, len(jobs)):
            copy(index).wait()

    def f32(*shape):
        return jax.ShapeDtypeStruct(shape, F32)

    in_vmem = pl.BlockSpec(memory_space=pltpu.VMEM)
    flat = [qkv_sum] + [sums[layer][0] for layer in range(1, LAYERS)]
    for kind in range(1, 4):
        flat += [sums[layer][kind] for layer in range(LAYERS)]
    count = len(flat)
    for layer in range(LAYERS):
        flat += list(vecs[layer])
    flat += list(lanes)
    small = f32(LAYERS, width // n)
    jobs = 1 + 3 * LAYERS + 3 * LAYERS
    return pl.pallas_call(
        kernel,
        out_shape=(
            f32(place, 2, width),
            f32(place, 2, width),
            small,
            small,
            f32(LAYERS, 3, half, features),
            f32(LAYERS, 3, features),
            f32(LAYERS, half, features),
            small,
            small,
            small,
            f32(LAYERS, half, hidden_units),
            f32(LAYERS, hidden_units),
            f32(LAYERS, half, hidden_units),
            small,
        ),
        in_specs=[ANYWHERE] * count + [in_vmem] * (4 * LAYERS) + [ANYWHERE] + [in_vmem] * 3,
        out_specs=(
            in_vmem,
            in_vmem,
            in_vmem,
            in_vmem,
            ANYWHERE,
            in_vmem,
            ANYWHERE,
            in_vmem,
            in_vmem,
            in_vmem,
            ANYWHERE,
            in_vmem,
            ANYWHERE,
            in_vmem,
        ),
        scratch_shapes=[pltpu.VMEM((place, width), F32), pltpu.SemaphoreType.DMA((jobs,))],
        compiler_params=pltpu.CompilerParams(vmem_limit_bytes=VMEM_BYTES),
        name="assemble",
    )(*flat)


def per_chip(
    tokens,
    d_out,
    norm1_gain,
    norm1_shift,
    w_qkv,
    b_qkv,
    w_out,
    b_out,
    norm2_gain,
    norm2_shift,
    w_up,
    b_up,
    w_down,
    b_down,
    episode_frames,
    live,
):
    n = lax.axis_size("seq")
    rows = tokens.shape[0]
    features = w_qkv.shape[3]
    fixed, ahead = turn_constants(rows * n // FRAME)
    qkv = w_qkv.transpose(0, 2, 1, 3)

    gathered, key_bias, frames, query, key, value, first = gather_and_project(
        tokens, live, episode_frames, norm1_gain, norm1_shift, qkv, b_qkv, fixed, ahead, n
    )
    streams, kept, d_lane = [gathered], [], None
    for layer in range(LAYERS):
        following = None
        if layer + 1 < LAYERS:
            following = (qkv, norm1_gain, norm1_shift, b_qkv, fixed, frames)
        results = layer_forward(
            layer,
            query,
            key,
            value,
            key_bias,
            streams[layer],
            (w_out, w_up, w_down),
            (b_out, norm2_gain, norm2_shift, b_up, b_down),
            following,
            d_out if layer == 0 else None,
            n,
            1 + layer,
        )
        kept.append((query, key, value, first, *results[:6]))
        streams.append(results[6])
        if following is not None:
            query, key, value, first = results[7:11]
        if layer == 0:
            d_lane = results[-1]

    sums = [[None] * 4 for _ in range(LAYERS)]
    vecs = [[None] * 4 for _ in range(LAYERS)]
    entry, pending, pending_rows = (d_lane,), [], [(streams[LAYERS], rows)]
    out_other = None
    for layer in reversed(range(LAYERS)):
        query, key, value, first, probs, mixed, middle, second, act, slope = kept[layer]
        upper = (
            layer,
            act,
            slope,
            middle,
            second,
            mixed,
            w_out,
            w_up,
            w_down,
            norm2_gain,
        )
        results = rows_backward(entry, upper, 1 + LAYERS + 2 * (LAYERS - 1 - layer))
        if layer + 1 < LAYERS:
            qkv_sum, vec1 = results[:2]
            results = results[2:]
            pending = [(0, layer + 1, qkv_sum)]
            pending_rows = [(vec1, 0)]
        grad_middle, grad_mixed, out_sum, up_sum, down_sum, vec2 = results
        pending = pending + [(1, layer, out_sum), (2, layer, up_sum), (3, layer, down_sum)]
        pending_rows = pending_rows + [(vec2, 0)]
        results = attention_backward(
            probs,
            query,
            key,
            value,
            grad_mixed,
            fixed,
            frames,
            [item for _, _, item in pending],
            pending_rows,
            2 + LAYERS + 2 * (LAYERS - 1 - layer),
        )
        grad_query, grad_key, grad_value = results[:3]
        swapped = results[3:]
        for (kind, owner, _), item in zip(pending, swapped):
            sums[owner][kind] = item
        others = swapped[len(pending) :]
        if out_other is None:
            out_other = others[0]
        else:
            vecs[layer + 1][:2] = [pending_rows[0][0], others[0]]
        vecs[layer][2:] = [vec2, others[1]]
        entry = (
            layer,
            grad_query,
            grad_key,
            grad_value,
            streams[layer],
            grad_middle,
            first,
            qkv,
            norm1_gain,
        )
    qkv_sum, vec1, dx_own, dx_other, vec_other = rows_backward(entry, None, 1 + 3 * LAYERS)
    vecs[0][:2] = [vec1, vec_other]
    results = list(
        assemble(
            sums,
            vecs,
            (streams[LAYERS], out_other, dx_own, dx_other),
            qkv_sum,
            n,
            features,
            w_up.shape[2],
        )
    )
    results[4] = results[4].transpose(0, 2, 1, 3)
    results[6] = results[6].transpose(0, 2, 1)
    results[12] = results[12].transpose(0, 2, 1)
    return tuple(results)


def lane_fits(mesh, tokens):
    n = mesh.shape["seq"]
    positions, lanes, width = tokens.shape
    rows = positions // n
    return (
        lanes == 2
        and n % 4 == 0
        and positions <= 4 * FRAME
        and positions % FRAME == 0
        and FRAME % rows == 0
        and width // n * 2 == PAIR
        and mesh.shape["tp"] == 2
    )


def solution(mesh):
    placed = (
        P("seq", None, None),
        P("seq", None, None),
        P(),
        P(),
        P(None, None, None, "tp"),
        P(None, None, "tp"),
        P(None, "tp", None),
        P(),
        P(),
        P(),
        P(None, None, "tp"),
        P(None, "tp"),
        P(None, "tp", None),
        P(),
        P(),
        P("seq", None),
    )
    def mapped(body):
        return jax.shard_map(
            body,
            mesh=mesh,
            in_specs=placed,
            out_specs=(
                P("seq", None, None),
                P("seq", None, None),
                P(None, "seq"),
                P(None, "seq"),
                P(None, "seq", None, "tp"),
                P(None, None, "tp"),
                P(None, "tp", "seq"),
                P(None, "seq"),
                P(None, "seq"),
                P(None, "seq"),
                P(None, "seq", "tp"),
                P(None, "tp"),
                P(None, "tp", "seq"),
                P(None, "seq"),
            ),
            check_vma=False,
        )

    def run(tokens, *others):
        if lane_fits(mesh, tokens):
            return mapped(per_chip)(tokens, *others)
        return mapped(per_device)(tokens, *others)

    return run
```

```python
import math

import jax
import jax.numpy as jnp
import numpy as np
from jax import lax
from jax.experimental import pallas as pl
from jax.experimental.pallas import tpu as pltpu
from jax.sharding import PartitionSpec as P

HEAD_DIM = 64
GRID = 16
FRAME = 256
LAYERS = 2
MICRO = 2


EPSILON = 1e-06
MASKED = -1e30
SCORE_SCALE = 0.125


def layer_norm(stream, norm_gain, norm_shift):
    center = stream - jnp.mean(stream, axis=-1, keepdims=True)
    spread = jnp.mean(center * center, axis=-1, keepdims=True)
    return center * lax.rsqrt(spread + EPSILON) * norm_gain + norm_shift


def rotate(values, frame_place, row_place, column_place):
    frequency = jnp.exp(jnp.arange(10, dtype=jnp.float32) * (-math.log(10000.0) / 10.0))
    pieces = []
    for section, place in enumerate((frame_place, row_place, column_place)):
        lower = values[..., 20 * section : 20 * section + 10]
        upper = values[..., 20 * section + 10 : 20 * section + 20]
        angles = place.astype(jnp.float32)[..., None, None] * frequency
        cosine = jnp.cos(angles)
        sine_part = jnp.sin(angles)
        pieces.append(lower * cosine - upper * sine_part)
        pieces.append(lower * sine_part + upper * cosine)
    pieces.append(values[..., 60:])
    return jnp.concatenate(pieces, axis=-1)


def episode_tags(frame_counts, positions):
    endings = jnp.cumsum(frame_counts) * FRAME
    passed = (positions[:, None] >= endings[None, :]).astype(jnp.int32)
    episode = jnp.sum(passed, axis=1)
    opening = jnp.sum(passed * frame_counts[None, :], axis=1)
    frame_index = positions // FRAME - opening
    within = positions % FRAME
    return (episode, frame_index, within // GRID, within % GRID)


def gelu_exact(values):
    return jax.nn.gelu(values, approximate=False)


def sum_heads(partial_sum):
    return lax.psum(partial_sum.astype(jnp.bfloat16), "tp").astype(jnp.float32)


def sum_inputs(partial_sum):
    return lax.psum(partial_sum.astype(jnp.bfloat16), "tp").astype(jnp.float32)


def lane_scores(query, keys_all, lane_index, query_tags, key_tags):
    head_count = query.shape[2] // HEAD_DIM
    query_lane = lax.dynamic_index_in_dim(query, lane_index, 1, False).reshape(
        query.shape[0], head_count, HEAD_DIM
    )
    keys_lane = lax.dynamic_index_in_dim(keys_all, lane_index, 1, False).reshape(
        keys_all.shape[0], head_count, HEAD_DIM
    )
    query_episode, query_frame = [
        lax.dynamic_index_in_dim(item, lane_index, 1, False) for item in query_tags
    ]
    key_episode, key_frame, key_live = [
        lax.dynamic_index_in_dim(item, lane_index, 1, False) for item in key_tags
    ]
    allowed = (
        (query_episode[:, None] == key_episode[None, :])
        & (key_frame[None, :] <= query_frame[:, None])
        & (key_live[None, :] > 0)
    )
    scores = (
        jnp.einsum("qhd,khd->hqk", query_lane, keys_lane, preferred_element_type=jnp.float32)
        * SCORE_SCALE
    )
    return (jnp.where(allowed[None], scores, MASKED), query_lane, keys_lane)


def attend_forward(query, keys_all, values_all, query_tags, key_tags):
    rows_dev, lane_count, features = query.shape
    head_count = features // HEAD_DIM

    def one_lane(lane_index, carry):
        scores, query_lane, keys_lane = lane_scores(
            query, keys_all, lane_index, query_tags, key_tags
        )
        highest = jnp.max(scores, axis=-1, keepdims=True)
        shifted = jnp.exp(scores - highest)
        summed = jnp.sum(shifted, axis=-1, keepdims=True)
        attention = (shifted / summed).astype(jnp.bfloat16)
        values_lane = lax.dynamic_index_in_dim(values_all, lane_index, 1, False).reshape(
            values_all.shape[0], head_count, HEAD_DIM
        )
        result = jnp.einsum(
            "hqk,khd->qhd", attention, values_lane, preferred_element_type=jnp.float32
        ).reshape(rows_dev, 1, features)
        log_total = (highest + jnp.log(summed))[None, :, :, 0]
        return (result, log_total)

    initial = (
        jnp.zeros((rows_dev, lane_count, features), jnp.float32),
        jnp.zeros((lane_count, head_count, rows_dev), jnp.float32),
    )
    return lax.fori_loop(0, lane_count, one_lane, initial)


def attend_backward(query, keys_all, values_all, log_total, grad_mixed, query_tags, key_tags):
    rows_dev, lane_count, features = query.shape
    head_count = features // HEAD_DIM
    key_rows = keys_all.shape[0]

    def one_lane(lane_index, carry):
        scores, query_lane, keys_lane = lane_scores(
            query, keys_all, lane_index, query_tags, key_tags
        )
        values_lane = lax.dynamic_index_in_dim(values_all, lane_index, 1, False).reshape(
            key_rows, head_count, HEAD_DIM
        )
        grad_lane = lax.dynamic_index_in_dim(grad_mixed, lane_index, 1, False).reshape(
            rows_dev, head_count, HEAD_DIM
        )
        attention = jnp.exp(
            scores - lax.dynamic_index_in_dim(log_total, lane_index, 0, False)[:, :, None]
        )
        grad_attention = jnp.einsum(
            "qhd,khd->hqk", grad_lane, values_lane, preferred_element_type=jnp.float32
        )
        inner = jnp.sum(attention * grad_attention, axis=-1, keepdims=True)
        grad_scores = (attention * (grad_attention - inner)).astype(jnp.bfloat16)
        query_part = (
            jnp.einsum("hqk,khd->qhd", grad_scores, keys_lane, preferred_element_type=jnp.float32)
            * SCORE_SCALE
        )
        key_part = (
            jnp.einsum("hqk,qhd->khd", grad_scores, query_lane, preferred_element_type=jnp.float32)
            * SCORE_SCALE
        )
        value_part = jnp.einsum(
            "hqk,qhd->khd",
            attention.astype(jnp.bfloat16),
            grad_lane,
            preferred_element_type=jnp.float32,
        )
        stacked = jnp.stack(
            [key_part.reshape(key_rows, features), value_part.reshape(key_rows, features)], axis=1
        )
        key_terms = stacked[:, None]
        grad_query = query_part.reshape(rows_dev, 1, features)
        return (grad_query, key_terms)

    initial = (
        jnp.zeros((rows_dev, lane_count, features), jnp.float32),
        jnp.zeros((key_rows, lane_count, 2, features), jnp.float32),
    )
    return lax.fori_loop(0, lane_count, one_lane, initial)


def front(stream, layer_index, params, query_tags, key_tags, positions):
    (
        gain_one,
        shift_one,
        mat_qkv,
        bias_qkv,
        mat_out,
        bias_out,
        gain_two,
        shift_two,
        mat_up,
        bias_up,
        mat_down,
        bias_down,
    ) = [item[layer_index] for item in params]
    rows_dev, lane_count, width = stream.shape
    features = mat_qkv.shape[2]
    head_count = features // HEAD_DIM
    frame_place, row_place, column_place = positions
    first = layer_norm(stream, gain_one, shift_one).astype(jnp.bfloat16)
    projected = (
        jnp.einsum("tbd,dcf->tbcf", first, mat_qkv, preferred_element_type=jnp.float32) + bias_qkv
    )
    split = projected.reshape(rows_dev, lane_count, 3, head_count, HEAD_DIM)
    query = (
        rotate(split[:, :, 0], frame_place, row_place, column_place)
        .reshape(rows_dev, lane_count, features)
        .astype(jnp.bfloat16)
    )
    keys = (
        rotate(split[:, :, 1], frame_place, row_place, column_place)
        .reshape(rows_dev, lane_count, features)
        .astype(jnp.bfloat16)
    )
    values = projected[:, :, 2].astype(jnp.bfloat16)
    keys_all, values_all = (
        lax.all_gather(keys, "seq", axis=0, tiled=True),
        lax.all_gather(values, "seq", axis=0, tiled=True),
    )
    mixed_full, log_total = attend_forward(query, keys_all, values_all, query_tags, key_tags)
    mixed = mixed_full.astype(jnp.bfloat16)
    middle = (
        stream
        + sum_heads(jnp.einsum("tbf,fd->tbd", mixed, mat_out, preferred_element_type=jnp.float32))
        + bias_out
    )
    second = layer_norm(middle, gain_two, shift_two).astype(jnp.bfloat16)
    hidden = jnp.einsum("tbd,df->tbf", second, mat_up, preferred_element_type=jnp.float32) + bias_up
    activation = gelu_exact(hidden).astype(jnp.bfloat16)
    return (
        first,
        query,
        keys_all,
        values_all,
        log_total,
        mixed,
        middle,
        second,
        hidden,
        activation,
        mixed_full,
    )


def layer_backward(stream, gradient, layer_index, params, query_tags, key_tags, positions):
    (
        gain_one,
        shift_one,
        mat_qkv,
        bias_qkv,
        mat_out,
        bias_out,
        gain_two,
        shift_two,
        mat_up,
        bias_up,
        mat_down,
        bias_down,
    ) = [item[layer_index] for item in params]
    (
        first,
        query,
        keys_all,
        values_all,
        log_total,
        mixed,
        middle,
        second,
        hidden,
        activation,
        mixed_full,
    ) = front(stream, layer_index, params, query_tags, key_tags, positions)
    frame_place, row_place, column_place = positions
    rows_dev, lane_count, width = stream.shape
    features = query.shape[2]
    head_count = features // HEAD_DIM
    grad_low = gradient.astype(jnp.bfloat16)
    grad_w_down = jnp.einsum(
        "tbf,tbd->fd", activation, grad_low, preferred_element_type=jnp.float32
    )
    grad_b_down = jnp.sum(gradient, axis=(0, 1))
    grad_activation = jnp.einsum(
        "tbd,fd->tbf", grad_low, mat_down, preferred_element_type=jnp.float32
    )
    grad_hidden = jax.vjp(gelu_exact, hidden)[1](grad_activation)[0].astype(jnp.bfloat16)
    grad_b_up = jnp.sum(grad_hidden.astype(jnp.float32), axis=(0, 1))
    grad_w_up = jnp.einsum("tbd,tbf->df", second, grad_hidden, preferred_element_type=jnp.float32)
    grad_second = sum_inputs(
        jnp.einsum("tbf,df->tbd", grad_hidden, mat_up, preferred_element_type=jnp.float32)
    )
    middle_pull = jax.vjp(layer_norm, middle, gain_two, shift_two)[1]
    grad_inner, grad_gain_two, grad_shift_two = middle_pull(grad_second)
    grad_middle = gradient + grad_inner
    grad_b_out = jnp.sum(grad_middle, axis=(0, 1))
    middle_low = grad_middle.astype(jnp.bfloat16)
    grad_w_out = jnp.einsum("tbf,tbd->fd", mixed, middle_low, preferred_element_type=jnp.float32)
    grad_mixed = jnp.einsum(
        "tbd,fd->tbf", middle_low, mat_out, preferred_element_type=jnp.float32
    ).astype(jnp.bfloat16)
    grad_query, key_terms = attend_backward(
        query, keys_all, values_all, log_total, grad_mixed, query_tags, key_tags
    )
    returned = lax.psum_scatter(key_terms, "seq", scatter_dimension=0, tiled=True)
    turned_query = rotate(
        grad_query.reshape(rows_dev, lane_count, head_count, HEAD_DIM),
        -frame_place,
        -row_place,
        -column_place,
    )
    turned_keys = rotate(
        returned[:, :, 0].reshape(rows_dev, lane_count, head_count, HEAD_DIM),
        -frame_place,
        -row_place,
        -column_place,
    )
    grad_projected = jnp.stack(
        [
            turned_query.reshape(rows_dev, lane_count, features),
            turned_keys.reshape(rows_dev, lane_count, features),
            returned[:, :, 1],
        ],
        axis=2,
    ).astype(jnp.bfloat16)
    grad_b_qkv = jnp.sum(grad_projected.astype(jnp.float32), axis=(0, 1))
    grad_w_qkv = jnp.einsum(
        "tbd,tbcf->dcf", first, grad_projected, preferred_element_type=jnp.float32
    )
    grad_first = sum_inputs(
        jnp.einsum("tbcf,dcf->tbd", grad_projected, mat_qkv, preferred_element_type=jnp.float32)
    )
    first_pull = jax.vjp(layer_norm, stream, gain_one, shift_one)[1]
    grad_entry, grad_gain_one, grad_shift_one = first_pull(grad_first)
    grads = (
        grad_gain_one,
        grad_shift_one,
        grad_w_qkv,
        grad_b_qkv,
        grad_w_out,
        grad_b_out,
        grad_gain_two,
        grad_shift_two,
        grad_w_up,
        grad_b_up,
        grad_w_down,
        grad_b_down,
    )
    return (grad_middle + grad_entry, grads)


def per_device(
    tokens,
    d_out,
    norm1_gain,
    norm1_shift,
    w_qkv,
    b_qkv,
    w_out,
    b_out,
    norm2_gain,
    norm2_shift,
    w_up,
    b_up,
    w_down,
    b_down,
    episode_frames,
    live,
):
    rows_dev = tokens.shape[0]
    lane_count = tokens.shape[1] // MICRO
    total_rows = rows_dev * lax.axis_size("seq")
    local_positions = lax.axis_index("seq") * rows_dev + jnp.arange(rows_dev, dtype=jnp.int32)
    key_positions = jnp.arange(total_rows, dtype=jnp.int32)
    tagger = jax.vmap(episode_tags, in_axes=(0, None), out_axes=1)
    query_episode, query_frame, query_row, query_column = tagger(episode_frames, local_positions)
    key_episode, key_frame, key_row, key_column = tagger(episode_frames, key_positions)
    live_keys = lax.all_gather(live, "seq", axis=0, tiled=True)
    params = (
        norm1_gain,
        norm1_shift,
        w_qkv,
        b_qkv,
        w_out,
        b_out,
        norm2_gain,
        norm2_shift,
        w_up,
        b_up,
        w_down,
        b_down,
    )
    layer_grads = [None] * LAYERS
    outputs = []
    grad_tokens = []
    for micro_index in range(MICRO):
        first_lane = micro_index * lane_count
        last_lane = first_lane + lane_count
        query_tags = (query_episode[:, first_lane:last_lane], query_frame[:, first_lane:last_lane])
        key_tags = (
            key_episode[:, first_lane:last_lane],
            key_frame[:, first_lane:last_lane],
            live_keys[:, first_lane:last_lane],
        )
        positions = (
            query_frame[:, first_lane:last_lane],
            query_row[:, first_lane:last_lane],
            query_column[:, first_lane:last_lane],
        )
        stream = tokens[:, first_lane:last_lane].astype(jnp.float32)
        inputs = []
        gathered = []
        for layer_index in range(LAYERS):
            inputs.append(stream)
            layer_state = front(stream, layer_index, params, query_tags, key_tags, positions)
            gathered.append((layer_state[2], layer_state[3]))
            branch = jnp.einsum(
                "tbf,fd->tbd",
                layer_state[9],
                w_down[layer_index],
                preferred_element_type=jnp.float32,
            )
            stream = layer_state[6] + sum_heads(branch) + b_down[layer_index]
        outputs.append(stream)
        gradient = d_out[:, first_lane:last_lane]
        for layer_index in reversed(range(LAYERS)):
            gradient, grads = layer_backward(
                inputs[layer_index], gradient, layer_index, params, query_tags, key_tags, positions
            )
            if layer_grads[layer_index] is None:
                layer_grads[layer_index] = grads
            else:
                layer_grads[layer_index] = jax.tree.map(jnp.add, layer_grads[layer_index], grads)
        grad_tokens.append(gradient)
    stacked = [
        jnp.stack([layer_grads[layer_index][entry] for layer_index in range(LAYERS)])
        for entry in range(12)
    ]
    (
        grad_gain_one,
        grad_shift_one,
        grad_w_qkv,
        grad_b_qkv,
        grad_w_out,
        grad_b_out,
        grad_gain_two,
        grad_shift_two,
        grad_w_up,
        grad_b_up,
        grad_w_down,
        grad_b_down,
    ) = stacked
    in_sums = (
        lax.psum_scatter(grad_w_qkv, "seq", scatter_dimension=1, tiled=True),
        lax.psum_scatter(grad_w_up, "seq", scatter_dimension=1, tiled=True),
        lax.psum_scatter(grad_gain_one, "seq", scatter_dimension=1, tiled=True),
        lax.psum_scatter(grad_shift_one, "seq", scatter_dimension=1, tiled=True),
        lax.psum_scatter(grad_gain_two, "seq", scatter_dimension=1, tiled=True),
        lax.psum_scatter(grad_shift_two, "seq", scatter_dimension=1, tiled=True),
        lax.psum_scatter(grad_b_out, "seq", scatter_dimension=1, tiled=True),
        lax.psum_scatter(grad_b_down, "seq", scatter_dimension=1, tiled=True),
    )
    out_sums = (
        lax.psum_scatter(grad_w_out, "seq", scatter_dimension=2, tiled=True),
        lax.psum_scatter(grad_w_down, "seq", scatter_dimension=2, tiled=True),
    )
    bias_total = lax.psum((grad_b_qkv, grad_b_up), "seq")
    return (
        jnp.concatenate(outputs, axis=1),
        jnp.concatenate(grad_tokens, axis=1),
        in_sums[2],
        in_sums[3],
        in_sums[0],
        bias_total[0],
        out_sums[0],
        in_sums[6],
        in_sums[4],
        in_sums[5],
        in_sums[1],
        bias_total[1],
        out_sums[1],
        in_sums[7],
    )


MESH = pl.DeviceIdType.MESH
BF16 = jnp.bfloat16
F32 = jnp.float32
VMEM_BYTES = 60 * 1024 * 1024
PAIR = 128
VEC = 2048


def nn(left, right):
    return lax.dot_general(left, right, (((1,), (0,)), ((), ())), preferred_element_type=F32)


def nt(left, right):
    return lax.dot_general(left, right, (((1,), (1,)), ((), ())), preferred_element_type=F32)


def tn(left, right):
    return lax.dot_general(left, right, (((0,), (0,)), ((), ())), preferred_element_type=F32)


def at(start, size):
    return pl.ds(pl.multiple_of(start, size), size)


def remote(src, dst, send, recv, seq, tp):
    return pltpu.make_async_remote_copy(
        src_ref=src,
        dst_ref=dst,
        send_sem=send,
        recv_sem=recv,
        device_id=(seq, tp),
        device_id_type=MESH,
    )


def greet(partners):
    barrier = pltpu.get_barrier_semaphore()
    for seq, tp in partners:
        pl.semaphore_signal(barrier, inc=1, device_id=(seq, tp), device_id_type=MESH)
    pl.semaphore_wait(barrier, len(partners))


def whole(array):
    zeros = (0,) * array.ndim
    return pl.BlockSpec(array.shape, lambda s: zeros, pipeline_mode=pl.Buffered(1))


def whole_out(shape):
    zeros = (0,) * len(shape)
    return pl.BlockSpec(shape, lambda s: zeros)


ANYWHERE = pl.BlockSpec(memory_space=pl.ANY)


def turn_row(table, place, section):
    frequency = np.exp(np.arange(10, dtype=np.float32) * np.float32(-math.log(10000.0) / 10.0))
    angle = place.astype(np.float32)[:, None] * frequency
    for base in range(20 * section, PAIR, HEAD_DIM):
        table[0, :, base : base + 10] = np.cos(angle)
        table[0, :, base + 10 : base + 20] = np.cos(angle)
        table[1, :, base : base + 10] = -np.sin(angle)
        table[2, :, base + 10 : base + 20] = np.sin(angle)


def turn_constants(frames):
    within, ahead = np.zeros((3, FRAME, PAIR), np.float32), np.zeros((3, frames, PAIR), np.float32)
    turn_row(within, np.arange(FRAME) // GRID, 1)
    turn_row(within, np.arange(FRAME) % GRID, 2)
    for base in range(60, PAIR, HEAD_DIM):
        within[0, :, base : base + 4] = 1.0
    turn_row(ahead, np.arange(frames), 0)
    return jnp.asarray(within), jnp.asarray(ahead)


def turn(values, tables, back=False):
    cosine, lower, upper = tables
    pieces = []
    for start in range(0, values.shape[1], PAIR):
        slab = values[:, start : start + PAIR]
        moved = pltpu.roll(slab, PAIR - 10, 1) * lower + pltpu.roll(slab, 10, 1) * upper
        pieces.append(slab * cosine - moved if back else slab * cosine + moved)
    return jnp.concatenate(pieces, axis=1)


def tables_of(fixed_ref, frames_ref, chunk):
    return [fixed_ref[i] + frames_ref[i, pl.ds(chunk, 1), :] for i in range(3)]


def normed(stream):
    center = stream - jnp.mean(stream, axis=-1, keepdims=True)
    spread = jnp.mean(center * center, axis=-1, keepdims=True)
    scale = lax.rsqrt(spread + EPSILON)
    return center * scale, scale


def norm_pull(grad, gain, unit, scale):
    scaled = grad * gain
    return scale * (
        scaled
        - jnp.mean(scaled, axis=-1, keepdims=True)
        - unit * jnp.mean(scaled * unit, axis=-1, keepdims=True)
    )


def column_sum(values):
    return jnp.sum(values, axis=0, keepdims=True)


def gelu_both(hidden):
    normal = 0.5 + 0.5 * lax.erf(hidden * math.sqrt(0.5))
    density = jnp.exp(hidden * hidden * -0.5) * (1.0 / math.sqrt(2.0 * math.pi))
    return hidden * normal, normal + hidden * density


def project(stream, chunk, layer, pair, refs, outs, first_full):
    gain, shift, weight, bias, fixed, frames = refs
    query_ref, key_ref, value_ref, first_ref = outs
    unit, _ = normed(stream)
    first = (unit * gain[layer : layer + 1, :] + shift[layer : layer + 1, :]).astype(BF16)
    first_full[...] = first
    first_ref[...] = first_full[:, at(pair * PAIR, PAIR)]
    tables = tables_of(fixed, frames, chunk)
    query = nn(first, weight[0]) + bias[0, layer : layer + 1, :]
    query_ref[...] = (turn(query, tables) * SCORE_SCALE).astype(BF16)
    key = nn(first, weight[1]) + bias[1, layer : layer + 1, :]
    key_ref[...] = turn(key, tables).astype(BF16)
    value = nn(first, weight[2]) + bias[2, layer : layer + 1, :]
    value_ref[...] = value.astype(BF16)


class Relay:
    sems = 6

    def __init__(self, n, rows, buffer, other, sems, lives=None, live_other=None):
        self.n, self.rows, self.buffer, self.other = n, rows, buffer, other
        self.lives, self.live_other = lives, live_other
        self.z_send, self.z_recv, self.y_send, self.y_recv, self.c_send, self.c_recv = sems
        self.planes = n // 4
        self.me, self.core = lax.axis_index("seq"), lax.axis_index("tp")
        me = self.me
        self.x, self.y, self.z = lax.rem(me, 2), lax.rem(me // 2, 2), me // 4
        self.across = me + 2 - 4 * self.y

    @staticmethod
    def scratch(n):
        dma, planes = pltpu.SemaphoreType.DMA, n // 4
        shapes = [(planes, 2, 2)] * 2 + [(planes, 2)] * 2 + [(2 * planes,)] * 2
        return [dma(shape) for shape in shapes]

    @property
    def events(self):
        return self.planes

    def plane(self, step):
        return lax.rem(self.z + step, self.planes)

    def place(self, plane, lane):
        return plane * 4 + self.y * 2 + lane

    def reached(self):
        return [(step, far) for step in range(self.planes) for far in (0, 1) if step or far]

    def hello(self):
        barrier = pltpu.get_barrier_semaphore()
        partners = [(self.across, self.core), (self.me, 1 - self.core)]
        for step, far in self.reached():
            lane = 1 - self.x if far else self.x
            partners.append((self.place(self.plane(step), lane), self.core))
        for seq, tp in partners:
            pl.semaphore_signal(barrier, inc=1, device_id=(seq, tp), device_id_type=MESH)

    def met(self):
        pl.semaphore_wait(pltpu.get_barrier_semaphore(), 2 + len(self.reached()))

    def rows_of(self, side, seq):
        return self.buffer.at[side, at(seq * self.rows, self.rows), :]

    def block(self, side, pair):
        return self.buffer.at[side, at(pair * 2 * self.rows, 2 * self.rows), :]

    def items(self, pair):
        found = [self.block(self.core, pair)]
        if self.lives is not None:
            found.append(self.lives.at[at(pair * 2, 2)])
        return found

    def each(self, copy, what):
        for index in range(1 if self.lives is None else 2):
            getattr(copy(index), what)()

    def z_copy(self, step, far):
        def copy(index):
            lane = 1 - self.x if far else self.x
            if index == 0:
                source = self.other.at[self.core] if far else self.rows_of(self.core, self.me)
                target = self.rows_of(self.core, self.me)
            else:
                source = self.live_other if far else self.lives.at[self.me]
                target = self.lives.at[self.me]
            return remote(
                source,
                target,
                self.z_send.at[step, far, index],
                self.z_recv.at[step, far, index],
                self.place(self.plane(step), lane),
                self.core,
            )

        return copy

    def y_copy(self, plane, row):
        def copy(index):
            item = self.items(plane * 2 + row)[index]
            return remote(
                item,
                item,
                self.y_send.at[plane, index],
                self.y_recv.at[plane, index],
                self.across,
                self.core,
            )

        return copy

    def c_copy(self, pair, side):
        item = self.block(side, pair)
        return remote(
            item, item, self.c_send.at[pair], self.c_recv.at[pair], self.me, 1 - self.core
        )

    def begin(self):
        for step, far in self.reached():
            self.each(self.z_copy(step, far), "start")

    def arrive(self, event):
        for far in (0, 1) if event else (1,):
            self.each(self.z_copy(event, far), "wait_recv")
        plane = self.plane(self.planes - event)
        self.each(self.y_copy(plane, self.y), "start")
        self.c_copy(plane * 2 + self.y, self.core).start()

    def complete(self, event):
        plane = self.plane(self.planes - event)
        self.each(self.y_copy(plane, 1 - self.y), "wait_recv")
        self.c_copy(plane * 2 + 1 - self.y, self.core).start()

    def ready(self, event):
        plane = self.plane(self.planes - event)
        self.c_copy(plane * 2, 1 - self.core).wait_recv()
        self.c_copy(plane * 2 + 1, 1 - self.core).wait_recv()
        return plane

    def finish(self):
        for step, far in self.reached():
            self.each(self.z_copy(step, far), "wait_send")
        for plane in range(self.planes):
            self.each(self.y_copy(plane, self.y), "wait_send")
        for pair in range(2 * self.planes):
            self.c_copy(pair, self.core).wait_send()


def split_lanes(values, x, buffer, other, start, rows):
    half = values.shape[2] // 2
    zero, one = values[:, 0, :], values[:, 1, :]
    own, far = jnp.where(x == 0, zero, one), jnp.where(x == 0, one, zero)
    core = lax.axis_index("tp")
    own = jnp.where(core == 0, own[:, :half], own[:, half:]).astype(BF16)
    buffer[core, at(start, rows), :] = own
    for side in range(2):
        other[side] = far[:, side * half : (side + 1) * half].astype(BF16)


def gather_and_project(tokens, live, episode_frames, gain, shift, qkv, bias, fixed, ahead, n):
    rows, lanes, width = tokens.shape
    half = width // 2
    total = n * rows
    chunks = total // FRAME
    per_frame = FRAME // rows
    features = qkv.shape[3]
    slots = episode_frames.shape[1]

    def kernel(*refs):
        refs = list(refs)

        def take(count):
            taken = refs[:count]
            del refs[:count]
            return taken

        tokens_ref, live_ref, counts_ref, gain_ref, shift_ref, w_any, bias_ref = take(7)
        fixed_ref, ahead_ref = take(2)
        all_ref, mask_ref, frames_ref, q_ref, k_ref, v_ref, first_ref = take(7)
        other, lives, live_other, weight, full, w_sem = take(6)
        relay = Relay(n, rows, all_ref, other, take(Relay.sems), lives, live_other)
        load = pltpu.make_async_copy(w_any.at[0], weight, w_sem)
        load.start()
        relay.hello()
        x, me = relay.x, relay.me
        split_lanes(tokens_ref[...].astype(F32), x, all_ref, other, me * rows, rows)
        lane = lax.broadcasted_iota(jnp.int32, (1, FRAME), 1)
        here = lane // rows == lax.rem(me, per_frame)
        tiles = []
        for index in range(lanes):
            alive = live_ref[index : index + 1, :].astype(F32)
            alive = jnp.where(here, jnp.concatenate([alive] * per_frame, axis=1), 0.0)
            tiles.append(jnp.broadcast_to(alive, (8, FRAME)))
        lives[me] = jnp.where(x == 0, tiles[0], tiles[1])
        live_other[...] = jnp.where(x == 0, tiles[1], tiles[0])
        relay.met()
        relay.begin()

        counts = [counts_ref[x, slot] for slot in range(slots)]
        episodes, openings = [], []
        for frame in range(chunks):
            end, episode, opening = 0, 0, 0
            for slot in range(slots):
                end = end + counts[slot]
                passed = frame >= end
                episode = episode + passed.astype(jnp.int32)
                opening = opening + jnp.where(passed, counts[slot], 0)
            episodes.append(episode)
            openings.append(frame - opening)
        for index in range(3):
            table = []
            for frame in range(chunks):
                line = jnp.zeros((1, PAIR), F32)
                for choice in range(chunks):
                    line = jnp.where(
                        openings[frame] == choice, ahead_ref[index, choice : choice + 1, :], line
                    )
                table.append(line)
            frames_ref[index] = jnp.concatenate(
                table + [jnp.zeros((8 - chunks, PAIR), F32)], axis=0
            )
        load.wait()

        def project_frame(frame):
            place = at(frame * FRAME, FRAME)
            stream = jnp.concatenate([all_ref[0, place, :], all_ref[1, place, :]], axis=1)
            project(
                stream.astype(F32),
                frame,
                0,
                me // 2,
                (gain_ref, shift_ref, weight, bias_ref, fixed_ref, frames_ref),
                [ref.at[place, :] for ref in (q_ref, k_ref, v_ref, first_ref)],
                full,
            )

        for event in range(relay.events):
            relay.arrive(event)
            if event:
                relay.complete(event - 1)
        relay.complete(relay.events - 1)

        def one_frame(event, carry):
            project_frame(relay.ready(event))
            return carry

        lax.fori_loop(0, relay.events, one_frame, 0)
        relay.finish()

        for key_frame in range(chunks):
            alive = lives[key_frame * per_frame, 0:1, :]
            for part in range(1, per_frame):
                alive = alive + lives[key_frame * per_frame + part, 0:1, :]
            closed = (alive - 1.0) * -MASKED
            lines = []
            for query_frame in range(chunks):
                allowed = (episodes[query_frame] == episodes[key_frame]) & (
                    openings[key_frame] <= openings[query_frame]
                )
                lines.append(jnp.where(allowed, closed, MASKED))
            lines.append(jnp.zeros((PAIR - chunks, FRAME), F32))
            mask_ref[key_frame * FRAME : (key_frame + 1) * FRAME, :] = jnp.concatenate(
                lines, axis=0
            ).T.astype(BF16)

    in_vmem = pl.BlockSpec(memory_space=pltpu.VMEM)
    in_smem = pl.BlockSpec(memory_space=pltpu.SMEM)
    projected = jax.ShapeDtypeStruct((total, features), BF16)
    return pl.pallas_call(
        kernel,
        out_shape=(
            jax.ShapeDtypeStruct((2, total, half), BF16),
            jax.ShapeDtypeStruct((total, PAIR), BF16),
            jax.ShapeDtypeStruct((3, 8, PAIR), F32),
            projected,
            projected,
            projected,
            jax.ShapeDtypeStruct((total, PAIR), BF16),
        ),
        in_specs=[in_vmem, in_vmem, in_smem, in_vmem, in_vmem, ANYWHERE] + [in_vmem] * 3,
        out_specs=(in_vmem,) * 7,
        scratch_shapes=[
            pltpu.VMEM((2, rows, half), BF16),
            pltpu.VMEM((n, 8, FRAME), F32),
            pltpu.VMEM((8, FRAME), F32),
            pltpu.VMEM(qkv.shape[1:], BF16),
            pltpu.VMEM((FRAME, width), BF16),
            pltpu.SemaphoreType.DMA,
        ]
        + Relay.scratch(n),
        compiler_params=pltpu.CompilerParams(
            collective_id=0, has_side_effects=True, vmem_limit_bytes=VMEM_BYTES
        ),
        name="gather_and_project",
    )(tokens, live, episode_frames, gain, shift, qkv, bias, fixed, ahead)


def halves(ref):
    return jnp.concatenate([ref[0], ref[1]], axis=1).astype(F32)


def halves_spec(shape, chunks, behind):
    return pl.BlockSpec(
        (2, FRAME, shape[2]), lambda s: (0, jnp.clip(s - behind, 0, chunks - 1), 0)
    )


def layer_forward(layer, query, key, value, key_bias, stream, mats, rows_of, next_refs, d_out, n, identity):
    total, features = query.shape
    split = stream.ndim == 3
    width = mats[1].shape[1]
    rows_here = total // n
    hidden_units = mats[1].shape[2]
    chunks = total // FRAME
    heads = features // HEAD_DIM
    slabs = features // PAIR
    columns = 512
    last = next_refs is None
    b_out, gain, shift, b_up, b_down = rows_of
    mat_out, mat_up, mat_down = mats

    def kernel(*refs):
        refs = list(refs)

        def take(count):
            taken = refs[:count]
            del refs[:count]
            return taken

        q_ref, k_ref, v_ref, kb_ref, x_ref = take(5)
        wo_any, wu_any, wd_any = take(3)
        bo_ref, gain_ref, shift_ref, bu_ref, bd_ref = take(5)
        if not last:
            wq_any, ngain, nshift, nbias, fixed, frames = take(6)
        if d_out is not None:
            (d_ref,) = take(1)
        p_ref, mixed_ref, middle_ref, second_ref, act_ref, gp_ref, x_out = take(7)
        if not last:
            nq_ref, nk_ref, nv_ref, nf_ref = take(4)
        if d_out is not None:
            (d_all,) = take(1)
        wo, wu, wd, mid, full, low = take(6)
        if not last:
            (wq,) = take(1)
        a_send, a_recv, b_send, b_recv, w_sem, send_sem, recv_sem = take(7)
        relay = None
        if d_out is not None:
            buffer, other, d_sem = take(3)
            relay = Relay(n, rows_here, buffer, other, take(Relay.sems))

        step = pl.program_id(0)
        me, core = lax.axis_index("seq"), lax.axis_index("tp")

        items = [(wo_any, wo), (wu_any, wu), (wd_any, wd)]
        if not last:
            items.append((wq_any, wq))

        def load(index):
            source, target = items[index]
            return pltpu.make_async_copy(
                source.at[layer if index < 3 else layer + 1], target, w_sem.at[index]
            )

        def exchange(kind, chunk):
            source, target = ((a_send, a_recv), (b_send, b_recv))[kind]
            return remote(
                source.at[chunk],
                target.at[chunk],
                send_sem.at[kind, chunk],
                recv_sem.at[kind, chunk],
                me,
                1 - core,
            )

        @pl.when(step == 0)
        def _():
            for index in range(len(items)):
                load(index).start()
            if relay is None:
                greet([(me, 1 - core)])
            else:
                relay.hello()
                split_lanes(d_ref[...], relay.x, buffer, other, me * rows_here, rows_here)
                relay.met()
                relay.begin()

        if relay is not None:
            for event in range(relay.events):

                @pl.when(step == 1 + event // 2)
                def _():
                    relay.arrive(event)

                @pl.when(step == 2 + event // 2)
                def _():
                    relay.complete(event)

            @pl.when(step == chunks + 1)
            def _():
                for event in range(relay.events):
                    relay.ready(event)
                relay.finish()
                pltpu.make_async_copy(buffer, d_all, d_sem).start()

        lane = lax.broadcasted_iota(jnp.int32, (1, PAIR), 1)
        sides = [(lane < HEAD_DIM).astype(F32).astype(BF16), (lane >= HEAD_DIM).astype(F32).astype(BF16)]
        for frame in range(chunks):

            @pl.when(step == frame)
            def _():
                keys = FRAME * (frame + 1)
                mask = kb_ref[:keys, :]
                asked = jnp.broadcast_to((lane == frame).astype(F32), (FRAME, PAIR)).astype(BF16)

                def one_slab(slab, carry):
                    lanes = at(slab * PAIR, PAIR)
                    q2, k2, v2 = q_ref[:, lanes], k_ref[:keys, lanes], v_ref[:keys, lanes]
                    k2 = jnp.concatenate([k2, mask], axis=1)
                    turned = v2.T
                    results = []
                    for side in range(2):
                        scores = nt(k2, jnp.concatenate([q2 * sides[side], asked], axis=1))
                        highest = jnp.max(scores, axis=0, keepdims=True)
                        shifted = jnp.exp(scores - highest)
                        summed = jnp.sum(shifted, axis=0, keepdims=True)
                        attention = (shifted * (1.0 / summed)).astype(BF16)
                        p_ref[0, slab * 2 + side, :keys, :] = attention
                        results.append(nn(turned[side * HEAD_DIM : (side + 1) * HEAD_DIM], attention))
                    mixed_ref[:, lanes] = jnp.concatenate(results, axis=0).T.astype(BF16)
                    return carry

                lax.fori_loop(0, slabs, one_slab, 0)

        @pl.when(step == 0)
        def _():
            load(0).wait()

        @pl.when(step < chunks)
        def _():
            a_send[step] = nn(mixed_ref[...], wo[...]).astype(BF16)
            exchange(0, step).start()

        @pl.when(step == 1)
        def _():
            load(1).wait()
            load(2).wait()

        @pl.when((step >= 1) & (step <= chunks))
        def _():
            chunk = step - 1
            exchange(0, chunk).wait_recv()
            middle = (halves(x_ref) if split else x_ref[...]) + (a_send[chunk].astype(F32) + a_recv[chunk].astype(F32))
            middle = middle + bo_ref[layer : layer + 1, :]
            middle_ref[...] = middle
            mid[lax.rem(chunk, 2)] = middle
            unit, _ = normed(middle)
            second = (unit * gain_ref[layer : layer + 1, :] + shift_ref[layer : layer + 1, :]).astype(BF16)
            full[...] = second
            second_ref[...] = full[:, at((me // 2) * PAIR, PAIR)]
            for start in range(0, hidden_units, columns):
                part = slice(start, start + columns)
                hidden = nn(second, wu[:, part]) + bu_ref[layer : layer + 1, part]
                act, slope = gelu_both(hidden)
                act = act.astype(BF16)
                act_ref[:, part] = act
                gp_ref[:, part] = slope.astype(BF16)
                down = nn(act, wd[part, :])
                if start == 0:
                    low[...] = down
                else:
                    low[...] += down
            b_send[chunk] = low[...].astype(BF16)
            exchange(1, chunk).start()

        if not last:

            @pl.when(step == 2)
            def _():
                load(3).wait()

        @pl.when(step >= 2)
        def _():
            chunk = step - 2
            exchange(1, chunk).wait_recv()
            result = (
                mid[lax.rem(chunk, 2)]
                + (b_send[chunk].astype(F32) + b_recv[chunk].astype(F32))
                + bd_ref[layer : layer + 1, :]
            )
            x_out[...] = result
            if not last:
                project(
                    result,
                    chunk,
                    layer + 1,
                    me // 2,
                    (ngain, nshift, wq, nbias, fixed, frames),
                    (nq_ref, nk_ref, nv_ref, nf_ref),
                    full,
                )

        @pl.when(step == chunks + 1)
        def _():
            for kind in range(2):
                for chunk in range(chunks):
                    exchange(kind, chunk).wait_send()
            if relay is not None:
                pltpu.make_async_copy(buffer, d_all, d_sem).wait()

    def rows(columns, behind):
        return pl.BlockSpec(
            (FRAME, columns), lambda s: (jnp.clip(s - behind, 0, chunks - 1), 0)
        )

    in_specs = [rows(features, 0), whole(key), whole(value), whole(key_bias)]
    in_specs += [halves_spec(stream.shape, chunks, 1) if split else rows(width, 1)]
    in_specs += [ANYWHERE] * 3 + [whole(item) for item in rows_of]
    operands = [query, key, value, key_bias, stream, *mats, *rows_of]
    if not last:
        in_specs += [ANYWHERE] + [whole(item) for item in next_refs[1:]]
        operands += list(next_refs)
    if d_out is not None:
        in_specs += [whole(d_out)]
        operands += [d_out]
    out_shape = [
        jax.ShapeDtypeStruct((chunks, heads, total, FRAME), BF16),
        jax.ShapeDtypeStruct((total, features), BF16),
        jax.ShapeDtypeStruct((total, width), F32),
        jax.ShapeDtypeStruct((total, PAIR), BF16),
        jax.ShapeDtypeStruct((total, hidden_units), BF16),
        jax.ShapeDtypeStruct((total, hidden_units), BF16),
        jax.ShapeDtypeStruct((total, width), F32),
    ]
    out_specs = [
        pl.BlockSpec((1, heads, total, FRAME), lambda s: (jnp.minimum(s, chunks - 1), 0, 0, 0)),
        rows(features, 0),
        rows(width, 1),
        rows(PAIR, 1),
        rows(hidden_units, 1),
        rows(hidden_units, 1),
        rows(width, 2),
    ]
    scratch = [
        pltpu.VMEM(mat_out.shape[1:], BF16),
        pltpu.VMEM(mat_up.shape[1:], BF16),
        pltpu.VMEM(mat_down.shape[1:], BF16),
        pltpu.VMEM((2, FRAME, width), F32),
        pltpu.VMEM((FRAME, width), BF16),
        pltpu.VMEM((FRAME, width), F32),
    ]
    if not last:
        out_shape += [jax.ShapeDtypeStruct((total, features), BF16)] * 3
        out_shape += [jax.ShapeDtypeStruct((total, PAIR), BF16)]
        out_specs += [rows(features, 2)] * 3 + [rows(PAIR, 2)]
    if d_out is not None:
        out_shape += [jax.ShapeDtypeStruct((2, total, width // 2), BF16)]
        out_specs += [ANYWHERE]
        scratch += [pltpu.VMEM(next_refs[0].shape[1:], BF16)]
    scratch += [pltpu.VMEM((chunks, FRAME, width), BF16)] * 4
    scratch += [
        pltpu.SemaphoreType.DMA((4,)),
        pltpu.SemaphoreType.DMA((2, chunks)),
        pltpu.SemaphoreType.DMA((2, chunks)),
    ]
    if d_out is not None:
        scratch += [
            pltpu.VMEM((2, total, width // 2), BF16),
            pltpu.VMEM((2, rows_here, width // 2), BF16),
            pltpu.SemaphoreType.DMA,
        ]
        scratch += Relay.scratch(n)
    return pl.pallas_call(
        kernel,
        grid=(chunks + 2,),
        out_shape=out_shape,
        in_specs=in_specs,
        out_specs=out_specs,
        scratch_shapes=scratch,
        compiler_params=pltpu.CompilerParams(
            collective_id=identity, has_side_effects=True, vmem_limit_bytes=VMEM_BYTES
        ),
        name=f"layer_forward_{layer}",
    )(*operands)


def attention_backward(probs, query, key, value, grad_mixed, fixed, frames, ships, lane_rows, identity):
    total, features = query.shape
    chunks = total // FRAME
    slabs = features // PAIR
    half = PAIR // 2
    ship_count, row_count = len(ships), len(lane_rows)

    def kernel(*refs):
        refs = list(refs)

        def take(count):
            taken = refs[:count]
            del refs[:count]
            return taken

        p_ref, q_ref, k_ref, v_ref, g_ref, fixed_ref, frames_ref = take(7)
        ship_refs, row_refs = take(ship_count), take(row_count)
        dq_ref, dk_ref, dv_ref = take(3)
        ship_outs, row_outs = take(ship_count), take(row_count)
        dk_sum, dv_sum = take(2)
        ship_sends, ship_recvs = take(ship_count), take(ship_count)
        send_sem, recv_sem = take(2)

        step = pl.program_id(0)
        me, core = lax.axis_index("seq"), lax.axis_index("tp")
        x = lax.rem(me, 2)
        beside = me + 1 - 2 * x

        def copies():
            items = [
                (send, recv) for send, recv in zip(ship_sends, ship_recvs)
            ]
            for (_, count), ref, out in zip(lane_rows, row_refs, row_outs):
                items.append((ref.at[at(beside * count, count), :] if count else ref, out))
            return [
                remote(source, target, send_sem.at[i], recv_sem.at[i], beside, core)
                for i, (source, target) in enumerate(items)
            ]

        @pl.when(step == 0)
        def _():
            greet([(beside, core)])
            for ref, send in zip(ship_refs, ship_sends):
                send[...] = ref[at((1 - x) * half, half), :].astype(BF16)
            for copy in copies():
                copy.start()

        lane = lax.broadcasted_iota(jnp.int32, (1, PAIR), 1)
        sides = [(lane < HEAD_DIM).astype(F32).astype(BF16), (lane >= HEAD_DIM).astype(F32).astype(BF16)]
        turned = k_ref[...].T
        for frame in reversed(range(chunks)):
            keys = FRAME * (frame + 1)
            own = slice(frame * FRAME, keys)
            tables = tables_of(fixed_ref, frames_ref, frame)
            query_parts, score_parts, prob_parts, q_parts, g_parts = [], [], [], [], []
            for side in range(2):
                g2 = g_ref[own, :] * sides[side]
                attention = p_ref[frame, side, :keys, :]
                grad = nt(v_ref[:keys, :], g2)
                wide = attention.astype(F32)
                inner = jnp.sum(wide * grad, axis=0, keepdims=True)
                grad_scores = (wide * (grad - inner)).astype(BF16)
                query_parts.append(nn(turned[side * HEAD_DIM : (side + 1) * HEAD_DIM, :keys], grad_scores))
                score_parts.append(grad_scores)
                prob_parts.append(attention)
                q_parts.append(q_ref[own, :] * sides[side])
                g_parts.append(g2)
            grad_query = jnp.concatenate(query_parts, axis=0).T
            key_parts = nn(jnp.concatenate(score_parts, axis=1), jnp.concatenate(q_parts, axis=0))
            value_parts = nn(jnp.concatenate(prob_parts, axis=1), jnp.concatenate(g_parts, axis=0))
            dq_ref[own, :] = (turn(grad_query, tables, True) * SCORE_SCALE).astype(BF16)
            if frame == chunks - 1:
                dk_sum[...] = key_parts
                dv_sum[...] = value_parts
            else:
                dk_sum[:keys, :] += key_parts
                dv_sum[:keys, :] += value_parts
            dk_ref[own, :] = turn(dk_sum[own, :], tables, True).astype(BF16)
            dv_ref[own, :] = dv_sum[own, :].astype(BF16)

        @pl.when(step == slabs - 1)
        def _():
            for copy in copies():
                copy.wait_recv()
            for ref, recv, out in zip(ship_refs, ship_recvs, ship_outs):
                out[...] = ref[at(x * half, half), :] + recv[...].astype(F32)
            for copy in copies():
                copy.wait_send()

    slab = pl.BlockSpec((total, PAIR), lambda s: (0, s))
    in_specs = [pl.BlockSpec((chunks, 2, total, FRAME), lambda s: (0, s, 0, 0))]
    in_specs += [slab] * 4 + [whole(fixed), whole(frames)]
    in_specs += [whole(item) for item in ships] + [ANYWHERE] * row_count
    out_shape = [jax.ShapeDtypeStruct((total, features), BF16)] * 3
    out_specs = [slab] * 3
    for item in ships:
        out_shape.append(jax.ShapeDtypeStruct((half, item.shape[1]), F32))
        out_specs.append(whole_out((half, item.shape[1])))
    for item, count in lane_rows:
        shape = (count or item.shape[0], item.shape[1])
        out_shape.append(jax.ShapeDtypeStruct(shape, item.dtype))
        out_specs.append(ANYWHERE)
    scratch = [pltpu.VMEM((total, PAIR), F32)] * 2
    scratch += [pltpu.VMEM((half, item.shape[1]), BF16) for item in ships] * 2
    scratch += [pltpu.SemaphoreType.DMA((ship_count + row_count,))] * 2
    return pl.pallas_call(
        kernel,
        grid=(slabs,),
        out_shape=out_shape,
        in_specs=in_specs,
        out_specs=out_specs,
        scratch_shapes=scratch,
        compiler_params=pltpu.CompilerParams(
            collective_id=identity, has_side_effects=True, vmem_limit_bytes=VMEM_BYTES
        ),
        name=f"attention_backward_{identity}",
    )(probs, query, key, value, grad_mixed, fixed, frames, *ships, *[item for item, _ in lane_rows])


def rows_backward(entry, upper, identity):
    top, bottom = len(entry) == 1, upper is None
    if not top:
        above, entry = entry[0], entry[1:]
        split = entry[3].ndim == 3
    total = entry[0].shape[1] if top else entry[0].shape[0]
    chunks = total // FRAME
    columns = 512
    ahead = 0 if top else 1
    if top:
        width = 2 * entry[0].shape[2]
    else:
        features, width = entry[0].shape[1], entry[4].shape[1]
    if not bottom:
        layer = upper[0]
        hidden_units, mixed_features = upper[1].shape[1], upper[5].shape[1]
    half = PAIR // 2
    place_rows = total // lax.axis_size("seq")

    def kernel(*refs):
        refs = list(refs)

        def take(count):
            taken = refs[:count]
            del refs[:count]
            return taken

        if top:
            (d_out_ref,) = take(1)
        else:
            dq_ref, dk_ref, dv_ref, x_ref, dm_ref, first_ref, wq, gain1 = take(8)
        if not bottom:
            act_ref, gp_ref, middle_ref, second_ref, mixed_ref = take(5)
            wo_any, wu_any, wd_any, gain2 = take(4)
        if not top:
            qkv_sum, vec1 = take(2)
        if not bottom:
            dmid_out, dmix_out, out_sum, up_sum, down_sum, vec2 = take(6)
        else:
            dx_out, dx_other, vec_other = take(3)
        if not top:
            a_send, a_recv = take(2)
        if not bottom:
            b_send, b_recv, grad_keep, part_keep, low_keep, wo, wu, wd, w_sem = take(9)
        else:
            dx_keep, dx_recv, vec_recv, qkv_send, qkv_recv, x_send_sem, x_recv_sem = take(7)
        send_sem, recv_sem = take(2)

        step = pl.program_id(0)
        me, core = lax.axis_index("seq"), lax.axis_index("tp")
        pair = at((me // 2) * PAIR, PAIR)
        x = lax.rem(me, 2)
        beside = me + 1 - 2 * x

        def exchange(kind, chunk):
            source, target = (a_send, a_recv) if kind == 0 else (b_send, b_recv)
            return remote(
                source.at[chunk],
                target.at[chunk],
                send_sem.at[kind, chunk],
                recv_sem.at[kind, chunk],
                me,
                1 - core,
            )

        def load(index):
            source, target = ((wd_any, wd), (wu_any, wu), (wo_any, wo))[index]
            return pltpu.make_async_copy(source.at[layer], target, w_sem.at[index])

        @pl.when(step == 0)
        def _():
            if not bottom:
                for index in range(3):
                    load(index).start()
                out_sum[...] = jnp.zeros_like(out_sum)
                up_sum[...] = jnp.zeros_like(up_sum)
                down_sum[...] = jnp.zeros_like(down_sum)
                vec2[...] = jnp.zeros_like(vec2)
            if not top:
                qkv_sum[...] = jnp.zeros_like(qkv_sum)
                vec1[...] = jnp.zeros_like(vec1)
            greet([(me, 1 - core)] + ([(beside, core)] if bottom else []))

        if not top:

            @pl.when(step < chunks)
            def _():
                first = first_ref[...]
                partial = None
                for part, ref in enumerate((dq_ref, dk_ref, dv_ref)):
                    piece = slice(part * features, (part + 1) * features)
                    grad = ref[...]
                    term = nt(grad, wq[0, part])
                    partial = term if partial is None else partial + term
                    qkv_sum[:, piece] += tn(first, grad)
                    vec1[0:1, piece] += column_sum(grad.astype(F32))
                a_send[step] = partial.astype(BF16)
                exchange(0, step).start()

        @pl.when((step >= ahead) & (step < chunks + ahead))
        def _():
            chunk = step - ahead
            if top:
                gradient = halves(d_out_ref)
            else:
                exchange(0, chunk).wait_recv()
                grad_first = a_send[chunk].astype(F32) + a_recv[chunk].astype(F32)
                unit, scale = normed(halves(x_ref) if split else x_ref[...])
                vec1[1:2, :width] += column_sum(grad_first * unit)
                vec1[2:3, :width] += column_sum(grad_first)
                gradient = dm_ref[...] + norm_pull(
                    grad_first, gain1[above : above + 1, :], unit, scale
                )
            if bottom:
                dx_keep[at(chunk * FRAME, FRAME), :] = gradient
                return

            @pl.when(chunk == 0)
            def _():
                load(0).wait()
                load(1).wait()

            grad_keep[lax.rem(chunk, 2)] = gradient
            vec2[1:2, :width] += column_sum(gradient)
            low = gradient.astype(BF16)
            low_keep[...] = low
            low_columns = low_keep[:, pair]
            second = second_ref[...]
            for start in range(0, hidden_units, columns):
                part = slice(start, start + columns)
                down_sum[:, part] += tn(low_columns, act_ref[:, part])
                grad_act = nt(low, wd[part, :])
                grad_hidden = (grad_act * gp_ref[:, part].astype(F32)).astype(BF16)
                vec2[0:1, part] += column_sum(grad_hidden.astype(F32))
                up_sum[:, part] += tn(second, grad_hidden)
                term = nt(grad_hidden, wu[:, part])
                if start == 0:
                    part_keep[...] = term
                else:
                    part_keep[...] += term
            b_send[chunk] = part_keep[...].astype(BF16)
            exchange(1, chunk).start()

        if not bottom:

            @pl.when(step == ahead + 1)
            def _():
                load(2).wait()

            @pl.when(step >= ahead + 1)
            def _():
                chunk = step - ahead - 1
                exchange(1, chunk).wait_recv()
                grad_second = b_send[chunk].astype(F32) + b_recv[chunk].astype(F32)
                unit, scale = normed(middle_ref[...])
                vec2[2:3, :width] += column_sum(grad_second * unit)
                vec2[3:4, :width] += column_sum(grad_second)
                grad_middle = grad_keep[lax.rem(chunk, 2)] + norm_pull(
                    grad_second, gain2[layer : layer + 1, :], unit, scale
                )
                dmid_out[...] = grad_middle
                vec2[4:5, :width] += column_sum(grad_middle)
                low = grad_middle.astype(BF16)
                low_keep[...] = low
                out_sum[...] += tn(low_keep[:, pair], mixed_ref[...])
                dmix_out[...] = nt(low, wo[...]).astype(BF16)

        if bottom:

            def x_copy(index):
                source, target = (
                    (qkv_send, qkv_recv),
                    (dx_keep.at[at(beside * place_rows, place_rows), :], dx_recv),
                    (vec1, vec_recv),
                )[index]
                return remote(
                    source, target, x_send_sem.at[index], x_recv_sem.at[index], beside, core
                )

            @pl.when(step == chunks - 1)
            def _():
                qkv_send[...] = qkv_sum[at((1 - x) * half, half), :].astype(BF16)
                x_copy(0).start()

            @pl.when(step == chunks)
            def _():
                x_copy(1).start()
                x_copy(2).start()
                dx_out[...] = dx_keep[at(me * place_rows, place_rows), :]
                for index in range(3):
                    x_copy(index).wait_recv()
                qkv_sum[at(x * half, half), :] += qkv_recv[...].astype(F32)
                dx_other[...] = dx_recv[...]
                for index in range(3):
                    x_copy(index).wait_send()
                vec_other[...] = vec_recv[...]

        @pl.when(step == pl.num_programs(0) - 1)
        def _():
            for kind in ([] if top else [0]) + ([] if bottom else [1]):
                for chunk in range(chunks):
                    exchange(kind, chunk).wait_send()

    def rows(columns, behind):
        return pl.BlockSpec(
            (FRAME, columns), lambda s: (jnp.clip(s - behind, 0, chunks - 1), 0)
        )

    vec = jax.ShapeDtypeStruct((8, VEC), F32)
    operands, in_specs, out_shape, out_specs, scratch = [], [], [], [], []
    if top:
        operands += list(entry)
        in_specs += [halves_spec(entry[0].shape, chunks, 0)]
    else:
        operands += list(entry)
        in_specs += [rows(features, 0)] * 3
        in_specs += [halves_spec(entry[3].shape, chunks, 1) if split else rows(width, 1)]
        in_specs += [rows(width, 1), rows(PAIR, 0)]
        in_specs += [
            pl.BlockSpec(
                (1, *entry[6].shape[1:]),
                lambda s: (above, 0, 0, 0),
                pipeline_mode=pl.Buffered(1),
            ),
            whole(entry[7]),
        ]
        out_shape += [jax.ShapeDtypeStruct((PAIR, 3 * features), F32), vec]
        out_specs += [whole_out((PAIR, 3 * features)), whole_out((8, VEC))]
        scratch += [pltpu.VMEM((chunks, FRAME, width), BF16)] * 2
    if not bottom:
        operands += list(upper[1:])
        in_specs += [rows(hidden_units, ahead)] * 2 + [rows(width, ahead + 1), rows(PAIR, ahead)]
        in_specs += [rows(mixed_features, ahead + 1)] + [ANYWHERE] * 3 + [whole(upper[9])]
        sums = [mixed_features, hidden_units, hidden_units]
        out_shape += [
            jax.ShapeDtypeStruct((total, width), F32),
            jax.ShapeDtypeStruct((total, mixed_features), BF16),
        ]
        out_shape += [jax.ShapeDtypeStruct((PAIR, size), F32) for size in sums] + [vec]
        out_specs += [rows(width, ahead + 1), rows(mixed_features, ahead + 1)]
        out_specs += [whole_out((PAIR, size)) for size in sums] + [whole_out((8, VEC))]
        scratch += [pltpu.VMEM((chunks, FRAME, width), BF16)] * 2
        scratch += [
            pltpu.VMEM((2, FRAME, width), F32),
            pltpu.VMEM((FRAME, width), F32),
            pltpu.VMEM((FRAME, width), BF16),
            pltpu.VMEM(upper[6].shape[1:], BF16),
            pltpu.VMEM(upper[7].shape[1:], BF16),
            pltpu.VMEM(upper[8].shape[1:], BF16),
            pltpu.SemaphoreType.DMA((3,)),
        ]
    else:
        out_shape += [
            jax.ShapeDtypeStruct((place_rows, width), F32),
            jax.ShapeDtypeStruct((place_rows, width), F32),
            vec,
        ]
        out_specs += [whole_out((place_rows, width))] * 2 + [whole_out((8, VEC))]
        scratch += [
            pltpu.VMEM((total, width), F32),
            pltpu.VMEM((place_rows, width), F32),
            pltpu.VMEM((8, VEC), F32),
            pltpu.VMEM((half, 3 * features), BF16),
            pltpu.VMEM((half, 3 * features), BF16),
            pltpu.SemaphoreType.DMA((3,)),
            pltpu.SemaphoreType.DMA((3,)),
        ]
    scratch += [pltpu.SemaphoreType.DMA((2, chunks))] * 2
    return pl.pallas_call(
        kernel,
        grid=(chunks + (1 if top or bottom else 2),),
        out_shape=out_shape,
        in_specs=in_specs,
        out_specs=out_specs,
        scratch_shapes=scratch,
        compiler_params=pltpu.CompilerParams(
            collective_id=identity, has_side_effects=True, vmem_limit_bytes=VMEM_BYTES
        ),
        name=f"rows_backward_{identity}",
    )(*operands)


def assemble(sums, vecs, lanes, qkv_sum, n, features, hidden_units):
    place = lanes[1].shape[0]
    width = lanes[1].shape[1]
    half = PAIR // 2

    def kernel(*refs):
        refs = list(refs)

        def take(count):
            taken = refs[:count]
            del refs[:count]
            return taken

        (qkv_low,) = take(1)
        qkv_high = take(LAYERS - 1)
        outs, ups, downs = take(LAYERS), take(LAYERS), take(LAYERS)
        vec_refs = [take(4) for _ in range(LAYERS)]
        out_own, out_other, dx_own, dx_other = take(4)
        out_ref, dx_ref, gain1, shift1, g_qkv, b_qkv, g_out, b_out = take(8)
        gain2, shift2, g_up, b_up, g_down, b_down = take(6)
        me = lax.axis_index("seq")
        x = lax.rem(me, 2)
        pair = at((me // 2) * PAIR, PAIR)

        for part in range(3):
            piece = slice(part * features, (part + 1) * features)
            g_qkv[0, part] = qkv_low[at(x * half, half), piece]
            for layer, ref in enumerate(qkv_high):
                g_qkv[layer + 1, part] = ref[:, piece]
        for layer in range(LAYERS):
            for ref, target in ((outs, g_out), (ups, g_up), (downs, g_down)):
                target[layer] = ref[layer][...]

        for layer, (entry_own, entry_other, upper_own, upper_other) in enumerate(vec_refs):
            line = slice(layer, layer + 1)
            for part in range(3):
                piece = slice(part * features, (part + 1) * features)
                b_qkv[part, line, :] = entry_own[0:1, piece] + entry_other[0:1, piece]
            b_up[line, :] = upper_own[0:1, :hidden_units] + upper_other[0:1, :hidden_units]

            def owned(mine, other, row):
                both = mine[row : row + 1, pair] + other[row : row + 1, pair]
                return jnp.where(x == 0, both[:, :half], both[:, half:])

            gain1[line, :] = owned(entry_own, entry_other, 1)
            shift1[line, :] = owned(entry_own, entry_other, 2)
            b_down[line, :] = owned(upper_own, upper_other, 1)
            gain2[line, :] = owned(upper_own, upper_other, 2)
            shift2[line, :] = owned(upper_own, upper_other, 3)
            b_out[line, :] = owned(upper_own, upper_other, 4)

        def both_lanes(target, mine, other):
            target[:, 0, :] = jnp.where(x == 0, mine, other)
            target[:, 1, :] = jnp.where(x == 0, other, mine)

        both_lanes(dx_ref, dx_own[...], dx_other[...])
        both_lanes(out_ref, out_own[...], out_other[...])

    def f32(*shape):
        return jax.ShapeDtypeStruct(shape, F32)

    in_vmem = pl.BlockSpec(memory_space=pltpu.VMEM)
    flat = [qkv_sum] + [sums[layer][0] for layer in range(1, LAYERS)]
    for kind in range(1, 4):
        flat += [sums[layer][kind] for layer in range(LAYERS)]
    for layer in range(LAYERS):
        flat += list(vecs[layer])
    flat += list(lanes)
    small = f32(LAYERS, width // n)
    return pl.pallas_call(
        kernel,
        out_shape=(
            f32(place, 2, width),
            f32(place, 2, width),
            small,
            small,
            f32(LAYERS, 3, half, features),
            f32(3, LAYERS, features),
            f32(LAYERS, half, features),
            small,
            small,
            small,
            f32(LAYERS, half, hidden_units),
            f32(LAYERS, hidden_units),
            f32(LAYERS, half, hidden_units),
            small,
        ),
        in_specs=[in_vmem] * len(flat),
        out_specs=(in_vmem,) * 14,
        compiler_params=pltpu.CompilerParams(vmem_limit_bytes=VMEM_BYTES),
        name="assemble",
    )(*flat)


def per_chip(
    tokens,
    d_out,
    norm1_gain,
    norm1_shift,
    w_qkv,
    b_qkv,
    w_out,
    b_out,
    norm2_gain,
    norm2_shift,
    w_up,
    b_up,
    w_down,
    b_down,
    episode_frames,
    live,
):
    n = lax.axis_size("seq")
    rows = tokens.shape[0]
    features = w_qkv.shape[3]
    fixed, ahead = turn_constants(rows * n // FRAME)
    qkv, qkv_bias = w_qkv.transpose(0, 2, 1, 3), b_qkv.transpose(1, 0, 2)

    gathered, key_bias, frames, query, key, value, first = gather_and_project(
        tokens, live.T, episode_frames, norm1_gain, norm1_shift, qkv, qkv_bias, fixed, ahead, n
    )
    streams, kept, d_lane = [gathered], [], None
    for layer in range(LAYERS):
        following = None
        if layer + 1 < LAYERS:
            following = (qkv, norm1_gain, norm1_shift, qkv_bias, fixed, frames)
        results = layer_forward(
            layer,
            query,
            key,
            value,
            key_bias,
            streams[layer],
            (w_out, w_up, w_down),
            (b_out, norm2_gain, norm2_shift, b_up, b_down),
            following,
            d_out if layer == 0 else None,
            n,
            1 + layer,
        )
        kept.append((query, key, value, first, *results[:6]))
        streams.append(results[6])
        if following is not None:
            query, key, value, first = results[7:11]
        if layer == 0:
            d_lane = results[-1]

    sums = [[None] * 4 for _ in range(LAYERS)]
    vecs = [[None] * 4 for _ in range(LAYERS)]
    entry, pending, pending_rows = (d_lane,), [], [(streams[LAYERS], rows)]
    out_other = None
    for layer in reversed(range(LAYERS)):
        query, key, value, first, probs, mixed, middle, second, act, slope = kept[layer]
        upper = (
            layer,
            act,
            slope,
            middle,
            second,
            mixed,
            w_out,
            w_up,
            w_down,
            norm2_gain,
        )
        results = rows_backward(entry, upper, 1 + LAYERS + 2 * (LAYERS - 1 - layer))
        if layer + 1 < LAYERS:
            qkv_sum, vec1 = results[:2]
            results = results[2:]
            pending = [(0, layer + 1, qkv_sum)]
            pending_rows = [(vec1, 0)]
        grad_middle, grad_mixed, out_sum, up_sum, down_sum, vec2 = results
        pending = pending + [(1, layer, out_sum), (2, layer, up_sum), (3, layer, down_sum)]
        pending_rows = pending_rows + [(vec2, 0)]
        results = attention_backward(
            probs,
            query,
            key,
            value,
            grad_mixed,
            fixed,
            frames,
            [item for _, _, item in pending],
            pending_rows,
            2 + LAYERS + 2 * (LAYERS - 1 - layer),
        )
        grad_query, grad_key, grad_value = results[:3]
        swapped = results[3:]
        for (kind, owner, _), item in zip(pending, swapped):
            sums[owner][kind] = item
        others = swapped[len(pending) :]
        if out_other is None:
            out_other = others[0]
        else:
            vecs[layer + 1][:2] = [pending_rows[0][0], others[0]]
        vecs[layer][2:] = [vec2, others[1]]
        entry = (
            layer,
            grad_query,
            grad_key,
            grad_value,
            streams[layer],
            grad_middle,
            first,
            qkv,
            norm1_gain,
        )
    qkv_sum, vec1, dx_own, dx_other, vec_other = rows_backward(entry, None, 1 + 3 * LAYERS)
    vecs[0][:2] = [vec1, vec_other]
    results = list(
        assemble(
            sums,
            vecs,
            (
                lax.dynamic_slice_in_dim(streams[LAYERS], lax.axis_index("seq") * rows, rows, 0),
                out_other,
                dx_own,
                dx_other,
            ),
            qkv_sum,
            n,
            features,
            w_up.shape[2],
        )
    )
    results[4] = results[4].transpose(0, 2, 1, 3)
    results[5] = results[5].transpose(1, 0, 2)
    results[6] = results[6].transpose(0, 2, 1)
    results[12] = results[12].transpose(0, 2, 1)
    return tuple(results)


def lane_fits(mesh, tokens):
    n = mesh.shape["seq"]
    positions, lanes, width = tokens.shape
    rows = positions // n
    return (
        lanes == 2
        and n % 4 == 0
        and positions <= 4 * FRAME
        and positions % FRAME == 0
        and FRAME % rows == 0
        and width // n * 2 == PAIR
        and mesh.shape["tp"] == 2
    )


def solution(mesh):
    placed = (
        P("seq", None, None),
        P("seq", None, None),
        P(),
        P(),
        P(None, None, None, "tp"),
        P(None, None, "tp"),
        P(None, "tp", None),
        P(),
        P(),
        P(),
        P(None, None, "tp"),
        P(None, "tp"),
        P(None, "tp", None),
        P(),
        P(),
        P("seq", None),
    )
    def mapped(body):
        return jax.shard_map(
            body,
            mesh=mesh,
            in_specs=placed,
            out_specs=(
                P("seq", None, None),
                P("seq", None, None),
                P(None, "seq"),
                P(None, "seq"),
                P(None, "seq", None, "tp"),
                P(None, None, "tp"),
                P(None, "tp", "seq"),
                P(None, "seq"),
                P(None, "seq"),
                P(None, "seq"),
                P(None, "seq", "tp"),
                P(None, "tp"),
                P(None, "tp", "seq"),
                P(None, "seq"),
            ),
            check_vma=False,
        )

    def run(tokens, *others):
        if lane_fits(mesh, tokens):
            return mapped(per_chip)(tokens, *others)
        return mapped(per_device)(tokens, *others)

    return run
```

```python
import math

import jax
import jax.numpy as jnp
import numpy as np
from jax import lax
from jax.experimental import pallas as pl
from jax.experimental.pallas import tpu as pltpu
from jax.sharding import PartitionSpec as P

HEAD_DIM = 64
GRID = 16
FRAME = 256
LAYERS = 2
MICRO = 2


EPSILON = 1e-06
MASKED = -1e30
SCORE_SCALE = 0.125


def layer_norm(stream, norm_gain, norm_shift):
    center = stream - jnp.mean(stream, axis=-1, keepdims=True)
    spread = jnp.mean(center * center, axis=-1, keepdims=True)
    return center * lax.rsqrt(spread + EPSILON) * norm_gain + norm_shift


def rotate(values, frame_place, row_place, column_place):
    frequency = jnp.exp(jnp.arange(10, dtype=jnp.float32) * (-math.log(10000.0) / 10.0))
    pieces = []
    for section, place in enumerate((frame_place, row_place, column_place)):
        lower = values[..., 20 * section : 20 * section + 10]
        upper = values[..., 20 * section + 10 : 20 * section + 20]
        angles = place.astype(jnp.float32)[..., None, None] * frequency
        cosine = jnp.cos(angles)
        sine_part = jnp.sin(angles)
        pieces.append(lower * cosine - upper * sine_part)
        pieces.append(lower * sine_part + upper * cosine)
    pieces.append(values[..., 60:])
    return jnp.concatenate(pieces, axis=-1)


def episode_tags(frame_counts, positions):
    endings = jnp.cumsum(frame_counts) * FRAME
    passed = (positions[:, None] >= endings[None, :]).astype(jnp.int32)
    episode = jnp.sum(passed, axis=1)
    opening = jnp.sum(passed * frame_counts[None, :], axis=1)
    frame_index = positions // FRAME - opening
    within = positions % FRAME
    return (episode, frame_index, within // GRID, within % GRID)


def gelu_exact(values):
    return jax.nn.gelu(values, approximate=False)


def sum_heads(partial_sum):
    return lax.psum(partial_sum.astype(jnp.bfloat16), "tp").astype(jnp.float32)


def sum_inputs(partial_sum):
    return lax.psum(partial_sum.astype(jnp.bfloat16), "tp").astype(jnp.float32)


def lane_scores(query, keys_all, lane_index, query_tags, key_tags):
    head_count = query.shape[2] // HEAD_DIM
    query_lane = lax.dynamic_index_in_dim(query, lane_index, 1, False).reshape(
        query.shape[0], head_count, HEAD_DIM
    )
    keys_lane = lax.dynamic_index_in_dim(keys_all, lane_index, 1, False).reshape(
        keys_all.shape[0], head_count, HEAD_DIM
    )
    query_episode, query_frame = [
        lax.dynamic_index_in_dim(item, lane_index, 1, False) for item in query_tags
    ]
    key_episode, key_frame, key_live = [
        lax.dynamic_index_in_dim(item, lane_index, 1, False) for item in key_tags
    ]
    allowed = (
        (query_episode[:, None] == key_episode[None, :])
        & (key_frame[None, :] <= query_frame[:, None])
        & (key_live[None, :] > 0)
    )
    scores = (
        jnp.einsum("qhd,khd->hqk", query_lane, keys_lane, preferred_element_type=jnp.float32)
        * SCORE_SCALE
    )
    return (jnp.where(allowed[None], scores, MASKED), query_lane, keys_lane)


def attend_forward(query, keys_all, values_all, query_tags, key_tags):
    rows_dev, lane_count, features = query.shape
    head_count = features // HEAD_DIM

    def one_lane(lane_index, carry):
        scores, query_lane, keys_lane = lane_scores(
            query, keys_all, lane_index, query_tags, key_tags
        )
        highest = jnp.max(scores, axis=-1, keepdims=True)
        shifted = jnp.exp(scores - highest)
        summed = jnp.sum(shifted, axis=-1, keepdims=True)
        attention = (shifted / summed).astype(jnp.bfloat16)
        values_lane = lax.dynamic_index_in_dim(values_all, lane_index, 1, False).reshape(
            values_all.shape[0], head_count, HEAD_DIM
        )
        result = jnp.einsum(
            "hqk,khd->qhd", attention, values_lane, preferred_element_type=jnp.float32
        ).reshape(rows_dev, 1, features)
        log_total = (highest + jnp.log(summed))[None, :, :, 0]
        return (result, log_total)

    initial = (
        jnp.zeros((rows_dev, lane_count, features), jnp.float32),
        jnp.zeros((lane_count, head_count, rows_dev), jnp.float32),
    )
    return lax.fori_loop(0, lane_count, one_lane, initial)


def attend_backward(query, keys_all, values_all, log_total, grad_mixed, query_tags, key_tags):
    rows_dev, lane_count, features = query.shape
    head_count = features // HEAD_DIM
    key_rows = keys_all.shape[0]

    def one_lane(lane_index, carry):
        scores, query_lane, keys_lane = lane_scores(
            query, keys_all, lane_index, query_tags, key_tags
        )
        values_lane = lax.dynamic_index_in_dim(values_all, lane_index, 1, False).reshape(
            key_rows, head_count, HEAD_DIM
        )
        grad_lane = lax.dynamic_index_in_dim(grad_mixed, lane_index, 1, False).reshape(
            rows_dev, head_count, HEAD_DIM
        )
        attention = jnp.exp(
            scores - lax.dynamic_index_in_dim(log_total, lane_index, 0, False)[:, :, None]
        )
        grad_attention = jnp.einsum(
            "qhd,khd->hqk", grad_lane, values_lane, preferred_element_type=jnp.float32
        )
        inner = jnp.sum(attention * grad_attention, axis=-1, keepdims=True)
        grad_scores = (attention * (grad_attention - inner)).astype(jnp.bfloat16)
        query_part = (
            jnp.einsum("hqk,khd->qhd", grad_scores, keys_lane, preferred_element_type=jnp.float32)
            * SCORE_SCALE
        )
        key_part = (
            jnp.einsum("hqk,qhd->khd", grad_scores, query_lane, preferred_element_type=jnp.float32)
            * SCORE_SCALE
        )
        value_part = jnp.einsum(
            "hqk,qhd->khd",
            attention.astype(jnp.bfloat16),
            grad_lane,
            preferred_element_type=jnp.float32,
        )
        stacked = jnp.stack(
            [key_part.reshape(key_rows, features), value_part.reshape(key_rows, features)], axis=1
        )
        key_terms = stacked[:, None]
        grad_query = query_part.reshape(rows_dev, 1, features)
        return (grad_query, key_terms)

    initial = (
        jnp.zeros((rows_dev, lane_count, features), jnp.float32),
        jnp.zeros((key_rows, lane_count, 2, features), jnp.float32),
    )
    return lax.fori_loop(0, lane_count, one_lane, initial)


def front(stream, layer_index, params, query_tags, key_tags, positions):
    (
        gain_one,
        shift_one,
        mat_qkv,
        bias_qkv,
        mat_out,
        bias_out,
        gain_two,
        shift_two,
        mat_up,
        bias_up,
        mat_down,
        bias_down,
    ) = [item[layer_index] for item in params]
    rows_dev, lane_count, width = stream.shape
    features = mat_qkv.shape[2]
    head_count = features // HEAD_DIM
    frame_place, row_place, column_place = positions
    first = layer_norm(stream, gain_one, shift_one).astype(jnp.bfloat16)
    projected = (
        jnp.einsum("tbd,dcf->tbcf", first, mat_qkv, preferred_element_type=jnp.float32) + bias_qkv
    )
    split = projected.reshape(rows_dev, lane_count, 3, head_count, HEAD_DIM)
    query = (
        rotate(split[:, :, 0], frame_place, row_place, column_place)
        .reshape(rows_dev, lane_count, features)
        .astype(jnp.bfloat16)
    )
    keys = (
        rotate(split[:, :, 1], frame_place, row_place, column_place)
        .reshape(rows_dev, lane_count, features)
        .astype(jnp.bfloat16)
    )
    values = projected[:, :, 2].astype(jnp.bfloat16)
    keys_all, values_all = (
        lax.all_gather(keys, "seq", axis=0, tiled=True),
        lax.all_gather(values, "seq", axis=0, tiled=True),
    )
    mixed_full, log_total = attend_forward(query, keys_all, values_all, query_tags, key_tags)
    mixed = mixed_full.astype(jnp.bfloat16)
    middle = (
        stream
        + sum_heads(jnp.einsum("tbf,fd->tbd", mixed, mat_out, preferred_element_type=jnp.float32))
        + bias_out
    )
    second = layer_norm(middle, gain_two, shift_two).astype(jnp.bfloat16)
    hidden = jnp.einsum("tbd,df->tbf", second, mat_up, preferred_element_type=jnp.float32) + bias_up
    activation = gelu_exact(hidden).astype(jnp.bfloat16)
    return (
        first,
        query,
        keys_all,
        values_all,
        log_total,
        mixed,
        middle,
        second,
        hidden,
        activation,
        mixed_full,
    )


def layer_backward(stream, gradient, layer_index, params, query_tags, key_tags, positions):
    (
        gain_one,
        shift_one,
        mat_qkv,
        bias_qkv,
        mat_out,
        bias_out,
        gain_two,
        shift_two,
        mat_up,
        bias_up,
        mat_down,
        bias_down,
    ) = [item[layer_index] for item in params]
    (
        first,
        query,
        keys_all,
        values_all,
        log_total,
        mixed,
        middle,
        second,
        hidden,
        activation,
        mixed_full,
    ) = front(stream, layer_index, params, query_tags, key_tags, positions)
    frame_place, row_place, column_place = positions
    rows_dev, lane_count, width = stream.shape
    features = query.shape[2]
    head_count = features // HEAD_DIM
    grad_low = gradient.astype(jnp.bfloat16)
    grad_w_down = jnp.einsum(
        "tbf,tbd->fd", activation, grad_low, preferred_element_type=jnp.float32
    )
    grad_b_down = jnp.sum(gradient, axis=(0, 1))
    grad_activation = jnp.einsum(
        "tbd,fd->tbf", grad_low, mat_down, preferred_element_type=jnp.float32
    )
    grad_hidden = jax.vjp(gelu_exact, hidden)[1](grad_activation)[0].astype(jnp.bfloat16)
    grad_b_up = jnp.sum(grad_hidden.astype(jnp.float32), axis=(0, 1))
    grad_w_up = jnp.einsum("tbd,tbf->df", second, grad_hidden, preferred_element_type=jnp.float32)
    grad_second = sum_inputs(
        jnp.einsum("tbf,df->tbd", grad_hidden, mat_up, preferred_element_type=jnp.float32)
    )
    middle_pull = jax.vjp(layer_norm, middle, gain_two, shift_two)[1]
    grad_inner, grad_gain_two, grad_shift_two = middle_pull(grad_second)
    grad_middle = gradient + grad_inner
    grad_b_out = jnp.sum(grad_middle, axis=(0, 1))
    middle_low = grad_middle.astype(jnp.bfloat16)
    grad_w_out = jnp.einsum("tbf,tbd->fd", mixed, middle_low, preferred_element_type=jnp.float32)
    grad_mixed = jnp.einsum(
        "tbd,fd->tbf", middle_low, mat_out, preferred_element_type=jnp.float32
    ).astype(jnp.bfloat16)
    grad_query, key_terms = attend_backward(
        query, keys_all, values_all, log_total, grad_mixed, query_tags, key_tags
    )
    returned = lax.psum_scatter(key_terms, "seq", scatter_dimension=0, tiled=True)
    turned_query = rotate(
        grad_query.reshape(rows_dev, lane_count, head_count, HEAD_DIM),
        -frame_place,
        -row_place,
        -column_place,
    )
    turned_keys = rotate(
        returned[:, :, 0].reshape(rows_dev, lane_count, head_count, HEAD_DIM),
        -frame_place,
        -row_place,
        -column_place,
    )
    grad_projected = jnp.stack(
        [
            turned_query.reshape(rows_dev, lane_count, features),
            turned_keys.reshape(rows_dev, lane_count, features),
            returned[:, :, 1],
        ],
        axis=2,
    ).astype(jnp.bfloat16)
    grad_b_qkv = jnp.sum(grad_projected.astype(jnp.float32), axis=(0, 1))
    grad_w_qkv = jnp.einsum(
        "tbd,tbcf->dcf", first, grad_projected, preferred_element_type=jnp.float32
    )
    grad_first = sum_inputs(
        jnp.einsum("tbcf,dcf->tbd", grad_projected, mat_qkv, preferred_element_type=jnp.float32)
    )
    first_pull = jax.vjp(layer_norm, stream, gain_one, shift_one)[1]
    grad_entry, grad_gain_one, grad_shift_one = first_pull(grad_first)
    grads = (
        grad_gain_one,
        grad_shift_one,
        grad_w_qkv,
        grad_b_qkv,
        grad_w_out,
        grad_b_out,
        grad_gain_two,
        grad_shift_two,
        grad_w_up,
        grad_b_up,
        grad_w_down,
        grad_b_down,
    )
    return (grad_middle + grad_entry, grads)


def per_device(
    tokens,
    d_out,
    norm1_gain,
    norm1_shift,
    w_qkv,
    b_qkv,
    w_out,
    b_out,
    norm2_gain,
    norm2_shift,
    w_up,
    b_up,
    w_down,
    b_down,
    episode_frames,
    live,
):
    rows_dev = tokens.shape[0]
    lane_count = tokens.shape[1] // MICRO
    total_rows = rows_dev * lax.axis_size("seq")
    local_positions = lax.axis_index("seq") * rows_dev + jnp.arange(rows_dev, dtype=jnp.int32)
    key_positions = jnp.arange(total_rows, dtype=jnp.int32)
    tagger = jax.vmap(episode_tags, in_axes=(0, None), out_axes=1)
    query_episode, query_frame, query_row, query_column = tagger(episode_frames, local_positions)
    key_episode, key_frame, key_row, key_column = tagger(episode_frames, key_positions)
    live_keys = lax.all_gather(live, "seq", axis=0, tiled=True)
    params = (
        norm1_gain,
        norm1_shift,
        w_qkv,
        b_qkv,
        w_out,
        b_out,
        norm2_gain,
        norm2_shift,
        w_up,
        b_up,
        w_down,
        b_down,
    )
    layer_grads = [None] * LAYERS
    outputs = []
    grad_tokens = []
    for micro_index in range(MICRO):
        first_lane = micro_index * lane_count
        last_lane = first_lane + lane_count
        query_tags = (query_episode[:, first_lane:last_lane], query_frame[:, first_lane:last_lane])
        key_tags = (
            key_episode[:, first_lane:last_lane],
            key_frame[:, first_lane:last_lane],
            live_keys[:, first_lane:last_lane],
        )
        positions = (
            query_frame[:, first_lane:last_lane],
            query_row[:, first_lane:last_lane],
            query_column[:, first_lane:last_lane],
        )
        stream = tokens[:, first_lane:last_lane].astype(jnp.float32)
        inputs = []
        gathered = []
        for layer_index in range(LAYERS):
            inputs.append(stream)
            layer_state = front(stream, layer_index, params, query_tags, key_tags, positions)
            gathered.append((layer_state[2], layer_state[3]))
            branch = jnp.einsum(
                "tbf,fd->tbd",
                layer_state[9],
                w_down[layer_index],
                preferred_element_type=jnp.float32,
            )
            stream = layer_state[6] + sum_heads(branch) + b_down[layer_index]
        outputs.append(stream)
        gradient = d_out[:, first_lane:last_lane]
        for layer_index in reversed(range(LAYERS)):
            gradient, grads = layer_backward(
                inputs[layer_index], gradient, layer_index, params, query_tags, key_tags, positions
            )
            if layer_grads[layer_index] is None:
                layer_grads[layer_index] = grads
            else:
                layer_grads[layer_index] = jax.tree.map(jnp.add, layer_grads[layer_index], grads)
        grad_tokens.append(gradient)
    stacked = [
        jnp.stack([layer_grads[layer_index][entry] for layer_index in range(LAYERS)])
        for entry in range(12)
    ]
    (
        grad_gain_one,
        grad_shift_one,
        grad_w_qkv,
        grad_b_qkv,
        grad_w_out,
        grad_b_out,
        grad_gain_two,
        grad_shift_two,
        grad_w_up,
        grad_b_up,
        grad_w_down,
        grad_b_down,
    ) = stacked
    in_sums = (
        lax.psum_scatter(grad_w_qkv, "seq", scatter_dimension=1, tiled=True),
        lax.psum_scatter(grad_w_up, "seq", scatter_dimension=1, tiled=True),
        lax.psum_scatter(grad_gain_one, "seq", scatter_dimension=1, tiled=True),
        lax.psum_scatter(grad_shift_one, "seq", scatter_dimension=1, tiled=True),
        lax.psum_scatter(grad_gain_two, "seq", scatter_dimension=1, tiled=True),
        lax.psum_scatter(grad_shift_two, "seq", scatter_dimension=1, tiled=True),
        lax.psum_scatter(grad_b_out, "seq", scatter_dimension=1, tiled=True),
        lax.psum_scatter(grad_b_down, "seq", scatter_dimension=1, tiled=True),
    )
    out_sums = (
        lax.psum_scatter(grad_w_out, "seq", scatter_dimension=2, tiled=True),
        lax.psum_scatter(grad_w_down, "seq", scatter_dimension=2, tiled=True),
    )
    bias_total = lax.psum((grad_b_qkv, grad_b_up), "seq")
    return (
        jnp.concatenate(outputs, axis=1),
        jnp.concatenate(grad_tokens, axis=1),
        in_sums[2],
        in_sums[3],
        in_sums[0],
        bias_total[0],
        out_sums[0],
        in_sums[6],
        in_sums[4],
        in_sums[5],
        in_sums[1],
        bias_total[1],
        out_sums[1],
        in_sums[7],
    )


MESH = pl.DeviceIdType.MESH
BF16 = jnp.bfloat16
F32 = jnp.float32
VMEM_BYTES = 60 * 1024 * 1024
PAIR = 128
VEC = 2048


def nn(left, right):
    return lax.dot_general(left, right, (((1,), (0,)), ((), ())), preferred_element_type=F32)


def nt(left, right):
    return lax.dot_general(left, right, (((1,), (1,)), ((), ())), preferred_element_type=F32)


def tn(left, right):
    return lax.dot_general(left, right, (((0,), (0,)), ((), ())), preferred_element_type=F32)


def at(start, size):
    return pl.ds(pl.multiple_of(start, size), size)


def remote(src, dst, send, recv, seq, tp):
    return pltpu.make_async_remote_copy(
        src_ref=src,
        dst_ref=dst,
        send_sem=send,
        recv_sem=recv,
        device_id=(seq, tp),
        device_id_type=MESH,
    )


def greet(partners):
    barrier = pltpu.get_barrier_semaphore()
    for seq, tp in partners:
        pl.semaphore_signal(barrier, inc=1, device_id=(seq, tp), device_id_type=MESH)
    pl.semaphore_wait(barrier, len(partners))


def whole(array):
    zeros = (0,) * array.ndim
    return pl.BlockSpec(array.shape, lambda s: zeros, pipeline_mode=pl.Buffered(1))


def whole_out(shape):
    zeros = (0,) * len(shape)
    return pl.BlockSpec(shape, lambda s: zeros)


ANYWHERE = pl.BlockSpec(memory_space=pl.ANY)


def turn_row(table, place, section):
    frequency = np.exp(np.arange(10, dtype=np.float32) * np.float32(-math.log(10000.0) / 10.0))
    angle = place.astype(np.float32)[:, None] * frequency
    for base in range(20 * section, PAIR, HEAD_DIM):
        table[0, :, base : base + 10] = np.cos(angle)
        table[0, :, base + 10 : base + 20] = np.cos(angle)
        table[1, :, base : base + 10] = -np.sin(angle)
        table[2, :, base + 10 : base + 20] = np.sin(angle)


def turn_constants(frames):
    within, ahead = np.zeros((3, FRAME, PAIR), np.float32), np.zeros((3, frames, PAIR), np.float32)
    turn_row(within, np.arange(FRAME) // GRID, 1)
    turn_row(within, np.arange(FRAME) % GRID, 2)
    for base in range(60, PAIR, HEAD_DIM):
        within[0, :, base : base + 4] = 1.0
    turn_row(ahead, np.arange(frames), 0)
    return jnp.asarray(within), jnp.asarray(ahead)


def turn(values, tables, back=False):
    cosine, lower, upper = tables
    pieces = []
    for start in range(0, values.shape[1], PAIR):
        slab = values[:, start : start + PAIR]
        moved = pltpu.roll(slab, PAIR - 10, 1) * lower + pltpu.roll(slab, 10, 1) * upper
        pieces.append(slab * cosine - moved if back else slab * cosine + moved)
    return jnp.concatenate(pieces, axis=1)


def tables_of(fixed_ref, frames_ref, chunk):
    return [fixed_ref[i] + frames_ref[i, pl.ds(chunk, 1), :] for i in range(3)]


def normed(stream):
    center = stream - jnp.mean(stream, axis=-1, keepdims=True)
    spread = jnp.mean(center * center, axis=-1, keepdims=True)
    scale = lax.rsqrt(spread + EPSILON)
    return center * scale, scale


def norm_pull(grad, gain, unit, scale):
    scaled = grad * gain
    return scale * (
        scaled
        - jnp.mean(scaled, axis=-1, keepdims=True)
        - unit * jnp.mean(scaled * unit, axis=-1, keepdims=True)
    )


def column_sum(values):
    return jnp.sum(values, axis=0, keepdims=True)


def gelu_both(hidden):
    normal = 0.5 + 0.5 * lax.erf(hidden * math.sqrt(0.5))
    density = jnp.exp(hidden * hidden * -0.5) * (1.0 / math.sqrt(2.0 * math.pi))
    return hidden * normal, normal + hidden * density


def project(stream, chunk, layer, pair, refs, outs, first_full):
    gain, shift, weight, bias, fixed, frames = refs
    query_ref, key_ref, value_ref, first_ref = outs
    unit, _ = normed(stream)
    first = (unit * gain[layer : layer + 1, :] + shift[layer : layer + 1, :]).astype(BF16)
    first_full[...] = first
    first_ref[...] = first_full[:, at(pair * PAIR, PAIR)]
    tables = tables_of(fixed, frames, chunk)
    query = nn(first, weight[0]) + bias[0, layer : layer + 1, :]
    query_ref[...] = (turn(query, tables) * SCORE_SCALE).astype(BF16)
    key = nn(first, weight[1]) + bias[1, layer : layer + 1, :]
    key_ref[...] = turn(key, tables).astype(BF16)
    value = nn(first, weight[2]) + bias[2, layer : layer + 1, :]
    value_ref[...] = value.astype(BF16)


class Relay:
    sems = 6

    def __init__(self, n, rows, buffer, other, sems, lives=None, live_other=None):
        self.n, self.rows, self.buffer, self.other = n, rows, buffer, other
        self.lives, self.live_other = lives, live_other
        self.z_send, self.z_recv, self.y_send, self.y_recv, self.c_send, self.c_recv = sems
        self.planes = n // 4
        self.me, self.core = lax.axis_index("seq"), lax.axis_index("tp")
        me = self.me
        self.x, self.y, self.z = lax.rem(me, 2), lax.rem(me // 2, 2), me // 4
        self.across = me + 2 - 4 * self.y

    @staticmethod
    def scratch(n):
        dma, planes = pltpu.SemaphoreType.DMA, n // 4
        shapes = [(planes, 2, 2)] * 2 + [(planes, 2)] * 2 + [(2 * planes,)] * 2
        return [dma(shape) for shape in shapes]

    @property
    def events(self):
        return self.planes

    def plane(self, step):
        return lax.rem(self.z + step, self.planes)

    def place(self, plane, lane):
        return plane * 4 + self.y * 2 + lane

    def reached(self):
        return [(step, far) for step in range(self.planes) for far in (0, 1) if step or far]

    def hello(self):
        barrier = pltpu.get_barrier_semaphore()
        partners = [(self.across, self.core), (self.me, 1 - self.core)]
        for step, far in self.reached():
            lane = 1 - self.x if far else self.x
            partners.append((self.place(self.plane(step), lane), self.core))
        for seq, tp in partners:
            pl.semaphore_signal(barrier, inc=1, device_id=(seq, tp), device_id_type=MESH)

    def met(self):
        pl.semaphore_wait(pltpu.get_barrier_semaphore(), 2 + len(self.reached()))

    def rows_of(self, side, seq):
        return self.buffer.at[side, at(seq * self.rows, self.rows), :]

    def block(self, side, pair):
        return self.buffer.at[side, at(pair * 2 * self.rows, 2 * self.rows), :]

    def items(self, pair):
        found = [self.block(self.core, pair)]
        if self.lives is not None:
            found.append(self.lives.at[at(pair * 2, 2)])
        return found

    def each(self, copy, what):
        for index in range(1 if self.lives is None else 2):
            getattr(copy(index), what)()

    def z_copy(self, step, far):
        def copy(index):
            lane = 1 - self.x if far else self.x
            if index == 0:
                source = self.other.at[self.core] if far else self.rows_of(self.core, self.me)
                target = self.rows_of(self.core, self.me)
            else:
                source = self.live_other if far else self.lives.at[self.me]
                target = self.lives.at[self.me]
            return remote(
                source,
                target,
                self.z_send.at[step, far, index],
                self.z_recv.at[step, far, index],
                self.place(self.plane(step), lane),
                self.core,
            )

        return copy

    def y_copy(self, plane, row):
        def copy(index):
            item = self.items(plane * 2 + row)[index]
            return remote(
                item,
                item,
                self.y_send.at[plane, index],
                self.y_recv.at[plane, index],
                self.across,
                self.core,
            )

        return copy

    def c_copy(self, pair, side):
        item = self.block(side, pair)
        return remote(
            item, item, self.c_send.at[pair], self.c_recv.at[pair], self.me, 1 - self.core
        )

    def begin(self):
        for step, far in self.reached():
            self.each(self.z_copy(step, far), "start")

    def arrive(self, event):
        for far in (0, 1) if event else (1,):
            self.each(self.z_copy(event, far), "wait_recv")
        plane = self.plane(self.planes - event)
        self.each(self.y_copy(plane, self.y), "start")
        self.c_copy(plane * 2 + self.y, self.core).start()

    def complete(self, event):
        plane = self.plane(self.planes - event)
        self.each(self.y_copy(plane, 1 - self.y), "wait_recv")
        self.c_copy(plane * 2 + 1 - self.y, self.core).start()

    def ready(self, event):
        plane = self.plane(self.planes - event)
        self.c_copy(plane * 2, 1 - self.core).wait_recv()
        self.c_copy(plane * 2 + 1, 1 - self.core).wait_recv()
        return plane

    def finish(self):
        for step, far in self.reached():
            self.each(self.z_copy(step, far), "wait_send")
        for plane in range(self.planes):
            self.each(self.y_copy(plane, self.y), "wait_send")
        for pair in range(2 * self.planes):
            self.c_copy(pair, self.core).wait_send()


def split_lanes(values, x, buffer, other, start, rows):
    half = values.shape[2] // 2
    zero, one = values[:, 0, :], values[:, 1, :]
    own, far = jnp.where(x == 0, zero, one), jnp.where(x == 0, one, zero)
    core = lax.axis_index("tp")
    own = jnp.where(core == 0, own[:, :half], own[:, half:]).astype(BF16)
    buffer[core, at(start, rows), :] = own
    for side in range(2):
        other[side] = far[:, side * half : (side + 1) * half].astype(BF16)


def gather_and_project(tokens, live, episode_frames, gain, shift, qkv, bias, fixed, ahead, n):
    rows, lanes, width = tokens.shape
    half = width // 2
    total = n * rows
    chunks = total // FRAME
    per_frame = FRAME // rows
    features = qkv.shape[3]
    slots = episode_frames.shape[1]

    def kernel(*refs):
        refs = list(refs)

        def take(count):
            taken = refs[:count]
            del refs[:count]
            return taken

        tokens_ref, live_ref, counts_ref, gain_ref, shift_ref, w_any, bias_ref = take(7)
        fixed_ref, ahead_ref = take(2)
        all_ref, mask_ref, frames_ref, q_ref, k_ref, v_ref, first_ref = take(7)
        other, lives, live_other, weight, full, w_sem = take(6)
        relay = Relay(n, rows, all_ref, other, take(Relay.sems), lives, live_other)
        load = pltpu.make_async_copy(w_any.at[0], weight, w_sem)
        load.start()
        relay.hello()
        x, me = relay.x, relay.me
        split_lanes(tokens_ref[...].astype(F32), x, all_ref, other, me * rows, rows)
        lane = lax.broadcasted_iota(jnp.int32, (1, FRAME), 1)
        here = lane // rows == lax.rem(me, per_frame)
        tiles = []
        for index in range(lanes):
            alive = live_ref[index : index + 1, :].astype(F32)
            alive = jnp.where(here, jnp.concatenate([alive] * per_frame, axis=1), 0.0)
            tiles.append(jnp.broadcast_to(alive, (8, FRAME)))
        lives[me] = jnp.where(x == 0, tiles[0], tiles[1])
        live_other[...] = jnp.where(x == 0, tiles[1], tiles[0])
        relay.met()
        relay.begin()

        counts = [counts_ref[x, slot] for slot in range(slots)]
        episodes, openings = [], []
        for frame in range(chunks):
            end, episode, opening = 0, 0, 0
            for slot in range(slots):
                end = end + counts[slot]
                passed = frame >= end
                episode = episode + passed.astype(jnp.int32)
                opening = opening + jnp.where(passed, counts[slot], 0)
            episodes.append(episode)
            openings.append(frame - opening)
        for index in range(3):
            table = []
            for frame in range(chunks):
                line = jnp.zeros((1, PAIR), F32)
                for choice in range(chunks):
                    line = jnp.where(
                        openings[frame] == choice, ahead_ref[index, choice : choice + 1, :], line
                    )
                table.append(line)
            frames_ref[index] = jnp.concatenate(
                table + [jnp.zeros((8 - chunks, PAIR), F32)], axis=0
            )
        load.wait()

        def project_frame(frame):
            place = at(frame * FRAME, FRAME)
            stream = jnp.concatenate([all_ref[0, place, :], all_ref[1, place, :]], axis=1)
            project(
                stream.astype(F32),
                frame,
                0,
                me // 2,
                (gain_ref, shift_ref, weight, bias_ref, fixed_ref, frames_ref),
                [ref.at[place, :] for ref in (q_ref, k_ref, v_ref, first_ref)],
                full,
            )

        for event in range(relay.events):
            relay.arrive(event)
            if event:
                relay.complete(event - 1)
        relay.complete(relay.events - 1)

        def one_frame(event, carry):
            project_frame(relay.ready(event))
            return carry

        lax.fori_loop(0, relay.events, one_frame, 0)
        relay.finish()

        for key_frame in range(chunks):
            alive = lives[key_frame * per_frame, 0:1, :]
            for part in range(1, per_frame):
                alive = alive + lives[key_frame * per_frame + part, 0:1, :]
            closed = (alive - 1.0) * -MASKED
            lines = []
            for query_frame in range(chunks):
                allowed = (episodes[query_frame] == episodes[key_frame]) & (
                    openings[key_frame] <= openings[query_frame]
                )
                lines.append(jnp.where(allowed, closed, MASKED))
            lines.append(jnp.zeros((PAIR - chunks, FRAME), F32))
            mask_ref[key_frame * FRAME : (key_frame + 1) * FRAME, :] = jnp.concatenate(
                lines, axis=0
            ).T.astype(BF16)

    in_vmem = pl.BlockSpec(memory_space=pltpu.VMEM)
    in_smem = pl.BlockSpec(memory_space=pltpu.SMEM)
    projected = jax.ShapeDtypeStruct((total, features), BF16)
    return pl.pallas_call(
        kernel,
        out_shape=(
            jax.ShapeDtypeStruct((2, total, half), BF16),
            jax.ShapeDtypeStruct((total, PAIR), BF16),
            jax.ShapeDtypeStruct((3, 8, PAIR), F32),
            projected,
            projected,
            projected,
            jax.ShapeDtypeStruct((total, PAIR), BF16),
        ),
        in_specs=[in_vmem, in_vmem, in_smem, in_vmem, in_vmem, ANYWHERE] + [in_vmem] * 3,
        out_specs=(in_vmem,) * 7,
        scratch_shapes=[
            pltpu.VMEM((2, rows, half), BF16),
            pltpu.VMEM((n, 8, FRAME), F32),
            pltpu.VMEM((8, FRAME), F32),
            pltpu.VMEM(qkv.shape[1:], BF16),
            pltpu.VMEM((FRAME, width), BF16),
            pltpu.SemaphoreType.DMA,
        ]
        + Relay.scratch(n),
        compiler_params=pltpu.CompilerParams(
            collective_id=0, has_side_effects=True, vmem_limit_bytes=VMEM_BYTES
        ),
        name="gather_and_project",
    )(tokens, live, episode_frames, gain, shift, qkv, bias, fixed, ahead)


def halves(ref):
    return jnp.concatenate([ref[0], ref[1]], axis=1).astype(F32)


def halves_spec(shape, chunks, behind):
    return pl.BlockSpec(
        (2, FRAME, shape[2]), lambda s: (0, jnp.clip(s - behind, 0, chunks - 1), 0)
    )


def layer_forward(layer, query, key, value, key_bias, stream, mats, rows_of, next_refs, d_out, n, identity):
    total, features = query.shape
    split = stream.ndim == 3
    width = mats[1].shape[1]
    rows_here = total // n
    hidden_units = mats[1].shape[2]
    chunks = total // FRAME
    heads = features // HEAD_DIM
    slabs = features // PAIR
    columns = 256
    last = next_refs is None
    b_out, gain, shift, b_up, b_down = rows_of
    mat_out, mat_up, mat_down = mats

    def kernel(*refs):
        refs = list(refs)

        def take(count):
            taken = refs[:count]
            del refs[:count]
            return taken

        q_ref, k_ref, v_ref, kb_ref, x_ref = take(5)
        wo_any, wu_any, wd_any = take(3)
        bo_ref, gain_ref, shift_ref, bu_ref, bd_ref = take(5)
        if not last:
            wq_any, ngain, nshift, nbias, fixed, frames = take(6)
        if d_out is not None:
            (d_ref,) = take(1)
        p_ref, r_ref, mixed_ref, middle_ref, second_ref, act_ref, gp_ref, x_out = take(8)
        if not last:
            nq_ref, nk_ref, nv_ref, nf_ref = take(4)
        if d_out is not None:
            (d_all,) = take(1)
        wo, wu, wd, mid, full = take(5)
        if not last:
            (wq,) = take(1)
        a_send, a_recv, b_send, b_recv, w_sem, send_sem, recv_sem = take(7)
        relay = None
        if d_out is not None:
            buffer, other, d_sem = take(3)
            relay = Relay(n, rows_here, buffer, other, take(Relay.sems))

        step = pl.program_id(0)
        me, core = lax.axis_index("seq"), lax.axis_index("tp")

        items = [(wo_any, wo), (wu_any, wu), (wd_any, wd)]
        if not last:
            items.append((wq_any, wq))

        def load(index):
            source, target = items[index]
            return pltpu.make_async_copy(
                source.at[layer if index < 3 else layer + 1], target, w_sem.at[index]
            )

        def exchange(kind, chunk):
            source, target = ((a_send, a_recv), (b_send, b_recv))[kind]
            return remote(
                source.at[chunk],
                target.at[chunk],
                send_sem.at[kind, chunk],
                recv_sem.at[kind, chunk],
                me,
                1 - core,
            )

        @pl.when(step == 0)
        def _():
            for index in range(len(items)):
                load(index).start()
            if relay is None:
                greet([(me, 1 - core)])
            else:
                relay.hello()
                split_lanes(d_ref[...], relay.x, buffer, other, me * rows_here, rows_here)
                relay.met()
                relay.begin()

        if relay is not None:
            for event in range(relay.events):

                @pl.when(step == 1 + event // 2)
                def _():
                    relay.arrive(event)

                @pl.when(step == 2 + event // 2)
                def _():
                    relay.complete(event)

            @pl.when(step == chunks + 1)
            def _():
                for event in range(relay.events):
                    relay.ready(event)
                relay.finish()
                pltpu.make_async_copy(buffer, d_all, d_sem).start()

        lane = lax.broadcasted_iota(jnp.int32, (1, PAIR), 1)
        sides = [(lane < HEAD_DIM).astype(F32).astype(BF16), (lane >= HEAD_DIM).astype(F32).astype(BF16)]
        for frame in range(chunks):

            @pl.when(step == frame)
            def _():
                keys = FRAME * (frame + 1)
                mask = kb_ref[:keys, :]
                asked = jnp.broadcast_to((lane == frame).astype(F32), (FRAME, PAIR)).astype(BF16)

                def one_slab(slab, carry):
                    lanes = at(slab * PAIR, PAIR)
                    q2, v2 = q_ref[:, lanes], v_ref[:keys, lanes]
                    k2 = jnp.concatenate([k_ref[:keys, lanes], mask], axis=1)
                    sums = []
                    for side in range(2):
                        scores = nt(jnp.concatenate([q2 * sides[side], asked], axis=1), k2)
                        highest = jnp.max(scores, axis=1, keepdims=True)
                        shifted = jnp.exp(scores - highest).astype(BF16)
                        p_ref[0, slab * 2 + side, :keys, :] = shifted.T
                        sums.append(nn(shifted, v2 * sides[side] + sides[1 - side]))
                    low_side = lane < HEAD_DIM
                    divisor = 1.0 / jnp.where(
                        low_side, pltpu.roll(sums[0], HEAD_DIM, 1), pltpu.roll(sums[1], HEAD_DIM, 1)
                    )
                    r_ref[:, lanes] = divisor
                    mixed_ref[:, lanes] = (jnp.where(low_side, sums[0], sums[1]) * divisor).astype(BF16)
                    return carry

                lax.fori_loop(0, slabs, one_slab, 0)

        @pl.when(step == 0)
        def _():
            load(0).wait()

        @pl.when(step < chunks)
        def _():
            a_send[step] = nn(mixed_ref[...], wo[...]).astype(BF16)
            exchange(0, step).start()

        @pl.when(step == 1)
        def _():
            load(1).wait()
            load(2).wait()

        @pl.when((step >= 1) & (step <= chunks))
        def _():
            chunk = step - 1
            exchange(0, chunk).wait_recv()
            middle = (halves(x_ref) if split else x_ref[...]) + (a_send[chunk].astype(F32) + a_recv[chunk].astype(F32))
            middle = middle + bo_ref[layer : layer + 1, :]
            middle_ref[...] = middle
            mid[lax.rem(chunk, 2)] = middle
            unit, _ = normed(middle)
            second = (unit * gain_ref[layer : layer + 1, :] + shift_ref[layer : layer + 1, :]).astype(BF16)
            full[...] = second
            second_ref[...] = full[:, at((me // 2) * PAIR, PAIR)]
            parts = [slice(start, start + columns) for start in range(0, hidden_units, columns)]
            hidden = nn(second, wu[:, parts[0]])
            for index, part in enumerate(parts):
                following = nn(second, wu[:, parts[index + 1]]) if index + 1 < len(parts) else None
                act, slope = gelu_both(hidden + bu_ref[layer : layer + 1, part])
                act_ref[:, part] = act.astype(BF16)
                gp_ref[:, part] = slope.astype(BF16)
                hidden = following
            b_send[chunk] = nn(act_ref[...], wd[...]).astype(BF16)
            exchange(1, chunk).start()

        if not last:

            @pl.when(step == 2)
            def _():
                load(3).wait()

        @pl.when(step >= 2)
        def _():
            chunk = step - 2
            exchange(1, chunk).wait_recv()
            result = (
                mid[lax.rem(chunk, 2)]
                + (b_send[chunk].astype(F32) + b_recv[chunk].astype(F32))
                + bd_ref[layer : layer + 1, :]
            )
            x_out[...] = result
            if not last:
                project(
                    result,
                    chunk,
                    layer + 1,
                    me // 2,
                    (ngain, nshift, wq, nbias, fixed, frames),
                    (nq_ref, nk_ref, nv_ref, nf_ref),
                    full,
                )

        @pl.when(step == chunks + 1)
        def _():
            for kind in range(2):
                for chunk in range(chunks):
                    exchange(kind, chunk).wait_send()
            if relay is not None:
                pltpu.make_async_copy(buffer, d_all, d_sem).wait()

    def rows(columns, behind):
        return pl.BlockSpec(
            (FRAME, columns), lambda s: (jnp.clip(s - behind, 0, chunks - 1), 0)
        )

    in_specs = [rows(features, 0), whole(key), whole(value), whole(key_bias)]
    in_specs += [halves_spec(stream.shape, chunks, 1) if split else rows(width, 1)]
    in_specs += [ANYWHERE] * 3 + [whole(item) for item in rows_of]
    operands = [query, key, value, key_bias, stream, *mats, *rows_of]
    if not last:
        in_specs += [ANYWHERE] + [whole(item) for item in next_refs[1:]]
        operands += list(next_refs)
    if d_out is not None:
        in_specs += [whole(d_out)]
        operands += [d_out]
    out_shape = [
        jax.ShapeDtypeStruct((chunks, heads, total, FRAME), BF16),
        jax.ShapeDtypeStruct((total, features), F32),
        jax.ShapeDtypeStruct((total, features), BF16),
        jax.ShapeDtypeStruct((total, width), F32),
        jax.ShapeDtypeStruct((total, PAIR), BF16),
        jax.ShapeDtypeStruct((total, hidden_units), BF16),
        jax.ShapeDtypeStruct((total, hidden_units), BF16),
        jax.ShapeDtypeStruct((total, width), F32),
    ]
    out_specs = [
        pl.BlockSpec((1, heads, total, FRAME), lambda s: (jnp.minimum(s, chunks - 1), 0, 0, 0)),
        rows(features, 0),
        rows(features, 0),
        rows(width, 1),
        rows(PAIR, 1),
        rows(hidden_units, 1),
        rows(hidden_units, 1),
        rows(width, 2),
    ]
    scratch = [
        pltpu.VMEM(mat_out.shape[1:], BF16),
        pltpu.VMEM(mat_up.shape[1:], BF16),
        pltpu.VMEM(mat_down.shape[1:], BF16),
        pltpu.VMEM((2, FRAME, width), F32),
        pltpu.VMEM((FRAME, width), BF16),
    ]
    if not last:
        out_shape += [jax.ShapeDtypeStruct((total, features), BF16)] * 3
        out_shape += [jax.ShapeDtypeStruct((total, PAIR), BF16)]
        out_specs += [rows(features, 2)] * 3 + [rows(PAIR, 2)]
    if d_out is not None:
        out_shape += [jax.ShapeDtypeStruct((2, total, width // 2), BF16)]
        out_specs += [ANYWHERE]
        scratch += [pltpu.VMEM(next_refs[0].shape[1:], BF16)]
    scratch += [pltpu.VMEM((chunks, FRAME, width), BF16)] * 4
    scratch += [
        pltpu.SemaphoreType.DMA((4,)),
        pltpu.SemaphoreType.DMA((2, chunks)),
        pltpu.SemaphoreType.DMA((2, chunks)),
    ]
    if d_out is not None:
        scratch += [
            pltpu.VMEM((2, total, width // 2), BF16),
            pltpu.VMEM((2, rows_here, width // 2), BF16),
            pltpu.SemaphoreType.DMA,
        ]
        scratch += Relay.scratch(n)
    return pl.pallas_call(
        kernel,
        grid=(chunks + 2,),
        out_shape=out_shape,
        in_specs=in_specs,
        out_specs=out_specs,
        scratch_shapes=scratch,
        compiler_params=pltpu.CompilerParams(
            collective_id=identity, has_side_effects=True, vmem_limit_bytes=VMEM_BYTES
        ),
        name=f"layer_forward_{layer}",
    )(*operands)


def attention_backward(
    probs, divisor, mixed, query, key, value, grad_mixed, first, fixed, frames, ships, lane_rows, identity
):
    total, features = query.shape
    chunks = total // FRAME
    slabs = features // PAIR
    half = PAIR // 2
    ship_count, row_count = len(ships), len(lane_rows)

    def kernel(*refs):
        refs = list(refs)

        def take(count):
            taken = refs[:count]
            del refs[:count]
            return taken

        p_ref, r_ref, o_ref, q_ref, k_ref, v_ref, g_ref, first_ref, fixed_ref, frames_ref = take(10)
        ship_refs, row_refs = take(ship_count), take(row_count)
        dq_ref, dk_ref, dv_ref, qkv_out = take(4)
        ship_outs, row_outs = take(ship_count), take(row_count)
        dk_sum, dv_sum, first_turned, qkv_own, qkv_send, qkv_recv = take(6)
        ship_sends, ship_recvs = take(ship_count), take(ship_count)
        qkv_sems, send_sem, recv_sem = take(3)

        step = pl.program_id(0)
        me, core = lax.axis_index("seq"), lax.axis_index("tp")
        x = lax.rem(me, 2)
        beside = me + 1 - 2 * x

        def copy(index):
            if index < ship_count:
                source, target = ship_sends[index], ship_recvs[index]
            else:
                index_row = index - ship_count
                count = lane_rows[index_row][1]
                source, target = row_refs[index_row], row_outs[index_row]
                if count:
                    source = source.at[at(beside * count, count), :]
            return remote(source, target, send_sem.at[index], recv_sem.at[index], beside, core)

        def qkv_copy(slab):
            return remote(
                qkv_send.at[slab],
                qkv_recv.at[slab],
                qkv_sems.at[0, slab],
                qkv_sems.at[1, slab],
                beside,
                core,
            )

        @pl.when(step == 0)
        def _():
            greet([(beside, core)])
            for ref, send in zip(ship_refs, ship_sends):
                send[...] = ref[at((1 - x) * half, half), :].astype(BF16)
            for index in range(ship_count + row_count):
                copy(index).start()
            first_turned[...] = first_ref[...].T

        lane = lax.broadcasted_iota(jnp.int32, (1, PAIR), 1)
        sides = [(lane < HEAD_DIM).astype(F32).astype(BF16), (lane >= HEAD_DIM).astype(F32).astype(BF16)]
        turned = k_ref[...].T
        ones = jnp.broadcast_to((lane < 2).astype(F32), (total, PAIR)).astype(BF16)
        values = jnp.concatenate([v_ref[...], ones], axis=1)
        for frame in reversed(range(chunks)):
            keys = FRAME * (frame + 1)
            own = slice(frame * FRAME, keys)
            tables = tables_of(fixed_ref, frames_ref, frame)
            scaled = (g_ref[own, :].astype(F32) * r_ref[own, :]).astype(BF16)
            inner = scaled.astype(F32) * o_ref[own, :].astype(F32)
            query_parts, score_parts, prob_parts, q_parts, g_parts = [], [], [], [], []
            for side in range(2):
                delta = jnp.sum(
                    jnp.where((lane < HEAD_DIM) == (side == 0), inner, 0.0), axis=1, keepdims=True
                )
                coarse = delta.astype(BF16).astype(F32)
                rest = jnp.where(lane == 0, -coarse, jnp.where(lane == 1, coarse - delta, 0.0))
                g2 = scaled * sides[side]
                attention = p_ref[frame, side, :keys, :]
                grad = nt(values[:keys], jnp.concatenate([g2, rest.astype(BF16)], axis=1))
                grad_scores = (attention.astype(F32) * grad).astype(BF16)
                query_parts.append(nn(turned[side * HEAD_DIM : (side + 1) * HEAD_DIM, :keys], grad_scores))
                score_parts.append(grad_scores)
                prob_parts.append(attention)
                q_parts.append(q_ref[own, :] * sides[side])
                g_parts.append(g2)
            grad_query = jnp.concatenate(query_parts, axis=0).T
            key_parts = nn(jnp.concatenate(score_parts, axis=1), jnp.concatenate(q_parts, axis=0))
            value_parts = nn(jnp.concatenate(prob_parts, axis=1), jnp.concatenate(g_parts, axis=0))
            dq_ref[own, :] = (turn(grad_query, tables, True) * SCORE_SCALE).astype(BF16)
            if frame == chunks - 1:
                dk_sum[...] = key_parts
                dv_sum[...] = value_parts
            else:
                dk_sum[:keys, :] += key_parts
                dv_sum[:keys, :] += value_parts
            dk_ref[own, :] = turn(dk_sum[own, :], tables, True).astype(BF16)
            dv_ref[own, :] = dv_sum[own, :].astype(BF16)

        for part, ref in enumerate((dq_ref, dk_ref, dv_ref)):
            piece = slice(part * PAIR, (part + 1) * PAIR)
            qkv_own[step, :, piece] = nn(first_turned[...], ref[...])
            qkv_send[step, :, piece] = qkv_own[step, at((1 - x) * half, half), piece].astype(BF16)
        qkv_copy(step).start()

        @pl.when(step == slabs - 1)
        def _():
            for index in range(ship_count + row_count):
                copy(index).wait_recv()
            for ref, recv, out in zip(ship_refs, ship_recvs, ship_outs):
                out[...] = ref[at(x * half, half), :] + recv[...].astype(F32)
            for slab in range(slabs):
                qkv_copy(slab).wait_recv()
                for part in range(3):
                    piece = slice(part * PAIR, (part + 1) * PAIR)
                    qkv_out[part, :, slab * PAIR : (slab + 1) * PAIR] = qkv_own[
                        slab, at(x * half, half), piece
                    ] + qkv_recv[slab, :, piece].astype(F32)
            for index in range(ship_count + row_count):
                copy(index).wait_send()
            for slab in range(slabs):
                qkv_copy(slab).wait_send()

    slab = pl.BlockSpec((total, PAIR), lambda s: (0, s))
    in_specs = [pl.BlockSpec((chunks, 2, total, FRAME), lambda s: (0, s, 0, 0))]
    in_specs += [slab] * 6 + [whole(first), whole(fixed), whole(frames)]
    in_specs += [whole(item) for item in ships] + [ANYWHERE] * row_count
    out_shape = [jax.ShapeDtypeStruct((total, features), BF16)] * 3
    out_specs = [slab] * 3
    out_shape.append(jax.ShapeDtypeStruct((3, half, features), F32))
    out_specs.append(whole_out((3, half, features)))
    for item in ships:
        out_shape.append(jax.ShapeDtypeStruct((half, item.shape[1]), F32))
        out_specs.append(whole_out((half, item.shape[1])))
    for item, count in lane_rows:
        shape = (count or item.shape[0], item.shape[1])
        out_shape.append(jax.ShapeDtypeStruct(shape, item.dtype))
        out_specs.append(ANYWHERE)
    scratch = [pltpu.VMEM((total, PAIR), F32)] * 2
    scratch += [pltpu.VMEM((PAIR, total), BF16), pltpu.VMEM((slabs, PAIR, 3 * PAIR), F32)]
    scratch += [pltpu.VMEM((slabs, half, 3 * PAIR), BF16)] * 2
    scratch += [pltpu.VMEM((half, item.shape[1]), BF16) for item in ships] * 2
    scratch += [pltpu.SemaphoreType.DMA((2, slabs))]
    scratch += [pltpu.SemaphoreType.DMA((ship_count + row_count,))] * 2
    return pl.pallas_call(
        kernel,
        grid=(slabs,),
        out_shape=out_shape,
        in_specs=in_specs,
        out_specs=out_specs,
        scratch_shapes=scratch,
        compiler_params=pltpu.CompilerParams(
            collective_id=identity, has_side_effects=True, vmem_limit_bytes=VMEM_BYTES
        ),
        name=f"attention_backward_{identity}",
    )(
        probs,
        divisor,
        mixed,
        query,
        key,
        value,
        grad_mixed,
        first,
        fixed,
        frames,
        *ships,
        *[item for item, _ in lane_rows],
    )


def rows_backward(entry, upper, identity):
    top, bottom = len(entry) == 1, upper is None
    if not top:
        above, entry = entry[0], entry[1:]
        split = entry[3].ndim == 3
    total = entry[0].shape[1] if top else entry[0].shape[0]
    chunks = total // FRAME
    columns = 256
    ahead = 0 if top else 1
    if top:
        width = 2 * entry[0].shape[2]
    else:
        features, width = entry[0].shape[1], entry[4].shape[1]
    if not bottom:
        layer = upper[0]
        hidden_units, mixed_features = upper[1].shape[1], upper[5].shape[1]
    place_rows = total // lax.axis_size("seq")

    def kernel(*refs):
        refs = list(refs)

        def take(count):
            taken = refs[:count]
            del refs[:count]
            return taken

        if top:
            (d_out_ref,) = take(1)
        else:
            dq_ref, dk_ref, dv_ref, x_ref, dm_ref, wq, gain1 = take(7)
        if not bottom:
            act_ref, gp_ref, middle_ref, second_ref, mixed_ref = take(5)
            wo_any, wu_any, wd_any, gain2 = take(4)
        if not top:
            (vec1,) = take(1)
        if not bottom:
            dmid_out, dmix_out, out_sum, up_sum, down_sum, vec2 = take(6)
        else:
            dx_out, dx_other, vec_other = take(3)
        if not top:
            a_send, a_recv = take(2)
        if not bottom:
            b_send, b_recv, grad_keep, hidden_keep, low_keep, wo, wu, wd, w_sem = take(9)
        else:
            dx_keep, dx_send, dx_recv, vec_recv, x_send_sem, x_recv_sem = take(6)
        send_sem, recv_sem = take(2)

        step = pl.program_id(0)
        me, core = lax.axis_index("seq"), lax.axis_index("tp")
        pair = at((me // 2) * PAIR, PAIR)
        x = lax.rem(me, 2)
        beside = me + 1 - 2 * x

        def exchange(kind, chunk):
            source, target = (a_send, a_recv) if kind == 0 else (b_send, b_recv)
            return remote(
                source.at[chunk],
                target.at[chunk],
                send_sem.at[kind, chunk],
                recv_sem.at[kind, chunk],
                me,
                1 - core,
            )

        def load(index):
            source, target = ((wd_any, wd), (wu_any, wu), (wo_any, wo))[index]
            return pltpu.make_async_copy(source.at[layer], target, w_sem.at[index])

        @pl.when(step == 0)
        def _():
            if not bottom:
                for index in range(3):
                    load(index).start()
                out_sum[...] = jnp.zeros_like(out_sum)
                up_sum[...] = jnp.zeros_like(up_sum)
                down_sum[...] = jnp.zeros_like(down_sum)
                vec2[...] = jnp.zeros_like(vec2)
            if not top:
                vec1[...] = jnp.zeros_like(vec1)
            greet([(me, 1 - core)] + ([(beside, core)] if bottom else []))

        if not top:

            @pl.when(step < chunks)
            def _():
                partial = None
                for part, ref in enumerate((dq_ref, dk_ref, dv_ref)):
                    grad = ref[...]
                    term = nt(grad, wq[0, part])
                    partial = term if partial is None else partial + term
                    vec1[part : part + 1, :] += column_sum(grad.astype(F32))
                a_send[step] = partial.astype(BF16)
                exchange(0, step).start()

        @pl.when((step >= ahead) & (step < chunks + ahead))
        def _():
            chunk = step - ahead
            if top:
                gradient = halves(d_out_ref)
            else:
                exchange(0, chunk).wait_recv()
                grad_first = a_send[chunk].astype(F32) + a_recv[chunk].astype(F32)
                unit, scale = normed(halves(x_ref) if split else x_ref[...])
                for start, sums in ((3, column_sum(grad_first * unit)), (5, column_sum(grad_first))):
                    for side in range(width // features):
                        piece = slice(side * features, (side + 1) * features)
                        vec1[start + side : start + side + 1, :] += sums[:, piece]
                gradient = dm_ref[...] + norm_pull(
                    grad_first, gain1[above : above + 1, :], unit, scale
                )
            if bottom:
                dx_keep[at(chunk * FRAME, FRAME), :] = gradient
                return

            @pl.when(chunk == 0)
            def _():
                load(0).wait()
                load(1).wait()

            grad_keep[lax.rem(chunk, 2)] = gradient
            vec2[1:2, :width] += column_sum(gradient)
            low = gradient.astype(BF16)
            low_keep[...] = low
            low_columns = low_keep[:, pair]
            second = second_ref[...]
            parts = [slice(start, start + columns) for start in range(0, hidden_units, columns)]
            grad_act = nt(low, wd[parts[0], :])
            for index, part in enumerate(parts):
                following = nt(low, wd[parts[index + 1], :]) if index + 1 < len(parts) else None
                grad_hidden = grad_act * gp_ref[:, part].astype(F32)
                hidden_keep[:, part] = grad_hidden.astype(BF16)
                vec2[0:1, part] += column_sum(grad_hidden)
                grad_act = following
            b_send[chunk] = nt(hidden_keep[...], wu[...]).astype(BF16)
            down_sum[...] += tn(low_columns, act_ref[...])
            up_sum[...] += tn(second, hidden_keep[...])
            exchange(1, chunk).start()

        if not bottom:

            @pl.when(step == ahead + 1)
            def _():
                load(2).wait()

            @pl.when(step >= ahead + 1)
            def _():
                chunk = step - ahead - 1
                exchange(1, chunk).wait_recv()
                grad_second = b_send[chunk].astype(F32) + b_recv[chunk].astype(F32)
                unit, scale = normed(middle_ref[...])
                vec2[2:3, :width] += column_sum(grad_second * unit)
                vec2[3:4, :width] += column_sum(grad_second)
                grad_middle = grad_keep[lax.rem(chunk, 2)] + norm_pull(
                    grad_second, gain2[layer : layer + 1, :], unit, scale
                )
                dmid_out[...] = grad_middle
                vec2[4:5, :width] += column_sum(grad_middle)
                low = grad_middle.astype(BF16)
                low_keep[...] = low
                out_sum[...] += tn(low_keep[:, pair], mixed_ref[...])
                dmix_out[...] = nt(low, wo[...]).astype(BF16)

        if bottom:

            def x_copy(index):
                source, target = ((dx_send, dx_recv), (vec1, vec_recv))[index]
                return remote(
                    source, target, x_send_sem.at[index], x_recv_sem.at[index], beside, core
                )

            @pl.when(step == chunks)
            def _():
                dx_send[...] = dx_keep[at(beside * place_rows, place_rows), :].astype(BF16)
                x_copy(0).start()
                x_copy(1).start()
                dx_out[...] = dx_keep[at(me * place_rows, place_rows), :]
                x_copy(0).wait_recv()
                x_copy(1).wait_recv()
                dx_other[...] = dx_recv[...].astype(F32)
                vec_other[...] = vec_recv[...]
                x_copy(0).wait_send()
                x_copy(1).wait_send()

        @pl.when(step == pl.num_programs(0) - 1)
        def _():
            for kind in ([] if top else [0]) + ([] if bottom else [1]):
                for chunk in range(chunks):
                    exchange(kind, chunk).wait_send()

    def rows(columns, behind):
        return pl.BlockSpec(
            (FRAME, columns), lambda s: (jnp.clip(s - behind, 0, chunks - 1), 0)
        )

    vec = jax.ShapeDtypeStruct((8, VEC), F32)
    operands, in_specs, out_shape, out_specs, scratch = [], [], [], [], []
    if top:
        operands += list(entry)
        in_specs += [halves_spec(entry[0].shape, chunks, 0)]
    else:
        operands += list(entry)
        in_specs += [rows(features, 0)] * 3
        in_specs += [halves_spec(entry[3].shape, chunks, 1) if split else rows(width, 1)]
        in_specs += [rows(width, 1)]
        in_specs += [
            pl.BlockSpec(
                (1, *entry[5].shape[1:]),
                lambda s: (above, 0, 0, 0),
                pipeline_mode=pl.Buffered(1),
            ),
            whole(entry[6]),
        ]
        narrow = jax.ShapeDtypeStruct((8, features), F32)
        out_shape += [narrow]
        out_specs += [whole_out((8, features))]
        scratch += [pltpu.VMEM((chunks, FRAME, width), BF16)] * 2
    if not bottom:
        operands += list(upper[1:])
        in_specs += [rows(hidden_units, ahead)] * 2 + [rows(width, ahead + 1), rows(PAIR, ahead)]
        in_specs += [rows(mixed_features, ahead + 1)] + [ANYWHERE] * 3 + [whole(upper[9])]
        sums = [mixed_features, hidden_units, hidden_units]
        out_shape += [
            jax.ShapeDtypeStruct((total, width), F32),
            jax.ShapeDtypeStruct((total, mixed_features), BF16),
        ]
        out_shape += [jax.ShapeDtypeStruct((PAIR, size), F32) for size in sums] + [vec]
        out_specs += [rows(width, ahead + 1), rows(mixed_features, ahead + 1)]
        out_specs += [whole_out((PAIR, size)) for size in sums] + [whole_out((8, VEC))]
        scratch += [pltpu.VMEM((chunks, FRAME, width), BF16)] * 2
        scratch += [
            pltpu.VMEM((2, FRAME, width), F32),
            pltpu.VMEM((FRAME, hidden_units), BF16),
            pltpu.VMEM((FRAME, width), BF16),
            pltpu.VMEM(upper[6].shape[1:], BF16),
            pltpu.VMEM(upper[7].shape[1:], BF16),
            pltpu.VMEM(upper[8].shape[1:], BF16),
            pltpu.SemaphoreType.DMA((3,)),
        ]
    else:
        out_shape += [
            jax.ShapeDtypeStruct((place_rows, width), F32),
            jax.ShapeDtypeStruct((place_rows, width), F32),
            narrow,
        ]
        out_specs += [whole_out((place_rows, width))] * 2 + [whole_out((8, features))]
        scratch += [
            pltpu.VMEM((total, width), F32),
            pltpu.VMEM((place_rows, width), BF16),
            pltpu.VMEM((place_rows, width), BF16),
            pltpu.VMEM((8, features), F32),
            pltpu.SemaphoreType.DMA((2,)),
            pltpu.SemaphoreType.DMA((2,)),
        ]
    scratch += [pltpu.SemaphoreType.DMA((2, chunks))] * 2
    return pl.pallas_call(
        kernel,
        grid=(chunks + (1 if top or bottom else 2),),
        out_shape=out_shape,
        in_specs=in_specs,
        out_specs=out_specs,
        scratch_shapes=scratch,
        compiler_params=pltpu.CompilerParams(
            collective_id=identity, has_side_effects=True, vmem_limit_bytes=VMEM_BYTES
        ),
        name=f"rows_backward_{identity}",
    )(*operands)


def assemble(sums, vecs, lanes, n, features, hidden_units):
    place = lanes[1].shape[0]
    width = lanes[1].shape[1]
    half = PAIR // 2

    def kernel(*refs):
        refs = list(refs)

        def take(count):
            taken = refs[:count]
            del refs[:count]
            return taken

        qkvs, outs, ups, downs = take(LAYERS), take(LAYERS), take(LAYERS), take(LAYERS)
        vec_refs = [take(4) for _ in range(LAYERS)]
        out_own, out_other, dx_own, dx_other = take(4)
        out_ref, dx_ref, gain1, shift1, g_qkv, b_qkv, g_out, b_out = take(8)
        gain2, shift2, g_up, b_up, g_down, b_down = take(6)
        me = lax.axis_index("seq")
        x = lax.rem(me, 2)

        for layer in range(LAYERS):
            for ref, target in ((qkvs, g_qkv), (outs, g_out), (ups, g_up), (downs, g_down)):
                target[layer] = ref[layer][...]

        for layer, (entry_own, entry_other, upper_own, upper_other) in enumerate(vec_refs):
            line = slice(layer, layer + 1)
            for part in range(3):
                row = slice(part, part + 1)
                b_qkv[part, line, :] = entry_own[row, :] + entry_other[row, :]
            b_up[line, :] = upper_own[0:1, :hidden_units] + upper_other[0:1, :hidden_units]

            def owned(mine, other, row):
                wide = mine.shape[1]
                place = (me // 2) * PAIR
                pair = at(lax.rem(place, wide), PAIR)
                both = mine[row : row + 1, pair] + other[row : row + 1, pair]
                for later in range(1, width // wide):
                    line = slice(row + later, row + later + 1)
                    both = jnp.where(place // wide == later, mine[line, pair] + other[line, pair], both)
                return jnp.where(x == 0, both[:, :half], both[:, half:])

            gain1[line, :] = owned(entry_own, entry_other, 3)
            shift1[line, :] = owned(entry_own, entry_other, 5)
            b_down[line, :] = owned(upper_own, upper_other, 1)
            gain2[line, :] = owned(upper_own, upper_other, 2)
            shift2[line, :] = owned(upper_own, upper_other, 3)
            b_out[line, :] = owned(upper_own, upper_other, 4)

        def both_lanes(target, mine, other):
            target[:, 0, :] = jnp.where(x == 0, mine, other)
            target[:, 1, :] = jnp.where(x == 0, other, mine)

        both_lanes(dx_ref, dx_own[...], dx_other[...])
        both_lanes(out_ref, out_own[...], out_other[...])

    def f32(*shape):
        return jax.ShapeDtypeStruct(shape, F32)

    in_vmem = pl.BlockSpec(memory_space=pltpu.VMEM)
    flat = []
    for kind in range(4):
        flat += [sums[layer][kind] for layer in range(LAYERS)]
    for layer in range(LAYERS):
        flat += list(vecs[layer])
    flat += list(lanes)
    small = f32(LAYERS, width // n)
    return pl.pallas_call(
        kernel,
        out_shape=(
            f32(place, 2, width),
            f32(place, 2, width),
            small,
            small,
            f32(LAYERS, 3, half, features),
            f32(3, LAYERS, features),
            f32(LAYERS, half, features),
            small,
            small,
            small,
            f32(LAYERS, half, hidden_units),
            f32(LAYERS, hidden_units),
            f32(LAYERS, half, hidden_units),
            small,
        ),
        in_specs=[in_vmem] * len(flat),
        out_specs=(in_vmem,) * 14,
        compiler_params=pltpu.CompilerParams(vmem_limit_bytes=VMEM_BYTES),
        name="assemble",
    )(*flat)


def per_chip(
    tokens,
    d_out,
    norm1_gain,
    norm1_shift,
    w_qkv,
    b_qkv,
    w_out,
    b_out,
    norm2_gain,
    norm2_shift,
    w_up,
    b_up,
    w_down,
    b_down,
    episode_frames,
    live,
):
    n = lax.axis_size("seq")
    rows = tokens.shape[0]
    features = w_qkv.shape[3]
    fixed, ahead = turn_constants(rows * n // FRAME)
    qkv, qkv_bias = w_qkv.transpose(0, 2, 1, 3), b_qkv.transpose(1, 0, 2)

    gathered, key_bias, frames, query, key, value, first = gather_and_project(
        tokens, live.T, episode_frames, norm1_gain, norm1_shift, qkv, qkv_bias, fixed, ahead, n
    )
    streams, kept, d_lane = [gathered], [], None
    for layer in range(LAYERS):
        following = None
        if layer + 1 < LAYERS:
            following = (qkv, norm1_gain, norm1_shift, qkv_bias, fixed, frames)
        results = layer_forward(
            layer,
            query,
            key,
            value,
            key_bias,
            streams[layer],
            (w_out, w_up, w_down),
            (b_out, norm2_gain, norm2_shift, b_up, b_down),
            following,
            d_out if layer == 0 else None,
            n,
            1 + layer,
        )
        kept.append((query, key, value, first, *results[:7]))
        streams.append(results[7])
        if following is not None:
            query, key, value, first = results[8:12]
        if layer == 0:
            d_lane = results[-1]

    sums = [None] * LAYERS
    vecs = [[None] * 4 for _ in range(LAYERS)]
    entry, pending_rows = (d_lane,), [(streams[LAYERS], rows)]
    out_other = None
    for layer in reversed(range(LAYERS)):
        query, key, value, first, probs, divisor, mixed, middle, second, act, slope = kept[layer]
        upper = (
            layer,
            act,
            slope,
            middle,
            second,
            mixed,
            w_out,
            w_up,
            w_down,
            norm2_gain,
        )
        results = rows_backward(entry, upper, 1 + LAYERS + 2 * (LAYERS - 1 - layer))
        if layer + 1 < LAYERS:
            pending_rows = [(results[0], 0)]
            results = results[1:]
        grad_middle, grad_mixed, *pending, vec2 = results
        pending_rows = pending_rows + [(vec2, 0)]
        results = attention_backward(
            probs,
            divisor,
            mixed,
            query,
            key,
            value,
            grad_mixed,
            first,
            fixed,
            frames,
            pending,
            pending_rows,
            2 + LAYERS + 2 * (LAYERS - 1 - layer),
        )
        grad_query, grad_key, grad_value = results[:3]
        sums[layer] = results[3:7]
        others = results[7:]
        if out_other is None:
            out_other = others[0]
        else:
            vecs[layer + 1][:2] = [pending_rows[0][0], others[0]]
        vecs[layer][2:] = [vec2, others[1]]
        entry = (
            layer,
            grad_query,
            grad_key,
            grad_value,
            streams[layer],
            grad_middle,
            qkv,
            norm1_gain,
        )
    vec1, dx_own, dx_other, vec_other = rows_backward(entry, None, 1 + 3 * LAYERS)
    vecs[0][:2] = [vec1, vec_other]
    results = list(
        assemble(
            sums,
            vecs,
            (
                lax.dynamic_slice_in_dim(streams[LAYERS], lax.axis_index("seq") * rows, rows, 0),
                out_other,
                dx_own,
                dx_other,
            ),
            n,
            features,
            w_up.shape[2],
        )
    )
    results[4] = results[4].transpose(0, 2, 1, 3)
    results[5] = results[5].transpose(1, 0, 2)
    results[6] = results[6].transpose(0, 2, 1)
    results[12] = results[12].transpose(0, 2, 1)
    return tuple(results)


def lane_fits(mesh, tokens):
    n = mesh.shape["seq"]
    positions, lanes, width = tokens.shape
    rows = positions // n
    return (
        lanes == 2
        and n % 4 == 0
        and positions <= 4 * FRAME
        and positions % FRAME == 0
        and FRAME % rows == 0
        and width // n * 2 == PAIR
        and mesh.shape["tp"] == 2
    )


def solution(mesh):
    placed = (
        P("seq", None, None),
        P("seq", None, None),
        P(),
        P(),
        P(None, None, None, "tp"),
        P(None, None, "tp"),
        P(None, "tp", None),
        P(),
        P(),
        P(),
        P(None, None, "tp"),
        P(None, "tp"),
        P(None, "tp", None),
        P(),
        P(),
        P("seq", None),
    )
    def mapped(body):
        return jax.shard_map(
            body,
            mesh=mesh,
            in_specs=placed,
            out_specs=(
                P("seq", None, None),
                P("seq", None, None),
                P(None, "seq"),
                P(None, "seq"),
                P(None, "seq", None, "tp"),
                P(None, None, "tp"),
                P(None, "tp", "seq"),
                P(None, "seq"),
                P(None, "seq"),
                P(None, "seq"),
                P(None, "seq", "tp"),
                P(None, "tp"),
                P(None, "tp", "seq"),
                P(None, "seq"),
            ),
            check_vma=False,
        )

    def run(tokens, *others):
        if lane_fits(mesh, tokens):
            return mapped(per_chip)(tokens, *others)
        return mapped(per_device)(tokens, *others)

    return run
```

```python
import math

import jax
import jax.numpy as jnp
import numpy as np
from jax import lax
from jax.experimental import pallas as pl
from jax.experimental.pallas import tpu as pltpu
from jax.sharding import PartitionSpec as P

HEAD_DIM = 64
GRID = 16
FRAME = 256
LAYERS = 2
MICRO = 2


EPSILON = 1e-06
MASKED = -1e30
SCORE_SCALE = 0.125


def layer_norm(stream, norm_gain, norm_shift):
    center = stream - jnp.mean(stream, axis=-1, keepdims=True)
    spread = jnp.mean(center * center, axis=-1, keepdims=True)
    return center * lax.rsqrt(spread + EPSILON) * norm_gain + norm_shift


def rotate(values, frame_place, row_place, column_place):
    frequency = jnp.exp(jnp.arange(10, dtype=jnp.float32) * (-math.log(10000.0) / 10.0))
    pieces = []
    for section, place in enumerate((frame_place, row_place, column_place)):
        lower = values[..., 20 * section : 20 * section + 10]
        upper = values[..., 20 * section + 10 : 20 * section + 20]
        angles = place.astype(jnp.float32)[..., None, None] * frequency
        cosine = jnp.cos(angles)
        sine_part = jnp.sin(angles)
        pieces.append(lower * cosine - upper * sine_part)
        pieces.append(lower * sine_part + upper * cosine)
    pieces.append(values[..., 60:])
    return jnp.concatenate(pieces, axis=-1)


def episode_tags(frame_counts, positions):
    endings = jnp.cumsum(frame_counts) * FRAME
    passed = (positions[:, None] >= endings[None, :]).astype(jnp.int32)
    episode = jnp.sum(passed, axis=1)
    opening = jnp.sum(passed * frame_counts[None, :], axis=1)
    frame_index = positions // FRAME - opening
    within = positions % FRAME
    return (episode, frame_index, within // GRID, within % GRID)


def gelu_exact(values):
    return jax.nn.gelu(values, approximate=False)


def sum_heads(partial_sum):
    return lax.psum(partial_sum.astype(jnp.bfloat16), "tp").astype(jnp.float32)


def sum_inputs(partial_sum):
    return lax.psum(partial_sum.astype(jnp.bfloat16), "tp").astype(jnp.float32)


def lane_scores(query, keys_all, lane_index, query_tags, key_tags):
    head_count = query.shape[2] // HEAD_DIM
    query_lane = lax.dynamic_index_in_dim(query, lane_index, 1, False).reshape(
        query.shape[0], head_count, HEAD_DIM
    )
    keys_lane = lax.dynamic_index_in_dim(keys_all, lane_index, 1, False).reshape(
        keys_all.shape[0], head_count, HEAD_DIM
    )
    query_episode, query_frame = [
        lax.dynamic_index_in_dim(item, lane_index, 1, False) for item in query_tags
    ]
    key_episode, key_frame, key_live = [
        lax.dynamic_index_in_dim(item, lane_index, 1, False) for item in key_tags
    ]
    allowed = (
        (query_episode[:, None] == key_episode[None, :])
        & (key_frame[None, :] <= query_frame[:, None])
        & (key_live[None, :] > 0)
    )
    scores = (
        jnp.einsum("qhd,khd->hqk", query_lane, keys_lane, preferred_element_type=jnp.float32)
        * SCORE_SCALE
    )
    return (jnp.where(allowed[None], scores, MASKED), query_lane, keys_lane)


def attend_forward(query, keys_all, values_all, query_tags, key_tags):
    rows_dev, lane_count, features = query.shape
    head_count = features // HEAD_DIM

    def one_lane(lane_index, carry):
        scores, query_lane, keys_lane = lane_scores(
            query, keys_all, lane_index, query_tags, key_tags
        )
        highest = jnp.max(scores, axis=-1, keepdims=True)
        shifted = jnp.exp(scores - highest)
        summed = jnp.sum(shifted, axis=-1, keepdims=True)
        attention = (shifted / summed).astype(jnp.bfloat16)
        values_lane = lax.dynamic_index_in_dim(values_all, lane_index, 1, False).reshape(
            values_all.shape[0], head_count, HEAD_DIM
        )
        result = jnp.einsum(
            "hqk,khd->qhd", attention, values_lane, preferred_element_type=jnp.float32
        ).reshape(rows_dev, 1, features)
        log_total = (highest + jnp.log(summed))[None, :, :, 0]
        return (result, log_total)

    initial = (
        jnp.zeros((rows_dev, lane_count, features), jnp.float32),
        jnp.zeros((lane_count, head_count, rows_dev), jnp.float32),
    )
    return lax.fori_loop(0, lane_count, one_lane, initial)


def attend_backward(query, keys_all, values_all, log_total, grad_mixed, query_tags, key_tags):
    rows_dev, lane_count, features = query.shape
    head_count = features // HEAD_DIM
    key_rows = keys_all.shape[0]

    def one_lane(lane_index, carry):
        scores, query_lane, keys_lane = lane_scores(
            query, keys_all, lane_index, query_tags, key_tags
        )
        values_lane = lax.dynamic_index_in_dim(values_all, lane_index, 1, False).reshape(
            key_rows, head_count, HEAD_DIM
        )
        grad_lane = lax.dynamic_index_in_dim(grad_mixed, lane_index, 1, False).reshape(
            rows_dev, head_count, HEAD_DIM
        )
        attention = jnp.exp(
            scores - lax.dynamic_index_in_dim(log_total, lane_index, 0, False)[:, :, None]
        )
        grad_attention = jnp.einsum(
            "qhd,khd->hqk", grad_lane, values_lane, preferred_element_type=jnp.float32
        )
        inner = jnp.sum(attention * grad_attention, axis=-1, keepdims=True)
        grad_scores = (attention * (grad_attention - inner)).astype(jnp.bfloat16)
        query_part = (
            jnp.einsum("hqk,khd->qhd", grad_scores, keys_lane, preferred_element_type=jnp.float32)
            * SCORE_SCALE
        )
        key_part = (
            jnp.einsum("hqk,qhd->khd", grad_scores, query_lane, preferred_element_type=jnp.float32)
            * SCORE_SCALE
        )
        value_part = jnp.einsum(
            "hqk,qhd->khd",
            attention.astype(jnp.bfloat16),
            grad_lane,
            preferred_element_type=jnp.float32,
        )
        stacked = jnp.stack(
            [key_part.reshape(key_rows, features), value_part.reshape(key_rows, features)], axis=1
        )
        key_terms = stacked[:, None]
        grad_query = query_part.reshape(rows_dev, 1, features)
        return (grad_query, key_terms)

    initial = (
        jnp.zeros((rows_dev, lane_count, features), jnp.float32),
        jnp.zeros((key_rows, lane_count, 2, features), jnp.float32),
    )
    return lax.fori_loop(0, lane_count, one_lane, initial)


def front(stream, layer_index, params, query_tags, key_tags, positions):
    (
        gain_one,
        shift_one,
        mat_qkv,
        bias_qkv,
        mat_out,
        bias_out,
        gain_two,
        shift_two,
        mat_up,
        bias_up,
        mat_down,
        bias_down,
    ) = [item[layer_index] for item in params]
    rows_dev, lane_count, width = stream.shape
    features = mat_qkv.shape[2]
    head_count = features // HEAD_DIM
    frame_place, row_place, column_place = positions
    first = layer_norm(stream, gain_one, shift_one).astype(jnp.bfloat16)
    projected = (
        jnp.einsum("tbd,dcf->tbcf", first, mat_qkv, preferred_element_type=jnp.float32) + bias_qkv
    )
    split = projected.reshape(rows_dev, lane_count, 3, head_count, HEAD_DIM)
    query = (
        rotate(split[:, :, 0], frame_place, row_place, column_place)
        .reshape(rows_dev, lane_count, features)
        .astype(jnp.bfloat16)
    )
    keys = (
        rotate(split[:, :, 1], frame_place, row_place, column_place)
        .reshape(rows_dev, lane_count, features)
        .astype(jnp.bfloat16)
    )
    values = projected[:, :, 2].astype(jnp.bfloat16)
    keys_all, values_all = (
        lax.all_gather(keys, "seq", axis=0, tiled=True),
        lax.all_gather(values, "seq", axis=0, tiled=True),
    )
    mixed_full, log_total = attend_forward(query, keys_all, values_all, query_tags, key_tags)
    mixed = mixed_full.astype(jnp.bfloat16)
    middle = (
        stream
        + sum_heads(jnp.einsum("tbf,fd->tbd", mixed, mat_out, preferred_element_type=jnp.float32))
        + bias_out
    )
    second = layer_norm(middle, gain_two, shift_two).astype(jnp.bfloat16)
    hidden = jnp.einsum("tbd,df->tbf", second, mat_up, preferred_element_type=jnp.float32) + bias_up
    activation = gelu_exact(hidden).astype(jnp.bfloat16)
    return (
        first,
        query,
        keys_all,
        values_all,
        log_total,
        mixed,
        middle,
        second,
        hidden,
        activation,
        mixed_full,
    )


def layer_backward(stream, gradient, layer_index, params, query_tags, key_tags, positions):
    (
        gain_one,
        shift_one,
        mat_qkv,
        bias_qkv,
        mat_out,
        bias_out,
        gain_two,
        shift_two,
        mat_up,
        bias_up,
        mat_down,
        bias_down,
    ) = [item[layer_index] for item in params]
    (
        first,
        query,
        keys_all,
        values_all,
        log_total,
        mixed,
        middle,
        second,
        hidden,
        activation,
        mixed_full,
    ) = front(stream, layer_index, params, query_tags, key_tags, positions)
    frame_place, row_place, column_place = positions
    rows_dev, lane_count, width = stream.shape
    features = query.shape[2]
    head_count = features // HEAD_DIM
    grad_low = gradient.astype(jnp.bfloat16)
    grad_w_down = jnp.einsum(
        "tbf,tbd->fd", activation, grad_low, preferred_element_type=jnp.float32
    )
    grad_b_down = jnp.sum(gradient, axis=(0, 1))
    grad_activation = jnp.einsum(
        "tbd,fd->tbf", grad_low, mat_down, preferred_element_type=jnp.float32
    )
    grad_hidden = jax.vjp(gelu_exact, hidden)[1](grad_activation)[0].astype(jnp.bfloat16)
    grad_b_up = jnp.sum(grad_hidden.astype(jnp.float32), axis=(0, 1))
    grad_w_up = jnp.einsum("tbd,tbf->df", second, grad_hidden, preferred_element_type=jnp.float32)
    grad_second = sum_inputs(
        jnp.einsum("tbf,df->tbd", grad_hidden, mat_up, preferred_element_type=jnp.float32)
    )
    middle_pull = jax.vjp(layer_norm, middle, gain_two, shift_two)[1]
    grad_inner, grad_gain_two, grad_shift_two = middle_pull(grad_second)
    grad_middle = gradient + grad_inner
    grad_b_out = jnp.sum(grad_middle, axis=(0, 1))
    middle_low = grad_middle.astype(jnp.bfloat16)
    grad_w_out = jnp.einsum("tbf,tbd->fd", mixed, middle_low, preferred_element_type=jnp.float32)
    grad_mixed = jnp.einsum(
        "tbd,fd->tbf", middle_low, mat_out, preferred_element_type=jnp.float32
    ).astype(jnp.bfloat16)
    grad_query, key_terms = attend_backward(
        query, keys_all, values_all, log_total, grad_mixed, query_tags, key_tags
    )
    returned = lax.psum_scatter(key_terms, "seq", scatter_dimension=0, tiled=True)
    turned_query = rotate(
        grad_query.reshape(rows_dev, lane_count, head_count, HEAD_DIM),
        -frame_place,
        -row_place,
        -column_place,
    )
    turned_keys = rotate(
        returned[:, :, 0].reshape(rows_dev, lane_count, head_count, HEAD_DIM),
        -frame_place,
        -row_place,
        -column_place,
    )
    grad_projected = jnp.stack(
        [
            turned_query.reshape(rows_dev, lane_count, features),
            turned_keys.reshape(rows_dev, lane_count, features),
            returned[:, :, 1],
        ],
        axis=2,
    ).astype(jnp.bfloat16)
    grad_b_qkv = jnp.sum(grad_projected.astype(jnp.float32), axis=(0, 1))
    grad_w_qkv = jnp.einsum(
        "tbd,tbcf->dcf", first, grad_projected, preferred_element_type=jnp.float32
    )
    grad_first = sum_inputs(
        jnp.einsum("tbcf,dcf->tbd", grad_projected, mat_qkv, preferred_element_type=jnp.float32)
    )
    first_pull = jax.vjp(layer_norm, stream, gain_one, shift_one)[1]
    grad_entry, grad_gain_one, grad_shift_one = first_pull(grad_first)
    grads = (
        grad_gain_one,
        grad_shift_one,
        grad_w_qkv,
        grad_b_qkv,
        grad_w_out,
        grad_b_out,
        grad_gain_two,
        grad_shift_two,
        grad_w_up,
        grad_b_up,
        grad_w_down,
        grad_b_down,
    )
    return (grad_middle + grad_entry, grads)


def per_device(
    tokens,
    d_out,
    norm1_gain,
    norm1_shift,
    w_qkv,
    b_qkv,
    w_out,
    b_out,
    norm2_gain,
    norm2_shift,
    w_up,
    b_up,
    w_down,
    b_down,
    episode_frames,
    live,
):
    rows_dev = tokens.shape[0]
    lane_count = tokens.shape[1] // MICRO
    total_rows = rows_dev * lax.axis_size("seq")
    local_positions = lax.axis_index("seq") * rows_dev + jnp.arange(rows_dev, dtype=jnp.int32)
    key_positions = jnp.arange(total_rows, dtype=jnp.int32)
    tagger = jax.vmap(episode_tags, in_axes=(0, None), out_axes=1)
    query_episode, query_frame, query_row, query_column = tagger(episode_frames, local_positions)
    key_episode, key_frame, key_row, key_column = tagger(episode_frames, key_positions)
    live_keys = lax.all_gather(live, "seq", axis=0, tiled=True)
    params = (
        norm1_gain,
        norm1_shift,
        w_qkv,
        b_qkv,
        w_out,
        b_out,
        norm2_gain,
        norm2_shift,
        w_up,
        b_up,
        w_down,
        b_down,
    )
    layer_grads = [None] * LAYERS
    outputs = []
    grad_tokens = []
    for micro_index in range(MICRO):
        first_lane = micro_index * lane_count
        last_lane = first_lane + lane_count
        query_tags = (query_episode[:, first_lane:last_lane], query_frame[:, first_lane:last_lane])
        key_tags = (
            key_episode[:, first_lane:last_lane],
            key_frame[:, first_lane:last_lane],
            live_keys[:, first_lane:last_lane],
        )
        positions = (
            query_frame[:, first_lane:last_lane],
            query_row[:, first_lane:last_lane],
            query_column[:, first_lane:last_lane],
        )
        stream = tokens[:, first_lane:last_lane].astype(jnp.float32)
        inputs = []
        gathered = []
        for layer_index in range(LAYERS):
            inputs.append(stream)
            layer_state = front(stream, layer_index, params, query_tags, key_tags, positions)
            gathered.append((layer_state[2], layer_state[3]))
            branch = jnp.einsum(
                "tbf,fd->tbd",
                layer_state[9],
                w_down[layer_index],
                preferred_element_type=jnp.float32,
            )
            stream = layer_state[6] + sum_heads(branch) + b_down[layer_index]
        outputs.append(stream)
        gradient = d_out[:, first_lane:last_lane]
        for layer_index in reversed(range(LAYERS)):
            gradient, grads = layer_backward(
                inputs[layer_index], gradient, layer_index, params, query_tags, key_tags, positions
            )
            if layer_grads[layer_index] is None:
                layer_grads[layer_index] = grads
            else:
                layer_grads[layer_index] = jax.tree.map(jnp.add, layer_grads[layer_index], grads)
        grad_tokens.append(gradient)
    stacked = [
        jnp.stack([layer_grads[layer_index][entry] for layer_index in range(LAYERS)])
        for entry in range(12)
    ]
    (
        grad_gain_one,
        grad_shift_one,
        grad_w_qkv,
        grad_b_qkv,
        grad_w_out,
        grad_b_out,
        grad_gain_two,
        grad_shift_two,
        grad_w_up,
        grad_b_up,
        grad_w_down,
        grad_b_down,
    ) = stacked
    in_sums = (
        lax.psum_scatter(grad_w_qkv, "seq", scatter_dimension=1, tiled=True),
        lax.psum_scatter(grad_w_up, "seq", scatter_dimension=1, tiled=True),
        lax.psum_scatter(grad_gain_one, "seq", scatter_dimension=1, tiled=True),
        lax.psum_scatter(grad_shift_one, "seq", scatter_dimension=1, tiled=True),
        lax.psum_scatter(grad_gain_two, "seq", scatter_dimension=1, tiled=True),
        lax.psum_scatter(grad_shift_two, "seq", scatter_dimension=1, tiled=True),
        lax.psum_scatter(grad_b_out, "seq", scatter_dimension=1, tiled=True),
        lax.psum_scatter(grad_b_down, "seq", scatter_dimension=1, tiled=True),
    )
    out_sums = (
        lax.psum_scatter(grad_w_out, "seq", scatter_dimension=2, tiled=True),
        lax.psum_scatter(grad_w_down, "seq", scatter_dimension=2, tiled=True),
    )
    bias_total = lax.psum((grad_b_qkv, grad_b_up), "seq")
    return (
        jnp.concatenate(outputs, axis=1),
        jnp.concatenate(grad_tokens, axis=1),
        in_sums[2],
        in_sums[3],
        in_sums[0],
        bias_total[0],
        out_sums[0],
        in_sums[6],
        in_sums[4],
        in_sums[5],
        in_sums[1],
        bias_total[1],
        out_sums[1],
        in_sums[7],
    )


MESH = pl.DeviceIdType.MESH
BF16 = jnp.bfloat16
F32 = jnp.float32
VMEM_BYTES = 60 * 1024 * 1024
PAIR = 128
VEC = 2048


def nn(left, right):
    return lax.dot_general(left, right, (((1,), (0,)), ((), ())), preferred_element_type=F32)


def nt(left, right):
    return lax.dot_general(left, right, (((1,), (1,)), ((), ())), preferred_element_type=F32)


def tn(left, right):
    return lax.dot_general(left, right, (((0,), (0,)), ((), ())), preferred_element_type=F32)


def at(start, size):
    return pl.ds(pl.multiple_of(start, size), size)


def remote(src, dst, send, recv, seq, tp):
    return pltpu.make_async_remote_copy(
        src_ref=src,
        dst_ref=dst,
        send_sem=send,
        recv_sem=recv,
        device_id=(seq, tp),
        device_id_type=MESH,
    )


def greet(partners):
    barrier = pltpu.get_barrier_semaphore()
    for seq, tp in partners:
        pl.semaphore_signal(barrier, inc=1, device_id=(seq, tp), device_id_type=MESH)
    pl.semaphore_wait(barrier, len(partners))


def whole(array):
    zeros = (0,) * array.ndim
    return pl.BlockSpec(array.shape, lambda s: zeros, pipeline_mode=pl.Buffered(1))


def whole_out(shape):
    zeros = (0,) * len(shape)
    return pl.BlockSpec(shape, lambda s: zeros)


ANYWHERE = pl.BlockSpec(memory_space=pl.ANY)


def turn_row(table, place, section):
    frequency = np.exp(np.arange(10, dtype=np.float32) * np.float32(-math.log(10000.0) / 10.0))
    angle = place.astype(np.float32)[:, None] * frequency
    for base in range(20 * section, PAIR, HEAD_DIM):
        table[0, :, base : base + 10] = np.cos(angle)
        table[0, :, base + 10 : base + 20] = np.cos(angle)
        table[1, :, base : base + 10] = -np.sin(angle)
        table[2, :, base + 10 : base + 20] = np.sin(angle)


def turn_constants(frames):
    within, ahead = np.zeros((3, FRAME, PAIR), np.float32), np.zeros((3, frames, PAIR), np.float32)
    turn_row(within, np.arange(FRAME) // GRID, 1)
    turn_row(within, np.arange(FRAME) % GRID, 2)
    for base in range(60, PAIR, HEAD_DIM):
        within[0, :, base : base + 4] = 1.0
    turn_row(ahead, np.arange(frames), 0)
    return jnp.asarray(within), jnp.asarray(ahead)


def turn(values, tables, back=False):
    cosine, lower, upper = tables
    pieces = []
    for start in range(0, values.shape[1], PAIR):
        slab = values[:, start : start + PAIR]
        moved = pltpu.roll(slab, PAIR - 10, 1) * lower + pltpu.roll(slab, 10, 1) * upper
        pieces.append(slab * cosine - moved if back else slab * cosine + moved)
    return jnp.concatenate(pieces, axis=1)


def tables_of(fixed_ref, frames_ref, chunk):
    return [fixed_ref[i] + frames_ref[i, pl.ds(chunk, 1), :] for i in range(3)]


def normed(stream):
    center = stream - jnp.mean(stream, axis=-1, keepdims=True)
    spread = jnp.mean(center * center, axis=-1, keepdims=True)
    scale = lax.rsqrt(spread + EPSILON)
    return center * scale, scale


def norm_pull(grad, gain, unit, scale):
    scaled = grad * gain
    return scale * (
        scaled
        - jnp.mean(scaled, axis=-1, keepdims=True)
        - unit * jnp.mean(scaled * unit, axis=-1, keepdims=True)
    )


def column_sum(values):
    return jnp.sum(values, axis=0, keepdims=True)


def gelu_both(hidden):
    normal = 0.5 + 0.5 * lax.erf(hidden * math.sqrt(0.5))
    density = jnp.exp(hidden * hidden * -0.5) * (1.0 / math.sqrt(2.0 * math.pi))
    return hidden * normal, normal + hidden * density


def project(stream, chunk, layer, pair, refs, outs, first_full):
    gain, shift, weight, bias, fixed, frames = refs
    query_ref, key_ref, value_ref, first_ref = outs
    unit, _ = normed(stream)
    first = (unit * gain[layer : layer + 1, :] + shift[layer : layer + 1, :]).astype(BF16)
    first_full[...] = first
    first_ref[...] = first_full[:, at(pair * PAIR, PAIR)]
    tables = tables_of(fixed, frames, chunk)
    query = nn(first, weight[0]) + bias[0, layer : layer + 1, :]
    query_ref[...] = (turn(query, tables) * SCORE_SCALE).astype(BF16)
    key = nn(first, weight[1]) + bias[1, layer : layer + 1, :]
    key_ref[...] = turn(key, tables).astype(BF16)
    value = nn(first, weight[2]) + bias[2, layer : layer + 1, :]
    value_ref[...] = value.astype(BF16)


class Relay:
    sems = 6

    def __init__(self, n, rows, buffer, other, sems, lives=None, live_other=None):
        self.n, self.rows, self.buffer, self.other = n, rows, buffer, other
        self.lives, self.live_other = lives, live_other
        self.z_send, self.z_recv, self.y_send, self.y_recv, self.c_send, self.c_recv = sems
        self.planes = n // 4
        self.me, self.core = lax.axis_index("seq"), lax.axis_index("tp")
        me = self.me
        self.x, self.y, self.z = lax.rem(me, 2), lax.rem(me // 2, 2), me // 4
        self.across = me + 2 - 4 * self.y

    @staticmethod
    def scratch(n):
        dma, planes = pltpu.SemaphoreType.DMA, n // 4
        shapes = [(planes, 2, 2)] * 2 + [(planes, 2)] * 2 + [(2 * planes,)] * 2
        return [dma(shape) for shape in shapes]

    @property
    def events(self):
        return self.planes

    def plane(self, step):
        return lax.rem(self.z + step, self.planes)

    def place(self, plane, lane):
        return plane * 4 + self.y * 2 + lane

    def reached(self):
        return [(step, far) for step in range(self.planes) for far in (0, 1) if step or far]

    def hello(self):
        barrier = pltpu.get_barrier_semaphore()
        partners = [(self.across, self.core), (self.me, 1 - self.core)]
        for step, far in self.reached():
            lane = 1 - self.x if far else self.x
            partners.append((self.place(self.plane(step), lane), self.core))
        for seq, tp in partners:
            pl.semaphore_signal(barrier, inc=1, device_id=(seq, tp), device_id_type=MESH)

    def met(self):
        pl.semaphore_wait(pltpu.get_barrier_semaphore(), 2 + len(self.reached()))

    def rows_of(self, side, seq):
        return self.buffer.at[side, at(seq * self.rows, self.rows), :]

    def block(self, side, pair):
        return self.buffer.at[side, at(pair * 2 * self.rows, 2 * self.rows), :]

    def items(self, pair):
        found = [self.block(self.core, pair)]
        if self.lives is not None:
            found.append(self.lives.at[at(pair * 2, 2)])
        return found

    def each(self, copy, what):
        for index in range(1 if self.lives is None else 2):
            getattr(copy(index), what)()

    def z_copy(self, step, far):
        def copy(index):
            lane = 1 - self.x if far else self.x
            if index == 0:
                source = self.other.at[self.core] if far else self.rows_of(self.core, self.me)
                target = self.rows_of(self.core, self.me)
            else:
                source = self.live_other if far else self.lives.at[self.me]
                target = self.lives.at[self.me]
            return remote(
                source,
                target,
                self.z_send.at[step, far, index],
                self.z_recv.at[step, far, index],
                self.place(self.plane(step), lane),
                self.core,
            )

        return copy

    def y_copy(self, plane, row):
        def copy(index):
            item = self.items(plane * 2 + row)[index]
            return remote(
                item,
                item,
                self.y_send.at[plane, index],
                self.y_recv.at[plane, index],
                self.across,
                self.core,
            )

        return copy

    def c_copy(self, pair, side):
        item = self.block(side, pair)
        return remote(
            item, item, self.c_send.at[pair], self.c_recv.at[pair], self.me, 1 - self.core
        )

    def begin(self):
        for step, far in self.reached():
            self.each(self.z_copy(step, far), "start")

    def arrive(self, event):
        for far in (0, 1) if event else (1,):
            self.each(self.z_copy(event, far), "wait_recv")
        plane = self.plane(self.planes - event)
        self.each(self.y_copy(plane, self.y), "start")
        self.c_copy(plane * 2 + self.y, self.core).start()

    def complete(self, event):
        plane = self.plane(self.planes - event)
        self.each(self.y_copy(plane, 1 - self.y), "wait_recv")
        self.c_copy(plane * 2 + 1 - self.y, self.core).start()

    def ready(self, event):
        plane = self.plane(self.planes - event)
        self.c_copy(plane * 2, 1 - self.core).wait_recv()
        self.c_copy(plane * 2 + 1, 1 - self.core).wait_recv()
        return plane

    def finish(self):
        for step, far in self.reached():
            self.each(self.z_copy(step, far), "wait_send")
        for plane in range(self.planes):
            self.each(self.y_copy(plane, self.y), "wait_send")
        for pair in range(2 * self.planes):
            self.c_copy(pair, self.core).wait_send()


def split_lanes(values, x, buffer, other, start, rows):
    half = values.shape[2] // 2
    zero, one = values[:, 0, :], values[:, 1, :]
    own, far = jnp.where(x == 0, zero, one), jnp.where(x == 0, one, zero)
    core = lax.axis_index("tp")
    own = jnp.where(core == 0, own[:, :half], own[:, half:]).astype(BF16)
    buffer[core, at(start, rows), :] = own
    for side in range(2):
        other[side] = far[:, side * half : (side + 1) * half].astype(BF16)


def gather_and_project(tokens, live, episode_frames, gain, shift, qkv, bias, fixed, ahead, n):
    rows, lanes, width = tokens.shape
    half = width // 2
    total = n * rows
    chunks = total // FRAME
    per_frame = FRAME // rows
    features = qkv.shape[3]
    slots = episode_frames.shape[1]

    def kernel(*refs):
        refs = list(refs)

        def take(count):
            taken = refs[:count]
            del refs[:count]
            return taken

        tokens_ref, live_ref, counts_ref, gain_ref, shift_ref, w_any, bias_ref = take(7)
        fixed_ref, ahead_ref = take(2)
        all_ref, mask_ref, frames_ref, q_ref, k_ref, v_ref, first_ref = take(7)
        other, lives, live_other, weight, full, w_sem = take(6)
        relay = Relay(n, rows, all_ref, other, take(Relay.sems), lives, live_other)
        load = pltpu.make_async_copy(w_any.at[0], weight, w_sem)
        load.start()
        relay.hello()
        x, me = relay.x, relay.me
        split_lanes(tokens_ref[...].astype(F32), x, all_ref, other, me * rows, rows)
        lane = lax.broadcasted_iota(jnp.int32, (1, FRAME), 1)
        here = lane // rows == lax.rem(me, per_frame)
        tiles = []
        for index in range(lanes):
            alive = live_ref[index : index + 1, :].astype(F32)
            alive = jnp.where(here, jnp.concatenate([alive] * per_frame, axis=1), 0.0)
            tiles.append(jnp.broadcast_to(alive, (8, FRAME)))
        lives[me] = jnp.where(x == 0, tiles[0], tiles[1])
        live_other[...] = jnp.where(x == 0, tiles[1], tiles[0])
        relay.met()
        relay.begin()

        counts = [counts_ref[x, slot] for slot in range(slots)]
        episodes, openings = [], []
        for frame in range(chunks):
            end, episode, opening = 0, 0, 0
            for slot in range(slots):
                end = end + counts[slot]
                passed = frame >= end
                episode = episode + passed.astype(jnp.int32)
                opening = opening + jnp.where(passed, counts[slot], 0)
            episodes.append(episode)
            openings.append(frame - opening)
        for index in range(3):
            table = []
            for frame in range(chunks):
                line = jnp.zeros((1, PAIR), F32)
                for choice in range(chunks):
                    line = jnp.where(
                        openings[frame] == choice, ahead_ref[index, choice : choice + 1, :], line
                    )
                table.append(line)
            frames_ref[index] = jnp.concatenate(
                table + [jnp.zeros((8 - chunks, PAIR), F32)], axis=0
            )
        load.wait()

        def project_frame(frame):
            place = at(frame * FRAME, FRAME)
            stream = jnp.concatenate([all_ref[0, place, :], all_ref[1, place, :]], axis=1)
            project(
                stream.astype(F32),
                frame,
                0,
                me // 2,
                (gain_ref, shift_ref, weight, bias_ref, fixed_ref, frames_ref),
                [ref.at[place, :] for ref in (q_ref, k_ref, v_ref, first_ref)],
                full,
            )

        for event in range(relay.events):
            relay.arrive(event)
            if event:
                relay.complete(event - 1)
            if event > 1:
                project_frame(relay.ready(event - 2))
        relay.complete(relay.events - 1)
        for event in range(max(0, relay.events - 2), relay.events):
            project_frame(relay.ready(event))
        relay.finish()

        for key_frame in range(chunks):
            alive = lives[key_frame * per_frame, 0:1, :]
            for part in range(1, per_frame):
                alive = alive + lives[key_frame * per_frame + part, 0:1, :]
            closed = (alive - 1.0) * -MASKED
            lines = []
            for query_frame in range(chunks):
                allowed = (episodes[query_frame] == episodes[key_frame]) & (
                    openings[key_frame] <= openings[query_frame]
                )
                lines.append(jnp.where(allowed, closed, MASKED))
            lines.append(jnp.zeros((PAIR - chunks, FRAME), F32))
            mask_ref[key_frame * FRAME : (key_frame + 1) * FRAME, :] = jnp.concatenate(
                lines, axis=0
            ).T.astype(BF16)

    in_vmem = pl.BlockSpec(memory_space=pltpu.VMEM)
    in_smem = pl.BlockSpec(memory_space=pltpu.SMEM)
    projected = jax.ShapeDtypeStruct((total, features), BF16)
    return pl.pallas_call(
        kernel,
        out_shape=(
            jax.ShapeDtypeStruct((2, total, half), BF16),
            jax.ShapeDtypeStruct((total, PAIR), BF16),
            jax.ShapeDtypeStruct((3, 8, PAIR), F32),
            projected,
            projected,
            projected,
            jax.ShapeDtypeStruct((total, PAIR), BF16),
        ),
        in_specs=[in_vmem, in_vmem, in_smem, in_vmem, in_vmem, ANYWHERE] + [in_vmem] * 3,
        out_specs=(in_vmem,) * 7,
        scratch_shapes=[
            pltpu.VMEM((2, rows, half), BF16),
            pltpu.VMEM((n, 8, FRAME), F32),
            pltpu.VMEM((8, FRAME), F32),
            pltpu.VMEM(qkv.shape[1:], BF16),
            pltpu.VMEM((FRAME, width), BF16),
            pltpu.SemaphoreType.DMA,
        ]
        + Relay.scratch(n),
        compiler_params=pltpu.CompilerParams(
            collective_id=0, has_side_effects=True, vmem_limit_bytes=VMEM_BYTES
        ),
        name="gather_and_project",
    )(tokens, live, episode_frames, gain, shift, qkv, bias, fixed, ahead)


def halves(ref):
    return jnp.concatenate([ref[0], ref[1]], axis=1).astype(F32)


def halves_spec(shape, chunks, behind, span=FRAME):
    return pl.BlockSpec(
        (2, span, shape[2]), lambda s: (0, jnp.clip(s - behind, 0, chunks - 1), 0)
    )


def layer_forward(layer, query, key, value, key_bias, stream, mats, rows_of, next_refs, d_out, n, identity):
    total, features = query.shape
    split = stream.ndim == 3
    width = mats[1].shape[1]
    rows_here = total // n
    hidden_units = mats[1].shape[2]
    chunks = total // FRAME
    heads = features // HEAD_DIM
    slabs = features // PAIR
    columns = 256
    last = next_refs is None
    b_out, gain, shift, b_up, b_down = rows_of
    mat_out, mat_up, mat_down = mats

    def kernel(*refs):
        refs = list(refs)

        def take(count):
            taken = refs[:count]
            del refs[:count]
            return taken

        q_ref, k_ref, v_ref, kb_ref, x_ref = take(5)
        wo_any, wu_any, wd_any = take(3)
        bo_ref, gain_ref, shift_ref, bu_ref, bd_ref = take(5)
        if not last:
            wq_any, ngain, nshift, nbias, fixed, frames = take(6)
        if d_out is not None:
            (d_ref,) = take(1)
        p_ref, r_ref, mixed_ref, middle_ref, second_ref, act_ref, gp_ref, x_out = take(8)
        if not last:
            nq_ref, nk_ref, nv_ref, nf_ref = take(4)
        if d_out is not None:
            (d_all,) = take(1)
        wo, wu, wd, mid, full = take(5)
        if not last:
            (wq,) = take(1)
        a_send, a_recv, b_send, b_recv, w_sem, send_sem, recv_sem = take(7)
        relay = None
        if d_out is not None:
            buffer, other, d_sem = take(3)
            relay = Relay(n, rows_here, buffer, other, take(Relay.sems))

        step = pl.program_id(0)
        me, core = lax.axis_index("seq"), lax.axis_index("tp")

        items = [(wo_any, wo), (wu_any, wu), (wd_any, wd)]
        if not last:
            items.append((wq_any, wq))

        def load(index):
            source, target = items[index]
            return pltpu.make_async_copy(
                source.at[layer if index < 3 else layer + 1], target, w_sem.at[index]
            )

        def exchange(kind, chunk):
            source, target = ((a_send, a_recv), (b_send, b_recv))[kind]
            return remote(
                source.at[chunk],
                target.at[chunk],
                send_sem.at[kind, chunk],
                recv_sem.at[kind, chunk],
                me,
                1 - core,
            )

        @pl.when(step == 0)
        def _():
            for index in range(len(items)):
                load(index).start()
            if relay is None:
                greet([(me, 1 - core)])
            else:
                relay.hello()
                split_lanes(d_ref[...], relay.x, buffer, other, me * rows_here, rows_here)
                relay.met()
                relay.begin()

        if relay is not None:
            for event in range(relay.events):

                @pl.when(step == 1 + event // 2)
                def _():
                    relay.arrive(event)

                @pl.when(step == 2 + event // 2)
                def _():
                    relay.complete(event)

            @pl.when(step == chunks + 1)
            def _():
                for event in range(relay.events):
                    relay.ready(event)
                relay.finish()
                pltpu.make_async_copy(buffer, d_all, d_sem).start()

        lane = lax.broadcasted_iota(jnp.int32, (1, PAIR), 1)
        sides = [(lane < HEAD_DIM).astype(F32).astype(BF16), (lane >= HEAD_DIM).astype(F32).astype(BF16)]
        for frame in range(chunks):

            @pl.when(step == frame)
            def _():
                keys = FRAME * (frame + 1)
                mask = kb_ref[:keys, :]
                asked = jnp.broadcast_to((lane == frame).astype(F32), (FRAME, PAIR)).astype(BF16)

                def one_slab(slab, carry):
                    lanes = at(slab * PAIR, PAIR)
                    q2, v2 = q_ref[:, lanes], v_ref[:keys, lanes]
                    k2 = jnp.concatenate([k_ref[:keys, lanes], mask], axis=1)
                    sums = []
                    for side in range(2):
                        scores = nt(jnp.concatenate([q2 * sides[side], asked], axis=1), k2)
                        highest = jnp.max(scores, axis=1, keepdims=True)
                        shifted = jnp.exp(scores - highest).astype(BF16)
                        p_ref[0, slab * 2 + side, :keys, :] = shifted.T
                        sums.append(nn(shifted, v2 * sides[side] + sides[1 - side]))
                    low_side = lane < HEAD_DIM
                    divisor = 1.0 / jnp.where(
                        low_side, pltpu.roll(sums[0], HEAD_DIM, 1), pltpu.roll(sums[1], HEAD_DIM, 1)
                    )
                    r_ref[:, lanes] = divisor
                    mixed_ref[:, lanes] = (jnp.where(low_side, sums[0], sums[1]) * divisor).astype(BF16)
                    return carry

                lax.fori_loop(0, slabs, one_slab, 0)

        @pl.when(step == 0)
        def _():
            load(0).wait()

        @pl.when(step < chunks)
        def _():
            a_send[step] = nn(mixed_ref[...], wo[...]).astype(BF16)
            exchange(0, step).start()

        @pl.when(step == 1)
        def _():
            load(1).wait()
            load(2).wait()

        @pl.when((step >= 1) & (step <= chunks))
        def _():
            chunk = step - 1
            exchange(0, chunk).wait_recv()
            middle = (halves(x_ref) if split else x_ref[...]) + (a_send[chunk].astype(F32) + a_recv[chunk].astype(F32))
            middle = middle + bo_ref[layer : layer + 1, :]
            middle_ref[...] = middle
            mid[lax.rem(chunk, 2)] = middle
            unit, _ = normed(middle)
            second = (unit * gain_ref[layer : layer + 1, :] + shift_ref[layer : layer + 1, :]).astype(BF16)
            full[...] = second
            second_ref[...] = full[:, at((me // 2) * PAIR, PAIR)]
            parts = [slice(start, start + columns) for start in range(0, hidden_units, columns)]
            hidden = nn(second, wu[:, parts[0]])
            for index, part in enumerate(parts):
                following = nn(second, wu[:, parts[index + 1]]) if index + 1 < len(parts) else None
                act, slope = gelu_both(hidden + bu_ref[layer : layer + 1, part])
                act_ref[:, part] = act.astype(BF16)
                gp_ref[:, part] = slope.astype(BF16)
                hidden = following
            b_send[chunk] = nn(act_ref[...], wd[...]).astype(BF16)
            exchange(1, chunk).start()

        if not last:

            @pl.when(step == 2)
            def _():
                load(3).wait()

        @pl.when(step >= 2)
        def _():
            chunk = step - 2
            exchange(1, chunk).wait_recv()
            result = (
                mid[lax.rem(chunk, 2)]
                + (b_send[chunk].astype(F32) + b_recv[chunk].astype(F32))
                + bd_ref[layer : layer + 1, :]
            )
            x_out[...] = result
            if not last:
                project(
                    result,
                    chunk,
                    layer + 1,
                    me // 2,
                    (ngain, nshift, wq, nbias, fixed, frames),
                    (nq_ref, nk_ref, nv_ref, nf_ref),
                    full,
                )

        @pl.when(step == chunks + 1)
        def _():
            for kind in range(2):
                for chunk in range(chunks):
                    exchange(kind, chunk).wait_send()
            if relay is not None:
                pltpu.make_async_copy(buffer, d_all, d_sem).wait()

    def rows(columns, behind):
        return pl.BlockSpec(
            (FRAME, columns), lambda s: (jnp.clip(s - behind, 0, chunks - 1), 0)
        )

    in_specs = [rows(features, 0), whole(key), whole(value), whole(key_bias)]
    in_specs += [halves_spec(stream.shape, chunks, 1) if split else rows(width, 1)]
    in_specs += [ANYWHERE] * 3 + [whole(item) for item in rows_of]
    operands = [query, key, value, key_bias, stream, *mats, *rows_of]
    if not last:
        in_specs += [ANYWHERE] + [whole(item) for item in next_refs[1:]]
        operands += list(next_refs)
    if d_out is not None:
        in_specs += [whole(d_out)]
        operands += [d_out]
    out_shape = [
        jax.ShapeDtypeStruct((chunks, heads, total, FRAME), BF16),
        jax.ShapeDtypeStruct((total, features), F32),
        jax.ShapeDtypeStruct((total, features), BF16),
        jax.ShapeDtypeStruct((total, width), F32),
        jax.ShapeDtypeStruct((total, PAIR), BF16),
        jax.ShapeDtypeStruct((total, hidden_units), BF16),
        jax.ShapeDtypeStruct((total, hidden_units), BF16),
        jax.ShapeDtypeStruct((total, width), F32),
    ]
    out_specs = [
        pl.BlockSpec((1, heads, total, FRAME), lambda s: (jnp.minimum(s, chunks - 1), 0, 0, 0)),
        rows(features, 0),
        rows(features, 0),
        rows(width, 1),
        rows(PAIR, 1),
        rows(hidden_units, 1),
        rows(hidden_units, 1),
        rows(width, 2),
    ]
    scratch = [
        pltpu.VMEM(mat_out.shape[1:], BF16),
        pltpu.VMEM(mat_up.shape[1:], BF16),
        pltpu.VMEM(mat_down.shape[1:], BF16),
        pltpu.VMEM((2, FRAME, width), F32),
        pltpu.VMEM((FRAME, width), BF16),
    ]
    if not last:
        out_shape += [jax.ShapeDtypeStruct((total, features), BF16)] * 3
        out_shape += [jax.ShapeDtypeStruct((total, PAIR), BF16)]
        out_specs += [rows(features, 2)] * 3 + [rows(PAIR, 2)]
    if d_out is not None:
        out_shape += [jax.ShapeDtypeStruct((2, total, width // 2), BF16)]
        out_specs += [ANYWHERE]
        scratch += [pltpu.VMEM(next_refs[0].shape[1:], BF16)]
    scratch += [pltpu.VMEM((chunks, FRAME, width), BF16)] * 4
    scratch += [
        pltpu.SemaphoreType.DMA((4,)),
        pltpu.SemaphoreType.DMA((2, chunks)),
        pltpu.SemaphoreType.DMA((2, chunks)),
    ]
    if d_out is not None:
        scratch += [
            pltpu.VMEM((2, total, width // 2), BF16),
            pltpu.VMEM((2, rows_here, width // 2), BF16),
            pltpu.SemaphoreType.DMA,
        ]
        scratch += Relay.scratch(n)
    return pl.pallas_call(
        kernel,
        grid=(chunks + 2,),
        out_shape=out_shape,
        in_specs=in_specs,
        out_specs=out_specs,
        scratch_shapes=scratch,
        compiler_params=pltpu.CompilerParams(
            collective_id=identity, has_side_effects=True, vmem_limit_bytes=VMEM_BYTES
        ),
        name=f"layer_forward_{layer}",
    )(*operands)


class Swap:
    def __init__(self, ships, lane_rows):
        self.ships, self.lane_rows = ships, lane_rows
        self.count = len(ships) + len(lane_rows)

    def operands(self):
        return [*self.ships, *[item for item, _ in self.lane_rows]]

    def in_specs(self):
        return [whole(item) for item in self.ships] + [ANYWHERE] * len(self.lane_rows)

    def outputs(self):
        shapes, specs = [], []
        for item in self.ships:
            shape = (item.shape[0] // 2, item.shape[1])
            shapes.append(jax.ShapeDtypeStruct(shape, F32))
            specs.append(whole_out(shape))
        for item, count in self.lane_rows:
            shapes.append(jax.ShapeDtypeStruct((count or item.shape[0], item.shape[1]), item.dtype))
            specs.append(ANYWHERE)
        return shapes, specs

    def scratch(self):
        if not self.count:
            return []
        buffers = [pltpu.VMEM((item.shape[0] // 2, item.shape[1]), BF16) for item in self.ships]
        return buffers * 2 + [pltpu.SemaphoreType.DMA((self.count,))] * 2

    def bind(self, sources, targets, scratch):
        ships = len(self.ships)
        me, core = lax.axis_index("seq"), lax.axis_index("tp")
        x = lax.rem(me, 2)
        beside = me + 1 - 2 * x
        half = PAIR // 2

        def copy(index):
            if index < ships:
                source, target = scratch[index], scratch[ships + index]
            else:
                source, target = sources[index], targets[index]
                count = self.lane_rows[index - ships][1]
                if count:
                    source = source.at[at(beside * count, count), :]
            send, recv = scratch[2 * ships].at[index], scratch[2 * ships + 1].at[index]
            return remote(source, target, send, recv, beside, core)

        def start():
            for index in range(self.count):
                if index < ships:
                    scratch[index][...] = sources[index][at((1 - x) * half, half), :].astype(BF16)
                copy(index).start()

        def finish():
            for index in range(self.count):
                copy(index).wait_recv()
                if index < ships:
                    own = sources[index][at(x * half, half), :]
                    targets[index][...] = own + scratch[ships + index][...].astype(F32)
            for index in range(self.count):
                copy(index).wait_send()

        return start, finish


def attention_backward(
    probs, divisor, mixed, query, key, value, grad_mixed, first, fixed, frames, swap, swap_qkv, identity
):
    total, features = query.shape
    chunks = total // FRAME
    slabs = features // PAIR
    half = PAIR // 2

    def kernel(*refs):
        refs = list(refs)

        def take(count):
            taken = refs[:count]
            del refs[:count]
            return taken

        p_ref, r_ref, o_ref, q_ref, k_ref, v_ref, g_ref, first_ref, fixed_ref, frames_ref = take(10)
        sources = take(swap.count)
        dq_ref, dk_ref, dv_ref, qkv_out = take(4)
        targets = take(swap.count)
        dk_sum, dv_sum, first_turned = take(3)
        if swap_qkv:
            qkv_own, qkv_send, qkv_recv, qkv_sems = take(4)
        start, finish = swap.bind(sources, targets, refs)

        step = pl.program_id(0)
        me, core = lax.axis_index("seq"), lax.axis_index("tp")
        x = lax.rem(me, 2)
        beside = me + 1 - 2 * x

        def qkv_copy(slab):
            return remote(
                qkv_send.at[slab],
                qkv_recv.at[slab],
                qkv_sems.at[0, slab],
                qkv_sems.at[1, slab],
                beside,
                core,
            )

        @pl.when(step == 0)
        def _():
            greet([(beside, core)])
            start()
            first_turned[...] = first_ref[...].T

        lane = lax.broadcasted_iota(jnp.int32, (1, PAIR), 1)
        sides = [(lane < HEAD_DIM).astype(F32).astype(BF16), (lane >= HEAD_DIM).astype(F32).astype(BF16)]
        turned = k_ref[...].T
        ones = jnp.broadcast_to((lane < 2).astype(F32), (total, PAIR)).astype(BF16)
        values = jnp.concatenate([v_ref[...], ones], axis=1)
        for frame in reversed(range(chunks)):
            keys = FRAME * (frame + 1)
            own = slice(frame * FRAME, keys)
            tables = tables_of(fixed_ref, frames_ref, frame)
            scaled = (g_ref[own, :].astype(F32) * r_ref[own, :]).astype(BF16)
            inner = scaled.astype(F32) * o_ref[own, :].astype(F32)
            query_parts, score_parts, prob_parts, q_parts, g_parts = [], [], [], [], []
            for side in range(2):
                delta = jnp.sum(
                    jnp.where((lane < HEAD_DIM) == (side == 0), inner, 0.0), axis=1, keepdims=True
                )
                coarse = delta.astype(BF16).astype(F32)
                rest = jnp.where(lane == 0, -coarse, jnp.where(lane == 1, coarse - delta, 0.0))
                g2 = scaled * sides[side]
                attention = p_ref[frame, side, :keys, :]
                grad = nt(values[:keys], jnp.concatenate([g2, rest.astype(BF16)], axis=1))
                grad_scores = (attention.astype(F32) * grad).astype(BF16)
                query_parts.append(nn(turned[side * HEAD_DIM : (side + 1) * HEAD_DIM, :keys], grad_scores))
                score_parts.append(grad_scores)
                prob_parts.append(attention)
                q_parts.append(q_ref[own, :] * sides[side])
                g_parts.append(g2)
            grad_query = jnp.concatenate(query_parts, axis=0).T
            key_parts = nn(jnp.concatenate(score_parts, axis=1), jnp.concatenate(q_parts, axis=0))
            value_parts = nn(jnp.concatenate(prob_parts, axis=1), jnp.concatenate(g_parts, axis=0))
            dq_ref[own, :] = (turn(grad_query, tables, True) * SCORE_SCALE).astype(BF16)
            if frame == chunks - 1:
                dk_sum[...] = key_parts
                dv_sum[...] = value_parts
            else:
                dk_sum[:keys, :] += key_parts
                dv_sum[:keys, :] += value_parts
            dk_ref[own, :] = turn(dk_sum[own, :], tables, True).astype(BF16)
            dv_ref[own, :] = dv_sum[own, :].astype(BF16)

        for part, ref in enumerate((dq_ref, dk_ref, dv_ref)):
            piece = slice(part * PAIR, (part + 1) * PAIR)
            terms = nn(first_turned[...], ref[...])
            if swap_qkv:
                qkv_own[step, :, piece] = terms
                qkv_send[step, :, piece] = qkv_own[step, at((1 - x) * half, half), piece].astype(BF16)
            else:
                qkv_out[:, at(part * features + step * PAIR, PAIR)] = terms
        if swap_qkv:
            qkv_copy(step).start()

        @pl.when(step == slabs - 1)
        def _():
            finish()
            for slab in range(slabs if swap_qkv else 0):
                qkv_copy(slab).wait_recv()
                for part in range(3):
                    piece = slice(part * PAIR, (part + 1) * PAIR)
                    place = part * features + slab * PAIR
                    qkv_out[:, place : place + PAIR] = qkv_own[
                        slab, at(x * half, half), piece
                    ] + qkv_recv[slab, :, piece].astype(F32)
            for slab in range(slabs if swap_qkv else 0):
                qkv_copy(slab).wait_send()

    slab = pl.BlockSpec((total, PAIR), lambda s: (0, s))
    in_specs = [pl.BlockSpec((chunks, 2, total, FRAME), lambda s: (0, s, 0, 0))]
    in_specs += [slab] * 6 + [whole(first), whole(fixed), whole(frames)]
    in_specs += swap.in_specs()
    qkv_shape = (half if swap_qkv else PAIR, 3 * features)
    shapes, specs = swap.outputs()
    out_shape = [jax.ShapeDtypeStruct((total, features), BF16)] * 3
    out_shape += [jax.ShapeDtypeStruct(qkv_shape, F32)] + shapes
    out_specs = [slab] * 3 + [whole_out(qkv_shape)] + specs
    scratch = [pltpu.VMEM((total, PAIR), F32)] * 2 + [pltpu.VMEM((PAIR, total), BF16)]
    if swap_qkv:
        scratch += [pltpu.VMEM((slabs, PAIR, 3 * PAIR), F32)]
        scratch += [pltpu.VMEM((slabs, half, 3 * PAIR), BF16)] * 2
        scratch += [pltpu.SemaphoreType.DMA((2, slabs))]
    scratch += swap.scratch()
    return pl.pallas_call(
        kernel,
        grid=(slabs,),
        out_shape=out_shape,
        in_specs=in_specs,
        out_specs=out_specs,
        scratch_shapes=scratch,
        compiler_params=pltpu.CompilerParams(
            collective_id=identity, has_side_effects=True, vmem_limit_bytes=VMEM_BYTES
        ),
        name=f"attention_backward_{identity}",
    )(
        probs,
        divisor,
        mixed,
        query,
        key,
        value,
        grad_mixed,
        first,
        fixed,
        frames,
        *swap.operands(),
    )


def rows_backward(entry, upper, identity, span, swap):
    top, bottom = len(entry) == 1, upper is None
    if not top:
        above, entry = entry[0], entry[1:]
        split = entry[3].ndim == 3
    total = entry[0].shape[1] if top else entry[0].shape[0]
    chunks = total // span
    columns = 256
    ahead = 0 if top else 1
    if top:
        width = 2 * entry[0].shape[2]
    else:
        features, width = entry[0].shape[1], entry[4].shape[1]
    if not bottom:
        layer = upper[0]
        hidden_units, mixed_features = upper[1].shape[1], upper[5].shape[1]
    place_rows = total // lax.axis_size("seq")

    def kernel(*refs):
        refs = list(refs)

        def take(count):
            taken = refs[:count]
            del refs[:count]
            return taken

        if top:
            (d_out_ref,) = take(1)
        else:
            dq_ref, dk_ref, dv_ref, x_ref, dm_ref, wq, gain1 = take(7)
        if not bottom:
            act_ref, gp_ref, middle_ref, second_ref, mixed_ref = take(5)
            wo_any, wu_any, wd_any, gain2 = take(4)
        sources = take(swap.count)
        if not top:
            (vec1,) = take(1)
        if not bottom:
            dmid_out, dmix_out, out_sum, up_sum, down_sum, vec2 = take(6)
        else:
            dx_out, dx_other, vec_other = take(3)
        targets = take(swap.count)
        if not top:
            a_send, a_recv = take(2)
        if not bottom:
            b_send, b_recv, grad_keep, hidden_keep, low_keep, wo, wu, wd, w_sem = take(9)
        else:
            dx_keep, dx_send, dx_recv, vec_recv, x_send_sem, x_recv_sem = take(6)
        send_sem, recv_sem = take(2)
        start_swap, finish_swap = swap.bind(sources, targets, refs)

        step = pl.program_id(0)
        me, core = lax.axis_index("seq"), lax.axis_index("tp")
        pair = at((me // 2) * PAIR, PAIR)
        x = lax.rem(me, 2)
        beside = me + 1 - 2 * x

        def exchange(kind, chunk):
            source, target = (a_send, a_recv) if kind == 0 else (b_send, b_recv)
            return remote(
                source.at[chunk],
                target.at[chunk],
                send_sem.at[kind, chunk],
                recv_sem.at[kind, chunk],
                me,
                1 - core,
            )

        def load(index):
            source, target = ((wd_any, wd), (wu_any, wu), (wo_any, wo))[index]
            return pltpu.make_async_copy(source.at[layer], target, w_sem.at[index])

        @pl.when(step == 0)
        def _():
            if not bottom:
                for index in range(3):
                    load(index).start()
                out_sum[...] = jnp.zeros_like(out_sum)
                up_sum[...] = jnp.zeros_like(up_sum)
                down_sum[...] = jnp.zeros_like(down_sum)
                vec2[...] = jnp.zeros_like(vec2)
            if not top:
                vec1[...] = jnp.zeros_like(vec1)
            greet([(me, 1 - core)] + ([(beside, core)] if bottom or swap.count else []))
            start_swap()

        if not top:

            @pl.when(step < chunks)
            def _():
                partial = None
                for part, ref in enumerate((dq_ref, dk_ref, dv_ref)):
                    grad = ref[...]
                    term = nt(grad, wq[0, part])
                    partial = term if partial is None else partial + term
                    vec1[part : part + 1, :] += column_sum(grad.astype(F32))
                a_send[step] = partial.astype(BF16)
                exchange(0, step).start()

        @pl.when((step >= ahead) & (step < chunks + ahead))
        def _():
            chunk = step - ahead
            if top:
                gradient = halves(d_out_ref)
            else:
                exchange(0, chunk).wait_recv()
                grad_first = a_send[chunk].astype(F32) + a_recv[chunk].astype(F32)
                unit, scale = normed(halves(x_ref) if split else x_ref[...])
                for start, sums in ((3, column_sum(grad_first * unit)), (5, column_sum(grad_first))):
                    for side in range(width // features):
                        piece = slice(side * features, (side + 1) * features)
                        vec1[start + side : start + side + 1, :] += sums[:, piece]
                gradient = dm_ref[...] + norm_pull(
                    grad_first, gain1[above : above + 1, :], unit, scale
                )
            if bottom:
                dx_keep[at(chunk * span, span), :] = gradient
                return

            @pl.when(chunk == 0)
            def _():
                load(0).wait()

            grad_keep[lax.rem(chunk, 2)] = gradient
            vec2[1:2, :width] += column_sum(gradient)
            low = gradient.astype(BF16)
            low_keep[...] = low
            low_columns = low_keep[:, pair]
            second = second_ref[...]
            parts = [slice(start, start + columns) for start in range(0, hidden_units, columns)]
            grad_act = nt(low, wd[parts[0], :])
            for index, part in enumerate(parts):
                following = nt(low, wd[parts[index + 1], :]) if index + 1 < len(parts) else None
                grad_hidden = grad_act * gp_ref[:, part].astype(F32)
                hidden_keep[:, part] = grad_hidden.astype(BF16)
                vec2[0:1, part] += column_sum(grad_hidden)
                grad_act = following

            @pl.when(chunk == 0)
            def _():
                load(1).wait()

            b_send[chunk] = nt(hidden_keep[...], wu[...]).astype(BF16)
            down_sum[...] += tn(low_columns, act_ref[...])
            up_sum[...] += tn(second, hidden_keep[...])
            exchange(1, chunk).start()

        if not bottom:

            @pl.when(step == ahead + 1)
            def _():
                load(2).wait()

            @pl.when(step >= ahead + 1)
            def _():
                chunk = step - ahead - 1
                exchange(1, chunk).wait_recv()
                grad_second = b_send[chunk].astype(F32) + b_recv[chunk].astype(F32)
                unit, scale = normed(middle_ref[...])
                vec2[2:3, :width] += column_sum(grad_second * unit)
                vec2[3:4, :width] += column_sum(grad_second)
                grad_middle = grad_keep[lax.rem(chunk, 2)] + norm_pull(
                    grad_second, gain2[layer : layer + 1, :], unit, scale
                )
                dmid_out[...] = grad_middle
                vec2[4:5, :width] += column_sum(grad_middle)
                low = grad_middle.astype(BF16)
                low_keep[...] = low
                out_sum[...] += tn(low_keep[:, pair], mixed_ref[...])
                dmix_out[...] = nt(low, wo[...]).astype(BF16)

        if bottom:

            def x_copy(index):
                source, target = ((dx_send, dx_recv), (vec1, vec_recv))[index]
                return remote(
                    source, target, x_send_sem.at[index], x_recv_sem.at[index], beside, core
                )

            @pl.when(step == chunks)
            def _():
                dx_send[...] = dx_keep[at(beside * place_rows, place_rows), :].astype(BF16)
                x_copy(0).start()
                x_copy(1).start()
                dx_out[...] = dx_keep[at(me * place_rows, place_rows), :]
                x_copy(0).wait_recv()
                x_copy(1).wait_recv()
                dx_other[...] = dx_recv[...].astype(F32)
                vec_other[...] = vec_recv[...]
                x_copy(0).wait_send()
                x_copy(1).wait_send()

        @pl.when(step == pl.num_programs(0) - 1)
        def _():
            for kind in ([] if top else [0]) + ([] if bottom else [1]):
                for chunk in range(chunks):
                    exchange(kind, chunk).wait_send()
            finish_swap()

    def rows(columns, behind):
        return pl.BlockSpec(
            (span, columns), lambda s: (jnp.clip(s - behind, 0, chunks - 1), 0)
        )

    vec = jax.ShapeDtypeStruct((8, VEC), F32)
    operands, in_specs, out_shape, out_specs, scratch = [], [], [], [], []
    if top:
        operands += list(entry)
        in_specs += [halves_spec(entry[0].shape, chunks, 0, span)]
    else:
        operands += list(entry)
        in_specs += [rows(features, 0)] * 3
        in_specs += [halves_spec(entry[3].shape, chunks, 1, span) if split else rows(width, 1)]
        in_specs += [rows(width, 1)]
        in_specs += [
            pl.BlockSpec(
                (1, *entry[5].shape[1:]),
                lambda s: (above, 0, 0, 0),
                pipeline_mode=pl.Buffered(1),
            ),
            whole(entry[6]),
        ]
        narrow = jax.ShapeDtypeStruct((8, features), F32)
        out_shape += [narrow]
        out_specs += [whole_out((8, features))]
        scratch += [pltpu.VMEM((chunks, span, width), BF16)] * 2
    if not bottom:
        operands += list(upper[1:])
        in_specs += [rows(hidden_units, ahead)] * 2 + [rows(width, ahead + 1), rows(PAIR, ahead)]
        in_specs += [rows(mixed_features, ahead + 1)] + [ANYWHERE] * 3 + [whole(upper[9])]
        sums = [mixed_features, hidden_units, hidden_units]
        out_shape += [
            jax.ShapeDtypeStruct((total, width), F32),
            jax.ShapeDtypeStruct((total, mixed_features), BF16),
        ]
        out_shape += [jax.ShapeDtypeStruct((PAIR, size), F32) for size in sums] + [vec]
        out_specs += [rows(width, ahead + 1), rows(mixed_features, ahead + 1)]
        out_specs += [whole_out((PAIR, size)) for size in sums] + [whole_out((8, VEC))]
        scratch += [pltpu.VMEM((chunks, span, width), BF16)] * 2
        scratch += [
            pltpu.VMEM((2, span, width), F32),
            pltpu.VMEM((span, hidden_units), BF16),
            pltpu.VMEM((span, width), BF16),
            pltpu.VMEM(upper[6].shape[1:], BF16),
            pltpu.VMEM(upper[7].shape[1:], BF16),
            pltpu.VMEM(upper[8].shape[1:], BF16),
            pltpu.SemaphoreType.DMA((3,)),
        ]
    else:
        out_shape += [
            jax.ShapeDtypeStruct((place_rows, width), F32),
            jax.ShapeDtypeStruct((place_rows, width), F32),
            narrow,
        ]
        out_specs += [whole_out((place_rows, width))] * 2 + [whole_out((8, features))]
        scratch += [
            pltpu.VMEM((total, width), F32),
            pltpu.VMEM((place_rows, width), BF16),
            pltpu.VMEM((place_rows, width), BF16),
            pltpu.VMEM((8, features), F32),
            pltpu.SemaphoreType.DMA((2,)),
            pltpu.SemaphoreType.DMA((2,)),
        ]
    scratch += [pltpu.SemaphoreType.DMA((2, chunks))] * 2
    operands += swap.operands()
    in_specs += swap.in_specs()
    shapes, specs = swap.outputs()
    out_shape += shapes
    out_specs += specs
    scratch += swap.scratch()
    return pl.pallas_call(
        kernel,
        grid=(chunks + (1 if top or bottom else 2),),
        out_shape=out_shape,
        in_specs=in_specs,
        out_specs=out_specs,
        scratch_shapes=scratch,
        compiler_params=pltpu.CompilerParams(
            collective_id=identity, has_side_effects=True, vmem_limit_bytes=VMEM_BYTES
        ),
        name=f"rows_backward_{identity}",
    )(*operands)


def assemble(sums, vecs, lanes, n, features, hidden_units):
    place = lanes[1].shape[0]
    width = lanes[1].shape[1]
    half = PAIR // 2

    def kernel(*refs):
        refs = list(refs)

        def take(count):
            taken = refs[:count]
            del refs[:count]
            return taken

        qkvs, outs, ups, downs = take(LAYERS), take(LAYERS), take(LAYERS), take(LAYERS)
        vec_refs = [take(4) for _ in range(LAYERS)]
        out_lane, out_other, dx_own, dx_other = take(4)
        out_ref, dx_ref, gain1, shift1, g_qkv, b_qkv, g_out, b_out = take(8)
        gain2, shift2, g_up, b_up, g_down, b_down = take(6)
        out_own, sem = refs
        me = lax.axis_index("seq")
        x = lax.rem(me, 2)
        fetch = pltpu.make_async_copy(out_lane.at[at(me * place, place), :], out_own, sem)
        fetch.start()

        for layer in range(LAYERS):
            for part in range(3):
                g_qkv[layer, part] = qkvs[layer][:, part * features : (part + 1) * features]
            for ref, target in ((outs, g_out), (ups, g_up), (downs, g_down)):
                target[layer] = ref[layer][...]

        for layer, (entry_own, entry_other, upper_own, upper_other) in enumerate(vec_refs):
            line = slice(layer, layer + 1)
            for part in range(3):
                row = slice(part, part + 1)
                b_qkv[part, line, :] = entry_own[row, :] + entry_other[row, :]
            b_up[line, :] = upper_own[0:1, :hidden_units] + upper_other[0:1, :hidden_units]

            def owned(mine, other, row):
                wide = mine.shape[1]
                place = (me // 2) * PAIR
                pair = at(lax.rem(place, wide), PAIR)
                both = mine[row : row + 1, pair] + other[row : row + 1, pair]
                for later in range(1, width // wide):
                    line = slice(row + later, row + later + 1)
                    both = jnp.where(place // wide == later, mine[line, pair] + other[line, pair], both)
                return jnp.where(x == 0, both[:, :half], both[:, half:])

            gain1[line, :] = owned(entry_own, entry_other, 3)
            shift1[line, :] = owned(entry_own, entry_other, 5)
            b_down[line, :] = owned(upper_own, upper_other, 1)
            gain2[line, :] = owned(upper_own, upper_other, 2)
            shift2[line, :] = owned(upper_own, upper_other, 3)
            b_out[line, :] = owned(upper_own, upper_other, 4)

        def both_lanes(target, mine, other):
            target[:, 0, :] = jnp.where(x == 0, mine, other)
            target[:, 1, :] = jnp.where(x == 0, other, mine)

        both_lanes(dx_ref, dx_own[...], dx_other[...])
        fetch.wait()
        both_lanes(out_ref, out_own[...], out_other[...])

    def f32(*shape):
        return jax.ShapeDtypeStruct(shape, F32)

    in_vmem = pl.BlockSpec(memory_space=pltpu.VMEM)
    flat = []
    for kind in range(4):
        flat += [sums[layer][kind] for layer in range(LAYERS)]
    for layer in range(LAYERS):
        flat += list(vecs[layer])
    flat += list(lanes)
    small = f32(LAYERS, width // n)
    return pl.pallas_call(
        kernel,
        out_shape=(
            f32(place, 2, width),
            f32(place, 2, width),
            small,
            small,
            f32(LAYERS, 3, half, features),
            f32(3, LAYERS, features),
            f32(LAYERS, half, features),
            small,
            small,
            small,
            f32(LAYERS, half, hidden_units),
            f32(LAYERS, hidden_units),
            f32(LAYERS, half, hidden_units),
            small,
        ),
        in_specs=[in_vmem] * (len(flat) - 4) + [ANYWHERE] + [in_vmem] * 3,
        out_specs=(in_vmem,) * 14,
        scratch_shapes=[pltpu.VMEM((place, width), F32), pltpu.SemaphoreType.DMA],
        compiler_params=pltpu.CompilerParams(vmem_limit_bytes=VMEM_BYTES),
        name="assemble",
    )(*flat)


def per_chip(
    tokens,
    d_out,
    norm1_gain,
    norm1_shift,
    w_qkv,
    b_qkv,
    w_out,
    b_out,
    norm2_gain,
    norm2_shift,
    w_up,
    b_up,
    w_down,
    b_down,
    episode_frames,
    live,
):
    n = lax.axis_size("seq")
    rows = tokens.shape[0]
    features = w_qkv.shape[3]
    fixed, ahead = turn_constants(rows * n // FRAME)
    qkv, qkv_bias = w_qkv.transpose(0, 2, 1, 3), b_qkv.transpose(1, 0, 2)

    gathered, key_bias, frames, query, key, value, first = gather_and_project(
        tokens, live.T, episode_frames, norm1_gain, norm1_shift, qkv, qkv_bias, fixed, ahead, n
    )
    streams, kept, d_lane = [gathered], [], None
    for layer in range(LAYERS):
        following = None
        if layer + 1 < LAYERS:
            following = (qkv, norm1_gain, norm1_shift, qkv_bias, fixed, frames)
        results = layer_forward(
            layer,
            query,
            key,
            value,
            key_bias,
            streams[layer],
            (w_out, w_up, w_down),
            (b_out, norm2_gain, norm2_shift, b_up, b_down),
            following,
            d_out if layer == 0 else None,
            n,
            1 + layer,
        )
        kept.append((query, key, value, first, *results[:7]))
        streams.append(results[7])
        if following is not None:
            query, key, value, first = results[8:12]
        if layer == 0:
            d_lane = results[-1]

    sums = [[None] * 4 for _ in range(LAYERS)]
    vecs = [[None] * 4 for _ in range(LAYERS)]
    entry, later = (d_lane,), None
    for layer in reversed(range(LAYERS)):
        query, key, value, first, probs, divisor, mixed, middle, second, act, slope = kept[layer]
        upper = (
            layer,
            act,
            slope,
            middle,
            second,
            mixed,
            w_out,
            w_up,
            w_down,
            norm2_gain,
        )
        identity = 1 + LAYERS + 2 * (LAYERS - 1 - layer)
        if later is None:
            results = rows_backward(entry, upper, identity, 2 * FRAME, Swap([], []))
        else:
            swap = Swap(later[:2], [(later[2], 0), (streams[LAYERS], rows)])
            vec1, *results = rows_backward(entry, upper, identity, FRAME, swap)
            results, swapped = results[:6], results[6:]
            sums[layer + 1][3], sums[layer + 1][0] = swapped[:2]
            vecs[layer + 1][3], out_other = swapped[2:]
            vecs[layer + 1][0] = vec1
        grad_middle, grad_mixed, out_sum, up_sum, down_sum, vec2 = results
        vecs[layer][2] = vec2
        last = layer == 0
        if last:
            swap = Swap([out_sum, up_sum, down_sum], [(vec2, 0), (vecs[layer + 1][0], 0)])
        else:
            swap = Swap([out_sum, up_sum], [])
        results = attention_backward(
            probs,
            divisor,
            mixed,
            query,
            key,
            value,
            grad_mixed,
            first,
            fixed,
            frames,
            swap,
            last,
            identity + 1,
        )
        grad_query, grad_key, grad_value, qkv_sum = results[:4]
        if last:
            sums[layer] = [qkv_sum, *results[4:7]]
            vecs[layer][3], vecs[layer + 1][1] = results[7:9]
        else:
            sums[layer][1:3] = results[4:6]
            later = [down_sum, qkv_sum, vec2]
        entry = (
            layer,
            grad_query,
            grad_key,
            grad_value,
            streams[layer],
            grad_middle,
            qkv,
            norm1_gain,
        )
    vec1, dx_own, dx_other, vec_other = rows_backward(
        entry, None, 1 + 3 * LAYERS, FRAME, Swap([], [])
    )
    vecs[0][:2] = [vec1, vec_other]
    results = list(
        assemble(
            sums,
            vecs,
            (streams[LAYERS], out_other, dx_own, dx_other),
            n,
            features,
            w_up.shape[2],
        )
    )
    results[4] = results[4].transpose(0, 2, 1, 3)
    results[5] = results[5].transpose(1, 0, 2)
    results[6] = results[6].transpose(0, 2, 1)
    results[12] = results[12].transpose(0, 2, 1)
    return tuple(results)


def lane_fits(mesh, tokens):
    n = mesh.shape["seq"]
    positions, lanes, width = tokens.shape
    rows = positions // n
    return (
        lanes == 2
        and n % 4 == 0
        and positions <= 4 * FRAME
        and positions % FRAME == 0
        and FRAME % rows == 0
        and width // n * 2 == PAIR
        and mesh.shape["tp"] == 2
    )


def solution(mesh):
    placed = (
        P("seq", None, None),
        P("seq", None, None),
        P(),
        P(),
        P(None, None, None, "tp"),
        P(None, None, "tp"),
        P(None, "tp", None),
        P(),
        P(),
        P(),
        P(None, None, "tp"),
        P(None, "tp"),
        P(None, "tp", None),
        P(),
        P(),
        P("seq", None),
    )
    def mapped(body):
        return jax.shard_map(
            body,
            mesh=mesh,
            in_specs=placed,
            out_specs=(
                P("seq", None, None),
                P("seq", None, None),
                P(None, "seq"),
                P(None, "seq"),
                P(None, "seq", None, "tp"),
                P(None, None, "tp"),
                P(None, "tp", "seq"),
                P(None, "seq"),
                P(None, "seq"),
                P(None, "seq"),
                P(None, "seq", "tp"),
                P(None, "tp"),
                P(None, "tp", "seq"),
                P(None, "seq"),
            ),
            check_vma=False,
        )

    def run(tokens, *others):
        if lane_fits(mesh, tokens):
            return mapped(per_chip)(tokens, *others)
        return mapped(per_device)(tokens, *others)

    return run
```

```python
import math

import jax
import jax.numpy as jnp
import numpy as np
from jax import lax
from jax.experimental import pallas as pl
from jax.experimental.pallas import tpu as pltpu
from jax.sharding import PartitionSpec as P

HEAD_DIM = 64
GRID = 16
FRAME = 256
LAYERS = 2
MICRO = 2


EPSILON = 1e-06
MASKED = -1e30
SCORE_SCALE = 0.125


def layer_norm(stream, norm_gain, norm_shift):
    center = stream - jnp.mean(stream, axis=-1, keepdims=True)
    spread = jnp.mean(center * center, axis=-1, keepdims=True)
    return center * lax.rsqrt(spread + EPSILON) * norm_gain + norm_shift


def rotate(values, frame_place, row_place, column_place):
    frequency = jnp.exp(jnp.arange(10, dtype=jnp.float32) * (-math.log(10000.0) / 10.0))
    pieces = []
    for section, place in enumerate((frame_place, row_place, column_place)):
        lower = values[..., 20 * section : 20 * section + 10]
        upper = values[..., 20 * section + 10 : 20 * section + 20]
        angles = place.astype(jnp.float32)[..., None, None] * frequency
        cosine = jnp.cos(angles)
        sine_part = jnp.sin(angles)
        pieces.append(lower * cosine - upper * sine_part)
        pieces.append(lower * sine_part + upper * cosine)
    pieces.append(values[..., 60:])
    return jnp.concatenate(pieces, axis=-1)


def episode_tags(frame_counts, positions):
    endings = jnp.cumsum(frame_counts) * FRAME
    passed = (positions[:, None] >= endings[None, :]).astype(jnp.int32)
    episode = jnp.sum(passed, axis=1)
    opening = jnp.sum(passed * frame_counts[None, :], axis=1)
    frame_index = positions // FRAME - opening
    within = positions % FRAME
    return (episode, frame_index, within // GRID, within % GRID)


def gelu_exact(values):
    return jax.nn.gelu(values, approximate=False)


def sum_heads(partial_sum):
    return lax.psum(partial_sum.astype(jnp.bfloat16), "tp").astype(jnp.float32)


def sum_inputs(partial_sum):
    return lax.psum(partial_sum.astype(jnp.bfloat16), "tp").astype(jnp.float32)


def lane_scores(query, keys_all, lane_index, query_tags, key_tags):
    head_count = query.shape[2] // HEAD_DIM
    query_lane = lax.dynamic_index_in_dim(query, lane_index, 1, False).reshape(
        query.shape[0], head_count, HEAD_DIM
    )
    keys_lane = lax.dynamic_index_in_dim(keys_all, lane_index, 1, False).reshape(
        keys_all.shape[0], head_count, HEAD_DIM
    )
    query_episode, query_frame = [
        lax.dynamic_index_in_dim(item, lane_index, 1, False) for item in query_tags
    ]
    key_episode, key_frame, key_live = [
        lax.dynamic_index_in_dim(item, lane_index, 1, False) for item in key_tags
    ]
    allowed = (
        (query_episode[:, None] == key_episode[None, :])
        & (key_frame[None, :] <= query_frame[:, None])
        & (key_live[None, :] > 0)
    )
    scores = (
        jnp.einsum("qhd,khd->hqk", query_lane, keys_lane, preferred_element_type=jnp.float32)
        * SCORE_SCALE
    )
    return (jnp.where(allowed[None], scores, MASKED), query_lane, keys_lane)


def attend_forward(query, keys_all, values_all, query_tags, key_tags):
    rows_dev, lane_count, features = query.shape
    head_count = features // HEAD_DIM

    def one_lane(lane_index, carry):
        scores, query_lane, keys_lane = lane_scores(
            query, keys_all, lane_index, query_tags, key_tags
        )
        highest = jnp.max(scores, axis=-1, keepdims=True)
        shifted = jnp.exp(scores - highest)
        summed = jnp.sum(shifted, axis=-1, keepdims=True)
        attention = (shifted / summed).astype(jnp.bfloat16)
        values_lane = lax.dynamic_index_in_dim(values_all, lane_index, 1, False).reshape(
            values_all.shape[0], head_count, HEAD_DIM
        )
        result = jnp.einsum(
            "hqk,khd->qhd", attention, values_lane, preferred_element_type=jnp.float32
        ).reshape(rows_dev, 1, features)
        log_total = (highest + jnp.log(summed))[None, :, :, 0]
        return (result, log_total)

    initial = (
        jnp.zeros((rows_dev, lane_count, features), jnp.float32),
        jnp.zeros((lane_count, head_count, rows_dev), jnp.float32),
    )
    return lax.fori_loop(0, lane_count, one_lane, initial)


def attend_backward(query, keys_all, values_all, log_total, grad_mixed, query_tags, key_tags):
    rows_dev, lane_count, features = query.shape
    head_count = features // HEAD_DIM
    key_rows = keys_all.shape[0]

    def one_lane(lane_index, carry):
        scores, query_lane, keys_lane = lane_scores(
            query, keys_all, lane_index, query_tags, key_tags
        )
        values_lane = lax.dynamic_index_in_dim(values_all, lane_index, 1, False).reshape(
            key_rows, head_count, HEAD_DIM
        )
        grad_lane = lax.dynamic_index_in_dim(grad_mixed, lane_index, 1, False).reshape(
            rows_dev, head_count, HEAD_DIM
        )
        attention = jnp.exp(
            scores - lax.dynamic_index_in_dim(log_total, lane_index, 0, False)[:, :, None]
        )
        grad_attention = jnp.einsum(
            "qhd,khd->hqk", grad_lane, values_lane, preferred_element_type=jnp.float32
        )
        inner = jnp.sum(attention * grad_attention, axis=-1, keepdims=True)
        grad_scores = (attention * (grad_attention - inner)).astype(jnp.bfloat16)
        query_part = (
            jnp.einsum("hqk,khd->qhd", grad_scores, keys_lane, preferred_element_type=jnp.float32)
            * SCORE_SCALE
        )
        key_part = (
            jnp.einsum("hqk,qhd->khd", grad_scores, query_lane, preferred_element_type=jnp.float32)
            * SCORE_SCALE
        )
        value_part = jnp.einsum(
            "hqk,qhd->khd",
            attention.astype(jnp.bfloat16),
            grad_lane,
            preferred_element_type=jnp.float32,
        )
        stacked = jnp.stack(
            [key_part.reshape(key_rows, features), value_part.reshape(key_rows, features)], axis=1
        )
        key_terms = stacked[:, None]
        grad_query = query_part.reshape(rows_dev, 1, features)
        return (grad_query, key_terms)

    initial = (
        jnp.zeros((rows_dev, lane_count, features), jnp.float32),
        jnp.zeros((key_rows, lane_count, 2, features), jnp.float32),
    )
    return lax.fori_loop(0, lane_count, one_lane, initial)


def front(stream, layer_index, params, query_tags, key_tags, positions):
    (
        gain_one,
        shift_one,
        mat_qkv,
        bias_qkv,
        mat_out,
        bias_out,
        gain_two,
        shift_two,
        mat_up,
        bias_up,
        mat_down,
        bias_down,
    ) = [item[layer_index] for item in params]
    rows_dev, lane_count, width = stream.shape
    features = mat_qkv.shape[2]
    head_count = features // HEAD_DIM
    frame_place, row_place, column_place = positions
    first = layer_norm(stream, gain_one, shift_one).astype(jnp.bfloat16)
    projected = (
        jnp.einsum("tbd,dcf->tbcf", first, mat_qkv, preferred_element_type=jnp.float32) + bias_qkv
    )
    split = projected.reshape(rows_dev, lane_count, 3, head_count, HEAD_DIM)
    query = (
        rotate(split[:, :, 0], frame_place, row_place, column_place)
        .reshape(rows_dev, lane_count, features)
        .astype(jnp.bfloat16)
    )
    keys = (
        rotate(split[:, :, 1], frame_place, row_place, column_place)
        .reshape(rows_dev, lane_count, features)
        .astype(jnp.bfloat16)
    )
    values = projected[:, :, 2].astype(jnp.bfloat16)
    keys_all, values_all = (
        lax.all_gather(keys, "seq", axis=0, tiled=True),
        lax.all_gather(values, "seq", axis=0, tiled=True),
    )
    mixed_full, log_total = attend_forward(query, keys_all, values_all, query_tags, key_tags)
    mixed = mixed_full.astype(jnp.bfloat16)
    middle = (
        stream
        + sum_heads(jnp.einsum("tbf,fd->tbd", mixed, mat_out, preferred_element_type=jnp.float32))
        + bias_out
    )
    second = layer_norm(middle, gain_two, shift_two).astype(jnp.bfloat16)
    hidden = jnp.einsum("tbd,df->tbf", second, mat_up, preferred_element_type=jnp.float32) + bias_up
    activation = gelu_exact(hidden).astype(jnp.bfloat16)
    return (
        first,
        query,
        keys_all,
        values_all,
        log_total,
        mixed,
        middle,
        second,
        hidden,
        activation,
        mixed_full,
    )


def layer_backward(stream, gradient, layer_index, params, query_tags, key_tags, positions):
    (
        gain_one,
        shift_one,
        mat_qkv,
        bias_qkv,
        mat_out,
        bias_out,
        gain_two,
        shift_two,
        mat_up,
        bias_up,
        mat_down,
        bias_down,
    ) = [item[layer_index] for item in params]
    (
        first,
        query,
        keys_all,
        values_all,
        log_total,
        mixed,
        middle,
        second,
        hidden,
        activation,
        mixed_full,
    ) = front(stream, layer_index, params, query_tags, key_tags, positions)
    frame_place, row_place, column_place = positions
    rows_dev, lane_count, width = stream.shape
    features = query.shape[2]
    head_count = features // HEAD_DIM
    grad_low = gradient.astype(jnp.bfloat16)
    grad_w_down = jnp.einsum(
        "tbf,tbd->fd", activation, grad_low, preferred_element_type=jnp.float32
    )
    grad_b_down = jnp.sum(gradient, axis=(0, 1))
    grad_activation = jnp.einsum(
        "tbd,fd->tbf", grad_low, mat_down, preferred_element_type=jnp.float32
    )
    grad_hidden = jax.vjp(gelu_exact, hidden)[1](grad_activation)[0].astype(jnp.bfloat16)
    grad_b_up = jnp.sum(grad_hidden.astype(jnp.float32), axis=(0, 1))
    grad_w_up = jnp.einsum("tbd,tbf->df", second, grad_hidden, preferred_element_type=jnp.float32)
    grad_second = sum_inputs(
        jnp.einsum("tbf,df->tbd", grad_hidden, mat_up, preferred_element_type=jnp.float32)
    )
    middle_pull = jax.vjp(layer_norm, middle, gain_two, shift_two)[1]
    grad_inner, grad_gain_two, grad_shift_two = middle_pull(grad_second)
    grad_middle = gradient + grad_inner
    grad_b_out = jnp.sum(grad_middle, axis=(0, 1))
    middle_low = grad_middle.astype(jnp.bfloat16)
    grad_w_out = jnp.einsum("tbf,tbd->fd", mixed, middle_low, preferred_element_type=jnp.float32)
    grad_mixed = jnp.einsum(
        "tbd,fd->tbf", middle_low, mat_out, preferred_element_type=jnp.float32
    ).astype(jnp.bfloat16)
    grad_query, key_terms = attend_backward(
        query, keys_all, values_all, log_total, grad_mixed, query_tags, key_tags
    )
    returned = lax.psum_scatter(key_terms, "seq", scatter_dimension=0, tiled=True)
    turned_query = rotate(
        grad_query.reshape(rows_dev, lane_count, head_count, HEAD_DIM),
        -frame_place,
        -row_place,
        -column_place,
    )
    turned_keys = rotate(
        returned[:, :, 0].reshape(rows_dev, lane_count, head_count, HEAD_DIM),
        -frame_place,
        -row_place,
        -column_place,
    )
    grad_projected = jnp.stack(
        [
            turned_query.reshape(rows_dev, lane_count, features),
            turned_keys.reshape(rows_dev, lane_count, features),
            returned[:, :, 1],
        ],
        axis=2,
    ).astype(jnp.bfloat16)
    grad_b_qkv = jnp.sum(grad_projected.astype(jnp.float32), axis=(0, 1))
    grad_w_qkv = jnp.einsum(
        "tbd,tbcf->dcf", first, grad_projected, preferred_element_type=jnp.float32
    )
    grad_first = sum_inputs(
        jnp.einsum("tbcf,dcf->tbd", grad_projected, mat_qkv, preferred_element_type=jnp.float32)
    )
    first_pull = jax.vjp(layer_norm, stream, gain_one, shift_one)[1]
    grad_entry, grad_gain_one, grad_shift_one = first_pull(grad_first)
    grads = (
        grad_gain_one,
        grad_shift_one,
        grad_w_qkv,
        grad_b_qkv,
        grad_w_out,
        grad_b_out,
        grad_gain_two,
        grad_shift_two,
        grad_w_up,
        grad_b_up,
        grad_w_down,
        grad_b_down,
    )
    return (grad_middle + grad_entry, grads)


def per_device(
    tokens,
    d_out,
    norm1_gain,
    norm1_shift,
    w_qkv,
    b_qkv,
    w_out,
    b_out,
    norm2_gain,
    norm2_shift,
    w_up,
    b_up,
    w_down,
    b_down,
    episode_frames,
    live,
):
    rows_dev = tokens.shape[0]
    lane_count = tokens.shape[1] // MICRO
    total_rows = rows_dev * lax.axis_size("seq")
    local_positions = lax.axis_index("seq") * rows_dev + jnp.arange(rows_dev, dtype=jnp.int32)
    key_positions = jnp.arange(total_rows, dtype=jnp.int32)
    tagger = jax.vmap(episode_tags, in_axes=(0, None), out_axes=1)
    query_episode, query_frame, query_row, query_column = tagger(episode_frames, local_positions)
    key_episode, key_frame, key_row, key_column = tagger(episode_frames, key_positions)
    live_keys = lax.all_gather(live, "seq", axis=0, tiled=True)
    params = (
        norm1_gain,
        norm1_shift,
        w_qkv,
        b_qkv,
        w_out,
        b_out,
        norm2_gain,
        norm2_shift,
        w_up,
        b_up,
        w_down,
        b_down,
    )
    layer_grads = [None] * LAYERS
    outputs = []
    grad_tokens = []
    for micro_index in range(MICRO):
        first_lane = micro_index * lane_count
        last_lane = first_lane + lane_count
        query_tags = (query_episode[:, first_lane:last_lane], query_frame[:, first_lane:last_lane])
        key_tags = (
            key_episode[:, first_lane:last_lane],
            key_frame[:, first_lane:last_lane],
            live_keys[:, first_lane:last_lane],
        )
        positions = (
            query_frame[:, first_lane:last_lane],
            query_row[:, first_lane:last_lane],
            query_column[:, first_lane:last_lane],
        )
        stream = tokens[:, first_lane:last_lane].astype(jnp.float32)
        inputs = []
        gathered = []
        for layer_index in range(LAYERS):
            inputs.append(stream)
            layer_state = front(stream, layer_index, params, query_tags, key_tags, positions)
            gathered.append((layer_state[2], layer_state[3]))
            branch = jnp.einsum(
                "tbf,fd->tbd",
                layer_state[9],
                w_down[layer_index],
                preferred_element_type=jnp.float32,
            )
            stream = layer_state[6] + sum_heads(branch) + b_down[layer_index]
        outputs.append(stream)
        gradient = d_out[:, first_lane:last_lane]
        for layer_index in reversed(range(LAYERS)):
            gradient, grads = layer_backward(
                inputs[layer_index], gradient, layer_index, params, query_tags, key_tags, positions
            )
            if layer_grads[layer_index] is None:
                layer_grads[layer_index] = grads
            else:
                layer_grads[layer_index] = jax.tree.map(jnp.add, layer_grads[layer_index], grads)
        grad_tokens.append(gradient)
    stacked = [
        jnp.stack([layer_grads[layer_index][entry] for layer_index in range(LAYERS)])
        for entry in range(12)
    ]
    (
        grad_gain_one,
        grad_shift_one,
        grad_w_qkv,
        grad_b_qkv,
        grad_w_out,
        grad_b_out,
        grad_gain_two,
        grad_shift_two,
        grad_w_up,
        grad_b_up,
        grad_w_down,
        grad_b_down,
    ) = stacked
    in_sums = (
        lax.psum_scatter(grad_w_qkv, "seq", scatter_dimension=1, tiled=True),
        lax.psum_scatter(grad_w_up, "seq", scatter_dimension=1, tiled=True),
        lax.psum_scatter(grad_gain_one, "seq", scatter_dimension=1, tiled=True),
        lax.psum_scatter(grad_shift_one, "seq", scatter_dimension=1, tiled=True),
        lax.psum_scatter(grad_gain_two, "seq", scatter_dimension=1, tiled=True),
        lax.psum_scatter(grad_shift_two, "seq", scatter_dimension=1, tiled=True),
        lax.psum_scatter(grad_b_out, "seq", scatter_dimension=1, tiled=True),
        lax.psum_scatter(grad_b_down, "seq", scatter_dimension=1, tiled=True),
    )
    out_sums = (
        lax.psum_scatter(grad_w_out, "seq", scatter_dimension=2, tiled=True),
        lax.psum_scatter(grad_w_down, "seq", scatter_dimension=2, tiled=True),
    )
    bias_total = lax.psum((grad_b_qkv, grad_b_up), "seq")
    return (
        jnp.concatenate(outputs, axis=1),
        jnp.concatenate(grad_tokens, axis=1),
        in_sums[2],
        in_sums[3],
        in_sums[0],
        bias_total[0],
        out_sums[0],
        in_sums[6],
        in_sums[4],
        in_sums[5],
        in_sums[1],
        bias_total[1],
        out_sums[1],
        in_sums[7],
    )


MESH = pl.DeviceIdType.MESH
BF16 = jnp.bfloat16
F32 = jnp.float32
VMEM_BYTES = 60 * 1024 * 1024
PAIR = 128
VEC = 2048


def nn(left, right):
    return lax.dot_general(left, right, (((1,), (0,)), ((), ())), preferred_element_type=F32)


def nt(left, right):
    return lax.dot_general(left, right, (((1,), (1,)), ((), ())), preferred_element_type=F32)


def tn(left, right):
    return lax.dot_general(left, right, (((0,), (0,)), ((), ())), preferred_element_type=F32)


def at(start, size):
    return pl.ds(pl.multiple_of(start, size), size)


def remote(src, dst, send, recv, seq, tp):
    return pltpu.make_async_remote_copy(
        src_ref=src,
        dst_ref=dst,
        send_sem=send,
        recv_sem=recv,
        device_id=(seq, tp),
        device_id_type=MESH,
    )


def greet(partners):
    barrier = pltpu.get_barrier_semaphore()
    for seq, tp in partners:
        pl.semaphore_signal(barrier, inc=1, device_id=(seq, tp), device_id_type=MESH)
    pl.semaphore_wait(barrier, len(partners))


def whole(array):
    zeros = (0,) * array.ndim
    return pl.BlockSpec(array.shape, lambda s: zeros, pipeline_mode=pl.Buffered(1))


def whole_out(shape):
    zeros = (0,) * len(shape)
    return pl.BlockSpec(shape, lambda s: zeros)


ANYWHERE = pl.BlockSpec(memory_space=pl.ANY)


def turn_row(table, place, section):
    frequency = np.exp(np.arange(10, dtype=np.float32) * np.float32(-math.log(10000.0) / 10.0))
    angle = place.astype(np.float32)[:, None] * frequency
    for base in range(20 * section, PAIR, HEAD_DIM):
        table[0, :, base : base + 10] = np.cos(angle)
        table[0, :, base + 10 : base + 20] = np.cos(angle)
        table[1, :, base : base + 10] = -np.sin(angle)
        table[2, :, base + 10 : base + 20] = np.sin(angle)


def turn_constants(frames):
    within, ahead = np.zeros((3, FRAME, PAIR), np.float32), np.zeros((3, frames, PAIR), np.float32)
    turn_row(within, np.arange(FRAME) // GRID, 1)
    turn_row(within, np.arange(FRAME) % GRID, 2)
    for base in range(60, PAIR, HEAD_DIM):
        within[0, :, base : base + 4] = 1.0
    turn_row(ahead, np.arange(frames), 0)
    return jnp.asarray(within), jnp.asarray(ahead)


def turn(values, tables, back=False):
    cosine, lower, upper = tables
    pieces = []
    for start in range(0, values.shape[1], PAIR):
        slab = values[:, start : start + PAIR]
        moved = pltpu.roll(slab, PAIR - 10, 1) * lower + pltpu.roll(slab, 10, 1) * upper
        pieces.append(slab * cosine - moved if back else slab * cosine + moved)
    return jnp.concatenate(pieces, axis=1)


def tables_of(fixed_ref, frames_ref, chunk):
    return [fixed_ref[i] + frames_ref[i, pl.ds(chunk, 1), :] for i in range(3)]


def normed(stream):
    center = stream - jnp.mean(stream, axis=-1, keepdims=True)
    spread = jnp.mean(center * center, axis=-1, keepdims=True)
    scale = lax.rsqrt(spread + EPSILON)
    return center * scale, scale


def norm_pull(grad, gain, unit, scale):
    scaled = grad * gain
    return scale * (
        scaled
        - jnp.mean(scaled, axis=-1, keepdims=True)
        - unit * jnp.mean(scaled * unit, axis=-1, keepdims=True)
    )


def keep_norm(unit, scale, unit_ref, scale_ref):
    unit_ref[...] = unit.astype(BF16)
    scale_ref[...] = jnp.broadcast_to(scale, scale_ref.shape)


def kept_norm(unit_ref, scale_ref):
    copies = unit_ref.shape[1] // scale_ref.shape[1]
    return unit_ref[...].astype(F32), jnp.concatenate([scale_ref[...]] * copies, axis=1)


def column_sum(values):
    return jnp.sum(values, axis=0, keepdims=True)


def gelu_both(hidden):
    normal = 0.5 + 0.5 * lax.erf(hidden * math.sqrt(0.5))
    density = jnp.exp(hidden * hidden * -0.5) * (1.0 / math.sqrt(2.0 * math.pi))
    return hidden * normal, normal + hidden * density


def project(stream, chunk, layer, pair, refs, outs, first_full):
    gain, shift, weight, bias, fixed, frames = refs
    query_ref, key_ref, value_ref, first_ref, unit_ref, scale_ref = outs
    unit, scale = normed(stream)
    keep_norm(unit, scale, unit_ref, scale_ref)
    first = (unit * gain[layer : layer + 1, :] + shift[layer : layer + 1, :]).astype(BF16)
    first_full[...] = first
    first_ref[...] = first_full[:, at(pair * PAIR, PAIR)]
    tables = tables_of(fixed, frames, chunk)
    query = nn(first, weight[0]) + bias[0, layer : layer + 1, :]
    query_ref[...] = (turn(query, tables) * SCORE_SCALE).astype(BF16)
    key = nn(first, weight[1]) + bias[1, layer : layer + 1, :]
    key_ref[...] = turn(key, tables).astype(BF16)
    value = nn(first, weight[2]) + bias[2, layer : layer + 1, :]
    value_ref[...] = value.astype(BF16)


class Relay:
    sems = 6

    def __init__(self, n, rows, buffer, other, sems, lives=None, live_other=None):
        self.n, self.rows, self.buffer, self.other = n, rows, buffer, other
        self.lives, self.live_other = lives, live_other
        self.z_send, self.z_recv, self.y_send, self.y_recv, self.c_send, self.c_recv = sems
        self.planes = n // 4
        self.me, self.core = lax.axis_index("seq"), lax.axis_index("tp")
        me = self.me
        self.x, self.y, self.z = lax.rem(me, 2), lax.rem(me // 2, 2), me // 4
        self.across = me + 2 - 4 * self.y

    @staticmethod
    def scratch(n):
        dma, planes = pltpu.SemaphoreType.DMA, n // 4
        shapes = [(planes, 2, 2)] * 2 + [(planes, 2)] * 2 + [(2 * planes,)] * 2
        return [dma(shape) for shape in shapes]

    @property
    def events(self):
        return self.planes

    def plane(self, step):
        return lax.rem(self.z + step, self.planes)

    def place(self, plane, lane):
        return plane * 4 + self.y * 2 + lane

    def reached(self):
        return [(step, far) for step in range(self.planes) for far in (0, 1) if step or far]

    def hello(self):
        barrier = pltpu.get_barrier_semaphore()
        partners = [(self.across, self.core), (self.me, 1 - self.core)]
        for step, far in self.reached():
            lane = 1 - self.x if far else self.x
            partners.append((self.place(self.plane(step), lane), self.core))
        for seq, tp in partners:
            pl.semaphore_signal(barrier, inc=1, device_id=(seq, tp), device_id_type=MESH)

    def met(self):
        pl.semaphore_wait(pltpu.get_barrier_semaphore(), 2 + len(self.reached()))

    def rows_of(self, side, seq):
        return self.buffer.at[side, at(seq * self.rows, self.rows), :]

    def block(self, side, pair):
        return self.buffer.at[side, at(pair * 2 * self.rows, 2 * self.rows), :]

    def items(self, pair):
        found = [self.block(self.core, pair)]
        if self.lives is not None:
            found.append(self.lives.at[at(pair * 2, 2)])
        return found

    def each(self, copy, what):
        for index in range(1 if self.lives is None else 2):
            getattr(copy(index), what)()

    def z_copy(self, step, far):
        def copy(index):
            lane = 1 - self.x if far else self.x
            if index == 0:
                source = self.other.at[self.core] if far else self.rows_of(self.core, self.me)
                target = self.rows_of(self.core, self.me)
            else:
                source = self.live_other if far else self.lives.at[self.me]
                target = self.lives.at[self.me]
            return remote(
                source,
                target,
                self.z_send.at[step, far, index],
                self.z_recv.at[step, far, index],
                self.place(self.plane(step), lane),
                self.core,
            )

        return copy

    def y_copy(self, plane, row):
        def copy(index):
            item = self.items(plane * 2 + row)[index]
            return remote(
                item,
                item,
                self.y_send.at[plane, index],
                self.y_recv.at[plane, index],
                self.across,
                self.core,
            )

        return copy

    def c_copy(self, pair, side):
        item = self.block(side, pair)
        return remote(
            item, item, self.c_send.at[pair], self.c_recv.at[pair], self.me, 1 - self.core
        )

    def begin(self):
        for step, far in self.reached():
            self.each(self.z_copy(step, far), "start")

    def arrive(self, event):
        for far in (0, 1) if event else (1,):
            self.each(self.z_copy(event, far), "wait_recv")
        plane = self.plane(self.planes - event)
        self.each(self.y_copy(plane, self.y), "start")
        self.c_copy(plane * 2 + self.y, self.core).start()

    def complete(self, event):
        plane = self.plane(self.planes - event)
        self.each(self.y_copy(plane, 1 - self.y), "wait_recv")
        self.c_copy(plane * 2 + 1 - self.y, self.core).start()

    def ready(self, event):
        plane = self.plane(self.planes - event)
        self.c_copy(plane * 2, 1 - self.core).wait_recv()
        self.c_copy(plane * 2 + 1, 1 - self.core).wait_recv()
        return plane

    def finish(self):
        for step, far in self.reached():
            self.each(self.z_copy(step, far), "wait_send")
        for plane in range(self.planes):
            self.each(self.y_copy(plane, self.y), "wait_send")
        for pair in range(2 * self.planes):
            self.c_copy(pair, self.core).wait_send()


def split_lanes(values, x, buffer, other, start, rows):
    half = values.shape[2] // 2
    zero, one = values[:, 0, :], values[:, 1, :]
    own, far = jnp.where(x == 0, zero, one), jnp.where(x == 0, one, zero)
    core = lax.axis_index("tp")
    own = jnp.where(core == 0, own[:, :half], own[:, half:]).astype(BF16)
    buffer[core, at(start, rows), :] = own
    for side in range(2):
        other[side] = far[:, side * half : (side + 1) * half].astype(BF16)


def gather_and_project(tokens, live, episode_frames, gain, shift, qkv, bias, fixed, ahead, n):
    rows, lanes, width = tokens.shape
    half = width // 2
    total = n * rows
    chunks = total // FRAME
    per_frame = FRAME // rows
    features = qkv.shape[3]
    slots = episode_frames.shape[1]

    def kernel(*refs):
        refs = list(refs)

        def take(count):
            taken = refs[:count]
            del refs[:count]
            return taken

        tokens_ref, live_ref, counts_ref, gain_ref, shift_ref, w_any, bias_ref = take(7)
        fixed_ref, ahead_ref = take(2)
        all_ref, mask_ref, frames_ref = take(3)
        projected = take(6)
        other, lives, live_other, weight, full, w_sem = take(6)
        relay = Relay(n, rows, all_ref, other, take(Relay.sems), lives, live_other)
        load = pltpu.make_async_copy(w_any.at[0], weight, w_sem)
        load.start()
        relay.hello()
        x, me = relay.x, relay.me
        split_lanes(tokens_ref[...].astype(F32), x, all_ref, other, me * rows, rows)
        lane = lax.broadcasted_iota(jnp.int32, (1, FRAME), 1)
        here = lane // rows == lax.rem(me, per_frame)
        tiles = []
        for index in range(lanes):
            alive = live_ref[index : index + 1, :].astype(F32)
            alive = jnp.where(here, jnp.concatenate([alive] * per_frame, axis=1), 0.0)
            tiles.append(jnp.broadcast_to(alive, (8, FRAME)))
        lives[me] = jnp.where(x == 0, tiles[0], tiles[1])
        live_other[...] = jnp.where(x == 0, tiles[1], tiles[0])
        relay.met()
        relay.begin()

        counts = [counts_ref[x, slot] for slot in range(slots)]
        episodes, openings = [], []
        for frame in range(chunks):
            end, episode, opening = 0, 0, 0
            for slot in range(slots):
                end = end + counts[slot]
                passed = frame >= end
                episode = episode + passed.astype(jnp.int32)
                opening = opening + jnp.where(passed, counts[slot], 0)
            episodes.append(episode)
            openings.append(frame - opening)
        for index in range(3):
            table = []
            for frame in range(chunks):
                line = jnp.zeros((1, PAIR), F32)
                for choice in range(chunks):
                    line = jnp.where(
                        openings[frame] == choice, ahead_ref[index, choice : choice + 1, :], line
                    )
                table.append(line)
            frames_ref[index] = jnp.concatenate(
                table + [jnp.zeros((8 - chunks, PAIR), F32)], axis=0
            )
        load.wait()

        def project_frame(frame):
            place = at(frame * FRAME, FRAME)
            stream = jnp.concatenate([all_ref[0, place, :], all_ref[1, place, :]], axis=1)
            project(
                stream.astype(F32),
                frame,
                0,
                me // 2,
                (gain_ref, shift_ref, weight, bias_ref, fixed_ref, frames_ref),
                [ref.at[place, :] for ref in projected],
                full,
            )

        for event in range(relay.events):
            relay.arrive(event)
            if event:
                relay.complete(event - 1)
            if event > 1:
                project_frame(relay.ready(event - 2))
        relay.complete(relay.events - 1)
        for event in range(max(0, relay.events - 2), relay.events):
            project_frame(relay.ready(event))
        relay.finish()

        for key_frame in range(chunks):
            alive = lives[key_frame * per_frame, 0:1, :]
            for part in range(1, per_frame):
                alive = alive + lives[key_frame * per_frame + part, 0:1, :]
            closed = (alive - 1.0) * -MASKED
            lines = []
            for query_frame in range(chunks):
                allowed = (episodes[query_frame] == episodes[key_frame]) & (
                    openings[key_frame] <= openings[query_frame]
                )
                lines.append(jnp.where(allowed, closed, MASKED))
            lines.append(jnp.zeros((PAIR - chunks, FRAME), F32))
            mask_ref[key_frame * FRAME : (key_frame + 1) * FRAME, :] = jnp.concatenate(
                lines, axis=0
            ).T.astype(BF16)

    in_vmem = pl.BlockSpec(memory_space=pltpu.VMEM)
    in_smem = pl.BlockSpec(memory_space=pltpu.SMEM)
    projected = jax.ShapeDtypeStruct((total, features), BF16)
    return pl.pallas_call(
        kernel,
        out_shape=(
            jax.ShapeDtypeStruct((2, total, half), BF16),
            jax.ShapeDtypeStruct((total, PAIR), BF16),
            jax.ShapeDtypeStruct((3, 8, PAIR), F32),
            projected,
            projected,
            projected,
            jax.ShapeDtypeStruct((total, PAIR), BF16),
            jax.ShapeDtypeStruct((total, width), BF16),
            jax.ShapeDtypeStruct((total, PAIR), F32),
        ),
        in_specs=[in_vmem, in_vmem, in_smem, in_vmem, in_vmem, ANYWHERE] + [in_vmem] * 3,
        out_specs=(in_vmem,) * 9,
        scratch_shapes=[
            pltpu.VMEM((2, rows, half), BF16),
            pltpu.VMEM((n, 8, FRAME), F32),
            pltpu.VMEM((8, FRAME), F32),
            pltpu.VMEM(qkv.shape[1:], BF16),
            pltpu.VMEM((FRAME, width), BF16),
            pltpu.SemaphoreType.DMA,
        ]
        + Relay.scratch(n),
        compiler_params=pltpu.CompilerParams(
            collective_id=0, has_side_effects=True, vmem_limit_bytes=VMEM_BYTES
        ),
        name="gather_and_project",
    )(tokens, live, episode_frames, gain, shift, qkv, bias, fixed, ahead)


def halves(ref):
    return jnp.concatenate([ref[0], ref[1]], axis=1).astype(F32)


def halves_spec(shape, chunks, behind, span=FRAME):
    return pl.BlockSpec(
        (2, span, shape[2]), lambda s: (0, jnp.clip(s - behind, 0, chunks - 1), 0)
    )


def layer_forward(layer, query, key, value, key_bias, stream, mats, rows_of, next_refs, d_out, n, identity):
    total, features = query.shape
    split = stream.ndim == 3
    width = mats[1].shape[1]
    rows_here = total // n
    hidden_units = mats[1].shape[2]
    chunks = total // FRAME
    heads = features // HEAD_DIM
    slabs = features // PAIR
    columns = 256
    last = next_refs is None
    b_out, gain, shift, b_up, b_down = rows_of
    mat_out, mat_up, mat_down = mats

    def kernel(*refs):
        refs = list(refs)

        def take(count):
            taken = refs[:count]
            del refs[:count]
            return taken

        q_ref, k_ref, v_ref, kb_ref, x_ref = take(5)
        wo_any, wu_any, wd_any = take(3)
        bo_ref, gain_ref, shift_ref, bu_ref, bd_ref = take(5)
        if not last:
            wq_any, ngain, nshift, nbias, fixed, frames = take(6)
        if d_out is not None:
            (d_ref,) = take(1)
        p_ref, r_ref, mixed_ref, unit_ref, scale_ref, second_ref, act_ref, gp_ref, x_out = take(9)
        if not last:
            next_outs = take(6)
        if d_out is not None:
            (d_all,) = take(1)
        wo, wu, wd, mid, full, next_full = take(6)
        if not last:
            (wq,) = take(1)
        a_send, a_recv, b_send, b_recv, w_sem, send_sem, recv_sem = take(7)
        relay = None
        if d_out is not None:
            buffer, other, d_sem = take(3)
            relay = Relay(n, rows_here, buffer, other, take(Relay.sems))

        step = pl.program_id(0)
        me, core = lax.axis_index("seq"), lax.axis_index("tp")

        items = [(wo_any, wo), (wu_any, wu), (wd_any, wd)]
        if not last:
            items.append((wq_any, wq))

        def load(index):
            source, target = items[index]
            return pltpu.make_async_copy(
                source.at[layer if index < 3 else layer + 1], target, w_sem.at[index]
            )

        def exchange(kind, chunk):
            source, target = ((a_send, a_recv), (b_send, b_recv))[kind]
            return remote(
                source.at[chunk],
                target.at[chunk],
                send_sem.at[kind, chunk],
                recv_sem.at[kind, chunk],
                me,
                1 - core,
            )

        @pl.when(step == 0)
        def _():
            for index in range(len(items)):
                load(index).start()
            if relay is None:
                greet([(me, 1 - core)])
            else:
                relay.hello()
                split_lanes(d_ref[...], relay.x, buffer, other, me * rows_here, rows_here)
                relay.met()
                relay.begin()

        if relay is not None:
            for event in range(relay.events):

                @pl.when(step == 1 + event // 2)
                def _():
                    relay.arrive(event)

                @pl.when(step == 2 + event // 2)
                def _():
                    relay.complete(event)

            @pl.when(step == chunks + 1)
            def _():
                for event in range(relay.events):
                    relay.ready(event)
                relay.finish()
                pltpu.make_async_copy(buffer, d_all, d_sem).start()

        lane = lax.broadcasted_iota(jnp.int32, (1, PAIR), 1)
        sides = [(lane < HEAD_DIM).astype(F32).astype(BF16), (lane >= HEAD_DIM).astype(F32).astype(BF16)]
        for frame in range(chunks):

            @pl.when(step == frame)
            def _():
                keys = FRAME * (frame + 1)
                mask = kb_ref[:keys, :]
                asked = jnp.broadcast_to((lane == frame).astype(F32), (FRAME, PAIR)).astype(BF16)

                def one_slab(slab, carry):
                    lanes = at(slab * PAIR, PAIR)
                    q2, v2 = q_ref[:, lanes], v_ref[:keys, lanes]
                    k2 = jnp.concatenate([k_ref[:keys, lanes], mask], axis=1)
                    sums = []
                    for side in range(2):
                        scores = nt(jnp.concatenate([q2 * sides[side], asked], axis=1), k2)
                        highest = jnp.max(scores, axis=1, keepdims=True)
                        shifted = jnp.exp(scores - highest).astype(BF16)
                        p_ref[0, slab * 2 + side, :keys, :] = shifted.T
                        sums.append(nn(shifted, v2 * sides[side] + sides[1 - side]))
                    low_side = lane < HEAD_DIM
                    divisor = 1.0 / jnp.where(
                        low_side, pltpu.roll(sums[0], HEAD_DIM, 1), pltpu.roll(sums[1], HEAD_DIM, 1)
                    )
                    r_ref[:, lanes] = divisor
                    mixed_ref[:, lanes] = (jnp.where(low_side, sums[0], sums[1]) * divisor).astype(BF16)
                    return carry

                lax.fori_loop(0, slabs, one_slab, 0, unroll=True)

        @pl.when(step == 0)
        def _():
            load(0).wait()

        @pl.when(step < chunks)
        def _():
            a_send[step] = nn(mixed_ref[...], wo[...]).astype(BF16)
            exchange(0, step).start()

        def feed_forward():
            chunk = step - 1
            middle = (halves(x_ref) if split else x_ref[...]) + (
                a_send[chunk].astype(F32) + a_recv[chunk].astype(F32)
            )
            middle = middle + bo_ref[layer : layer + 1, :]
            mid[lax.rem(chunk, 2)] = middle
            unit, scale = normed(middle)
            keep_norm(unit, scale, unit_ref, scale_ref)
            second = (unit * gain_ref[layer : layer + 1, :] + shift_ref[layer : layer + 1, :]).astype(BF16)
            full[...] = second
            second_ref[...] = full[:, at((me // 2) * PAIR, PAIR)]
            parts = [slice(start, start + columns) for start in range(0, hidden_units, columns)]
            hidden = nn(second, wu[:, parts[0]])
            for index, part in enumerate(parts):
                following = nn(second, wu[:, parts[index + 1]]) if index + 1 < len(parts) else None
                act, slope = gelu_both(hidden + bu_ref[layer : layer + 1, part])
                act_ref[:, part] = act.astype(BF16)
                gp_ref[:, part] = slope.astype(BF16)
                hidden = following
            b_send[chunk] = nn(act_ref[...], wd[...]).astype(BF16)

        def close():
            chunk = step - 2
            result = mid[lax.rem(chunk, 2)] + (b_send[chunk].astype(F32) + b_recv[chunk].astype(F32))
            result = result + bd_ref[layer : layer + 1, :]
            x_out[...] = result
            if not last:
                project(
                    result,
                    chunk,
                    layer + 1,
                    me // 2,
                    (ngain, nshift, wq, nbias, fixed, frames),
                    next_outs,
                    next_full,
                )

        @pl.when(step == 1)
        def _():
            load(1).wait()
            load(2).wait()
            exchange(0, step - 1).wait_recv()
            feed_forward()
            exchange(1, step - 1).start()
            if not last:
                load(3).wait()

        @pl.when((step >= 2) & (step <= chunks))
        def _():
            exchange(0, step - 1).wait_recv()
            exchange(1, step - 2).wait_recv()
            close()
            feed_forward()
            exchange(1, step - 1).start()

        @pl.when(step == chunks + 1)
        def _():
            exchange(1, step - 2).wait_recv()
            close()

        @pl.when(step == chunks + 1)
        def _():
            for kind in range(2):
                for chunk in range(chunks):
                    exchange(kind, chunk).wait_send()
            if relay is not None:
                pltpu.make_async_copy(buffer, d_all, d_sem).wait()

    def rows(columns, behind):
        return pl.BlockSpec(
            (FRAME, columns), lambda s: (jnp.clip(s - behind, 0, chunks - 1), 0)
        )

    in_specs = [rows(features, 0), whole(key), whole(value), whole(key_bias)]
    in_specs += [halves_spec(stream.shape, chunks, 1) if split else rows(width, 1)]
    in_specs += [ANYWHERE] * 3 + [whole(item) for item in rows_of]
    operands = [query, key, value, key_bias, stream, *mats, *rows_of]
    if not last:
        in_specs += [ANYWHERE] + [whole(item) for item in next_refs[1:]]
        operands += list(next_refs)
    if d_out is not None:
        in_specs += [whole(d_out)]
        operands += [d_out]
    out_shape = [
        jax.ShapeDtypeStruct((chunks, heads, total, FRAME), BF16),
        jax.ShapeDtypeStruct((total, features), F32),
        jax.ShapeDtypeStruct((total, features), BF16),
        jax.ShapeDtypeStruct((total, width), BF16),
        jax.ShapeDtypeStruct((total, PAIR), F32),
        jax.ShapeDtypeStruct((total, PAIR), BF16),
        jax.ShapeDtypeStruct((total, hidden_units), BF16),
        jax.ShapeDtypeStruct((total, hidden_units), BF16),
        jax.ShapeDtypeStruct((total, width), F32),
    ]
    out_specs = [
        pl.BlockSpec((1, heads, total, FRAME), lambda s: (jnp.minimum(s, chunks - 1), 0, 0, 0)),
        rows(features, 0),
        rows(features, 0),
        rows(width, 1),
        rows(PAIR, 1),
        rows(PAIR, 1),
        rows(hidden_units, 1),
        rows(hidden_units, 1),
        rows(width, 2),
    ]
    scratch = [
        pltpu.VMEM(mat_out.shape[1:], BF16),
        pltpu.VMEM(mat_up.shape[1:], BF16),
        pltpu.VMEM(mat_down.shape[1:], BF16),
        pltpu.VMEM((2, FRAME, width), F32),
        pltpu.VMEM((FRAME, width), BF16),
        pltpu.VMEM((FRAME, width), BF16),
    ]
    if not last:
        out_shape += [jax.ShapeDtypeStruct((total, features), BF16)] * 3
        out_shape += [jax.ShapeDtypeStruct((total, PAIR), BF16)]
        out_shape += [jax.ShapeDtypeStruct((total, width), BF16)]
        out_shape += [jax.ShapeDtypeStruct((total, PAIR), F32)]
        out_specs += [rows(features, 2)] * 3 + [rows(PAIR, 2), rows(width, 2), rows(PAIR, 2)]
    if d_out is not None:
        out_shape += [jax.ShapeDtypeStruct((2, total, width // 2), BF16)]
        out_specs += [ANYWHERE]
        scratch += [pltpu.VMEM(next_refs[0].shape[1:], BF16)]
    scratch += [pltpu.VMEM((chunks, FRAME, width), BF16)] * 4
    scratch += [
        pltpu.SemaphoreType.DMA((4,)),
        pltpu.SemaphoreType.DMA((2, chunks)),
        pltpu.SemaphoreType.DMA((2, chunks)),
    ]
    if d_out is not None:
        scratch += [
            pltpu.VMEM((2, total, width // 2), BF16),
            pltpu.VMEM((2, rows_here, width // 2), BF16),
            pltpu.SemaphoreType.DMA,
        ]
        scratch += Relay.scratch(n)
    return pl.pallas_call(
        kernel,
        grid=(chunks + 2,),
        out_shape=out_shape,
        in_specs=in_specs,
        out_specs=out_specs,
        scratch_shapes=scratch,
        compiler_params=pltpu.CompilerParams(
            collective_id=identity, has_side_effects=True, vmem_limit_bytes=VMEM_BYTES
        ),
        name=f"layer_forward_{layer}",
    )(*operands)


class Swap:
    def __init__(self, ships, lane_rows):
        self.ships, self.lane_rows = ships, lane_rows
        self.count = len(ships) + len(lane_rows)

    def operands(self):
        return [*self.ships, *[item for item, _ in self.lane_rows]]

    def in_specs(self):
        return [whole(item) for item in self.ships] + [ANYWHERE] * len(self.lane_rows)

    def outputs(self):
        shapes, specs = [], []
        for item in self.ships:
            shape = (item.shape[0] // 2, item.shape[1])
            shapes.append(jax.ShapeDtypeStruct(shape, F32))
            specs.append(whole_out(shape))
        for item, count in self.lane_rows:
            shapes.append(jax.ShapeDtypeStruct((count or item.shape[0], item.shape[1]), item.dtype))
            specs.append(ANYWHERE)
        return shapes, specs

    def scratch(self):
        if not self.count:
            return []
        buffers = [pltpu.VMEM((item.shape[0] // 2, item.shape[1]), BF16) for item in self.ships]
        return buffers * 2 + [pltpu.SemaphoreType.DMA((self.count,))] * 2

    def bind(self, sources, targets, scratch):
        ships = len(self.ships)
        me, core = lax.axis_index("seq"), lax.axis_index("tp")
        x = lax.rem(me, 2)
        beside = me + 1 - 2 * x
        half = PAIR // 2

        def copy(index):
            if index < ships:
                source, target = scratch[index], scratch[ships + index]
            else:
                source, target = sources[index], targets[index]
                count = self.lane_rows[index - ships][1]
                if count:
                    source = source.at[at(beside * count, count), :]
            send, recv = scratch[2 * ships].at[index], scratch[2 * ships + 1].at[index]
            return remote(source, target, send, recv, beside, core)

        def start():
            for index in range(self.count):
                if index < ships:
                    scratch[index][...] = sources[index][at((1 - x) * half, half), :].astype(BF16)
                copy(index).start()

        def finish():
            for index in range(self.count):
                copy(index).wait_recv()
                if index < ships:
                    own = sources[index][at(x * half, half), :]
                    targets[index][...] = own + scratch[ships + index][...].astype(F32)
            for index in range(self.count):
                copy(index).wait_send()

        return start, finish


def attention_backward(
    probs, divisor, mixed, query, key, value, grad_mixed, first, fixed, frames, swap, swap_qkv, identity
):
    total, features = query.shape
    chunks = total // FRAME
    slabs = features // PAIR
    half = PAIR // 2

    def kernel(*refs):
        refs = list(refs)

        def take(count):
            taken = refs[:count]
            del refs[:count]
            return taken

        p_ref, r_ref, o_ref, q_ref, k_ref, v_ref, g_ref, first_ref, fixed_ref, frames_ref = take(10)
        sources = take(swap.count)
        dq_ref, dk_ref, dv_ref, qkv_out = take(4)
        targets = take(swap.count)
        dk_sum, dv_sum, first_turned = take(3)
        if swap_qkv:
            qkv_own, qkv_send, qkv_recv, qkv_sems = take(4)
        start, finish = swap.bind(sources, targets, refs)

        step = pl.program_id(0)
        me, core = lax.axis_index("seq"), lax.axis_index("tp")
        x = lax.rem(me, 2)
        beside = me + 1 - 2 * x

        def qkv_copy(slab):
            return remote(
                qkv_send.at[slab],
                qkv_recv.at[slab],
                qkv_sems.at[0, slab],
                qkv_sems.at[1, slab],
                beside,
                core,
            )

        @pl.when(step == 0)
        def _():
            greet([(beside, core)])
            start()
            first_turned[...] = first_ref[...].T

        lane = lax.broadcasted_iota(jnp.int32, (1, PAIR), 1)
        sides = [(lane < HEAD_DIM).astype(F32).astype(BF16), (lane >= HEAD_DIM).astype(F32).astype(BF16)]
        turned = k_ref[...].T
        ones = jnp.broadcast_to((lane < 2).astype(F32), (total, PAIR)).astype(BF16)
        values = jnp.concatenate([v_ref[...], ones], axis=1)
        for frame in reversed(range(chunks)):
            keys = FRAME * (frame + 1)
            own = slice(frame * FRAME, keys)
            tables = tables_of(fixed_ref, frames_ref, frame)
            scaled = (g_ref[own, :].astype(F32) * r_ref[own, :]).astype(BF16)
            inner = scaled.astype(F32) * o_ref[own, :].astype(F32)
            query_parts, score_parts, prob_parts, q_parts, g_parts = [], [], [], [], []
            for side in range(2):
                delta = jnp.sum(
                    jnp.where((lane < HEAD_DIM) == (side == 0), inner, 0.0), axis=1, keepdims=True
                )
                coarse = delta.astype(BF16).astype(F32)
                rest = jnp.where(lane == 0, -coarse, jnp.where(lane == 1, coarse - delta, 0.0))
                g2 = scaled * sides[side]
                attention = p_ref[frame, side, :keys, :]
                grad = nt(values[:keys], jnp.concatenate([g2, rest.astype(BF16)], axis=1))
                grad_scores = (attention.astype(F32) * grad).astype(BF16)
                query_parts.append(nn(turned[side * HEAD_DIM : (side + 1) * HEAD_DIM, :keys], grad_scores))
                score_parts.append(grad_scores)
                prob_parts.append(attention)
                q_parts.append(q_ref[own, :] * sides[side])
                g_parts.append(g2)
            grad_query = jnp.concatenate(query_parts, axis=0).T
            key_parts = nn(jnp.concatenate(score_parts, axis=1), jnp.concatenate(q_parts, axis=0))
            value_parts = nn(jnp.concatenate(prob_parts, axis=1), jnp.concatenate(g_parts, axis=0))
            dq_ref[own, :] = (turn(grad_query, tables, True) * SCORE_SCALE).astype(BF16)
            if frame == chunks - 1:
                dk_sum[...] = key_parts
                dv_sum[...] = value_parts
            else:
                dk_sum[:keys, :] += key_parts
                dv_sum[:keys, :] += value_parts
            dk_ref[own, :] = turn(dk_sum[own, :], tables, True).astype(BF16)
            dv_ref[own, :] = dv_sum[own, :].astype(BF16)

        for part, ref in enumerate((dq_ref, dk_ref, dv_ref)):
            piece = slice(part * PAIR, (part + 1) * PAIR)
            terms = nn(first_turned[...], ref[...])
            if swap_qkv:
                qkv_own[step, :, piece] = terms
                qkv_send[step, :, piece] = qkv_own[step, at((1 - x) * half, half), piece].astype(BF16)
            else:
                qkv_out[:, at(part * features + step * PAIR, PAIR)] = terms
        if swap_qkv:
            qkv_copy(step).start()

        @pl.when(step == slabs - 1)
        def _():
            finish()
            for slab in range(slabs if swap_qkv else 0):
                qkv_copy(slab).wait_recv()
                for part in range(3):
                    piece = slice(part * PAIR, (part + 1) * PAIR)
                    place = part * features + slab * PAIR
                    qkv_out[:, place : place + PAIR] = qkv_own[
                        slab, at(x * half, half), piece
                    ] + qkv_recv[slab, :, piece].astype(F32)
            for slab in range(slabs if swap_qkv else 0):
                qkv_copy(slab).wait_send()

    slab = pl.BlockSpec((total, PAIR), lambda s: (0, s))
    in_specs = [pl.BlockSpec((chunks, 2, total, FRAME), lambda s: (0, s, 0, 0))]
    in_specs += [slab] * 6 + [whole(first), whole(fixed), whole(frames)]
    in_specs += swap.in_specs()
    qkv_shape = (half if swap_qkv else PAIR, 3 * features)
    shapes, specs = swap.outputs()
    out_shape = [jax.ShapeDtypeStruct((total, features), BF16)] * 3
    out_shape += [jax.ShapeDtypeStruct(qkv_shape, F32)] + shapes
    out_specs = [slab] * 3 + [whole_out(qkv_shape)] + specs
    scratch = [pltpu.VMEM((total, PAIR), F32)] * 2 + [pltpu.VMEM((PAIR, total), BF16)]
    if swap_qkv:
        scratch += [pltpu.VMEM((slabs, PAIR, 3 * PAIR), F32)]
        scratch += [pltpu.VMEM((slabs, half, 3 * PAIR), BF16)] * 2
        scratch += [pltpu.SemaphoreType.DMA((2, slabs))]
    scratch += swap.scratch()
    return pl.pallas_call(
        kernel,
        grid=(slabs,),
        out_shape=out_shape,
        in_specs=in_specs,
        out_specs=out_specs,
        scratch_shapes=scratch,
        compiler_params=pltpu.CompilerParams(
            collective_id=identity, has_side_effects=True, vmem_limit_bytes=VMEM_BYTES
        ),
        name=f"attention_backward_{identity}",
    )(
        probs,
        divisor,
        mixed,
        query,
        key,
        value,
        grad_mixed,
        first,
        fixed,
        frames,
        *swap.operands(),
    )


def rows_backward(entry, upper, identity, span, swap):
    top, bottom = len(entry) == 1, upper is None
    if not top:
        above, entry = entry[0], entry[1:]
    total = entry[0].shape[1] if top else entry[0].shape[0]
    chunks = total // span
    columns = 256
    ahead = 0 if top else 1
    if top:
        width = 2 * entry[0].shape[2]
    else:
        features, width = entry[0].shape[1], entry[5].shape[1]
    if not bottom:
        layer = upper[0]
        hidden_units, mixed_features = upper[1].shape[1], upper[6].shape[1]
    place_rows = total // lax.axis_size("seq")

    def kernel(*refs):
        refs = list(refs)

        def take(count):
            taken = refs[:count]
            del refs[:count]
            return taken

        if top:
            (d_out_ref,) = take(1)
        else:
            dq_ref, dk_ref, dv_ref, unit1, scale1, dm_ref, wq, gain1 = take(8)
        if not bottom:
            act_ref, gp_ref, unit2, scale2, second_ref, mixed_ref = take(6)
            wo_any, wu_any, wd_any, gain2 = take(4)
        sources = take(swap.count)
        if not top:
            (vec1,) = take(1)
        if not bottom:
            dmid_out, dmix_out, out_sum, up_sum, down_sum, vec2 = take(6)
        else:
            dx_out, dx_other, vec_other = take(3)
        targets = take(swap.count)
        if not top:
            a_send, a_recv = take(2)
        if not bottom:
            b_send, b_recv, grad_keep, hidden_keep, low_keep, last_keep, wo, wu, wd, w_sem = take(10)
        else:
            dx_keep, dx_send, dx_recv, vec_recv, x_send_sem, x_recv_sem = take(6)
        send_sem, recv_sem = take(2)
        start_swap, finish_swap = swap.bind(sources, targets, refs)

        step = pl.program_id(0)
        me, core = lax.axis_index("seq"), lax.axis_index("tp")
        pair = at((me // 2) * PAIR, PAIR)
        x = lax.rem(me, 2)
        beside = me + 1 - 2 * x

        def exchange(kind, chunk):
            source, target = (a_send, a_recv) if kind == 0 else (b_send, b_recv)
            return remote(
                source.at[chunk],
                target.at[chunk],
                send_sem.at[kind, chunk],
                recv_sem.at[kind, chunk],
                me,
                1 - core,
            )

        def load(index):
            source, target = ((wd_any, wd), (wu_any, wu), (wo_any, wo))[index]
            return pltpu.make_async_copy(source.at[layer], target, w_sem.at[index])

        @pl.when(step == 0)
        def _():
            if not bottom:
                for index in range(3):
                    load(index).start()
                out_sum[...] = jnp.zeros_like(out_sum)
                up_sum[...] = jnp.zeros_like(up_sum)
                down_sum[...] = jnp.zeros_like(down_sum)
                vec2[...] = jnp.zeros_like(vec2)
            if not top:
                vec1[...] = jnp.zeros_like(vec1)
            greet([(me, 1 - core)] + ([(beside, core)] if bottom or swap.count else []))
            start_swap()

        def entry_products():
            partial = None
            for part, ref in enumerate((dq_ref, dk_ref, dv_ref)):
                grad = ref[...]
                term = nt(grad, wq[0, part])
                partial = term if partial is None else partial + term
                vec1[part : part + 1, :] += column_sum(grad.astype(F32))
            a_send[step] = partial.astype(BF16)

        def entry_norm(chunk):
            if top:
                return halves(d_out_ref)
            grad_first = a_send[chunk].astype(F32) + a_recv[chunk].astype(F32)
            unit, scale = kept_norm(unit1, scale1)
            for start, sums in ((3, column_sum(grad_first * unit)), (5, column_sum(grad_first))):
                for side in range(width // features):
                    piece = slice(side * features, (side + 1) * features)
                    vec1[start + side : start + side + 1, :] += sums[:, piece]
            return dm_ref[...] + norm_pull(grad_first, gain1[above : above + 1, :], unit, scale)

        def feed_forward(between=None):
            chunk = step - ahead
            gradient = entry_norm(chunk)
            if bottom:
                dx_keep[at(chunk * span, span), :] = gradient
                return
            grad_keep[lax.rem(chunk, 2)] = gradient
            vec2[1:2, :width] += column_sum(gradient)
            low = gradient.astype(BF16)
            low_keep[...] = low
            low_columns = low_keep[:, pair]
            second = second_ref[...]
            parts = [slice(start, start + columns) for start in range(0, hidden_units, columns)]
            grad_act = nt(low, wd[parts[0], :])
            for index, part in enumerate(parts):
                following = nt(low, wd[parts[index + 1], :]) if index + 1 < len(parts) else None
                grad_hidden = grad_act * gp_ref[:, part].astype(F32)
                hidden_keep[:, part] = grad_hidden.astype(BF16)
                vec2[0:1, part] += column_sum(grad_hidden)
                grad_act = following
            if between is not None:
                between()
            b_send[chunk] = nt(hidden_keep[...], wu[...]).astype(BF16)
            down_sum[...] += tn(low_columns, act_ref[...])
            up_sum[...] += tn(second, hidden_keep[...])

        def close():
            chunk = step - ahead - 1
            grad_second = b_send[chunk].astype(F32) + b_recv[chunk].astype(F32)
            unit, scale = kept_norm(unit2, scale2)
            vec2[2:3, :width] += column_sum(grad_second * unit)
            vec2[3:4, :width] += column_sum(grad_second)
            grad_middle = grad_keep[lax.rem(chunk, 2)] + norm_pull(
                grad_second, gain2[layer : layer + 1, :], unit, scale
            )
            dmid_out[...] = grad_middle
            vec2[4:5, :width] += column_sum(grad_middle)
            low = grad_middle.astype(BF16)
            last_keep[...] = low
            out_sum[...] += tn(last_keep[:, pair], mixed_ref[...])
            dmix_out[...] = nt(low, wo[...]).astype(BF16)

        def one_step(first, second, third, start=False):
            if second and not top:
                exchange(0, step - ahead).wait_recv()
            if third:
                exchange(1, step - ahead - 1).wait_recv()
            if start and not bottom:
                load(0).wait()
            if first:
                entry_products()
            if third:
                close()
            if second:
                feed_forward((lambda: load(1).wait()) if start and not bottom else None)
            if start and not bottom:
                load(2).wait()
            if first:
                exchange(0, step).start()
            if second and not bottom:
                exchange(1, step - ahead).start()

        steps = chunks + (1 if top or bottom else 2)
        kinds = []
        for index in range(steps):
            first = not top and index < chunks
            second = ahead <= index < chunks + ahead
            third = not bottom and index >= ahead + 1
            kinds.append((first, second, third, index == ahead))
        begun = 0
        for index in range(1, steps + 1):
            if index == steps or kinds[index] != kinds[begun]:

                @pl.when((step >= begun) & (step < index))
                def _():
                    one_step(*kinds[begun])

                begun = index

        if bottom:

            def x_copy(index):
                source, target = ((dx_send, dx_recv), (vec1, vec_recv))[index]
                return remote(
                    source, target, x_send_sem.at[index], x_recv_sem.at[index], beside, core
                )

            @pl.when(step == chunks)
            def _():
                dx_send[...] = dx_keep[at(beside * place_rows, place_rows), :].astype(BF16)
                x_copy(0).start()
                x_copy(1).start()
                dx_out[...] = dx_keep[at(me * place_rows, place_rows), :]
                x_copy(0).wait_recv()
                x_copy(1).wait_recv()
                dx_other[...] = dx_recv[...].astype(F32)
                vec_other[...] = vec_recv[...]
                x_copy(0).wait_send()
                x_copy(1).wait_send()

        @pl.when(step == pl.num_programs(0) - 1)
        def _():
            for kind in ([] if top else [0]) + ([] if bottom else [1]):
                for chunk in range(chunks):
                    exchange(kind, chunk).wait_send()
            finish_swap()

    def rows(columns, behind):
        return pl.BlockSpec(
            (span, columns), lambda s: (jnp.clip(s - behind, 0, chunks - 1), 0)
        )

    vec = jax.ShapeDtypeStruct((8, VEC), F32)
    operands, in_specs, out_shape, out_specs, scratch = [], [], [], [], []
    if top:
        operands += list(entry)
        in_specs += [halves_spec(entry[0].shape, chunks, 0, span)]
    else:
        operands += list(entry)
        in_specs += [rows(features, 0)] * 3
        in_specs += [rows(width, 1), rows(PAIR, 1), rows(width, 1)]
        in_specs += [
            pl.BlockSpec(
                (1, *entry[6].shape[1:]),
                lambda s: (above, 0, 0, 0),
                pipeline_mode=pl.Buffered(1),
            ),
            whole(entry[7]),
        ]
        narrow = jax.ShapeDtypeStruct((8, features), F32)
        out_shape += [narrow]
        out_specs += [whole_out((8, features))]
        scratch += [pltpu.VMEM((chunks, span, width), BF16)] * 2
    if not bottom:
        operands += list(upper[1:])
        in_specs += [rows(hidden_units, ahead)] * 2
        in_specs += [rows(width, ahead + 1), rows(PAIR, ahead + 1), rows(PAIR, ahead)]
        in_specs += [rows(mixed_features, ahead + 1)] + [ANYWHERE] * 3 + [whole(upper[10])]
        sums = [mixed_features, hidden_units, hidden_units]
        out_shape += [
            jax.ShapeDtypeStruct((total, width), F32),
            jax.ShapeDtypeStruct((total, mixed_features), BF16),
        ]
        out_shape += [jax.ShapeDtypeStruct((PAIR, size), F32) for size in sums] + [vec]
        out_specs += [rows(width, ahead + 1), rows(mixed_features, ahead + 1)]
        out_specs += [whole_out((PAIR, size)) for size in sums] + [whole_out((8, VEC))]
        scratch += [pltpu.VMEM((chunks, span, width), BF16)] * 2
        scratch += [
            pltpu.VMEM((2, span, width), F32),
            pltpu.VMEM((span, hidden_units), BF16),
            pltpu.VMEM((span, width), BF16),
            pltpu.VMEM((span, width), BF16),
            pltpu.VMEM(upper[7].shape[1:], BF16),
            pltpu.VMEM(upper[8].shape[1:], BF16),
            pltpu.VMEM(upper[9].shape[1:], BF16),
            pltpu.SemaphoreType.DMA((3,)),
        ]
    else:
        out_shape += [
            jax.ShapeDtypeStruct((place_rows, width), F32),
            jax.ShapeDtypeStruct((place_rows, width), F32),
            narrow,
        ]
        out_specs += [whole_out((place_rows, width))] * 2 + [whole_out((8, features))]
        scratch += [
            pltpu.VMEM((total, width), F32),
            pltpu.VMEM((place_rows, width), BF16),
            pltpu.VMEM((place_rows, width), BF16),
            pltpu.VMEM((8, features), F32),
            pltpu.SemaphoreType.DMA((2,)),
            pltpu.SemaphoreType.DMA((2,)),
        ]
    scratch += [pltpu.SemaphoreType.DMA((2, chunks))] * 2
    operands += swap.operands()
    in_specs += swap.in_specs()
    shapes, specs = swap.outputs()
    out_shape += shapes
    out_specs += specs
    scratch += swap.scratch()
    return pl.pallas_call(
        kernel,
        grid=(chunks + (1 if top or bottom else 2),),
        out_shape=out_shape,
        in_specs=in_specs,
        out_specs=out_specs,
        scratch_shapes=scratch,
        compiler_params=pltpu.CompilerParams(
            collective_id=identity, has_side_effects=True, vmem_limit_bytes=VMEM_BYTES
        ),
        name=f"rows_backward_{identity}",
    )(*operands)


def assemble(sums, vecs, lanes, n, features, hidden_units):
    place = lanes[1].shape[0]
    width = lanes[1].shape[1]
    half = PAIR // 2

    def kernel(*refs):
        refs = list(refs)

        def take(count):
            taken = refs[:count]
            del refs[:count]
            return taken

        qkvs, outs, ups, downs = take(LAYERS), take(LAYERS), take(LAYERS), take(LAYERS)
        vec_refs = [take(4) for _ in range(LAYERS)]
        out_lane, out_other, dx_own, dx_other = take(4)
        out_ref, dx_ref, gain1, shift1, g_qkv, b_qkv, g_out, b_out = take(8)
        gain2, shift2, g_up, b_up, g_down, b_down = take(6)
        out_own, sem = refs
        me = lax.axis_index("seq")
        x = lax.rem(me, 2)
        fetch = pltpu.make_async_copy(out_lane.at[at(me * place, place), :], out_own, sem)
        fetch.start()

        for layer in range(LAYERS):
            for part in range(3):
                g_qkv[layer, part] = qkvs[layer][:, part * features : (part + 1) * features]
            for ref, target in ((outs, g_out), (ups, g_up), (downs, g_down)):
                target[layer] = ref[layer][...]

        for layer, (entry_own, entry_other, upper_own, upper_other) in enumerate(vec_refs):
            line = slice(layer, layer + 1)
            for part in range(3):
                row = slice(part, part + 1)
                b_qkv[part, line, :] = entry_own[row, :] + entry_other[row, :]
            b_up[line, :] = upper_own[0:1, :hidden_units] + upper_other[0:1, :hidden_units]

            def owned(mine, other, row):
                wide = mine.shape[1]
                place = (me // 2) * PAIR
                pair = at(lax.rem(place, wide), PAIR)
                both = mine[row : row + 1, pair] + other[row : row + 1, pair]
                for later in range(1, width // wide):
                    line = slice(row + later, row + later + 1)
                    both = jnp.where(place // wide == later, mine[line, pair] + other[line, pair], both)
                return jnp.where(x == 0, both[:, :half], both[:, half:])

            gain1[line, :] = owned(entry_own, entry_other, 3)
            shift1[line, :] = owned(entry_own, entry_other, 5)
            b_down[line, :] = owned(upper_own, upper_other, 1)
            gain2[line, :] = owned(upper_own, upper_other, 2)
            shift2[line, :] = owned(upper_own, upper_other, 3)
            b_out[line, :] = owned(upper_own, upper_other, 4)

        def both_lanes(target, mine, other):
            target[:, 0, :] = jnp.where(x == 0, mine, other)
            target[:, 1, :] = jnp.where(x == 0, other, mine)

        both_lanes(dx_ref, dx_own[...], dx_other[...])
        fetch.wait()
        both_lanes(out_ref, out_own[...], out_other[...])

    def f32(*shape):
        return jax.ShapeDtypeStruct(shape, F32)

    in_vmem = pl.BlockSpec(memory_space=pltpu.VMEM)
    flat = []
    for kind in range(4):
        flat += [sums[layer][kind] for layer in range(LAYERS)]
    for layer in range(LAYERS):
        flat += list(vecs[layer])
    flat += list(lanes)
    small = f32(LAYERS, width // n)
    return pl.pallas_call(
        kernel,
        out_shape=(
            f32(place, 2, width),
            f32(place, 2, width),
            small,
            small,
            f32(LAYERS, 3, half, features),
            f32(3, LAYERS, features),
            f32(LAYERS, half, features),
            small,
            small,
            small,
            f32(LAYERS, half, hidden_units),
            f32(LAYERS, hidden_units),
            f32(LAYERS, half, hidden_units),
            small,
        ),
        in_specs=[in_vmem] * (len(flat) - 4) + [ANYWHERE] + [in_vmem] * 3,
        out_specs=(in_vmem,) * 14,
        scratch_shapes=[pltpu.VMEM((place, width), F32), pltpu.SemaphoreType.DMA],
        compiler_params=pltpu.CompilerParams(vmem_limit_bytes=VMEM_BYTES),
        name="assemble",
    )(*flat)


def per_chip(
    tokens,
    d_out,
    norm1_gain,
    norm1_shift,
    w_qkv,
    b_qkv,
    w_out,
    b_out,
    norm2_gain,
    norm2_shift,
    w_up,
    b_up,
    w_down,
    b_down,
    episode_frames,
    live,
):
    n = lax.axis_size("seq")
    rows = tokens.shape[0]
    features = w_qkv.shape[3]
    fixed, ahead = turn_constants(rows * n // FRAME)
    qkv, qkv_bias = w_qkv.transpose(0, 2, 1, 3), b_qkv.transpose(1, 0, 2)

    gathered, key_bias, frames, *projected = gather_and_project(
        tokens, live.T, episode_frames, norm1_gain, norm1_shift, qkv, qkv_bias, fixed, ahead, n
    )
    streams, kept, d_lane = [gathered], [], None
    for layer in range(LAYERS):
        following = None
        if layer + 1 < LAYERS:
            following = (qkv, norm1_gain, norm1_shift, qkv_bias, fixed, frames)
        results = layer_forward(
            layer,
            *projected[:3],
            key_bias,
            streams[layer],
            (w_out, w_up, w_down),
            (b_out, norm2_gain, norm2_shift, b_up, b_down),
            following,
            d_out if layer == 0 else None,
            n,
            1 + layer,
        )
        kept.append((*projected, *results[:8]))
        streams.append(results[8])
        if following is not None:
            projected = results[9:15]
        if layer == 0:
            d_lane = results[-1]

    sums = [[None] * 4 for _ in range(LAYERS)]
    vecs = [[None] * 4 for _ in range(LAYERS)]
    entry, later = (d_lane,), None
    for layer in reversed(range(LAYERS)):
        query, key, value, first, unit1, scale1, probs, divisor, mixed = kept[layer][:9]
        unit2, scale2, second, act, slope = kept[layer][9:]
        upper = (
            layer,
            act,
            slope,
            unit2,
            scale2,
            second,
            mixed,
            w_out,
            w_up,
            w_down,
            norm2_gain,
        )
        identity = 1 + LAYERS + 2 * (LAYERS - 1 - layer)
        if later is None:
            results = rows_backward(entry, upper, identity, FRAME, Swap([], []))
        else:
            swap = Swap(later[:2], [(later[2], 0), (streams[LAYERS], rows)])
            vec1, *results = rows_backward(entry, upper, identity, FRAME, swap)
            results, swapped = results[:6], results[6:]
            sums[layer + 1][3], sums[layer + 1][0] = swapped[:2]
            vecs[layer + 1][3], out_other = swapped[2:]
            vecs[layer + 1][0] = vec1
        grad_middle, grad_mixed, out_sum, up_sum, down_sum, vec2 = results
        vecs[layer][2] = vec2
        last = layer == 0
        if last:
            swap = Swap([out_sum, up_sum, down_sum], [(vec2, 0), (vecs[layer + 1][0], 0)])
        else:
            swap = Swap([out_sum, up_sum], [])
        results = attention_backward(
            probs,
            divisor,
            mixed,
            query,
            key,
            value,
            grad_mixed,
            first,
            fixed,
            frames,
            swap,
            last,
            identity + 1,
        )
        grad_query, grad_key, grad_value, qkv_sum = results[:4]
        if last:
            sums[layer] = [qkv_sum, *results[4:7]]
            vecs[layer][3], vecs[layer + 1][1] = results[7:9]
        else:
            sums[layer][1:3] = results[4:6]
            later = [down_sum, qkv_sum, vec2]
        entry = (
            layer,
            grad_query,
            grad_key,
            grad_value,
            unit1,
            scale1,
            grad_middle,
            qkv,
            norm1_gain,
        )
    vec1, dx_own, dx_other, vec_other = rows_backward(
        entry, None, 1 + 3 * LAYERS, FRAME, Swap([], [])
    )
    vecs[0][:2] = [vec1, vec_other]
    results = list(
        assemble(
            sums,
            vecs,
            (streams[LAYERS], out_other, dx_own, dx_other),
            n,
            features,
            w_up.shape[2],
        )
    )
    results[4] = results[4].transpose(0, 2, 1, 3)
    results[5] = results[5].transpose(1, 0, 2)
    results[6] = results[6].transpose(0, 2, 1)
    results[12] = results[12].transpose(0, 2, 1)
    return tuple(results)


def lane_fits(mesh, tokens):
    n = mesh.shape["seq"]
    positions, lanes, width = tokens.shape
    rows = positions // n
    return (
        lanes == 2
        and n % 4 == 0
        and positions <= 4 * FRAME
        and positions % FRAME == 0
        and FRAME % rows == 0
        and width // n * 2 == PAIR
        and mesh.shape["tp"] == 2
    )


def solution(mesh):
    placed = (
        P("seq", None, None),
        P("seq", None, None),
        P(),
        P(),
        P(None, None, None, "tp"),
        P(None, None, "tp"),
        P(None, "tp", None),
        P(),
        P(),
        P(),
        P(None, None, "tp"),
        P(None, "tp"),
        P(None, "tp", None),
        P(),
        P(),
        P("seq", None),
    )
    def mapped(body):
        return jax.shard_map(
            body,
            mesh=mesh,
            in_specs=placed,
            out_specs=(
                P("seq", None, None),
                P("seq", None, None),
                P(None, "seq"),
                P(None, "seq"),
                P(None, "seq", None, "tp"),
                P(None, None, "tp"),
                P(None, "tp", "seq"),
                P(None, "seq"),
                P(None, "seq"),
                P(None, "seq"),
                P(None, "seq", "tp"),
                P(None, "tp"),
                P(None, "tp", "seq"),
                P(None, "seq"),
            ),
            check_vma=False,
        )

    def run(tokens, *others):
        if lane_fits(mesh, tokens):
            return mapped(per_chip)(tokens, *others)
        return mapped(per_device)(tokens, *others)

    return run
```

```python
import math

import jax
import jax.numpy as jnp
import numpy as np
from jax import lax
from jax.experimental import pallas as pl
from jax.experimental.pallas import tpu as pltpu
from jax.sharding import PartitionSpec as P

HEAD_DIM = 64
GRID = 16
FRAME = 256
LAYERS = 2
MICRO = 2


EPSILON = 1e-06
MASKED = -1e30
SCORE_SCALE = 0.125


def layer_norm(stream, norm_gain, norm_shift):
    center = stream - jnp.mean(stream, axis=-1, keepdims=True)
    spread = jnp.mean(center * center, axis=-1, keepdims=True)
    return center * lax.rsqrt(spread + EPSILON) * norm_gain + norm_shift


def rotate(values, frame_place, row_place, column_place):
    frequency = jnp.exp(jnp.arange(10, dtype=jnp.float32) * (-math.log(10000.0) / 10.0))
    pieces = []
    for section, place in enumerate((frame_place, row_place, column_place)):
        lower = values[..., 20 * section : 20 * section + 10]
        upper = values[..., 20 * section + 10 : 20 * section + 20]
        angles = place.astype(jnp.float32)[..., None, None] * frequency
        cosine = jnp.cos(angles)
        sine_part = jnp.sin(angles)
        pieces.append(lower * cosine - upper * sine_part)
        pieces.append(lower * sine_part + upper * cosine)
    pieces.append(values[..., 60:])
    return jnp.concatenate(pieces, axis=-1)


def episode_tags(frame_counts, positions):
    endings = jnp.cumsum(frame_counts) * FRAME
    passed = (positions[:, None] >= endings[None, :]).astype(jnp.int32)
    episode = jnp.sum(passed, axis=1)
    opening = jnp.sum(passed * frame_counts[None, :], axis=1)
    frame_index = positions // FRAME - opening
    within = positions % FRAME
    return (episode, frame_index, within // GRID, within % GRID)


def gelu_exact(values):
    return jax.nn.gelu(values, approximate=False)


def sum_heads(partial_sum):
    return lax.psum(partial_sum.astype(jnp.bfloat16), "tp").astype(jnp.float32)


def sum_inputs(partial_sum):
    return lax.psum(partial_sum.astype(jnp.bfloat16), "tp").astype(jnp.float32)


def lane_scores(query, keys_all, lane_index, query_tags, key_tags):
    head_count = query.shape[2] // HEAD_DIM
    query_lane = lax.dynamic_index_in_dim(query, lane_index, 1, False).reshape(
        query.shape[0], head_count, HEAD_DIM
    )
    keys_lane = lax.dynamic_index_in_dim(keys_all, lane_index, 1, False).reshape(
        keys_all.shape[0], head_count, HEAD_DIM
    )
    query_episode, query_frame = [
        lax.dynamic_index_in_dim(item, lane_index, 1, False) for item in query_tags
    ]
    key_episode, key_frame, key_live = [
        lax.dynamic_index_in_dim(item, lane_index, 1, False) for item in key_tags
    ]
    allowed = (
        (query_episode[:, None] == key_episode[None, :])
        & (key_frame[None, :] <= query_frame[:, None])
        & (key_live[None, :] > 0)
    )
    scores = (
        jnp.einsum("qhd,khd->hqk", query_lane, keys_lane, preferred_element_type=jnp.float32)
        * SCORE_SCALE
    )
    return (jnp.where(allowed[None], scores, MASKED), query_lane, keys_lane)


def attend_forward(query, keys_all, values_all, query_tags, key_tags):
    rows_dev, lane_count, features = query.shape
    head_count = features // HEAD_DIM

    def one_lane(lane_index, carry):
        scores, query_lane, keys_lane = lane_scores(
            query, keys_all, lane_index, query_tags, key_tags
        )
        highest = jnp.max(scores, axis=-1, keepdims=True)
        shifted = jnp.exp(scores - highest)
        summed = jnp.sum(shifted, axis=-1, keepdims=True)
        attention = (shifted / summed).astype(jnp.bfloat16)
        values_lane = lax.dynamic_index_in_dim(values_all, lane_index, 1, False).reshape(
            values_all.shape[0], head_count, HEAD_DIM
        )
        result = jnp.einsum(
            "hqk,khd->qhd", attention, values_lane, preferred_element_type=jnp.float32
        ).reshape(rows_dev, 1, features)
        log_total = (highest + jnp.log(summed))[None, :, :, 0]
        return (result, log_total)

    initial = (
        jnp.zeros((rows_dev, lane_count, features), jnp.float32),
        jnp.zeros((lane_count, head_count, rows_dev), jnp.float32),
    )
    return lax.fori_loop(0, lane_count, one_lane, initial)


def attend_backward(query, keys_all, values_all, log_total, grad_mixed, query_tags, key_tags):
    rows_dev, lane_count, features = query.shape
    head_count = features // HEAD_DIM
    key_rows = keys_all.shape[0]

    def one_lane(lane_index, carry):
        scores, query_lane, keys_lane = lane_scores(
            query, keys_all, lane_index, query_tags, key_tags
        )
        values_lane = lax.dynamic_index_in_dim(values_all, lane_index, 1, False).reshape(
            key_rows, head_count, HEAD_DIM
        )
        grad_lane = lax.dynamic_index_in_dim(grad_mixed, lane_index, 1, False).reshape(
            rows_dev, head_count, HEAD_DIM
        )
        attention = jnp.exp(
            scores - lax.dynamic_index_in_dim(log_total, lane_index, 0, False)[:, :, None]
        )
        grad_attention = jnp.einsum(
            "qhd,khd->hqk", grad_lane, values_lane, preferred_element_type=jnp.float32
        )
        inner = jnp.sum(attention * grad_attention, axis=-1, keepdims=True)
        grad_scores = (attention * (grad_attention - inner)).astype(jnp.bfloat16)
        query_part = (
            jnp.einsum("hqk,khd->qhd", grad_scores, keys_lane, preferred_element_type=jnp.float32)
            * SCORE_SCALE
        )
        key_part = (
            jnp.einsum("hqk,qhd->khd", grad_scores, query_lane, preferred_element_type=jnp.float32)
            * SCORE_SCALE
        )
        value_part = jnp.einsum(
            "hqk,qhd->khd",
            attention.astype(jnp.bfloat16),
            grad_lane,
            preferred_element_type=jnp.float32,
        )
        stacked = jnp.stack(
            [key_part.reshape(key_rows, features), value_part.reshape(key_rows, features)], axis=1
        )
        key_terms = stacked[:, None]
        grad_query = query_part.reshape(rows_dev, 1, features)
        return (grad_query, key_terms)

    initial = (
        jnp.zeros((rows_dev, lane_count, features), jnp.float32),
        jnp.zeros((key_rows, lane_count, 2, features), jnp.float32),
    )
    return lax.fori_loop(0, lane_count, one_lane, initial)


def front(stream, layer_index, params, query_tags, key_tags, positions):
    (
        gain_one,
        shift_one,
        mat_qkv,
        bias_qkv,
        mat_out,
        bias_out,
        gain_two,
        shift_two,
        mat_up,
        bias_up,
        mat_down,
        bias_down,
    ) = [item[layer_index] for item in params]
    rows_dev, lane_count, width = stream.shape
    features = mat_qkv.shape[2]
    head_count = features // HEAD_DIM
    frame_place, row_place, column_place = positions
    first = layer_norm(stream, gain_one, shift_one).astype(jnp.bfloat16)
    projected = (
        jnp.einsum("tbd,dcf->tbcf", first, mat_qkv, preferred_element_type=jnp.float32) + bias_qkv
    )
    split = projected.reshape(rows_dev, lane_count, 3, head_count, HEAD_DIM)
    query = (
        rotate(split[:, :, 0], frame_place, row_place, column_place)
        .reshape(rows_dev, lane_count, features)
        .astype(jnp.bfloat16)
    )
    keys = (
        rotate(split[:, :, 1], frame_place, row_place, column_place)
        .reshape(rows_dev, lane_count, features)
        .astype(jnp.bfloat16)
    )
    values = projected[:, :, 2].astype(jnp.bfloat16)
    keys_all, values_all = (
        lax.all_gather(keys, "seq", axis=0, tiled=True),
        lax.all_gather(values, "seq", axis=0, tiled=True),
    )
    mixed_full, log_total = attend_forward(query, keys_all, values_all, query_tags, key_tags)
    mixed = mixed_full.astype(jnp.bfloat16)
    middle = (
        stream
        + sum_heads(jnp.einsum("tbf,fd->tbd", mixed, mat_out, preferred_element_type=jnp.float32))
        + bias_out
    )
    second = layer_norm(middle, gain_two, shift_two).astype(jnp.bfloat16)
    hidden = jnp.einsum("tbd,df->tbf", second, mat_up, preferred_element_type=jnp.float32) + bias_up
    activation = gelu_exact(hidden).astype(jnp.bfloat16)
    return (
        first,
        query,
        keys_all,
        values_all,
        log_total,
        mixed,
        middle,
        second,
        hidden,
        activation,
        mixed_full,
    )


def layer_backward(stream, gradient, layer_index, params, query_tags, key_tags, positions):
    (
        gain_one,
        shift_one,
        mat_qkv,
        bias_qkv,
        mat_out,
        bias_out,
        gain_two,
        shift_two,
        mat_up,
        bias_up,
        mat_down,
        bias_down,
    ) = [item[layer_index] for item in params]
    (
        first,
        query,
        keys_all,
        values_all,
        log_total,
        mixed,
        middle,
        second,
        hidden,
        activation,
        mixed_full,
    ) = front(stream, layer_index, params, query_tags, key_tags, positions)
    frame_place, row_place, column_place = positions
    rows_dev, lane_count, width = stream.shape
    features = query.shape[2]
    head_count = features // HEAD_DIM
    grad_low = gradient.astype(jnp.bfloat16)
    grad_w_down = jnp.einsum(
        "tbf,tbd->fd", activation, grad_low, preferred_element_type=jnp.float32
    )
    grad_b_down = jnp.sum(gradient, axis=(0, 1))
    grad_activation = jnp.einsum(
        "tbd,fd->tbf", grad_low, mat_down, preferred_element_type=jnp.float32
    )
    grad_hidden = jax.vjp(gelu_exact, hidden)[1](grad_activation)[0].astype(jnp.bfloat16)
    grad_b_up = jnp.sum(grad_hidden.astype(jnp.float32), axis=(0, 1))
    grad_w_up = jnp.einsum("tbd,tbf->df", second, grad_hidden, preferred_element_type=jnp.float32)
    grad_second = sum_inputs(
        jnp.einsum("tbf,df->tbd", grad_hidden, mat_up, preferred_element_type=jnp.float32)
    )
    middle_pull = jax.vjp(layer_norm, middle, gain_two, shift_two)[1]
    grad_inner, grad_gain_two, grad_shift_two = middle_pull(grad_second)
    grad_middle = gradient + grad_inner
    grad_b_out = jnp.sum(grad_middle, axis=(0, 1))
    middle_low = grad_middle.astype(jnp.bfloat16)
    grad_w_out = jnp.einsum("tbf,tbd->fd", mixed, middle_low, preferred_element_type=jnp.float32)
    grad_mixed = jnp.einsum(
        "tbd,fd->tbf", middle_low, mat_out, preferred_element_type=jnp.float32
    ).astype(jnp.bfloat16)
    grad_query, key_terms = attend_backward(
        query, keys_all, values_all, log_total, grad_mixed, query_tags, key_tags
    )
    returned = lax.psum_scatter(key_terms, "seq", scatter_dimension=0, tiled=True)
    turned_query = rotate(
        grad_query.reshape(rows_dev, lane_count, head_count, HEAD_DIM),
        -frame_place,
        -row_place,
        -column_place,
    )
    turned_keys = rotate(
        returned[:, :, 0].reshape(rows_dev, lane_count, head_count, HEAD_DIM),
        -frame_place,
        -row_place,
        -column_place,
    )
    grad_projected = jnp.stack(
        [
            turned_query.reshape(rows_dev, lane_count, features),
            turned_keys.reshape(rows_dev, lane_count, features),
            returned[:, :, 1],
        ],
        axis=2,
    ).astype(jnp.bfloat16)
    grad_b_qkv = jnp.sum(grad_projected.astype(jnp.float32), axis=(0, 1))
    grad_w_qkv = jnp.einsum(
        "tbd,tbcf->dcf", first, grad_projected, preferred_element_type=jnp.float32
    )
    grad_first = sum_inputs(
        jnp.einsum("tbcf,dcf->tbd", grad_projected, mat_qkv, preferred_element_type=jnp.float32)
    )
    first_pull = jax.vjp(layer_norm, stream, gain_one, shift_one)[1]
    grad_entry, grad_gain_one, grad_shift_one = first_pull(grad_first)
    grads = (
        grad_gain_one,
        grad_shift_one,
        grad_w_qkv,
        grad_b_qkv,
        grad_w_out,
        grad_b_out,
        grad_gain_two,
        grad_shift_two,
        grad_w_up,
        grad_b_up,
        grad_w_down,
        grad_b_down,
    )
    return (grad_middle + grad_entry, grads)


def per_device(
    tokens,
    d_out,
    norm1_gain,
    norm1_shift,
    w_qkv,
    b_qkv,
    w_out,
    b_out,
    norm2_gain,
    norm2_shift,
    w_up,
    b_up,
    w_down,
    b_down,
    episode_frames,
    live,
):
    rows_dev = tokens.shape[0]
    lane_count = tokens.shape[1] // MICRO
    total_rows = rows_dev * lax.axis_size("seq")
    local_positions = lax.axis_index("seq") * rows_dev + jnp.arange(rows_dev, dtype=jnp.int32)
    key_positions = jnp.arange(total_rows, dtype=jnp.int32)
    tagger = jax.vmap(episode_tags, in_axes=(0, None), out_axes=1)
    query_episode, query_frame, query_row, query_column = tagger(episode_frames, local_positions)
    key_episode, key_frame, key_row, key_column = tagger(episode_frames, key_positions)
    live_keys = lax.all_gather(live, "seq", axis=0, tiled=True)
    params = (
        norm1_gain,
        norm1_shift,
        w_qkv,
        b_qkv,
        w_out,
        b_out,
        norm2_gain,
        norm2_shift,
        w_up,
        b_up,
        w_down,
        b_down,
    )
    layer_grads = [None] * LAYERS
    outputs = []
    grad_tokens = []
    for micro_index in range(MICRO):
        first_lane = micro_index * lane_count
        last_lane = first_lane + lane_count
        query_tags = (query_episode[:, first_lane:last_lane], query_frame[:, first_lane:last_lane])
        key_tags = (
            key_episode[:, first_lane:last_lane],
            key_frame[:, first_lane:last_lane],
            live_keys[:, first_lane:last_lane],
        )
        positions = (
            query_frame[:, first_lane:last_lane],
            query_row[:, first_lane:last_lane],
            query_column[:, first_lane:last_lane],
        )
        stream = tokens[:, first_lane:last_lane].astype(jnp.float32)
        inputs = []
        gathered = []
        for layer_index in range(LAYERS):
            inputs.append(stream)
            layer_state = front(stream, layer_index, params, query_tags, key_tags, positions)
            gathered.append((layer_state[2], layer_state[3]))
            branch = jnp.einsum(
                "tbf,fd->tbd",
                layer_state[9],
                w_down[layer_index],
                preferred_element_type=jnp.float32,
            )
            stream = layer_state[6] + sum_heads(branch) + b_down[layer_index]
        outputs.append(stream)
        gradient = d_out[:, first_lane:last_lane]
        for layer_index in reversed(range(LAYERS)):
            gradient, grads = layer_backward(
                inputs[layer_index], gradient, layer_index, params, query_tags, key_tags, positions
            )
            if layer_grads[layer_index] is None:
                layer_grads[layer_index] = grads
            else:
                layer_grads[layer_index] = jax.tree.map(jnp.add, layer_grads[layer_index], grads)
        grad_tokens.append(gradient)
    stacked = [
        jnp.stack([layer_grads[layer_index][entry] for layer_index in range(LAYERS)])
        for entry in range(12)
    ]
    (
        grad_gain_one,
        grad_shift_one,
        grad_w_qkv,
        grad_b_qkv,
        grad_w_out,
        grad_b_out,
        grad_gain_two,
        grad_shift_two,
        grad_w_up,
        grad_b_up,
        grad_w_down,
        grad_b_down,
    ) = stacked
    in_sums = (
        lax.psum_scatter(grad_w_qkv, "seq", scatter_dimension=1, tiled=True),
        lax.psum_scatter(grad_w_up, "seq", scatter_dimension=1, tiled=True),
        lax.psum_scatter(grad_gain_one, "seq", scatter_dimension=1, tiled=True),
        lax.psum_scatter(grad_shift_one, "seq", scatter_dimension=1, tiled=True),
        lax.psum_scatter(grad_gain_two, "seq", scatter_dimension=1, tiled=True),
        lax.psum_scatter(grad_shift_two, "seq", scatter_dimension=1, tiled=True),
        lax.psum_scatter(grad_b_out, "seq", scatter_dimension=1, tiled=True),
        lax.psum_scatter(grad_b_down, "seq", scatter_dimension=1, tiled=True),
    )
    out_sums = (
        lax.psum_scatter(grad_w_out, "seq", scatter_dimension=2, tiled=True),
        lax.psum_scatter(grad_w_down, "seq", scatter_dimension=2, tiled=True),
    )
    bias_total = lax.psum((grad_b_qkv, grad_b_up), "seq")
    return (
        jnp.concatenate(outputs, axis=1),
        jnp.concatenate(grad_tokens, axis=1),
        in_sums[2],
        in_sums[3],
        in_sums[0],
        bias_total[0],
        out_sums[0],
        in_sums[6],
        in_sums[4],
        in_sums[5],
        in_sums[1],
        bias_total[1],
        out_sums[1],
        in_sums[7],
    )


MESH = pl.DeviceIdType.MESH
BF16 = jnp.bfloat16
F32 = jnp.float32
VMEM_BYTES = 60 * 1024 * 1024
PAIR = 128
VEC = 2048


def nn(left, right):
    return lax.dot_general(left, right, (((1,), (0,)), ((), ())), preferred_element_type=F32)


def nt(left, right):
    return lax.dot_general(left, right, (((1,), (1,)), ((), ())), preferred_element_type=F32)


def tn(left, right):
    return lax.dot_general(left, right, (((0,), (0,)), ((), ())), preferred_element_type=F32)


def at(start, size):
    return pl.ds(pl.multiple_of(start, size), size)


TILE = 256
PIECE = 128


def tile(index):
    return at(index * TILE, TILE)


def repeat(count, body):
    def one(index, carry):
        body(index)
        return carry

    lax.fori_loop(0, count, one, 0)


def remote(src, dst, send, recv, seq, tp):
    return pltpu.make_async_remote_copy(
        src_ref=src,
        dst_ref=dst,
        send_sem=send,
        recv_sem=recv,
        device_id=(seq, tp),
        device_id_type=MESH,
    )


def greet(partners):
    barrier = pltpu.get_barrier_semaphore()
    for seq, tp in partners:
        pl.semaphore_signal(barrier, inc=1, device_id=(seq, tp), device_id_type=MESH)
    pl.semaphore_wait(barrier, len(partners))


def whole(array):
    zeros = (0,) * array.ndim
    return pl.BlockSpec(array.shape, lambda s: zeros, pipeline_mode=pl.Buffered(1))


def whole_out(shape):
    zeros = (0,) * len(shape)
    return pl.BlockSpec(shape, lambda s: zeros)


ANYWHERE = pl.BlockSpec(memory_space=pl.ANY)


def turn_row(table, place, section):
    frequency = np.exp(np.arange(10, dtype=np.float32) * np.float32(-math.log(10000.0) / 10.0))
    angle = place.astype(np.float32)[:, None] * frequency
    for base in range(20 * section, PAIR, HEAD_DIM):
        table[0, :, base : base + 10] = np.cos(angle)
        table[0, :, base + 10 : base + 20] = np.cos(angle)
        table[1, :, base : base + 10] = -np.sin(angle)
        table[2, :, base + 10 : base + 20] = np.sin(angle)


def turn_constants(frames):
    within, ahead = np.zeros((3, FRAME, PAIR), np.float32), np.zeros((3, frames, PAIR), np.float32)
    turn_row(within, np.arange(FRAME) // GRID, 1)
    turn_row(within, np.arange(FRAME) % GRID, 2)
    for base in range(60, PAIR, HEAD_DIM):
        within[0, :, base : base + 4] = 1.0
    turn_row(ahead, np.arange(frames), 0)
    return jnp.asarray(within), jnp.asarray(ahead)


def turn(values, tables, back=False):
    cosine, lower, upper = tables
    pieces = []
    for start in range(0, values.shape[1], PAIR):
        slab = values[:, start : start + PAIR]
        moved = pltpu.roll(slab, PAIR - 10, 1) * lower + pltpu.roll(slab, 10, 1) * upper
        pieces.append(slab * cosine - moved if back else slab * cosine + moved)
    return jnp.concatenate(pieces, axis=1)


def tables_of(fixed_ref, frames_ref, chunk):
    return [fixed_ref[i] + frames_ref[i, pl.ds(chunk, 1), :] for i in range(3)]


def normed(stream):
    center = stream - jnp.mean(stream, axis=-1, keepdims=True)
    spread = jnp.mean(center * center, axis=-1, keepdims=True)
    scale = lax.rsqrt(spread + EPSILON)
    return center * scale, scale


def norm_pull(grad, gain, unit, scale):
    scaled = grad * gain
    return scale * (
        scaled
        - jnp.mean(scaled, axis=-1, keepdims=True)
        - unit * jnp.mean(scaled * unit, axis=-1, keepdims=True)
    )


def kept_norm(unit_ref, scale_ref, piece):
    copies = unit_ref.shape[1] // scale_ref.shape[1]
    unit = unit_ref[piece, :].astype(F32)
    return unit, jnp.concatenate([scale_ref[piece, :]] * copies, axis=1)


def norm_rows(read, gain, shift, layer, full, unit_ref, scale_ref):
    def one(index):
        piece = at(index * PIECE, PIECE)
        unit, scale = normed(read(piece))
        unit_ref[piece, :] = unit.astype(BF16)
        scale_ref[piece, :] = jnp.broadcast_to(scale, (PIECE, PAIR))
        full[piece, :] = (unit * gain[layer : layer + 1, :] + shift[layer : layer + 1, :]).astype(BF16)

    repeat(full.shape[0] // PIECE, one)


def column_sum(values):
    return jnp.sum(values, axis=0, keepdims=True)


def gelu_both(hidden):
    normal = 0.5 + 0.5 * lax.erf(hidden * math.sqrt(0.5))
    density = jnp.exp(hidden * hidden * -0.5) * (1.0 / math.sqrt(2.0 * math.pi))
    return hidden * normal, normal + hidden * density


def project(read, chunk, layer, pair, refs, outs, full):
    gain, shift, weight, bias, fixed, frames = refs
    qkv_ref, first_ref, unit_ref, scale_ref = outs
    norm_rows(read, gain, shift, layer, full, unit_ref, scale_ref)
    first_ref[...] = full[:, at(pair * PAIR, PAIR)]
    tiles = qkv_ref.shape[2] // TILE

    def product(part, index):
        columns = tile(index)
        line = bias[part, layer : layer + 1, columns]
        return nn(full[...], weight[part, :, columns]) + line

    def turned(index):
        part, column = index // tiles, lax.rem(index, tiles)
        scale = jnp.where(part == 0, SCORE_SCALE, 1.0)
        values = turn(product(part, column), tables_of(fixed, frames, chunk)) * scale
        qkv_ref[part, :, tile(column)] = values.astype(BF16)

    def plain(index):
        qkv_ref[2, :, tile(index)] = product(2, index).astype(BF16)

    repeat(2 * tiles, turned)
    repeat(tiles, plain)


class Relay:
    sems = 6

    def __init__(self, n, rows, buffer, other, sems, lives=None, live_other=None):
        self.n, self.rows, self.buffer, self.other = n, rows, buffer, other
        self.lives, self.live_other = lives, live_other
        self.z_send, self.z_recv, self.y_send, self.y_recv, self.c_send, self.c_recv = sems
        self.planes = n // 4
        self.me, self.core = lax.axis_index("seq"), lax.axis_index("tp")
        me = self.me
        self.x, self.y, self.z = lax.rem(me, 2), lax.rem(me // 2, 2), me // 4
        self.across = me + 2 - 4 * self.y

    @staticmethod
    def scratch(n):
        dma, planes = pltpu.SemaphoreType.DMA, n // 4
        shapes = [(planes, 2, 2)] * 2 + [(planes, 2)] * 2 + [(2 * planes,)] * 2
        return [dma(shape) for shape in shapes]

    @property
    def events(self):
        return self.planes

    def plane(self, step):
        return lax.rem(self.z + step, self.planes)

    def place(self, plane, lane):
        return plane * 4 + self.y * 2 + lane

    def reached(self):
        return [(step, far) for step in range(self.planes) for far in (0, 1) if step or far]

    def hello(self):
        barrier = pltpu.get_barrier_semaphore()
        partners = [(self.across, self.core), (self.me, 1 - self.core)]
        for step, far in self.reached():
            lane = 1 - self.x if far else self.x
            partners.append((self.place(self.plane(step), lane), self.core))
        for seq, tp in partners:
            pl.semaphore_signal(barrier, inc=1, device_id=(seq, tp), device_id_type=MESH)

    def met(self):
        pl.semaphore_wait(pltpu.get_barrier_semaphore(), 2 + len(self.reached()))

    def rows_of(self, side, seq):
        return self.buffer.at[side, at(seq * self.rows, self.rows), :]

    def block(self, side, pair):
        return self.buffer.at[side, at(pair * 2 * self.rows, 2 * self.rows), :]

    def items(self, pair):
        found = [self.block(self.core, pair)]
        if self.lives is not None:
            found.append(self.lives.at[at(pair * 2, 2)])
        return found

    def each(self, copy, what):
        for index in range(1 if self.lives is None else 2):
            getattr(copy(index), what)()

    def z_copy(self, step, far):
        def copy(index):
            lane = 1 - self.x if far else self.x
            if index == 0:
                source = self.other.at[self.core] if far else self.rows_of(self.core, self.me)
                target = self.rows_of(self.core, self.me)
            else:
                source = self.live_other if far else self.lives.at[self.me]
                target = self.lives.at[self.me]
            return remote(
                source,
                target,
                self.z_send.at[step, far, index],
                self.z_recv.at[step, far, index],
                self.place(self.plane(step), lane),
                self.core,
            )

        return copy

    def y_copy(self, plane, row):
        def copy(index):
            item = self.items(plane * 2 + row)[index]
            return remote(
                item,
                item,
                self.y_send.at[plane, index],
                self.y_recv.at[plane, index],
                self.across,
                self.core,
            )

        return copy

    def c_copy(self, pair, side):
        item = self.block(side, pair)
        return remote(
            item, item, self.c_send.at[pair], self.c_recv.at[pair], self.me, 1 - self.core
        )

    def begin(self):
        for step, far in self.reached():
            self.each(self.z_copy(step, far), "start")

    def arrive(self, event):
        @pl.when(event > 0)
        def _():
            self.each(self.z_copy(event, 0), "wait_recv")

        self.each(self.z_copy(event, 1), "wait_recv")
        plane = self.plane(self.planes - event)
        self.each(self.y_copy(plane, self.y), "start")
        self.c_copy(plane * 2 + self.y, self.core).start()

    def complete(self, event):
        plane = self.plane(self.planes - event)
        self.each(self.y_copy(plane, 1 - self.y), "wait_recv")
        self.c_copy(plane * 2 + 1 - self.y, self.core).start()

    def ready(self, event):
        plane = self.plane(self.planes - event)
        self.c_copy(plane * 2, 1 - self.core).wait_recv()
        self.c_copy(plane * 2 + 1, 1 - self.core).wait_recv()
        return plane

    def finish(self):
        for step, far in self.reached():
            self.each(self.z_copy(step, far), "wait_send")
        for plane in range(self.planes):
            self.each(self.y_copy(plane, self.y), "wait_send")
        for pair in range(2 * self.planes):
            self.c_copy(pair, self.core).wait_send()


def split_lanes(values, x, buffer, other, start, rows):
    half = values.shape[2] // 2
    zero, one = values[:, 0, :], values[:, 1, :]
    own, far = jnp.where(x == 0, zero, one), jnp.where(x == 0, one, zero)
    core = lax.axis_index("tp")
    own = jnp.where(core == 0, own[:, :half], own[:, half:]).astype(BF16)
    buffer[core, at(start, rows), :] = own
    for side in range(2):
        other[side] = far[:, side * half : (side + 1) * half].astype(BF16)


def gather_and_project(tokens, live, episode_frames, gain, shift, qkv, bias, fixed, ahead, n):
    rows, lanes, width = tokens.shape
    half = width // 2
    total = n * rows
    chunks = total // FRAME
    per_frame = FRAME // rows
    features = qkv.shape[3]
    slots = episode_frames.shape[1]

    def kernel(*refs):
        refs = list(refs)

        def take(count):
            taken = refs[:count]
            del refs[:count]
            return taken

        tokens_ref, live_ref, counts_ref, gain_ref, shift_ref, w_any, bias_ref = take(7)
        fixed_ref, ahead_ref = take(2)
        all_ref, mask_ref, frames_ref = take(3)
        qkv_ref, *projected = take(4)
        other, lives, live_other, weight, full, w_sem = take(6)
        relay = Relay(n, rows, all_ref, other, take(Relay.sems), lives, live_other)
        load = pltpu.make_async_copy(w_any.at[0], weight, w_sem)
        load.start()
        relay.hello()
        x, me = relay.x, relay.me
        split_lanes(tokens_ref[...].astype(F32), x, all_ref, other, me * rows, rows)
        lane = lax.broadcasted_iota(jnp.int32, (1, FRAME), 1)
        here = lane // rows == lax.rem(me, per_frame)
        tiles = []
        for index in range(lanes):
            alive = live_ref[index : index + 1, :].astype(F32)
            alive = jnp.where(here, jnp.concatenate([alive] * per_frame, axis=1), 0.0)
            tiles.append(jnp.broadcast_to(alive, (8, FRAME)))
        lives[me] = jnp.where(x == 0, tiles[0], tiles[1])
        live_other[...] = jnp.where(x == 0, tiles[1], tiles[0])
        relay.met()
        relay.begin()

        counts = [counts_ref[x, slot] for slot in range(slots)]
        episodes, openings = [], []
        for frame in range(chunks):
            end, episode, opening = 0, 0, 0
            for slot in range(slots):
                end = end + counts[slot]
                passed = frame >= end
                episode = episode + passed.astype(jnp.int32)
                opening = opening + jnp.where(passed, counts[slot], 0)
            episodes.append(episode)
            openings.append(frame - opening)
        for index in range(3):
            table = []
            for frame in range(chunks):
                line = jnp.zeros((1, PAIR), F32)
                for choice in range(chunks):
                    line = jnp.where(
                        openings[frame] == choice, ahead_ref[index, choice : choice + 1, :], line
                    )
                table.append(line)
            frames_ref[index] = jnp.concatenate(
                table + [jnp.zeros((8 - chunks, PAIR), F32)], axis=0
            )
        load.wait()

        def project_frame(frame):
            place = frame * FRAME

            def read(piece):
                piece = at(place + piece.start, PIECE)
                return jnp.concatenate([all_ref[0, piece, :], all_ref[1, piece, :]], axis=1).astype(F32)

            rows_here = at(place, FRAME)
            project(
                read,
                frame,
                0,
                me // 2,
                (gain_ref, shift_ref, weight, bias_ref, fixed_ref, frames_ref),
                [qkv_ref.at[:, rows_here, :]] + [ref.at[rows_here, :] for ref in projected],
                full,
            )

        def one_event(event):
            @pl.when(event < relay.events)
            def _():
                relay.arrive(event)

            @pl.when((event >= 1) & (event <= relay.events))
            def _():
                relay.complete(event - 1)

            @pl.when(event >= 2)
            def _():
                project_frame(relay.ready(event - 2))

        repeat(relay.events + 2, one_event)
        relay.finish()

        for key_frame in range(chunks):
            alive = lives[key_frame * per_frame, 0:1, :]
            for part in range(1, per_frame):
                alive = alive + lives[key_frame * per_frame + part, 0:1, :]
            closed = (alive - 1.0) * -MASKED
            lines = []
            for query_frame in range(chunks):
                allowed = (episodes[query_frame] == episodes[key_frame]) & (
                    openings[key_frame] <= openings[query_frame]
                )
                lines.append(jnp.where(allowed, closed, MASKED))
            lines.append(jnp.zeros((PAIR - chunks, FRAME), F32))
            mask_ref[key_frame * FRAME : (key_frame + 1) * FRAME, :] = jnp.concatenate(
                lines, axis=0
            ).T.astype(BF16)

    in_vmem = pl.BlockSpec(memory_space=pltpu.VMEM)
    in_smem = pl.BlockSpec(memory_space=pltpu.SMEM)
    return pl.pallas_call(
        kernel,
        out_shape=(
            jax.ShapeDtypeStruct((2, total, half), BF16),
            jax.ShapeDtypeStruct((total, PAIR), BF16),
            jax.ShapeDtypeStruct((3, 8, PAIR), F32),
            jax.ShapeDtypeStruct((3, total, features), BF16),
            jax.ShapeDtypeStruct((total, PAIR), BF16),
            jax.ShapeDtypeStruct((total, width), BF16),
            jax.ShapeDtypeStruct((total, PAIR), F32),
        ),
        in_specs=[in_vmem, in_vmem, in_smem, in_vmem, in_vmem, ANYWHERE] + [in_vmem] * 3,
        out_specs=(in_vmem,) * 7,
        scratch_shapes=[
            pltpu.VMEM((2, rows, half), BF16),
            pltpu.VMEM((n, 8, FRAME), F32),
            pltpu.VMEM((8, FRAME), F32),
            pltpu.VMEM(qkv.shape[1:], BF16),
            pltpu.VMEM((FRAME, width), BF16),
            pltpu.SemaphoreType.DMA,
        ]
        + Relay.scratch(n),
        compiler_params=pltpu.CompilerParams(
            collective_id=0, has_side_effects=True, vmem_limit_bytes=VMEM_BYTES
        ),
        name="gather_and_project",
    )(tokens, live, episode_frames, gain, shift, qkv, bias, fixed, ahead)


def halves(ref):
    return jnp.concatenate([ref[0], ref[1]], axis=1).astype(F32)


def halves_spec(shape, chunks, behind, span=FRAME):
    return pl.BlockSpec(
        (2, span, shape[2]), lambda s: (0, jnp.clip(s - behind, 0, chunks - 1), 0)
    )


def layer_forward(layer, qkv, key_bias, stream, mats, rows_of, next_refs, d_out, n, identity):
    _, total, features = qkv.shape
    split = stream.ndim == 3
    width = mats[1].shape[1]
    rows_here = total // n
    hidden_units = mats[1].shape[2]
    chunks = total // FRAME
    heads = features // HEAD_DIM
    group = 2
    last = next_refs is None
    b_out, gain, shift, b_up, b_down = rows_of
    mat_out, mat_up, mat_down = mats

    def kernel(*refs):
        refs = list(refs)

        def take(count):
            taken = refs[:count]
            del refs[:count]
            return taken

        q_ref, k_ref, v_ref, kb_ref, x_ref = take(5)
        wo_any, wu_any, wd_any = take(3)
        bo_ref, gain_ref, shift_ref, bu_ref, bd_ref = take(5)
        if not last:
            wq_any, ngain, nshift, nbias, fixed, frames = take(6)
        if d_out is not None:
            (d_ref,) = take(1)
        p_ref, r_ref, mixed_ref, unit_ref, scale_ref, second_ref, act_ref, gp_ref, x_out = take(9)
        if not last:
            next_outs = take(4)
        if d_out is not None:
            (d_all,) = take(1)
        wo, wu, wd, mid, full, hidden, asks, scores, tops, sums = take(10)
        if not last:
            (wq,) = take(1)
        a_send, a_recv, b_send, b_recv, w_sem, send_sem, recv_sem = take(7)
        relay = None
        if d_out is not None:
            buffer, other, d_sem = take(3)
            relay = Relay(n, rows_here, buffer, other, take(Relay.sems))

        step = pl.program_id(0)
        me, core = lax.axis_index("seq"), lax.axis_index("tp")

        items = [(wo_any, wo), (wu_any, wu), (wd_any, wd)]
        if not last:
            items.append((wq_any, wq))

        def load(index):
            source, target = items[index]
            return pltpu.make_async_copy(
                source.at[layer if index < 3 else layer + 1], target, w_sem.at[index]
            )

        def exchange(kind, chunk):
            source, target = ((a_send, a_recv), (b_send, b_recv))[kind]
            return remote(
                source.at[chunk],
                target.at[chunk],
                send_sem.at[kind, chunk],
                recv_sem.at[kind, chunk],
                me,
                1 - core,
            )

        @pl.when(step == 0)
        def _():
            for index in range(len(items)):
                load(index).start()
            if relay is None:
                greet([(me, 1 - core)])
            else:
                relay.hello()
                split_lanes(d_ref[...], relay.x, buffer, other, me * rows_here, rows_here)
                relay.met()
                relay.begin()

        if relay is not None:
            for event in range(relay.events):

                @pl.when(step == 1 + event // 2)
                def _():
                    relay.arrive(event)

                @pl.when(step == 2 + event // 2)
                def _():
                    relay.complete(event)

            @pl.when(step == chunks + 1)
            def _():
                for event in range(relay.events):
                    relay.ready(event)
                relay.finish()
                pltpu.make_async_copy(buffer, d_all, d_sem).start()

        lane = lax.broadcasted_iota(jnp.int32, (1, PAIR), 1)
        sides = [(lane < HEAD_DIM).astype(F32).astype(BF16), (lane >= HEAD_DIM).astype(F32).astype(BF16)]
        low_side = lane < HEAD_DIM

        def attend(first_slab):
            keys = step + 1
            asked = jnp.broadcast_to((lane == step).astype(F32), (FRAME, PAIR)).astype(BF16)
            spots = [(slab, side, slab * 2 + side) for slab in range(group) for side in range(2)]

            def lanes(slab):
                return at((first_slab + slab) * PAIR, PAIR)

            for slab, side, head in spots:
                asks[head] = jnp.concatenate([q_ref[0, :, lanes(slab)] * sides[side], asked], axis=1)
                tops[head] = jnp.full((FRAME, PAIR), MASKED, F32)
                sums[head] = jnp.zeros((FRAME, PAIR), F32)

            def score(block):
                rows_here = tile(block)
                for slab, side, head in spots:
                    key = jnp.concatenate([k_ref[0, rows_here, lanes(slab)], kb_ref[rows_here, :]], axis=1)
                    found = nt(asks[head], key)
                    scores[head, block] = found
                    tops[head] = jnp.maximum(
                        tops[head], jnp.maximum(found[:, :PAIR], found[:, PAIR:])
                    )

            repeat(keys, score)
            for head in range(2 * group):
                top = jnp.max(tops[head], axis=1, keepdims=True)
                tops[head] = jnp.broadcast_to(top, (FRAME, PAIR))

            def mix(block):
                rows_here = tile(block)
                for slab, side, head in spots:
                    top = jnp.concatenate([tops[head]] * (FRAME // PAIR), axis=1)
                    shifted = jnp.exp(scores[head, block] - top).astype(BF16)
                    p_ref[0, first_slab * 2 + head, rows_here, :] = shifted.T
                    value = v_ref[0, rows_here, lanes(slab)] * sides[side] + sides[1 - side]
                    sums[head] += nn(shifted, value)

            repeat(keys, mix)
            for slab in range(group):
                one, two = sums[2 * slab], sums[2 * slab + 1]
                divisor = 1.0 / jnp.where(
                    low_side, pltpu.roll(one, HEAD_DIM, 1), pltpu.roll(two, HEAD_DIM, 1)
                )
                r_ref[:, lanes(slab)] = divisor
                mixed_ref[:, lanes(slab)] = (jnp.where(low_side, one, two) * divisor).astype(BF16)

        @pl.when(step < chunks)
        def _():
            repeat(features // (group * PAIR), lambda index: attend(index * group))

        @pl.when(step == 0)
        def _():
            load(0).wait()

        @pl.when(step < chunks)
        def _():
            def one(index):
                a_send[step, :, tile(index)] = nn(mixed_ref[...], wo[:, tile(index)]).astype(BF16)

            repeat(width // TILE, one)
            exchange(0, step).start()

        @pl.when(step == 1)
        def _():
            load(1).wait()
            load(2).wait()

        @pl.when((step >= 1) & (step <= chunks))
        def _():
            chunk = step - 1
            slot = lax.rem(chunk, 2)
            exchange(0, chunk).wait_recv()

            def read(piece):
                middle = jnp.concatenate([x_ref[0, piece, :], x_ref[1, piece, :]], axis=1) if split else x_ref[piece, :]
                arrived = a_send[chunk, piece, :].astype(F32) + a_recv[chunk, piece, :].astype(F32)
                middle = middle.astype(F32) + arrived + bo_ref[layer : layer + 1, :]
                mid[slot, piece, :] = middle
                return middle

            norm_rows(read, gain_ref, shift_ref, layer, full, unit_ref, scale_ref)
            second_ref[...] = full[:, at((me // 2) * PAIR, PAIR)]
            tiles = hidden_units // TILE
            hidden[0] = nn(full[...], wu[:, :TILE])

            def one(index):
                following = tile(lax.rem(index + 1, tiles))
                hidden[lax.rem(index + 1, 2)] = nn(full[...], wu[:, following])
                line = bu_ref[layer : layer + 1, tile(index)]
                act, slope = gelu_both(hidden[lax.rem(index, 2)] + line)
                act_ref[:, tile(index)] = act.astype(BF16)
                gp_ref[:, tile(index)] = slope.astype(BF16)

            repeat(tiles, one)

            def down(index):
                b_send[chunk, :, tile(index)] = nn(act_ref[...], wd[:, tile(index)]).astype(BF16)

            repeat(width // TILE, down)
            exchange(1, chunk).start()

        if not last:

            @pl.when(step == 2)
            def _():
                load(3).wait()

        @pl.when(step >= 2)
        def _():
            chunk = step - 2
            slot = lax.rem(chunk, 2)
            exchange(1, chunk).wait_recv()

            def read(piece):
                arrived = b_send[chunk, piece, :].astype(F32) + b_recv[chunk, piece, :].astype(F32)
                result = mid[slot, piece, :] + arrived + bd_ref[layer : layer + 1, :]
                x_out[piece, :] = result
                return result

            if last:
                repeat(FRAME // PIECE, lambda index: read(at(index * PIECE, PIECE)) is None)
            else:
                project(
                    read,
                    chunk,
                    layer + 1,
                    me // 2,
                    (ngain, nshift, wq, nbias, fixed, frames),
                    next_outs,
                    full,
                )

        @pl.when(step == chunks + 1)
        def _():
            for kind in range(2):
                for chunk in range(chunks):
                    exchange(kind, chunk).wait_send()
            if relay is not None:
                pltpu.make_async_copy(buffer, d_all, d_sem).wait()

    def rows(columns, behind):
        return pl.BlockSpec(
            (FRAME, columns), lambda s: (jnp.clip(s - behind, 0, chunks - 1), 0)
        )

    def part_of(part):
        return pl.BlockSpec(
            (1, total, features), lambda s: (part, 0, 0), pipeline_mode=pl.Buffered(1)
        )

    in_specs = [
        pl.BlockSpec((1, FRAME, features), lambda s: (0, jnp.minimum(s, chunks - 1), 0)),
        part_of(1),
        part_of(2),
        whole(key_bias),
    ]
    in_specs += [halves_spec(stream.shape, chunks, 1) if split else rows(width, 1)]
    in_specs += [ANYWHERE] * 3 + [whole(item) for item in rows_of]
    operands = [qkv, qkv, qkv, key_bias, stream, *mats, *rows_of]
    if not last:
        in_specs += [ANYWHERE] + [whole(item) for item in next_refs[1:]]
        operands += list(next_refs)
    if d_out is not None:
        in_specs += [whole(d_out)]
        operands += [d_out]
    out_shape = [
        jax.ShapeDtypeStruct((chunks, heads, total, FRAME), BF16),
        jax.ShapeDtypeStruct((total, features), F32),
        jax.ShapeDtypeStruct((total, features), BF16),
        jax.ShapeDtypeStruct((total, width), BF16),
        jax.ShapeDtypeStruct((total, PAIR), F32),
        jax.ShapeDtypeStruct((total, PAIR), BF16),
        jax.ShapeDtypeStruct((total, hidden_units), BF16),
        jax.ShapeDtypeStruct((total, hidden_units), BF16),
        jax.ShapeDtypeStruct((total, width), F32),
    ]
    out_specs = [
        pl.BlockSpec((1, heads, total, FRAME), lambda s: (jnp.minimum(s, chunks - 1), 0, 0, 0)),
        rows(features, 0),
        rows(features, 0),
        rows(width, 1),
        rows(PAIR, 1),
        rows(PAIR, 1),
        rows(hidden_units, 1),
        rows(hidden_units, 1),
        rows(width, 2),
    ]
    scratch = [
        pltpu.VMEM(mat_out.shape[1:], BF16),
        pltpu.VMEM(mat_up.shape[1:], BF16),
        pltpu.VMEM(mat_down.shape[1:], BF16),
        pltpu.VMEM((2, FRAME, width), F32),
        pltpu.VMEM((FRAME, width), BF16),
        pltpu.VMEM((2, FRAME, TILE), F32),
        pltpu.VMEM((2 * group, FRAME, 2 * PAIR), BF16),
        pltpu.VMEM((2 * group, chunks, FRAME, FRAME), F32),
        pltpu.VMEM((2 * group, FRAME, PAIR), F32),
        pltpu.VMEM((2 * group, FRAME, PAIR), F32),
    ]
    if not last:
        out_shape += [jax.ShapeDtypeStruct((3, total, features), BF16)]
        out_shape += [jax.ShapeDtypeStruct((total, PAIR), BF16)]
        out_shape += [jax.ShapeDtypeStruct((total, width), BF16)]
        out_shape += [jax.ShapeDtypeStruct((total, PAIR), F32)]
        out_specs += [
            pl.BlockSpec((3, FRAME, features), lambda s: (0, jnp.clip(s - 2, 0, chunks - 1), 0))
        ]
        out_specs += [rows(PAIR, 2), rows(width, 2), rows(PAIR, 2)]
    if d_out is not None:
        out_shape += [jax.ShapeDtypeStruct((2, total, width // 2), BF16)]
        out_specs += [ANYWHERE]
        scratch += [pltpu.VMEM(next_refs[0].shape[1:], BF16)]
    scratch += [pltpu.VMEM((chunks, FRAME, width), BF16)] * 4
    scratch += [
        pltpu.SemaphoreType.DMA((4,)),
        pltpu.SemaphoreType.DMA((2, chunks)),
        pltpu.SemaphoreType.DMA((2, chunks)),
    ]
    if d_out is not None:
        scratch += [
            pltpu.VMEM((2, total, width // 2), BF16),
            pltpu.VMEM((2, rows_here, width // 2), BF16),
            pltpu.SemaphoreType.DMA,
        ]
        scratch += Relay.scratch(n)
    return pl.pallas_call(
        kernel,
        grid=(chunks + 2,),
        out_shape=out_shape,
        in_specs=in_specs,
        out_specs=out_specs,
        scratch_shapes=scratch,
        compiler_params=pltpu.CompilerParams(
            collective_id=identity, has_side_effects=True, vmem_limit_bytes=VMEM_BYTES
        ),
        name=f"layer_forward_{layer}",
    )(*operands)


class Swap:
    def __init__(self, ships, lane_rows):
        self.ships, self.lane_rows = ships, lane_rows
        self.count = len(ships) + len(lane_rows)

    def operands(self):
        return [*self.ships, *[item for item, _ in self.lane_rows]]

    def in_specs(self):
        return [whole(item) for item in self.ships] + [ANYWHERE] * len(self.lane_rows)

    def outputs(self):
        shapes, specs = [], []
        for item in self.ships:
            shape = (item.shape[0] // 2, item.shape[1])
            shapes.append(jax.ShapeDtypeStruct(shape, F32))
            specs.append(whole_out(shape))
        for item, count in self.lane_rows:
            shapes.append(jax.ShapeDtypeStruct((count or item.shape[0], item.shape[1]), item.dtype))
            specs.append(ANYWHERE)
        return shapes, specs

    def scratch(self):
        if not self.count:
            return []
        buffers = [pltpu.VMEM((item.shape[0] // 2, item.shape[1]), BF16) for item in self.ships]
        return buffers * 2 + [pltpu.SemaphoreType.DMA((self.count,))] * 2

    def bind(self, sources, targets, scratch):
        ships = len(self.ships)
        me, core = lax.axis_index("seq"), lax.axis_index("tp")
        x = lax.rem(me, 2)
        beside = me + 1 - 2 * x
        half = PAIR // 2

        def copy(index):
            if index < ships:
                source, target = scratch[index], scratch[ships + index]
            else:
                source, target = sources[index], targets[index]
                count = self.lane_rows[index - ships][1]
                if count:
                    source = source.at[at(beside * count, count), :]
            send, recv = scratch[2 * ships].at[index], scratch[2 * ships + 1].at[index]
            return remote(source, target, send, recv, beside, core)

        def start():
            for index in range(self.count):
                if index < ships:
                    scratch[index][...] = sources[index][at((1 - x) * half, half), :].astype(BF16)
                copy(index).start()

        def finish():
            for index in range(self.count):
                copy(index).wait_recv()
                if index < ships:
                    own = sources[index][at(x * half, half), :]
                    targets[index][...] = own + scratch[ships + index][...].astype(F32)
            for index in range(self.count):
                copy(index).wait_send()

        return start, finish


def attention_backward(
    probs, divisor, mixed, qkv, grad_mixed, first, fixed, frames, swap, swap_qkv, identity
):
    _, total, features = qkv.shape
    chunks = total // FRAME
    slabs = features // PAIR
    half = PAIR // 2

    def kernel(*refs):
        refs = list(refs)

        def take(count):
            taken = refs[:count]
            del refs[:count]
            return taken

        p_ref, r_ref, o_ref, q_ref, k_ref, v_ref, g_ref, first_ref, fixed_ref, frames_ref = take(10)
        sources = take(swap.count)
        grad_ref, qkv_out = take(2)
        targets = take(swap.count)
        dk_sum, dv_sum, dq_sum, first_turned, key_turned, values, asks, gives, ends = take(9)
        if swap_qkv:
            qkv_own, qkv_send, qkv_recv, qkv_sems = take(4)
        start, finish = swap.bind(sources, targets, refs)

        step = pl.program_id(0)
        me, core = lax.axis_index("seq"), lax.axis_index("tp")
        x = lax.rem(me, 2)
        beside = me + 1 - 2 * x

        def qkv_copy(slab):
            return remote(
                qkv_send.at[slab],
                qkv_recv.at[slab],
                qkv_sems.at[0, slab],
                qkv_sems.at[1, slab],
                beside,
                core,
            )

        @pl.when(step == 0)
        def _():
            greet([(beside, core)])
            start()
            first_turned[...] = first_ref[...].T

        lane = lax.broadcasted_iota(jnp.int32, (1, PAIR), 1)
        sides = [(lane < HEAD_DIM).astype(F32).astype(BF16), (lane >= HEAD_DIM).astype(F32).astype(BF16)]
        key_turned[...] = k_ref[0].T
        ones = jnp.broadcast_to((lane < 2).astype(F32), (total, PAIR)).astype(BF16)
        values[...] = jnp.concatenate([v_ref[0], ones], axis=1)
        dk_sum[...] = jnp.zeros_like(dk_sum)
        dv_sum[...] = jnp.zeros_like(dv_sum)

        def one_frame(frame):
            own = tile(frame)
            scaled = (g_ref[own, :].astype(F32) * r_ref[own, :]).astype(BF16)
            inner = scaled.astype(F32) * o_ref[own, :].astype(F32)
            for side in range(2):
                delta = jnp.sum(
                    jnp.where((lane < HEAD_DIM) == (side == 0), inner, 0.0), axis=1, keepdims=True
                )
                coarse = delta.astype(BF16).astype(F32)
                rest = jnp.where(lane == 0, -coarse, jnp.where(lane == 1, coarse - delta, 0.0))
                give = scaled * sides[side]
                part = slice(side * FRAME, (side + 1) * FRAME)
                gives[part, :] = give
                ends[side] = jnp.concatenate([give, rest.astype(BF16)], axis=1)
                asks[part, :] = q_ref[0, own, :] * sides[side]
            dq_sum[...] = jnp.zeros_like(dq_sum)

            def one_block(block):
                here = tile(block)
                grads, probs_here = [], []
                for side in range(2):
                    attention = p_ref[frame, side, here, :]
                    grad = nt(values[here, :], ends[side])
                    grad = (attention.astype(F32) * grad).astype(BF16)
                    part = slice(side * HEAD_DIM, (side + 1) * HEAD_DIM)
                    dq_sum[part, :] += nn(key_turned[part, here], grad)
                    grads.append(grad)
                    probs_here.append(attention)
                dk_sum[here, :] += nn(jnp.concatenate(grads, axis=1), asks[...])
                dv_sum[here, :] += nn(jnp.concatenate(probs_here, axis=1), gives[...])

            repeat(frame + 1, one_block)
            tables = tables_of(fixed_ref, frames_ref, frame)
            grad_ref[0, own, :] = (turn(dq_sum[...].T, tables, True) * SCORE_SCALE).astype(BF16)

        repeat(chunks, one_frame)

        def turn_back(frame):
            own = tile(frame)
            tables = tables_of(fixed_ref, frames_ref, frame)
            grad_ref[1, own, :] = turn(dk_sum[own, :], tables, True).astype(BF16)
            grad_ref[2, own, :] = dv_sum[own, :].astype(BF16)

        repeat(chunks, turn_back)
        for part in range(3):
            piece = slice(part * PAIR, (part + 1) * PAIR)
            terms = nn(first_turned[...], grad_ref[part])
            if swap_qkv:
                qkv_own[step, :, piece] = terms
                qkv_send[step, :, piece] = qkv_own[step, at((1 - x) * half, half), piece].astype(BF16)
            else:
                qkv_out[:, at(part * features + step * PAIR, PAIR)] = terms
        if swap_qkv:
            qkv_copy(step).start()

        @pl.when(step == slabs - 1)
        def _():
            finish()
            for slab in range(slabs if swap_qkv else 0):
                qkv_copy(slab).wait_recv()
                for part in range(3):
                    piece = slice(part * PAIR, (part + 1) * PAIR)
                    place = part * features + slab * PAIR
                    qkv_out[:, place : place + PAIR] = qkv_own[
                        slab, at(x * half, half), piece
                    ] + qkv_recv[slab, :, piece].astype(F32)
            for slab in range(slabs if swap_qkv else 0):
                qkv_copy(slab).wait_send()

    slab = pl.BlockSpec((total, PAIR), lambda s: (0, s))
    in_specs = [pl.BlockSpec((chunks, 2, total, FRAME), lambda s: (0, s, 0, 0))]
    in_specs += [slab] * 2
    for part in range(3):
        in_specs.append(pl.BlockSpec((1, total, PAIR), lambda s, part=part: (part, 0, s)))
    in_specs += [slab] + [whole(first), whole(fixed), whole(frames)]
    in_specs += swap.in_specs()
    qkv_shape = (half if swap_qkv else PAIR, 3 * features)
    shapes, specs = swap.outputs()
    out_shape = [jax.ShapeDtypeStruct((3, total, features), BF16)]
    out_shape += [jax.ShapeDtypeStruct(qkv_shape, F32)] + shapes
    out_specs = [pl.BlockSpec((3, total, PAIR), lambda s: (0, 0, s))] + [whole_out(qkv_shape)] + specs
    scratch = [pltpu.VMEM((total, PAIR), F32)] * 2 + [pltpu.VMEM((PAIR, FRAME), F32)]
    scratch += [pltpu.VMEM((PAIR, total), BF16)] * 2 + [pltpu.VMEM((total, 2 * PAIR), BF16)]
    scratch += [pltpu.VMEM((2 * FRAME, PAIR), BF16)] * 2
    scratch += [pltpu.VMEM((2, FRAME, 2 * PAIR), BF16)]
    if swap_qkv:
        scratch += [pltpu.VMEM((slabs, PAIR, 3 * PAIR), F32)]
        scratch += [pltpu.VMEM((slabs, half, 3 * PAIR), BF16)] * 2
        scratch += [pltpu.SemaphoreType.DMA((2, slabs))]
    scratch += swap.scratch()
    return pl.pallas_call(
        kernel,
        grid=(slabs,),
        out_shape=out_shape,
        in_specs=in_specs,
        out_specs=out_specs,
        scratch_shapes=scratch,
        compiler_params=pltpu.CompilerParams(
            collective_id=identity, has_side_effects=True, vmem_limit_bytes=VMEM_BYTES
        ),
        name=f"attention_backward_{identity}",
    )(
        probs,
        divisor,
        mixed,
        qkv,
        qkv,
        qkv,
        grad_mixed,
        first,
        fixed,
        frames,
        *swap.operands(),
    )


def rows_backward(entry, upper, identity, swap):
    top, bottom = len(entry) == 1, upper is None
    if not top:
        above, entry = entry[0], entry[1:]
    total = entry[0].shape[1]
    chunks = total // FRAME
    ahead = 0 if top else 1
    if top:
        width = 2 * entry[0].shape[2]
    else:
        features, width = entry[0].shape[2], entry[3].shape[1]
    if not bottom:
        layer = upper[0]
        hidden_units, mixed_features = upper[1].shape[1], upper[6].shape[1]
    place_rows = total // lax.axis_size("seq")

    def kernel(*refs):
        refs = list(refs)

        def take(count):
            taken = refs[:count]
            del refs[:count]
            return taken

        if top:
            (d_out_ref,) = take(1)
        else:
            dqkv_ref, unit1, scale1, dm_ref, wq, gain1 = take(6)
        if not bottom:
            act_ref, gp_ref, unit2, scale2, second_ref, mixed_ref = take(6)
            wo_any, wu_any, wd_any, gain2 = take(4)
        sources = take(swap.count)
        if not top:
            (vec1,) = take(1)
        if not bottom:
            dmid_out, dmix_out, out_sum, up_sum, down_sum, vec2 = take(6)
        else:
            dx_out, dx_other, vec_other = take(3)
        targets = take(swap.count)
        if not top:
            a_send, a_recv = take(2)
        if not bottom:
            b_send, b_recv, grad_keep, hidden_keep, low_keep, low_turned, second_turned, wo, wu, wd, w_sem = take(11)
        else:
            dx_keep, dx_send, dx_recv, vec_recv, x_send_sem, x_recv_sem = take(6)
        send_sem, recv_sem = take(2)
        start_swap, finish_swap = swap.bind(sources, targets, refs)

        step = pl.program_id(0)
        me, core = lax.axis_index("seq"), lax.axis_index("tp")
        pair = at((me // 2) * PAIR, PAIR)
        x = lax.rem(me, 2)
        beside = me + 1 - 2 * x

        def exchange(kind, chunk):
            source, target = (a_send, a_recv) if kind == 0 else (b_send, b_recv)
            return remote(
                source.at[chunk],
                target.at[chunk],
                send_sem.at[kind, chunk],
                recv_sem.at[kind, chunk],
                me,
                1 - core,
            )

        def load(index):
            source, target = ((wd_any, wd), (wu_any, wu), (wo_any, wo))[index]
            return pltpu.make_async_copy(source.at[layer], target, w_sem.at[index])

        @pl.when(step == 0)
        def _():
            if not bottom:
                for index in range(3):
                    load(index).start()
                out_sum[...] = jnp.zeros_like(out_sum)
                up_sum[...] = jnp.zeros_like(up_sum)
                down_sum[...] = jnp.zeros_like(down_sum)
                vec2[...] = jnp.zeros_like(vec2)
            if not top:
                vec1[...] = jnp.zeros_like(vec1)
            greet([(me, 1 - core)] + ([(beside, core)] if bottom or swap.count else []))
            start_swap()

        if not top:

            @pl.when(step < chunks)
            def _():
                def one(index):
                    here = tile(index)
                    partial = nt(dqkv_ref[0], wq[0, 0, here, :])
                    for part in range(1, 3):
                        partial = partial + nt(dqkv_ref[part], wq[0, part, here, :])
                    a_send[step, :, here] = partial.astype(BF16)

                repeat(width // TILE, one)
                exchange(0, step).start()
                for part in range(3):
                    vec1[part : part + 1, :] += column_sum(dqkv_ref[part].astype(F32))

        @pl.when((step >= ahead) & (step < chunks + ahead))
        def _():
            chunk = step - ahead
            slot = lax.rem(chunk, 2)
            if not top:
                exchange(0, chunk).wait_recv()

            def entry_norm(index):
                piece = at(index * PIECE, PIECE)
                if top:
                    gradient = jnp.concatenate([d_out_ref[0, piece, :], d_out_ref[1, piece, :]], axis=1)
                    gradient = gradient.astype(F32)
                else:
                    grad_first = a_send[chunk, piece, :].astype(F32) + a_recv[chunk, piece, :].astype(F32)
                    unit, scale = kept_norm(unit1, scale1, piece)
                    for start, sums in ((3, column_sum(grad_first * unit)), (5, column_sum(grad_first))):
                        for side in range(width // features):
                            part = slice(side * features, (side + 1) * features)
                            vec1[start + side : start + side + 1, :] += sums[:, part]
                    gradient = dm_ref[piece, :] + norm_pull(
                        grad_first, gain1[above : above + 1, :], unit, scale
                    )
                if bottom:
                    dx_keep[at(chunk * FRAME + index * PIECE, PIECE), :] = gradient
                else:
                    grad_keep[slot, piece, :] = gradient
                    vec2[1:2, :width] += column_sum(gradient)
                    low_keep[piece, :] = gradient.astype(BF16)

            repeat(FRAME // PIECE, entry_norm)
            if bottom:
                return

            @pl.when(chunk == 0)
            def _():
                load(0).wait()

            low_turned[...] = low_keep[:, pair].T
            second_turned[...] = second_ref[...].T

            def spread(index):
                here = tile(index)
                grad_hidden = nt(low_keep[...], wd[here, :]) * gp_ref[:, here].astype(F32)
                hidden_keep[:, here] = grad_hidden.astype(BF16)
                vec2[0:1, here] += column_sum(grad_hidden)
                down_sum[:, here] += nn(low_turned[...], act_ref[:, here])

            repeat(hidden_units // TILE, spread)

            @pl.when(chunk == 0)
            def _():
                load(1).wait()

            def gather(index):
                here = tile(index)
                b_send[chunk, :, here] = nt(hidden_keep[...], wu[here, :]).astype(BF16)
                wide = hidden_units // (width // TILE)
                some = at(index * wide, wide)
                up_sum[:, some] += nn(second_turned[...], hidden_keep[:, some])

            repeat(width // TILE, gather)
            exchange(1, chunk).start()

        if not bottom:

            @pl.when(step == ahead + 1)
            def _():
                load(2).wait()

            @pl.when(step >= ahead + 1)
            def _():
                chunk = step - ahead - 1
                slot = lax.rem(chunk, 2)
                exchange(1, chunk).wait_recv()

                def middle_norm(index):
                    piece = at(index * PIECE, PIECE)
                    grad_second = b_send[chunk, piece, :].astype(F32) + b_recv[chunk, piece, :].astype(F32)
                    unit, scale = kept_norm(unit2, scale2, piece)
                    vec2[2:3, :width] += column_sum(grad_second * unit)
                    vec2[3:4, :width] += column_sum(grad_second)
                    grad_middle = grad_keep[slot, piece, :] + norm_pull(
                        grad_second, gain2[layer : layer + 1, :], unit, scale
                    )
                    dmid_out[piece, :] = grad_middle
                    vec2[4:5, :width] += column_sum(grad_middle)
                    low_keep[piece, :] = grad_middle.astype(BF16)

                repeat(FRAME // PIECE, middle_norm)
                low_turned[...] = low_keep[:, pair].T

                def one(index):
                    here = tile(index)
                    dmix_out[:, here] = nt(low_keep[...], wo[here, :]).astype(BF16)
                    out_sum[:, here] += nn(low_turned[...], mixed_ref[:, here])

                repeat(mixed_features // TILE, one)

        if bottom:

            def x_copy(index):
                source, target = ((dx_send, dx_recv), (vec1, vec_recv))[index]
                return remote(
                    source, target, x_send_sem.at[index], x_recv_sem.at[index], beside, core
                )

            @pl.when(step == chunks)
            def _():
                dx_send[...] = dx_keep[at(beside * place_rows, place_rows), :].astype(BF16)
                x_copy(0).start()
                x_copy(1).start()
                dx_out[...] = dx_keep[at(me * place_rows, place_rows), :]
                x_copy(0).wait_recv()
                x_copy(1).wait_recv()
                dx_other[...] = dx_recv[...].astype(F32)
                vec_other[...] = vec_recv[...]
                x_copy(0).wait_send()
                x_copy(1).wait_send()

        @pl.when(step == pl.num_programs(0) - 1)
        def _():
            for kind in ([] if top else [0]) + ([] if bottom else [1]):
                for chunk in range(chunks):
                    exchange(kind, chunk).wait_send()
            finish_swap()

    def rows(columns, behind):
        return pl.BlockSpec(
            (FRAME, columns), lambda s: (jnp.clip(s - behind, 0, chunks - 1), 0)
        )

    vec = jax.ShapeDtypeStruct((8, VEC), F32)
    operands, in_specs, out_shape, out_specs, scratch = [], [], [], [], []
    if top:
        operands += list(entry)
        in_specs += [halves_spec(entry[0].shape, chunks, 0, FRAME)]
    else:
        operands += list(entry)
        in_specs += [
            pl.BlockSpec((3, FRAME, features), lambda s: (0, jnp.minimum(s, chunks - 1), 0))
        ]
        in_specs += [rows(width, 1), rows(PAIR, 1), rows(width, 1)]
        in_specs += [
            pl.BlockSpec(
                (1, *entry[4].shape[1:]),
                lambda s: (above, 0, 0, 0),
                pipeline_mode=pl.Buffered(1),
            ),
            whole(entry[5]),
        ]
        narrow = jax.ShapeDtypeStruct((8, features), F32)
        out_shape += [narrow]
        out_specs += [whole_out((8, features))]
        scratch += [pltpu.VMEM((chunks, FRAME, width), BF16)] * 2
    if not bottom:
        operands += list(upper[1:])
        in_specs += [rows(hidden_units, ahead)] * 2
        in_specs += [rows(width, ahead + 1), rows(PAIR, ahead + 1), rows(PAIR, ahead)]
        in_specs += [rows(mixed_features, ahead + 1)] + [ANYWHERE] * 3 + [whole(upper[10])]
        sums = [mixed_features, hidden_units, hidden_units]
        out_shape += [
            jax.ShapeDtypeStruct((total, width), F32),
            jax.ShapeDtypeStruct((total, mixed_features), BF16),
        ]
        out_shape += [jax.ShapeDtypeStruct((PAIR, size), F32) for size in sums] + [vec]
        out_specs += [rows(width, ahead + 1), rows(mixed_features, ahead + 1)]
        out_specs += [whole_out((PAIR, size)) for size in sums] + [whole_out((8, VEC))]
        scratch += [pltpu.VMEM((chunks, FRAME, width), BF16)] * 2
        scratch += [
            pltpu.VMEM((2, FRAME, width), F32),
            pltpu.VMEM((FRAME, hidden_units), BF16),
            pltpu.VMEM((FRAME, width), BF16),
            pltpu.VMEM((PAIR, FRAME), BF16),
            pltpu.VMEM((PAIR, FRAME), BF16),
            pltpu.VMEM(upper[7].shape[1:], BF16),
            pltpu.VMEM(upper[8].shape[1:], BF16),
            pltpu.VMEM(upper[9].shape[1:], BF16),
            pltpu.SemaphoreType.DMA((3,)),
        ]
    else:
        out_shape += [
            jax.ShapeDtypeStruct((place_rows, width), F32),
            jax.ShapeDtypeStruct((place_rows, width), F32),
            narrow,
        ]
        out_specs += [whole_out((place_rows, width))] * 2 + [whole_out((8, features))]
        scratch += [
            pltpu.VMEM((total, width), F32),
            pltpu.VMEM((place_rows, width), BF16),
            pltpu.VMEM((place_rows, width), BF16),
            pltpu.VMEM((8, features), F32),
            pltpu.SemaphoreType.DMA((2,)),
            pltpu.SemaphoreType.DMA((2,)),
        ]
    scratch += [pltpu.SemaphoreType.DMA((2, chunks))] * 2
    operands += swap.operands()
    in_specs += swap.in_specs()
    shapes, specs = swap.outputs()
    out_shape += shapes
    out_specs += specs
    scratch += swap.scratch()
    return pl.pallas_call(
        kernel,
        grid=(chunks + (1 if top or bottom else 2),),
        out_shape=out_shape,
        in_specs=in_specs,
        out_specs=out_specs,
        scratch_shapes=scratch,
        compiler_params=pltpu.CompilerParams(
            collective_id=identity, has_side_effects=True, vmem_limit_bytes=VMEM_BYTES
        ),
        name=f"rows_backward_{identity}",
    )(*operands)


def assemble(sums, vecs, lanes, n, features, hidden_units):
    place = lanes[1].shape[0]
    width = lanes[1].shape[1]
    half = PAIR // 2

    def kernel(*refs):
        refs = list(refs)

        def take(count):
            taken = refs[:count]
            del refs[:count]
            return taken

        qkvs, outs, ups, downs = take(LAYERS), take(LAYERS), take(LAYERS), take(LAYERS)
        vec_refs = [take(4) for _ in range(LAYERS)]
        out_lane, out_other, dx_own, dx_other = take(4)
        out_ref, dx_ref, gain1, shift1, g_qkv, b_qkv, g_out, b_out = take(8)
        gain2, shift2, g_up, b_up, g_down, b_down = take(6)
        out_own, sem = refs
        me = lax.axis_index("seq")
        x = lax.rem(me, 2)
        fetch = pltpu.make_async_copy(out_lane.at[at(me * place, place), :], out_own, sem)
        fetch.start()

        for layer in range(LAYERS):
            for part in range(3):
                g_qkv[layer, part] = qkvs[layer][:, part * features : (part + 1) * features]
            for ref, target in ((outs, g_out), (ups, g_up), (downs, g_down)):

                def one(index):
                    columns = at(index * 4 * PAIR, 4 * PAIR)
                    target[layer, :, columns] = ref[layer][:, columns]

                repeat(target.shape[2] // (4 * PAIR), one)

        for layer, (entry_own, entry_other, upper_own, upper_other) in enumerate(vec_refs):
            line = slice(layer, layer + 1)
            for part in range(3):
                row = slice(part, part + 1)
                b_qkv[part, line, :] = entry_own[row, :] + entry_other[row, :]
            b_up[line, :] = upper_own[0:1, :hidden_units] + upper_other[0:1, :hidden_units]

            def owned(mine, other, row):
                wide = mine.shape[1]
                place = (me // 2) * PAIR
                pair = at(lax.rem(place, wide), PAIR)
                both = mine[row : row + 1, pair] + other[row : row + 1, pair]
                for later in range(1, width // wide):
                    line = slice(row + later, row + later + 1)
                    both = jnp.where(place // wide == later, mine[line, pair] + other[line, pair], both)
                return jnp.where(x == 0, both[:, :half], both[:, half:])

            gain1[line, :] = owned(entry_own, entry_other, 3)
            shift1[line, :] = owned(entry_own, entry_other, 5)
            b_down[line, :] = owned(upper_own, upper_other, 1)
            gain2[line, :] = owned(upper_own, upper_other, 2)
            shift2[line, :] = owned(upper_own, upper_other, 3)
            b_out[line, :] = owned(upper_own, upper_other, 4)

        def both_lanes(target, mine, other):
            target[:, 0, :] = jnp.where(x == 0, mine, other)
            target[:, 1, :] = jnp.where(x == 0, other, mine)

        both_lanes(dx_ref, dx_own[...], dx_other[...])
        fetch.wait()
        both_lanes(out_ref, out_own[...], out_other[...])

    def f32(*shape):
        return jax.ShapeDtypeStruct(shape, F32)

    in_vmem = pl.BlockSpec(memory_space=pltpu.VMEM)
    flat = []
    for kind in range(4):
        flat += [sums[layer][kind] for layer in range(LAYERS)]
    for layer in range(LAYERS):
        flat += list(vecs[layer])
    flat += list(lanes)
    small = f32(LAYERS, width // n)
    return pl.pallas_call(
        kernel,
        out_shape=(
            f32(place, 2, width),
            f32(place, 2, width),
            small,
            small,
            f32(LAYERS, 3, half, features),
            f32(3, LAYERS, features),
            f32(LAYERS, half, features),
            small,
            small,
            small,
            f32(LAYERS, half, hidden_units),
            f32(LAYERS, hidden_units),
            f32(LAYERS, half, hidden_units),
            small,
        ),
        in_specs=[in_vmem] * (len(flat) - 4) + [ANYWHERE] + [in_vmem] * 3,
        out_specs=(in_vmem,) * 14,
        scratch_shapes=[pltpu.VMEM((place, width), F32), pltpu.SemaphoreType.DMA],
        compiler_params=pltpu.CompilerParams(vmem_limit_bytes=VMEM_BYTES),
        name="assemble",
    )(*flat)


def per_chip(
    tokens,
    d_out,
    norm1_gain,
    norm1_shift,
    w_qkv,
    b_qkv,
    w_out,
    b_out,
    norm2_gain,
    norm2_shift,
    w_up,
    b_up,
    w_down,
    b_down,
    episode_frames,
    live,
):
    n = lax.axis_size("seq")
    rows = tokens.shape[0]
    features = w_qkv.shape[3]
    fixed, ahead = turn_constants(rows * n // FRAME)
    qkv, qkv_bias = w_qkv.transpose(0, 2, 1, 3), b_qkv.transpose(1, 0, 2)

    gathered, key_bias, frames, *projected = gather_and_project(
        tokens, live.T, episode_frames, norm1_gain, norm1_shift, qkv, qkv_bias, fixed, ahead, n
    )
    streams, kept, d_lane = [gathered], [], None
    for layer in range(LAYERS):
        following = None
        if layer + 1 < LAYERS:
            following = (qkv, norm1_gain, norm1_shift, qkv_bias, fixed, frames)
        results = layer_forward(
            layer,
            projected[0],
            key_bias,
            streams[layer],
            (w_out, w_up, w_down),
            (b_out, norm2_gain, norm2_shift, b_up, b_down),
            following,
            d_out if layer == 0 else None,
            n,
            1 + layer,
        )
        kept.append((*projected, *results[:8]))
        streams.append(results[8])
        if following is not None:
            projected = results[9:13]
        if layer == 0:
            d_lane = results[-1]

    sums = [[None] * 4 for _ in range(LAYERS)]
    vecs = [[None] * 4 for _ in range(LAYERS)]
    entry, later = (d_lane,), None
    for layer in reversed(range(LAYERS)):
        turned, first, unit1, scale1, probs, divisor, mixed = kept[layer][:7]
        unit2, scale2, second, act, slope = kept[layer][7:]
        upper = (
            layer,
            act,
            slope,
            unit2,
            scale2,
            second,
            mixed,
            w_out,
            w_up,
            w_down,
            norm2_gain,
        )
        identity = 1 + LAYERS + 2 * (LAYERS - 1 - layer)
        if later is None:
            results = rows_backward(entry, upper, identity, Swap([], []))
        else:
            swap = Swap(later[:2], [(later[2], 0), (streams[LAYERS], rows)])
            vec1, *results = rows_backward(entry, upper, identity, swap)
            results, swapped = results[:6], results[6:]
            sums[layer + 1][3], sums[layer + 1][0] = swapped[:2]
            vecs[layer + 1][3], out_other = swapped[2:]
            vecs[layer + 1][0] = vec1
        grad_middle, grad_mixed, out_sum, up_sum, down_sum, vec2 = results
        vecs[layer][2] = vec2
        last = layer == 0
        if last:
            swap = Swap([out_sum, up_sum, down_sum], [(vec2, 0), (vecs[layer + 1][0], 0)])
        else:
            swap = Swap([out_sum, up_sum], [])
        results = attention_backward(
            probs,
            divisor,
            mixed,
            turned,
            grad_mixed,
            first,
            fixed,
            frames,
            swap,
            last,
            identity + 1,
        )
        grad_qkv, qkv_sum = results[:2]
        if last:
            sums[layer] = [qkv_sum, *results[2:5]]
            vecs[layer][3], vecs[layer + 1][1] = results[5:7]
        else:
            sums[layer][1:3] = results[2:4]
            later = [down_sum, qkv_sum, vec2]
        entry = (
            layer,
            grad_qkv,
            unit1,
            scale1,
            grad_middle,
            qkv,
            norm1_gain,
        )
    vec1, dx_own, dx_other, vec_other = rows_backward(entry, None, 1 + 3 * LAYERS, Swap([], []))
    vecs[0][:2] = [vec1, vec_other]
    results = list(
        assemble(
            sums,
            vecs,
            (streams[LAYERS], out_other, dx_own, dx_other),
            n,
            features,
            w_up.shape[2],
        )
    )
    results[4] = results[4].transpose(0, 2, 1, 3)
    results[5] = results[5].transpose(1, 0, 2)
    results[6] = results[6].transpose(0, 2, 1)
    results[12] = results[12].transpose(0, 2, 1)
    return tuple(results)


def lane_fits(mesh, tokens):
    n = mesh.shape["seq"]
    positions, lanes, width = tokens.shape
    rows = positions // n
    return (
        lanes == 2
        and n % 4 == 0
        and positions <= 4 * FRAME
        and positions % FRAME == 0
        and FRAME % rows == 0
        and width // n * 2 == PAIR
        and mesh.shape["tp"] == 2
    )


def solution(mesh):
    placed = (
        P("seq", None, None),
        P("seq", None, None),
        P(),
        P(),
        P(None, None, None, "tp"),
        P(None, None, "tp"),
        P(None, "tp", None),
        P(),
        P(),
        P(),
        P(None, None, "tp"),
        P(None, "tp"),
        P(None, "tp", None),
        P(),
        P(),
        P("seq", None),
    )
    def mapped(body):
        return jax.shard_map(
            body,
            mesh=mesh,
            in_specs=placed,
            out_specs=(
                P("seq", None, None),
                P("seq", None, None),
                P(None, "seq"),
                P(None, "seq"),
                P(None, "seq", None, "tp"),
                P(None, None, "tp"),
                P(None, "tp", "seq"),
                P(None, "seq"),
                P(None, "seq"),
                P(None, "seq"),
                P(None, "seq", "tp"),
                P(None, "tp"),
                P(None, "tp", "seq"),
                P(None, "seq"),
            ),
            check_vma=False,
        )

    def run(tokens, *others):
        if lane_fits(mesh, tokens):
            return mapped(per_chip)(tokens, *others)
        return mapped(per_device)(tokens, *others)

    return run
```

```python
import math

import jax
import jax.numpy as jnp
import numpy as np
from jax import lax
from jax.experimental import pallas as pl
from jax.experimental.pallas import tpu as pltpu
from jax.sharding import PartitionSpec as P

HEAD_DIM = 64
GRID = 16
FRAME = 256
LAYERS = 2
MICRO = 2


EPSILON = 1e-06
MASKED = -1e30
SCORE_SCALE = 0.125


def layer_norm(stream, norm_gain, norm_shift):
    center = stream - jnp.mean(stream, axis=-1, keepdims=True)
    spread = jnp.mean(center * center, axis=-1, keepdims=True)
    return center * lax.rsqrt(spread + EPSILON) * norm_gain + norm_shift


def rotate(values, frame_place, row_place, column_place):
    frequency = jnp.exp(jnp.arange(10, dtype=jnp.float32) * (-math.log(10000.0) / 10.0))
    pieces = []
    for section, place in enumerate((frame_place, row_place, column_place)):
        lower = values[..., 20 * section : 20 * section + 10]
        upper = values[..., 20 * section + 10 : 20 * section + 20]
        angles = place.astype(jnp.float32)[..., None, None] * frequency
        cosine = jnp.cos(angles)
        sine_part = jnp.sin(angles)
        pieces.append(lower * cosine - upper * sine_part)
        pieces.append(lower * sine_part + upper * cosine)
    pieces.append(values[..., 60:])
    return jnp.concatenate(pieces, axis=-1)


def episode_tags(frame_counts, positions):
    endings = jnp.cumsum(frame_counts) * FRAME
    passed = (positions[:, None] >= endings[None, :]).astype(jnp.int32)
    episode = jnp.sum(passed, axis=1)
    opening = jnp.sum(passed * frame_counts[None, :], axis=1)
    frame_index = positions // FRAME - opening
    within = positions % FRAME
    return (episode, frame_index, within // GRID, within % GRID)


def gelu_exact(values):
    return jax.nn.gelu(values, approximate=False)


def sum_heads(partial_sum):
    return lax.psum(partial_sum.astype(jnp.bfloat16), "tp").astype(jnp.float32)


def sum_inputs(partial_sum):
    return lax.psum(partial_sum.astype(jnp.bfloat16), "tp").astype(jnp.float32)


def lane_scores(query, keys_all, lane_index, query_tags, key_tags):
    head_count = query.shape[2] // HEAD_DIM
    query_lane = lax.dynamic_index_in_dim(query, lane_index, 1, False).reshape(
        query.shape[0], head_count, HEAD_DIM
    )
    keys_lane = lax.dynamic_index_in_dim(keys_all, lane_index, 1, False).reshape(
        keys_all.shape[0], head_count, HEAD_DIM
    )
    query_episode, query_frame = [
        lax.dynamic_index_in_dim(item, lane_index, 1, False) for item in query_tags
    ]
    key_episode, key_frame, key_live = [
        lax.dynamic_index_in_dim(item, lane_index, 1, False) for item in key_tags
    ]
    allowed = (
        (query_episode[:, None] == key_episode[None, :])
        & (key_frame[None, :] <= query_frame[:, None])
        & (key_live[None, :] > 0)
    )
    scores = (
        jnp.einsum("qhd,khd->hqk", query_lane, keys_lane, preferred_element_type=jnp.float32)
        * SCORE_SCALE
    )
    return (jnp.where(allowed[None], scores, MASKED), query_lane, keys_lane)


def attend_forward(query, keys_all, values_all, query_tags, key_tags):
    rows_dev, lane_count, features = query.shape
    head_count = features // HEAD_DIM

    def one_lane(lane_index, carry):
        scores, query_lane, keys_lane = lane_scores(
            query, keys_all, lane_index, query_tags, key_tags
        )
        highest = jnp.max(scores, axis=-1, keepdims=True)
        shifted = jnp.exp(scores - highest)
        summed = jnp.sum(shifted, axis=-1, keepdims=True)
        attention = (shifted / summed).astype(jnp.bfloat16)
        values_lane = lax.dynamic_index_in_dim(values_all, lane_index, 1, False).reshape(
            values_all.shape[0], head_count, HEAD_DIM
        )
        result = jnp.einsum(
            "hqk,khd->qhd", attention, values_lane, preferred_element_type=jnp.float32
        ).reshape(rows_dev, 1, features)
        log_total = (highest + jnp.log(summed))[None, :, :, 0]
        return (result, log_total)

    initial = (
        jnp.zeros((rows_dev, lane_count, features), jnp.float32),
        jnp.zeros((lane_count, head_count, rows_dev), jnp.float32),
    )
    return lax.fori_loop(0, lane_count, one_lane, initial)


def attend_backward(query, keys_all, values_all, log_total, grad_mixed, query_tags, key_tags):
    rows_dev, lane_count, features = query.shape
    head_count = features // HEAD_DIM
    key_rows = keys_all.shape[0]

    def one_lane(lane_index, carry):
        scores, query_lane, keys_lane = lane_scores(
            query, keys_all, lane_index, query_tags, key_tags
        )
        values_lane = lax.dynamic_index_in_dim(values_all, lane_index, 1, False).reshape(
            key_rows, head_count, HEAD_DIM
        )
        grad_lane = lax.dynamic_index_in_dim(grad_mixed, lane_index, 1, False).reshape(
            rows_dev, head_count, HEAD_DIM
        )
        attention = jnp.exp(
            scores - lax.dynamic_index_in_dim(log_total, lane_index, 0, False)[:, :, None]
        )
        grad_attention = jnp.einsum(
            "qhd,khd->hqk", grad_lane, values_lane, preferred_element_type=jnp.float32
        )
        inner = jnp.sum(attention * grad_attention, axis=-1, keepdims=True)
        grad_scores = (attention * (grad_attention - inner)).astype(jnp.bfloat16)
        query_part = (
            jnp.einsum("hqk,khd->qhd", grad_scores, keys_lane, preferred_element_type=jnp.float32)
            * SCORE_SCALE
        )
        key_part = (
            jnp.einsum("hqk,qhd->khd", grad_scores, query_lane, preferred_element_type=jnp.float32)
            * SCORE_SCALE
        )
        value_part = jnp.einsum(
            "hqk,qhd->khd",
            attention.astype(jnp.bfloat16),
            grad_lane,
            preferred_element_type=jnp.float32,
        )
        stacked = jnp.stack(
            [key_part.reshape(key_rows, features), value_part.reshape(key_rows, features)], axis=1
        )
        key_terms = stacked[:, None]
        grad_query = query_part.reshape(rows_dev, 1, features)
        return (grad_query, key_terms)

    initial = (
        jnp.zeros((rows_dev, lane_count, features), jnp.float32),
        jnp.zeros((key_rows, lane_count, 2, features), jnp.float32),
    )
    return lax.fori_loop(0, lane_count, one_lane, initial)


def front(stream, layer_index, params, query_tags, key_tags, positions):
    (
        gain_one,
        shift_one,
        mat_qkv,
        bias_qkv,
        mat_out,
        bias_out,
        gain_two,
        shift_two,
        mat_up,
        bias_up,
        mat_down,
        bias_down,
    ) = [item[layer_index] for item in params]
    rows_dev, lane_count, width = stream.shape
    features = mat_qkv.shape[2]
    head_count = features // HEAD_DIM
    frame_place, row_place, column_place = positions
    first = layer_norm(stream, gain_one, shift_one).astype(jnp.bfloat16)
    projected = (
        jnp.einsum("tbd,dcf->tbcf", first, mat_qkv, preferred_element_type=jnp.float32) + bias_qkv
    )
    split = projected.reshape(rows_dev, lane_count, 3, head_count, HEAD_DIM)
    query = (
        rotate(split[:, :, 0], frame_place, row_place, column_place)
        .reshape(rows_dev, lane_count, features)
        .astype(jnp.bfloat16)
    )
    keys = (
        rotate(split[:, :, 1], frame_place, row_place, column_place)
        .reshape(rows_dev, lane_count, features)
        .astype(jnp.bfloat16)
    )
    values = projected[:, :, 2].astype(jnp.bfloat16)
    keys_all, values_all = (
        lax.all_gather(keys, "seq", axis=0, tiled=True),
        lax.all_gather(values, "seq", axis=0, tiled=True),
    )
    mixed_full, log_total = attend_forward(query, keys_all, values_all, query_tags, key_tags)
    mixed = mixed_full.astype(jnp.bfloat16)
    middle = (
        stream
        + sum_heads(jnp.einsum("tbf,fd->tbd", mixed, mat_out, preferred_element_type=jnp.float32))
        + bias_out
    )
    second = layer_norm(middle, gain_two, shift_two).astype(jnp.bfloat16)
    hidden = jnp.einsum("tbd,df->tbf", second, mat_up, preferred_element_type=jnp.float32) + bias_up
    activation = gelu_exact(hidden).astype(jnp.bfloat16)
    return (
        first,
        query,
        keys_all,
        values_all,
        log_total,
        mixed,
        middle,
        second,
        hidden,
        activation,
        mixed_full,
    )


def layer_backward(stream, gradient, layer_index, params, query_tags, key_tags, positions):
    (
        gain_one,
        shift_one,
        mat_qkv,
        bias_qkv,
        mat_out,
        bias_out,
        gain_two,
        shift_two,
        mat_up,
        bias_up,
        mat_down,
        bias_down,
    ) = [item[layer_index] for item in params]
    (
        first,
        query,
        keys_all,
        values_all,
        log_total,
        mixed,
        middle,
        second,
        hidden,
        activation,
        mixed_full,
    ) = front(stream, layer_index, params, query_tags, key_tags, positions)
    frame_place, row_place, column_place = positions
    rows_dev, lane_count, width = stream.shape
    features = query.shape[2]
    head_count = features // HEAD_DIM
    grad_low = gradient.astype(jnp.bfloat16)
    grad_w_down = jnp.einsum(
        "tbf,tbd->fd", activation, grad_low, preferred_element_type=jnp.float32
    )
    grad_b_down = jnp.sum(gradient, axis=(0, 1))
    grad_activation = jnp.einsum(
        "tbd,fd->tbf", grad_low, mat_down, preferred_element_type=jnp.float32
    )
    grad_hidden = jax.vjp(gelu_exact, hidden)[1](grad_activation)[0].astype(jnp.bfloat16)
    grad_b_up = jnp.sum(grad_hidden.astype(jnp.float32), axis=(0, 1))
    grad_w_up = jnp.einsum("tbd,tbf->df", second, grad_hidden, preferred_element_type=jnp.float32)
    grad_second = sum_inputs(
        jnp.einsum("tbf,df->tbd", grad_hidden, mat_up, preferred_element_type=jnp.float32)
    )
    middle_pull = jax.vjp(layer_norm, middle, gain_two, shift_two)[1]
    grad_inner, grad_gain_two, grad_shift_two = middle_pull(grad_second)
    grad_middle = gradient + grad_inner
    grad_b_out = jnp.sum(grad_middle, axis=(0, 1))
    middle_low = grad_middle.astype(jnp.bfloat16)
    grad_w_out = jnp.einsum("tbf,tbd->fd", mixed, middle_low, preferred_element_type=jnp.float32)
    grad_mixed = jnp.einsum(
        "tbd,fd->tbf", middle_low, mat_out, preferred_element_type=jnp.float32
    ).astype(jnp.bfloat16)
    grad_query, key_terms = attend_backward(
        query, keys_all, values_all, log_total, grad_mixed, query_tags, key_tags
    )
    returned = lax.psum_scatter(key_terms, "seq", scatter_dimension=0, tiled=True)
    turned_query = rotate(
        grad_query.reshape(rows_dev, lane_count, head_count, HEAD_DIM),
        -frame_place,
        -row_place,
        -column_place,
    )
    turned_keys = rotate(
        returned[:, :, 0].reshape(rows_dev, lane_count, head_count, HEAD_DIM),
        -frame_place,
        -row_place,
        -column_place,
    )
    grad_projected = jnp.stack(
        [
            turned_query.reshape(rows_dev, lane_count, features),
            turned_keys.reshape(rows_dev, lane_count, features),
            returned[:, :, 1],
        ],
        axis=2,
    ).astype(jnp.bfloat16)
    grad_b_qkv = jnp.sum(grad_projected.astype(jnp.float32), axis=(0, 1))
    grad_w_qkv = jnp.einsum(
        "tbd,tbcf->dcf", first, grad_projected, preferred_element_type=jnp.float32
    )
    grad_first = sum_inputs(
        jnp.einsum("tbcf,dcf->tbd", grad_projected, mat_qkv, preferred_element_type=jnp.float32)
    )
    first_pull = jax.vjp(layer_norm, stream, gain_one, shift_one)[1]
    grad_entry, grad_gain_one, grad_shift_one = first_pull(grad_first)
    grads = (
        grad_gain_one,
        grad_shift_one,
        grad_w_qkv,
        grad_b_qkv,
        grad_w_out,
        grad_b_out,
        grad_gain_two,
        grad_shift_two,
        grad_w_up,
        grad_b_up,
        grad_w_down,
        grad_b_down,
    )
    return (grad_middle + grad_entry, grads)


def per_device(
    tokens,
    d_out,
    norm1_gain,
    norm1_shift,
    w_qkv,
    b_qkv,
    w_out,
    b_out,
    norm2_gain,
    norm2_shift,
    w_up,
    b_up,
    w_down,
    b_down,
    episode_frames,
    live,
):
    rows_dev = tokens.shape[0]
    lane_count = tokens.shape[1] // MICRO
    total_rows = rows_dev * lax.axis_size("seq")
    local_positions = lax.axis_index("seq") * rows_dev + jnp.arange(rows_dev, dtype=jnp.int32)
    key_positions = jnp.arange(total_rows, dtype=jnp.int32)
    tagger = jax.vmap(episode_tags, in_axes=(0, None), out_axes=1)
    query_episode, query_frame, query_row, query_column = tagger(episode_frames, local_positions)
    key_episode, key_frame, key_row, key_column = tagger(episode_frames, key_positions)
    live_keys = lax.all_gather(live, "seq", axis=0, tiled=True)
    params = (
        norm1_gain,
        norm1_shift,
        w_qkv,
        b_qkv,
        w_out,
        b_out,
        norm2_gain,
        norm2_shift,
        w_up,
        b_up,
        w_down,
        b_down,
    )
    layer_grads = [None] * LAYERS
    outputs = []
    grad_tokens = []
    for micro_index in range(MICRO):
        first_lane = micro_index * lane_count
        last_lane = first_lane + lane_count
        query_tags = (query_episode[:, first_lane:last_lane], query_frame[:, first_lane:last_lane])
        key_tags = (
            key_episode[:, first_lane:last_lane],
            key_frame[:, first_lane:last_lane],
            live_keys[:, first_lane:last_lane],
        )
        positions = (
            query_frame[:, first_lane:last_lane],
            query_row[:, first_lane:last_lane],
            query_column[:, first_lane:last_lane],
        )
        stream = tokens[:, first_lane:last_lane].astype(jnp.float32)
        inputs = []
        gathered = []
        for layer_index in range(LAYERS):
            inputs.append(stream)
            layer_state = front(stream, layer_index, params, query_tags, key_tags, positions)
            gathered.append((layer_state[2], layer_state[3]))
            branch = jnp.einsum(
                "tbf,fd->tbd",
                layer_state[9],
                w_down[layer_index],
                preferred_element_type=jnp.float32,
            )
            stream = layer_state[6] + sum_heads(branch) + b_down[layer_index]
        outputs.append(stream)
        gradient = d_out[:, first_lane:last_lane]
        for layer_index in reversed(range(LAYERS)):
            gradient, grads = layer_backward(
                inputs[layer_index], gradient, layer_index, params, query_tags, key_tags, positions
            )
            if layer_grads[layer_index] is None:
                layer_grads[layer_index] = grads
            else:
                layer_grads[layer_index] = jax.tree.map(jnp.add, layer_grads[layer_index], grads)
        grad_tokens.append(gradient)
    stacked = [
        jnp.stack([layer_grads[layer_index][entry] for layer_index in range(LAYERS)])
        for entry in range(12)
    ]
    (
        grad_gain_one,
        grad_shift_one,
        grad_w_qkv,
        grad_b_qkv,
        grad_w_out,
        grad_b_out,
        grad_gain_two,
        grad_shift_two,
        grad_w_up,
        grad_b_up,
        grad_w_down,
        grad_b_down,
    ) = stacked
    in_sums = (
        lax.psum_scatter(grad_w_qkv, "seq", scatter_dimension=1, tiled=True),
        lax.psum_scatter(grad_w_up, "seq", scatter_dimension=1, tiled=True),
        lax.psum_scatter(grad_gain_one, "seq", scatter_dimension=1, tiled=True),
        lax.psum_scatter(grad_shift_one, "seq", scatter_dimension=1, tiled=True),
        lax.psum_scatter(grad_gain_two, "seq", scatter_dimension=1, tiled=True),
        lax.psum_scatter(grad_shift_two, "seq", scatter_dimension=1, tiled=True),
        lax.psum_scatter(grad_b_out, "seq", scatter_dimension=1, tiled=True),
        lax.psum_scatter(grad_b_down, "seq", scatter_dimension=1, tiled=True),
    )
    out_sums = (
        lax.psum_scatter(grad_w_out, "seq", scatter_dimension=2, tiled=True),
        lax.psum_scatter(grad_w_down, "seq", scatter_dimension=2, tiled=True),
    )
    bias_total = lax.psum((grad_b_qkv, grad_b_up), "seq")
    return (
        jnp.concatenate(outputs, axis=1),
        jnp.concatenate(grad_tokens, axis=1),
        in_sums[2],
        in_sums[3],
        in_sums[0],
        bias_total[0],
        out_sums[0],
        in_sums[6],
        in_sums[4],
        in_sums[5],
        in_sums[1],
        bias_total[1],
        out_sums[1],
        in_sums[7],
    )


MESH = pl.DeviceIdType.MESH
BF16 = jnp.bfloat16
F32 = jnp.float32
VMEM_BYTES = 60 * 1024 * 1024
PAIR = 128
VEC = 2048


def nn(left, right):
    return lax.dot_general(left, right, (((1,), (0,)), ((), ())), preferred_element_type=F32)


def nt(left, right):
    return lax.dot_general(left, right, (((1,), (1,)), ((), ())), preferred_element_type=F32)


def tn(left, right):
    return lax.dot_general(left, right, (((0,), (0,)), ((), ())), preferred_element_type=F32)


def at(start, size):
    return pl.ds(pl.multiple_of(start, size), size)


def remote(src, dst, send, recv, seq, tp):
    return pltpu.make_async_remote_copy(
        src_ref=src,
        dst_ref=dst,
        send_sem=send,
        recv_sem=recv,
        device_id=(seq, tp),
        device_id_type=MESH,
    )


def hello(partners):
    barrier = pltpu.get_barrier_semaphore()
    for seq, tp in partners:
        pl.semaphore_signal(barrier, inc=1, device_id=(seq, tp), device_id_type=MESH)


def met(partners):
    pl.semaphore_wait(pltpu.get_barrier_semaphore(), len(partners))


def whole(array):
    zeros = (0,) * array.ndim
    return pl.BlockSpec(array.shape, lambda s: zeros, pipeline_mode=pl.Buffered(1))


def whole_out(shape):
    zeros = (0,) * len(shape)
    return pl.BlockSpec(shape, lambda s: zeros)


ANYWHERE = pl.BlockSpec(memory_space=pl.ANY)


def turn_row(table, place, section):
    frequency = np.exp(np.arange(10, dtype=np.float32) * np.float32(-math.log(10000.0) / 10.0))
    angle = place.astype(np.float32)[:, None] * frequency
    for base in range(20 * section, PAIR, HEAD_DIM):
        table[0, :, base : base + 10] = np.cos(angle)
        table[0, :, base + 10 : base + 20] = np.cos(angle)
        table[1, :, base : base + 10] = -np.sin(angle)
        table[2, :, base + 10 : base + 20] = np.sin(angle)


def turn_constants(frames):
    within, ahead = np.zeros((3, FRAME, PAIR), np.float32), np.zeros((3, frames, PAIR), np.float32)
    turn_row(within, np.arange(FRAME) // GRID, 1)
    turn_row(within, np.arange(FRAME) % GRID, 2)
    for base in range(60, PAIR, HEAD_DIM):
        within[0, :, base : base + 4] = 1.0
    turn_row(ahead, np.arange(frames), 0)
    return jnp.asarray(within), jnp.asarray(ahead)


def turn(values, tables, back=False):
    cosine, lower, upper = tables
    pieces = []
    for start in range(0, values.shape[1], PAIR):
        slab = values[:, start : start + PAIR]
        moved = pltpu.roll(slab, PAIR - 10, 1) * lower + pltpu.roll(slab, 10, 1) * upper
        pieces.append(slab * cosine - moved if back else slab * cosine + moved)
    return jnp.concatenate(pieces, axis=1)


def tables_of(fixed_ref, frames_ref, chunk):
    return [fixed_ref[i] + frames_ref[i, pl.ds(chunk, 1), :] for i in range(3)]


def normed(stream):
    center = stream - jnp.mean(stream, axis=-1, keepdims=True)
    spread = jnp.mean(center * center, axis=-1, keepdims=True)
    scale = lax.rsqrt(spread + EPSILON)
    return center * scale, scale


def norm_pull(grad, gain, unit, scale):
    scaled = grad * gain
    return scale * (
        scaled
        - jnp.mean(scaled, axis=-1, keepdims=True)
        - unit * jnp.mean(scaled * unit, axis=-1, keepdims=True)
    )


def keep_norm(unit, scale, unit_ref, scale_ref):
    unit_ref[...] = unit.astype(BF16)
    scale_ref[...] = jnp.broadcast_to(scale, scale_ref.shape)


def kept_norm(unit_ref, scale_ref):
    copies = unit_ref.shape[1] // scale_ref.shape[1]
    return unit_ref[...].astype(F32), jnp.concatenate([scale_ref[...]] * copies, axis=1)


def column_sum(values):
    return jnp.sum(values, axis=0, keepdims=True)


def gelu_both(hidden):
    normal = 0.5 + 0.5 * lax.erf(hidden * math.sqrt(0.5))
    density = jnp.exp(hidden * hidden * -0.5) * (1.0 / math.sqrt(2.0 * math.pi))
    return hidden * normal, normal + hidden * density


def project(stream, chunk, layer, pair, refs, outs, first_full):
    gain, shift, weight, bias, fixed, frames = refs
    query_ref, key_ref, value_ref, first_ref, unit_ref, scale_ref = outs
    unit, scale = normed(stream)
    keep_norm(unit, scale, unit_ref, scale_ref)
    first = (unit * gain[layer : layer + 1, :] + shift[layer : layer + 1, :]).astype(BF16)
    first_full[...] = first
    first_ref[...] = first_full[:, at(pair * PAIR, PAIR)]
    tables = tables_of(fixed, frames, chunk)
    query = nn(first, weight[0]) + bias[0, layer : layer + 1, :]
    query_ref[...] = (turn(query, tables) * SCORE_SCALE).astype(BF16)
    key = nn(first, weight[1]) + bias[1, layer : layer + 1, :]
    key_ref[...] = turn(key, tables).astype(BF16)
    value = nn(first, weight[2]) + bias[2, layer : layer + 1, :]
    value_ref[...] = value.astype(BF16)


class Relay:
    sems = 6

    def __init__(self, n, rows, buffer, other, sems, lives=None, live_other=None):
        self.n, self.rows, self.buffer, self.other = n, rows, buffer, other
        self.lives, self.live_other = lives, live_other
        self.z_send, self.z_recv, self.y_send, self.y_recv, self.c_send, self.c_recv = sems
        self.planes = n // 4
        self.me, self.core = lax.axis_index("seq"), lax.axis_index("tp")
        me = self.me
        self.x, self.y, self.z = lax.rem(me, 2), lax.rem(me // 2, 2), me // 4
        self.across = me + 2 - 4 * self.y

    @staticmethod
    def scratch(n):
        dma, planes = pltpu.SemaphoreType.DMA, n // 4
        shapes = [(planes, 2, 2)] * 2 + [(planes, 2)] * 2 + [(2 * planes,)] * 2
        return [dma(shape) for shape in shapes]

    @property
    def events(self):
        return self.planes

    def plane(self, step):
        return lax.rem(self.z + step, self.planes)

    def place(self, plane, lane):
        return plane * 4 + self.y * 2 + lane

    def reached(self):
        return [(step, far) for step in range(self.planes) for far in (0, 1) if step or far]

    def hello(self):
        barrier = pltpu.get_barrier_semaphore()
        partners = [(self.across, self.core), (self.me, 1 - self.core)]
        for step, far in self.reached():
            lane = 1 - self.x if far else self.x
            partners.append((self.place(self.plane(step), lane), self.core))
        for seq, tp in partners:
            pl.semaphore_signal(barrier, inc=1, device_id=(seq, tp), device_id_type=MESH)

    def met(self):
        pl.semaphore_wait(pltpu.get_barrier_semaphore(), 2 + len(self.reached()))

    def rows_of(self, side, seq):
        return self.buffer.at[side, at(seq * self.rows, self.rows), :]

    def block(self, side, pair):
        return self.buffer.at[side, at(pair * 2 * self.rows, 2 * self.rows), :]

    def items(self, pair):
        found = [self.block(self.core, pair)]
        if self.lives is not None:
            found.append(self.lives.at[at(pair * 2, 2)])
        return found

    def each(self, copy, what):
        for index in range(1 if self.lives is None else 2):
            getattr(copy(index), what)()

    def z_copy(self, step, far):
        def copy(index):
            lane = 1 - self.x if far else self.x
            if index == 0:
                source = self.other.at[self.core] if far else self.rows_of(self.core, self.me)
                target = self.rows_of(self.core, self.me)
            else:
                source = self.live_other if far else self.lives.at[self.me]
                target = self.lives.at[self.me]
            return remote(
                source,
                target,
                self.z_send.at[step, far, index],
                self.z_recv.at[step, far, index],
                self.place(self.plane(step), lane),
                self.core,
            )

        return copy

    def y_copy(self, plane, row):
        def copy(index):
            item = self.items(plane * 2 + row)[index]
            return remote(
                item,
                item,
                self.y_send.at[plane, index],
                self.y_recv.at[plane, index],
                self.across,
                self.core,
            )

        return copy

    def c_copy(self, pair, side):
        item = self.block(side, pair)
        return remote(
            item, item, self.c_send.at[pair], self.c_recv.at[pair], self.me, 1 - self.core
        )

    def begin(self):
        for step, far in self.reached():
            self.each(self.z_copy(step, far), "start")

    def arrive(self, event):
        for far in (0, 1) if event else (1,):
            self.each(self.z_copy(event, far), "wait_recv")
        plane = self.plane(self.planes - event)
        self.each(self.y_copy(plane, self.y), "start")
        self.c_copy(plane * 2 + self.y, self.core).start()

    def complete(self, event):
        plane = self.plane(self.planes - event)
        self.each(self.y_copy(plane, 1 - self.y), "wait_recv")
        self.c_copy(plane * 2 + 1 - self.y, self.core).start()

    def ready(self, event):
        plane = self.plane(self.planes - event)
        self.c_copy(plane * 2, 1 - self.core).wait_recv()
        self.c_copy(plane * 2 + 1, 1 - self.core).wait_recv()
        return plane

    def finish(self):
        for step, far in self.reached():
            self.each(self.z_copy(step, far), "wait_send")
        for plane in range(self.planes):
            self.each(self.y_copy(plane, self.y), "wait_send")
        for pair in range(2 * self.planes):
            self.c_copy(pair, self.core).wait_send()


def split_lanes(values, x, buffer, other, start, rows):
    half = values.shape[2] // 2
    zero, one = values[:, 0, :], values[:, 1, :]
    own, far = jnp.where(x == 0, zero, one), jnp.where(x == 0, one, zero)
    core = lax.axis_index("tp")
    own = jnp.where(core == 0, own[:, :half], own[:, half:]).astype(BF16)
    buffer[core, at(start, rows), :] = own
    for side in range(2):
        other[side] = far[:, side * half : (side + 1) * half].astype(BF16)


def gather_and_project(tokens, live, episode_frames, gain, shift, qkv, bias, fixed, ahead, n):
    rows, lanes, width = tokens.shape
    half = width // 2
    total = n * rows
    chunks = total // FRAME
    per_frame = FRAME // rows
    features = qkv.shape[3]
    slots = episode_frames.shape[1]

    def kernel(*refs):
        refs = list(refs)

        def take(count):
            taken = refs[:count]
            del refs[:count]
            return taken

        tokens_ref, live_ref, counts_ref, gain_ref, shift_ref, w_any, bias_ref = take(7)
        fixed_ref, ahead_ref = take(2)
        all_ref, mask_ref, frames_ref = take(3)
        projected = take(6)
        other, lives, live_other, weight, full, w_sem = take(6)
        relay = Relay(n, rows, all_ref, other, take(Relay.sems), lives, live_other)
        load = pltpu.make_async_copy(w_any.at[0], weight, w_sem)
        load.start()
        relay.hello()
        x, me = relay.x, relay.me
        split_lanes(tokens_ref[...].astype(F32), x, all_ref, other, me * rows, rows)
        lane = lax.broadcasted_iota(jnp.int32, (1, FRAME), 1)
        here = lane // rows == lax.rem(me, per_frame)
        tiles = []
        for index in range(lanes):
            alive = live_ref[index : index + 1, :].astype(F32)
            alive = jnp.where(here, jnp.concatenate([alive] * per_frame, axis=1), 0.0)
            tiles.append(jnp.broadcast_to(alive, (8, FRAME)))
        lives[me] = jnp.where(x == 0, tiles[0], tiles[1])
        live_other[...] = jnp.where(x == 0, tiles[1], tiles[0])
        relay.met()
        relay.begin()

        counts = [counts_ref[x, slot] for slot in range(slots)]
        episodes, openings = [], []
        for frame in range(chunks):
            end, episode, opening = 0, 0, 0
            for slot in range(slots):
                end = end + counts[slot]
                passed = frame >= end
                episode = episode + passed.astype(jnp.int32)
                opening = opening + jnp.where(passed, counts[slot], 0)
            episodes.append(episode)
            openings.append(frame - opening)
        for index in range(3):
            table = []
            for frame in range(chunks):
                line = jnp.zeros((1, PAIR), F32)
                for choice in range(chunks):
                    line = jnp.where(
                        openings[frame] == choice, ahead_ref[index, choice : choice + 1, :], line
                    )
                table.append(line)
            frames_ref[index] = jnp.concatenate(
                table + [jnp.zeros((8 - chunks, PAIR), F32)], axis=0
            )
        load.wait()

        def project_frame(frame):
            place = at(frame * FRAME, FRAME)
            stream = jnp.concatenate([all_ref[0, place, :], all_ref[1, place, :]], axis=1)
            project(
                stream.astype(F32),
                frame,
                0,
                me // 2,
                (gain_ref, shift_ref, weight, bias_ref, fixed_ref, frames_ref),
                [ref.at[place, :] for ref in projected],
                full,
            )

        for event in range(relay.events):
            relay.arrive(event)
            if event:
                relay.complete(event - 1)
            if event > 1:
                project_frame(relay.ready(event - 2))
        relay.complete(relay.events - 1)
        for event in range(max(0, relay.events - 2), relay.events):
            project_frame(relay.ready(event))
        relay.finish()

        for key_frame in range(chunks):
            alive = lives[key_frame * per_frame, 0:1, :]
            for part in range(1, per_frame):
                alive = alive + lives[key_frame * per_frame + part, 0:1, :]
            closed = (alive - 1.0) * -MASKED
            lines = []
            for query_frame in range(chunks):
                allowed = (episodes[query_frame] == episodes[key_frame]) & (
                    openings[key_frame] <= openings[query_frame]
                )
                lines.append(jnp.where(allowed, closed, MASKED))
            lines.append(jnp.zeros((PAIR - chunks, FRAME), F32))
            mask_ref[key_frame * FRAME : (key_frame + 1) * FRAME, :] = jnp.concatenate(
                lines, axis=0
            ).T.astype(BF16)

    in_vmem = pl.BlockSpec(memory_space=pltpu.VMEM)
    in_smem = pl.BlockSpec(memory_space=pltpu.SMEM)
    projected = jax.ShapeDtypeStruct((total, features), BF16)
    return pl.pallas_call(
        kernel,
        out_shape=(
            jax.ShapeDtypeStruct((2, total, half), BF16),
            jax.ShapeDtypeStruct((total, PAIR), BF16),
            jax.ShapeDtypeStruct((3, 8, PAIR), F32),
            projected,
            projected,
            projected,
            jax.ShapeDtypeStruct((total, PAIR), BF16),
            jax.ShapeDtypeStruct((total, width), BF16),
            jax.ShapeDtypeStruct((total, PAIR), F32),
        ),
        in_specs=[in_vmem, in_vmem, in_smem, in_vmem, in_vmem, ANYWHERE] + [in_vmem] * 3,
        out_specs=(in_vmem,) * 9,
        scratch_shapes=[
            pltpu.VMEM((2, rows, half), BF16),
            pltpu.VMEM((n, 8, FRAME), F32),
            pltpu.VMEM((8, FRAME), F32),
            pltpu.VMEM(qkv.shape[1:], BF16),
            pltpu.VMEM((FRAME, width), BF16),
            pltpu.SemaphoreType.DMA,
        ]
        + Relay.scratch(n),
        compiler_params=pltpu.CompilerParams(
            collective_id=0, has_side_effects=True, vmem_limit_bytes=VMEM_BYTES
        ),
        name="gather_and_project",
    )(tokens, live, episode_frames, gain, shift, qkv, bias, fixed, ahead)


def halves(ref):
    return jnp.concatenate([ref[0], ref[1]], axis=1).astype(F32)


def halves_spec(shape, chunks, behind, span=FRAME):
    return pl.BlockSpec(
        (2, span, shape[2]), lambda s: (0, jnp.clip(s - behind, 0, chunks - 1), 0)
    )


def layer_forward(layer, query, key, value, key_bias, stream, mats, rows_of, next_refs, d_out, n, identity):
    total, features = query.shape
    split = stream.ndim == 3
    width = mats[1].shape[1]
    rows_here = total // n
    hidden_units = mats[1].shape[2]
    chunks = total // FRAME
    heads = features // HEAD_DIM
    slabs = features // PAIR
    columns = 256
    last = next_refs is None
    b_out, gain, shift, b_up, b_down = rows_of
    mat_out, mat_up, mat_down = mats

    def kernel(*refs):
        refs = list(refs)

        def take(count):
            taken = refs[:count]
            del refs[:count]
            return taken

        q_ref, k_ref, v_ref, kb_ref, x_ref = take(5)
        wo_any, wu_any, wd_any = take(3)
        bo_ref, gain_ref, shift_ref, bu_ref, bd_ref = take(5)
        if not last:
            wq_any, ngain, nshift, nbias, fixed, frames = take(6)
        if d_out is not None:
            (d_ref,) = take(1)
        p_ref, r_ref, mixed_ref, unit_ref, scale_ref, second_ref, act_ref, gp_ref, x_out = take(9)
        if not last:
            next_outs = take(6)
        if d_out is not None:
            (d_all,) = take(1)
        wo, wu, wd, mid, full, next_full = take(6)
        if not last:
            (wq,) = take(1)
        a_send, a_recv, b_send, b_recv, w_sem, send_sem, recv_sem = take(7)
        relay = None
        if d_out is not None:
            buffer, other, d_sem = take(3)
            relay = Relay(n, rows_here, buffer, other, take(Relay.sems))

        step = pl.program_id(0)
        me, core = lax.axis_index("seq"), lax.axis_index("tp")

        items = [(wo_any, wo), (wu_any, wu), (wd_any, wd)]
        if not last:
            items.append((wq_any, wq))

        def load(index):
            source, target = items[index]
            return pltpu.make_async_copy(
                source.at[layer if index < 3 else layer + 1], target, w_sem.at[index]
            )

        def exchange(kind, chunk):
            source, target = ((a_send, a_recv), (b_send, b_recv))[kind]
            return remote(
                source.at[chunk],
                target.at[chunk],
                send_sem.at[kind, chunk],
                recv_sem.at[kind, chunk],
                me,
                1 - core,
            )

        @pl.when(step == 0)
        def _():
            for index in range(len(items)):
                load(index).start()
            if relay is None:
                hello([(me, 1 - core)])
            else:
                relay.hello()
                split_lanes(d_ref[...], relay.x, buffer, other, me * rows_here, rows_here)

        lane = lax.broadcasted_iota(jnp.int32, (1, PAIR), 1)
        sides = [(lane < HEAD_DIM).astype(F32).astype(BF16), (lane >= HEAD_DIM).astype(F32).astype(BF16)]
        for frame in range(chunks):

            @pl.when(step == frame)
            def _():
                keys = FRAME * (frame + 1)
                mask = kb_ref[:keys, :]
                asked = jnp.broadcast_to((lane == frame).astype(F32), (FRAME, PAIR)).astype(BF16)

                slab_lanes = [slice(slab * PAIR, (slab + 1) * PAIR) for slab in range(slabs)]

                def score(head):
                    lanes, side = slab_lanes[head // 2], head % 2
                    key = jnp.concatenate([k_ref[:keys, lanes], mask], axis=1)
                    return nt(jnp.concatenate([q_ref[:, lanes] * sides[side], asked], axis=1), key)

                scores, sums = score(0), []
                for head in range(heads):
                    lanes, side = slab_lanes[head // 2], head % 2
                    following = score(head + 1) if head + 1 < heads else None
                    highest = jnp.max(scores, axis=1, keepdims=True)
                    shifted = jnp.exp(scores - highest).astype(BF16)
                    p_ref[0, head, :keys, :] = shifted.T
                    sums.append(nn(shifted, v_ref[:keys, lanes] * sides[side] + sides[1 - side]))
                    scores = following
                    if side == 1:
                        one, two = sums[head - 1 :]
                        low_side = lane < HEAD_DIM
                        divisor = 1.0 / jnp.where(
                            low_side, pltpu.roll(one, HEAD_DIM, 1), pltpu.roll(two, HEAD_DIM, 1)
                        )
                        r_ref[:, lanes] = divisor
                        mixed_ref[:, lanes] = (jnp.where(low_side, one, two) * divisor).astype(BF16)

        @pl.when(step == 0)
        def _():
            load(0).wait()
            if relay is None:
                met([(me, 1 - core)])
            else:
                relay.met()
                relay.begin()

        @pl.when(step < chunks)
        def _():
            a_send[step] = nn(mixed_ref[...], wo[...]).astype(BF16)
            exchange(0, step).start()

        if relay is not None:
            for event in range(relay.events):

                @pl.when(step == 2 + event // 2)
                def _():
                    relay.arrive(event)

                @pl.when(step == 3 + event // 2)
                def _():
                    relay.complete(event)

            @pl.when(step == chunks + 1)
            def _():
                for event in range(relay.events):
                    relay.ready(event)
                relay.finish()
                pltpu.make_async_copy(buffer, d_all, d_sem).start()

        def feed_forward():
            chunk = step - 1
            middle = (halves(x_ref) if split else x_ref[...]) + (
                a_send[chunk].astype(F32) + a_recv[chunk].astype(F32)
            )
            middle = middle + bo_ref[layer : layer + 1, :]
            mid[lax.rem(chunk, 2)] = middle
            unit, scale = normed(middle)
            keep_norm(unit, scale, unit_ref, scale_ref)
            second = (unit * gain_ref[layer : layer + 1, :] + shift_ref[layer : layer + 1, :]).astype(BF16)
            full[...] = second
            second_ref[...] = full[:, at((me // 2) * PAIR, PAIR)]
            parts = [slice(start, start + columns) for start in range(0, hidden_units, columns)]
            hidden = nn(second, wu[:, parts[0]])
            for index, part in enumerate(parts):
                following = nn(second, wu[:, parts[index + 1]]) if index + 1 < len(parts) else None
                act, slope = gelu_both(hidden + bu_ref[layer : layer + 1, part])
                act_ref[:, part] = act.astype(BF16)
                gp_ref[:, part] = slope.astype(BF16)
                hidden = following
            b_send[chunk] = nn(act_ref[...], wd[...]).astype(BF16)

        def close():
            chunk = step - 2
            result = mid[lax.rem(chunk, 2)] + (b_send[chunk].astype(F32) + b_recv[chunk].astype(F32))
            result = result + bd_ref[layer : layer + 1, :]
            x_out[...] = result
            if not last:
                project(
                    result,
                    chunk,
                    layer + 1,
                    me // 2,
                    (ngain, nshift, wq, nbias, fixed, frames),
                    next_outs,
                    next_full,
                )

        @pl.when(step == 1)
        def _():
            load(1).wait()
            load(2).wait()

        @pl.when((step >= 1) & (step <= chunks))
        def _():
            exchange(0, step - 1).wait_recv()
            feed_forward()
            exchange(1, step - 1).start()

        if not last:

            @pl.when(step == 2)
            def _():
                load(3).wait()

        @pl.when(step >= 2)
        def _():
            exchange(1, step - 2).wait_recv()
            close()

        @pl.when(step == chunks + 1)
        def _():
            for kind in range(2):
                for chunk in range(chunks):
                    exchange(kind, chunk).wait_send()
            if relay is not None:
                pltpu.make_async_copy(buffer, d_all, d_sem).wait()

    def rows(columns, behind):
        return pl.BlockSpec(
            (FRAME, columns), lambda s: (jnp.clip(s - behind, 0, chunks - 1), 0)
        )

    in_specs = [rows(features, 0), whole(key), whole(value), whole(key_bias)]
    in_specs += [halves_spec(stream.shape, chunks, 1) if split else rows(width, 1)]
    in_specs += [ANYWHERE] * 3 + [whole(item) for item in rows_of]
    operands = [query, key, value, key_bias, stream, *mats, *rows_of]
    if not last:
        in_specs += [ANYWHERE] + [whole(item) for item in next_refs[1:]]
        operands += list(next_refs)
    if d_out is not None:
        in_specs += [whole(d_out)]
        operands += [d_out]
    out_shape = [
        jax.ShapeDtypeStruct((chunks, heads, total, FRAME), BF16),
        jax.ShapeDtypeStruct((total, features), F32),
        jax.ShapeDtypeStruct((total, features), BF16),
        jax.ShapeDtypeStruct((total, width), BF16),
        jax.ShapeDtypeStruct((total, PAIR), F32),
        jax.ShapeDtypeStruct((total, PAIR), BF16),
        jax.ShapeDtypeStruct((total, hidden_units), BF16),
        jax.ShapeDtypeStruct((total, hidden_units), BF16),
        jax.ShapeDtypeStruct((total, width), F32),
    ]
    out_specs = [
        pl.BlockSpec((1, heads, total, FRAME), lambda s: (jnp.minimum(s, chunks - 1), 0, 0, 0)),
        rows(features, 0),
        rows(features, 0),
        rows(width, 1),
        rows(PAIR, 1),
        rows(PAIR, 1),
        rows(hidden_units, 1),
        rows(hidden_units, 1),
        rows(width, 2),
    ]
    scratch = [
        pltpu.VMEM(mat_out.shape[1:], BF16),
        pltpu.VMEM(mat_up.shape[1:], BF16),
        pltpu.VMEM(mat_down.shape[1:], BF16),
        pltpu.VMEM((2, FRAME, width), F32),
        pltpu.VMEM((FRAME, width), BF16),
        pltpu.VMEM((FRAME, width), BF16),
    ]
    if not last:
        out_shape += [jax.ShapeDtypeStruct((total, features), BF16)] * 3
        out_shape += [jax.ShapeDtypeStruct((total, PAIR), BF16)]
        out_shape += [jax.ShapeDtypeStruct((total, width), BF16)]
        out_shape += [jax.ShapeDtypeStruct((total, PAIR), F32)]
        out_specs += [rows(features, 2)] * 3 + [rows(PAIR, 2), rows(width, 2), rows(PAIR, 2)]
    if d_out is not None:
        out_shape += [jax.ShapeDtypeStruct((2, total, width // 2), BF16)]
        out_specs += [ANYWHERE]
        scratch += [pltpu.VMEM(next_refs[0].shape[1:], BF16)]
    scratch += [pltpu.VMEM((chunks, FRAME, width), BF16)] * 4
    scratch += [
        pltpu.SemaphoreType.DMA((4,)),
        pltpu.SemaphoreType.DMA((2, chunks)),
        pltpu.SemaphoreType.DMA((2, chunks)),
    ]
    if d_out is not None:
        scratch += [
            pltpu.VMEM((2, total, width // 2), BF16),
            pltpu.VMEM((2, rows_here, width // 2), BF16),
            pltpu.SemaphoreType.DMA,
        ]
        scratch += Relay.scratch(n)
    return pl.pallas_call(
        kernel,
        grid=(chunks + 2,),
        out_shape=out_shape,
        in_specs=in_specs,
        out_specs=out_specs,
        scratch_shapes=scratch,
        compiler_params=pltpu.CompilerParams(
            collective_id=identity, has_side_effects=True, vmem_limit_bytes=VMEM_BYTES
        ),
        name=f"layer_forward_{layer}",
    )(*operands)


class Swap:
    def __init__(self, ships, lane_rows):
        self.ships, self.lane_rows = ships, lane_rows
        self.count = len(ships) + len(lane_rows)

    def operands(self):
        return [*self.ships, *[item for item, _ in self.lane_rows]]

    def in_specs(self):
        return [whole(item) for item in self.ships] + [ANYWHERE] * len(self.lane_rows)

    def outputs(self):
        shapes, specs = [], []
        for item in self.ships:
            shape = (item.shape[0] // 2, item.shape[1])
            shapes.append(jax.ShapeDtypeStruct(shape, F32))
            specs.append(whole_out(shape))
        for item, count in self.lane_rows:
            shapes.append(jax.ShapeDtypeStruct((count or item.shape[0], item.shape[1]), item.dtype))
            specs.append(ANYWHERE)
        return shapes, specs

    def scratch(self):
        if not self.count:
            return []
        buffers = [pltpu.VMEM((item.shape[0] // 2, item.shape[1]), BF16) for item in self.ships]
        return buffers * 2 + [pltpu.SemaphoreType.DMA((self.count,))] * 2

    def bind(self, sources, targets, scratch):
        ships = len(self.ships)
        me, core = lax.axis_index("seq"), lax.axis_index("tp")
        x = lax.rem(me, 2)
        beside = me + 1 - 2 * x
        half = PAIR // 2

        def copy(index):
            if index < ships:
                source, target = scratch[index], scratch[ships + index]
            else:
                source, target = sources[index], targets[index]
                count = self.lane_rows[index - ships][1]
                if count:
                    source = source.at[at(beside * count, count), :]
            send, recv = scratch[2 * ships].at[index], scratch[2 * ships + 1].at[index]
            return remote(source, target, send, recv, beside, core)

        def start():
            for index in range(self.count):
                if index < ships:
                    scratch[index][...] = sources[index][at((1 - x) * half, half), :].astype(BF16)
                copy(index).start()

        def finish():
            for index in range(self.count):
                copy(index).wait_recv()
                if index < ships:
                    own = sources[index][at(x * half, half), :]
                    targets[index][...] = own + scratch[ships + index][...].astype(F32)
            for index in range(self.count):
                copy(index).wait_send()

        return start, finish


def attention_backward(
    probs, divisor, mixed, query, key, value, grad_mixed, first, fixed, frames, swap, swap_qkv, identity
):
    total, features = query.shape
    chunks = total // FRAME
    slabs = features // PAIR
    half = PAIR // 2

    def kernel(*refs):
        refs = list(refs)

        def take(count):
            taken = refs[:count]
            del refs[:count]
            return taken

        p_ref, r_ref, o_ref, q_ref, k_ref, v_ref, g_ref, first_ref, fixed_ref, frames_ref = take(10)
        sources = take(swap.count)
        dq_ref, dk_ref, dv_ref, qkv_out = take(4)
        targets = take(swap.count)
        dk_sum, dv_sum, first_turned = take(3)
        if swap_qkv:
            qkv_own, qkv_send, qkv_recv, qkv_sems = take(4)
        start, finish = swap.bind(sources, targets, refs)

        step = pl.program_id(0)
        me, core = lax.axis_index("seq"), lax.axis_index("tp")
        x = lax.rem(me, 2)
        beside = me + 1 - 2 * x

        def qkv_copy(slab):
            return remote(
                qkv_send.at[slab],
                qkv_recv.at[slab],
                qkv_sems.at[0, slab],
                qkv_sems.at[1, slab],
                beside,
                core,
            )

        @pl.when(step == 0)
        def _():
            hello([(beside, core)])
            first_turned[...] = first_ref[...].T

        lane = lax.broadcasted_iota(jnp.int32, (1, PAIR), 1)
        sides = [(lane < HEAD_DIM).astype(F32).astype(BF16), (lane >= HEAD_DIM).astype(F32).astype(BF16)]
        turned = k_ref[...].T
        ones = jnp.broadcast_to((lane < 2).astype(F32), (total, PAIR)).astype(BF16)
        values = jnp.concatenate([v_ref[...], ones], axis=1)

        def give(frame):
            keys = FRAME * (frame + 1)
            own = slice(frame * FRAME, keys)
            scaled = (g_ref[own, :].astype(F32) * r_ref[own, :]).astype(BF16)
            inner = scaled.astype(F32) * o_ref[own, :].astype(F32)
            grads, q_parts, g_parts = [], [], []
            for side in range(2):
                delta = jnp.sum(
                    jnp.where((lane < HEAD_DIM) == (side == 0), inner, 0.0), axis=1, keepdims=True
                )
                coarse = delta.astype(BF16).astype(F32)
                rest = jnp.where(lane == 0, -coarse, jnp.where(lane == 1, coarse - delta, 0.0))
                g2 = scaled * sides[side]
                grads.append(nt(values[:keys], jnp.concatenate([g2, rest.astype(BF16)], axis=1)))
                q_parts.append(q_ref[own, :] * sides[side])
                g_parts.append(g2)
            return grads, jnp.concatenate(q_parts, axis=0), jnp.concatenate(g_parts, axis=0)

        given = give(chunks - 1)
        for frame in reversed(range(chunks)):
            keys = FRAME * (frame + 1)
            own = slice(frame * FRAME, keys)
            tables = tables_of(fixed_ref, frames_ref, frame)
            grads, q_part, g_part = given
            given = give(frame - 1) if frame else None
            query_parts, score_parts, prob_parts = [], [], []
            for side in range(2):
                attention = p_ref[frame, side, :keys, :]
                grad_scores = (attention.astype(F32) * grads[side]).astype(BF16)
                query_parts.append(nn(turned[side * HEAD_DIM : (side + 1) * HEAD_DIM, :keys], grad_scores))
                score_parts.append(grad_scores)
                prob_parts.append(attention)
            grad_query = jnp.concatenate(query_parts, axis=0).T
            key_parts = nn(jnp.concatenate(score_parts, axis=1), q_part)
            value_parts = nn(jnp.concatenate(prob_parts, axis=1), g_part)
            dq_ref[own, :] = (turn(grad_query, tables, True) * SCORE_SCALE).astype(BF16)
            if frame == chunks - 1:
                dk_sum[...] = key_parts
                dv_sum[...] = value_parts
            else:
                dk_sum[:keys, :] += key_parts
                dv_sum[:keys, :] += value_parts
            dk_ref[own, :] = turn(dk_sum[own, :], tables, True).astype(BF16)
            dv_ref[own, :] = dv_sum[own, :].astype(BF16)

        for part, ref in enumerate((dq_ref, dk_ref, dv_ref)):
            piece = slice(part * PAIR, (part + 1) * PAIR)
            terms = nn(first_turned[...], ref[...])
            if swap_qkv:
                qkv_own[step, :, piece] = terms
                qkv_send[step, :, piece] = qkv_own[step, at((1 - x) * half, half), piece].astype(BF16)
            else:
                qkv_out[:, at(part * features + step * PAIR, PAIR)] = terms

        @pl.when(step == 0)
        def _():
            met([(beside, core)])
            start()

        if swap_qkv:
            qkv_copy(step).start()

        @pl.when(step == slabs - 1)
        def _():
            finish()
            for slab in range(slabs if swap_qkv else 0):
                qkv_copy(slab).wait_recv()
                for part in range(3):
                    piece = slice(part * PAIR, (part + 1) * PAIR)
                    place = part * features + slab * PAIR
                    qkv_out[:, place : place + PAIR] = qkv_own[
                        slab, at(x * half, half), piece
                    ] + qkv_recv[slab, :, piece].astype(F32)
            for slab in range(slabs if swap_qkv else 0):
                qkv_copy(slab).wait_send()

    slab = pl.BlockSpec((total, PAIR), lambda s: (0, s))
    in_specs = [pl.BlockSpec((chunks, 2, total, FRAME), lambda s: (0, s, 0, 0))]
    in_specs += [slab] * 6 + [whole(first), whole(fixed), whole(frames)]
    in_specs += swap.in_specs()
    qkv_shape = (half if swap_qkv else PAIR, 3 * features)
    shapes, specs = swap.outputs()
    out_shape = [jax.ShapeDtypeStruct((total, features), BF16)] * 3
    out_shape += [jax.ShapeDtypeStruct(qkv_shape, F32)] + shapes
    out_specs = [slab] * 3 + [whole_out(qkv_shape)] + specs
    scratch = [pltpu.VMEM((total, PAIR), F32)] * 2 + [pltpu.VMEM((PAIR, total), BF16)]
    if swap_qkv:
        scratch += [pltpu.VMEM((slabs, PAIR, 3 * PAIR), F32)]
        scratch += [pltpu.VMEM((slabs, half, 3 * PAIR), BF16)] * 2
        scratch += [pltpu.SemaphoreType.DMA((2, slabs))]
    scratch += swap.scratch()
    return pl.pallas_call(
        kernel,
        grid=(slabs,),
        out_shape=out_shape,
        in_specs=in_specs,
        out_specs=out_specs,
        scratch_shapes=scratch,
        compiler_params=pltpu.CompilerParams(
            collective_id=identity, has_side_effects=True, vmem_limit_bytes=VMEM_BYTES
        ),
        name=f"attention_backward_{identity}",
    )(
        probs,
        divisor,
        mixed,
        query,
        key,
        value,
        grad_mixed,
        first,
        fixed,
        frames,
        *swap.operands(),
    )


def rows_backward(entry, upper, identity, span, swap):
    top, bottom = len(entry) == 1, upper is None
    if not top:
        above, entry = entry[0], entry[1:]
    total = entry[0].shape[1] if top else entry[0].shape[0]
    chunks = total // span
    columns = 256
    ahead = 0 if top else 2 if bottom else 1
    if top:
        width = 2 * entry[0].shape[2]
    else:
        features, width = entry[0].shape[1], entry[5].shape[1]
    if not bottom:
        layer = upper[0]
        hidden_units, mixed_features = upper[1].shape[1], upper[6].shape[1]
    place_rows = total // lax.axis_size("seq")

    def kernel(*refs):
        refs = list(refs)

        def take(count):
            taken = refs[:count]
            del refs[:count]
            return taken

        if top:
            (d_out_ref,) = take(1)
        else:
            dq_ref, dk_ref, dv_ref, unit1, scale1, dm_ref, wq, gain1 = take(8)
        if not bottom:
            act_ref, gp_ref, unit2, scale2, second_ref, mixed_ref = take(6)
            wo_any, wu_any, wd_any, gain2 = take(4)
        sources = take(swap.count)
        if not top:
            (vec1,) = take(1)
        if not bottom:
            dmid_out, dmix_out, out_sum, up_sum, down_sum, vec2 = take(6)
        else:
            dx_out, dx_other, vec_other = take(3)
        targets = take(swap.count)
        if not top:
            a_send, a_recv = take(2)
        if not bottom:
            b_send, b_recv, grad_keep, hidden_keep, low_keep, last_keep, wo, wu, wd, w_sem = take(10)
        else:
            dx_keep, dx_send, dx_recv, vec_recv, x_send_sem, x_recv_sem = take(6)
        send_sem, recv_sem = take(2)
        start_swap, finish_swap = swap.bind(sources, targets, refs)

        step = pl.program_id(0)
        me, core = lax.axis_index("seq"), lax.axis_index("tp")
        pair = at((me // 2) * PAIR, PAIR)
        x = lax.rem(me, 2)
        beside = me + 1 - 2 * x

        def exchange(kind, chunk):
            source, target = (a_send, a_recv) if kind == 0 else (b_send, b_recv)
            return remote(
                source.at[chunk],
                target.at[chunk],
                send_sem.at[kind, chunk],
                recv_sem.at[kind, chunk],
                me,
                1 - core,
            )

        def load(index):
            source, target = ((wd_any, wd), (wu_any, wu), (wo_any, wo))[index]
            return pltpu.make_async_copy(source.at[layer], target, w_sem.at[index])

        partners = [(me, 1 - core)] + ([(beside, core)] if bottom or swap.count else [])

        @pl.when(step == 0)
        def _():
            if not bottom:
                for index in range(3):
                    load(index).start()
                out_sum[...] = jnp.zeros_like(out_sum)
                up_sum[...] = jnp.zeros_like(up_sum)
                down_sum[...] = jnp.zeros_like(down_sum)
                vec2[...] = jnp.zeros_like(vec2)
            if not top:
                vec1[...] = jnp.zeros_like(vec1)
            hello(partners)

        def meet():
            @pl.when(step == 0)
            def _():
                met(partners)
                start_swap()

        def entry_products():
            partial = None
            for part, ref in enumerate((dq_ref, dk_ref, dv_ref)):
                grad = ref[...]
                term = nt(grad, wq[0, part])
                partial = term if partial is None else partial + term
                vec1[part : part + 1, :] += column_sum(grad.astype(F32))
            a_send[step] = partial.astype(BF16)

        def entry_norm(chunk):
            if top:
                return halves(d_out_ref)
            grad_first = a_send[chunk].astype(F32) + a_recv[chunk].astype(F32)
            unit, scale = kept_norm(unit1, scale1)
            for start, sums in ((3, column_sum(grad_first * unit)), (5, column_sum(grad_first))):
                for side in range(width // features):
                    piece = slice(side * features, (side + 1) * features)
                    vec1[start + side : start + side + 1, :] += sums[:, piece]
            return dm_ref[...] + norm_pull(grad_first, gain1[above : above + 1, :], unit, scale)

        def feed_forward(between=None):
            chunk = step - ahead
            gradient = entry_norm(chunk)
            if bottom:
                dx_keep[at(chunk * span, span), :] = gradient
                return
            grad_keep[lax.rem(chunk, 2)] = gradient
            vec2[1:2, :width] += column_sum(gradient)
            low = gradient.astype(BF16)
            low_keep[...] = low
            low_columns = low_keep[:, pair]
            second = second_ref[...]
            parts = [slice(start, start + columns) for start in range(0, hidden_units, columns)]
            grad_act = nt(low, wd[parts[0], :])
            for index, part in enumerate(parts):
                following = nt(low, wd[parts[index + 1], :]) if index + 1 < len(parts) else None
                grad_hidden = grad_act * gp_ref[:, part].astype(F32)
                hidden_keep[:, part] = grad_hidden.astype(BF16)
                vec2[0:1, part] += column_sum(grad_hidden)
                grad_act = following
            if between is not None:
                between()
            b_send[chunk] = nt(hidden_keep[...], wu[...]).astype(BF16)
            down_sum[...] += tn(low_columns, act_ref[...])
            up_sum[...] += tn(second, hidden_keep[...])

        def close():
            chunk = step - ahead - 1
            grad_second = b_send[chunk].astype(F32) + b_recv[chunk].astype(F32)
            unit, scale = kept_norm(unit2, scale2)
            vec2[2:3, :width] += column_sum(grad_second * unit)
            vec2[3:4, :width] += column_sum(grad_second)
            grad_middle = grad_keep[lax.rem(chunk, 2)] + norm_pull(
                grad_second, gain2[layer : layer + 1, :], unit, scale
            )
            dmid_out[...] = grad_middle
            vec2[4:5, :width] += column_sum(grad_middle)
            low = grad_middle.astype(BF16)
            last_keep[...] = low
            out_sum[...] += tn(last_keep[:, pair], mixed_ref[...])
            dmix_out[...] = nt(low, wo[...]).astype(BF16)

        if not top:

            @pl.when(step < chunks)
            def _():
                entry_products()
                meet()
                exchange(0, step).start()

        @pl.when((step >= ahead) & (step < chunks + ahead))
        def _():
            if not top:
                exchange(0, step - ahead).wait_recv()
            if not bottom:

                @pl.when(step == ahead)
                def _():
                    load(0).wait()

            feed_forward(lambda: pl.when(step == ahead)(lambda: load(1).wait()))
            if not bottom:
                if top:
                    meet()
                exchange(1, step - ahead).start()

        if not bottom:

            @pl.when(step == ahead + 1)
            def _():
                load(2).wait()

            @pl.when(step >= ahead + 1)
            def _():
                exchange(1, step - ahead - 1).wait_recv()
                close()

        if bottom:

            def x_copy(index):
                source, target = ((dx_send, dx_recv), (vec1, vec_recv))[index]
                return remote(
                    source, target, x_send_sem.at[index], x_recv_sem.at[index], beside, core
                )

            @pl.when(step == chunks + 1)
            def _():
                dx_send[...] = dx_keep[at(beside * place_rows, place_rows), :].astype(BF16)
                x_copy(0).start()
                x_copy(1).start()
                dx_out[...] = dx_keep[at(me * place_rows, place_rows), :]
                x_copy(0).wait_recv()
                x_copy(1).wait_recv()
                dx_other[...] = dx_recv[...].astype(F32)
                vec_other[...] = vec_recv[...]
                x_copy(0).wait_send()
                x_copy(1).wait_send()

        @pl.when(step == pl.num_programs(0) - 1)
        def _():
            for kind in ([] if top else [0]) + ([] if bottom else [1]):
                for chunk in range(chunks):
                    exchange(kind, chunk).wait_send()
            finish_swap()

    def rows(columns, behind):
        return pl.BlockSpec(
            (span, columns), lambda s: (jnp.clip(s - behind, 0, chunks - 1), 0)
        )

    vec = jax.ShapeDtypeStruct((8, VEC), F32)
    operands, in_specs, out_shape, out_specs, scratch = [], [], [], [], []
    if top:
        operands += list(entry)
        in_specs += [halves_spec(entry[0].shape, chunks, 0, span)]
    else:
        operands += list(entry)
        in_specs += [rows(features, 0)] * 3
        in_specs += [rows(width, ahead), rows(PAIR, ahead), rows(width, ahead)]
        in_specs += [
            pl.BlockSpec(
                (1, *entry[6].shape[1:]),
                lambda s: (above, 0, 0, 0),
                pipeline_mode=pl.Buffered(1),
            ),
            whole(entry[7]),
        ]
        narrow = jax.ShapeDtypeStruct((8, features), F32)
        out_shape += [narrow]
        out_specs += [whole_out((8, features))]
        scratch += [pltpu.VMEM((chunks, span, width), BF16)] * 2
    if not bottom:
        operands += list(upper[1:])
        in_specs += [rows(hidden_units, ahead)] * 2
        in_specs += [rows(width, ahead + 1), rows(PAIR, ahead + 1), rows(PAIR, ahead)]
        in_specs += [rows(mixed_features, ahead + 1)] + [ANYWHERE] * 3 + [whole(upper[10])]
        sums = [mixed_features, hidden_units, hidden_units]
        out_shape += [
            jax.ShapeDtypeStruct((total, width), F32),
            jax.ShapeDtypeStruct((total, mixed_features), BF16),
        ]
        out_shape += [jax.ShapeDtypeStruct((PAIR, size), F32) for size in sums] + [vec]
        out_specs += [rows(width, ahead + 1), rows(mixed_features, ahead + 1)]
        out_specs += [whole_out((PAIR, size)) for size in sums] + [whole_out((8, VEC))]
        scratch += [pltpu.VMEM((chunks, span, width), BF16)] * 2
        scratch += [
            pltpu.VMEM((2, span, width), F32),
            pltpu.VMEM((span, hidden_units), BF16),
            pltpu.VMEM((span, width), BF16),
            pltpu.VMEM((span, width), BF16),
            pltpu.VMEM(upper[7].shape[1:], BF16),
            pltpu.VMEM(upper[8].shape[1:], BF16),
            pltpu.VMEM(upper[9].shape[1:], BF16),
            pltpu.SemaphoreType.DMA((3,)),
        ]
    else:
        out_shape += [
            jax.ShapeDtypeStruct((place_rows, width), F32),
            jax.ShapeDtypeStruct((place_rows, width), F32),
            narrow,
        ]
        out_specs += [whole_out((place_rows, width))] * 2 + [whole_out((8, features))]
        scratch += [
            pltpu.VMEM((total, width), F32),
            pltpu.VMEM((place_rows, width), BF16),
            pltpu.VMEM((place_rows, width), BF16),
            pltpu.VMEM((8, features), F32),
            pltpu.SemaphoreType.DMA((2,)),
            pltpu.SemaphoreType.DMA((2,)),
        ]
    scratch += [pltpu.SemaphoreType.DMA((2, chunks))] * 2
    operands += swap.operands()
    in_specs += swap.in_specs()
    shapes, specs = swap.outputs()
    out_shape += shapes
    out_specs += specs
    scratch += swap.scratch()
    return pl.pallas_call(
        kernel,
        grid=(chunks + (1 if top else 2),),
        out_shape=out_shape,
        in_specs=in_specs,
        out_specs=out_specs,
        scratch_shapes=scratch,
        compiler_params=pltpu.CompilerParams(
            collective_id=identity, has_side_effects=True, vmem_limit_bytes=VMEM_BYTES
        ),
        name=f"rows_backward_{identity}",
    )(*operands)


def assemble(sums, vecs, lanes, n, features, hidden_units):
    place = lanes[1].shape[0]
    width = lanes[1].shape[1]
    half = PAIR // 2

    def kernel(*refs):
        refs = list(refs)

        def take(count):
            taken = refs[:count]
            del refs[:count]
            return taken

        qkvs, outs, ups, downs = take(LAYERS), take(LAYERS), take(LAYERS), take(LAYERS)
        vec_refs = [take(4) for _ in range(LAYERS)]
        out_lane, out_other, dx_own, dx_other = take(4)
        out_ref, dx_ref, gain1, shift1, g_qkv, b_qkv, g_out, b_out = take(8)
        gain2, shift2, g_up, b_up, g_down, b_down = take(6)
        out_own, sem = refs
        me = lax.axis_index("seq")
        x = lax.rem(me, 2)
        fetch = pltpu.make_async_copy(out_lane.at[at(me * place, place), :], out_own, sem)
        fetch.start()

        for layer in range(LAYERS):
            for part in range(3):
                g_qkv[layer, part] = qkvs[layer][:, part * features : (part + 1) * features]
            for ref, target in ((outs, g_out), (ups, g_up), (downs, g_down)):
                target[layer] = ref[layer][...]

        for layer, (entry_own, entry_other, upper_own, upper_other) in enumerate(vec_refs):
            line = slice(layer, layer + 1)
            for part in range(3):
                row = slice(part, part + 1)
                b_qkv[part, line, :] = entry_own[row, :] + entry_other[row, :]
            b_up[line, :] = upper_own[0:1, :hidden_units] + upper_other[0:1, :hidden_units]

            def owned(mine, other, row):
                wide = mine.shape[1]
                place = (me // 2) * PAIR
                pair = at(lax.rem(place, wide), PAIR)
                both = mine[row : row + 1, pair] + other[row : row + 1, pair]
                for later in range(1, width // wide):
                    line = slice(row + later, row + later + 1)
                    both = jnp.where(place // wide == later, mine[line, pair] + other[line, pair], both)
                return jnp.where(x == 0, both[:, :half], both[:, half:])

            gain1[line, :] = owned(entry_own, entry_other, 3)
            shift1[line, :] = owned(entry_own, entry_other, 5)
            b_down[line, :] = owned(upper_own, upper_other, 1)
            gain2[line, :] = owned(upper_own, upper_other, 2)
            shift2[line, :] = owned(upper_own, upper_other, 3)
            b_out[line, :] = owned(upper_own, upper_other, 4)

        def both_lanes(target, mine, other):
            target[:, 0, :] = jnp.where(x == 0, mine, other)
            target[:, 1, :] = jnp.where(x == 0, other, mine)

        both_lanes(dx_ref, dx_own[...], dx_other[...])
        fetch.wait()
        both_lanes(out_ref, out_own[...], out_other[...])

    def f32(*shape):
        return jax.ShapeDtypeStruct(shape, F32)

    in_vmem = pl.BlockSpec(memory_space=pltpu.VMEM)
    flat = []
    for kind in range(4):
        flat += [sums[layer][kind] for layer in range(LAYERS)]
    for layer in range(LAYERS):
        flat += list(vecs[layer])
    flat += list(lanes)
    small = f32(LAYERS, width // n)
    return pl.pallas_call(
        kernel,
        out_shape=(
            f32(place, 2, width),
            f32(place, 2, width),
            small,
            small,
            f32(LAYERS, 3, half, features),
            f32(3, LAYERS, features),
            f32(LAYERS, half, features),
            small,
            small,
            small,
            f32(LAYERS, half, hidden_units),
            f32(LAYERS, hidden_units),
            f32(LAYERS, half, hidden_units),
            small,
        ),
        in_specs=[in_vmem] * (len(flat) - 4) + [ANYWHERE] + [in_vmem] * 3,
        out_specs=(in_vmem,) * 14,
        scratch_shapes=[pltpu.VMEM((place, width), F32), pltpu.SemaphoreType.DMA],
        compiler_params=pltpu.CompilerParams(vmem_limit_bytes=VMEM_BYTES),
        name="assemble",
    )(*flat)


def per_chip(
    tokens,
    d_out,
    norm1_gain,
    norm1_shift,
    w_qkv,
    b_qkv,
    w_out,
    b_out,
    norm2_gain,
    norm2_shift,
    w_up,
    b_up,
    w_down,
    b_down,
    episode_frames,
    live,
):
    n = lax.axis_size("seq")
    rows = tokens.shape[0]
    features = w_qkv.shape[3]
    fixed, ahead = turn_constants(rows * n // FRAME)
    qkv, qkv_bias = w_qkv.transpose(0, 2, 1, 3), b_qkv.transpose(1, 0, 2)

    gathered, key_bias, frames, *projected = gather_and_project(
        tokens, live.T, episode_frames, norm1_gain, norm1_shift, qkv, qkv_bias, fixed, ahead, n
    )
    streams, kept, d_lane = [gathered], [], None
    for layer in range(LAYERS):
        following = None
        if layer + 1 < LAYERS:
            following = (qkv, norm1_gain, norm1_shift, qkv_bias, fixed, frames)
        results = layer_forward(
            layer,
            *projected[:3],
            key_bias,
            streams[layer],
            (w_out, w_up, w_down),
            (b_out, norm2_gain, norm2_shift, b_up, b_down),
            following,
            d_out if layer == 0 else None,
            n,
            1 + layer,
        )
        kept.append((*projected, *results[:8]))
        streams.append(results[8])
        if following is not None:
            projected = results[9:15]
        if layer == 0:
            d_lane = results[-1]

    sums = [[None] * 4 for _ in range(LAYERS)]
    vecs = [[None] * 4 for _ in range(LAYERS)]
    entry, later = (d_lane,), None
    for layer in reversed(range(LAYERS)):
        query, key, value, first, unit1, scale1, probs, divisor, mixed = kept[layer][:9]
        unit2, scale2, second, act, slope = kept[layer][9:]
        upper = (
            layer,
            act,
            slope,
            unit2,
            scale2,
            second,
            mixed,
            w_out,
            w_up,
            w_down,
            norm2_gain,
        )
        identity = 1 + LAYERS + 2 * (LAYERS - 1 - layer)
        if later is None:
            results = rows_backward(entry, upper, identity, FRAME, Swap([], []))
        else:
            swap = Swap(later[:2], [(later[2], 0), (streams[LAYERS], rows)])
            vec1, *results = rows_backward(entry, upper, identity, FRAME, swap)
            results, swapped = results[:6], results[6:]
            sums[layer + 1][3], sums[layer + 1][0] = swapped[:2]
            vecs[layer + 1][3], out_other = swapped[2:]
            vecs[layer + 1][0] = vec1
        grad_middle, grad_mixed, out_sum, up_sum, down_sum, vec2 = results
        vecs[layer][2] = vec2
        last = layer == 0
        if last:
            swap = Swap([out_sum, up_sum, down_sum], [(vec2, 0), (vecs[layer + 1][0], 0)])
        else:
            swap = Swap([out_sum, up_sum], [])
        results = attention_backward(
            probs,
            divisor,
            mixed,
            query,
            key,
            value,
            grad_mixed,
            first,
            fixed,
            frames,
            swap,
            last,
            identity + 1,
        )
        grad_query, grad_key, grad_value, qkv_sum = results[:4]
        if last:
            sums[layer] = [qkv_sum, *results[4:7]]
            vecs[layer][3], vecs[layer + 1][1] = results[7:9]
        else:
            sums[layer][1:3] = results[4:6]
            later = [down_sum, qkv_sum, vec2]
        entry = (
            layer,
            grad_query,
            grad_key,
            grad_value,
            unit1,
            scale1,
            grad_middle,
            qkv,
            norm1_gain,
        )
    vec1, dx_own, dx_other, vec_other = rows_backward(
        entry, None, 1 + 3 * LAYERS, FRAME, Swap([], [])
    )
    vecs[0][:2] = [vec1, vec_other]
    results = list(
        assemble(
            sums,
            vecs,
            (streams[LAYERS], out_other, dx_own, dx_other),
            n,
            features,
            w_up.shape[2],
        )
    )
    results[4] = results[4].transpose(0, 2, 1, 3)
    results[5] = results[5].transpose(1, 0, 2)
    results[6] = results[6].transpose(0, 2, 1)
    results[12] = results[12].transpose(0, 2, 1)
    return tuple(results)


def lane_fits(mesh, tokens):
    n = mesh.shape["seq"]
    positions, lanes, width = tokens.shape
    rows = positions // n
    return (
        lanes == 2
        and n % 4 == 0
        and positions <= 4 * FRAME
        and positions % FRAME == 0
        and FRAME % rows == 0
        and width // n * 2 == PAIR
        and mesh.shape["tp"] == 2
    )


def solution(mesh):
    placed = (
        P("seq", None, None),
        P("seq", None, None),
        P(),
        P(),
        P(None, None, None, "tp"),
        P(None, None, "tp"),
        P(None, "tp", None),
        P(),
        P(),
        P(),
        P(None, None, "tp"),
        P(None, "tp"),
        P(None, "tp", None),
        P(),
        P(),
        P("seq", None),
    )
    def mapped(body):
        return jax.shard_map(
            body,
            mesh=mesh,
            in_specs=placed,
            out_specs=(
                P("seq", None, None),
                P("seq", None, None),
                P(None, "seq"),
                P(None, "seq"),
                P(None, "seq", None, "tp"),
                P(None, None, "tp"),
                P(None, "tp", "seq"),
                P(None, "seq"),
                P(None, "seq"),
                P(None, "seq"),
                P(None, "seq", "tp"),
                P(None, "tp"),
                P(None, "tp", "seq"),
                P(None, "seq"),
            ),
            check_vma=False,
        )

    def run(tokens, *others):
        if lane_fits(mesh, tokens):
            return mapped(per_chip)(tokens, *others)
        return mapped(per_device)(tokens, *others)

    return run
```

```python
import math

import jax
import jax.numpy as jnp
import numpy as np
from jax import lax
from jax.experimental import pallas as pl
from jax.experimental.pallas import tpu as pltpu
from jax.sharding import PartitionSpec as P

HEAD_DIM = 64
GRID = 16
FRAME = 256
LAYERS = 2
MICRO = 2


EPSILON = 1e-06
MASKED = -1e30
SCORE_SCALE = 0.125


def layer_norm(stream, norm_gain, norm_shift):
    center = stream - jnp.mean(stream, axis=-1, keepdims=True)
    spread = jnp.mean(center * center, axis=-1, keepdims=True)
    return center * lax.rsqrt(spread + EPSILON) * norm_gain + norm_shift


def rotate(values, frame_place, row_place, column_place):
    frequency = jnp.exp(jnp.arange(10, dtype=jnp.float32) * (-math.log(10000.0) / 10.0))
    pieces = []
    for section, place in enumerate((frame_place, row_place, column_place)):
        lower = values[..., 20 * section : 20 * section + 10]
        upper = values[..., 20 * section + 10 : 20 * section + 20]
        angles = place.astype(jnp.float32)[..., None, None] * frequency
        cosine = jnp.cos(angles)
        sine_part = jnp.sin(angles)
        pieces.append(lower * cosine - upper * sine_part)
        pieces.append(lower * sine_part + upper * cosine)
    pieces.append(values[..., 60:])
    return jnp.concatenate(pieces, axis=-1)


def episode_tags(frame_counts, positions):
    endings = jnp.cumsum(frame_counts) * FRAME
    passed = (positions[:, None] >= endings[None, :]).astype(jnp.int32)
    episode = jnp.sum(passed, axis=1)
    opening = jnp.sum(passed * frame_counts[None, :], axis=1)
    frame_index = positions // FRAME - opening
    within = positions % FRAME
    return (episode, frame_index, within // GRID, within % GRID)


def gelu_exact(values):
    return jax.nn.gelu(values, approximate=False)


def sum_heads(partial_sum):
    return lax.psum(partial_sum.astype(jnp.bfloat16), "tp").astype(jnp.float32)


def sum_inputs(partial_sum):
    return lax.psum(partial_sum.astype(jnp.bfloat16), "tp").astype(jnp.float32)


def lane_scores(query, keys_all, lane_index, query_tags, key_tags):
    head_count = query.shape[2] // HEAD_DIM
    query_lane = lax.dynamic_index_in_dim(query, lane_index, 1, False).reshape(
        query.shape[0], head_count, HEAD_DIM
    )
    keys_lane = lax.dynamic_index_in_dim(keys_all, lane_index, 1, False).reshape(
        keys_all.shape[0], head_count, HEAD_DIM
    )
    query_episode, query_frame = [
        lax.dynamic_index_in_dim(item, lane_index, 1, False) for item in query_tags
    ]
    key_episode, key_frame, key_live = [
        lax.dynamic_index_in_dim(item, lane_index, 1, False) for item in key_tags
    ]
    allowed = (
        (query_episode[:, None] == key_episode[None, :])
        & (key_frame[None, :] <= query_frame[:, None])
        & (key_live[None, :] > 0)
    )
    scores = (
        jnp.einsum("qhd,khd->hqk", query_lane, keys_lane, preferred_element_type=jnp.float32)
        * SCORE_SCALE
    )
    return (jnp.where(allowed[None], scores, MASKED), query_lane, keys_lane)


def attend_forward(query, keys_all, values_all, query_tags, key_tags):
    rows_dev, lane_count, features = query.shape
    head_count = features // HEAD_DIM

    def one_lane(lane_index, carry):
        scores, query_lane, keys_lane = lane_scores(
            query, keys_all, lane_index, query_tags, key_tags
        )
        highest = jnp.max(scores, axis=-1, keepdims=True)
        shifted = jnp.exp(scores - highest)
        summed = jnp.sum(shifted, axis=-1, keepdims=True)
        attention = (shifted / summed).astype(jnp.bfloat16)
        values_lane = lax.dynamic_index_in_dim(values_all, lane_index, 1, False).reshape(
            values_all.shape[0], head_count, HEAD_DIM
        )
        result = jnp.einsum(
            "hqk,khd->qhd", attention, values_lane, preferred_element_type=jnp.float32
        ).reshape(rows_dev, 1, features)
        log_total = (highest + jnp.log(summed))[None, :, :, 0]
        return (result, log_total)

    initial = (
        jnp.zeros((rows_dev, lane_count, features), jnp.float32),
        jnp.zeros((lane_count, head_count, rows_dev), jnp.float32),
    )
    return lax.fori_loop(0, lane_count, one_lane, initial)


def attend_backward(query, keys_all, values_all, log_total, grad_mixed, query_tags, key_tags):
    rows_dev, lane_count, features = query.shape
    head_count = features // HEAD_DIM
    key_rows = keys_all.shape[0]

    def one_lane(lane_index, carry):
        scores, query_lane, keys_lane = lane_scores(
            query, keys_all, lane_index, query_tags, key_tags
        )
        values_lane = lax.dynamic_index_in_dim(values_all, lane_index, 1, False).reshape(
            key_rows, head_count, HEAD_DIM
        )
        grad_lane = lax.dynamic_index_in_dim(grad_mixed, lane_index, 1, False).reshape(
            rows_dev, head_count, HEAD_DIM
        )
        attention = jnp.exp(
            scores - lax.dynamic_index_in_dim(log_total, lane_index, 0, False)[:, :, None]
        )
        grad_attention = jnp.einsum(
            "qhd,khd->hqk", grad_lane, values_lane, preferred_element_type=jnp.float32
        )
        inner = jnp.sum(attention * grad_attention, axis=-1, keepdims=True)
        grad_scores = (attention * (grad_attention - inner)).astype(jnp.bfloat16)
        query_part = (
            jnp.einsum("hqk,khd->qhd", grad_scores, keys_lane, preferred_element_type=jnp.float32)
            * SCORE_SCALE
        )
        key_part = (
            jnp.einsum("hqk,qhd->khd", grad_scores, query_lane, preferred_element_type=jnp.float32)
            * SCORE_SCALE
        )
        value_part = jnp.einsum(
            "hqk,qhd->khd",
            attention.astype(jnp.bfloat16),
            grad_lane,
            preferred_element_type=jnp.float32,
        )
        stacked = jnp.stack(
            [key_part.reshape(key_rows, features), value_part.reshape(key_rows, features)], axis=1
        )
        key_terms = stacked[:, None]
        grad_query = query_part.reshape(rows_dev, 1, features)
        return (grad_query, key_terms)

    initial = (
        jnp.zeros((rows_dev, lane_count, features), jnp.float32),
        jnp.zeros((key_rows, lane_count, 2, features), jnp.float32),
    )
    return lax.fori_loop(0, lane_count, one_lane, initial)


def front(stream, layer_index, params, query_tags, key_tags, positions):
    (
        gain_one,
        shift_one,
        mat_qkv,
        bias_qkv,
        mat_out,
        bias_out,
        gain_two,
        shift_two,
        mat_up,
        bias_up,
        mat_down,
        bias_down,
    ) = [item[layer_index] for item in params]
    rows_dev, lane_count, width = stream.shape
    features = mat_qkv.shape[2]
    head_count = features // HEAD_DIM
    frame_place, row_place, column_place = positions
    first = layer_norm(stream, gain_one, shift_one).astype(jnp.bfloat16)
    projected = (
        jnp.einsum("tbd,dcf->tbcf", first, mat_qkv, preferred_element_type=jnp.float32) + bias_qkv
    )
    split = projected.reshape(rows_dev, lane_count, 3, head_count, HEAD_DIM)
    query = (
        rotate(split[:, :, 0], frame_place, row_place, column_place)
        .reshape(rows_dev, lane_count, features)
        .astype(jnp.bfloat16)
    )
    keys = (
        rotate(split[:, :, 1], frame_place, row_place, column_place)
        .reshape(rows_dev, lane_count, features)
        .astype(jnp.bfloat16)
    )
    values = projected[:, :, 2].astype(jnp.bfloat16)
    keys_all, values_all = (
        lax.all_gather(keys, "seq", axis=0, tiled=True),
        lax.all_gather(values, "seq", axis=0, tiled=True),
    )
    mixed_full, log_total = attend_forward(query, keys_all, values_all, query_tags, key_tags)
    mixed = mixed_full.astype(jnp.bfloat16)
    middle = (
        stream
        + sum_heads(jnp.einsum("tbf,fd->tbd", mixed, mat_out, preferred_element_type=jnp.float32))
        + bias_out
    )
    second = layer_norm(middle, gain_two, shift_two).astype(jnp.bfloat16)
    hidden = jnp.einsum("tbd,df->tbf", second, mat_up, preferred_element_type=jnp.float32) + bias_up
    activation = gelu_exact(hidden).astype(jnp.bfloat16)
    return (
        first,
        query,
        keys_all,
        values_all,
        log_total,
        mixed,
        middle,
        second,
        hidden,
        activation,
        mixed_full,
    )


def layer_backward(stream, gradient, layer_index, params, query_tags, key_tags, positions):
    (
        gain_one,
        shift_one,
        mat_qkv,
        bias_qkv,
        mat_out,
        bias_out,
        gain_two,
        shift_two,
        mat_up,
        bias_up,
        mat_down,
        bias_down,
    ) = [item[layer_index] for item in params]
    (
        first,
        query,
        keys_all,
        values_all,
        log_total,
        mixed,
        middle,
        second,
        hidden,
        activation,
        mixed_full,
    ) = front(stream, layer_index, params, query_tags, key_tags, positions)
    frame_place, row_place, column_place = positions
    rows_dev, lane_count, width = stream.shape
    features = query.shape[2]
    head_count = features // HEAD_DIM
    grad_low = gradient.astype(jnp.bfloat16)
    grad_w_down = jnp.einsum(
        "tbf,tbd->fd", activation, grad_low, preferred_element_type=jnp.float32
    )
    grad_b_down = jnp.sum(gradient, axis=(0, 1))
    grad_activation = jnp.einsum(
        "tbd,fd->tbf", grad_low, mat_down, preferred_element_type=jnp.float32
    )
    grad_hidden = jax.vjp(gelu_exact, hidden)[1](grad_activation)[0].astype(jnp.bfloat16)
    grad_b_up = jnp.sum(grad_hidden.astype(jnp.float32), axis=(0, 1))
    grad_w_up = jnp.einsum("tbd,tbf->df", second, grad_hidden, preferred_element_type=jnp.float32)
    grad_second = sum_inputs(
        jnp.einsum("tbf,df->tbd", grad_hidden, mat_up, preferred_element_type=jnp.float32)
    )
    middle_pull = jax.vjp(layer_norm, middle, gain_two, shift_two)[1]
    grad_inner, grad_gain_two, grad_shift_two = middle_pull(grad_second)
    grad_middle = gradient + grad_inner
    grad_b_out = jnp.sum(grad_middle, axis=(0, 1))
    middle_low = grad_middle.astype(jnp.bfloat16)
    grad_w_out = jnp.einsum("tbf,tbd->fd", mixed, middle_low, preferred_element_type=jnp.float32)
    grad_mixed = jnp.einsum(
        "tbd,fd->tbf", middle_low, mat_out, preferred_element_type=jnp.float32
    ).astype(jnp.bfloat16)
    grad_query, key_terms = attend_backward(
        query, keys_all, values_all, log_total, grad_mixed, query_tags, key_tags
    )
    returned = lax.psum_scatter(key_terms, "seq", scatter_dimension=0, tiled=True)
    turned_query = rotate(
        grad_query.reshape(rows_dev, lane_count, head_count, HEAD_DIM),
        -frame_place,
        -row_place,
        -column_place,
    )
    turned_keys = rotate(
        returned[:, :, 0].reshape(rows_dev, lane_count, head_count, HEAD_DIM),
        -frame_place,
        -row_place,
        -column_place,
    )
    grad_projected = jnp.stack(
        [
            turned_query.reshape(rows_dev, lane_count, features),
            turned_keys.reshape(rows_dev, lane_count, features),
            returned[:, :, 1],
        ],
        axis=2,
    ).astype(jnp.bfloat16)
    grad_b_qkv = jnp.sum(grad_projected.astype(jnp.float32), axis=(0, 1))
    grad_w_qkv = jnp.einsum(
        "tbd,tbcf->dcf", first, grad_projected, preferred_element_type=jnp.float32
    )
    grad_first = sum_inputs(
        jnp.einsum("tbcf,dcf->tbd", grad_projected, mat_qkv, preferred_element_type=jnp.float32)
    )
    first_pull = jax.vjp(layer_norm, stream, gain_one, shift_one)[1]
    grad_entry, grad_gain_one, grad_shift_one = first_pull(grad_first)
    grads = (
        grad_gain_one,
        grad_shift_one,
        grad_w_qkv,
        grad_b_qkv,
        grad_w_out,
        grad_b_out,
        grad_gain_two,
        grad_shift_two,
        grad_w_up,
        grad_b_up,
        grad_w_down,
        grad_b_down,
    )
    return (grad_middle + grad_entry, grads)


def per_device(
    tokens,
    d_out,
    norm1_gain,
    norm1_shift,
    w_qkv,
    b_qkv,
    w_out,
    b_out,
    norm2_gain,
    norm2_shift,
    w_up,
    b_up,
    w_down,
    b_down,
    episode_frames,
    live,
):
    rows_dev = tokens.shape[0]
    lane_count = tokens.shape[1] // MICRO
    total_rows = rows_dev * lax.axis_size("seq")
    local_positions = lax.axis_index("seq") * rows_dev + jnp.arange(rows_dev, dtype=jnp.int32)
    key_positions = jnp.arange(total_rows, dtype=jnp.int32)
    tagger = jax.vmap(episode_tags, in_axes=(0, None), out_axes=1)
    query_episode, query_frame, query_row, query_column = tagger(episode_frames, local_positions)
    key_episode, key_frame, key_row, key_column = tagger(episode_frames, key_positions)
    live_keys = lax.all_gather(live, "seq", axis=0, tiled=True)
    params = (
        norm1_gain,
        norm1_shift,
        w_qkv,
        b_qkv,
        w_out,
        b_out,
        norm2_gain,
        norm2_shift,
        w_up,
        b_up,
        w_down,
        b_down,
    )
    layer_grads = [None] * LAYERS
    outputs = []
    grad_tokens = []
    for micro_index in range(MICRO):
        first_lane = micro_index * lane_count
        last_lane = first_lane + lane_count
        query_tags = (query_episode[:, first_lane:last_lane], query_frame[:, first_lane:last_lane])
        key_tags = (
            key_episode[:, first_lane:last_lane],
            key_frame[:, first_lane:last_lane],
            live_keys[:, first_lane:last_lane],
        )
        positions = (
            query_frame[:, first_lane:last_lane],
            query_row[:, first_lane:last_lane],
            query_column[:, first_lane:last_lane],
        )
        stream = tokens[:, first_lane:last_lane].astype(jnp.float32)
        inputs = []
        gathered = []
        for layer_index in range(LAYERS):
            inputs.append(stream)
            layer_state = front(stream, layer_index, params, query_tags, key_tags, positions)
            gathered.append((layer_state[2], layer_state[3]))
            branch = jnp.einsum(
                "tbf,fd->tbd",
                layer_state[9],
                w_down[layer_index],
                preferred_element_type=jnp.float32,
            )
            stream = layer_state[6] + sum_heads(branch) + b_down[layer_index]
        outputs.append(stream)
        gradient = d_out[:, first_lane:last_lane]
        for layer_index in reversed(range(LAYERS)):
            gradient, grads = layer_backward(
                inputs[layer_index], gradient, layer_index, params, query_tags, key_tags, positions
            )
            if layer_grads[layer_index] is None:
                layer_grads[layer_index] = grads
            else:
                layer_grads[layer_index] = jax.tree.map(jnp.add, layer_grads[layer_index], grads)
        grad_tokens.append(gradient)
    stacked = [
        jnp.stack([layer_grads[layer_index][entry] for layer_index in range(LAYERS)])
        for entry in range(12)
    ]
    (
        grad_gain_one,
        grad_shift_one,
        grad_w_qkv,
        grad_b_qkv,
        grad_w_out,
        grad_b_out,
        grad_gain_two,
        grad_shift_two,
        grad_w_up,
        grad_b_up,
        grad_w_down,
        grad_b_down,
    ) = stacked
    in_sums = (
        lax.psum_scatter(grad_w_qkv, "seq", scatter_dimension=1, tiled=True),
        lax.psum_scatter(grad_w_up, "seq", scatter_dimension=1, tiled=True),
        lax.psum_scatter(grad_gain_one, "seq", scatter_dimension=1, tiled=True),
        lax.psum_scatter(grad_shift_one, "seq", scatter_dimension=1, tiled=True),
        lax.psum_scatter(grad_gain_two, "seq", scatter_dimension=1, tiled=True),
        lax.psum_scatter(grad_shift_two, "seq", scatter_dimension=1, tiled=True),
        lax.psum_scatter(grad_b_out, "seq", scatter_dimension=1, tiled=True),
        lax.psum_scatter(grad_b_down, "seq", scatter_dimension=1, tiled=True),
    )
    out_sums = (
        lax.psum_scatter(grad_w_out, "seq", scatter_dimension=2, tiled=True),
        lax.psum_scatter(grad_w_down, "seq", scatter_dimension=2, tiled=True),
    )
    bias_total = lax.psum((grad_b_qkv, grad_b_up), "seq")
    return (
        jnp.concatenate(outputs, axis=1),
        jnp.concatenate(grad_tokens, axis=1),
        in_sums[2],
        in_sums[3],
        in_sums[0],
        bias_total[0],
        out_sums[0],
        in_sums[6],
        in_sums[4],
        in_sums[5],
        in_sums[1],
        bias_total[1],
        out_sums[1],
        in_sums[7],
    )


MESH = pl.DeviceIdType.MESH
BF16 = jnp.bfloat16
F32 = jnp.float32
VMEM_BYTES = 60 * 1024 * 1024
PAIR = 128
VEC = 2048


def nn(left, right):
    return lax.dot_general(left, right, (((1,), (0,)), ((), ())), preferred_element_type=F32)


def nt(left, right):
    return lax.dot_general(left, right, (((1,), (1,)), ((), ())), preferred_element_type=F32)


def tn(left, right):
    return lax.dot_general(left, right, (((0,), (0,)), ((), ())), preferred_element_type=F32)


def at(start, size):
    return pl.ds(pl.multiple_of(start, size), size)


def remote(src, dst, send, recv, seq, tp):
    return pltpu.make_async_remote_copy(
        src_ref=src,
        dst_ref=dst,
        send_sem=send,
        recv_sem=recv,
        device_id=(seq, tp),
        device_id_type=MESH,
    )


def hello(partners):
    barrier = pltpu.get_barrier_semaphore()
    for seq, tp in partners:
        pl.semaphore_signal(barrier, inc=1, device_id=(seq, tp), device_id_type=MESH)


def met(partners):
    pl.semaphore_wait(pltpu.get_barrier_semaphore(), len(partners))


def whole(array):
    zeros = (0,) * array.ndim
    return pl.BlockSpec(array.shape, lambda s: zeros, pipeline_mode=pl.Buffered(1))


def whole_out(shape):
    zeros = (0,) * len(shape)
    return pl.BlockSpec(shape, lambda s: zeros)


ANYWHERE = pl.BlockSpec(memory_space=pl.ANY)


def turn_row(table, place, section):
    frequency = np.exp(np.arange(10, dtype=np.float32) * np.float32(-math.log(10000.0) / 10.0))
    angle = place.astype(np.float32)[:, None] * frequency
    for base in range(20 * section, PAIR, HEAD_DIM):
        table[0, :, base : base + 10] = np.cos(angle)
        table[0, :, base + 10 : base + 20] = np.cos(angle)
        table[1, :, base : base + 10] = -np.sin(angle)
        table[2, :, base + 10 : base + 20] = np.sin(angle)


def turn_constants(frames):
    within, ahead = np.zeros((3, FRAME, PAIR), np.float32), np.zeros((3, frames, PAIR), np.float32)
    turn_row(within, np.arange(FRAME) // GRID, 1)
    turn_row(within, np.arange(FRAME) % GRID, 2)
    for base in range(60, PAIR, HEAD_DIM):
        within[0, :, base : base + 4] = 1.0
    turn_row(ahead, np.arange(frames), 0)
    return jnp.asarray(within), jnp.asarray(ahead)


def turn(values, tables, back=False):
    cosine, lower, upper = tables
    pieces = []
    for start in range(0, values.shape[1], PAIR):
        slab = values[:, start : start + PAIR]
        moved = pltpu.roll(slab, PAIR - 10, 1) * lower + pltpu.roll(slab, 10, 1) * upper
        pieces.append(slab * cosine - moved if back else slab * cosine + moved)
    return jnp.concatenate(pieces, axis=1)


def tables_of(fixed_ref, frames_ref, chunk):
    return [fixed_ref[i] + frames_ref[i, pl.ds(chunk, 1), :] for i in range(3)]


def normed(stream):
    center = stream - jnp.mean(stream, axis=-1, keepdims=True)
    spread = jnp.mean(center * center, axis=-1, keepdims=True)
    scale = lax.rsqrt(spread + EPSILON)
    return center * scale, scale


def norm_pull(grad, gain, unit, scale):
    scaled = grad * gain
    return scale * (
        scaled
        - jnp.mean(scaled, axis=-1, keepdims=True)
        - unit * jnp.mean(scaled * unit, axis=-1, keepdims=True)
    )


def keep_norm(unit, scale, unit_ref, scale_ref):
    unit_ref[...] = unit.astype(BF16)
    scale_ref[...] = jnp.broadcast_to(scale, scale_ref.shape)


def kept_norm(unit_ref, scale_ref):
    copies = unit_ref.shape[1] // scale_ref.shape[1]
    return unit_ref[...].astype(F32), jnp.concatenate([scale_ref[...]] * copies, axis=1)


def column_sum(values):
    return jnp.sum(values, axis=0, keepdims=True)


TAIL_SCALE = 0.28
TAIL = (
    0.11652094356158241,
    0.06749571043567162,
    0.2689127891325277,
    -0.2369967598579576,
    0.38987605334580333,
    -0.1058087459000828,
)


def gelu_both(hidden):
    falling = jnp.exp(hidden * hidden * -0.5)
    place = 1.0 / (1.0 + TAIL_SCALE * jnp.abs(hidden))
    tail = TAIL[-1]
    for factor in reversed(TAIL[:-1]):
        tail = tail * place + factor
    tail = tail * place * falling
    normal = jnp.where(hidden >= 0.0, 1.0 - tail, tail)
    return hidden * normal, normal + hidden * (1.0 / math.sqrt(2.0 * math.pi)) * falling


def project(stream, chunk, layer, pair, refs, outs, first_full):
    gain, shift, weight, bias, fixed, frames = refs
    query_ref, key_ref, value_ref, first_ref, unit_ref, scale_ref = outs
    unit, scale = normed(stream)
    keep_norm(unit, scale, unit_ref, scale_ref)
    first = (unit * gain[layer : layer + 1, :] + shift[layer : layer + 1, :]).astype(BF16)
    first_full[...] = first
    first_ref[...] = first_full[:, at(pair * PAIR, PAIR)]
    tables = tables_of(fixed, frames, chunk)
    query = nn(first, weight[0]) + bias[0, layer : layer + 1, :]
    query_ref[...] = (turn(query, tables) * SCORE_SCALE).astype(BF16)
    key = nn(first, weight[1]) + bias[1, layer : layer + 1, :]
    key_ref[...] = turn(key, tables).astype(BF16)
    value = nn(first, weight[2]) + bias[2, layer : layer + 1, :]
    value_ref[...] = value.astype(BF16)


class Relay:
    sems = 6

    def __init__(self, n, rows, buffer, other, sems, lives=None, live_other=None):
        self.n, self.rows, self.buffer, self.other = n, rows, buffer, other
        self.lives, self.live_other = lives, live_other
        self.z_send, self.z_recv, self.y_send, self.y_recv, self.c_send, self.c_recv = sems
        self.planes = n // 4
        self.me, self.core = lax.axis_index("seq"), lax.axis_index("tp")
        me = self.me
        self.x, self.y, self.z = lax.rem(me, 2), lax.rem(me // 2, 2), me // 4
        self.across = me + 2 - 4 * self.y

    @staticmethod
    def scratch(n):
        dma, planes = pltpu.SemaphoreType.DMA, n // 4
        shapes = [(planes, 2, 2)] * 2 + [(planes, 2)] * 2 + [(2 * planes,)] * 2
        return [dma(shape) for shape in shapes]

    @property
    def events(self):
        return self.planes

    def plane(self, step):
        return lax.rem(self.z + step, self.planes)

    def place(self, plane, lane):
        return plane * 4 + self.y * 2 + lane

    def reached(self):
        return [(step, far) for step in range(self.planes) for far in (0, 1) if step or far]

    def hello(self):
        barrier = pltpu.get_barrier_semaphore()
        partners = [(self.across, self.core), (self.me, 1 - self.core)]
        for step, far in self.reached():
            lane = 1 - self.x if far else self.x
            partners.append((self.place(self.plane(step), lane), self.core))
        for seq, tp in partners:
            pl.semaphore_signal(barrier, inc=1, device_id=(seq, tp), device_id_type=MESH)

    def met(self):
        pl.semaphore_wait(pltpu.get_barrier_semaphore(), 2 + len(self.reached()))

    def rows_of(self, side, seq):
        return self.buffer.at[side, at(seq * self.rows, self.rows), :]

    def block(self, side, pair):
        return self.buffer.at[side, at(pair * 2 * self.rows, 2 * self.rows), :]

    def items(self, pair):
        found = [self.block(self.core, pair)]
        if self.lives is not None:
            found.append(self.lives.at[at(pair * 2, 2)])
        return found

    def each(self, copy, what):
        for index in range(1 if self.lives is None else 2):
            getattr(copy(index), what)()

    def z_copy(self, step, far):
        def copy(index):
            lane = 1 - self.x if far else self.x
            if index == 0:
                source = self.other.at[self.core] if far else self.rows_of(self.core, self.me)
                target = self.rows_of(self.core, self.me)
            else:
                source = self.live_other if far else self.lives.at[self.me]
                target = self.lives.at[self.me]
            return remote(
                source,
                target,
                self.z_send.at[step, far, index],
                self.z_recv.at[step, far, index],
                self.place(self.plane(step), lane),
                self.core,
            )

        return copy

    def y_copy(self, plane, row):
        def copy(index):
            item = self.items(plane * 2 + row)[index]
            return remote(
                item,
                item,
                self.y_send.at[plane, index],
                self.y_recv.at[plane, index],
                self.across,
                self.core,
            )

        return copy

    def c_copy(self, pair, side):
        item = self.block(side, pair)
        return remote(
            item, item, self.c_send.at[pair], self.c_recv.at[pair], self.me, 1 - self.core
        )

    def begin(self):
        for step, far in self.reached():
            self.each(self.z_copy(step, far), "start")

    def arrive(self, event):
        for far in (0, 1) if event else (1,):
            self.each(self.z_copy(event, far), "wait_recv")
        plane = self.plane(self.planes - event)
        self.each(self.y_copy(plane, self.y), "start")
        self.c_copy(plane * 2 + self.y, self.core).start()

    def complete(self, event):
        plane = self.plane(self.planes - event)
        self.each(self.y_copy(plane, 1 - self.y), "wait_recv")
        self.c_copy(plane * 2 + 1 - self.y, self.core).start()

    def ready(self, event):
        plane = self.plane(self.planes - event)
        self.c_copy(plane * 2, 1 - self.core).wait_recv()
        self.c_copy(plane * 2 + 1, 1 - self.core).wait_recv()
        return plane

    def finish(self):
        for step, far in self.reached():
            self.each(self.z_copy(step, far), "wait_send")
        for plane in range(self.planes):
            self.each(self.y_copy(plane, self.y), "wait_send")
        for pair in range(2 * self.planes):
            self.c_copy(pair, self.core).wait_send()


def split_lanes(values, x, buffer, other, start, rows):
    half = values.shape[2] // 2
    zero, one = values[:, 0, :], values[:, 1, :]
    own, far = jnp.where(x == 0, zero, one), jnp.where(x == 0, one, zero)
    core = lax.axis_index("tp")
    own = jnp.where(core == 0, own[:, :half], own[:, half:]).astype(BF16)
    buffer[core, at(start, rows), :] = own
    for side in range(2):
        other[side] = far[:, side * half : (side + 1) * half].astype(BF16)


def gather_and_project(tokens, d_out, live, episode_frames, gain, shift, qkv, bias, fixed, ahead, n):
    rows, lanes, width = tokens.shape
    half = width // 2
    total = n * rows
    chunks = total // FRAME
    per_frame = FRAME // rows
    features = qkv.shape[3]
    slots = episode_frames.shape[1]

    def kernel(*refs):
        refs = list(refs)

        def take(count):
            taken = refs[:count]
            del refs[:count]
            return taken

        tokens_ref, d_ref, live_ref, counts_ref, gain_ref, shift_ref, w_any, bias_ref = take(8)
        fixed_ref, ahead_ref = take(2)
        all_ref, d_all, mask_ref, frames_ref = take(4)
        projected = take(6)
        other, d_other, lives, live_other, weight, full, w_sem = take(7)
        relay = Relay(n, rows, all_ref, other, take(Relay.sems), lives, live_other)
        d_relay = Relay(n, rows, d_all, d_other, take(Relay.sems))
        load = pltpu.make_async_copy(w_any.at[0], weight, w_sem)
        load.start()
        relay.hello()
        x, me = relay.x, relay.me
        split_lanes(tokens_ref[...].astype(F32), x, all_ref, other, me * rows, rows)
        lane = lax.broadcasted_iota(jnp.int32, (1, FRAME), 1)
        here = lane // rows == lax.rem(me, per_frame)
        tiles = []
        for index in range(lanes):
            alive = live_ref[index : index + 1, :].astype(F32)
            alive = jnp.where(here, jnp.concatenate([alive] * per_frame, axis=1), 0.0)
            tiles.append(jnp.broadcast_to(alive, (8, FRAME)))
        lives[me] = jnp.where(x == 0, tiles[0], tiles[1])
        live_other[...] = jnp.where(x == 0, tiles[1], tiles[0])
        relay.met()
        relay.begin()
        split_lanes(d_ref[...], x, d_all, d_other, me * rows, rows)
        d_relay.begin()

        counts = [counts_ref[x, slot] for slot in range(slots)]
        episodes, openings = [], []
        for frame in range(chunks):
            end, episode, opening = 0, 0, 0
            for slot in range(slots):
                end = end + counts[slot]
                passed = frame >= end
                episode = episode + passed.astype(jnp.int32)
                opening = opening + jnp.where(passed, counts[slot], 0)
            episodes.append(episode)
            openings.append(frame - opening)
        for index in range(3):
            table = []
            for frame in range(chunks):
                line = jnp.zeros((1, PAIR), F32)
                for choice in range(chunks):
                    line = jnp.where(
                        openings[frame] == choice, ahead_ref[index, choice : choice + 1, :], line
                    )
                table.append(line)
            frames_ref[index] = jnp.concatenate(
                table + [jnp.zeros((8 - chunks, PAIR), F32)], axis=0
            )
        load.wait()

        def project_frame(frame):
            place = at(frame * FRAME, FRAME)
            stream = jnp.concatenate([all_ref[0, place, :], all_ref[1, place, :]], axis=1)
            project(
                stream.astype(F32),
                frame,
                0,
                me // 2,
                (gain_ref, shift_ref, weight, bias_ref, fixed_ref, frames_ref),
                [ref.at[place, :] for ref in projected],
                full,
            )

        for event in range(relay.events):
            relay.arrive(event)
            if event:
                relay.complete(event - 1)
            if event > 1:
                project_frame(relay.ready(event - 2))
        relay.complete(relay.events - 1)
        for event in range(relay.events):
            d_relay.arrive(event)
            if event:
                d_relay.complete(event - 1)
            if event >= relay.events - 2:
                project_frame(relay.ready(event))
        d_relay.complete(relay.events - 1)
        relay.finish()
        for event in range(relay.events):
            d_relay.ready(event)
        d_relay.finish()

        for key_frame in range(chunks):
            alive = lives[key_frame * per_frame, 0:1, :]
            for part in range(1, per_frame):
                alive = alive + lives[key_frame * per_frame + part, 0:1, :]
            closed = (alive - 1.0) * -MASKED
            lines = []
            for query_frame in range(chunks):
                allowed = (episodes[query_frame] == episodes[key_frame]) & (
                    openings[key_frame] <= openings[query_frame]
                )
                lines.append(jnp.where(allowed, closed, MASKED))
            lines.append(jnp.zeros((PAIR - chunks, FRAME), F32))
            mask_ref[key_frame * FRAME : (key_frame + 1) * FRAME, :] = jnp.concatenate(
                lines, axis=0
            ).T.astype(BF16)

    in_vmem = pl.BlockSpec(memory_space=pltpu.VMEM)
    in_smem = pl.BlockSpec(memory_space=pltpu.SMEM)
    projected = jax.ShapeDtypeStruct((total, features), BF16)
    return pl.pallas_call(
        kernel,
        out_shape=(
            jax.ShapeDtypeStruct((2, total, half), BF16),
            jax.ShapeDtypeStruct((2, total, half), BF16),
            jax.ShapeDtypeStruct((total, PAIR), BF16),
            jax.ShapeDtypeStruct((3, 8, PAIR), F32),
            projected,
            projected,
            projected,
            jax.ShapeDtypeStruct((total, PAIR), BF16),
            jax.ShapeDtypeStruct((total, width), BF16),
            jax.ShapeDtypeStruct((total, PAIR), F32),
        ),
        in_specs=[in_vmem, in_vmem, in_vmem, in_smem, in_vmem, in_vmem, ANYWHERE] + [in_vmem] * 3,
        out_specs=(in_vmem,) * 10,
        scratch_shapes=[
            pltpu.VMEM((2, rows, half), BF16),
            pltpu.VMEM((2, rows, half), BF16),
            pltpu.VMEM((n, 8, FRAME), F32),
            pltpu.VMEM((8, FRAME), F32),
            pltpu.VMEM(qkv.shape[1:], BF16),
            pltpu.VMEM((FRAME, width), BF16),
            pltpu.SemaphoreType.DMA,
        ]
        + Relay.scratch(n) * 2,
        compiler_params=pltpu.CompilerParams(
            collective_id=0, has_side_effects=True, vmem_limit_bytes=VMEM_BYTES
        ),
        name="gather_and_project",
    )(tokens, d_out, live, episode_frames, gain, shift, qkv, bias, fixed, ahead)


def halves(ref):
    return jnp.concatenate([ref[0], ref[1]], axis=1).astype(F32)


def halves_spec(shape, chunks, behind, span=FRAME):
    return pl.BlockSpec(
        (2, span, shape[2]), lambda s: (0, jnp.clip(s - behind, 0, chunks - 1), 0)
    )


def layer_forward(layer, query, key, value, key_bias, stream, mats, rows_of, next_refs, identity):
    total, features = query.shape
    split = stream.ndim == 3
    width = mats[1].shape[1]
    hidden_units = mats[1].shape[2]
    chunks = total // FRAME
    heads = features // HEAD_DIM
    slabs = features // PAIR
    columns = 256
    last = next_refs is None
    b_out, gain, shift, b_up, b_down = rows_of
    mat_out, mat_up, mat_down = mats

    def kernel(*refs):
        refs = list(refs)

        def take(count):
            taken = refs[:count]
            del refs[:count]
            return taken

        q_ref, k_ref, v_ref, kb_ref, x_ref = take(5)
        wo_any, wu_any, wd_any = take(3)
        bo_ref, gain_ref, shift_ref, bu_ref, bd_ref = take(5)
        if not last:
            wq_any, ngain, nshift, nbias, fixed, frames = take(6)
        p_ref, r_ref, mixed_ref, unit_ref, scale_ref, second_ref, act_ref, gp_ref, x_out = take(9)
        if not last:
            next_outs = take(6)
        wo, wu, wd, mid, full, next_full = take(6)
        if not last:
            (wq,) = take(1)
        a_send, a_recv, b_send, b_recv, w_sem, send_sem, recv_sem = take(7)

        step = pl.program_id(0)
        me, core = lax.axis_index("seq"), lax.axis_index("tp")

        items = [(wo_any, wo), (wu_any, wu), (wd_any, wd)]
        if not last:
            items.append((wq_any, wq))

        def load(index):
            source, target = items[index]
            return pltpu.make_async_copy(
                source.at[layer if index < 3 else layer + 1], target, w_sem.at[index]
            )

        def exchange(kind, chunk):
            source, target = ((a_send, a_recv), (b_send, b_recv))[kind]
            return remote(
                source.at[chunk],
                target.at[chunk],
                send_sem.at[kind, chunk],
                recv_sem.at[kind, chunk],
                me,
                1 - core,
            )

        @pl.when(step == 0)
        def _():
            for index in range(len(items)):
                load(index).start()
            hello([(me, 1 - core)])

        lane = lax.broadcasted_iota(jnp.int32, (1, PAIR), 1)
        sides = [(lane < HEAD_DIM).astype(F32).astype(BF16), (lane >= HEAD_DIM).astype(F32).astype(BF16)]
        for frame in range(chunks):

            @pl.when(step == frame)
            def _():
                keys = FRAME * (frame + 1)
                mask = kb_ref[:keys, :]
                asked = jnp.broadcast_to((lane == frame).astype(F32), (FRAME, PAIR)).astype(BF16)

                slab_lanes = [slice(slab * PAIR, (slab + 1) * PAIR) for slab in range(slabs)]

                def score(head):
                    lanes, side = slab_lanes[head // 2], head % 2
                    key = jnp.concatenate([k_ref[:keys, lanes], mask], axis=1)
                    return nt(jnp.concatenate([q_ref[:, lanes] * sides[side], asked], axis=1), key)

                scores, sums = score(0), []
                for head in range(heads):
                    lanes, side = slab_lanes[head // 2], head % 2
                    following = score(head + 1) if head + 1 < heads else None
                    highest = jnp.max(scores, axis=1, keepdims=True)
                    shifted = jnp.exp(scores - highest).astype(BF16)
                    p_ref[0, head, :keys, :] = shifted.T
                    sums.append(nn(shifted, v_ref[:keys, lanes] * sides[side] + sides[1 - side]))
                    scores = following
                    if side == 1:
                        one, two = sums[head - 1 :]
                        low_side = lane < HEAD_DIM
                        divisor = 1.0 / jnp.where(
                            low_side, pltpu.roll(one, HEAD_DIM, 1), pltpu.roll(two, HEAD_DIM, 1)
                        )
                        r_ref[:, lanes] = divisor
                        mixed_ref[:, lanes] = (jnp.where(low_side, one, two) * divisor).astype(BF16)

        @pl.when(step == 0)
        def _():
            load(0).wait()
            met([(me, 1 - core)])

        @pl.when(step < chunks)
        def _():
            a_send[step] = nn(mixed_ref[...], wo[...]).astype(BF16)
            exchange(0, step).start()

        def feed_forward():
            chunk = step - 1
            middle = (halves(x_ref) if split else x_ref[...]) + (
                a_send[chunk].astype(F32) + a_recv[chunk].astype(F32)
            )
            middle = middle + bo_ref[layer : layer + 1, :]
            mid[lax.rem(chunk, 2)] = middle
            unit, scale = normed(middle)
            keep_norm(unit, scale, unit_ref, scale_ref)
            second = (unit * gain_ref[layer : layer + 1, :] + shift_ref[layer : layer + 1, :]).astype(BF16)
            full[...] = second
            second_ref[...] = full[:, at((me // 2) * PAIR, PAIR)]
            parts = [slice(start, start + columns) for start in range(0, hidden_units, columns)]
            hidden = nn(second, wu[:, parts[0]])
            for index, part in enumerate(parts):
                following = nn(second, wu[:, parts[index + 1]]) if index + 1 < len(parts) else None
                act, slope = gelu_both(hidden + bu_ref[layer : layer + 1, part])
                act_ref[:, part] = act.astype(BF16)
                gp_ref[:, part] = slope.astype(BF16)
                hidden = following
            b_send[chunk] = nn(act_ref[...], wd[...]).astype(BF16)

        def close():
            chunk = step - 2
            result = mid[lax.rem(chunk, 2)] + (b_send[chunk].astype(F32) + b_recv[chunk].astype(F32))
            result = result + bd_ref[layer : layer + 1, :]
            x_out[...] = result
            if not last:
                project(
                    result,
                    chunk,
                    layer + 1,
                    me // 2,
                    (ngain, nshift, wq, nbias, fixed, frames),
                    next_outs,
                    next_full,
                )

        @pl.when(step == 1)
        def _():
            load(1).wait()
            load(2).wait()

        @pl.when((step >= 1) & (step <= chunks))
        def _():
            exchange(0, step - 1).wait_recv()
            feed_forward()
            exchange(1, step - 1).start()

        if not last:

            @pl.when(step == 2)
            def _():
                load(3).wait()

        @pl.when(step >= 2)
        def _():
            exchange(1, step - 2).wait_recv()
            close()

        @pl.when(step == chunks + 1)
        def _():
            for kind in range(2):
                for chunk in range(chunks):
                    exchange(kind, chunk).wait_send()

    def rows(columns, behind):
        return pl.BlockSpec(
            (FRAME, columns), lambda s: (jnp.clip(s - behind, 0, chunks - 1), 0)
        )

    in_specs = [rows(features, 0), whole(key), whole(value), whole(key_bias)]
    in_specs += [halves_spec(stream.shape, chunks, 1) if split else rows(width, 1)]
    in_specs += [ANYWHERE] * 3 + [whole(item) for item in rows_of]
    operands = [query, key, value, key_bias, stream, *mats, *rows_of]
    if not last:
        in_specs += [ANYWHERE] + [whole(item) for item in next_refs[1:]]
        operands += list(next_refs)
    out_shape = [
        jax.ShapeDtypeStruct((chunks, heads, total, FRAME), BF16),
        jax.ShapeDtypeStruct((total, features), F32),
        jax.ShapeDtypeStruct((total, features), BF16),
        jax.ShapeDtypeStruct((total, width), BF16),
        jax.ShapeDtypeStruct((total, PAIR), F32),
        jax.ShapeDtypeStruct((total, PAIR), BF16),
        jax.ShapeDtypeStruct((total, hidden_units), BF16),
        jax.ShapeDtypeStruct((total, hidden_units), BF16),
        jax.ShapeDtypeStruct((total, width), F32),
    ]
    out_specs = [
        pl.BlockSpec((1, heads, total, FRAME), lambda s: (jnp.minimum(s, chunks - 1), 0, 0, 0)),
        rows(features, 0),
        rows(features, 0),
        rows(width, 1),
        rows(PAIR, 1),
        rows(PAIR, 1),
        rows(hidden_units, 1),
        rows(hidden_units, 1),
        rows(width, 2),
    ]
    scratch = [
        pltpu.VMEM(mat_out.shape[1:], BF16),
        pltpu.VMEM(mat_up.shape[1:], BF16),
        pltpu.VMEM(mat_down.shape[1:], BF16),
        pltpu.VMEM((2, FRAME, width), F32),
        pltpu.VMEM((FRAME, width), BF16),
        pltpu.VMEM((FRAME, width), BF16),
    ]
    if not last:
        out_shape += [jax.ShapeDtypeStruct((total, features), BF16)] * 3
        out_shape += [jax.ShapeDtypeStruct((total, PAIR), BF16)]
        out_shape += [jax.ShapeDtypeStruct((total, width), BF16)]
        out_shape += [jax.ShapeDtypeStruct((total, PAIR), F32)]
        out_specs += [rows(features, 2)] * 3 + [rows(PAIR, 2), rows(width, 2), rows(PAIR, 2)]
        scratch += [pltpu.VMEM(next_refs[0].shape[1:], BF16)]
    scratch += [pltpu.VMEM((chunks, FRAME, width), BF16)] * 4
    scratch += [
        pltpu.SemaphoreType.DMA((4,)),
        pltpu.SemaphoreType.DMA((2, chunks)),
        pltpu.SemaphoreType.DMA((2, chunks)),
    ]
    return pl.pallas_call(
        kernel,
        grid=(chunks + 2,),
        out_shape=out_shape,
        in_specs=in_specs,
        out_specs=out_specs,
        scratch_shapes=scratch,
        compiler_params=pltpu.CompilerParams(
            collective_id=identity, has_side_effects=True, vmem_limit_bytes=VMEM_BYTES
        ),
        name=f"layer_forward_{layer}",
    )(*operands)


class Swap:
    def __init__(self, ships, lane_rows):
        self.ships, self.lane_rows = ships, lane_rows
        self.count = len(ships) + len(lane_rows)

    def operands(self):
        return [*self.ships, *[item for item, _ in self.lane_rows]]

    def in_specs(self):
        return [whole(item) for item in self.ships] + [ANYWHERE] * len(self.lane_rows)

    def outputs(self):
        shapes, specs = [], []
        for item in self.ships:
            shape = (item.shape[0] // 2, item.shape[1])
            shapes.append(jax.ShapeDtypeStruct(shape, F32))
            specs.append(whole_out(shape))
        for item, count in self.lane_rows:
            shapes.append(jax.ShapeDtypeStruct((count or item.shape[0], item.shape[1]), item.dtype))
            specs.append(ANYWHERE)
        return shapes, specs

    def scratch(self):
        if not self.count:
            return []
        buffers = [pltpu.VMEM((item.shape[0] // 2, item.shape[1]), BF16) for item in self.ships]
        return buffers * 2 + [pltpu.SemaphoreType.DMA((self.count,))] * 2

    def bind(self, sources, targets, scratch):
        ships = len(self.ships)
        me, core = lax.axis_index("seq"), lax.axis_index("tp")
        x = lax.rem(me, 2)
        beside = me + 1 - 2 * x
        half = PAIR // 2

        def copy(index):
            if index < ships:
                source, target = scratch[index], scratch[ships + index]
            else:
                source, target = sources[index], targets[index]
                count = self.lane_rows[index - ships][1]
                if count:
                    source = source.at[at(beside * count, count), :]
            send, recv = scratch[2 * ships].at[index], scratch[2 * ships + 1].at[index]
            return remote(source, target, send, recv, beside, core)

        def start():
            for index in range(self.count):
                if index < ships:
                    scratch[index][...] = sources[index][at((1 - x) * half, half), :].astype(BF16)
                copy(index).start()

        def finish():
            for index in range(self.count):
                copy(index).wait_recv()
                if index < ships:
                    own = sources[index][at(x * half, half), :]
                    targets[index][...] = own + scratch[ships + index][...].astype(F32)
            for index in range(self.count):
                copy(index).wait_send()

        return start, finish


def attention_backward(
    probs, divisor, mixed, query, key, value, grad_mixed, first, fixed, frames, swap, swap_qkv, identity
):
    total, features = query.shape
    chunks = total // FRAME
    slabs = features // PAIR
    half = PAIR // 2

    def kernel(*refs):
        refs = list(refs)

        def take(count):
            taken = refs[:count]
            del refs[:count]
            return taken

        p_ref, r_ref, o_ref, q_ref, k_ref, v_ref, g_ref, first_ref, fixed_ref, frames_ref = take(10)
        sources = take(swap.count)
        dq_ref, dk_ref, dv_ref, qkv_out = take(4)
        targets = take(swap.count)
        dk_sum, dv_sum, first_turned = take(3)
        if swap_qkv:
            qkv_own, qkv_send, qkv_recv, qkv_sems = take(4)
        start, finish = swap.bind(sources, targets, refs)

        step = pl.program_id(0)
        me, core = lax.axis_index("seq"), lax.axis_index("tp")
        x = lax.rem(me, 2)
        beside = me + 1 - 2 * x

        def qkv_copy(slab):
            return remote(
                qkv_send.at[slab],
                qkv_recv.at[slab],
                qkv_sems.at[0, slab],
                qkv_sems.at[1, slab],
                beside,
                core,
            )

        @pl.when(step == 0)
        def _():
            hello([(beside, core)])
            first_turned[...] = first_ref[...].T
            met([(beside, core)])
            start()

        lane = lax.broadcasted_iota(jnp.int32, (1, PAIR), 1)
        sides = [(lane < HEAD_DIM).astype(F32).astype(BF16), (lane >= HEAD_DIM).astype(F32).astype(BF16)]
        turned = k_ref[...].T
        ones = jnp.broadcast_to((lane < 2).astype(F32), (total, PAIR)).astype(BF16)
        values = jnp.concatenate([v_ref[...], ones], axis=1)

        def give(frame):
            keys = FRAME * (frame + 1)
            own = slice(frame * FRAME, keys)
            scaled = (g_ref[own, :].astype(F32) * r_ref[own, :]).astype(BF16)
            inner = scaled.astype(F32) * o_ref[own, :].astype(F32)
            grads, q_parts, g_parts = [], [], []
            for side in range(2):
                delta = jnp.sum(
                    jnp.where((lane < HEAD_DIM) == (side == 0), inner, 0.0), axis=1, keepdims=True
                )
                coarse = delta.astype(BF16).astype(F32)
                rest = jnp.where(lane == 0, -coarse, jnp.where(lane == 1, coarse - delta, 0.0))
                g2 = scaled * sides[side]
                grads.append(nt(values[:keys], jnp.concatenate([g2, rest.astype(BF16)], axis=1)))
                q_parts.append(q_ref[own, :] * sides[side])
                g_parts.append(g2)
            return grads, jnp.concatenate(q_parts, axis=0), jnp.concatenate(g_parts, axis=0)

        given = give(chunks - 1)
        for frame in reversed(range(chunks)):
            keys = FRAME * (frame + 1)
            own = slice(frame * FRAME, keys)
            tables = tables_of(fixed_ref, frames_ref, frame)
            grads, q_part, g_part = given
            given = give(frame - 1) if frame else None
            query_parts, score_parts, prob_parts = [], [], []
            for side in range(2):
                attention = p_ref[frame, side, :keys, :]
                grad_scores = (attention.astype(F32) * grads[side]).astype(BF16)
                query_parts.append(nn(turned[side * HEAD_DIM : (side + 1) * HEAD_DIM, :keys], grad_scores))
                score_parts.append(grad_scores)
                prob_parts.append(attention)
            grad_query = jnp.concatenate(query_parts, axis=0).T
            key_parts = nn(jnp.concatenate(score_parts, axis=1), q_part)
            value_parts = nn(jnp.concatenate(prob_parts, axis=1), g_part)
            dq_ref[own, :] = (turn(grad_query, tables, True) * SCORE_SCALE).astype(BF16)
            if frame == chunks - 1:
                dk_sum[...] = key_parts
                dv_sum[...] = value_parts
            else:
                dk_sum[:keys, :] += key_parts
                dv_sum[:keys, :] += value_parts
            dk_ref[own, :] = turn(dk_sum[own, :], tables, True).astype(BF16)
            dv_ref[own, :] = dv_sum[own, :].astype(BF16)

        for part, ref in enumerate((dq_ref, dk_ref, dv_ref)):
            piece = slice(part * PAIR, (part + 1) * PAIR)
            terms = nn(first_turned[...], ref[...])
            if swap_qkv:
                qkv_own[step, :, piece] = terms
                qkv_send[step, :, piece] = qkv_own[step, at((1 - x) * half, half), piece].astype(BF16)
            else:
                qkv_out[:, at(part * features + step * PAIR, PAIR)] = terms
        if swap_qkv:
            qkv_copy(step).start()

        @pl.when(step == slabs - 1)
        def _():
            finish()
            for slab in range(slabs if swap_qkv else 0):
                qkv_copy(slab).wait_recv()
                for part in range(3):
                    piece = slice(part * PAIR, (part + 1) * PAIR)
                    place = part * features + slab * PAIR
                    qkv_out[:, place : place + PAIR] = qkv_own[
                        slab, at(x * half, half), piece
                    ] + qkv_recv[slab, :, piece].astype(F32)
            for slab in range(slabs if swap_qkv else 0):
                qkv_copy(slab).wait_send()

    slab = pl.BlockSpec((total, PAIR), lambda s: (0, s))
    in_specs = [pl.BlockSpec((chunks, 2, total, FRAME), lambda s: (0, s, 0, 0))]
    in_specs += [slab] * 6 + [whole(first), whole(fixed), whole(frames)]
    in_specs += swap.in_specs()
    qkv_shape = (half if swap_qkv else PAIR, 3 * features)
    shapes, specs = swap.outputs()
    out_shape = [jax.ShapeDtypeStruct((total, features), BF16)] * 3
    out_shape += [jax.ShapeDtypeStruct(qkv_shape, F32)] + shapes
    out_specs = [slab] * 3 + [whole_out(qkv_shape)] + specs
    scratch = [pltpu.VMEM((total, PAIR), F32)] * 2 + [pltpu.VMEM((PAIR, total), BF16)]
    if swap_qkv:
        scratch += [pltpu.VMEM((slabs, PAIR, 3 * PAIR), F32)]
        scratch += [pltpu.VMEM((slabs, half, 3 * PAIR), BF16)] * 2
        scratch += [pltpu.SemaphoreType.DMA((2, slabs))]
    scratch += swap.scratch()
    return pl.pallas_call(
        kernel,
        grid=(slabs,),
        out_shape=out_shape,
        in_specs=in_specs,
        out_specs=out_specs,
        scratch_shapes=scratch,
        compiler_params=pltpu.CompilerParams(
            collective_id=identity, has_side_effects=True, vmem_limit_bytes=VMEM_BYTES
        ),
        name=f"attention_backward_{identity}",
    )(
        probs,
        divisor,
        mixed,
        query,
        key,
        value,
        grad_mixed,
        first,
        fixed,
        frames,
        *swap.operands(),
    )


def rows_backward(entry, upper, identity, span, swap):
    top, bottom = len(entry) == 1, upper is None
    if not top:
        above, entry = entry[0], entry[1:]
    total = entry[0].shape[1] if top else entry[0].shape[0]
    chunks = total // span
    columns = 256
    ahead = 0 if top else 2 if bottom else 1
    if top:
        width = 2 * entry[0].shape[2]
    else:
        features, width = entry[0].shape[1], entry[5].shape[1]
    if not bottom:
        layer = upper[0]
        hidden_units, mixed_features = upper[1].shape[1], upper[6].shape[1]
    place_rows = total // lax.axis_size("seq")

    def kernel(*refs):
        refs = list(refs)

        def take(count):
            taken = refs[:count]
            del refs[:count]
            return taken

        if top:
            (d_out_ref,) = take(1)
        else:
            dq_ref, dk_ref, dv_ref, unit1, scale1, dm_ref, wq, gain1 = take(8)
        if not bottom:
            act_ref, gp_ref, unit2, scale2, second_ref, mixed_ref = take(6)
            wo_any, wu_any, wd_any, gain2 = take(4)
        sources = take(swap.count)
        if not top:
            (vec1,) = take(1)
        if not bottom:
            dmid_out, dmix_out, out_sum, up_sum, down_sum, vec2 = take(6)
        else:
            dx_out, dx_other, vec_other = take(3)
        targets = take(swap.count)
        if not top:
            a_send, a_recv = take(2)
        if not bottom:
            b_send, b_recv, grad_keep, hidden_keep, low_keep, last_keep, wo, wu, wd, w_sem = take(10)
        else:
            dx_keep, dx_send, dx_recv, vec_recv, x_send_sem, x_recv_sem = take(6)
        send_sem, recv_sem = take(2)
        start_swap, finish_swap = swap.bind(sources, targets, refs)

        step = pl.program_id(0)
        me, core = lax.axis_index("seq"), lax.axis_index("tp")
        pair = at((me // 2) * PAIR, PAIR)
        x = lax.rem(me, 2)
        beside = me + 1 - 2 * x

        def exchange(kind, chunk):
            source, target = (a_send, a_recv) if kind == 0 else (b_send, b_recv)
            return remote(
                source.at[chunk],
                target.at[chunk],
                send_sem.at[kind, chunk],
                recv_sem.at[kind, chunk],
                me,
                1 - core,
            )

        def load(index):
            source, target = ((wd_any, wd), (wu_any, wu), (wo_any, wo))[index]
            return pltpu.make_async_copy(source.at[layer], target, w_sem.at[index])

        partners = [(me, 1 - core)] + ([(beside, core)] if bottom or swap.count else [])

        @pl.when(step == 0)
        def _():
            if not bottom:
                for index in range(3):
                    load(index).start()
                out_sum[...] = jnp.zeros_like(out_sum)
                up_sum[...] = jnp.zeros_like(up_sum)
                down_sum[...] = jnp.zeros_like(down_sum)
                vec2[...] = jnp.zeros_like(vec2)
            if not top:
                vec1[...] = jnp.zeros_like(vec1)
            hello(partners)

        def meet():
            @pl.when(step == 0)
            def _():
                met(partners)
                start_swap()

        def entry_products():
            partial = None
            for part, ref in enumerate((dq_ref, dk_ref, dv_ref)):
                grad = ref[...]
                term = nt(grad, wq[0, part])
                partial = term if partial is None else partial + term
                vec1[part : part + 1, :] += column_sum(grad.astype(F32))
            a_send[step] = partial.astype(BF16)

        def entry_norm(chunk):
            if top:
                return halves(d_out_ref)
            grad_first = a_send[chunk].astype(F32) + a_recv[chunk].astype(F32)
            unit, scale = kept_norm(unit1, scale1)
            for start, sums in ((3, column_sum(grad_first * unit)), (5, column_sum(grad_first))):
                for side in range(width // features):
                    piece = slice(side * features, (side + 1) * features)
                    vec1[start + side : start + side + 1, :] += sums[:, piece]
            return dm_ref[...] + norm_pull(grad_first, gain1[above : above + 1, :], unit, scale)

        def feed_forward(between=None):
            chunk = step - ahead
            gradient = entry_norm(chunk)
            if bottom:
                dx_keep[at(chunk * span, span), :] = gradient
                return
            grad_keep[lax.rem(chunk, 2)] = gradient
            vec2[1:2, :width] += column_sum(gradient)
            low = gradient.astype(BF16)
            low_keep[...] = low
            low_columns = low_keep[:, pair]
            second = second_ref[...]
            parts = [slice(start, start + columns) for start in range(0, hidden_units, columns)]
            grad_act = nt(low, wd[parts[0], :])
            for index, part in enumerate(parts):
                following = nt(low, wd[parts[index + 1], :]) if index + 1 < len(parts) else None
                grad_hidden = grad_act * gp_ref[:, part].astype(F32)
                hidden_keep[:, part] = grad_hidden.astype(BF16)
                vec2[0:1, part] += column_sum(grad_hidden)
                grad_act = following
            if between is not None:
                between()
            b_send[chunk] = nt(hidden_keep[...], wu[...]).astype(BF16)
            down_sum[...] += tn(low_columns, act_ref[...])
            up_sum[...] += tn(second, hidden_keep[...])

        def close():
            chunk = step - ahead - 1
            grad_second = b_send[chunk].astype(F32) + b_recv[chunk].astype(F32)
            unit, scale = kept_norm(unit2, scale2)
            vec2[2:3, :width] += column_sum(grad_second * unit)
            vec2[3:4, :width] += column_sum(grad_second)
            grad_middle = grad_keep[lax.rem(chunk, 2)] + norm_pull(
                grad_second, gain2[layer : layer + 1, :], unit, scale
            )
            dmid_out[...] = grad_middle
            vec2[4:5, :width] += column_sum(grad_middle)
            low = grad_middle.astype(BF16)
            last_keep[...] = low
            out_sum[...] += tn(last_keep[:, pair], mixed_ref[...])
            dmix_out[...] = nt(low, wo[...]).astype(BF16)

        if not top:

            @pl.when(step < chunks)
            def _():
                entry_products()
                meet()
                exchange(0, step).start()

        @pl.when((step >= ahead) & (step < chunks + ahead))
        def _():
            if not top:
                exchange(0, step - ahead).wait_recv()
            if not bottom:

                @pl.when(step == ahead)
                def _():
                    load(0).wait()

            feed_forward(lambda: pl.when(step == ahead)(lambda: load(1).wait()))
            if not bottom:
                if top:
                    meet()
                exchange(1, step - ahead).start()

        if not bottom:

            @pl.when(step == ahead + 1)
            def _():
                load(2).wait()

            @pl.when(step >= ahead + 1)
            def _():
                exchange(1, step - ahead - 1).wait_recv()
                close()

        if bottom:

            def x_copy(index):
                source, target = ((dx_send, dx_recv), (vec1, vec_recv))[index]
                return remote(
                    source, target, x_send_sem.at[index], x_recv_sem.at[index], beside, core
                )

            @pl.when(step == chunks + 1)
            def _():
                dx_send[...] = dx_keep[at(beside * place_rows, place_rows), :].astype(BF16)
                x_copy(0).start()
                x_copy(1).start()
                dx_out[...] = dx_keep[at(me * place_rows, place_rows), :]
                x_copy(0).wait_recv()
                x_copy(1).wait_recv()
                dx_other[...] = dx_recv[...].astype(F32)
                vec_other[...] = vec_recv[...]
                x_copy(0).wait_send()
                x_copy(1).wait_send()

        @pl.when(step == pl.num_programs(0) - 1)
        def _():
            for kind in ([] if top else [0]) + ([] if bottom else [1]):
                for chunk in range(chunks):
                    exchange(kind, chunk).wait_send()
            finish_swap()

    def rows(columns, behind):
        return pl.BlockSpec(
            (span, columns), lambda s: (jnp.clip(s - behind, 0, chunks - 1), 0)
        )

    vec = jax.ShapeDtypeStruct((8, VEC), F32)
    operands, in_specs, out_shape, out_specs, scratch = [], [], [], [], []
    if top:
        operands += list(entry)
        in_specs += [halves_spec(entry[0].shape, chunks, 0, span)]
    else:
        operands += list(entry)
        in_specs += [rows(features, 0)] * 3
        in_specs += [rows(width, ahead), rows(PAIR, ahead), rows(width, ahead)]
        in_specs += [
            pl.BlockSpec(
                (1, *entry[6].shape[1:]),
                lambda s: (above, 0, 0, 0),
                pipeline_mode=pl.Buffered(1),
            ),
            whole(entry[7]),
        ]
        narrow = jax.ShapeDtypeStruct((8, features), F32)
        out_shape += [narrow]
        out_specs += [whole_out((8, features))]
        scratch += [pltpu.VMEM((chunks, span, width), BF16)] * 2
    if not bottom:
        operands += list(upper[1:])
        in_specs += [rows(hidden_units, ahead)] * 2
        in_specs += [rows(width, ahead + 1), rows(PAIR, ahead + 1), rows(PAIR, ahead)]
        in_specs += [rows(mixed_features, ahead + 1)] + [ANYWHERE] * 3 + [whole(upper[10])]
        sums = [mixed_features, hidden_units, hidden_units]
        out_shape += [
            jax.ShapeDtypeStruct((total, width), F32),
            jax.ShapeDtypeStruct((total, mixed_features), BF16),
        ]
        out_shape += [jax.ShapeDtypeStruct((PAIR, size), F32) for size in sums] + [vec]
        out_specs += [rows(width, ahead + 1), rows(mixed_features, ahead + 1)]
        out_specs += [whole_out((PAIR, size)) for size in sums] + [whole_out((8, VEC))]
        scratch += [pltpu.VMEM((chunks, span, width), BF16)] * 2
        scratch += [
            pltpu.VMEM((2, span, width), F32),
            pltpu.VMEM((span, hidden_units), BF16),
            pltpu.VMEM((span, width), BF16),
            pltpu.VMEM((span, width), BF16),
            pltpu.VMEM(upper[7].shape[1:], BF16),
            pltpu.VMEM(upper[8].shape[1:], BF16),
            pltpu.VMEM(upper[9].shape[1:], BF16),
            pltpu.SemaphoreType.DMA((3,)),
        ]
    else:
        out_shape += [
            jax.ShapeDtypeStruct((place_rows, width), F32),
            jax.ShapeDtypeStruct((place_rows, width), F32),
            narrow,
        ]
        out_specs += [whole_out((place_rows, width))] * 2 + [whole_out((8, features))]
        scratch += [
            pltpu.VMEM((total, width), F32),
            pltpu.VMEM((place_rows, width), BF16),
            pltpu.VMEM((place_rows, width), BF16),
            pltpu.VMEM((8, features), F32),
            pltpu.SemaphoreType.DMA((2,)),
            pltpu.SemaphoreType.DMA((2,)),
        ]
    scratch += [pltpu.SemaphoreType.DMA((2, chunks))] * 2
    operands += swap.operands()
    in_specs += swap.in_specs()
    shapes, specs = swap.outputs()
    out_shape += shapes
    out_specs += specs
    scratch += swap.scratch()
    return pl.pallas_call(
        kernel,
        grid=(chunks + (1 if top else 2),),
        out_shape=out_shape,
        in_specs=in_specs,
        out_specs=out_specs,
        scratch_shapes=scratch,
        compiler_params=pltpu.CompilerParams(
            collective_id=identity, has_side_effects=True, vmem_limit_bytes=VMEM_BYTES
        ),
        name=f"rows_backward_{identity}",
    )(*operands)


def assemble(sums, vecs, lanes, n, features, hidden_units):
    place = lanes[1].shape[0]
    width = lanes[1].shape[1]
    half = PAIR // 2

    def kernel(*refs):
        refs = list(refs)

        def take(count):
            taken = refs[:count]
            del refs[:count]
            return taken

        qkvs, outs, ups, downs = take(LAYERS), take(LAYERS), take(LAYERS), take(LAYERS)
        vec_refs = [take(4) for _ in range(LAYERS)]
        out_lane, out_other, dx_own, dx_other = take(4)
        out_ref, dx_ref, gain1, shift1, g_qkv, b_qkv, g_out, b_out = take(8)
        gain2, shift2, g_up, b_up, g_down, b_down = take(6)
        out_own, sem, up_keep, down_keep, out_keep, qkv_keep, sems = refs
        me = lax.axis_index("seq")
        x = lax.rem(me, 2)
        fetch = pltpu.make_async_copy(out_lane.at[at(me * place, place), :], out_own, sem)
        fetch.start()
        jobs = []
        for layer in range(LAYERS):
            for ref, through, target in ((ups, up_keep, g_up), (downs, down_keep, g_down), (outs, out_keep, g_out)):
                jobs.append(((ref[layer], through.at[layer]), (through.at[layer], target.at[layer])))
            for part in range(3):
                source = qkvs[layer].at[:, part * features : (part + 1) * features]
                through = qkv_keep.at[layer, part]
                jobs.append(((source, through), (through, g_qkv.at[layer, part])))

        def move(index, way):
            source, target = jobs[index][way]
            return pltpu.make_async_copy(source, target, sems.at[way, index])

        for index in range(len(jobs)):
            move(index, 0).start()
        for index in range(len(jobs)):
            move(index, 0).wait()
            move(index, 1).start()

        for layer, (entry_own, entry_other, upper_own, upper_other) in enumerate(vec_refs):
            line = slice(layer, layer + 1)
            for part in range(3):
                row = slice(part, part + 1)
                b_qkv[part, line, :] = entry_own[row, :] + entry_other[row, :]
            b_up[line, :] = upper_own[0:1, :hidden_units] + upper_other[0:1, :hidden_units]

            def owned(mine, other, row):
                wide = mine.shape[1]
                place = (me // 2) * PAIR
                pair = at(lax.rem(place, wide), PAIR)
                both = mine[row : row + 1, pair] + other[row : row + 1, pair]
                for later in range(1, width // wide):
                    line = slice(row + later, row + later + 1)
                    both = jnp.where(place // wide == later, mine[line, pair] + other[line, pair], both)
                return jnp.where(x == 0, both[:, :half], both[:, half:])

            gain1[line, :] = owned(entry_own, entry_other, 3)
            shift1[line, :] = owned(entry_own, entry_other, 5)
            b_down[line, :] = owned(upper_own, upper_other, 1)
            gain2[line, :] = owned(upper_own, upper_other, 2)
            shift2[line, :] = owned(upper_own, upper_other, 3)
            b_out[line, :] = owned(upper_own, upper_other, 4)

        def both_lanes(target, mine, other):
            target[:, 0, :] = jnp.where(x == 0, mine, other)
            target[:, 1, :] = jnp.where(x == 0, other, mine)

        both_lanes(dx_ref, dx_own[...], dx_other[...])
        fetch.wait()
        both_lanes(out_ref, out_own[...], out_other[...])
        for index in range(len(jobs)):
            move(index, 1).wait()

    def f32(*shape):
        return jax.ShapeDtypeStruct(shape, F32)

    in_vmem = pl.BlockSpec(memory_space=pltpu.VMEM)
    flat = []
    for kind in range(4):
        flat += [sums[layer][kind] for layer in range(LAYERS)]
    parts = len(flat)
    for layer in range(LAYERS):
        flat += list(vecs[layer])
    flat += list(lanes)
    small = f32(LAYERS, width // n)
    return pl.pallas_call(
        kernel,
        out_shape=(
            f32(place, 2, width),
            f32(place, 2, width),
            small,
            small,
            f32(LAYERS, 3, half, features),
            f32(3, LAYERS, features),
            f32(LAYERS, half, features),
            small,
            small,
            small,
            f32(LAYERS, half, hidden_units),
            f32(LAYERS, hidden_units),
            f32(LAYERS, half, hidden_units),
            small,
        ),
        in_specs=[ANYWHERE] * parts + [in_vmem] * (4 * LAYERS) + [ANYWHERE] + [in_vmem] * 3,
        out_specs=tuple(ANYWHERE if index in (4, 6, 10, 12) else in_vmem for index in range(14)),
        scratch_shapes=[
            pltpu.VMEM((place, width), F32),
            pltpu.SemaphoreType.DMA,
            pltpu.VMEM((LAYERS, half, hidden_units), F32),
            pltpu.VMEM((LAYERS, half, hidden_units), F32),
            pltpu.VMEM((LAYERS, half, features), F32),
            pltpu.VMEM((LAYERS, 3, half, features), F32),
            pltpu.SemaphoreType.DMA((2, 6 * LAYERS)),
        ],
        compiler_params=pltpu.CompilerParams(vmem_limit_bytes=VMEM_BYTES),
        name="assemble",
    )(*flat)


def per_chip(
    tokens,
    d_out,
    norm1_gain,
    norm1_shift,
    w_qkv,
    b_qkv,
    w_out,
    b_out,
    norm2_gain,
    norm2_shift,
    w_up,
    b_up,
    w_down,
    b_down,
    episode_frames,
    live,
):
    n = lax.axis_size("seq")
    rows = tokens.shape[0]
    features = w_qkv.shape[3]
    fixed, ahead = turn_constants(rows * n // FRAME)
    qkv, qkv_bias = w_qkv.transpose(0, 2, 1, 3), b_qkv.transpose(1, 0, 2)

    gathered, d_lane, key_bias, frames, *projected = gather_and_project(
        tokens, d_out, live.T, episode_frames, norm1_gain, norm1_shift, qkv, qkv_bias, fixed, ahead, n
    )
    streams, kept = [gathered], []
    for layer in range(LAYERS):
        following = None
        if layer + 1 < LAYERS:
            following = (qkv, norm1_gain, norm1_shift, qkv_bias, fixed, frames)
        results = layer_forward(
            layer,
            *projected[:3],
            key_bias,
            streams[layer],
            (w_out, w_up, w_down),
            (b_out, norm2_gain, norm2_shift, b_up, b_down),
            following,
            1 + layer,
        )
        kept.append((*projected, *results[:8]))
        streams.append(results[8])
        if following is not None:
            projected = results[9:15]

    sums = [[None] * 4 for _ in range(LAYERS)]
    vecs = [[None] * 4 for _ in range(LAYERS)]
    entry, later = (d_lane,), None
    for layer in reversed(range(LAYERS)):
        query, key, value, first, unit1, scale1, probs, divisor, mixed = kept[layer][:9]
        unit2, scale2, second, act, slope = kept[layer][9:]
        upper = (
            layer,
            act,
            slope,
            unit2,
            scale2,
            second,
            mixed,
            w_out,
            w_up,
            w_down,
            norm2_gain,
        )
        identity = 1 + LAYERS + 2 * (LAYERS - 1 - layer)
        if later is None:
            results = rows_backward(entry, upper, identity, FRAME, Swap([], []))
        else:
            swap = Swap(later[:2], [(later[2], 0), (streams[LAYERS], rows)])
            vec1, *results = rows_backward(entry, upper, identity, FRAME, swap)
            results, swapped = results[:6], results[6:]
            sums[layer + 1][3], sums[layer + 1][0] = swapped[:2]
            vecs[layer + 1][3], out_other = swapped[2:]
            vecs[layer + 1][0] = vec1
        grad_middle, grad_mixed, out_sum, up_sum, down_sum, vec2 = results
        vecs[layer][2] = vec2
        last = layer == 0
        if last:
            swap = Swap([out_sum, up_sum], [(vec2, 0), (vecs[layer + 1][0], 0)])
        else:
            swap = Swap([out_sum, up_sum], [])
        results = attention_backward(
            probs,
            divisor,
            mixed,
            query,
            key,
            value,
            grad_mixed,
            first,
            fixed,
            frames,
            swap,
            last,
            identity + 1,
        )
        grad_query, grad_key, grad_value, qkv_sum = results[:4]
        if last:
            sums[layer][:3] = [qkv_sum, *results[4:6]]
            vecs[layer][3], vecs[layer + 1][1] = results[6:8]
        else:
            sums[layer][1:3] = results[4:6]
            later = [down_sum, qkv_sum, vec2]
        entry = (
            layer,
            grad_query,
            grad_key,
            grad_value,
            unit1,
            scale1,
            grad_middle,
            qkv,
            norm1_gain,
        )
    vec1, dx_own, dx_other, vec_other, sums[0][3] = rows_backward(
        entry, None, 1 + 3 * LAYERS, FRAME, Swap([down_sum], [])
    )
    vecs[0][:2] = [vec1, vec_other]
    results = list(
        assemble(
            sums,
            vecs,
            (streams[LAYERS], out_other, dx_own, dx_other),
            n,
            features,
            w_up.shape[2],
        )
    )
    results[4] = results[4].transpose(0, 2, 1, 3)
    results[5] = results[5].transpose(1, 0, 2)
    results[6] = results[6].transpose(0, 2, 1)
    results[12] = results[12].transpose(0, 2, 1)
    return tuple(results)


def lane_fits(mesh, tokens):
    n = mesh.shape["seq"]
    positions, lanes, width = tokens.shape
    rows = positions // n
    return (
        lanes == 2
        and n % 4 == 0
        and positions <= 4 * FRAME
        and positions % FRAME == 0
        and FRAME % rows == 0
        and width // n * 2 == PAIR
        and mesh.shape["tp"] == 2
    )


def solution(mesh):
    placed = (
        P("seq", None, None),
        P("seq", None, None),
        P(),
        P(),
        P(None, None, None, "tp"),
        P(None, None, "tp"),
        P(None, "tp", None),
        P(),
        P(),
        P(),
        P(None, None, "tp"),
        P(None, "tp"),
        P(None, "tp", None),
        P(),
        P(),
        P("seq", None),
    )
    def mapped(body):
        return jax.shard_map(
            body,
            mesh=mesh,
            in_specs=placed,
            out_specs=(
                P("seq", None, None),
                P("seq", None, None),
                P(None, "seq"),
                P(None, "seq"),
                P(None, "seq", None, "tp"),
                P(None, None, "tp"),
                P(None, "tp", "seq"),
                P(None, "seq"),
                P(None, "seq"),
                P(None, "seq"),
                P(None, "seq", "tp"),
                P(None, "tp"),
                P(None, "tp", "seq"),
                P(None, "seq"),
            ),
            check_vma=False,
        )

    def run(tokens, *others):
        if lane_fits(mesh, tokens):
            return mapped(per_chip)(tokens, *others)
        return mapped(per_device)(tokens, *others)

    return run
```

```python
import math

import jax
import jax.numpy as jnp
import numpy as np
from jax import lax
from jax.experimental import pallas as pl
from jax.experimental.pallas import tpu as pltpu
from jax.sharding import PartitionSpec as P

HEAD_DIM = 64
GRID = 16
FRAME = 256
LAYERS = 2
MICRO = 2


EPSILON = 1e-06
MASKED = -1e30
SCORE_SCALE = 0.125


def layer_norm(stream, norm_gain, norm_shift):
    center = stream - jnp.mean(stream, axis=-1, keepdims=True)
    spread = jnp.mean(center * center, axis=-1, keepdims=True)
    return center * lax.rsqrt(spread + EPSILON) * norm_gain + norm_shift


def rotate(values, frame_place, row_place, column_place):
    frequency = jnp.exp(jnp.arange(10, dtype=jnp.float32) * (-math.log(10000.0) / 10.0))
    pieces = []
    for section, place in enumerate((frame_place, row_place, column_place)):
        lower = values[..., 20 * section : 20 * section + 10]
        upper = values[..., 20 * section + 10 : 20 * section + 20]
        angles = place.astype(jnp.float32)[..., None, None] * frequency
        cosine = jnp.cos(angles)
        sine_part = jnp.sin(angles)
        pieces.append(lower * cosine - upper * sine_part)
        pieces.append(lower * sine_part + upper * cosine)
    pieces.append(values[..., 60:])
    return jnp.concatenate(pieces, axis=-1)


def episode_tags(frame_counts, positions):
    endings = jnp.cumsum(frame_counts) * FRAME
    passed = (positions[:, None] >= endings[None, :]).astype(jnp.int32)
    episode = jnp.sum(passed, axis=1)
    opening = jnp.sum(passed * frame_counts[None, :], axis=1)
    frame_index = positions // FRAME - opening
    within = positions % FRAME
    return (episode, frame_index, within // GRID, within % GRID)


def gelu_exact(values):
    return jax.nn.gelu(values, approximate=False)


def sum_heads(partial_sum):
    return lax.psum(partial_sum.astype(jnp.bfloat16), "tp").astype(jnp.float32)


def sum_inputs(partial_sum):
    return lax.psum(partial_sum.astype(jnp.bfloat16), "tp").astype(jnp.float32)


def lane_scores(query, keys_all, lane_index, query_tags, key_tags):
    head_count = query.shape[2] // HEAD_DIM
    query_lane = lax.dynamic_index_in_dim(query, lane_index, 1, False).reshape(
        query.shape[0], head_count, HEAD_DIM
    )
    keys_lane = lax.dynamic_index_in_dim(keys_all, lane_index, 1, False).reshape(
        keys_all.shape[0], head_count, HEAD_DIM
    )
    query_episode, query_frame = [
        lax.dynamic_index_in_dim(item, lane_index, 1, False) for item in query_tags
    ]
    key_episode, key_frame, key_live = [
        lax.dynamic_index_in_dim(item, lane_index, 1, False) for item in key_tags
    ]
    allowed = (
        (query_episode[:, None] == key_episode[None, :])
        & (key_frame[None, :] <= query_frame[:, None])
        & (key_live[None, :] > 0)
    )
    scores = (
        jnp.einsum("qhd,khd->hqk", query_lane, keys_lane, preferred_element_type=jnp.float32)
        * SCORE_SCALE
    )
    return (jnp.where(allowed[None], scores, MASKED), query_lane, keys_lane)


def attend_forward(query, keys_all, values_all, query_tags, key_tags):
    rows_dev, lane_count, features = query.shape
    head_count = features // HEAD_DIM

    def one_lane(lane_index, carry):
        scores, query_lane, keys_lane = lane_scores(
            query, keys_all, lane_index, query_tags, key_tags
        )
        highest = jnp.max(scores, axis=-1, keepdims=True)
        shifted = jnp.exp(scores - highest)
        summed = jnp.sum(shifted, axis=-1, keepdims=True)
        attention = (shifted / summed).astype(jnp.bfloat16)
        values_lane = lax.dynamic_index_in_dim(values_all, lane_index, 1, False).reshape(
            values_all.shape[0], head_count, HEAD_DIM
        )
        result = jnp.einsum(
            "hqk,khd->qhd", attention, values_lane, preferred_element_type=jnp.float32
        ).reshape(rows_dev, 1, features)
        log_total = (highest + jnp.log(summed))[None, :, :, 0]
        return (result, log_total)

    initial = (
        jnp.zeros((rows_dev, lane_count, features), jnp.float32),
        jnp.zeros((lane_count, head_count, rows_dev), jnp.float32),
    )
    return lax.fori_loop(0, lane_count, one_lane, initial)


def attend_backward(query, keys_all, values_all, log_total, grad_mixed, query_tags, key_tags):
    rows_dev, lane_count, features = query.shape
    head_count = features // HEAD_DIM
    key_rows = keys_all.shape[0]

    def one_lane(lane_index, carry):
        scores, query_lane, keys_lane = lane_scores(
            query, keys_all, lane_index, query_tags, key_tags
        )
        values_lane = lax.dynamic_index_in_dim(values_all, lane_index, 1, False).reshape(
            key_rows, head_count, HEAD_DIM
        )
        grad_lane = lax.dynamic_index_in_dim(grad_mixed, lane_index, 1, False).reshape(
            rows_dev, head_count, HEAD_DIM
        )
        attention = jnp.exp(
            scores - lax.dynamic_index_in_dim(log_total, lane_index, 0, False)[:, :, None]
        )
        grad_attention = jnp.einsum(
            "qhd,khd->hqk", grad_lane, values_lane, preferred_element_type=jnp.float32
        )
        inner = jnp.sum(attention * grad_attention, axis=-1, keepdims=True)
        grad_scores = (attention * (grad_attention - inner)).astype(jnp.bfloat16)
        query_part = (
            jnp.einsum("hqk,khd->qhd", grad_scores, keys_lane, preferred_element_type=jnp.float32)
            * SCORE_SCALE
        )
        key_part = (
            jnp.einsum("hqk,qhd->khd", grad_scores, query_lane, preferred_element_type=jnp.float32)
            * SCORE_SCALE
        )
        value_part = jnp.einsum(
            "hqk,qhd->khd",
            attention.astype(jnp.bfloat16),
            grad_lane,
            preferred_element_type=jnp.float32,
        )
        stacked = jnp.stack(
            [key_part.reshape(key_rows, features), value_part.reshape(key_rows, features)], axis=1
        )
        key_terms = stacked[:, None]
        grad_query = query_part.reshape(rows_dev, 1, features)
        return (grad_query, key_terms)

    initial = (
        jnp.zeros((rows_dev, lane_count, features), jnp.float32),
        jnp.zeros((key_rows, lane_count, 2, features), jnp.float32),
    )
    return lax.fori_loop(0, lane_count, one_lane, initial)


def front(stream, layer_index, params, query_tags, key_tags, positions):
    (
        gain_one,
        shift_one,
        mat_qkv,
        bias_qkv,
        mat_out,
        bias_out,
        gain_two,
        shift_two,
        mat_up,
        bias_up,
        mat_down,
        bias_down,
    ) = [item[layer_index] for item in params]
    rows_dev, lane_count, width = stream.shape
    features = mat_qkv.shape[2]
    head_count = features // HEAD_DIM
    frame_place, row_place, column_place = positions
    first = layer_norm(stream, gain_one, shift_one).astype(jnp.bfloat16)
    projected = (
        jnp.einsum("tbd,dcf->tbcf", first, mat_qkv, preferred_element_type=jnp.float32) + bias_qkv
    )
    split = projected.reshape(rows_dev, lane_count, 3, head_count, HEAD_DIM)
    query = (
        rotate(split[:, :, 0], frame_place, row_place, column_place)
        .reshape(rows_dev, lane_count, features)
        .astype(jnp.bfloat16)
    )
    keys = (
        rotate(split[:, :, 1], frame_place, row_place, column_place)
        .reshape(rows_dev, lane_count, features)
        .astype(jnp.bfloat16)
    )
    values = projected[:, :, 2].astype(jnp.bfloat16)
    keys_all, values_all = (
        lax.all_gather(keys, "seq", axis=0, tiled=True),
        lax.all_gather(values, "seq", axis=0, tiled=True),
    )
    mixed_full, log_total = attend_forward(query, keys_all, values_all, query_tags, key_tags)
    mixed = mixed_full.astype(jnp.bfloat16)
    middle = (
        stream
        + sum_heads(jnp.einsum("tbf,fd->tbd", mixed, mat_out, preferred_element_type=jnp.float32))
        + bias_out
    )
    second = layer_norm(middle, gain_two, shift_two).astype(jnp.bfloat16)
    hidden = jnp.einsum("tbd,df->tbf", second, mat_up, preferred_element_type=jnp.float32) + bias_up
    activation = gelu_exact(hidden).astype(jnp.bfloat16)
    return (
        first,
        query,
        keys_all,
        values_all,
        log_total,
        mixed,
        middle,
        second,
        hidden,
        activation,
        mixed_full,
    )


def layer_backward(stream, gradient, layer_index, params, query_tags, key_tags, positions):
    (
        gain_one,
        shift_one,
        mat_qkv,
        bias_qkv,
        mat_out,
        bias_out,
        gain_two,
        shift_two,
        mat_up,
        bias_up,
        mat_down,
        bias_down,
    ) = [item[layer_index] for item in params]
    (
        first,
        query,
        keys_all,
        values_all,
        log_total,
        mixed,
        middle,
        second,
        hidden,
        activation,
        mixed_full,
    ) = front(stream, layer_index, params, query_tags, key_tags, positions)
    frame_place, row_place, column_place = positions
    rows_dev, lane_count, width = stream.shape
    features = query.shape[2]
    head_count = features // HEAD_DIM
    grad_low = gradient.astype(jnp.bfloat16)
    grad_w_down = jnp.einsum(
        "tbf,tbd->fd", activation, grad_low, preferred_element_type=jnp.float32
    )
    grad_b_down = jnp.sum(gradient, axis=(0, 1))
    grad_activation = jnp.einsum(
        "tbd,fd->tbf", grad_low, mat_down, preferred_element_type=jnp.float32
    )
    grad_hidden = jax.vjp(gelu_exact, hidden)[1](grad_activation)[0].astype(jnp.bfloat16)
    grad_b_up = jnp.sum(grad_hidden.astype(jnp.float32), axis=(0, 1))
    grad_w_up = jnp.einsum("tbd,tbf->df", second, grad_hidden, preferred_element_type=jnp.float32)
    grad_second = sum_inputs(
        jnp.einsum("tbf,df->tbd", grad_hidden, mat_up, preferred_element_type=jnp.float32)
    )
    middle_pull = jax.vjp(layer_norm, middle, gain_two, shift_two)[1]
    grad_inner, grad_gain_two, grad_shift_two = middle_pull(grad_second)
    grad_middle = gradient + grad_inner
    grad_b_out = jnp.sum(grad_middle, axis=(0, 1))
    middle_low = grad_middle.astype(jnp.bfloat16)
    grad_w_out = jnp.einsum("tbf,tbd->fd", mixed, middle_low, preferred_element_type=jnp.float32)
    grad_mixed = jnp.einsum(
        "tbd,fd->tbf", middle_low, mat_out, preferred_element_type=jnp.float32
    ).astype(jnp.bfloat16)
    grad_query, key_terms = attend_backward(
        query, keys_all, values_all, log_total, grad_mixed, query_tags, key_tags
    )
    returned = lax.psum_scatter(key_terms, "seq", scatter_dimension=0, tiled=True)
    turned_query = rotate(
        grad_query.reshape(rows_dev, lane_count, head_count, HEAD_DIM),
        -frame_place,
        -row_place,
        -column_place,
    )
    turned_keys = rotate(
        returned[:, :, 0].reshape(rows_dev, lane_count, head_count, HEAD_DIM),
        -frame_place,
        -row_place,
        -column_place,
    )
    grad_projected = jnp.stack(
        [
            turned_query.reshape(rows_dev, lane_count, features),
            turned_keys.reshape(rows_dev, lane_count, features),
            returned[:, :, 1],
        ],
        axis=2,
    ).astype(jnp.bfloat16)
    grad_b_qkv = jnp.sum(grad_projected.astype(jnp.float32), axis=(0, 1))
    grad_w_qkv = jnp.einsum(
        "tbd,tbcf->dcf", first, grad_projected, preferred_element_type=jnp.float32
    )
    grad_first = sum_inputs(
        jnp.einsum("tbcf,dcf->tbd", grad_projected, mat_qkv, preferred_element_type=jnp.float32)
    )
    first_pull = jax.vjp(layer_norm, stream, gain_one, shift_one)[1]
    grad_entry, grad_gain_one, grad_shift_one = first_pull(grad_first)
    grads = (
        grad_gain_one,
        grad_shift_one,
        grad_w_qkv,
        grad_b_qkv,
        grad_w_out,
        grad_b_out,
        grad_gain_two,
        grad_shift_two,
        grad_w_up,
        grad_b_up,
        grad_w_down,
        grad_b_down,
    )
    return (grad_middle + grad_entry, grads)


def per_device(
    tokens,
    d_out,
    norm1_gain,
    norm1_shift,
    w_qkv,
    b_qkv,
    w_out,
    b_out,
    norm2_gain,
    norm2_shift,
    w_up,
    b_up,
    w_down,
    b_down,
    episode_frames,
    live,
):
    rows_dev = tokens.shape[0]
    lane_count = tokens.shape[1] // MICRO
    total_rows = rows_dev * lax.axis_size("seq")
    local_positions = lax.axis_index("seq") * rows_dev + jnp.arange(rows_dev, dtype=jnp.int32)
    key_positions = jnp.arange(total_rows, dtype=jnp.int32)
    tagger = jax.vmap(episode_tags, in_axes=(0, None), out_axes=1)
    query_episode, query_frame, query_row, query_column = tagger(episode_frames, local_positions)
    key_episode, key_frame, key_row, key_column = tagger(episode_frames, key_positions)
    live_keys = lax.all_gather(live, "seq", axis=0, tiled=True)
    params = (
        norm1_gain,
        norm1_shift,
        w_qkv,
        b_qkv,
        w_out,
        b_out,
        norm2_gain,
        norm2_shift,
        w_up,
        b_up,
        w_down,
        b_down,
    )
    layer_grads = [None] * LAYERS
    outputs = []
    grad_tokens = []
    for micro_index in range(MICRO):
        first_lane = micro_index * lane_count
        last_lane = first_lane + lane_count
        query_tags = (query_episode[:, first_lane:last_lane], query_frame[:, first_lane:last_lane])
        key_tags = (
            key_episode[:, first_lane:last_lane],
            key_frame[:, first_lane:last_lane],
            live_keys[:, first_lane:last_lane],
        )
        positions = (
            query_frame[:, first_lane:last_lane],
            query_row[:, first_lane:last_lane],
            query_column[:, first_lane:last_lane],
        )
        stream = tokens[:, first_lane:last_lane].astype(jnp.float32)
        inputs = []
        gathered = []
        for layer_index in range(LAYERS):
            inputs.append(stream)
            layer_state = front(stream, layer_index, params, query_tags, key_tags, positions)
            gathered.append((layer_state[2], layer_state[3]))
            branch = jnp.einsum(
                "tbf,fd->tbd",
                layer_state[9],
                w_down[layer_index],
                preferred_element_type=jnp.float32,
            )
            stream = layer_state[6] + sum_heads(branch) + b_down[layer_index]
        outputs.append(stream)
        gradient = d_out[:, first_lane:last_lane]
        for layer_index in reversed(range(LAYERS)):
            gradient, grads = layer_backward(
                inputs[layer_index], gradient, layer_index, params, query_tags, key_tags, positions
            )
            if layer_grads[layer_index] is None:
                layer_grads[layer_index] = grads
            else:
                layer_grads[layer_index] = jax.tree.map(jnp.add, layer_grads[layer_index], grads)
        grad_tokens.append(gradient)
    stacked = [
        jnp.stack([layer_grads[layer_index][entry] for layer_index in range(LAYERS)])
        for entry in range(12)
    ]
    (
        grad_gain_one,
        grad_shift_one,
        grad_w_qkv,
        grad_b_qkv,
        grad_w_out,
        grad_b_out,
        grad_gain_two,
        grad_shift_two,
        grad_w_up,
        grad_b_up,
        grad_w_down,
        grad_b_down,
    ) = stacked
    in_sums = (
        lax.psum_scatter(grad_w_qkv, "seq", scatter_dimension=1, tiled=True),
        lax.psum_scatter(grad_w_up, "seq", scatter_dimension=1, tiled=True),
        lax.psum_scatter(grad_gain_one, "seq", scatter_dimension=1, tiled=True),
        lax.psum_scatter(grad_shift_one, "seq", scatter_dimension=1, tiled=True),
        lax.psum_scatter(grad_gain_two, "seq", scatter_dimension=1, tiled=True),
        lax.psum_scatter(grad_shift_two, "seq", scatter_dimension=1, tiled=True),
        lax.psum_scatter(grad_b_out, "seq", scatter_dimension=1, tiled=True),
        lax.psum_scatter(grad_b_down, "seq", scatter_dimension=1, tiled=True),
    )
    out_sums = (
        lax.psum_scatter(grad_w_out, "seq", scatter_dimension=2, tiled=True),
        lax.psum_scatter(grad_w_down, "seq", scatter_dimension=2, tiled=True),
    )
    bias_total = lax.psum((grad_b_qkv, grad_b_up), "seq")
    return (
        jnp.concatenate(outputs, axis=1),
        jnp.concatenate(grad_tokens, axis=1),
        in_sums[2],
        in_sums[3],
        in_sums[0],
        bias_total[0],
        out_sums[0],
        in_sums[6],
        in_sums[4],
        in_sums[5],
        in_sums[1],
        bias_total[1],
        out_sums[1],
        in_sums[7],
    )


MESH = pl.DeviceIdType.MESH
BF16 = jnp.bfloat16
F32 = jnp.float32
VMEM_BYTES = 60 * 1024 * 1024
PAIR = 128
VEC = 2048


def nn(left, right):
    return lax.dot_general(left, right, (((1,), (0,)), ((), ())), preferred_element_type=F32)


def nt(left, right):
    return lax.dot_general(left, right, (((1,), (1,)), ((), ())), preferred_element_type=F32)


def tn(left, right):
    return lax.dot_general(left, right, (((0,), (0,)), ((), ())), preferred_element_type=F32)


def at(start, size):
    return pl.ds(pl.multiple_of(start, size), size)


def repeat(count, body):
    def one(index, carry):
        body(index)
        return carry

    lax.fori_loop(0, count, one, 0)


def remote(src, dst, send, recv, seq, tp):
    return pltpu.make_async_remote_copy(
        src_ref=src,
        dst_ref=dst,
        send_sem=send,
        recv_sem=recv,
        device_id=(seq, tp),
        device_id_type=MESH,
    )


def hello(partners):
    barrier = pltpu.get_barrier_semaphore()
    for seq, tp in partners:
        pl.semaphore_signal(barrier, inc=1, device_id=(seq, tp), device_id_type=MESH)


def met(partners):
    pl.semaphore_wait(pltpu.get_barrier_semaphore(), len(partners))


def whole(array):
    zeros = (0,) * array.ndim
    return pl.BlockSpec(array.shape, lambda s: zeros, pipeline_mode=pl.Buffered(1))


def whole_out(shape):
    zeros = (0,) * len(shape)
    return pl.BlockSpec(shape, lambda s: zeros)


ANYWHERE = pl.BlockSpec(memory_space=pl.ANY)


def turn_row(table, place, section):
    frequency = np.exp(np.arange(10, dtype=np.float32) * np.float32(-math.log(10000.0) / 10.0))
    angle = place.astype(np.float32)[:, None] * frequency
    for base in range(20 * section, PAIR, HEAD_DIM):
        table[0, :, base : base + 10] = np.cos(angle)
        table[0, :, base + 10 : base + 20] = np.cos(angle)
        table[1, :, base : base + 10] = -np.sin(angle)
        table[2, :, base + 10 : base + 20] = np.sin(angle)


def turn_constants(frames):
    within, ahead = np.zeros((3, FRAME, PAIR), np.float32), np.zeros((3, frames, PAIR), np.float32)
    turn_row(within, np.arange(FRAME) // GRID, 1)
    turn_row(within, np.arange(FRAME) % GRID, 2)
    for base in range(60, PAIR, HEAD_DIM):
        within[0, :, base : base + 4] = 1.0
    turn_row(ahead, np.arange(frames), 0)
    return jnp.asarray(within), jnp.asarray(ahead)


def turn(values, tables, back=False):
    cosine, lower, upper = tables
    pieces = []
    for start in range(0, values.shape[1], PAIR):
        slab = values[:, start : start + PAIR]
        moved = pltpu.roll(slab, PAIR - 10, 1) * lower + pltpu.roll(slab, 10, 1) * upper
        pieces.append(slab * cosine - moved if back else slab * cosine + moved)
    return jnp.concatenate(pieces, axis=1)


def tables_of(fixed_ref, frames_ref, chunk):
    return [fixed_ref[i] + frames_ref[i, pl.ds(chunk, 1), :] for i in range(3)]


def normed(stream):
    center = stream - jnp.mean(stream, axis=-1, keepdims=True)
    spread = jnp.mean(center * center, axis=-1, keepdims=True)
    scale = lax.rsqrt(spread + EPSILON)
    return center * scale, scale


def norm_pull(grad, gain, unit, scale):
    scaled = grad * gain
    return scale * (
        scaled
        - jnp.mean(scaled, axis=-1, keepdims=True)
        - unit * jnp.mean(scaled * unit, axis=-1, keepdims=True)
    )


def keep_norm(unit, scale, unit_ref, scale_ref):
    unit_ref[...] = unit.astype(BF16)
    scale_ref[...] = jnp.broadcast_to(scale, scale_ref.shape)


def kept_norm(unit_ref, scale_ref):
    copies = unit_ref.shape[1] // scale_ref.shape[1]
    return unit_ref[...].astype(F32), jnp.concatenate([scale_ref[...]] * copies, axis=1)


def column_sum(values):
    return jnp.sum(values, axis=0, keepdims=True)


def gelu_both(hidden):
    normal = 0.5 + 0.5 * lax.erf(hidden * math.sqrt(0.5))
    density = jnp.exp(hidden * hidden * -0.5) * (1.0 / math.sqrt(2.0 * math.pi))
    return hidden * normal, normal + hidden * density


def project(stream, chunk, layer, pair, refs, outs, first_full):
    gain, shift, weight, bias, fixed, frames = refs
    query_ref, key_ref, value_ref, first_ref, unit_ref, scale_ref = outs
    unit, scale = normed(stream)
    keep_norm(unit, scale, unit_ref, scale_ref)
    first = (unit * gain[layer : layer + 1, :] + shift[layer : layer + 1, :]).astype(BF16)
    first_full[...] = first
    first_ref[...] = first_full[:, at(pair * PAIR, PAIR)]
    tables = tables_of(fixed, frames, chunk)
    query = nn(first, weight[0]) + bias[0, layer : layer + 1, :]
    query_ref[...] = (turn(query, tables) * SCORE_SCALE).astype(BF16)
    key = nn(first, weight[1]) + bias[1, layer : layer + 1, :]
    key_ref[...] = turn(key, tables).astype(BF16)
    value = nn(first, weight[2]) + bias[2, layer : layer + 1, :]
    value_ref[...] = value.astype(BF16)


class Relay:
    sems = 6

    def __init__(self, n, rows, buffer, other, sems, lives=None, live_other=None):
        self.n, self.rows, self.buffer, self.other = n, rows, buffer, other
        self.lives, self.live_other = lives, live_other
        self.z_send, self.z_recv, self.y_send, self.y_recv, self.c_send, self.c_recv = sems
        self.planes = n // 4
        self.me, self.core = lax.axis_index("seq"), lax.axis_index("tp")
        me = self.me
        self.x, self.y, self.z = lax.rem(me, 2), lax.rem(me // 2, 2), me // 4
        self.across = me + 2 - 4 * self.y

    @staticmethod
    def scratch(n):
        dma, planes = pltpu.SemaphoreType.DMA, n // 4
        shapes = [(planes, 2, 2)] * 2 + [(planes, 2)] * 2 + [(2 * planes,)] * 2
        return [dma(shape) for shape in shapes]

    @property
    def events(self):
        return self.planes

    def plane(self, step):
        return lax.rem(self.z + step, self.planes)

    def place(self, plane, lane):
        return plane * 4 + self.y * 2 + lane

    def reached(self):
        return [(step, far) for step in range(self.planes) for far in (0, 1) if step or far]

    def hello(self):
        barrier = pltpu.get_barrier_semaphore()
        partners = [(self.across, self.core), (self.me, 1 - self.core)]
        for step, far in self.reached():
            lane = 1 - self.x if far else self.x
            partners.append((self.place(self.plane(step), lane), self.core))
        for seq, tp in partners:
            pl.semaphore_signal(barrier, inc=1, device_id=(seq, tp), device_id_type=MESH)

    def met(self):
        pl.semaphore_wait(pltpu.get_barrier_semaphore(), 2 + len(self.reached()))

    def rows_of(self, side, seq):
        return self.buffer.at[side, at(seq * self.rows, self.rows), :]

    def block(self, side, pair):
        return self.buffer.at[side, at(pair * 2 * self.rows, 2 * self.rows), :]

    def items(self, pair):
        found = [self.block(self.core, pair)]
        if self.lives is not None:
            found.append(self.lives.at[at(pair * 2, 2)])
        return found

    def each(self, copy, what):
        for index in range(1 if self.lives is None else 2):
            getattr(copy(index), what)()

    def z_copy(self, step, far):
        def copy(index):
            lane = 1 - self.x if far else self.x
            if index == 0:
                source = self.other.at[self.core] if far else self.rows_of(self.core, self.me)
                target = self.rows_of(self.core, self.me)
            else:
                source = self.live_other if far else self.lives.at[self.me]
                target = self.lives.at[self.me]
            return remote(
                source,
                target,
                self.z_send.at[step, far, index],
                self.z_recv.at[step, far, index],
                self.place(self.plane(step), lane),
                self.core,
            )

        return copy

    def y_copy(self, plane, row):
        def copy(index):
            item = self.items(plane * 2 + row)[index]
            return remote(
                item,
                item,
                self.y_send.at[plane, index],
                self.y_recv.at[plane, index],
                self.across,
                self.core,
            )

        return copy

    def c_copy(self, pair, side):
        item = self.block(side, pair)
        return remote(
            item, item, self.c_send.at[pair], self.c_recv.at[pair], self.me, 1 - self.core
        )

    def begin(self):
        for step, far in self.reached():
            self.each(self.z_copy(step, far), "start")

    def arrive(self, event):
        for far in (0, 1) if event else (1,):
            self.each(self.z_copy(event, far), "wait_recv")
        plane = self.plane(self.planes - event)
        self.each(self.y_copy(plane, self.y), "start")
        self.c_copy(plane * 2 + self.y, self.core).start()

    def complete(self, event):
        plane = self.plane(self.planes - event)
        self.each(self.y_copy(plane, 1 - self.y), "wait_recv")
        self.c_copy(plane * 2 + 1 - self.y, self.core).start()

    def ready(self, event):
        plane = self.plane(self.planes - event)
        self.c_copy(plane * 2, 1 - self.core).wait_recv()
        self.c_copy(plane * 2 + 1, 1 - self.core).wait_recv()
        return plane

    def finish(self):
        for step, far in self.reached():
            self.each(self.z_copy(step, far), "wait_send")
        for plane in range(self.planes):
            self.each(self.y_copy(plane, self.y), "wait_send")
        for pair in range(2 * self.planes):
            self.c_copy(pair, self.core).wait_send()


def split_lanes(values, x, buffer, other, start, rows):
    half = values.shape[2] // 2
    zero, one = values[:, 0, :], values[:, 1, :]
    own, far = jnp.where(x == 0, zero, one), jnp.where(x == 0, one, zero)
    core = lax.axis_index("tp")
    own = jnp.where(core == 0, own[:, :half], own[:, half:]).astype(BF16)
    buffer[core, at(start, rows), :] = own
    for side in range(2):
        other[side] = far[:, side * half : (side + 1) * half].astype(BF16)


def gather_and_project(tokens, live, episode_frames, gain, shift, qkv, bias, fixed, ahead, n):
    rows, lanes, width = tokens.shape
    half = width // 2
    total = n * rows
    chunks = total // FRAME
    per_frame = FRAME // rows
    features = qkv.shape[3]
    slots = episode_frames.shape[1]

    def kernel(*refs):
        refs = list(refs)

        def take(count):
            taken = refs[:count]
            del refs[:count]
            return taken

        tokens_ref, live_ref, counts_ref, gain_ref, shift_ref, w_any, bias_ref = take(7)
        fixed_ref, ahead_ref = take(2)
        all_ref, mask_ref, frames_ref = take(3)
        projected = take(6)
        other, lives, live_other, weight, full, w_sem = take(6)
        relay = Relay(n, rows, all_ref, other, take(Relay.sems), lives, live_other)
        load = pltpu.make_async_copy(w_any.at[0], weight, w_sem)
        load.start()
        relay.hello()
        x, me = relay.x, relay.me
        split_lanes(tokens_ref[...].astype(F32), x, all_ref, other, me * rows, rows)
        lane = lax.broadcasted_iota(jnp.int32, (1, FRAME), 1)
        here = lane // rows == lax.rem(me, per_frame)
        tiles = []
        for index in range(lanes):
            alive = live_ref[index : index + 1, :].astype(F32)
            alive = jnp.where(here, jnp.concatenate([alive] * per_frame, axis=1), 0.0)
            tiles.append(jnp.broadcast_to(alive, (8, FRAME)))
        lives[me] = jnp.where(x == 0, tiles[0], tiles[1])
        live_other[...] = jnp.where(x == 0, tiles[1], tiles[0])
        relay.met()
        relay.begin()

        counts = [counts_ref[x, slot] for slot in range(slots)]
        episodes, openings = [], []
        for frame in range(chunks):
            end, episode, opening = 0, 0, 0
            for slot in range(slots):
                end = end + counts[slot]
                passed = frame >= end
                episode = episode + passed.astype(jnp.int32)
                opening = opening + jnp.where(passed, counts[slot], 0)
            episodes.append(episode)
            openings.append(frame - opening)
        for index in range(3):
            table = []
            for frame in range(chunks):
                line = jnp.zeros((1, PAIR), F32)
                for choice in range(chunks):
                    line = jnp.where(
                        openings[frame] == choice, ahead_ref[index, choice : choice + 1, :], line
                    )
                table.append(line)
            frames_ref[index] = jnp.concatenate(
                table + [jnp.zeros((8 - chunks, PAIR), F32)], axis=0
            )
        load.wait()

        def project_frame(frame):
            place = at(frame * FRAME, FRAME)
            stream = jnp.concatenate([all_ref[0, place, :], all_ref[1, place, :]], axis=1)
            project(
                stream.astype(F32),
                frame,
                0,
                me // 2,
                (gain_ref, shift_ref, weight, bias_ref, fixed_ref, frames_ref),
                [ref.at[place, :] for ref in projected],
                full,
            )

        for event in range(relay.events):
            relay.arrive(event)
            if event:
                relay.complete(event - 1)
            if event > 1:
                project_frame(relay.ready(event - 2))
        relay.complete(relay.events - 1)
        for event in range(max(0, relay.events - 2), relay.events):
            project_frame(relay.ready(event))
        relay.finish()

        for key_frame in range(chunks):
            alive = lives[key_frame * per_frame, 0:1, :]
            for part in range(1, per_frame):
                alive = alive + lives[key_frame * per_frame + part, 0:1, :]
            closed = (alive - 1.0) * -MASKED
            lines = []
            for query_frame in range(chunks):
                allowed = (episodes[query_frame] == episodes[key_frame]) & (
                    openings[key_frame] <= openings[query_frame]
                )
                lines.append(jnp.where(allowed, closed, MASKED))
            lines.append(jnp.zeros((PAIR - chunks, FRAME), F32))
            mask_ref[key_frame * FRAME : (key_frame + 1) * FRAME, :] = jnp.concatenate(
                lines, axis=0
            ).T.astype(BF16)

    in_vmem = pl.BlockSpec(memory_space=pltpu.VMEM)
    in_smem = pl.BlockSpec(memory_space=pltpu.SMEM)
    projected = jax.ShapeDtypeStruct((total, features), BF16)
    return pl.pallas_call(
        kernel,
        out_shape=(
            jax.ShapeDtypeStruct((2, total, half), BF16),
            jax.ShapeDtypeStruct((total, PAIR), BF16),
            jax.ShapeDtypeStruct((3, 8, PAIR), F32),
            projected,
            projected,
            projected,
            jax.ShapeDtypeStruct((total, PAIR), BF16),
            jax.ShapeDtypeStruct((total, width), BF16),
            jax.ShapeDtypeStruct((total, PAIR), F32),
        ),
        in_specs=[in_vmem, in_vmem, in_smem, in_vmem, in_vmem, ANYWHERE] + [in_vmem] * 3,
        out_specs=(in_vmem,) * 9,
        scratch_shapes=[
            pltpu.VMEM((2, rows, half), BF16),
            pltpu.VMEM((n, 8, FRAME), F32),
            pltpu.VMEM((8, FRAME), F32),
            pltpu.VMEM(qkv.shape[1:], BF16),
            pltpu.VMEM((FRAME, width), BF16),
            pltpu.SemaphoreType.DMA,
        ]
        + Relay.scratch(n),
        compiler_params=pltpu.CompilerParams(
            collective_id=0, has_side_effects=True, vmem_limit_bytes=VMEM_BYTES
        ),
        name="gather_and_project",
    )(tokens, live, episode_frames, gain, shift, qkv, bias, fixed, ahead)


def later_projection(layer, stream, gain, shift, qkv, bias, fixed, frames):
    total, width = stream.shape
    features = qkv.shape[3]

    def kernel(x_ref, gain, shift, weight, bias, fixed, frames, *rest):
        project(
            x_ref[...],
            pl.program_id(0),
            layer,
            lax.axis_index("seq") // 2,
            (gain, shift, weight.at[0], bias, fixed, frames),
            rest[:6],
            rest[6],
        )

    def rows(columns):
        return pl.BlockSpec((FRAME, columns), lambda s: (s, 0))

    widths = [(features, BF16)] * 3 + [(PAIR, BF16), (width, BF16), (PAIR, F32)]
    return pl.pallas_call(
        kernel,
        grid=(total // FRAME,),
        out_shape=[jax.ShapeDtypeStruct((total, size), kind) for size, kind in widths],
        in_specs=[rows(width), whole(gain), whole(shift)]
        + [
            pl.BlockSpec(
                (1, *qkv.shape[1:]), lambda s: (layer, 0, 0, 0), pipeline_mode=pl.Buffered(1)
            )
        ]
        + [whole(item) for item in (bias, fixed, frames)],
        out_specs=[rows(size) for size, _ in widths],
        scratch_shapes=[pltpu.VMEM((FRAME, width), BF16)],
        compiler_params=pltpu.CompilerParams(vmem_limit_bytes=VMEM_BYTES),
        name=f"projection_{layer}",
    )(stream, gain, shift, qkv, bias, fixed, frames)


def halves(ref):
    return jnp.concatenate([ref[0], ref[1]], axis=1).astype(F32)


def halves_spec(shape, chunks, behind, span=FRAME):
    return pl.BlockSpec(
        (2, span, shape[2]), lambda s: (0, jnp.clip(s - behind, 0, chunks - 1), 0)
    )


def layer_forward(layer, query, key, value, key_bias, stream, mats, rows_of, d_out, n, identity):
    total, features = query.shape
    split = stream.ndim == 3
    width = mats[1].shape[1]
    rows_here = total // n
    hidden_units = mats[1].shape[2]
    chunks = total // FRAME
    heads = features // HEAD_DIM
    slabs = features // PAIR
    columns = 256
    b_out, gain, shift, b_up, b_down = rows_of
    mat_out, mat_up, mat_down = mats

    def kernel(*refs):
        refs = list(refs)

        def take(count):
            taken = refs[:count]
            del refs[:count]
            return taken

        q_ref, k_ref, v_ref, kb_ref, x_ref = take(5)
        wo_any, wu_any, wd_any = take(3)
        bo_ref, gain_ref, shift_ref, bu_ref, bd_ref = take(5)
        if d_out is not None:
            (d_ref,) = take(1)
        p_ref, r_ref, mixed_ref, unit_ref, scale_ref, second_ref, act_ref, gp_ref, x_out = take(9)
        if d_out is not None:
            (d_all,) = take(1)
        wo, wu, wd, mid, full = take(5)
        a_send, a_recv, b_send, b_recv, w_sem, send_sem, recv_sem = take(7)
        relay = None
        if d_out is not None:
            buffer, other, d_sem = take(3)
            relay = Relay(n, rows_here, buffer, other, take(Relay.sems))

        step = pl.program_id(0)
        me, core = lax.axis_index("seq"), lax.axis_index("tp")

        items = [(wo_any, wo), (wu_any, wu), (wd_any, wd)]

        def load(index):
            source, target = items[index]
            return pltpu.make_async_copy(
                source.at[layer], target, w_sem.at[index]
            )

        def exchange(kind, chunk):
            source, target = ((a_send, a_recv), (b_send, b_recv))[kind]
            return remote(
                source.at[chunk],
                target.at[chunk],
                send_sem.at[kind, chunk],
                recv_sem.at[kind, chunk],
                me,
                1 - core,
            )

        @pl.when(step == 0)
        def _():
            for index in range(len(items)):
                load(index).start()
            if relay is None:
                hello([(me, 1 - core)])
            else:
                relay.hello()
                split_lanes(d_ref[...], relay.x, buffer, other, me * rows_here, rows_here)

        lane = lax.broadcasted_iota(jnp.int32, (1, PAIR), 1)
        sides = [(lane < HEAD_DIM).astype(F32).astype(BF16), (lane >= HEAD_DIM).astype(F32).astype(BF16)]
        for frame in range(chunks):

            @pl.when(step == frame)
            def _():
                keys = FRAME * (frame + 1)
                mask = kb_ref[:keys, :]
                asked = jnp.broadcast_to((lane == frame).astype(F32), (FRAME, PAIR)).astype(BF16)

                slab_lanes = [slice(slab * PAIR, (slab + 1) * PAIR) for slab in range(slabs)]

                def score(head):
                    lanes, side = slab_lanes[head // 2], head % 2
                    key = jnp.concatenate([k_ref[:keys, lanes], mask], axis=1)
                    return nt(jnp.concatenate([q_ref[:, lanes] * sides[side], asked], axis=1), key)

                scores, sums = score(0), []
                for head in range(heads):
                    lanes, side = slab_lanes[head // 2], head % 2
                    following = score(head + 1) if head + 1 < heads else None
                    highest = jnp.max(scores, axis=1, keepdims=True)
                    shifted = jnp.exp(scores - highest).astype(BF16)
                    p_ref[0, head, :keys, :] = shifted.T
                    sums.append(nn(shifted, v_ref[:keys, lanes] * sides[side] + sides[1 - side]))
                    scores = following
                    if side == 1:
                        one, two = sums[head - 1 :]
                        low_side = lane < HEAD_DIM
                        divisor = 1.0 / jnp.where(
                            low_side, pltpu.roll(one, HEAD_DIM, 1), pltpu.roll(two, HEAD_DIM, 1)
                        )
                        r_ref[:, lanes] = divisor
                        mixed_ref[:, lanes] = (jnp.where(low_side, one, two) * divisor).astype(BF16)

        @pl.when(step == 0)
        def _():
            load(0).wait()
            if relay is None:
                met([(me, 1 - core)])
            else:
                relay.met()
                relay.begin()

        @pl.when(step < chunks)
        def _():
            a_send[step] = nn(mixed_ref[...], wo[...]).astype(BF16)
            exchange(0, step).start()

        if relay is not None:
            for event in range(relay.events):

                @pl.when(step == 2 + event // 2)
                def _():
                    relay.arrive(event)

                @pl.when(step == 3 + event // 2)
                def _():
                    relay.complete(event)

            @pl.when(step == chunks + 1)
            def _():
                for event in range(relay.events):
                    relay.ready(event)
                relay.finish()
                pltpu.make_async_copy(buffer, d_all, d_sem).start()

        def feed_forward():
            chunk = step - 1
            middle = (halves(x_ref) if split else x_ref[...]) + (
                a_send[chunk].astype(F32) + a_recv[chunk].astype(F32)
            )
            middle = middle + bo_ref[layer : layer + 1, :]
            mid[lax.rem(chunk, 2)] = middle
            unit, scale = normed(middle)
            keep_norm(unit, scale, unit_ref, scale_ref)
            second = (unit * gain_ref[layer : layer + 1, :] + shift_ref[layer : layer + 1, :]).astype(BF16)
            full[...] = second
            second_ref[...] = full[:, at((me // 2) * PAIR, PAIR)]
            parts = [slice(start, start + columns) for start in range(0, hidden_units, columns)]
            hidden = nn(second, wu[:, parts[0]])
            for index, part in enumerate(parts):
                following = nn(second, wu[:, parts[index + 1]]) if index + 1 < len(parts) else None
                act, slope = gelu_both(hidden + bu_ref[layer : layer + 1, part])
                act_ref[:, part] = act.astype(BF16)
                gp_ref[:, part] = slope.astype(BF16)
                hidden = following
            b_send[chunk] = nn(act_ref[...], wd[...]).astype(BF16)

        def close():
            chunk = step - 2
            result = mid[lax.rem(chunk, 2)] + (b_send[chunk].astype(F32) + b_recv[chunk].astype(F32))
            result = result + bd_ref[layer : layer + 1, :]
            x_out[...] = result

        @pl.when(step == 1)
        def _():
            load(1).wait()
            load(2).wait()

        @pl.when((step >= 1) & (step <= chunks))
        def _():
            exchange(0, step - 1).wait_recv()
            feed_forward()
            exchange(1, step - 1).start()

        @pl.when(step >= 2)
        def _():
            exchange(1, step - 2).wait_recv()
            close()

        @pl.when(step == chunks + 1)
        def _():
            for kind in range(2):
                for chunk in range(chunks):
                    exchange(kind, chunk).wait_send()
            if relay is not None:
                pltpu.make_async_copy(buffer, d_all, d_sem).wait()

    def rows(columns, behind):
        return pl.BlockSpec(
            (FRAME, columns), lambda s: (jnp.clip(s - behind, 0, chunks - 1), 0)
        )

    in_specs = [rows(features, 0), whole(key), whole(value), whole(key_bias)]
    in_specs += [halves_spec(stream.shape, chunks, 1) if split else rows(width, 1)]
    in_specs += [ANYWHERE] * 3 + [whole(item) for item in rows_of]
    operands = [query, key, value, key_bias, stream, *mats, *rows_of]
    if d_out is not None:
        in_specs += [whole(d_out)]
        operands += [d_out]
    out_shape = [
        jax.ShapeDtypeStruct((chunks, heads, total, FRAME), BF16),
        jax.ShapeDtypeStruct((total, features), F32),
        jax.ShapeDtypeStruct((total, features), BF16),
        jax.ShapeDtypeStruct((total, width), BF16),
        jax.ShapeDtypeStruct((total, PAIR), F32),
        jax.ShapeDtypeStruct((total, PAIR), BF16),
        jax.ShapeDtypeStruct((total, hidden_units), BF16),
        jax.ShapeDtypeStruct((total, hidden_units), BF16),
        jax.ShapeDtypeStruct((total, width), F32),
    ]
    out_specs = [
        pl.BlockSpec((1, heads, total, FRAME), lambda s: (jnp.minimum(s, chunks - 1), 0, 0, 0)),
        rows(features, 0),
        rows(features, 0),
        rows(width, 1),
        rows(PAIR, 1),
        rows(PAIR, 1),
        rows(hidden_units, 1),
        rows(hidden_units, 1),
        rows(width, 2),
    ]
    scratch = [
        pltpu.VMEM(mat_out.shape[1:], BF16),
        pltpu.VMEM(mat_up.shape[1:], BF16),
        pltpu.VMEM(mat_down.shape[1:], BF16),
        pltpu.VMEM((2, FRAME, width), F32),
        pltpu.VMEM((FRAME, width), BF16),
    ]
    if d_out is not None:
        out_shape += [jax.ShapeDtypeStruct((2, total, width // 2), BF16)]
        out_specs += [ANYWHERE]
    scratch += [pltpu.VMEM((chunks, FRAME, width), BF16)] * 4
    scratch += [
        pltpu.SemaphoreType.DMA((4,)),
        pltpu.SemaphoreType.DMA((2, chunks)),
        pltpu.SemaphoreType.DMA((2, chunks)),
    ]
    if d_out is not None:
        scratch += [
            pltpu.VMEM((2, total, width // 2), BF16),
            pltpu.VMEM((2, rows_here, width // 2), BF16),
            pltpu.SemaphoreType.DMA,
        ]
        scratch += Relay.scratch(n)
    return pl.pallas_call(
        kernel,
        grid=(chunks + 2,),
        out_shape=out_shape,
        in_specs=in_specs,
        out_specs=out_specs,
        scratch_shapes=scratch,
        compiler_params=pltpu.CompilerParams(
            collective_id=identity, has_side_effects=True, vmem_limit_bytes=VMEM_BYTES
        ),
        name=f"layer_forward_{layer}",
    )(*operands)


class Swap:
    def __init__(self, ships, lane_rows):
        self.ships, self.lane_rows = ships, lane_rows
        self.count = len(ships) + len(lane_rows)

    def operands(self):
        return [*self.ships, *[item for item, _ in self.lane_rows]]

    def in_specs(self):
        return [whole(item) for item in self.ships] + [ANYWHERE] * len(self.lane_rows)

    def outputs(self):
        shapes, specs = [], []
        for item in self.ships:
            shape = (item.shape[0] // 2, item.shape[1])
            shapes.append(jax.ShapeDtypeStruct(shape, F32))
            specs.append(whole_out(shape))
        for item, count in self.lane_rows:
            shapes.append(jax.ShapeDtypeStruct((count or item.shape[0], item.shape[1]), item.dtype))
            specs.append(ANYWHERE)
        return shapes, specs

    def scratch(self):
        if not self.count:
            return []
        buffers = [pltpu.VMEM((item.shape[0] // 2, item.shape[1]), BF16) for item in self.ships]
        return buffers * 2 + [pltpu.SemaphoreType.DMA((self.count,))] * 2

    def bind(self, sources, targets, scratch):
        ships = len(self.ships)
        me, core = lax.axis_index("seq"), lax.axis_index("tp")
        x = lax.rem(me, 2)
        beside = me + 1 - 2 * x
        half = PAIR // 2

        def copy(index):
            if index < ships:
                source, target = scratch[index], scratch[ships + index]
            else:
                source, target = sources[index], targets[index]
                count = self.lane_rows[index - ships][1]
                if count:
                    source = source.at[at(beside * count, count), :]
            send, recv = scratch[2 * ships].at[index], scratch[2 * ships + 1].at[index]
            return remote(source, target, send, recv, beside, core)

        def start():
            for index in range(self.count):
                if index < ships:
                    scratch[index][...] = sources[index][at((1 - x) * half, half), :].astype(BF16)
                copy(index).start()

        def finish():
            for index in range(self.count):
                copy(index).wait_recv()
                if index < ships:
                    own = sources[index][at(x * half, half), :]
                    targets[index][...] = own + scratch[ships + index][...].astype(F32)
            for index in range(self.count):
                copy(index).wait_send()

        return start, finish


def attention_backward(
    probs, divisor, mixed, query, key, value, grad_mixed, first, fixed, frames, swap, swap_qkv, identity
):
    total, features = query.shape
    chunks = total // FRAME
    slabs = features // PAIR
    half = PAIR // 2

    def kernel(*refs):
        refs = list(refs)

        def take(count):
            taken = refs[:count]
            del refs[:count]
            return taken

        p_ref, r_ref, o_ref, q_ref, k_ref, v_ref, g_ref, first_ref, fixed_ref, frames_ref = take(10)
        sources = take(swap.count)
        dq_ref, dk_ref, dv_ref, qkv_out = take(4)
        targets = take(swap.count)
        dk_sum, dv_sum, first_turned = take(3)
        if swap_qkv:
            qkv_own, qkv_send, qkv_recv, qkv_sems = take(4)
        start, finish = swap.bind(sources, targets, refs)

        step = pl.program_id(0)
        me, core = lax.axis_index("seq"), lax.axis_index("tp")
        x = lax.rem(me, 2)
        beside = me + 1 - 2 * x

        def qkv_copy(slab):
            return remote(
                qkv_send.at[slab],
                qkv_recv.at[slab],
                qkv_sems.at[0, slab],
                qkv_sems.at[1, slab],
                beside,
                core,
            )

        @pl.when(step == 0)
        def _():
            hello([(beside, core)])
            first_turned[...] = first_ref[...].T
            met([(beside, core)])
            start()

        lane = lax.broadcasted_iota(jnp.int32, (1, PAIR), 1)
        sides = [(lane < HEAD_DIM).astype(F32).astype(BF16), (lane >= HEAD_DIM).astype(F32).astype(BF16)]
        turned = k_ref[...].T
        ones = jnp.broadcast_to((lane < 2).astype(F32), (total, PAIR)).astype(BF16)
        values = jnp.concatenate([v_ref[...], ones], axis=1)

        def give(frame):
            keys = FRAME * (frame + 1)
            own = slice(frame * FRAME, keys)
            scaled = (g_ref[own, :].astype(F32) * r_ref[own, :]).astype(BF16)
            inner = scaled.astype(F32) * o_ref[own, :].astype(F32)
            grads, q_parts, g_parts = [], [], []
            for side in range(2):
                delta = jnp.sum(
                    jnp.where((lane < HEAD_DIM) == (side == 0), inner, 0.0), axis=1, keepdims=True
                )
                coarse = delta.astype(BF16).astype(F32)
                rest = jnp.where(lane == 0, -coarse, jnp.where(lane == 1, coarse - delta, 0.0))
                g2 = scaled * sides[side]
                grads.append(nt(values[:keys], jnp.concatenate([g2, rest.astype(BF16)], axis=1)))
                q_parts.append(q_ref[own, :] * sides[side])
                g_parts.append(g2)
            return grads, jnp.concatenate(q_parts, axis=0), jnp.concatenate(g_parts, axis=0)

        given = give(chunks - 1)
        for frame in reversed(range(chunks)):
            keys = FRAME * (frame + 1)
            own = slice(frame * FRAME, keys)
            tables = tables_of(fixed_ref, frames_ref, frame)
            grads, q_part, g_part = given
            given = give(frame - 1) if frame else None
            query_parts, score_parts, prob_parts = [], [], []
            for side in range(2):
                attention = p_ref[frame, side, :keys, :]
                grad_scores = (attention.astype(F32) * grads[side]).astype(BF16)
                query_parts.append(nn(turned[side * HEAD_DIM : (side + 1) * HEAD_DIM, :keys], grad_scores))
                score_parts.append(grad_scores)
                prob_parts.append(attention)
            grad_query = jnp.concatenate(query_parts, axis=0).T
            key_parts = nn(jnp.concatenate(score_parts, axis=1), q_part)
            value_parts = nn(jnp.concatenate(prob_parts, axis=1), g_part)
            dq_ref[own, :] = (turn(grad_query, tables, True) * SCORE_SCALE).astype(BF16)
            if frame == chunks - 1:
                dk_sum[...] = key_parts
                dv_sum[...] = value_parts
            else:
                dk_sum[:keys, :] += key_parts
                dv_sum[:keys, :] += value_parts
            dk_ref[own, :] = turn(dk_sum[own, :], tables, True).astype(BF16)
            dv_ref[own, :] = dv_sum[own, :].astype(BF16)

        for part, ref in enumerate((dq_ref, dk_ref, dv_ref)):
            piece = slice(part * PAIR, (part + 1) * PAIR)
            terms = nn(first_turned[...], ref[...])
            if swap_qkv:
                qkv_own[step, :, piece] = terms
                qkv_send[step, :, piece] = qkv_own[step, at((1 - x) * half, half), piece].astype(BF16)
            else:
                qkv_out[:, at(part * features + step * PAIR, PAIR)] = terms
        if swap_qkv:
            qkv_copy(step).start()

        @pl.when(step == slabs - 1)
        def _():
            finish()
            for slab in range(slabs if swap_qkv else 0):
                qkv_copy(slab).wait_recv()
                for part in range(3):
                    piece = slice(part * PAIR, (part + 1) * PAIR)
                    place = part * features + slab * PAIR
                    qkv_out[:, place : place + PAIR] = qkv_own[
                        slab, at(x * half, half), piece
                    ] + qkv_recv[slab, :, piece].astype(F32)
            for slab in range(slabs if swap_qkv else 0):
                qkv_copy(slab).wait_send()

    slab = pl.BlockSpec((total, PAIR), lambda s: (0, s))
    in_specs = [pl.BlockSpec((chunks, 2, total, FRAME), lambda s: (0, s, 0, 0))]
    in_specs += [slab] * 6 + [whole(first), whole(fixed), whole(frames)]
    in_specs += swap.in_specs()
    qkv_shape = (half if swap_qkv else PAIR, 3 * features)
    shapes, specs = swap.outputs()
    out_shape = [jax.ShapeDtypeStruct((total, features), BF16)] * 3
    out_shape += [jax.ShapeDtypeStruct(qkv_shape, F32)] + shapes
    out_specs = [slab] * 3 + [whole_out(qkv_shape)] + specs
    scratch = [pltpu.VMEM((total, PAIR), F32)] * 2 + [pltpu.VMEM((PAIR, total), BF16)]
    if swap_qkv:
        scratch += [pltpu.VMEM((slabs, PAIR, 3 * PAIR), F32)]
        scratch += [pltpu.VMEM((slabs, half, 3 * PAIR), BF16)] * 2
        scratch += [pltpu.SemaphoreType.DMA((2, slabs))]
    scratch += swap.scratch()
    return pl.pallas_call(
        kernel,
        grid=(slabs,),
        out_shape=out_shape,
        in_specs=in_specs,
        out_specs=out_specs,
        scratch_shapes=scratch,
        compiler_params=pltpu.CompilerParams(
            collective_id=identity, has_side_effects=True, vmem_limit_bytes=VMEM_BYTES
        ),
        name=f"attention_backward_{identity}",
    )(
        probs,
        divisor,
        mixed,
        query,
        key,
        value,
        grad_mixed,
        first,
        fixed,
        frames,
        *swap.operands(),
    )


def rows_backward(entry, upper, identity, span, swap):
    top, bottom = len(entry) == 1, upper is None
    if not top:
        above, entry = entry[0], entry[1:]
    total = entry[0].shape[1] if top else entry[0].shape[0]
    chunks = total // span
    columns = 256
    ahead = 0 if top else 2 if bottom else 1
    if top:
        width = 2 * entry[0].shape[2]
    else:
        features, width = entry[0].shape[1], entry[5].shape[1]
    if not bottom:
        layer = upper[0]
        hidden_units, mixed_features = upper[1].shape[1], upper[6].shape[1]
    place_rows = total // lax.axis_size("seq")

    def kernel(*refs):
        refs = list(refs)

        def take(count):
            taken = refs[:count]
            del refs[:count]
            return taken

        if top:
            (d_out_ref,) = take(1)
        else:
            dq_ref, dk_ref, dv_ref, unit1, scale1, dm_ref, wq, gain1 = take(8)
        if not bottom:
            act_ref, gp_ref, unit2, scale2, second_ref, mixed_ref = take(6)
            wo_any, wu_any, wd_any, gain2 = take(4)
        sources = take(swap.count)
        if not top:
            (vec1,) = take(1)
        if not bottom:
            dmid_out, dmix_out, out_sum, up_sum, down_sum, vec2 = take(6)
        else:
            dx_out, dx_other, vec_other = take(3)
        targets = take(swap.count)
        if not top:
            a_send, a_recv = take(2)
        if not bottom:
            b_send, b_recv, grad_keep, hidden_keep, low_keep, last_keep, wo, wu, wd, w_sem = take(10)
        else:
            dx_keep, dx_send, dx_recv, vec_recv, x_send_sem, x_recv_sem = take(6)
        send_sem, recv_sem = take(2)
        start_swap, finish_swap = swap.bind(sources, targets, refs)

        step = pl.program_id(0)
        me, core = lax.axis_index("seq"), lax.axis_index("tp")
        pair = at((me // 2) * PAIR, PAIR)
        x = lax.rem(me, 2)
        beside = me + 1 - 2 * x

        def exchange(kind, chunk):
            source, target = (a_send, a_recv) if kind == 0 else (b_send, b_recv)
            return remote(
                source.at[chunk],
                target.at[chunk],
                send_sem.at[kind, chunk],
                recv_sem.at[kind, chunk],
                me,
                1 - core,
            )

        def load(index):
            source, target = ((wd_any, wd), (wu_any, wu), (wo_any, wo))[index]
            return pltpu.make_async_copy(source.at[layer], target, w_sem.at[index])

        partners = [(me, 1 - core)] + ([(beside, core)] if bottom or swap.count else [])

        @pl.when(step == 0)
        def _():
            if not bottom:
                for index in range(3):
                    load(index).start()
                out_sum[...] = jnp.zeros_like(out_sum)
                up_sum[...] = jnp.zeros_like(up_sum)
                down_sum[...] = jnp.zeros_like(down_sum)
                vec2[...] = jnp.zeros_like(vec2)
            if not top:
                vec1[...] = jnp.zeros_like(vec1)
            hello(partners)

        def meet():
            @pl.when(step == 0)
            def _():
                met(partners)
                start_swap()

        def entry_products():
            partial = None
            for part, ref in enumerate((dq_ref, dk_ref, dv_ref)):
                grad = ref[...]
                term = nt(grad, wq[0, part])
                partial = term if partial is None else partial + term
                vec1[part : part + 1, :] += column_sum(grad.astype(F32))
            a_send[step] = partial.astype(BF16)

        def entry_norm(chunk):
            if top:
                return halves(d_out_ref)
            grad_first = a_send[chunk].astype(F32) + a_recv[chunk].astype(F32)
            unit, scale = kept_norm(unit1, scale1)
            for start, sums in ((3, column_sum(grad_first * unit)), (5, column_sum(grad_first))):
                for side in range(width // features):
                    piece = slice(side * features, (side + 1) * features)
                    vec1[start + side : start + side + 1, :] += sums[:, piece]
            return dm_ref[...] + norm_pull(grad_first, gain1[above : above + 1, :], unit, scale)

        def feed_forward(between=None):
            chunk = step - ahead
            gradient = entry_norm(chunk)
            if bottom:
                dx_keep[at(chunk * span, span), :] = gradient
                return
            grad_keep[lax.rem(chunk, 2)] = gradient
            vec2[1:2, :width] += column_sum(gradient)
            low = gradient.astype(BF16)
            low_keep[...] = low
            low_columns = low_keep[:, pair]
            second = second_ref[...]
            parts = [slice(start, start + columns) for start in range(0, hidden_units, columns)]
            if top:
                wide = 4 * columns

                def some(index):
                    start = index * wide
                    places = [pl.ds(pl.multiple_of(start + k * columns, columns), columns) for k in range(4)]
                    grad_act = nt(low_keep[...], wd[places[0], :])
                    for k, part in enumerate(places):
                        following = nt(low_keep[...], wd[places[k + 1], :]) if k < 3 else None
                        grad_hidden = grad_act * gp_ref[:, part].astype(F32)
                        hidden_keep[:, part] = grad_hidden.astype(BF16)
                        vec2[0:1, part] += column_sum(grad_hidden)
                        grad_act = following

                repeat(hidden_units // wide, some)
            else:
                grad_act = nt(low, wd[parts[0], :])
                for index, part in enumerate(parts):
                    following = nt(low, wd[parts[index + 1], :]) if index + 1 < len(parts) else None
                    grad_hidden = grad_act * gp_ref[:, part].astype(F32)
                    hidden_keep[:, part] = grad_hidden.astype(BF16)
                    vec2[0:1, part] += column_sum(grad_hidden)
                    grad_act = following

            if between is not None:
                between()
            b_send[chunk] = nt(hidden_keep[...], wu[...]).astype(BF16)
            down_sum[...] += tn(low_columns, act_ref[...])
            up_sum[...] += tn(second, hidden_keep[...])

        def close():
            chunk = step - ahead - 1
            grad_second = b_send[chunk].astype(F32) + b_recv[chunk].astype(F32)
            unit, scale = kept_norm(unit2, scale2)
            vec2[2:3, :width] += column_sum(grad_second * unit)
            vec2[3:4, :width] += column_sum(grad_second)
            grad_middle = grad_keep[lax.rem(chunk, 2)] + norm_pull(
                grad_second, gain2[layer : layer + 1, :], unit, scale
            )
            dmid_out[...] = grad_middle
            vec2[4:5, :width] += column_sum(grad_middle)
            low = grad_middle.astype(BF16)
            last_keep[...] = low
            out_sum[...] += tn(last_keep[:, pair], mixed_ref[...])
            dmix_out[...] = nt(low, wo[...]).astype(BF16)

        if not top:

            @pl.when(step < chunks)
            def _():
                entry_products()
                meet()
                exchange(0, step).start()

        @pl.when((step >= ahead) & (step < chunks + ahead))
        def _():
            if not top:
                exchange(0, step - ahead).wait_recv()
            if not bottom:

                @pl.when(step == ahead)
                def _():
                    load(0).wait()

            feed_forward(lambda: pl.when(step == ahead)(lambda: load(1).wait()))
            if not bottom:
                if top:
                    meet()
                exchange(1, step - ahead).start()

        if not bottom:

            @pl.when(step == ahead + 1)
            def _():
                load(2).wait()

            @pl.when(step >= ahead + 1)
            def _():
                exchange(1, step - ahead - 1).wait_recv()
                close()

        if bottom:

            def x_copy(index):
                source, target = ((dx_send, dx_recv), (vec1, vec_recv))[index]
                return remote(
                    source, target, x_send_sem.at[index], x_recv_sem.at[index], beside, core
                )

            @pl.when(step == chunks + 1)
            def _():
                dx_send[...] = dx_keep[at(beside * place_rows, place_rows), :].astype(BF16)
                x_copy(0).start()
                x_copy(1).start()
                dx_out[...] = dx_keep[at(me * place_rows, place_rows), :]
                x_copy(0).wait_recv()
                x_copy(1).wait_recv()
                dx_other[...] = dx_recv[...].astype(F32)
                vec_other[...] = vec_recv[...]
                x_copy(0).wait_send()
                x_copy(1).wait_send()

        @pl.when(step == pl.num_programs(0) - 1)
        def _():
            for kind in ([] if top else [0]) + ([] if bottom else [1]):
                for chunk in range(chunks):
                    exchange(kind, chunk).wait_send()
            finish_swap()

    def rows(columns, behind):
        return pl.BlockSpec(
            (span, columns), lambda s: (jnp.clip(s - behind, 0, chunks - 1), 0)
        )

    vec = jax.ShapeDtypeStruct((8, VEC), F32)
    operands, in_specs, out_shape, out_specs, scratch = [], [], [], [], []
    if top:
        operands += list(entry)
        in_specs += [halves_spec(entry[0].shape, chunks, 0, span)]
    else:
        operands += list(entry)
        in_specs += [rows(features, 0)] * 3
        in_specs += [rows(width, ahead), rows(PAIR, ahead), rows(width, ahead)]
        in_specs += [
            pl.BlockSpec(
                (1, *entry[6].shape[1:]),
                lambda s: (above, 0, 0, 0),
                pipeline_mode=pl.Buffered(1),
            ),
            whole(entry[7]),
        ]
        narrow = jax.ShapeDtypeStruct((8, features), F32)
        out_shape += [narrow]
        out_specs += [whole_out((8, features))]
        scratch += [pltpu.VMEM((chunks, span, width), BF16)] * 2
    if not bottom:
        operands += list(upper[1:])
        in_specs += [rows(hidden_units, ahead)] * 2
        in_specs += [rows(width, ahead + 1), rows(PAIR, ahead + 1), rows(PAIR, ahead)]
        in_specs += [rows(mixed_features, ahead + 1)] + [ANYWHERE] * 3 + [whole(upper[10])]
        sums = [mixed_features, hidden_units, hidden_units]
        out_shape += [
            jax.ShapeDtypeStruct((total, width), F32),
            jax.ShapeDtypeStruct((total, mixed_features), BF16),
        ]
        out_shape += [jax.ShapeDtypeStruct((PAIR, size), F32) for size in sums] + [vec]
        out_specs += [rows(width, ahead + 1), rows(mixed_features, ahead + 1)]
        out_specs += [whole_out((PAIR, size)) for size in sums] + [whole_out((8, VEC))]
        scratch += [pltpu.VMEM((chunks, span, width), BF16)] * 2
        scratch += [
            pltpu.VMEM((2, span, width), F32),
            pltpu.VMEM((span, hidden_units), BF16),
            pltpu.VMEM((span, width), BF16),
            pltpu.VMEM((span, width), BF16),
            pltpu.VMEM(upper[7].shape[1:], BF16),
            pltpu.VMEM(upper[8].shape[1:], BF16),
            pltpu.VMEM(upper[9].shape[1:], BF16),
            pltpu.SemaphoreType.DMA((3,)),
        ]
    else:
        out_shape += [
            jax.ShapeDtypeStruct((place_rows, width), F32),
            jax.ShapeDtypeStruct((place_rows, width), F32),
            narrow,
        ]
        out_specs += [whole_out((place_rows, width))] * 2 + [whole_out((8, features))]
        scratch += [
            pltpu.VMEM((total, width), F32),
            pltpu.VMEM((place_rows, width), BF16),
            pltpu.VMEM((place_rows, width), BF16),
            pltpu.VMEM((8, features), F32),
            pltpu.SemaphoreType.DMA((2,)),
            pltpu.SemaphoreType.DMA((2,)),
        ]
    scratch += [pltpu.SemaphoreType.DMA((2, chunks))] * 2
    operands += swap.operands()
    in_specs += swap.in_specs()
    shapes, specs = swap.outputs()
    out_shape += shapes
    out_specs += specs
    scratch += swap.scratch()
    return pl.pallas_call(
        kernel,
        grid=(chunks + (1 if top else 2),),
        out_shape=out_shape,
        in_specs=in_specs,
        out_specs=out_specs,
        scratch_shapes=scratch,
        compiler_params=pltpu.CompilerParams(
            collective_id=identity, has_side_effects=True, vmem_limit_bytes=VMEM_BYTES
        ),
        name=f"rows_backward_{identity}",
    )(*operands)


def assemble(sums, vecs, lanes, n, features, hidden_units):
    place = lanes[1].shape[0]
    width = lanes[1].shape[1]
    half = PAIR // 2

    def kernel(*refs):
        refs = list(refs)

        def take(count):
            taken = refs[:count]
            del refs[:count]
            return taken

        qkvs, outs, ups, downs = take(LAYERS), take(LAYERS), take(LAYERS), take(LAYERS)
        vec_refs = [take(4) for _ in range(LAYERS)]
        out_lane, out_other, dx_own, dx_other = take(4)
        out_ref, dx_ref, gain1, shift1, g_qkv, b_qkv, g_out, b_out = take(8)
        gain2, shift2, g_up, b_up, g_down, b_down = take(6)
        out_own, sem = refs
        me = lax.axis_index("seq")
        x = lax.rem(me, 2)
        fetch = pltpu.make_async_copy(out_lane.at[at(me * place, place), :], out_own, sem)
        fetch.start()

        for layer in range(LAYERS):
            for part in range(3):
                g_qkv[layer, part] = qkvs[layer][:, part * features : (part + 1) * features]
            for ref, target in ((outs, g_out), (ups, g_up), (downs, g_down)):
                target[layer] = ref[layer][...]

        for layer, (entry_own, entry_other, upper_own, upper_other) in enumerate(vec_refs):
            line = slice(layer, layer + 1)
            for part in range(3):
                row = slice(part, part + 1)
                b_qkv[part, line, :] = entry_own[row, :] + entry_other[row, :]
            b_up[line, :] = upper_own[0:1, :hidden_units] + upper_other[0:1, :hidden_units]

            def owned(mine, other, row):
                wide = mine.shape[1]
                place = (me // 2) * PAIR
                pair = at(lax.rem(place, wide), PAIR)
                both = mine[row : row + 1, pair] + other[row : row + 1, pair]
                for later in range(1, width // wide):
                    line = slice(row + later, row + later + 1)
                    both = jnp.where(place // wide == later, mine[line, pair] + other[line, pair], both)
                return jnp.where(x == 0, both[:, :half], both[:, half:])

            gain1[line, :] = owned(entry_own, entry_other, 3)
            shift1[line, :] = owned(entry_own, entry_other, 5)
            b_down[line, :] = owned(upper_own, upper_other, 1)
            gain2[line, :] = owned(upper_own, upper_other, 2)
            shift2[line, :] = owned(upper_own, upper_other, 3)
            b_out[line, :] = owned(upper_own, upper_other, 4)

        def both_lanes(target, mine, other):
            target[:, 0, :] = jnp.where(x == 0, mine, other)
            target[:, 1, :] = jnp.where(x == 0, other, mine)

        both_lanes(dx_ref, dx_own[...], dx_other[...])
        fetch.wait()
        both_lanes(out_ref, out_own[...], out_other[...])

    def f32(*shape):
        return jax.ShapeDtypeStruct(shape, F32)

    in_vmem = pl.BlockSpec(memory_space=pltpu.VMEM)
    flat = []
    for kind in range(4):
        flat += [sums[layer][kind] for layer in range(LAYERS)]
    for layer in range(LAYERS):
        flat += list(vecs[layer])
    flat += list(lanes)
    small = f32(LAYERS, width // n)
    return pl.pallas_call(
        kernel,
        out_shape=(
            f32(place, 2, width),
            f32(place, 2, width),
            small,
            small,
            f32(LAYERS, 3, half, features),
            f32(3, LAYERS, features),
            f32(LAYERS, half, features),
            small,
            small,
            small,
            f32(LAYERS, half, hidden_units),
            f32(LAYERS, hidden_units),
            f32(LAYERS, half, hidden_units),
            small,
        ),
        in_specs=[in_vmem] * (len(flat) - 4) + [ANYWHERE] + [in_vmem] * 3,
        out_specs=(in_vmem,) * 14,
        scratch_shapes=[pltpu.VMEM((place, width), F32), pltpu.SemaphoreType.DMA],
        compiler_params=pltpu.CompilerParams(vmem_limit_bytes=VMEM_BYTES),
        name="assemble",
    )(*flat)


def per_chip(
    tokens,
    d_out,
    norm1_gain,
    norm1_shift,
    w_qkv,
    b_qkv,
    w_out,
    b_out,
    norm2_gain,
    norm2_shift,
    w_up,
    b_up,
    w_down,
    b_down,
    episode_frames,
    live,
):
    n = lax.axis_size("seq")
    rows = tokens.shape[0]
    features = w_qkv.shape[3]
    fixed, ahead = turn_constants(rows * n // FRAME)
    qkv, qkv_bias = w_qkv.transpose(0, 2, 1, 3), b_qkv.transpose(1, 0, 2)

    gathered, key_bias, frames, *projected = gather_and_project(
        tokens, live.T, episode_frames, norm1_gain, norm1_shift, qkv, qkv_bias, fixed, ahead, n
    )
    streams, kept, d_lane = [gathered], [], None
    for layer in range(LAYERS):
        results = layer_forward(
            layer,
            *projected[:3],
            key_bias,
            streams[layer],
            (w_out, w_up, w_down),
            (b_out, norm2_gain, norm2_shift, b_up, b_down),
            d_out if layer == 0 else None,
            n,
            1 + layer,
        )
        kept.append((*projected, *results[:8]))
        streams.append(results[8])
        if layer + 1 < LAYERS:
            projected = later_projection(
                layer + 1, results[8], norm1_gain, norm1_shift, qkv, qkv_bias, fixed, frames
            )
        if layer == 0:
            d_lane = results[-1]

    sums = [[None] * 4 for _ in range(LAYERS)]
    vecs = [[None] * 4 for _ in range(LAYERS)]
    entry, later = (d_lane,), None
    for layer in reversed(range(LAYERS)):
        query, key, value, first, unit1, scale1, probs, divisor, mixed = kept[layer][:9]
        unit2, scale2, second, act, slope = kept[layer][9:]
        upper = (
            layer,
            act,
            slope,
            unit2,
            scale2,
            second,
            mixed,
            w_out,
            w_up,
            w_down,
            norm2_gain,
        )
        identity = 1 + LAYERS + 2 * (LAYERS - 1 - layer)
        if later is None:
            results = rows_backward(entry, upper, identity, FRAME, Swap([], []))
        else:
            swap = Swap(later[:2], [(later[2], 0), (streams[LAYERS], rows)])
            vec1, *results = rows_backward(entry, upper, identity, FRAME, swap)
            results, swapped = results[:6], results[6:]
            sums[layer + 1][3], sums[layer + 1][0] = swapped[:2]
            vecs[layer + 1][3], out_other = swapped[2:]
            vecs[layer + 1][0] = vec1
        grad_middle, grad_mixed, out_sum, up_sum, down_sum, vec2 = results
        vecs[layer][2] = vec2
        last = layer == 0
        if last:
            swap = Swap([out_sum, up_sum], [(vec2, 0), (vecs[layer + 1][0], 0)])
        else:
            swap = Swap([out_sum, up_sum], [])
        results = attention_backward(
            probs,
            divisor,
            mixed,
            query,
            key,
            value,
            grad_mixed,
            first,
            fixed,
            frames,
            swap,
            last,
            identity + 1,
        )
        grad_query, grad_key, grad_value, qkv_sum = results[:4]
        if last:
            sums[layer][:3] = [qkv_sum, *results[4:6]]
            vecs[layer][3], vecs[layer + 1][1] = results[6:8]
        else:
            sums[layer][1:3] = results[4:6]
            later = [down_sum, qkv_sum, vec2]
        entry = (
            layer,
            grad_query,
            grad_key,
            grad_value,
            unit1,
            scale1,
            grad_middle,
            qkv,
            norm1_gain,
        )
    vec1, dx_own, dx_other, vec_other, sums[0][3] = rows_backward(
        entry, None, 1 + 3 * LAYERS, FRAME, Swap([down_sum], [])
    )
    vecs[0][:2] = [vec1, vec_other]
    results = list(
        assemble(
            sums,
            vecs,
            (streams[LAYERS], out_other, dx_own, dx_other),
            n,
            features,
            w_up.shape[2],
        )
    )
    results[4] = results[4].transpose(0, 2, 1, 3)
    results[5] = results[5].transpose(1, 0, 2)
    results[6] = results[6].transpose(0, 2, 1)
    results[12] = results[12].transpose(0, 2, 1)
    return tuple(results)


def lane_fits(mesh, tokens):
    n = mesh.shape["seq"]
    positions, lanes, width = tokens.shape
    rows = positions // n
    return (
        lanes == 2
        and n % 4 == 0
        and positions <= 4 * FRAME
        and positions % FRAME == 0
        and FRAME % rows == 0
        and width // n * 2 == PAIR
        and mesh.shape["tp"] == 2
    )


def solution(mesh):
    placed = (
        P("seq", None, None),
        P("seq", None, None),
        P(),
        P(),
        P(None, None, None, "tp"),
        P(None, None, "tp"),
        P(None, "tp", None),
        P(),
        P(),
        P(),
        P(None, None, "tp"),
        P(None, "tp"),
        P(None, "tp", None),
        P(),
        P(),
        P("seq", None),
    )
    def mapped(body):
        return jax.shard_map(
            body,
            mesh=mesh,
            in_specs=placed,
            out_specs=(
                P("seq", None, None),
                P("seq", None, None),
                P(None, "seq"),
                P(None, "seq"),
                P(None, "seq", None, "tp"),
                P(None, None, "tp"),
                P(None, "tp", "seq"),
                P(None, "seq"),
                P(None, "seq"),
                P(None, "seq"),
                P(None, "seq", "tp"),
                P(None, "tp"),
                P(None, "tp", "seq"),
                P(None, "seq"),
            ),
            check_vma=False,
        )

    def run(tokens, *others):
        if lane_fits(mesh, tokens):
            return mapped(per_chip)(tokens, *others)
        return mapped(per_device)(tokens, *others)

    return run
```

```python
import math

import jax
import jax.numpy as jnp
import numpy as np
from jax import lax
from jax.experimental import pallas as pl
from jax.experimental.pallas import tpu as pltpu
from jax.sharding import PartitionSpec as P

HEAD_DIM = 64
GRID = 16
FRAME = 256
LAYERS = 2
MICRO = 2


EPSILON = 1e-06
MASKED = -1e30
SCORE_SCALE = 0.125


def layer_norm(stream, norm_gain, norm_shift):
    center = stream - jnp.mean(stream, axis=-1, keepdims=True)
    spread = jnp.mean(center * center, axis=-1, keepdims=True)
    return center * lax.rsqrt(spread + EPSILON) * norm_gain + norm_shift


def rotate(values, frame_place, row_place, column_place):
    frequency = jnp.exp(jnp.arange(10, dtype=jnp.float32) * (-math.log(10000.0) / 10.0))
    pieces = []
    for section, place in enumerate((frame_place, row_place, column_place)):
        lower = values[..., 20 * section : 20 * section + 10]
        upper = values[..., 20 * section + 10 : 20 * section + 20]
        angles = place.astype(jnp.float32)[..., None, None] * frequency
        cosine = jnp.cos(angles)
        sine_part = jnp.sin(angles)
        pieces.append(lower * cosine - upper * sine_part)
        pieces.append(lower * sine_part + upper * cosine)
    pieces.append(values[..., 60:])
    return jnp.concatenate(pieces, axis=-1)


def episode_tags(frame_counts, positions):
    endings = jnp.cumsum(frame_counts) * FRAME
    passed = (positions[:, None] >= endings[None, :]).astype(jnp.int32)
    episode = jnp.sum(passed, axis=1)
    opening = jnp.sum(passed * frame_counts[None, :], axis=1)
    frame_index = positions // FRAME - opening
    within = positions % FRAME
    return (episode, frame_index, within // GRID, within % GRID)


def gelu_exact(values):
    return jax.nn.gelu(values, approximate=False)


def sum_heads(partial_sum):
    return lax.psum(partial_sum.astype(jnp.bfloat16), "tp").astype(jnp.float32)


def sum_inputs(partial_sum):
    return lax.psum(partial_sum.astype(jnp.bfloat16), "tp").astype(jnp.float32)


def lane_scores(query, keys_all, lane_index, query_tags, key_tags):
    head_count = query.shape[2] // HEAD_DIM
    query_lane = lax.dynamic_index_in_dim(query, lane_index, 1, False).reshape(
        query.shape[0], head_count, HEAD_DIM
    )
    keys_lane = lax.dynamic_index_in_dim(keys_all, lane_index, 1, False).reshape(
        keys_all.shape[0], head_count, HEAD_DIM
    )
    query_episode, query_frame = [
        lax.dynamic_index_in_dim(item, lane_index, 1, False) for item in query_tags
    ]
    key_episode, key_frame, key_live = [
        lax.dynamic_index_in_dim(item, lane_index, 1, False) for item in key_tags
    ]
    allowed = (
        (query_episode[:, None] == key_episode[None, :])
        & (key_frame[None, :] <= query_frame[:, None])
        & (key_live[None, :] > 0)
    )
    scores = (
        jnp.einsum("qhd,khd->hqk", query_lane, keys_lane, preferred_element_type=jnp.float32)
        * SCORE_SCALE
    )
    return (jnp.where(allowed[None], scores, MASKED), query_lane, keys_lane)


def attend_forward(query, keys_all, values_all, query_tags, key_tags):
    rows_dev, lane_count, features = query.shape
    head_count = features // HEAD_DIM

    def one_lane(lane_index, carry):
        scores, query_lane, keys_lane = lane_scores(
            query, keys_all, lane_index, query_tags, key_tags
        )
        highest = jnp.max(scores, axis=-1, keepdims=True)
        shifted = jnp.exp(scores - highest)
        summed = jnp.sum(shifted, axis=-1, keepdims=True)
        attention = (shifted / summed).astype(jnp.bfloat16)
        values_lane = lax.dynamic_index_in_dim(values_all, lane_index, 1, False).reshape(
            values_all.shape[0], head_count, HEAD_DIM
        )
        result = jnp.einsum(
            "hqk,khd->qhd", attention, values_lane, preferred_element_type=jnp.float32
        ).reshape(rows_dev, 1, features)
        log_total = (highest + jnp.log(summed))[None, :, :, 0]
        return (result, log_total)

    initial = (
        jnp.zeros((rows_dev, lane_count, features), jnp.float32),
        jnp.zeros((lane_count, head_count, rows_dev), jnp.float32),
    )
    return lax.fori_loop(0, lane_count, one_lane, initial)


def attend_backward(query, keys_all, values_all, log_total, grad_mixed, query_tags, key_tags):
    rows_dev, lane_count, features = query.shape
    head_count = features // HEAD_DIM
    key_rows = keys_all.shape[0]

    def one_lane(lane_index, carry):
        scores, query_lane, keys_lane = lane_scores(
            query, keys_all, lane_index, query_tags, key_tags
        )
        values_lane = lax.dynamic_index_in_dim(values_all, lane_index, 1, False).reshape(
            key_rows, head_count, HEAD_DIM
        )
        grad_lane = lax.dynamic_index_in_dim(grad_mixed, lane_index, 1, False).reshape(
            rows_dev, head_count, HEAD_DIM
        )
        attention = jnp.exp(
            scores - lax.dynamic_index_in_dim(log_total, lane_index, 0, False)[:, :, None]
        )
        grad_attention = jnp.einsum(
            "qhd,khd->hqk", grad_lane, values_lane, preferred_element_type=jnp.float32
        )
        inner = jnp.sum(attention * grad_attention, axis=-1, keepdims=True)
        grad_scores = (attention * (grad_attention - inner)).astype(jnp.bfloat16)
        query_part = (
            jnp.einsum("hqk,khd->qhd", grad_scores, keys_lane, preferred_element_type=jnp.float32)
            * SCORE_SCALE
        )
        key_part = (
            jnp.einsum("hqk,qhd->khd", grad_scores, query_lane, preferred_element_type=jnp.float32)
            * SCORE_SCALE
        )
        value_part = jnp.einsum(
            "hqk,qhd->khd",
            attention.astype(jnp.bfloat16),
            grad_lane,
            preferred_element_type=jnp.float32,
        )
        stacked = jnp.stack(
            [key_part.reshape(key_rows, features), value_part.reshape(key_rows, features)], axis=1
        )
        key_terms = stacked[:, None]
        grad_query = query_part.reshape(rows_dev, 1, features)
        return (grad_query, key_terms)

    initial = (
        jnp.zeros((rows_dev, lane_count, features), jnp.float32),
        jnp.zeros((key_rows, lane_count, 2, features), jnp.float32),
    )
    return lax.fori_loop(0, lane_count, one_lane, initial)


def front(stream, layer_index, params, query_tags, key_tags, positions):
    (
        gain_one,
        shift_one,
        mat_qkv,
        bias_qkv,
        mat_out,
        bias_out,
        gain_two,
        shift_two,
        mat_up,
        bias_up,
        mat_down,
        bias_down,
    ) = [item[layer_index] for item in params]
    rows_dev, lane_count, width = stream.shape
    features = mat_qkv.shape[2]
    head_count = features // HEAD_DIM
    frame_place, row_place, column_place = positions
    first = layer_norm(stream, gain_one, shift_one).astype(jnp.bfloat16)
    projected = (
        jnp.einsum("tbd,dcf->tbcf", first, mat_qkv, preferred_element_type=jnp.float32) + bias_qkv
    )
    split = projected.reshape(rows_dev, lane_count, 3, head_count, HEAD_DIM)
    query = (
        rotate(split[:, :, 0], frame_place, row_place, column_place)
        .reshape(rows_dev, lane_count, features)
        .astype(jnp.bfloat16)
    )
    keys = (
        rotate(split[:, :, 1], frame_place, row_place, column_place)
        .reshape(rows_dev, lane_count, features)
        .astype(jnp.bfloat16)
    )
    values = projected[:, :, 2].astype(jnp.bfloat16)
    keys_all, values_all = (
        lax.all_gather(keys, "seq", axis=0, tiled=True),
        lax.all_gather(values, "seq", axis=0, tiled=True),
    )
    mixed_full, log_total = attend_forward(query, keys_all, values_all, query_tags, key_tags)
    mixed = mixed_full.astype(jnp.bfloat16)
    middle = (
        stream
        + sum_heads(jnp.einsum("tbf,fd->tbd", mixed, mat_out, preferred_element_type=jnp.float32))
        + bias_out
    )
    second = layer_norm(middle, gain_two, shift_two).astype(jnp.bfloat16)
    hidden = jnp.einsum("tbd,df->tbf", second, mat_up, preferred_element_type=jnp.float32) + bias_up
    activation = gelu_exact(hidden).astype(jnp.bfloat16)
    return (
        first,
        query,
        keys_all,
        values_all,
        log_total,
        mixed,
        middle,
        second,
        hidden,
        activation,
        mixed_full,
    )


def layer_backward(stream, gradient, layer_index, params, query_tags, key_tags, positions):
    (
        gain_one,
        shift_one,
        mat_qkv,
        bias_qkv,
        mat_out,
        bias_out,
        gain_two,
        shift_two,
        mat_up,
        bias_up,
        mat_down,
        bias_down,
    ) = [item[layer_index] for item in params]
    (
        first,
        query,
        keys_all,
        values_all,
        log_total,
        mixed,
        middle,
        second,
        hidden,
        activation,
        mixed_full,
    ) = front(stream, layer_index, params, query_tags, key_tags, positions)
    frame_place, row_place, column_place = positions
    rows_dev, lane_count, width = stream.shape
    features = query.shape[2]
    head_count = features // HEAD_DIM
    grad_low = gradient.astype(jnp.bfloat16)
    grad_w_down = jnp.einsum(
        "tbf,tbd->fd", activation, grad_low, preferred_element_type=jnp.float32
    )
    grad_b_down = jnp.sum(gradient, axis=(0, 1))
    grad_activation = jnp.einsum(
        "tbd,fd->tbf", grad_low, mat_down, preferred_element_type=jnp.float32
    )
    grad_hidden = jax.vjp(gelu_exact, hidden)[1](grad_activation)[0].astype(jnp.bfloat16)
    grad_b_up = jnp.sum(grad_hidden.astype(jnp.float32), axis=(0, 1))
    grad_w_up = jnp.einsum("tbd,tbf->df", second, grad_hidden, preferred_element_type=jnp.float32)
    grad_second = sum_inputs(
        jnp.einsum("tbf,df->tbd", grad_hidden, mat_up, preferred_element_type=jnp.float32)
    )
    middle_pull = jax.vjp(layer_norm, middle, gain_two, shift_two)[1]
    grad_inner, grad_gain_two, grad_shift_two = middle_pull(grad_second)
    grad_middle = gradient + grad_inner
    grad_b_out = jnp.sum(grad_middle, axis=(0, 1))
    middle_low = grad_middle.astype(jnp.bfloat16)
    grad_w_out = jnp.einsum("tbf,tbd->fd", mixed, middle_low, preferred_element_type=jnp.float32)
    grad_mixed = jnp.einsum(
        "tbd,fd->tbf", middle_low, mat_out, preferred_element_type=jnp.float32
    ).astype(jnp.bfloat16)
    grad_query, key_terms = attend_backward(
        query, keys_all, values_all, log_total, grad_mixed, query_tags, key_tags
    )
    returned = lax.psum_scatter(key_terms, "seq", scatter_dimension=0, tiled=True)
    turned_query = rotate(
        grad_query.reshape(rows_dev, lane_count, head_count, HEAD_DIM),
        -frame_place,
        -row_place,
        -column_place,
    )
    turned_keys = rotate(
        returned[:, :, 0].reshape(rows_dev, lane_count, head_count, HEAD_DIM),
        -frame_place,
        -row_place,
        -column_place,
    )
    grad_projected = jnp.stack(
        [
            turned_query.reshape(rows_dev, lane_count, features),
            turned_keys.reshape(rows_dev, lane_count, features),
            returned[:, :, 1],
        ],
        axis=2,
    ).astype(jnp.bfloat16)
    grad_b_qkv = jnp.sum(grad_projected.astype(jnp.float32), axis=(0, 1))
    grad_w_qkv = jnp.einsum(
        "tbd,tbcf->dcf", first, grad_projected, preferred_element_type=jnp.float32
    )
    grad_first = sum_inputs(
        jnp.einsum("tbcf,dcf->tbd", grad_projected, mat_qkv, preferred_element_type=jnp.float32)
    )
    first_pull = jax.vjp(layer_norm, stream, gain_one, shift_one)[1]
    grad_entry, grad_gain_one, grad_shift_one = first_pull(grad_first)
    grads = (
        grad_gain_one,
        grad_shift_one,
        grad_w_qkv,
        grad_b_qkv,
        grad_w_out,
        grad_b_out,
        grad_gain_two,
        grad_shift_two,
        grad_w_up,
        grad_b_up,
        grad_w_down,
        grad_b_down,
    )
    return (grad_middle + grad_entry, grads)


def per_device(
    tokens,
    d_out,
    norm1_gain,
    norm1_shift,
    w_qkv,
    b_qkv,
    w_out,
    b_out,
    norm2_gain,
    norm2_shift,
    w_up,
    b_up,
    w_down,
    b_down,
    episode_frames,
    live,
):
    rows_dev = tokens.shape[0]
    lane_count = tokens.shape[1] // MICRO
    total_rows = rows_dev * lax.axis_size("seq")
    local_positions = lax.axis_index("seq") * rows_dev + jnp.arange(rows_dev, dtype=jnp.int32)
    key_positions = jnp.arange(total_rows, dtype=jnp.int32)
    tagger = jax.vmap(episode_tags, in_axes=(0, None), out_axes=1)
    query_episode, query_frame, query_row, query_column = tagger(episode_frames, local_positions)
    key_episode, key_frame, key_row, key_column = tagger(episode_frames, key_positions)
    live_keys = lax.all_gather(live, "seq", axis=0, tiled=True)
    params = (
        norm1_gain,
        norm1_shift,
        w_qkv,
        b_qkv,
        w_out,
        b_out,
        norm2_gain,
        norm2_shift,
        w_up,
        b_up,
        w_down,
        b_down,
    )
    layer_grads = [None] * LAYERS
    outputs = []
    grad_tokens = []
    for micro_index in range(MICRO):
        first_lane = micro_index * lane_count
        last_lane = first_lane + lane_count
        query_tags = (query_episode[:, first_lane:last_lane], query_frame[:, first_lane:last_lane])
        key_tags = (
            key_episode[:, first_lane:last_lane],
            key_frame[:, first_lane:last_lane],
            live_keys[:, first_lane:last_lane],
        )
        positions = (
            query_frame[:, first_lane:last_lane],
            query_row[:, first_lane:last_lane],
            query_column[:, first_lane:last_lane],
        )
        stream = tokens[:, first_lane:last_lane].astype(jnp.float32)
        inputs = []
        gathered = []
        for layer_index in range(LAYERS):
            inputs.append(stream)
            layer_state = front(stream, layer_index, params, query_tags, key_tags, positions)
            gathered.append((layer_state[2], layer_state[3]))
            branch = jnp.einsum(
                "tbf,fd->tbd",
                layer_state[9],
                w_down[layer_index],
                preferred_element_type=jnp.float32,
            )
            stream = layer_state[6] + sum_heads(branch) + b_down[layer_index]
        outputs.append(stream)
        gradient = d_out[:, first_lane:last_lane]
        for layer_index in reversed(range(LAYERS)):
            gradient, grads = layer_backward(
                inputs[layer_index], gradient, layer_index, params, query_tags, key_tags, positions
            )
            if layer_grads[layer_index] is None:
                layer_grads[layer_index] = grads
            else:
                layer_grads[layer_index] = jax.tree.map(jnp.add, layer_grads[layer_index], grads)
        grad_tokens.append(gradient)
    stacked = [
        jnp.stack([layer_grads[layer_index][entry] for layer_index in range(LAYERS)])
        for entry in range(12)
    ]
    (
        grad_gain_one,
        grad_shift_one,
        grad_w_qkv,
        grad_b_qkv,
        grad_w_out,
        grad_b_out,
        grad_gain_two,
        grad_shift_two,
        grad_w_up,
        grad_b_up,
        grad_w_down,
        grad_b_down,
    ) = stacked
    in_sums = (
        lax.psum_scatter(grad_w_qkv, "seq", scatter_dimension=1, tiled=True),
        lax.psum_scatter(grad_w_up, "seq", scatter_dimension=1, tiled=True),
        lax.psum_scatter(grad_gain_one, "seq", scatter_dimension=1, tiled=True),
        lax.psum_scatter(grad_shift_one, "seq", scatter_dimension=1, tiled=True),
        lax.psum_scatter(grad_gain_two, "seq", scatter_dimension=1, tiled=True),
        lax.psum_scatter(grad_shift_two, "seq", scatter_dimension=1, tiled=True),
        lax.psum_scatter(grad_b_out, "seq", scatter_dimension=1, tiled=True),
        lax.psum_scatter(grad_b_down, "seq", scatter_dimension=1, tiled=True),
    )
    out_sums = (
        lax.psum_scatter(grad_w_out, "seq", scatter_dimension=2, tiled=True),
        lax.psum_scatter(grad_w_down, "seq", scatter_dimension=2, tiled=True),
    )
    bias_total = lax.psum((grad_b_qkv, grad_b_up), "seq")
    return (
        jnp.concatenate(outputs, axis=1),
        jnp.concatenate(grad_tokens, axis=1),
        in_sums[2],
        in_sums[3],
        in_sums[0],
        bias_total[0],
        out_sums[0],
        in_sums[6],
        in_sums[4],
        in_sums[5],
        in_sums[1],
        bias_total[1],
        out_sums[1],
        in_sums[7],
    )


MESH = pl.DeviceIdType.MESH
BF16 = jnp.bfloat16
F32 = jnp.float32
VMEM_BYTES = 60 * 1024 * 1024
PAIR = 128
VEC = 2048


def nn(left, right):
    return lax.dot_general(left, right, (((1,), (0,)), ((), ())), preferred_element_type=F32)


def nt(left, right):
    return lax.dot_general(left, right, (((1,), (1,)), ((), ())), preferred_element_type=F32)


def tn(left, right):
    return lax.dot_general(left, right, (((0,), (0,)), ((), ())), preferred_element_type=F32)


def at(start, size):
    return pl.ds(pl.multiple_of(start, size), size)


def remote(src, dst, send, recv, seq, tp):
    return pltpu.make_async_remote_copy(
        src_ref=src,
        dst_ref=dst,
        send_sem=send,
        recv_sem=recv,
        device_id=(seq, tp),
        device_id_type=MESH,
    )


def hello(partners):
    barrier = pltpu.get_barrier_semaphore()
    for seq, tp in partners:
        pl.semaphore_signal(barrier, inc=1, device_id=(seq, tp), device_id_type=MESH)


def met(partners):
    pl.semaphore_wait(pltpu.get_barrier_semaphore(), len(partners))


def whole(array):
    zeros = (0,) * array.ndim
    return pl.BlockSpec(array.shape, lambda s: zeros, pipeline_mode=pl.Buffered(1))


def whole_out(shape):
    zeros = (0,) * len(shape)
    return pl.BlockSpec(shape, lambda s: zeros)


ANYWHERE = pl.BlockSpec(memory_space=pl.ANY)


def turn_row(table, place, section):
    frequency = np.exp(np.arange(10, dtype=np.float32) * np.float32(-math.log(10000.0) / 10.0))
    angle = place.astype(np.float32)[:, None] * frequency
    for base in range(20 * section, PAIR, HEAD_DIM):
        table[0, :, base : base + 10] = np.cos(angle)
        table[0, :, base + 10 : base + 20] = np.cos(angle)
        table[1, :, base : base + 10] = -np.sin(angle)
        table[2, :, base + 10 : base + 20] = np.sin(angle)


def turn_constants(frames):
    within, ahead = np.zeros((3, FRAME, PAIR), np.float32), np.zeros((3, frames, PAIR), np.float32)
    turn_row(within, np.arange(FRAME) // GRID, 1)
    turn_row(within, np.arange(FRAME) % GRID, 2)
    for base in range(60, PAIR, HEAD_DIM):
        within[0, :, base : base + 4] = 1.0
    turn_row(ahead, np.arange(frames), 0)
    return jnp.asarray(within), jnp.asarray(ahead)


def turn(values, tables, back=False):
    cosine, lower, upper = tables
    pieces = []
    for start in range(0, values.shape[1], PAIR):
        slab = values[:, start : start + PAIR]
        moved = pltpu.roll(slab, PAIR - 10, 1) * lower + pltpu.roll(slab, 10, 1) * upper
        pieces.append(slab * cosine - moved if back else slab * cosine + moved)
    return jnp.concatenate(pieces, axis=1)


def tables_of(fixed_ref, frames_ref, chunk):
    return [fixed_ref[i] + frames_ref[i, pl.ds(chunk, 1), :] for i in range(3)]


def normed(stream):
    center = stream - jnp.mean(stream, axis=-1, keepdims=True)
    spread = jnp.mean(center * center, axis=-1, keepdims=True)
    scale = lax.rsqrt(spread + EPSILON)
    return center * scale, scale


def norm_pull(grad, gain, unit, scale):
    scaled = grad * gain
    return scale * (
        scaled
        - jnp.mean(scaled, axis=-1, keepdims=True)
        - unit * jnp.mean(scaled * unit, axis=-1, keepdims=True)
    )


def keep_norm(unit, scale, unit_ref, scale_ref):
    unit_ref[...] = unit.astype(BF16)
    scale_ref[...] = jnp.broadcast_to(scale, scale_ref.shape)


def kept_norm(unit_ref, scale_ref):
    copies = unit_ref.shape[1] // scale_ref.shape[1]
    return unit_ref[...].astype(F32), jnp.concatenate([scale_ref[...]] * copies, axis=1)


def column_sum(values):
    return jnp.sum(values, axis=0, keepdims=True)


def gelu_both(hidden):
    normal = 0.5 + 0.5 * lax.erf(hidden * math.sqrt(0.5))
    density = jnp.exp(hidden * hidden * -0.5) * (1.0 / math.sqrt(2.0 * math.pi))
    return hidden * normal, normal + hidden * density


def project(stream, chunk, layer, pair, refs, outs, first_full):
    gain, shift, weight, bias, fixed, frames = refs
    query_ref, key_ref, value_ref, first_ref, unit_ref, scale_ref = outs
    unit, scale = normed(stream)
    keep_norm(unit, scale, unit_ref, scale_ref)
    first = (unit * gain[layer : layer + 1, :] + shift[layer : layer + 1, :]).astype(BF16)
    first_full[...] = first
    first_ref[...] = first_full[:, at(pair * PAIR, PAIR)]
    tables = tables_of(fixed, frames, chunk)
    query = nn(first, weight[0]) + bias[0, layer : layer + 1, :]
    query_ref[...] = (turn(query, tables) * SCORE_SCALE).astype(BF16)
    key = nn(first, weight[1]) + bias[1, layer : layer + 1, :]
    key_ref[...] = turn(key, tables).astype(BF16)
    value = nn(first, weight[2]) + bias[2, layer : layer + 1, :]
    value_ref[...] = value.astype(BF16)


class Relay:
    sems = 6

    def __init__(self, n, rows, buffer, other, sems, lives=None, live_other=None):
        self.n, self.rows, self.buffer, self.other = n, rows, buffer, other
        self.lives, self.live_other = lives, live_other
        self.z_send, self.z_recv, self.y_send, self.y_recv, self.c_send, self.c_recv = sems
        self.planes = n // 4
        self.me, self.core = lax.axis_index("seq"), lax.axis_index("tp")
        me = self.me
        self.x, self.y, self.z = lax.rem(me, 2), lax.rem(me // 2, 2), me // 4
        self.across = me + 2 - 4 * self.y

    @staticmethod
    def scratch(n):
        dma, planes = pltpu.SemaphoreType.DMA, n // 4
        shapes = [(planes, 2, 2)] * 2 + [(planes, 2)] * 2 + [(2 * planes,)] * 2
        return [dma(shape) for shape in shapes]

    @property
    def events(self):
        return self.planes

    def plane(self, step):
        return lax.rem(self.z + step, self.planes)

    def place(self, plane, lane):
        return plane * 4 + self.y * 2 + lane

    def reached(self):
        return [(step, far) for step in range(self.planes) for far in (0, 1) if step or far]

    def hello(self):
        barrier = pltpu.get_barrier_semaphore()
        partners = [(self.across, self.core), (self.me, 1 - self.core)]
        for step, far in self.reached():
            lane = 1 - self.x if far else self.x
            partners.append((self.place(self.plane(step), lane), self.core))
        for seq, tp in partners:
            pl.semaphore_signal(barrier, inc=1, device_id=(seq, tp), device_id_type=MESH)

    def met(self):
        pl.semaphore_wait(pltpu.get_barrier_semaphore(), 2 + len(self.reached()))

    def rows_of(self, side, seq):
        return self.buffer.at[side, at(seq * self.rows, self.rows), :]

    def block(self, side, pair):
        return self.buffer.at[side, at(pair * 2 * self.rows, 2 * self.rows), :]

    def items(self, pair):
        found = [self.block(self.core, pair)]
        if self.lives is not None:
            found.append(self.lives.at[at(pair * 2, 2)])
        return found

    def each(self, copy, what):
        for index in range(1 if self.lives is None else 2):
            getattr(copy(index), what)()

    def z_copy(self, step, far):
        def copy(index):
            lane = 1 - self.x if far else self.x
            if index == 0:
                source = self.other.at[self.core] if far else self.rows_of(self.core, self.me)
                target = self.rows_of(self.core, self.me)
            else:
                source = self.live_other if far else self.lives.at[self.me]
                target = self.lives.at[self.me]
            return remote(
                source,
                target,
                self.z_send.at[step, far, index],
                self.z_recv.at[step, far, index],
                self.place(self.plane(step), lane),
                self.core,
            )

        return copy

    def y_copy(self, plane, row):
        def copy(index):
            item = self.items(plane * 2 + row)[index]
            return remote(
                item,
                item,
                self.y_send.at[plane, index],
                self.y_recv.at[plane, index],
                self.across,
                self.core,
            )

        return copy

    def c_copy(self, pair, side):
        item = self.block(side, pair)
        return remote(
            item, item, self.c_send.at[pair], self.c_recv.at[pair], self.me, 1 - self.core
        )

    def begin(self):
        for step, far in self.reached():
            self.each(self.z_copy(step, far), "start")

    def arrive(self, event):
        for far in (0, 1) if event else (1,):
            self.each(self.z_copy(event, far), "wait_recv")
        plane = self.plane(self.planes - event)
        self.each(self.y_copy(plane, self.y), "start")
        self.c_copy(plane * 2 + self.y, self.core).start()

    def complete(self, event):
        plane = self.plane(self.planes - event)
        self.each(self.y_copy(plane, 1 - self.y), "wait_recv")
        self.c_copy(plane * 2 + 1 - self.y, self.core).start()

    def ready(self, event):
        plane = self.plane(self.planes - event)
        self.c_copy(plane * 2, 1 - self.core).wait_recv()
        self.c_copy(plane * 2 + 1, 1 - self.core).wait_recv()
        return plane

    def finish(self):
        for step, far in self.reached():
            self.each(self.z_copy(step, far), "wait_send")
        for plane in range(self.planes):
            self.each(self.y_copy(plane, self.y), "wait_send")
        for pair in range(2 * self.planes):
            self.c_copy(pair, self.core).wait_send()


def split_lanes(values, x, buffer, other, start, rows):
    half = values.shape[2] // 2
    zero, one = values[:, 0, :], values[:, 1, :]
    own, far = jnp.where(x == 0, zero, one), jnp.where(x == 0, one, zero)
    core = lax.axis_index("tp")
    own = jnp.where(core == 0, own[:, :half], own[:, half:]).astype(BF16)
    buffer[core, at(start, rows), :] = own
    for side in range(2):
        other[side] = far[:, side * half : (side + 1) * half].astype(BF16)


def gather_and_project(tokens, live, episode_frames, gain, shift, qkv, bias, fixed, ahead, n):
    rows, lanes, width = tokens.shape
    half = width // 2
    total = n * rows
    chunks = total // FRAME
    per_frame = FRAME // rows
    features = qkv.shape[3]
    slots = episode_frames.shape[1]

    def kernel(*refs):
        refs = list(refs)

        def take(count):
            taken = refs[:count]
            del refs[:count]
            return taken

        tokens_ref, live_ref, counts_ref, gain_ref, shift_ref, w_any, bias_ref = take(7)
        fixed_ref, ahead_ref = take(2)
        all_ref, mask_ref, frames_ref = take(3)
        projected = take(6)
        other, lives, live_other, weight, full, wide, taken_apart, w_sem = take(8)
        relay = Relay(n, rows, all_ref, other, take(Relay.sems), lives, live_other)
        load = pltpu.make_async_copy(w_any.at[0], weight, w_sem)
        load.start()
        relay.hello()
        x, me = relay.x, relay.me
        taken_apart[...] = tokens_ref[...].astype(F32)
        split_lanes(taken_apart, x, all_ref, other, me * rows, rows)
        lane = lax.broadcasted_iota(jnp.int32, (1, FRAME), 1)
        here = lane // rows == lax.rem(me, per_frame)
        tiles = []
        for index in range(lanes):
            alive = live_ref[index : index + 1, :].astype(F32)
            alive = jnp.where(here, jnp.concatenate([alive] * per_frame, axis=1), 0.0)
            tiles.append(jnp.broadcast_to(alive, (8, FRAME)))
        lives[me] = jnp.where(x == 0, tiles[0], tiles[1])
        live_other[...] = jnp.where(x == 0, tiles[1], tiles[0])
        relay.met()
        relay.begin()

        counts = [counts_ref[x, slot] for slot in range(slots)]
        episodes, openings = [], []
        for frame in range(chunks):
            end, episode, opening = 0, 0, 0
            for slot in range(slots):
                end = end + counts[slot]
                passed = frame >= end
                episode = episode + passed.astype(jnp.int32)
                opening = opening + jnp.where(passed, counts[slot], 0)
            episodes.append(episode)
            openings.append(frame - opening)
        for index in range(3):
            table = []
            for frame in range(chunks):
                line = jnp.zeros((1, PAIR), F32)
                for choice in range(chunks):
                    line = jnp.where(
                        openings[frame] == choice, ahead_ref[index, choice : choice + 1, :], line
                    )
                table.append(line)
            frames_ref[index] = jnp.concatenate(
                table + [jnp.zeros((8 - chunks, PAIR), F32)], axis=0
            )
        load.wait()

        def project_frame(frame):
            place = at(frame * FRAME, FRAME)
            widen(all_ref.at[:, place, :], wide)
            project(
                wide[...],
                frame,
                0,
                me // 2,
                (gain_ref, shift_ref, weight, bias_ref, fixed_ref, frames_ref),
                [ref.at[place, :] for ref in projected],
                full,
            )

        for event in range(relay.events):
            relay.arrive(event)
            if event:
                relay.complete(event - 1)
            if event > 1:
                project_frame(relay.ready(event - 2))
        relay.complete(relay.events - 1)
        for event in range(max(0, relay.events - 2), relay.events):
            project_frame(relay.ready(event))
        relay.finish()

        for key_frame in range(chunks):
            alive = lives[key_frame * per_frame, 0:1, :]
            for part in range(1, per_frame):
                alive = alive + lives[key_frame * per_frame + part, 0:1, :]
            closed = (alive - 1.0) * -MASKED
            lines = []
            for query_frame in range(chunks):
                allowed = (episodes[query_frame] == episodes[key_frame]) & (
                    openings[key_frame] <= openings[query_frame]
                )
                lines.append(jnp.where(allowed, closed, MASKED))
            lines.append(jnp.zeros((PAIR - chunks, FRAME), F32))
            mask_ref[key_frame * FRAME : (key_frame + 1) * FRAME, :] = jnp.concatenate(
                lines, axis=0
            ).T.astype(BF16)

    in_vmem = pl.BlockSpec(memory_space=pltpu.VMEM)
    in_smem = pl.BlockSpec(memory_space=pltpu.SMEM)
    projected = jax.ShapeDtypeStruct((total, features), BF16)
    return pl.pallas_call(
        kernel,
        out_shape=(
            jax.ShapeDtypeStruct((2, total, half), BF16),
            jax.ShapeDtypeStruct((total, PAIR), BF16),
            jax.ShapeDtypeStruct((3, 8, PAIR), F32),
            projected,
            projected,
            projected,
            jax.ShapeDtypeStruct((total, PAIR), BF16),
            jax.ShapeDtypeStruct((total, width), BF16),
            jax.ShapeDtypeStruct((total, PAIR), F32),
        ),
        in_specs=[in_vmem, in_vmem, in_smem, in_vmem, in_vmem, ANYWHERE] + [in_vmem] * 3,
        out_specs=(in_vmem,) * 9,
        scratch_shapes=[
            pltpu.VMEM((2, rows, half), BF16),
            pltpu.VMEM((n, 8, FRAME), F32),
            pltpu.VMEM((8, FRAME), F32),
            pltpu.VMEM(qkv.shape[1:], BF16),
            pltpu.VMEM((FRAME, width), BF16),
            pltpu.VMEM((FRAME, width), F32),
            pltpu.VMEM((rows, lanes, width), F32),
            pltpu.SemaphoreType.DMA,
        ]
        + Relay.scratch(n),
        compiler_params=pltpu.CompilerParams(
            collective_id=0, has_side_effects=True, vmem_limit_bytes=VMEM_BYTES
        ),
        name="gather_and_project",
    )(tokens, live, episode_frames, gain, shift, qkv, bias, fixed, ahead)


def widen(ref, target):
    half = ref.shape[2]
    target[:, :half] = ref[0].astype(F32)
    target[:, half:] = ref[1].astype(F32)


def halves_spec(shape, chunks, behind, span=FRAME):
    return pl.BlockSpec(
        (2, span, shape[2]), lambda s: (0, jnp.clip(s - behind, 0, chunks - 1), 0)
    )


def layer_forward(layer, query, key, value, key_bias, stream, mats, rows_of, next_refs, d_out, n, identity):
    total, features = query.shape
    split = stream.ndim == 3
    width = mats[1].shape[1]
    rows_here = total // n
    hidden_units = mats[1].shape[2]
    chunks = total // FRAME
    heads = features // HEAD_DIM
    slabs = features // PAIR
    columns = 256
    last = next_refs is None
    b_out, gain, shift, b_up, b_down = rows_of
    mat_out, mat_up, mat_down = mats

    def kernel(*refs):
        refs = list(refs)

        def take(count):
            taken = refs[:count]
            del refs[:count]
            return taken

        q_ref, k_ref, v_ref, kb_ref, x_ref = take(5)
        wo_any, wu_any, wd_any = take(3)
        bo_ref, gain_ref, shift_ref, bu_ref, bd_ref = take(5)
        if not last:
            wq_any, ngain, nshift, nbias, fixed, frames = take(6)
        if d_out is not None:
            (d_ref,) = take(1)
        p_ref, r_ref, mixed_ref, unit_ref, scale_ref, second_ref, act_ref, gp_ref, x_out = take(9)
        if not last:
            next_outs = take(6)
        if d_out is not None:
            (d_all,) = take(1)
        wo, wu, wd, mid, full, next_full, keys_wide, values_wide, asks = take(9)
        if not last:
            (wq,) = take(1)
        a_send, a_recv, b_send, b_recv, w_sem, send_sem, recv_sem = take(7)
        relay = None
        if d_out is not None:
            buffer, other, d_sem = take(3)
            relay = Relay(n, rows_here, buffer, other, take(Relay.sems))

        step = pl.program_id(0)
        me, core = lax.axis_index("seq"), lax.axis_index("tp")

        items = [(wo_any, wo), (wu_any, wu), (wd_any, wd)]
        if not last:
            items.append((wq_any, wq))

        def load(index):
            source, target = items[index]
            return pltpu.make_async_copy(
                source.at[layer if index < 3 else layer + 1], target, w_sem.at[index]
            )

        def exchange(kind, chunk):
            source, target = ((a_send, a_recv), (b_send, b_recv))[kind]
            return remote(
                source.at[chunk],
                target.at[chunk],
                send_sem.at[kind, chunk],
                recv_sem.at[kind, chunk],
                me,
                1 - core,
            )

        @pl.when(step == 0)
        def _():
            for index in range(len(items)):
                load(index).start()
            if relay is None:
                hello([(me, 1 - core)])
            else:
                relay.hello()
                split_lanes(d_ref, relay.x, buffer, other, me * rows_here, rows_here)
                relay.met()
                relay.begin()

        lane = lax.broadcasted_iota(jnp.int32, (1, PAIR), 1)
        sides = [(lane < HEAD_DIM).astype(F32).astype(BF16), (lane >= HEAD_DIM).astype(F32).astype(BF16)]
        @pl.when(step == 0)
        def _():
            for slab in range(slabs):
                lanes = slice(slab * PAIR, (slab + 1) * PAIR)
                keys_wide[slab, :, :PAIR] = k_ref[:, lanes]
                keys_wide[slab, :, PAIR:] = kb_ref[...]
                for side in range(2):
                    values_wide[2 * slab + side] = v_ref[:, lanes] * sides[side] + sides[1 - side]

        @pl.when(step < chunks)
        def _():
            asked = jnp.broadcast_to((lane == step).astype(F32), (FRAME, PAIR)).astype(BF16)
            for head in range(heads):
                lanes = slice(head // 2 * PAIR, (head // 2 + 1) * PAIR)
                asks[head, :, :PAIR] = q_ref[:, lanes] * sides[head % 2]
                asks[head, :, PAIR:] = asked

        for frame in range(chunks):

            @pl.when(step == frame)
            def _():
                keys = FRAME * (frame + 1)

                def score(head):
                    return nt(asks[head], keys_wide[head // 2, :keys, :])

                scores, sums = score(0), []
                for head in range(heads):
                    lanes, side = slice(head // 2 * PAIR, (head // 2 + 1) * PAIR), head % 2
                    following = score(head + 1) if head + 1 < heads else None
                    highest = jnp.max(scores, axis=1, keepdims=True)
                    shifted = jnp.exp(scores - highest).astype(BF16)
                    p_ref[0, head, :keys, :] = shifted.T
                    sums.append(nn(shifted, values_wide[head, :keys, :]))
                    scores = following
                    if side == 1:
                        one, two = sums[head - 1 :]
                        low_side = lane < HEAD_DIM
                        divisor = 1.0 / jnp.where(
                            low_side, pltpu.roll(one, HEAD_DIM, 1), pltpu.roll(two, HEAD_DIM, 1)
                        )
                        r_ref[:, lanes] = divisor
                        mixed_ref[:, lanes] = (jnp.where(low_side, one, two) * divisor).astype(BF16)

        @pl.when(step == 0)
        def _():
            load(0).wait()
            if relay is None:
                met([(me, 1 - core)])

        @pl.when(step < chunks)
        def _():
            a_send[step] = nn(mixed_ref[...], wo[...]).astype(BF16)
            exchange(0, step).start()

        if relay is not None:
            for event in range(relay.events):

                @pl.when(step == 2 + event // 2)
                def _():
                    relay.arrive(event)

                @pl.when(step == 3 + event // 2)
                def _():
                    relay.complete(event)

            @pl.when(step == chunks + 1)
            def _():
                for event in range(relay.events):
                    relay.ready(event)
                relay.finish()
                pltpu.make_async_copy(buffer, d_all, d_sem).start()

        def feed_forward():
            chunk = step - 1
            slot = lax.rem(chunk, 2)
            if split:
                widen(x_ref, mid.at[slot])
            arrived = a_send[chunk].astype(F32) + a_recv[chunk].astype(F32)
            middle = (mid[slot] if split else x_ref[...]) + arrived + bo_ref[layer : layer + 1, :]
            mid[slot] = middle
            unit, scale = normed(middle)
            keep_norm(unit, scale, unit_ref, scale_ref)
            second = (unit * gain_ref[layer : layer + 1, :] + shift_ref[layer : layer + 1, :]).astype(BF16)
            full[...] = second
            second_ref[...] = full[:, at((me // 2) * PAIR, PAIR)]
            parts = [slice(start, start + columns) for start in range(0, hidden_units, columns)]
            hidden = nn(second, wu[:, parts[0]])
            for index, part in enumerate(parts):
                following = nn(second, wu[:, parts[index + 1]]) if index + 1 < len(parts) else None
                act, slope = gelu_both(hidden + bu_ref[layer : layer + 1, part])
                act_ref[:, part] = act.astype(BF16)
                gp_ref[:, part] = slope.astype(BF16)
                hidden = following
            b_send[chunk] = nn(act_ref[...], wd[...]).astype(BF16)

        def close():
            chunk = step - 2
            result = mid[lax.rem(chunk, 2)] + (b_send[chunk].astype(F32) + b_recv[chunk].astype(F32))
            result = result + bd_ref[layer : layer + 1, :]
            x_out[...] = result
            if not last:
                project(
                    result,
                    chunk,
                    layer + 1,
                    me // 2,
                    (ngain, nshift, wq, nbias, fixed, frames),
                    next_outs,
                    next_full,
                )

        @pl.when(step == 1)
        def _():
            load(1).wait()
            load(2).wait()

        @pl.when((step >= 1) & (step <= chunks))
        def _():
            exchange(0, step - 1).wait_recv()
            feed_forward()
            exchange(1, step - 1).start()

        if not last:

            @pl.when(step == 2)
            def _():
                load(3).wait()

        @pl.when(step >= 2)
        def _():
            exchange(1, step - 2).wait_recv()
            close()

        @pl.when(step == chunks + 1)
        def _():
            for kind in range(2):
                for chunk in range(chunks):
                    exchange(kind, chunk).wait_send()
            if relay is not None:
                pltpu.make_async_copy(buffer, d_all, d_sem).wait()

    def rows(columns, behind):
        return pl.BlockSpec(
            (FRAME, columns), lambda s: (jnp.clip(s - behind, 0, chunks - 1), 0)
        )

    in_specs = [rows(features, 0), whole(key), whole(value), whole(key_bias)]
    in_specs += [halves_spec(stream.shape, chunks, 1) if split else rows(width, 1)]
    in_specs += [ANYWHERE] * 3 + [whole(item) for item in rows_of]
    operands = [query, key, value, key_bias, stream, *mats, *rows_of]
    if not last:
        in_specs += [ANYWHERE] + [whole(item) for item in next_refs[1:]]
        operands += list(next_refs)
    if d_out is not None:
        in_specs += [whole(d_out)]
        operands += [d_out]
    out_shape = [
        jax.ShapeDtypeStruct((chunks, heads, total, FRAME), BF16),
        jax.ShapeDtypeStruct((total, features), F32),
        jax.ShapeDtypeStruct((total, features), BF16),
        jax.ShapeDtypeStruct((total, width), BF16),
        jax.ShapeDtypeStruct((total, PAIR), F32),
        jax.ShapeDtypeStruct((total, PAIR), BF16),
        jax.ShapeDtypeStruct((total, hidden_units), BF16),
        jax.ShapeDtypeStruct((total, hidden_units), BF16),
        jax.ShapeDtypeStruct((total, width), F32),
    ]
    out_specs = [
        pl.BlockSpec((1, heads, total, FRAME), lambda s: (jnp.minimum(s, chunks - 1), 0, 0, 0)),
        rows(features, 0),
        rows(features, 0),
        rows(width, 1),
        rows(PAIR, 1),
        rows(PAIR, 1),
        rows(hidden_units, 1),
        rows(hidden_units, 1),
        rows(width, 2),
    ]
    scratch = [
        pltpu.VMEM(mat_out.shape[1:], BF16),
        pltpu.VMEM(mat_up.shape[1:], BF16),
        pltpu.VMEM(mat_down.shape[1:], BF16),
        pltpu.VMEM((2, FRAME, width), F32),
        pltpu.VMEM((FRAME, width), BF16),
        pltpu.VMEM((FRAME, width), BF16),
        pltpu.VMEM((slabs, total, 2 * PAIR), BF16),
        pltpu.VMEM((heads, total, PAIR), BF16),
        pltpu.VMEM((heads, FRAME, 2 * PAIR), BF16),
    ]
    if not last:
        out_shape += [jax.ShapeDtypeStruct((total, features), BF16)] * 3
        out_shape += [jax.ShapeDtypeStruct((total, PAIR), BF16)]
        out_shape += [jax.ShapeDtypeStruct((total, width), BF16)]
        out_shape += [jax.ShapeDtypeStruct((total, PAIR), F32)]
        out_specs += [rows(features, 2)] * 3 + [rows(PAIR, 2), rows(width, 2), rows(PAIR, 2)]
    if d_out is not None:
        out_shape += [jax.ShapeDtypeStruct((2, total, width // 2), BF16)]
        out_specs += [ANYWHERE]
        scratch += [pltpu.VMEM(next_refs[0].shape[1:], BF16)]
    scratch += [pltpu.VMEM((chunks, FRAME, width), BF16)] * 4
    scratch += [
        pltpu.SemaphoreType.DMA((4,)),
        pltpu.SemaphoreType.DMA((2, chunks)),
        pltpu.SemaphoreType.DMA((2, chunks)),
    ]
    if d_out is not None:
        scratch += [
            pltpu.VMEM((2, total, width // 2), BF16),
            pltpu.VMEM((2, rows_here, width // 2), BF16),
            pltpu.SemaphoreType.DMA,
        ]
        scratch += Relay.scratch(n)
    return pl.pallas_call(
        kernel,
        grid=(chunks + 2,),
        out_shape=out_shape,
        in_specs=in_specs,
        out_specs=out_specs,
        scratch_shapes=scratch,
        compiler_params=pltpu.CompilerParams(
            collective_id=identity, has_side_effects=True, vmem_limit_bytes=VMEM_BYTES
        ),
        name=f"layer_forward_{layer}",
    )(*operands)


class Swap:
    def __init__(self, ships, lane_rows):
        self.ships, self.lane_rows = ships, lane_rows
        self.count = len(ships) + len(lane_rows)

    def operands(self):
        return [*self.ships, *[item for item, _ in self.lane_rows]]

    def in_specs(self):
        return [whole(item) for item in self.ships] + [ANYWHERE] * len(self.lane_rows)

    def outputs(self):
        shapes, specs = [], []
        for item in self.ships:
            shape = (item.shape[0] // 2, item.shape[1])
            shapes.append(jax.ShapeDtypeStruct(shape, F32))
            specs.append(whole_out(shape))
        for item, count in self.lane_rows:
            shapes.append(jax.ShapeDtypeStruct((count or item.shape[0], item.shape[1]), item.dtype))
            specs.append(ANYWHERE)
        return shapes, specs

    def scratch(self):
        if not self.count:
            return []
        buffers = [pltpu.VMEM((item.shape[0] // 2, item.shape[1]), BF16) for item in self.ships]
        return buffers * 2 + [pltpu.SemaphoreType.DMA((self.count,))] * 2

    def bind(self, sources, targets, scratch):
        ships = len(self.ships)
        me, core = lax.axis_index("seq"), lax.axis_index("tp")
        x = lax.rem(me, 2)
        beside = me + 1 - 2 * x
        half = PAIR // 2

        def copy(index):
            if index < ships:
                source, target = scratch[index], scratch[ships + index]
            else:
                source, target = sources[index], targets[index]
                count = self.lane_rows[index - ships][1]
                if count:
                    source = source.at[at(beside * count, count), :]
            send, recv = scratch[2 * ships].at[index], scratch[2 * ships + 1].at[index]
            return remote(source, target, send, recv, beside, core)

        def start():
            for index in range(self.count):
                if index < ships:
                    scratch[index][...] = sources[index][at((1 - x) * half, half), :].astype(BF16)
                copy(index).start()

        def finish():
            for index in range(self.count):
                copy(index).wait_recv()
                if index < ships:
                    own = sources[index][at(x * half, half), :]
                    targets[index][...] = own + scratch[ships + index][...].astype(F32)
            for index in range(self.count):
                copy(index).wait_send()

        return start, finish


def attention_backward(
    probs, divisor, mixed, query, key, value, grad_mixed, first, fixed, frames, swap, swap_qkv, identity
):
    total, features = query.shape
    chunks = total // FRAME
    slabs = features // PAIR
    half = PAIR // 2

    def kernel(*refs):
        refs = list(refs)

        def take(count):
            taken = refs[:count]
            del refs[:count]
            return taken

        p_ref, r_ref, o_ref, q_ref, k_ref, v_ref, g_ref, first_ref, fixed_ref, frames_ref = take(10)
        sources = take(swap.count)
        dq_ref, dk_ref, dv_ref, qkv_out = take(4)
        targets = take(swap.count)
        dk_sum, dv_sum, first_turned, values, ends, asks, gives, scored, mixing = take(9)
        if swap_qkv:
            qkv_own, qkv_send, qkv_recv, qkv_sems = take(4)
        start, finish = swap.bind(sources, targets, refs)

        step = pl.program_id(0)
        me, core = lax.axis_index("seq"), lax.axis_index("tp")
        x = lax.rem(me, 2)
        beside = me + 1 - 2 * x

        def qkv_copy(slab):
            return remote(
                qkv_send.at[slab],
                qkv_recv.at[slab],
                qkv_sems.at[0, slab],
                qkv_sems.at[1, slab],
                beside,
                core,
            )

        @pl.when(step == 0)
        def _():
            hello([(beside, core)])
            first_turned[...] = first_ref[...].T
            met([(beside, core)])
            start()

        lane = lax.broadcasted_iota(jnp.int32, (1, PAIR), 1)
        sides = [(lane < HEAD_DIM).astype(F32).astype(BF16), (lane >= HEAD_DIM).astype(F32).astype(BF16)]
        turned = k_ref[...].T
        values[:, :PAIR] = v_ref[...]
        values[:, PAIR:] = jnp.broadcast_to((lane < 2).astype(F32), (total, PAIR)).astype(BF16)

        def give(frame):
            keys = FRAME * (frame + 1)
            own = slice(frame * FRAME, keys)
            scaled = (g_ref[own, :].astype(F32) * r_ref[own, :]).astype(BF16)
            inner = scaled.astype(F32) * o_ref[own, :].astype(F32)
            grads = []
            for side in range(2):
                delta = jnp.sum(
                    jnp.where((lane < HEAD_DIM) == (side == 0), inner, 0.0), axis=1, keepdims=True
                )
                coarse = delta.astype(BF16).astype(F32)
                rest = jnp.where(lane == 0, -coarse, jnp.where(lane == 1, coarse - delta, 0.0))
                g2 = scaled * sides[side]
                part = slice(side * FRAME, (side + 1) * FRAME)
                ends[frame, side, :, :PAIR] = g2
                ends[frame, side, :, PAIR:] = rest.astype(BF16)
                asks[frame, part, :] = q_ref[own, :] * sides[side]
                gives[frame, part, :] = g2
                grads.append(nt(values[:keys, :], ends[frame, side]))
            return grads

        given = give(chunks - 1)
        for frame in reversed(range(chunks)):
            keys = FRAME * (frame + 1)
            own = slice(frame * FRAME, keys)
            tables = tables_of(fixed_ref, frames_ref, frame)
            grads = given
            given = give(frame - 1) if frame else None
            query_parts = []
            slot = frame % 2
            for side in range(2):
                part = slice(side * FRAME, (side + 1) * FRAME)
                attention = p_ref[frame, side, :keys, :]
                grad_scores = (attention.astype(F32) * grads[side]).astype(BF16)
                scored[slot, :keys, part] = grad_scores
                mixing[slot, :keys, part] = attention
                query_parts.append(nn(turned[side * HEAD_DIM : (side + 1) * HEAD_DIM, :keys], grad_scores))
            grad_query = jnp.concatenate(query_parts, axis=0).T
            key_parts = nn(scored[slot, :keys, :], asks[frame])
            value_parts = nn(mixing[slot, :keys, :], gives[frame])
            dq_ref[own, :] = (turn(grad_query, tables, True) * SCORE_SCALE).astype(BF16)
            if frame == chunks - 1:
                dk_sum[...] = key_parts
                dv_sum[...] = value_parts
            else:
                dk_sum[:keys, :] += key_parts
                dv_sum[:keys, :] += value_parts
            dk_ref[own, :] = turn(dk_sum[own, :], tables, True).astype(BF16)
            dv_ref[own, :] = dv_sum[own, :].astype(BF16)

        for part, ref in enumerate((dq_ref, dk_ref, dv_ref)):
            piece = slice(part * PAIR, (part + 1) * PAIR)
            terms = nn(first_turned[...], ref[...])
            if swap_qkv:
                qkv_own[step, :, piece] = terms
                qkv_send[step, :, piece] = qkv_own[step, at((1 - x) * half, half), piece].astype(BF16)
            else:
                qkv_out[:, at(part * features + step * PAIR, PAIR)] = terms
        if swap_qkv:
            qkv_copy(step).start()

        @pl.when(step == slabs - 1)
        def _():
            finish()
            for slab in range(slabs if swap_qkv else 0):
                qkv_copy(slab).wait_recv()
                for part in range(3):
                    piece = slice(part * PAIR, (part + 1) * PAIR)
                    place = part * features + slab * PAIR
                    qkv_out[:, place : place + PAIR] = qkv_own[
                        slab, at(x * half, half), piece
                    ] + qkv_recv[slab, :, piece].astype(F32)
            for slab in range(slabs if swap_qkv else 0):
                qkv_copy(slab).wait_send()

    slab = pl.BlockSpec((total, PAIR), lambda s: (0, s))
    in_specs = [pl.BlockSpec((chunks, 2, total, FRAME), lambda s: (0, s, 0, 0))]
    in_specs += [slab] * 6 + [whole(first), whole(fixed), whole(frames)]
    in_specs += swap.in_specs()
    qkv_shape = (half if swap_qkv else PAIR, 3 * features)
    shapes, specs = swap.outputs()
    out_shape = [jax.ShapeDtypeStruct((total, features), BF16)] * 3
    out_shape += [jax.ShapeDtypeStruct(qkv_shape, F32)] + shapes
    out_specs = [slab] * 3 + [whole_out(qkv_shape)] + specs
    scratch = [pltpu.VMEM((total, PAIR), F32)] * 2 + [pltpu.VMEM((PAIR, total), BF16)]
    scratch += [pltpu.VMEM((total, 2 * PAIR), BF16), pltpu.VMEM((chunks, 2, FRAME, 2 * PAIR), BF16)]
    scratch += [pltpu.VMEM((chunks, 2 * FRAME, PAIR), BF16)] * 2
    scratch += [pltpu.VMEM((2, total, 2 * FRAME), BF16)] * 2
    if swap_qkv:
        scratch += [pltpu.VMEM((slabs, PAIR, 3 * PAIR), F32)]
        scratch += [pltpu.VMEM((slabs, half, 3 * PAIR), BF16)] * 2
        scratch += [pltpu.SemaphoreType.DMA((2, slabs))]
    scratch += swap.scratch()
    return pl.pallas_call(
        kernel,
        grid=(slabs,),
        out_shape=out_shape,
        in_specs=in_specs,
        out_specs=out_specs,
        scratch_shapes=scratch,
        compiler_params=pltpu.CompilerParams(
            collective_id=identity, has_side_effects=True, vmem_limit_bytes=VMEM_BYTES
        ),
        name=f"attention_backward_{identity}",
    )(
        probs,
        divisor,
        mixed,
        query,
        key,
        value,
        grad_mixed,
        first,
        fixed,
        frames,
        *swap.operands(),
    )


def rows_backward(entry, upper, identity, span, swap):
    top, bottom = len(entry) == 1, upper is None
    if not top:
        above, entry = entry[0], entry[1:]
    total = entry[0].shape[1] if top else entry[0].shape[0]
    chunks = total // span
    columns = 256
    ahead = 0 if top else 2 if bottom else 1
    if top:
        width = 2 * entry[0].shape[2]
    else:
        features, width = entry[0].shape[1], entry[5].shape[1]
    if not bottom:
        layer = upper[0]
        hidden_units, mixed_features = upper[1].shape[1], upper[6].shape[1]
    place_rows = total // lax.axis_size("seq")

    def kernel(*refs):
        refs = list(refs)

        def take(count):
            taken = refs[:count]
            del refs[:count]
            return taken

        if top:
            (d_out_ref,) = take(1)
        else:
            dq_ref, dk_ref, dv_ref, unit1, scale1, dm_ref, wq, gain1 = take(8)
        if not bottom:
            act_ref, gp_ref, unit2, scale2, second_ref, mixed_ref = take(6)
            wo_any, wu_any, wd_any, gain2 = take(4)
        sources = take(swap.count)
        if not top:
            (vec1,) = take(1)
        if not bottom:
            dmid_out, dmix_out, out_sum, up_sum, down_sum, vec2 = take(6)
        else:
            dx_out, dx_other, vec_other = take(3)
        targets = take(swap.count)
        if not top:
            a_send, a_recv = take(2)
        if not bottom:
            b_send, b_recv, grad_keep, hidden_keep, low_keep, last_keep, wo, wu, wd, w_sem = take(10)
        else:
            dx_keep, dx_send, dx_recv, vec_recv, x_send_sem, x_recv_sem = take(6)
        send_sem, recv_sem = take(2)
        start_swap, finish_swap = swap.bind(sources, targets, refs)

        step = pl.program_id(0)
        me, core = lax.axis_index("seq"), lax.axis_index("tp")
        pair = at((me // 2) * PAIR, PAIR)
        x = lax.rem(me, 2)
        beside = me + 1 - 2 * x

        def exchange(kind, chunk):
            source, target = (a_send, a_recv) if kind == 0 else (b_send, b_recv)
            return remote(
                source.at[chunk],
                target.at[chunk],
                send_sem.at[kind, chunk],
                recv_sem.at[kind, chunk],
                me,
                1 - core,
            )

        def load(index):
            source, target = ((wd_any, wd), (wu_any, wu), (wo_any, wo))[index]
            return pltpu.make_async_copy(source.at[layer], target, w_sem.at[index])

        partners = [(me, 1 - core)] + ([(beside, core)] if bottom or swap.count else [])

        @pl.when(step == 0)
        def _():
            if not bottom:
                for index in range(3):
                    load(index).start()
                out_sum[...] = jnp.zeros_like(out_sum)
                up_sum[...] = jnp.zeros_like(up_sum)
                down_sum[...] = jnp.zeros_like(down_sum)
                vec2[...] = jnp.zeros_like(vec2)
            if not top:
                vec1[...] = jnp.zeros_like(vec1)
            hello(partners)

        def meet():
            @pl.when(step == 0)
            def _():
                met(partners)
                start_swap()

        def entry_products():
            partial = None
            for part, ref in enumerate((dq_ref, dk_ref, dv_ref)):
                grad = ref[...]
                term = nt(grad, wq[0, part])
                partial = term if partial is None else partial + term
                vec1[part : part + 1, :] += column_sum(grad.astype(F32))
            a_send[step] = partial.astype(BF16)

        def entry_norm(chunk):
            if top:
                widen(d_out_ref, grad_keep.at[lax.rem(chunk, 2)])
                return grad_keep[lax.rem(chunk, 2)]
            grad_first = a_send[chunk].astype(F32) + a_recv[chunk].astype(F32)
            unit, scale = kept_norm(unit1, scale1)
            for start, sums in ((3, column_sum(grad_first * unit)), (5, column_sum(grad_first))):
                for side in range(width // features):
                    piece = slice(side * features, (side + 1) * features)
                    vec1[start + side : start + side + 1, :] += sums[:, piece]
            return dm_ref[...] + norm_pull(grad_first, gain1[above : above + 1, :], unit, scale)

        def feed_forward(between=None):
            chunk = step - ahead
            gradient = entry_norm(chunk)
            if bottom:
                dx_keep[at(chunk * span, span), :] = gradient
                return
            grad_keep[lax.rem(chunk, 2)] = gradient
            vec2[1:2, :width] += column_sum(gradient)
            low = gradient.astype(BF16)
            low_keep[...] = low
            low_columns = low_keep[:, pair]
            second = second_ref[...]
            parts = [slice(start, start + columns) for start in range(0, hidden_units, columns)]
            grad_act = nt(low, wd[parts[0], :])
            for index, part in enumerate(parts):
                following = nt(low, wd[parts[index + 1], :]) if index + 1 < len(parts) else None
                grad_hidden = grad_act * gp_ref[:, part].astype(F32)
                hidden_keep[:, part] = grad_hidden.astype(BF16)
                vec2[0:1, part] += column_sum(grad_hidden)
                grad_act = following
            if between is not None:
                between()
            b_send[chunk] = nt(hidden_keep[...], wu[...]).astype(BF16)
            down_sum[...] += tn(low_columns, act_ref[...])
            up_sum[...] += tn(second, hidden_keep[...])

        def close():
            chunk = step - ahead - 1
            grad_second = b_send[chunk].astype(F32) + b_recv[chunk].astype(F32)
            unit, scale = kept_norm(unit2, scale2)
            vec2[2:3, :width] += column_sum(grad_second * unit)
            vec2[3:4, :width] += column_sum(grad_second)
            grad_middle = grad_keep[lax.rem(chunk, 2)] + norm_pull(
                grad_second, gain2[layer : layer + 1, :], unit, scale
            )
            dmid_out[...] = grad_middle
            vec2[4:5, :width] += column_sum(grad_middle)
            low = grad_middle.astype(BF16)
            last_keep[...] = low
            out_sum[...] += tn(last_keep[:, pair], mixed_ref[...])
            dmix_out[...] = nt(low, wo[...]).astype(BF16)

        if not top:

            @pl.when(step < chunks)
            def _():
                entry_products()
                meet()
                exchange(0, step).start()

        @pl.when((step >= ahead) & (step < chunks + ahead))
        def _():
            if not top:
                exchange(0, step - ahead).wait_recv()
            if not bottom:

                @pl.when(step == ahead)
                def _():
                    load(0).wait()

            feed_forward(lambda: pl.when(step == ahead)(lambda: load(1).wait()))
            if not bottom:
                if top:
                    meet()
                exchange(1, step - ahead).start()

        if not bottom:

            @pl.when(step == ahead + 1)
            def _():
                load(2).wait()

            @pl.when(step >= ahead + 1)
            def _():
                exchange(1, step - ahead - 1).wait_recv()
                close()

        if bottom:

            def x_copy(index):
                source, target = ((dx_send, dx_recv), (vec1, vec_recv))[index]
                return remote(
                    source, target, x_send_sem.at[index], x_recv_sem.at[index], beside, core
                )

            @pl.when(step == chunks + 1)
            def _():
                dx_send[...] = dx_keep[at(beside * place_rows, place_rows), :].astype(BF16)
                x_copy(0).start()
                x_copy(1).start()
                dx_out[...] = dx_keep[at(me * place_rows, place_rows), :]
                x_copy(0).wait_recv()
                x_copy(1).wait_recv()
                dx_other[...] = dx_recv[...].astype(F32)
                vec_other[...] = vec_recv[...]
                x_copy(0).wait_send()
                x_copy(1).wait_send()

        @pl.when(step == pl.num_programs(0) - 1)
        def _():
            for kind in ([] if top else [0]) + ([] if bottom else [1]):
                for chunk in range(chunks):
                    exchange(kind, chunk).wait_send()
            finish_swap()

    def rows(columns, behind):
        return pl.BlockSpec(
            (span, columns), lambda s: (jnp.clip(s - behind, 0, chunks - 1), 0)
        )

    vec = jax.ShapeDtypeStruct((8, VEC), F32)
    operands, in_specs, out_shape, out_specs, scratch = [], [], [], [], []
    if top:
        operands += list(entry)
        in_specs += [halves_spec(entry[0].shape, chunks, 0, span)]
    else:
        operands += list(entry)
        in_specs += [rows(features, 0)] * 3
        in_specs += [rows(width, ahead), rows(PAIR, ahead), rows(width, ahead)]
        in_specs += [
            pl.BlockSpec(
                (1, *entry[6].shape[1:]),
                lambda s: (above, 0, 0, 0),
                pipeline_mode=pl.Buffered(1),
            ),
            whole(entry[7]),
        ]
        narrow = jax.ShapeDtypeStruct((8, features), F32)
        out_shape += [narrow]
        out_specs += [whole_out((8, features))]
        scratch += [pltpu.VMEM((chunks, span, width), BF16)] * 2
    if not bottom:
        operands += list(upper[1:])
        in_specs += [rows(hidden_units, ahead)] * 2
        in_specs += [rows(width, ahead + 1), rows(PAIR, ahead + 1), rows(PAIR, ahead)]
        in_specs += [rows(mixed_features, ahead + 1)] + [ANYWHERE] * 3 + [whole(upper[10])]
        sums = [mixed_features, hidden_units, hidden_units]
        out_shape += [
            jax.ShapeDtypeStruct((total, width), F32),
            jax.ShapeDtypeStruct((total, mixed_features), BF16),
        ]
        out_shape += [jax.ShapeDtypeStruct((PAIR, size), F32) for size in sums] + [vec]
        out_specs += [rows(width, ahead + 1), rows(mixed_features, ahead + 1)]
        out_specs += [whole_out((PAIR, size)) for size in sums] + [whole_out((8, VEC))]
        scratch += [pltpu.VMEM((chunks, span, width), BF16)] * 2
        scratch += [
            pltpu.VMEM((2, span, width), F32),
            pltpu.VMEM((span, hidden_units), BF16),
            pltpu.VMEM((span, width), BF16),
            pltpu.VMEM((span, width), BF16),
            pltpu.VMEM(upper[7].shape[1:], BF16),
            pltpu.VMEM(upper[8].shape[1:], BF16),
            pltpu.VMEM(upper[9].shape[1:], BF16),
            pltpu.SemaphoreType.DMA((3,)),
        ]
    else:
        out_shape += [
            jax.ShapeDtypeStruct((place_rows, width), F32),
            jax.ShapeDtypeStruct((place_rows, width), F32),
            narrow,
        ]
        out_specs += [whole_out((place_rows, width))] * 2 + [whole_out((8, features))]
        scratch += [
            pltpu.VMEM((total, width), F32),
            pltpu.VMEM((place_rows, width), BF16),
            pltpu.VMEM((place_rows, width), BF16),
            pltpu.VMEM((8, features), F32),
            pltpu.SemaphoreType.DMA((2,)),
            pltpu.SemaphoreType.DMA((2,)),
        ]
    scratch += [pltpu.SemaphoreType.DMA((2, chunks))] * 2
    operands += swap.operands()
    in_specs += swap.in_specs()
    shapes, specs = swap.outputs()
    out_shape += shapes
    out_specs += specs
    scratch += swap.scratch()
    return pl.pallas_call(
        kernel,
        grid=(chunks + (1 if top else 2),),
        out_shape=out_shape,
        in_specs=in_specs,
        out_specs=out_specs,
        scratch_shapes=scratch,
        compiler_params=pltpu.CompilerParams(
            collective_id=identity, has_side_effects=True, vmem_limit_bytes=VMEM_BYTES
        ),
        name=f"rows_backward_{identity}",
    )(*operands)


def assemble(sums, vecs, lanes, n, features, hidden_units):
    place = lanes[1].shape[0]
    width = lanes[1].shape[1]
    half = PAIR // 2

    def kernel(*refs):
        refs = list(refs)

        def take(count):
            taken = refs[:count]
            del refs[:count]
            return taken

        qkvs, outs, ups, downs = take(LAYERS), take(LAYERS), take(LAYERS), take(LAYERS)
        vec_refs = [take(4) for _ in range(LAYERS)]
        out_lane, out_other, dx_own, dx_other = take(4)
        out_ref, dx_ref, gain1, shift1, g_qkv, b_qkv, g_out, b_out = take(8)
        gain2, shift2, g_up, b_up, g_down, b_down = take(6)
        out_own, sem = refs
        me = lax.axis_index("seq")
        x = lax.rem(me, 2)
        fetch = pltpu.make_async_copy(out_lane.at[at(me * place, place), :], out_own, sem)
        fetch.start()

        for layer in range(LAYERS):
            for part in range(3):
                g_qkv[layer, part] = qkvs[layer][:, part * features : (part + 1) * features]
            for ref, target in ((outs, g_out), (ups, g_up), (downs, g_down)):
                target[layer] = ref[layer][...]

        for layer, (entry_own, entry_other, upper_own, upper_other) in enumerate(vec_refs):
            line = slice(layer, layer + 1)
            for part in range(3):
                row = slice(part, part + 1)
                b_qkv[part, line, :] = entry_own[row, :] + entry_other[row, :]
            b_up[line, :] = upper_own[0:1, :hidden_units] + upper_other[0:1, :hidden_units]

            def owned(mine, other, row):
                wide = mine.shape[1]
                place = (me // 2) * PAIR
                pair = at(lax.rem(place, wide), PAIR)
                both = mine[row : row + 1, pair] + other[row : row + 1, pair]
                for later in range(1, width // wide):
                    line = slice(row + later, row + later + 1)
                    both = jnp.where(place // wide == later, mine[line, pair] + other[line, pair], both)
                return jnp.where(x == 0, both[:, :half], both[:, half:])

            gain1[line, :] = owned(entry_own, entry_other, 3)
            shift1[line, :] = owned(entry_own, entry_other, 5)
            b_down[line, :] = owned(upper_own, upper_other, 1)
            gain2[line, :] = owned(upper_own, upper_other, 2)
            shift2[line, :] = owned(upper_own, upper_other, 3)
            b_out[line, :] = owned(upper_own, upper_other, 4)

        def both_lanes(target, mine, other):
            target[:, 0, :] = jnp.where(x == 0, mine, other)
            target[:, 1, :] = jnp.where(x == 0, other, mine)

        both_lanes(dx_ref, dx_own[...], dx_other[...])
        fetch.wait()
        both_lanes(out_ref, out_own[...], out_other[...])

    def f32(*shape):
        return jax.ShapeDtypeStruct(shape, F32)

    in_vmem = pl.BlockSpec(memory_space=pltpu.VMEM)
    flat = []
    for kind in range(4):
        flat += [sums[layer][kind] for layer in range(LAYERS)]
    for layer in range(LAYERS):
        flat += list(vecs[layer])
    flat += list(lanes)
    small = f32(LAYERS, width // n)
    return pl.pallas_call(
        kernel,
        out_shape=(
            f32(place, 2, width),
            f32(place, 2, width),
            small,
            small,
            f32(LAYERS, 3, half, features),
            f32(3, LAYERS, features),
            f32(LAYERS, half, features),
            small,
            small,
            small,
            f32(LAYERS, half, hidden_units),
            f32(LAYERS, hidden_units),
            f32(LAYERS, half, hidden_units),
            small,
        ),
        in_specs=[in_vmem] * (len(flat) - 4) + [ANYWHERE] + [in_vmem] * 3,
        out_specs=(in_vmem,) * 14,
        scratch_shapes=[pltpu.VMEM((place, width), F32), pltpu.SemaphoreType.DMA],
        compiler_params=pltpu.CompilerParams(vmem_limit_bytes=VMEM_BYTES),
        name="assemble",
    )(*flat)


def per_chip(
    tokens,
    d_out,
    norm1_gain,
    norm1_shift,
    w_qkv,
    b_qkv,
    w_out,
    b_out,
    norm2_gain,
    norm2_shift,
    w_up,
    b_up,
    w_down,
    b_down,
    episode_frames,
    live,
):
    n = lax.axis_size("seq")
    rows = tokens.shape[0]
    features = w_qkv.shape[3]
    fixed, ahead = turn_constants(rows * n // FRAME)
    qkv, qkv_bias = w_qkv.transpose(0, 2, 1, 3), b_qkv.transpose(1, 0, 2)

    gathered, key_bias, frames, *projected = gather_and_project(
        tokens, live.T, episode_frames, norm1_gain, norm1_shift, qkv, qkv_bias, fixed, ahead, n
    )
    streams, kept, d_lane = [gathered], [], None
    for layer in range(LAYERS):
        following = None
        if layer + 1 < LAYERS:
            following = (qkv, norm1_gain, norm1_shift, qkv_bias, fixed, frames)
        results = layer_forward(
            layer,
            *projected[:3],
            key_bias,
            streams[layer],
            (w_out, w_up, w_down),
            (b_out, norm2_gain, norm2_shift, b_up, b_down),
            following,
            d_out if layer == 0 else None,
            n,
            1 + layer,
        )
        kept.append((*projected, *results[:8]))
        streams.append(results[8])
        if following is not None:
            projected = results[9:15]
        if layer == 0:
            d_lane = results[-1]

    sums = [[None] * 4 for _ in range(LAYERS)]
    vecs = [[None] * 4 for _ in range(LAYERS)]
    entry, later = (d_lane,), None
    for layer in reversed(range(LAYERS)):
        query, key, value, first, unit1, scale1, probs, divisor, mixed = kept[layer][:9]
        unit2, scale2, second, act, slope = kept[layer][9:]
        upper = (
            layer,
            act,
            slope,
            unit2,
            scale2,
            second,
            mixed,
            w_out,
            w_up,
            w_down,
            norm2_gain,
        )
        identity = 1 + LAYERS + 2 * (LAYERS - 1 - layer)
        if later is None:
            results = rows_backward(entry, upper, identity, FRAME, Swap([], []))
        else:
            swap = Swap(later[:2], [(later[2], 0), (streams[LAYERS], rows)])
            vec1, *results = rows_backward(entry, upper, identity, FRAME, swap)
            results, swapped = results[:6], results[6:]
            sums[layer + 1][3], sums[layer + 1][0] = swapped[:2]
            vecs[layer + 1][3], out_other = swapped[2:]
            vecs[layer + 1][0] = vec1
        grad_middle, grad_mixed, out_sum, up_sum, down_sum, vec2 = results
        vecs[layer][2] = vec2
        last = layer == 0
        if last:
            swap = Swap([out_sum, up_sum], [(vec2, 0), (vecs[layer + 1][0], 0)])
        else:
            swap = Swap([out_sum, up_sum], [])
        results = attention_backward(
            probs,
            divisor,
            mixed,
            query,
            key,
            value,
            grad_mixed,
            first,
            fixed,
            frames,
            swap,
            last,
            identity + 1,
        )
        grad_query, grad_key, grad_value, qkv_sum = results[:4]
        if last:
            sums[layer][:3] = [qkv_sum, *results[4:6]]
            vecs[layer][3], vecs[layer + 1][1] = results[6:8]
        else:
            sums[layer][1:3] = results[4:6]
            later = [down_sum, qkv_sum, vec2]
        entry = (
            layer,
            grad_query,
            grad_key,
            grad_value,
            unit1,
            scale1,
            grad_middle,
            qkv,
            norm1_gain,
        )
    vec1, dx_own, dx_other, vec_other, sums[0][3] = rows_backward(
        entry, None, 1 + 3 * LAYERS, FRAME, Swap([down_sum], [])
    )
    vecs[0][:2] = [vec1, vec_other]
    results = list(
        assemble(
            sums,
            vecs,
            (streams[LAYERS], out_other, dx_own, dx_other),
            n,
            features,
            w_up.shape[2],
        )
    )
    results[4] = results[4].transpose(0, 2, 1, 3)
    results[5] = results[5].transpose(1, 0, 2)
    results[6] = results[6].transpose(0, 2, 1)
    results[12] = results[12].transpose(0, 2, 1)
    return tuple(results)


def lane_fits(mesh, tokens):
    n = mesh.shape["seq"]
    positions, lanes, width = tokens.shape
    rows = positions // n
    return (
        lanes == 2
        and n % 4 == 0
        and positions <= 4 * FRAME
        and positions % FRAME == 0
        and FRAME % rows == 0
        and width // n * 2 == PAIR
        and mesh.shape["tp"] == 2
    )


def solution(mesh):
    placed = (
        P("seq", None, None),
        P("seq", None, None),
        P(),
        P(),
        P(None, None, None, "tp"),
        P(None, None, "tp"),
        P(None, "tp", None),
        P(),
        P(),
        P(),
        P(None, None, "tp"),
        P(None, "tp"),
        P(None, "tp", None),
        P(),
        P(),
        P("seq", None),
    )
    def mapped(body):
        return jax.shard_map(
            body,
            mesh=mesh,
            in_specs=placed,
            out_specs=(
                P("seq", None, None),
                P("seq", None, None),
                P(None, "seq"),
                P(None, "seq"),
                P(None, "seq", None, "tp"),
                P(None, None, "tp"),
                P(None, "tp", "seq"),
                P(None, "seq"),
                P(None, "seq"),
                P(None, "seq"),
                P(None, "seq", "tp"),
                P(None, "tp"),
                P(None, "tp", "seq"),
                P(None, "seq"),
            ),
            check_vma=False,
        )

    def run(tokens, *others):
        if lane_fits(mesh, tokens):
            return mapped(per_chip)(tokens, *others)
        return mapped(per_device)(tokens, *others)

    return run
```

```python
import math

import jax
import jax.numpy as jnp
import numpy as np
from jax import lax
from jax.experimental import pallas as pl
from jax.experimental.pallas import tpu as pltpu
from jax.sharding import PartitionSpec as P

HEAD_DIM = 64
GRID = 16
FRAME = 256
LAYERS = 2
MICRO = 2


EPSILON = 1e-06
MASKED = -1e30
SCORE_SCALE = 0.125


def layer_norm(stream, norm_gain, norm_shift):
    center = stream - jnp.mean(stream, axis=-1, keepdims=True)
    spread = jnp.mean(center * center, axis=-1, keepdims=True)
    return center * lax.rsqrt(spread + EPSILON) * norm_gain + norm_shift


def rotate(values, frame_place, row_place, column_place):
    frequency = jnp.exp(jnp.arange(10, dtype=jnp.float32) * (-math.log(10000.0) / 10.0))
    pieces = []
    for section, place in enumerate((frame_place, row_place, column_place)):
        lower = values[..., 20 * section : 20 * section + 10]
        upper = values[..., 20 * section + 10 : 20 * section + 20]
        angles = place.astype(jnp.float32)[..., None, None] * frequency
        cosine = jnp.cos(angles)
        sine_part = jnp.sin(angles)
        pieces.append(lower * cosine - upper * sine_part)
        pieces.append(lower * sine_part + upper * cosine)
    pieces.append(values[..., 60:])
    return jnp.concatenate(pieces, axis=-1)


def episode_tags(frame_counts, positions):
    endings = jnp.cumsum(frame_counts) * FRAME
    passed = (positions[:, None] >= endings[None, :]).astype(jnp.int32)
    episode = jnp.sum(passed, axis=1)
    opening = jnp.sum(passed * frame_counts[None, :], axis=1)
    frame_index = positions // FRAME - opening
    within = positions % FRAME
    return (episode, frame_index, within // GRID, within % GRID)


def gelu_exact(values):
    return jax.nn.gelu(values, approximate=False)


def sum_heads(partial_sum):
    return lax.psum(partial_sum.astype(jnp.bfloat16), "tp").astype(jnp.float32)


def sum_inputs(partial_sum):
    return lax.psum(partial_sum.astype(jnp.bfloat16), "tp").astype(jnp.float32)


def lane_scores(query, keys_all, lane_index, query_tags, key_tags):
    head_count = query.shape[2] // HEAD_DIM
    query_lane = lax.dynamic_index_in_dim(query, lane_index, 1, False).reshape(
        query.shape[0], head_count, HEAD_DIM
    )
    keys_lane = lax.dynamic_index_in_dim(keys_all, lane_index, 1, False).reshape(
        keys_all.shape[0], head_count, HEAD_DIM
    )
    query_episode, query_frame = [
        lax.dynamic_index_in_dim(item, lane_index, 1, False) for item in query_tags
    ]
    key_episode, key_frame, key_live = [
        lax.dynamic_index_in_dim(item, lane_index, 1, False) for item in key_tags
    ]
    allowed = (
        (query_episode[:, None] == key_episode[None, :])
        & (key_frame[None, :] <= query_frame[:, None])
        & (key_live[None, :] > 0)
    )
    scores = (
        jnp.einsum("qhd,khd->hqk", query_lane, keys_lane, preferred_element_type=jnp.float32)
        * SCORE_SCALE
    )
    return (jnp.where(allowed[None], scores, MASKED), query_lane, keys_lane)


def attend_forward(query, keys_all, values_all, query_tags, key_tags):
    rows_dev, lane_count, features = query.shape
    head_count = features // HEAD_DIM

    def one_lane(lane_index, carry):
        scores, query_lane, keys_lane = lane_scores(
            query, keys_all, lane_index, query_tags, key_tags
        )
        highest = jnp.max(scores, axis=-1, keepdims=True)
        shifted = jnp.exp(scores - highest)
        summed = jnp.sum(shifted, axis=-1, keepdims=True)
        attention = (shifted / summed).astype(jnp.bfloat16)
        values_lane = lax.dynamic_index_in_dim(values_all, lane_index, 1, False).reshape(
            values_all.shape[0], head_count, HEAD_DIM
        )
        result = jnp.einsum(
            "hqk,khd->qhd", attention, values_lane, preferred_element_type=jnp.float32
        ).reshape(rows_dev, 1, features)
        log_total = (highest + jnp.log(summed))[None, :, :, 0]
        return (result, log_total)

    initial = (
        jnp.zeros((rows_dev, lane_count, features), jnp.float32),
        jnp.zeros((lane_count, head_count, rows_dev), jnp.float32),
    )
    return lax.fori_loop(0, lane_count, one_lane, initial)


def attend_backward(query, keys_all, values_all, log_total, grad_mixed, query_tags, key_tags):
    rows_dev, lane_count, features = query.shape
    head_count = features // HEAD_DIM
    key_rows = keys_all.shape[0]

    def one_lane(lane_index, carry):
        scores, query_lane, keys_lane = lane_scores(
            query, keys_all, lane_index, query_tags, key_tags
        )
        values_lane = lax.dynamic_index_in_dim(values_all, lane_index, 1, False).reshape(
            key_rows, head_count, HEAD_DIM
        )
        grad_lane = lax.dynamic_index_in_dim(grad_mixed, lane_index, 1, False).reshape(
            rows_dev, head_count, HEAD_DIM
        )
        attention = jnp.exp(
            scores - lax.dynamic_index_in_dim(log_total, lane_index, 0, False)[:, :, None]
        )
        grad_attention = jnp.einsum(
            "qhd,khd->hqk", grad_lane, values_lane, preferred_element_type=jnp.float32
        )
        inner = jnp.sum(attention * grad_attention, axis=-1, keepdims=True)
        grad_scores = (attention * (grad_attention - inner)).astype(jnp.bfloat16)
        query_part = (
            jnp.einsum("hqk,khd->qhd", grad_scores, keys_lane, preferred_element_type=jnp.float32)
            * SCORE_SCALE
        )
        key_part = (
            jnp.einsum("hqk,qhd->khd", grad_scores, query_lane, preferred_element_type=jnp.float32)
            * SCORE_SCALE
        )
        value_part = jnp.einsum(
            "hqk,qhd->khd",
            attention.astype(jnp.bfloat16),
            grad_lane,
            preferred_element_type=jnp.float32,
        )
        stacked = jnp.stack(
            [key_part.reshape(key_rows, features), value_part.reshape(key_rows, features)], axis=1
        )
        key_terms = stacked[:, None]
        grad_query = query_part.reshape(rows_dev, 1, features)
        return (grad_query, key_terms)

    initial = (
        jnp.zeros((rows_dev, lane_count, features), jnp.float32),
        jnp.zeros((key_rows, lane_count, 2, features), jnp.float32),
    )
    return lax.fori_loop(0, lane_count, one_lane, initial)


def front(stream, layer_index, params, query_tags, key_tags, positions):
    (
        gain_one,
        shift_one,
        mat_qkv,
        bias_qkv,
        mat_out,
        bias_out,
        gain_two,
        shift_two,
        mat_up,
        bias_up,
        mat_down,
        bias_down,
    ) = [item[layer_index] for item in params]
    rows_dev, lane_count, width = stream.shape
    features = mat_qkv.shape[2]
    head_count = features // HEAD_DIM
    frame_place, row_place, column_place = positions
    first = layer_norm(stream, gain_one, shift_one).astype(jnp.bfloat16)
    projected = (
        jnp.einsum("tbd,dcf->tbcf", first, mat_qkv, preferred_element_type=jnp.float32) + bias_qkv
    )
    split = projected.reshape(rows_dev, lane_count, 3, head_count, HEAD_DIM)
    query = (
        rotate(split[:, :, 0], frame_place, row_place, column_place)
        .reshape(rows_dev, lane_count, features)
        .astype(jnp.bfloat16)
    )
    keys = (
        rotate(split[:, :, 1], frame_place, row_place, column_place)
        .reshape(rows_dev, lane_count, features)
        .astype(jnp.bfloat16)
    )
    values = projected[:, :, 2].astype(jnp.bfloat16)
    keys_all, values_all = (
        lax.all_gather(keys, "seq", axis=0, tiled=True),
        lax.all_gather(values, "seq", axis=0, tiled=True),
    )
    mixed_full, log_total = attend_forward(query, keys_all, values_all, query_tags, key_tags)
    mixed = mixed_full.astype(jnp.bfloat16)
    middle = (
        stream
        + sum_heads(jnp.einsum("tbf,fd->tbd", mixed, mat_out, preferred_element_type=jnp.float32))
        + bias_out
    )
    second = layer_norm(middle, gain_two, shift_two).astype(jnp.bfloat16)
    hidden = jnp.einsum("tbd,df->tbf", second, mat_up, preferred_element_type=jnp.float32) + bias_up
    activation = gelu_exact(hidden).astype(jnp.bfloat16)
    return (
        first,
        query,
        keys_all,
        values_all,
        log_total,
        mixed,
        middle,
        second,
        hidden,
        activation,
        mixed_full,
    )


def layer_backward(stream, gradient, layer_index, params, query_tags, key_tags, positions):
    (
        gain_one,
        shift_one,
        mat_qkv,
        bias_qkv,
        mat_out,
        bias_out,
        gain_two,
        shift_two,
        mat_up,
        bias_up,
        mat_down,
        bias_down,
    ) = [item[layer_index] for item in params]
    (
        first,
        query,
        keys_all,
        values_all,
        log_total,
        mixed,
        middle,
        second,
        hidden,
        activation,
        mixed_full,
    ) = front(stream, layer_index, params, query_tags, key_tags, positions)
    frame_place, row_place, column_place = positions
    rows_dev, lane_count, width = stream.shape
    features = query.shape[2]
    head_count = features // HEAD_DIM
    grad_low = gradient.astype(jnp.bfloat16)
    grad_w_down = jnp.einsum(
        "tbf,tbd->fd", activation, grad_low, preferred_element_type=jnp.float32
    )
    grad_b_down = jnp.sum(gradient, axis=(0, 1))
    grad_activation = jnp.einsum(
        "tbd,fd->tbf", grad_low, mat_down, preferred_element_type=jnp.float32
    )
    grad_hidden = jax.vjp(gelu_exact, hidden)[1](grad_activation)[0].astype(jnp.bfloat16)
    grad_b_up = jnp.sum(grad_hidden.astype(jnp.float32), axis=(0, 1))
    grad_w_up = jnp.einsum("tbd,tbf->df", second, grad_hidden, preferred_element_type=jnp.float32)
    grad_second = sum_inputs(
        jnp.einsum("tbf,df->tbd", grad_hidden, mat_up, preferred_element_type=jnp.float32)
    )
    middle_pull = jax.vjp(layer_norm, middle, gain_two, shift_two)[1]
    grad_inner, grad_gain_two, grad_shift_two = middle_pull(grad_second)
    grad_middle = gradient + grad_inner
    grad_b_out = jnp.sum(grad_middle, axis=(0, 1))
    middle_low = grad_middle.astype(jnp.bfloat16)
    grad_w_out = jnp.einsum("tbf,tbd->fd", mixed, middle_low, preferred_element_type=jnp.float32)
    grad_mixed = jnp.einsum(
        "tbd,fd->tbf", middle_low, mat_out, preferred_element_type=jnp.float32
    ).astype(jnp.bfloat16)
    grad_query, key_terms = attend_backward(
        query, keys_all, values_all, log_total, grad_mixed, query_tags, key_tags
    )
    returned = lax.psum_scatter(key_terms, "seq", scatter_dimension=0, tiled=True)
    turned_query = rotate(
        grad_query.reshape(rows_dev, lane_count, head_count, HEAD_DIM),
        -frame_place,
        -row_place,
        -column_place,
    )
    turned_keys = rotate(
        returned[:, :, 0].reshape(rows_dev, lane_count, head_count, HEAD_DIM),
        -frame_place,
        -row_place,
        -column_place,
    )
    grad_projected = jnp.stack(
        [
            turned_query.reshape(rows_dev, lane_count, features),
            turned_keys.reshape(rows_dev, lane_count, features),
            returned[:, :, 1],
        ],
        axis=2,
    ).astype(jnp.bfloat16)
    grad_b_qkv = jnp.sum(grad_projected.astype(jnp.float32), axis=(0, 1))
    grad_w_qkv = jnp.einsum(
        "tbd,tbcf->dcf", first, grad_projected, preferred_element_type=jnp.float32
    )
    grad_first = sum_inputs(
        jnp.einsum("tbcf,dcf->tbd", grad_projected, mat_qkv, preferred_element_type=jnp.float32)
    )
    first_pull = jax.vjp(layer_norm, stream, gain_one, shift_one)[1]
    grad_entry, grad_gain_one, grad_shift_one = first_pull(grad_first)
    grads = (
        grad_gain_one,
        grad_shift_one,
        grad_w_qkv,
        grad_b_qkv,
        grad_w_out,
        grad_b_out,
        grad_gain_two,
        grad_shift_two,
        grad_w_up,
        grad_b_up,
        grad_w_down,
        grad_b_down,
    )
    return (grad_middle + grad_entry, grads)


def per_device(
    tokens,
    d_out,
    norm1_gain,
    norm1_shift,
    w_qkv,
    b_qkv,
    w_out,
    b_out,
    norm2_gain,
    norm2_shift,
    w_up,
    b_up,
    w_down,
    b_down,
    episode_frames,
    live,
):
    rows_dev = tokens.shape[0]
    lane_count = tokens.shape[1] // MICRO
    total_rows = rows_dev * lax.axis_size("seq")
    local_positions = lax.axis_index("seq") * rows_dev + jnp.arange(rows_dev, dtype=jnp.int32)
    key_positions = jnp.arange(total_rows, dtype=jnp.int32)
    tagger = jax.vmap(episode_tags, in_axes=(0, None), out_axes=1)
    query_episode, query_frame, query_row, query_column = tagger(episode_frames, local_positions)
    key_episode, key_frame, key_row, key_column = tagger(episode_frames, key_positions)
    live_keys = lax.all_gather(live, "seq", axis=0, tiled=True)
    params = (
        norm1_gain,
        norm1_shift,
        w_qkv,
        b_qkv,
        w_out,
        b_out,
        norm2_gain,
        norm2_shift,
        w_up,
        b_up,
        w_down,
        b_down,
    )
    layer_grads = [None] * LAYERS
    outputs = []
    grad_tokens = []
    for micro_index in range(MICRO):
        first_lane = micro_index * lane_count
        last_lane = first_lane + lane_count
        query_tags = (query_episode[:, first_lane:last_lane], query_frame[:, first_lane:last_lane])
        key_tags = (
            key_episode[:, first_lane:last_lane],
            key_frame[:, first_lane:last_lane],
            live_keys[:, first_lane:last_lane],
        )
        positions = (
            query_frame[:, first_lane:last_lane],
            query_row[:, first_lane:last_lane],
            query_column[:, first_lane:last_lane],
        )
        stream = tokens[:, first_lane:last_lane].astype(jnp.float32)
        inputs = []
        gathered = []
        for layer_index in range(LAYERS):
            inputs.append(stream)
            layer_state = front(stream, layer_index, params, query_tags, key_tags, positions)
            gathered.append((layer_state[2], layer_state[3]))
            branch = jnp.einsum(
                "tbf,fd->tbd",
                layer_state[9],
                w_down[layer_index],
                preferred_element_type=jnp.float32,
            )
            stream = layer_state[6] + sum_heads(branch) + b_down[layer_index]
        outputs.append(stream)
        gradient = d_out[:, first_lane:last_lane]
        for layer_index in reversed(range(LAYERS)):
            gradient, grads = layer_backward(
                inputs[layer_index], gradient, layer_index, params, query_tags, key_tags, positions
            )
            if layer_grads[layer_index] is None:
                layer_grads[layer_index] = grads
            else:
                layer_grads[layer_index] = jax.tree.map(jnp.add, layer_grads[layer_index], grads)
        grad_tokens.append(gradient)
    stacked = [
        jnp.stack([layer_grads[layer_index][entry] for layer_index in range(LAYERS)])
        for entry in range(12)
    ]
    (
        grad_gain_one,
        grad_shift_one,
        grad_w_qkv,
        grad_b_qkv,
        grad_w_out,
        grad_b_out,
        grad_gain_two,
        grad_shift_two,
        grad_w_up,
        grad_b_up,
        grad_w_down,
        grad_b_down,
    ) = stacked
    in_sums = (
        lax.psum_scatter(grad_w_qkv, "seq", scatter_dimension=1, tiled=True),
        lax.psum_scatter(grad_w_up, "seq", scatter_dimension=1, tiled=True),
        lax.psum_scatter(grad_gain_one, "seq", scatter_dimension=1, tiled=True),
        lax.psum_scatter(grad_shift_one, "seq", scatter_dimension=1, tiled=True),
        lax.psum_scatter(grad_gain_two, "seq", scatter_dimension=1, tiled=True),
        lax.psum_scatter(grad_shift_two, "seq", scatter_dimension=1, tiled=True),
        lax.psum_scatter(grad_b_out, "seq", scatter_dimension=1, tiled=True),
        lax.psum_scatter(grad_b_down, "seq", scatter_dimension=1, tiled=True),
    )
    out_sums = (
        lax.psum_scatter(grad_w_out, "seq", scatter_dimension=2, tiled=True),
        lax.psum_scatter(grad_w_down, "seq", scatter_dimension=2, tiled=True),
    )
    bias_total = lax.psum((grad_b_qkv, grad_b_up), "seq")
    return (
        jnp.concatenate(outputs, axis=1),
        jnp.concatenate(grad_tokens, axis=1),
        in_sums[2],
        in_sums[3],
        in_sums[0],
        bias_total[0],
        out_sums[0],
        in_sums[6],
        in_sums[4],
        in_sums[5],
        in_sums[1],
        bias_total[1],
        out_sums[1],
        in_sums[7],
    )


MESH = pl.DeviceIdType.MESH
BF16 = jnp.bfloat16
F32 = jnp.float32
VMEM_BYTES = 60 * 1024 * 1024
PAIR = 128
VEC = 2048


def nn(left, right):
    return lax.dot_general(left, right, (((1,), (0,)), ((), ())), preferred_element_type=F32)


def nt(left, right):
    return lax.dot_general(left, right, (((1,), (1,)), ((), ())), preferred_element_type=F32)


def tn(left, right):
    return lax.dot_general(left, right, (((0,), (0,)), ((), ())), preferred_element_type=F32)


def at(start, size):
    return pl.ds(pl.multiple_of(start, size), size)


def remote(src, dst, send, recv, seq, tp):
    return pltpu.make_async_remote_copy(
        src_ref=src,
        dst_ref=dst,
        send_sem=send,
        recv_sem=recv,
        device_id=(seq, tp),
        device_id_type=MESH,
    )


def hello(partners):
    barrier = pltpu.get_barrier_semaphore()
    for seq, tp in partners:
        pl.semaphore_signal(barrier, inc=1, device_id=(seq, tp), device_id_type=MESH)


def met(partners):
    pl.semaphore_wait(pltpu.get_barrier_semaphore(), len(partners))


def whole(array):
    zeros = (0,) * array.ndim
    return pl.BlockSpec(array.shape, lambda s: zeros, pipeline_mode=pl.Buffered(1))


def whole_out(shape):
    zeros = (0,) * len(shape)
    return pl.BlockSpec(shape, lambda s: zeros)


ANYWHERE = pl.BlockSpec(memory_space=pl.ANY)


def turn_row(table, place, section):
    frequency = np.exp(np.arange(10, dtype=np.float32) * np.float32(-math.log(10000.0) / 10.0))
    angle = place.astype(np.float32)[:, None] * frequency
    for base in range(20 * section, PAIR, HEAD_DIM):
        table[0, :, base : base + 10] = np.cos(angle)
        table[0, :, base + 10 : base + 20] = np.cos(angle)
        table[1, :, base : base + 10] = -np.sin(angle)
        table[2, :, base + 10 : base + 20] = np.sin(angle)


def turn_constants(frames):
    within, ahead = np.zeros((3, FRAME, PAIR), np.float32), np.zeros((3, frames, PAIR), np.float32)
    turn_row(within, np.arange(FRAME) // GRID, 1)
    turn_row(within, np.arange(FRAME) % GRID, 2)
    for base in range(60, PAIR, HEAD_DIM):
        within[0, :, base : base + 4] = 1.0
    turn_row(ahead, np.arange(frames), 0)
    return jnp.asarray(within), jnp.asarray(ahead)


def turn(values, tables, back=False):
    cosine, lower, upper = tables
    pieces = []
    for start in range(0, values.shape[1], PAIR):
        slab = values[:, start : start + PAIR]
        moved = pltpu.roll(slab, PAIR - 10, 1) * lower + pltpu.roll(slab, 10, 1) * upper
        pieces.append(slab * cosine - moved if back else slab * cosine + moved)
    return jnp.concatenate(pieces, axis=1)


def tables_of(fixed_ref, frames_ref, chunk):
    return [fixed_ref[i] + frames_ref[i, pl.ds(chunk, 1), :] for i in range(3)]


def normed(stream):
    center = stream - jnp.mean(stream, axis=-1, keepdims=True)
    spread = jnp.mean(center * center, axis=-1, keepdims=True)
    scale = lax.rsqrt(spread + EPSILON)
    return center * scale, scale


def norm_pull(grad, gain, unit, scale):
    scaled = grad * gain
    return scale * (
        scaled
        - jnp.mean(scaled, axis=-1, keepdims=True)
        - unit * jnp.mean(scaled * unit, axis=-1, keepdims=True)
    )


def keep_norm(unit, scale, unit_ref, scale_ref):
    unit_ref[...] = unit.astype(BF16)
    scale_ref[...] = jnp.broadcast_to(scale, scale_ref.shape)


def kept_norm(unit_ref, scale_ref):
    copies = unit_ref.shape[1] // scale_ref.shape[1]
    return unit_ref[...].astype(F32), jnp.concatenate([scale_ref[...]] * copies, axis=1)


def column_sum(values):
    return jnp.sum(values, axis=0, keepdims=True)


def gelu_both(hidden):
    normal = 0.5 + 0.5 * lax.erf(hidden * math.sqrt(0.5))
    density = jnp.exp(hidden * hidden * -0.5) * (1.0 / math.sqrt(2.0 * math.pi))
    return hidden * normal, normal + hidden * density


def project(stream, chunk, layer, pair, refs, outs, first_full):
    gain, shift, weight, bias, fixed, frames = refs
    query_ref, key_ref, value_ref, first_ref, unit_ref, scale_ref = outs
    unit, scale = normed(stream)
    keep_norm(unit, scale, unit_ref, scale_ref)
    first = (unit * gain[layer : layer + 1, :] + shift[layer : layer + 1, :]).astype(BF16)
    first_full[...] = first
    first_ref[...] = first_full[:, at(pair * PAIR, PAIR)]
    tables = tables_of(fixed, frames, chunk)
    query = nn(first, weight[0]) + bias[0, layer : layer + 1, :]
    query_ref[...] = (turn(query, tables) * SCORE_SCALE).astype(BF16)
    key = nn(first, weight[1]) + bias[1, layer : layer + 1, :]
    key_ref[...] = turn(key, tables).astype(BF16)
    value = nn(first, weight[2]) + bias[2, layer : layer + 1, :]
    value_ref[...] = value.astype(BF16)


class Relay:
    sems = 6

    def __init__(self, n, rows, buffer, other, sems, lives=None, live_other=None):
        self.n, self.rows, self.buffer, self.other = n, rows, buffer, other
        self.lives, self.live_other = lives, live_other
        self.z_send, self.z_recv, self.y_send, self.y_recv, self.c_send, self.c_recv = sems
        self.planes = n // 4
        self.me, self.core = lax.axis_index("seq"), lax.axis_index("tp")
        me = self.me
        self.x, self.y, self.z = lax.rem(me, 2), lax.rem(me // 2, 2), me // 4
        self.across = me + 2 - 4 * self.y

    @staticmethod
    def scratch(n):
        dma, planes = pltpu.SemaphoreType.DMA, n // 4
        shapes = [(planes, 2, 2)] * 2 + [(planes, 2)] * 2 + [(2 * planes,)] * 2
        return [dma(shape) for shape in shapes]

    @property
    def events(self):
        return self.planes

    def plane(self, step):
        return lax.rem(self.z + step, self.planes)

    def place(self, plane, lane):
        return plane * 4 + self.y * 2 + lane

    def reached(self):
        return [(step, far) for step in range(self.planes) for far in (0, 1) if step or far]

    def hello(self):
        barrier = pltpu.get_barrier_semaphore()
        partners = [(self.across, self.core), (self.me, 1 - self.core)]
        for step, far in self.reached():
            lane = 1 - self.x if far else self.x
            partners.append((self.place(self.plane(step), lane), self.core))
        for seq, tp in partners:
            pl.semaphore_signal(barrier, inc=1, device_id=(seq, tp), device_id_type=MESH)

    def met(self):
        pl.semaphore_wait(pltpu.get_barrier_semaphore(), 2 + len(self.reached()))

    def rows_of(self, side, seq):
        return self.buffer.at[side, at(seq * self.rows, self.rows), :]

    def block(self, side, pair):
        return self.buffer.at[side, at(pair * 2 * self.rows, 2 * self.rows), :]

    def items(self, pair):
        found = [self.block(self.core, pair)]
        if self.lives is not None:
            found.append(self.lives.at[at(pair * 2, 2)])
        return found

    def each(self, copy, what):
        for index in range(1 if self.lives is None else 2):
            getattr(copy(index), what)()

    def z_copy(self, step, far):
        def copy(index):
            lane = 1 - self.x if far else self.x
            if index == 0:
                source = self.other.at[self.core] if far else self.rows_of(self.core, self.me)
                target = self.rows_of(self.core, self.me)
            else:
                source = self.live_other if far else self.lives.at[self.me]
                target = self.lives.at[self.me]
            return remote(
                source,
                target,
                self.z_send.at[step, far, index],
                self.z_recv.at[step, far, index],
                self.place(self.plane(step), lane),
                self.core,
            )

        return copy

    def y_copy(self, plane, row):
        def copy(index):
            item = self.items(plane * 2 + row)[index]
            return remote(
                item,
                item,
                self.y_send.at[plane, index],
                self.y_recv.at[plane, index],
                self.across,
                self.core,
            )

        return copy

    def c_copy(self, pair, side):
        item = self.block(side, pair)
        return remote(
            item, item, self.c_send.at[pair], self.c_recv.at[pair], self.me, 1 - self.core
        )

    def begin(self):
        for step, far in self.reached():
            self.each(self.z_copy(step, far), "start")

    def arrive(self, event):
        for far in (0, 1) if event else (1,):
            self.each(self.z_copy(event, far), "wait_recv")
        plane = self.plane(self.planes - event)
        self.each(self.y_copy(plane, self.y), "start")
        self.c_copy(plane * 2 + self.y, self.core).start()

    def complete(self, event):
        plane = self.plane(self.planes - event)
        self.each(self.y_copy(plane, 1 - self.y), "wait_recv")
        self.c_copy(plane * 2 + 1 - self.y, self.core).start()

    def wait_straight(self):
        for step, far in self.reached():
            self.each(self.z_copy(step, far), "wait_recv")
        for step, far in self.reached():
            self.each(self.z_copy(step, far), "wait_send")

    def cross(self):
        for plane in range(self.planes):
            self.each(self.y_copy(plane, self.y), "start")
            self.c_copy(plane * 2 + self.y, self.core).start()

    def crossed(self, plane):
        self.each(self.y_copy(plane, 1 - self.y), "wait_recv")
        self.c_copy(plane * 2 + 1 - self.y, self.core).start()

    def wait_crossed(self):
        for pair in range(2 * self.planes):
            self.c_copy(pair, 1 - self.core).wait_recv()
        for plane in range(self.planes):
            self.each(self.y_copy(plane, self.y), "wait_send")
        for pair in range(2 * self.planes):
            self.c_copy(pair, self.core).wait_send()

    def ready(self, event):
        plane = self.plane(self.planes - event)
        self.c_copy(plane * 2, 1 - self.core).wait_recv()
        self.c_copy(plane * 2 + 1, 1 - self.core).wait_recv()
        return plane

    def finish(self):
        for step, far in self.reached():
            self.each(self.z_copy(step, far), "wait_send")
        for plane in range(self.planes):
            self.each(self.y_copy(plane, self.y), "wait_send")
        for pair in range(2 * self.planes):
            self.c_copy(pair, self.core).wait_send()


def split_lanes(values, x, buffer, other, start, rows):
    half = values.shape[2] // 2
    zero, one = values[:, 0, :], values[:, 1, :]
    own, far = jnp.where(x == 0, zero, one), jnp.where(x == 0, one, zero)
    core = lax.axis_index("tp")
    own = jnp.where(core == 0, own[:, :half], own[:, half:]).astype(BF16)
    buffer[core, at(start, rows), :] = own
    for side in range(2):
        other[side] = far[:, side * half : (side + 1) * half].astype(BF16)


def gather_and_project(tokens, live, episode_frames, gain, shift, qkv, bias, fixed, ahead, n):
    rows, lanes, width = tokens.shape
    half = width // 2
    total = n * rows
    chunks = total // FRAME
    per_frame = FRAME // rows
    features = qkv.shape[3]
    slots = episode_frames.shape[1]

    def kernel(*refs):
        refs = list(refs)

        def take(count):
            taken = refs[:count]
            del refs[:count]
            return taken

        tokens_ref, live_ref, counts_ref, gain_ref, shift_ref, w_any, bias_ref = take(7)
        fixed_ref, ahead_ref = take(2)
        all_ref, mask_ref, frames_ref = take(3)
        projected = take(6)
        other, lives, live_other, weight, full, w_sem = take(6)
        relay = Relay(n, rows, all_ref, other, take(Relay.sems), lives, live_other)
        load = pltpu.make_async_copy(w_any.at[0], weight, w_sem)
        load.start()
        relay.hello()
        x, me = relay.x, relay.me
        split_lanes(tokens_ref[...].astype(F32), x, all_ref, other, me * rows, rows)
        lane = lax.broadcasted_iota(jnp.int32, (1, FRAME), 1)
        here = lane // rows == lax.rem(me, per_frame)
        tiles = []
        for index in range(lanes):
            alive = live_ref[index : index + 1, :].astype(F32)
            alive = jnp.where(here, jnp.concatenate([alive] * per_frame, axis=1), 0.0)
            tiles.append(jnp.broadcast_to(alive, (8, FRAME)))
        lives[me] = jnp.where(x == 0, tiles[0], tiles[1])
        live_other[...] = jnp.where(x == 0, tiles[1], tiles[0])
        relay.met()
        relay.begin()

        counts = [counts_ref[x, slot] for slot in range(slots)]
        episodes, openings = [], []
        for frame in range(chunks):
            end, episode, opening = 0, 0, 0
            for slot in range(slots):
                end = end + counts[slot]
                passed = frame >= end
                episode = episode + passed.astype(jnp.int32)
                opening = opening + jnp.where(passed, counts[slot], 0)
            episodes.append(episode)
            openings.append(frame - opening)
        for index in range(3):
            table = []
            for frame in range(chunks):
                line = jnp.zeros((1, PAIR), F32)
                for choice in range(chunks):
                    line = jnp.where(
                        openings[frame] == choice, ahead_ref[index, choice : choice + 1, :], line
                    )
                table.append(line)
            frames_ref[index] = jnp.concatenate(
                table + [jnp.zeros((8 - chunks, PAIR), F32)], axis=0
            )
        load.wait()

        def project_frame(frame):
            place = at(frame * FRAME, FRAME)
            stream = jnp.concatenate([all_ref[0, place, :], all_ref[1, place, :]], axis=1)
            project(
                stream.astype(F32),
                frame,
                0,
                me // 2,
                (gain_ref, shift_ref, weight, bias_ref, fixed_ref, frames_ref),
                [ref.at[place, :] for ref in projected],
                full,
            )

        for event in range(relay.events):
            relay.arrive(event)
            if event:
                relay.complete(event - 1)
            if event > 1:
                project_frame(relay.ready(event - 2))
        relay.complete(relay.events - 1)
        for event in range(max(0, relay.events - 2), relay.events):
            project_frame(relay.ready(event))
        relay.finish()

        for key_frame in range(chunks):
            alive = lives[key_frame * per_frame, 0:1, :]
            for part in range(1, per_frame):
                alive = alive + lives[key_frame * per_frame + part, 0:1, :]
            closed = (alive - 1.0) * -MASKED
            lines = []
            for query_frame in range(chunks):
                allowed = (episodes[query_frame] == episodes[key_frame]) & (
                    openings[key_frame] <= openings[query_frame]
                )
                lines.append(jnp.where(allowed, closed, MASKED))
            lines.append(jnp.zeros((PAIR - chunks, FRAME), F32))
            mask_ref[key_frame * FRAME : (key_frame + 1) * FRAME, :] = jnp.concatenate(
                lines, axis=0
            ).T.astype(BF16)

    in_vmem = pl.BlockSpec(memory_space=pltpu.VMEM)
    in_smem = pl.BlockSpec(memory_space=pltpu.SMEM)
    projected = jax.ShapeDtypeStruct((total, features), BF16)
    return pl.pallas_call(
        kernel,
        out_shape=(
            jax.ShapeDtypeStruct((2, total, half), BF16),
            jax.ShapeDtypeStruct((total, PAIR), BF16),
            jax.ShapeDtypeStruct((3, 8, PAIR), F32),
            projected,
            projected,
            projected,
            jax.ShapeDtypeStruct((total, PAIR), BF16),
            jax.ShapeDtypeStruct((total, width), BF16),
            jax.ShapeDtypeStruct((total, PAIR), F32),
        ),
        in_specs=[in_vmem, in_vmem, in_smem, in_vmem, in_vmem, ANYWHERE] + [in_vmem] * 3,
        out_specs=(in_vmem,) * 9,
        scratch_shapes=[
            pltpu.VMEM((2, rows, half), BF16),
            pltpu.VMEM((n, 8, FRAME), F32),
            pltpu.VMEM((8, FRAME), F32),
            pltpu.VMEM(qkv.shape[1:], BF16),
            pltpu.VMEM((FRAME, width), BF16),
            pltpu.SemaphoreType.DMA,
        ]
        + Relay.scratch(n),
        compiler_params=pltpu.CompilerParams(
            collective_id=0, has_side_effects=True, vmem_limit_bytes=VMEM_BYTES
        ),
        name="gather_and_project",
    )(tokens, live, episode_frames, gain, shift, qkv, bias, fixed, ahead)


def halves(ref):
    return jnp.concatenate([ref[0], ref[1]], axis=1).astype(F32)


def halves_spec(shape, chunks, behind, span=FRAME):
    return pl.BlockSpec(
        (2, span, shape[2]), lambda s: (0, jnp.clip(s - behind, 0, chunks - 1), 0)
    )


def attention_forward(query, key, value, key_mask, d_out, d_part, n, identity):
    total, features = query.shape
    chunks = total // FRAME
    heads = features // HEAD_DIM
    slabs = features // PAIR
    rows_here = total // n
    first_phase = d_out is not None
    carried = d_out if first_phase else d_part
    half = carried.shape[2] // 2 if first_phase else carried.shape[1]

    def kernel(q_ref, k_ref, v_ref, mask_ref, d_ref, p_ref, r_ref, mixed_ref, d_to, buffer, other, d_sem, *sems):
        step = pl.program_id(0)
        relay = Relay(n, rows_here, buffer, other, sems)
        core = relay.core

        @pl.when(step == 0)
        def _():
            if first_phase:
                relay.hello()
                split_lanes(d_ref, relay.x, buffer, other, relay.me * rows_here, rows_here)
                relay.met()
                relay.begin()
            else:
                fetch = pltpu.make_async_copy(d_ref, buffer.at[core], d_sem)
                fetch.start()
                fetch.wait()
                partners = [(relay.across, core), (relay.me, 1 - core)]
                hello(partners)
                met(partners)
                relay.cross()

        if not first_phase:

            @pl.when(step == slabs - 2)
            def _():
                for plane in range(relay.planes // 2):
                    relay.crossed(plane)

        lane = lax.broadcasted_iota(jnp.int32, (1, PAIR), 1)
        low_side = lane < HEAD_DIM
        sides = [low_side.astype(F32).astype(BF16), (lane >= HEAD_DIM).astype(F32).astype(BF16)]
        keys_wide = jnp.concatenate([k_ref[...], mask_ref[...]], axis=1)
        values = [v_ref[...] * sides[side] + sides[1 - side] for side in range(2)]

        def score(frame, side):
            own = slice(frame * FRAME, (frame + 1) * FRAME)
            asked = jnp.broadcast_to((lane == frame).astype(F32), (FRAME, PAIR)).astype(BF16)
            ask = jnp.concatenate([q_ref[own, :] * sides[side], asked], axis=1)
            return nt(ask, keys_wide[: (frame + 1) * FRAME])

        turns = [(frame, side) for frame in reversed(range(chunks)) for side in range(2)]
        scores, sums = score(*turns[0]), []
        for index, (frame, side) in enumerate(turns):
            keys = FRAME * (frame + 1)
            own = slice(frame * FRAME, keys)
            following = score(*turns[index + 1]) if index + 1 < len(turns) else None
            highest = jnp.max(scores, axis=1, keepdims=True)
            shifted = jnp.exp(scores - highest).astype(BF16)
            p_ref[frame, side, :keys, :] = shifted.T
            sums.append(nn(shifted, values[side][:keys]))
            scores = following
            if side == 1:
                one, two = sums[-2:]
                divisor = 1.0 / jnp.where(
                    low_side, pltpu.roll(one, HEAD_DIM, 1), pltpu.roll(two, HEAD_DIM, 1)
                )
                r_ref[own, :] = divisor
                mixed_ref[own, :] = (jnp.where(low_side, one, two) * divisor).astype(BF16)

        @pl.when(step == slabs - 1)
        def _():
            if first_phase:
                relay.wait_straight()
                source = buffer.at[core]
            else:
                for plane in range(relay.planes // 2, relay.planes):
                    relay.crossed(plane)
                relay.wait_crossed()
                source = buffer
            keep = pltpu.make_async_copy(source, d_to, d_sem)
            keep.start()
            keep.wait()

    slab = pl.BlockSpec((total, PAIR), lambda s: (0, s))
    return pl.pallas_call(
        kernel,
        grid=(slabs,),
        out_shape=(
            jax.ShapeDtypeStruct((chunks, heads, total, FRAME), BF16),
            jax.ShapeDtypeStruct((total, features), F32),
            jax.ShapeDtypeStruct((total, features), BF16),
            jax.ShapeDtypeStruct((total, half) if first_phase else (2, total, half), BF16),
        ),
        in_specs=[slab] * 3 + [whole(key_mask), whole(carried) if first_phase else ANYWHERE],
        out_specs=(
            pl.BlockSpec((chunks, 2, total, FRAME), lambda s: (0, s, 0, 0)),
            slab,
            slab,
            ANYWHERE,
        ),
        scratch_shapes=[
            pltpu.VMEM((2, total, half), BF16),
            pltpu.VMEM((2, rows_here, half), BF16),
            pltpu.SemaphoreType.DMA,
        ]
        + Relay.scratch(n),
        compiler_params=pltpu.CompilerParams(
            collective_id=identity, has_side_effects=True, vmem_limit_bytes=VMEM_BYTES
        ),
        name=f"attention_forward_{identity}",
    )(query, key, value, key_mask, carried)


def layer_forward(layer, mixed, stream, mats, rows_of, next_refs, identity):
    total, features = mixed.shape
    split = stream.ndim == 3
    width = mats[1].shape[1]
    hidden_units = mats[1].shape[2]
    chunks = total // FRAME
    columns = 256
    last = next_refs is None
    b_out, gain, shift, b_up, b_down = rows_of
    mat_out, mat_up, mat_down = mats

    def kernel(*refs):
        refs = list(refs)

        def take(count):
            taken = refs[:count]
            del refs[:count]
            return taken

        mixed_ref, x_ref = take(2)
        wo_any, wu_any, wd_any = take(3)
        bo_ref, gain_ref, shift_ref, bu_ref, bd_ref = take(5)
        if not last:
            wq_any, ngain, nshift, nbias, fixed, frames = take(6)
        unit_ref, scale_ref, second_ref, act_ref, gp_ref, x_out = take(6)
        if not last:
            next_outs = take(6)
        wo, wu, wd, mid, full, next_full = take(6)
        if not last:
            (wq,) = take(1)
        a_send, a_recv, b_send, b_recv, w_sem, send_sem, recv_sem = take(7)

        step = pl.program_id(0)
        me, core = lax.axis_index("seq"), lax.axis_index("tp")

        items = [(wo_any, wo), (wu_any, wu), (wd_any, wd)]
        if not last:
            items.append((wq_any, wq))

        def load(index):
            source, target = items[index]
            return pltpu.make_async_copy(
                source.at[layer if index < 3 else layer + 1], target, w_sem.at[index]
            )

        def exchange(kind, chunk):
            source, target = ((a_send, a_recv), (b_send, b_recv))[kind]
            return remote(
                source.at[chunk],
                target.at[chunk],
                send_sem.at[kind, chunk],
                recv_sem.at[kind, chunk],
                me,
                1 - core,
            )

        @pl.when(step == 0)
        def _():
            for index in range(len(items)):
                load(index).start()
            hello([(me, 1 - core)])

        @pl.when(step == 0)
        def _():
            load(0).wait()
            met([(me, 1 - core)])

        @pl.when(step < chunks)
        def _():
            a_send[step] = nn(mixed_ref[...], wo[...]).astype(BF16)
            exchange(0, step).start()

        def feed_forward():
            chunk = step - 1
            middle = (halves(x_ref) if split else x_ref[...]) + (
                a_send[chunk].astype(F32) + a_recv[chunk].astype(F32)
            )
            middle = middle + bo_ref[layer : layer + 1, :]
            mid[lax.rem(chunk, 2)] = middle
            unit, scale = normed(middle)
            keep_norm(unit, scale, unit_ref, scale_ref)
            second = (unit * gain_ref[layer : layer + 1, :] + shift_ref[layer : layer + 1, :]).astype(BF16)
            full[...] = second
            second_ref[...] = full[:, at((me // 2) * PAIR, PAIR)]
            parts = [slice(start, start + columns) for start in range(0, hidden_units, columns)]
            hidden = nn(second, wu[:, parts[0]])
            for index, part in enumerate(parts):
                following = nn(second, wu[:, parts[index + 1]]) if index + 1 < len(parts) else None
                act, slope = gelu_both(hidden + bu_ref[layer : layer + 1, part])
                act_ref[:, part] = act.astype(BF16)
                gp_ref[:, part] = slope.astype(BF16)
                hidden = following
            b_send[chunk] = nn(act_ref[...], wd[...]).astype(BF16)

        def close():
            chunk = step - 2
            result = mid[lax.rem(chunk, 2)] + (b_send[chunk].astype(F32) + b_recv[chunk].astype(F32))
            result = result + bd_ref[layer : layer + 1, :]
            x_out[...] = result
            if not last:
                project(
                    result,
                    chunk,
                    layer + 1,
                    me // 2,
                    (ngain, nshift, wq, nbias, fixed, frames),
                    next_outs,
                    next_full,
                )

        @pl.when(step == 1)
        def _():
            load(1).wait()
            load(2).wait()

        @pl.when((step >= 1) & (step <= chunks))
        def _():
            exchange(0, step - 1).wait_recv()
            feed_forward()
            exchange(1, step - 1).start()

        if not last:

            @pl.when(step == 2)
            def _():
                load(3).wait()

        @pl.when(step >= 2)
        def _():
            exchange(1, step - 2).wait_recv()
            close()

        @pl.when(step == chunks + 1)
        def _():
            for kind in range(2):
                for chunk in range(chunks):
                    exchange(kind, chunk).wait_send()

    def rows(columns, behind):
        return pl.BlockSpec(
            (FRAME, columns), lambda s: (jnp.clip(s - behind, 0, chunks - 1), 0)
        )

    in_specs = [rows(features, 0)]
    in_specs += [halves_spec(stream.shape, chunks, 1) if split else rows(width, 1)]
    in_specs += [ANYWHERE] * 3 + [whole(item) for item in rows_of]
    operands = [mixed, stream, *mats, *rows_of]
    if not last:
        in_specs += [ANYWHERE] + [whole(item) for item in next_refs[1:]]
        operands += list(next_refs)
    out_shape = [
        jax.ShapeDtypeStruct((total, width), BF16),
        jax.ShapeDtypeStruct((total, PAIR), F32),
        jax.ShapeDtypeStruct((total, PAIR), BF16),
        jax.ShapeDtypeStruct((total, hidden_units), BF16),
        jax.ShapeDtypeStruct((total, hidden_units), BF16),
        jax.ShapeDtypeStruct((total, width), F32),
    ]
    out_specs = [
        rows(width, 1),
        rows(PAIR, 1),
        rows(PAIR, 1),
        rows(hidden_units, 1),
        rows(hidden_units, 1),
        rows(width, 2),
    ]
    scratch = [
        pltpu.VMEM(mat_out.shape[1:], BF16),
        pltpu.VMEM(mat_up.shape[1:], BF16),
        pltpu.VMEM(mat_down.shape[1:], BF16),
        pltpu.VMEM((2, FRAME, width), F32),
        pltpu.VMEM((FRAME, width), BF16),
        pltpu.VMEM((FRAME, width), BF16),
    ]
    if not last:
        out_shape += [jax.ShapeDtypeStruct((total, features), BF16)] * 3
        out_shape += [jax.ShapeDtypeStruct((total, PAIR), BF16)]
        out_shape += [jax.ShapeDtypeStruct((total, width), BF16)]
        out_shape += [jax.ShapeDtypeStruct((total, PAIR), F32)]
        out_specs += [rows(features, 2)] * 3 + [rows(PAIR, 2), rows(width, 2), rows(PAIR, 2)]
        scratch += [pltpu.VMEM(next_refs[0].shape[1:], BF16)]
    scratch += [pltpu.VMEM((chunks, FRAME, width), BF16)] * 4
    scratch += [
        pltpu.SemaphoreType.DMA((4,)),
        pltpu.SemaphoreType.DMA((2, chunks)),
        pltpu.SemaphoreType.DMA((2, chunks)),
    ]
    return pl.pallas_call(
        kernel,
        grid=(chunks + 2,),
        out_shape=out_shape,
        in_specs=in_specs,
        out_specs=out_specs,
        scratch_shapes=scratch,
        compiler_params=pltpu.CompilerParams(
            collective_id=identity, has_side_effects=True, vmem_limit_bytes=VMEM_BYTES
        ),
        name=f"layer_forward_{layer}",
    )(*operands)


class Swap:
    def __init__(self, ships, lane_rows):
        self.ships, self.lane_rows = ships, lane_rows
        self.count = len(ships) + len(lane_rows)

    def operands(self):
        return [*self.ships, *[item for item, _ in self.lane_rows]]

    def in_specs(self):
        return [whole(item) for item in self.ships] + [ANYWHERE] * len(self.lane_rows)

    def outputs(self):
        shapes, specs = [], []
        for item in self.ships:
            shape = (item.shape[0] // 2, item.shape[1])
            shapes.append(jax.ShapeDtypeStruct(shape, F32))
            specs.append(whole_out(shape))
        for item, count in self.lane_rows:
            shapes.append(jax.ShapeDtypeStruct((count or item.shape[0], item.shape[1]), item.dtype))
            specs.append(ANYWHERE)
        return shapes, specs

    def scratch(self):
        if not self.count:
            return []
        buffers = [pltpu.VMEM((item.shape[0] // 2, item.shape[1]), BF16) for item in self.ships]
        return buffers * 2 + [pltpu.SemaphoreType.DMA((self.count,))] * 2

    def bind(self, sources, targets, scratch):
        ships = len(self.ships)
        me, core = lax.axis_index("seq"), lax.axis_index("tp")
        x = lax.rem(me, 2)
        beside = me + 1 - 2 * x
        half = PAIR // 2

        def copy(index):
            if index < ships:
                source, target = scratch[index], scratch[ships + index]
            else:
                source, target = sources[index], targets[index]
                count = self.lane_rows[index - ships][1]
                if count:
                    source = source.at[at(beside * count, count), :]
            send, recv = scratch[2 * ships].at[index], scratch[2 * ships + 1].at[index]
            return remote(source, target, send, recv, beside, core)

        def start():
            for index in range(self.count):
                if index < ships:
                    scratch[index][...] = sources[index][at((1 - x) * half, half), :].astype(BF16)
                copy(index).start()

        def finish():
            for index in range(self.count):
                copy(index).wait_recv()
                if index < ships:
                    own = sources[index][at(x * half, half), :]
                    targets[index][...] = own + scratch[ships + index][...].astype(F32)
            for index in range(self.count):
                copy(index).wait_send()

        return start, finish


def attention_backward(
    probs, divisor, mixed, query, key, value, grad_mixed, first, fixed, frames, swap, swap_qkv, identity
):
    total, features = query.shape
    chunks = total // FRAME
    slabs = features // PAIR
    half = PAIR // 2

    def kernel(*refs):
        refs = list(refs)

        def take(count):
            taken = refs[:count]
            del refs[:count]
            return taken

        p_ref, r_ref, o_ref, q_ref, k_ref, v_ref, g_ref, first_ref, fixed_ref, frames_ref = take(10)
        sources = take(swap.count)
        dq_ref, dk_ref, dv_ref, qkv_out = take(4)
        targets = take(swap.count)
        dk_sum, dv_sum, first_turned = take(3)
        if swap_qkv:
            qkv_own, qkv_send, qkv_recv, qkv_sems = take(4)
        start, finish = swap.bind(sources, targets, refs)

        step = pl.program_id(0)
        me, core = lax.axis_index("seq"), lax.axis_index("tp")
        x = lax.rem(me, 2)
        beside = me + 1 - 2 * x

        def qkv_copy(slab):
            return remote(
                qkv_send.at[slab],
                qkv_recv.at[slab],
                qkv_sems.at[0, slab],
                qkv_sems.at[1, slab],
                beside,
                core,
            )

        @pl.when(step == 0)
        def _():
            hello([(beside, core)])
            first_turned[...] = first_ref[...].T
            met([(beside, core)])
            start()

        lane = lax.broadcasted_iota(jnp.int32, (1, PAIR), 1)
        sides = [(lane < HEAD_DIM).astype(F32).astype(BF16), (lane >= HEAD_DIM).astype(F32).astype(BF16)]
        turned = k_ref[...].T
        ones = jnp.broadcast_to((lane < 2).astype(F32), (total, PAIR)).astype(BF16)
        values = jnp.concatenate([v_ref[...], ones], axis=1)

        def give(frame):
            keys = FRAME * (frame + 1)
            own = slice(frame * FRAME, keys)
            scaled = (g_ref[own, :].astype(F32) * r_ref[own, :]).astype(BF16)
            inner = scaled.astype(F32) * o_ref[own, :].astype(F32)
            grads, q_parts, g_parts = [], [], []
            for side in range(2):
                delta = jnp.sum(
                    jnp.where((lane < HEAD_DIM) == (side == 0), inner, 0.0), axis=1, keepdims=True
                )
                coarse = delta.astype(BF16).astype(F32)
                rest = jnp.where(lane == 0, -coarse, jnp.where(lane == 1, coarse - delta, 0.0))
                g2 = scaled * sides[side]
                grads.append(nt(values[:keys], jnp.concatenate([g2, rest.astype(BF16)], axis=1)))
                q_parts.append(q_ref[own, :] * sides[side])
                g_parts.append(g2)
            return grads, jnp.concatenate(q_parts, axis=0), jnp.concatenate(g_parts, axis=0)

        given = give(chunks - 1)
        for frame in reversed(range(chunks)):
            keys = FRAME * (frame + 1)
            own = slice(frame * FRAME, keys)
            tables = tables_of(fixed_ref, frames_ref, frame)
            grads, q_part, g_part = given
            given = give(frame - 1) if frame else None
            query_parts, score_parts, prob_parts = [], [], []
            for side in range(2):
                attention = p_ref[frame, side, :keys, :]
                grad_scores = (attention.astype(F32) * grads[side]).astype(BF16)
                query_parts.append(nn(turned[side * HEAD_DIM : (side + 1) * HEAD_DIM, :keys], grad_scores))
                score_parts.append(grad_scores)
                prob_parts.append(attention)
            grad_query = jnp.concatenate(query_parts, axis=0).T
            key_parts = nn(jnp.concatenate(score_parts, axis=1), q_part)
            value_parts = nn(jnp.concatenate(prob_parts, axis=1), g_part)
            dq_ref[own, :] = (turn(grad_query, tables, True) * SCORE_SCALE).astype(BF16)
            if frame == chunks - 1:
                dk_sum[...] = key_parts
                dv_sum[...] = value_parts
            else:
                dk_sum[:keys, :] += key_parts
                dv_sum[:keys, :] += value_parts
            dk_ref[own, :] = turn(dk_sum[own, :], tables, True).astype(BF16)
            dv_ref[own, :] = dv_sum[own, :].astype(BF16)

        for part, ref in enumerate((dq_ref, dk_ref, dv_ref)):
            piece = slice(part * PAIR, (part + 1) * PAIR)
            terms = nn(first_turned[...], ref[...])
            if swap_qkv:
                qkv_own[step, :, piece] = terms
                qkv_send[step, :, piece] = qkv_own[step, at((1 - x) * half, half), piece].astype(BF16)
            else:
                qkv_out[:, at(part * features + step * PAIR, PAIR)] = terms
        if swap_qkv:
            qkv_copy(step).start()

        @pl.when(step == slabs - 1)
        def _():
            finish()
            for slab in range(slabs if swap_qkv else 0):
                qkv_copy(slab).wait_recv()
                for part in range(3):
                    piece = slice(part * PAIR, (part + 1) * PAIR)
                    place = part * features + slab * PAIR
                    qkv_out[:, place : place + PAIR] = qkv_own[
                        slab, at(x * half, half), piece
                    ] + qkv_recv[slab, :, piece].astype(F32)
            for slab in range(slabs if swap_qkv else 0):
                qkv_copy(slab).wait_send()

    slab = pl.BlockSpec((total, PAIR), lambda s: (0, s))
    in_specs = [pl.BlockSpec((chunks, 2, total, FRAME), lambda s: (0, s, 0, 0))]
    in_specs += [slab] * 6 + [whole(first), whole(fixed), whole(frames)]
    in_specs += swap.in_specs()
    qkv_shape = (half if swap_qkv else PAIR, 3 * features)
    shapes, specs = swap.outputs()
    out_shape = [jax.ShapeDtypeStruct((total, features), BF16)] * 3
    out_shape += [jax.ShapeDtypeStruct(qkv_shape, F32)] + shapes
    out_specs = [slab] * 3 + [whole_out(qkv_shape)] + specs
    scratch = [pltpu.VMEM((total, PAIR), F32)] * 2 + [pltpu.VMEM((PAIR, total), BF16)]
    if swap_qkv:
        scratch += [pltpu.VMEM((slabs, PAIR, 3 * PAIR), F32)]
        scratch += [pltpu.VMEM((slabs, half, 3 * PAIR), BF16)] * 2
        scratch += [pltpu.SemaphoreType.DMA((2, slabs))]
    scratch += swap.scratch()
    return pl.pallas_call(
        kernel,
        grid=(slabs,),
        out_shape=out_shape,
        in_specs=in_specs,
        out_specs=out_specs,
        scratch_shapes=scratch,
        compiler_params=pltpu.CompilerParams(
            collective_id=identity, has_side_effects=True, vmem_limit_bytes=VMEM_BYTES
        ),
        name=f"attention_backward_{identity}",
    )(
        probs,
        divisor,
        mixed,
        query,
        key,
        value,
        grad_mixed,
        first,
        fixed,
        frames,
        *swap.operands(),
    )


def rows_backward(entry, upper, identity, span, swap):
    top, bottom = len(entry) == 1, upper is None
    if not top:
        above, entry = entry[0], entry[1:]
    total = entry[0].shape[1] if top else entry[0].shape[0]
    chunks = total // span
    columns = 256
    ahead = 0 if top else 2 if bottom else 1
    if top:
        width = 2 * entry[0].shape[2]
    else:
        features, width = entry[0].shape[1], entry[5].shape[1]
    if not bottom:
        layer = upper[0]
        hidden_units, mixed_features = upper[1].shape[1], upper[6].shape[1]
    place_rows = total // lax.axis_size("seq")

    def kernel(*refs):
        refs = list(refs)

        def take(count):
            taken = refs[:count]
            del refs[:count]
            return taken

        if top:
            (d_out_ref,) = take(1)
        else:
            dq_ref, dk_ref, dv_ref, unit1, scale1, dm_ref, wq, gain1 = take(8)
        if not bottom:
            act_ref, gp_ref, unit2, scale2, second_ref, mixed_ref = take(6)
            wo_any, wu_any, wd_any, gain2 = take(4)
        sources = take(swap.count)
        if not top:
            (vec1,) = take(1)
        if not bottom:
            dmid_out, dmix_out, out_sum, up_sum, down_sum, vec2 = take(6)
        else:
            dx_out, dx_other, vec_other = take(3)
        targets = take(swap.count)
        if not top:
            a_send, a_recv = take(2)
        if not bottom:
            b_send, b_recv, grad_keep, hidden_keep, low_keep, last_keep, wo, wu, wd, w_sem = take(10)
        else:
            dx_keep, dx_send, dx_recv, vec_recv, x_send_sem, x_recv_sem = take(6)
        send_sem, recv_sem = take(2)
        start_swap, finish_swap = swap.bind(sources, targets, refs)

        step = pl.program_id(0)
        me, core = lax.axis_index("seq"), lax.axis_index("tp")
        pair = at((me // 2) * PAIR, PAIR)
        x = lax.rem(me, 2)
        beside = me + 1 - 2 * x

        def exchange(kind, chunk):
            source, target = (a_send, a_recv) if kind == 0 else (b_send, b_recv)
            return remote(
                source.at[chunk],
                target.at[chunk],
                send_sem.at[kind, chunk],
                recv_sem.at[kind, chunk],
                me,
                1 - core,
            )

        def load(index):
            source, target = ((wd_any, wd), (wu_any, wu), (wo_any, wo))[index]
            return pltpu.make_async_copy(source.at[layer], target, w_sem.at[index])

        partners = [(me, 1 - core)] + ([(beside, core)] if bottom or swap.count else [])

        @pl.when(step == 0)
        def _():
            if not bottom:
                for index in range(3):
                    load(index).start()
                out_sum[...] = jnp.zeros_like(out_sum)
                up_sum[...] = jnp.zeros_like(up_sum)
                down_sum[...] = jnp.zeros_like(down_sum)
                vec2[...] = jnp.zeros_like(vec2)
            if not top:
                vec1[...] = jnp.zeros_like(vec1)
            hello(partners)

        def meet():
            @pl.when(step == 0)
            def _():
                met(partners)
                start_swap()

        def entry_products():
            partial = None
            for part, ref in enumerate((dq_ref, dk_ref, dv_ref)):
                grad = ref[...]
                term = nt(grad, wq[0, part])
                partial = term if partial is None else partial + term
                vec1[part : part + 1, :] += column_sum(grad.astype(F32))
            a_send[step] = partial.astype(BF16)

        def entry_norm(chunk):
            if top:
                return halves(d_out_ref)
            grad_first = a_send[chunk].astype(F32) + a_recv[chunk].astype(F32)
            unit, scale = kept_norm(unit1, scale1)
            for start, sums in ((3, column_sum(grad_first * unit)), (5, column_sum(grad_first))):
                for side in range(width // features):
                    piece = slice(side * features, (side + 1) * features)
                    vec1[start + side : start + side + 1, :] += sums[:, piece]
            return dm_ref[...] + norm_pull(grad_first, gain1[above : above + 1, :], unit, scale)

        def feed_forward(between=None):
            chunk = step - ahead
            gradient = entry_norm(chunk)
            if bottom:
                dx_keep[at(chunk * span, span), :] = gradient
                return
            grad_keep[lax.rem(chunk, 2)] = gradient
            vec2[1:2, :width] += column_sum(gradient)
            low = gradient.astype(BF16)
            low_keep[...] = low
            low_columns = low_keep[:, pair]
            second = second_ref[...]
            parts = [slice(start, start + columns) for start in range(0, hidden_units, columns)]
            grad_act = nt(low, wd[parts[0], :])
            for index, part in enumerate(parts):
                following = nt(low, wd[parts[index + 1], :]) if index + 1 < len(parts) else None
                grad_hidden = grad_act * gp_ref[:, part].astype(F32)
                hidden_keep[:, part] = grad_hidden.astype(BF16)
                vec2[0:1, part] += column_sum(grad_hidden)
                grad_act = following
            if between is not None:
                between()
            b_send[chunk] = nt(hidden_keep[...], wu[...]).astype(BF16)
            down_sum[...] += tn(low_columns, act_ref[...])
            up_sum[...] += tn(second, hidden_keep[...])

        def close():
            chunk = step - ahead - 1
            grad_second = b_send[chunk].astype(F32) + b_recv[chunk].astype(F32)
            unit, scale = kept_norm(unit2, scale2)
            vec2[2:3, :width] += column_sum(grad_second * unit)
            vec2[3:4, :width] += column_sum(grad_second)
            grad_middle = grad_keep[lax.rem(chunk, 2)] + norm_pull(
                grad_second, gain2[layer : layer + 1, :], unit, scale
            )
            dmid_out[...] = grad_middle
            vec2[4:5, :width] += column_sum(grad_middle)
            low = grad_middle.astype(BF16)
            last_keep[...] = low
            out_sum[...] += tn(last_keep[:, pair], mixed_ref[...])
            dmix_out[...] = nt(low, wo[...]).astype(BF16)

        if not top:

            @pl.when(step < chunks)
            def _():
                entry_products()
                meet()
                exchange(0, step).start()

        @pl.when((step >= ahead) & (step < chunks + ahead))
        def _():
            if not top:
                exchange(0, step - ahead).wait_recv()
            if not bottom:

                @pl.when(step == ahead)
                def _():
                    load(0).wait()

            feed_forward(lambda: pl.when(step == ahead)(lambda: load(1).wait()))
            if not bottom:
                if top:
                    meet()
                exchange(1, step - ahead).start()

        if not bottom:

            @pl.when(step == ahead + 1)
            def _():
                load(2).wait()

            @pl.when(step >= ahead + 1)
            def _():
                exchange(1, step - ahead - 1).wait_recv()
                close()

        if bottom:

            def x_copy(index):
                source, target = ((dx_send, dx_recv), (vec1, vec_recv))[index]
                return remote(
                    source, target, x_send_sem.at[index], x_recv_sem.at[index], beside, core
                )

            @pl.when(step == chunks + 1)
            def _():
                dx_send[...] = dx_keep[at(beside * place_rows, place_rows), :].astype(BF16)
                x_copy(0).start()
                x_copy(1).start()
                dx_out[...] = dx_keep[at(me * place_rows, place_rows), :]
                x_copy(0).wait_recv()
                x_copy(1).wait_recv()
                dx_other[...] = dx_recv[...].astype(F32)
                vec_other[...] = vec_recv[...]
                x_copy(0).wait_send()
                x_copy(1).wait_send()

        @pl.when(step == pl.num_programs(0) - 1)
        def _():
            for kind in ([] if top else [0]) + ([] if bottom else [1]):
                for chunk in range(chunks):
                    exchange(kind, chunk).wait_send()
            finish_swap()

    def rows(columns, behind):
        return pl.BlockSpec(
            (span, columns), lambda s: (jnp.clip(s - behind, 0, chunks - 1), 0)
        )

    vec = jax.ShapeDtypeStruct((8, VEC), F32)
    operands, in_specs, out_shape, out_specs, scratch = [], [], [], [], []
    if top:
        operands += list(entry)
        in_specs += [halves_spec(entry[0].shape, chunks, 0, span)]
    else:
        operands += list(entry)
        in_specs += [rows(features, 0)] * 3
        in_specs += [rows(width, ahead), rows(PAIR, ahead), rows(width, ahead)]
        in_specs += [
            pl.BlockSpec(
                (1, *entry[6].shape[1:]),
                lambda s: (above, 0, 0, 0),
                pipeline_mode=pl.Buffered(1),
            ),
            whole(entry[7]),
        ]
        narrow = jax.ShapeDtypeStruct((8, features), F32)
        out_shape += [narrow]
        out_specs += [whole_out((8, features))]
        scratch += [pltpu.VMEM((chunks, span, width), BF16)] * 2
    if not bottom:
        operands += list(upper[1:])
        in_specs += [rows(hidden_units, ahead)] * 2
        in_specs += [rows(width, ahead + 1), rows(PAIR, ahead + 1), rows(PAIR, ahead)]
        in_specs += [rows(mixed_features, ahead + 1)] + [ANYWHERE] * 3 + [whole(upper[10])]
        sums = [mixed_features, hidden_units, hidden_units]
        out_shape += [
            jax.ShapeDtypeStruct((total, width), F32),
            jax.ShapeDtypeStruct((total, mixed_features), BF16),
        ]
        out_shape += [jax.ShapeDtypeStruct((PAIR, size), F32) for size in sums] + [vec]
        out_specs += [rows(width, ahead + 1), rows(mixed_features, ahead + 1)]
        out_specs += [whole_out((PAIR, size)) for size in sums] + [whole_out((8, VEC))]
        scratch += [pltpu.VMEM((chunks, span, width), BF16)] * 2
        scratch += [
            pltpu.VMEM((2, span, width), F32),
            pltpu.VMEM((span, hidden_units), BF16),
            pltpu.VMEM((span, width), BF16),
            pltpu.VMEM((span, width), BF16),
            pltpu.VMEM(upper[7].shape[1:], BF16),
            pltpu.VMEM(upper[8].shape[1:], BF16),
            pltpu.VMEM(upper[9].shape[1:], BF16),
            pltpu.SemaphoreType.DMA((3,)),
        ]
    else:
        out_shape += [
            jax.ShapeDtypeStruct((place_rows, width), F32),
            jax.ShapeDtypeStruct((place_rows, width), F32),
            narrow,
        ]
        out_specs += [whole_out((place_rows, width))] * 2 + [whole_out((8, features))]
        scratch += [
            pltpu.VMEM((total, width), F32),
            pltpu.VMEM((place_rows, width), BF16),
            pltpu.VMEM((place_rows, width), BF16),
            pltpu.VMEM((8, features), F32),
            pltpu.SemaphoreType.DMA((2,)),
            pltpu.SemaphoreType.DMA((2,)),
        ]
    scratch += [pltpu.SemaphoreType.DMA((2, chunks))] * 2
    operands += swap.operands()
    in_specs += swap.in_specs()
    shapes, specs = swap.outputs()
    out_shape += shapes
    out_specs += specs
    scratch += swap.scratch()
    return pl.pallas_call(
        kernel,
        grid=(chunks + (1 if top else 2),),
        out_shape=out_shape,
        in_specs=in_specs,
        out_specs=out_specs,
        scratch_shapes=scratch,
        compiler_params=pltpu.CompilerParams(
            collective_id=identity, has_side_effects=True, vmem_limit_bytes=VMEM_BYTES
        ),
        name=f"rows_backward_{identity}",
    )(*operands)


def assemble(sums, vecs, lanes, n, features, hidden_units):
    place = lanes[1].shape[0]
    width = lanes[1].shape[1]
    half = PAIR // 2

    def kernel(*refs):
        refs = list(refs)

        def take(count):
            taken = refs[:count]
            del refs[:count]
            return taken

        qkvs, outs, ups, downs = take(LAYERS), take(LAYERS), take(LAYERS), take(LAYERS)
        vec_refs = [take(4) for _ in range(LAYERS)]
        out_lane, out_other, dx_own, dx_other = take(4)
        out_ref, dx_ref, gain1, shift1, g_qkv, b_qkv, g_out, b_out = take(8)
        gain2, shift2, g_up, b_up, g_down, b_down = take(6)
        out_own, sem = refs
        me = lax.axis_index("seq")
        x = lax.rem(me, 2)
        fetch = pltpu.make_async_copy(out_lane.at[at(me * place, place), :], out_own, sem)
        fetch.start()

        for layer in range(LAYERS):
            for part in range(3):
                g_qkv[layer, part] = qkvs[layer][:, part * features : (part + 1) * features]
            for ref, target in ((outs, g_out), (ups, g_up), (downs, g_down)):
                target[layer] = ref[layer][...]

        for layer, (entry_own, entry_other, upper_own, upper_other) in enumerate(vec_refs):
            line = slice(layer, layer + 1)
            for part in range(3):
                row = slice(part, part + 1)
                b_qkv[part, line, :] = entry_own[row, :] + entry_other[row, :]
            b_up[line, :] = upper_own[0:1, :hidden_units] + upper_other[0:1, :hidden_units]

            def owned(mine, other, row):
                wide = mine.shape[1]
                place = (me // 2) * PAIR
                pair = at(lax.rem(place, wide), PAIR)
                both = mine[row : row + 1, pair] + other[row : row + 1, pair]
                for later in range(1, width // wide):
                    line = slice(row + later, row + later + 1)
                    both = jnp.where(place // wide == later, mine[line, pair] + other[line, pair], both)
                return jnp.where(x == 0, both[:, :half], both[:, half:])

            gain1[line, :] = owned(entry_own, entry_other, 3)
            shift1[line, :] = owned(entry_own, entry_other, 5)
            b_down[line, :] = owned(upper_own, upper_other, 1)
            gain2[line, :] = owned(upper_own, upper_other, 2)
            shift2[line, :] = owned(upper_own, upper_other, 3)
            b_out[line, :] = owned(upper_own, upper_other, 4)

        def both_lanes(target, mine, other):
            target[:, 0, :] = jnp.where(x == 0, mine, other)
            target[:, 1, :] = jnp.where(x == 0, other, mine)

        both_lanes(dx_ref, dx_own[...], dx_other[...])
        fetch.wait()
        both_lanes(out_ref, out_own[...], out_other[...])

    def f32(*shape):
        return jax.ShapeDtypeStruct(shape, F32)

    in_vmem = pl.BlockSpec(memory_space=pltpu.VMEM)
    flat = []
    for kind in range(4):
        flat += [sums[layer][kind] for layer in range(LAYERS)]
    for layer in range(LAYERS):
        flat += list(vecs[layer])
    flat += list(lanes)
    small = f32(LAYERS, width // n)
    return pl.pallas_call(
        kernel,
        out_shape=(
            f32(place, 2, width),
            f32(place, 2, width),
            small,
            small,
            f32(LAYERS, 3, half, features),
            f32(3, LAYERS, features),
            f32(LAYERS, half, features),
            small,
            small,
            small,
            f32(LAYERS, half, hidden_units),
            f32(LAYERS, hidden_units),
            f32(LAYERS, half, hidden_units),
            small,
        ),
        in_specs=[in_vmem] * (len(flat) - 4) + [ANYWHERE] + [in_vmem] * 3,
        out_specs=(in_vmem,) * 14,
        scratch_shapes=[pltpu.VMEM((place, width), F32), pltpu.SemaphoreType.DMA],
        compiler_params=pltpu.CompilerParams(vmem_limit_bytes=VMEM_BYTES),
        name="assemble",
    )(*flat)


def per_chip(
    tokens,
    d_out,
    norm1_gain,
    norm1_shift,
    w_qkv,
    b_qkv,
    w_out,
    b_out,
    norm2_gain,
    norm2_shift,
    w_up,
    b_up,
    w_down,
    b_down,
    episode_frames,
    live,
):
    n = lax.axis_size("seq")
    rows = tokens.shape[0]
    features = w_qkv.shape[3]
    fixed, ahead = turn_constants(rows * n // FRAME)
    qkv, qkv_bias = w_qkv.transpose(0, 2, 1, 3), b_qkv.transpose(1, 0, 2)

    gathered, key_bias, frames, *projected = gather_and_project(
        tokens, live.T, episode_frames, norm1_gain, norm1_shift, qkv, qkv_bias, fixed, ahead, n
    )
    streams, kept, d_part = [gathered], [], None
    for layer in range(LAYERS):
        following = None
        if layer + 1 < LAYERS:
            following = (qkv, norm1_gain, norm1_shift, qkv_bias, fixed, frames)
        probs, divisor, mixed, d_part = attention_forward(
            *projected[:3],
            key_bias,
            d_out if layer == 0 else None,
            d_part,
            n,
            1 + 2 * layer,
        )
        results = layer_forward(
            layer,
            mixed,
            streams[layer],
            (w_out, w_up, w_down),
            (b_out, norm2_gain, norm2_shift, b_up, b_down),
            following,
            2 + 2 * layer,
        )
        kept.append((*projected, probs, divisor, mixed, *results[:5]))
        streams.append(results[5])
        projected = results[6:]
    d_lane = d_part

    sums = [[None] * 4 for _ in range(LAYERS)]
    vecs = [[None] * 4 for _ in range(LAYERS)]
    entry, later = (d_lane,), None
    for layer in reversed(range(LAYERS)):
        query, key, value, first, unit1, scale1, probs, divisor, mixed = kept[layer][:9]
        unit2, scale2, second, act, slope = kept[layer][9:]
        upper = (
            layer,
            act,
            slope,
            unit2,
            scale2,
            second,
            mixed,
            w_out,
            w_up,
            w_down,
            norm2_gain,
        )
        identity = 1 + 2 * LAYERS + 2 * (LAYERS - 1 - layer)
        if later is None:
            results = rows_backward(entry, upper, identity, FRAME, Swap([], []))
        else:
            swap = Swap(later[:2], [(later[2], 0), (streams[LAYERS], rows)])
            vec1, *results = rows_backward(entry, upper, identity, FRAME, swap)
            results, swapped = results[:6], results[6:]
            sums[layer + 1][3], sums[layer + 1][0] = swapped[:2]
            vecs[layer + 1][3], out_other = swapped[2:]
            vecs[layer + 1][0] = vec1
        grad_middle, grad_mixed, out_sum, up_sum, down_sum, vec2 = results
        vecs[layer][2] = vec2
        last = layer == 0
        if last:
            swap = Swap([out_sum, up_sum], [(vec2, 0), (vecs[layer + 1][0], 0)])
        else:
            swap = Swap([out_sum, up_sum], [])
        results = attention_backward(
            probs,
            divisor,
            mixed,
            query,
            key,
            value,
            grad_mixed,
            first,
            fixed,
            frames,
            swap,
            last,
            identity + 1,
        )
        grad_query, grad_key, grad_value, qkv_sum = results[:4]
        if last:
            sums[layer][:3] = [qkv_sum, *results[4:6]]
            vecs[layer][3], vecs[layer + 1][1] = results[6:8]
        else:
            sums[layer][1:3] = results[4:6]
            later = [down_sum, qkv_sum, vec2]
        entry = (
            layer,
            grad_query,
            grad_key,
            grad_value,
            unit1,
            scale1,
            grad_middle,
            qkv,
            norm1_gain,
        )
    vec1, dx_own, dx_other, vec_other, sums[0][3] = rows_backward(
        entry, None, 1 + 4 * LAYERS, FRAME, Swap([down_sum], [])
    )
    vecs[0][:2] = [vec1, vec_other]
    results = list(
        assemble(
            sums,
            vecs,
            (streams[LAYERS], out_other, dx_own, dx_other),
            n,
            features,
            w_up.shape[2],
        )
    )
    results[4] = results[4].transpose(0, 2, 1, 3)
    results[5] = results[5].transpose(1, 0, 2)
    results[6] = results[6].transpose(0, 2, 1)
    results[12] = results[12].transpose(0, 2, 1)
    return tuple(results)


def lane_fits(mesh, tokens):
    n = mesh.shape["seq"]
    positions, lanes, width = tokens.shape
    rows = positions // n
    return (
        lanes == 2
        and n % 4 == 0
        and positions <= 4 * FRAME
        and positions % FRAME == 0
        and FRAME % rows == 0
        and width // n * 2 == PAIR
        and mesh.shape["tp"] == 2
    )


def solution(mesh):
    placed = (
        P("seq", None, None),
        P("seq", None, None),
        P(),
        P(),
        P(None, None, None, "tp"),
        P(None, None, "tp"),
        P(None, "tp", None),
        P(),
        P(),
        P(),
        P(None, None, "tp"),
        P(None, "tp"),
        P(None, "tp", None),
        P(),
        P(),
        P("seq", None),
    )
    def mapped(body):
        return jax.shard_map(
            body,
            mesh=mesh,
            in_specs=placed,
            out_specs=(
                P("seq", None, None),
                P("seq", None, None),
                P(None, "seq"),
                P(None, "seq"),
                P(None, "seq", None, "tp"),
                P(None, None, "tp"),
                P(None, "tp", "seq"),
                P(None, "seq"),
                P(None, "seq"),
                P(None, "seq"),
                P(None, "seq", "tp"),
                P(None, "tp"),
                P(None, "tp", "seq"),
                P(None, "seq"),
            ),
            check_vma=False,
        )

    def run(tokens, *others):
        if lane_fits(mesh, tokens):
            return mapped(per_chip)(tokens, *others)
        return mapped(per_device)(tokens, *others)

    return run
```

```python
import math

import jax
import jax.numpy as jnp
import numpy as np
from jax import lax
from jax.experimental import pallas as pl
from jax.experimental.pallas import tpu as pltpu
from jax.sharding import PartitionSpec as P

HEAD_DIM = 64
GRID = 16
FRAME = 256
LAYERS = 2
MICRO = 2


EPSILON = 1e-06
MASKED = -1e30
SCORE_SCALE = 0.125


def layer_norm(stream, norm_gain, norm_shift):
    center = stream - jnp.mean(stream, axis=-1, keepdims=True)
    spread = jnp.mean(center * center, axis=-1, keepdims=True)
    return center * lax.rsqrt(spread + EPSILON) * norm_gain + norm_shift


def rotate(values, frame_place, row_place, column_place):
    frequency = jnp.exp(jnp.arange(10, dtype=jnp.float32) * (-math.log(10000.0) / 10.0))
    pieces = []
    for section, place in enumerate((frame_place, row_place, column_place)):
        lower = values[..., 20 * section : 20 * section + 10]
        upper = values[..., 20 * section + 10 : 20 * section + 20]
        angles = place.astype(jnp.float32)[..., None, None] * frequency
        cosine = jnp.cos(angles)
        sine_part = jnp.sin(angles)
        pieces.append(lower * cosine - upper * sine_part)
        pieces.append(lower * sine_part + upper * cosine)
    pieces.append(values[..., 60:])
    return jnp.concatenate(pieces, axis=-1)


def episode_tags(frame_counts, positions):
    endings = jnp.cumsum(frame_counts) * FRAME
    passed = (positions[:, None] >= endings[None, :]).astype(jnp.int32)
    episode = jnp.sum(passed, axis=1)
    opening = jnp.sum(passed * frame_counts[None, :], axis=1)
    frame_index = positions // FRAME - opening
    within = positions % FRAME
    return (episode, frame_index, within // GRID, within % GRID)


def gelu_exact(values):
    return jax.nn.gelu(values, approximate=False)


def sum_heads(partial_sum):
    return lax.psum(partial_sum.astype(jnp.bfloat16), "tp").astype(jnp.float32)


def sum_inputs(partial_sum):
    return lax.psum(partial_sum.astype(jnp.bfloat16), "tp").astype(jnp.float32)


def lane_scores(query, keys_all, lane_index, query_tags, key_tags):
    head_count = query.shape[2] // HEAD_DIM
    query_lane = lax.dynamic_index_in_dim(query, lane_index, 1, False).reshape(
        query.shape[0], head_count, HEAD_DIM
    )
    keys_lane = lax.dynamic_index_in_dim(keys_all, lane_index, 1, False).reshape(
        keys_all.shape[0], head_count, HEAD_DIM
    )
    query_episode, query_frame = [
        lax.dynamic_index_in_dim(item, lane_index, 1, False) for item in query_tags
    ]
    key_episode, key_frame, key_live = [
        lax.dynamic_index_in_dim(item, lane_index, 1, False) for item in key_tags
    ]
    allowed = (
        (query_episode[:, None] == key_episode[None, :])
        & (key_frame[None, :] <= query_frame[:, None])
        & (key_live[None, :] > 0)
    )
    scores = (
        jnp.einsum("qhd,khd->hqk", query_lane, keys_lane, preferred_element_type=jnp.float32)
        * SCORE_SCALE
    )
    return (jnp.where(allowed[None], scores, MASKED), query_lane, keys_lane)


def attend_forward(query, keys_all, values_all, query_tags, key_tags):
    rows_dev, lane_count, features = query.shape
    head_count = features // HEAD_DIM

    def one_lane(lane_index, carry):
        scores, query_lane, keys_lane = lane_scores(
            query, keys_all, lane_index, query_tags, key_tags
        )
        highest = jnp.max(scores, axis=-1, keepdims=True)
        shifted = jnp.exp(scores - highest)
        summed = jnp.sum(shifted, axis=-1, keepdims=True)
        attention = (shifted / summed).astype(jnp.bfloat16)
        values_lane = lax.dynamic_index_in_dim(values_all, lane_index, 1, False).reshape(
            values_all.shape[0], head_count, HEAD_DIM
        )
        result = jnp.einsum(
            "hqk,khd->qhd", attention, values_lane, preferred_element_type=jnp.float32
        ).reshape(rows_dev, 1, features)
        log_total = (highest + jnp.log(summed))[None, :, :, 0]
        return (result, log_total)

    initial = (
        jnp.zeros((rows_dev, lane_count, features), jnp.float32),
        jnp.zeros((lane_count, head_count, rows_dev), jnp.float32),
    )
    return lax.fori_loop(0, lane_count, one_lane, initial)


def attend_backward(query, keys_all, values_all, log_total, grad_mixed, query_tags, key_tags):
    rows_dev, lane_count, features = query.shape
    head_count = features // HEAD_DIM
    key_rows = keys_all.shape[0]

    def one_lane(lane_index, carry):
        scores, query_lane, keys_lane = lane_scores(
            query, keys_all, lane_index, query_tags, key_tags
        )
        values_lane = lax.dynamic_index_in_dim(values_all, lane_index, 1, False).reshape(
            key_rows, head_count, HEAD_DIM
        )
        grad_lane = lax.dynamic_index_in_dim(grad_mixed, lane_index, 1, False).reshape(
            rows_dev, head_count, HEAD_DIM
        )
        attention = jnp.exp(
            scores - lax.dynamic_index_in_dim(log_total, lane_index, 0, False)[:, :, None]
        )
        grad_attention = jnp.einsum(
            "qhd,khd->hqk", grad_lane, values_lane, preferred_element_type=jnp.float32
        )
        inner = jnp.sum(attention * grad_attention, axis=-1, keepdims=True)
        grad_scores = (attention * (grad_attention - inner)).astype(jnp.bfloat16)
        query_part = (
            jnp.einsum("hqk,khd->qhd", grad_scores, keys_lane, preferred_element_type=jnp.float32)
            * SCORE_SCALE
        )
        key_part = (
            jnp.einsum("hqk,qhd->khd", grad_scores, query_lane, preferred_element_type=jnp.float32)
            * SCORE_SCALE
        )
        value_part = jnp.einsum(
            "hqk,qhd->khd",
            attention.astype(jnp.bfloat16),
            grad_lane,
            preferred_element_type=jnp.float32,
        )
        stacked = jnp.stack(
            [key_part.reshape(key_rows, features), value_part.reshape(key_rows, features)], axis=1
        )
        key_terms = stacked[:, None]
        grad_query = query_part.reshape(rows_dev, 1, features)
        return (grad_query, key_terms)

    initial = (
        jnp.zeros((rows_dev, lane_count, features), jnp.float32),
        jnp.zeros((key_rows, lane_count, 2, features), jnp.float32),
    )
    return lax.fori_loop(0, lane_count, one_lane, initial)


def front(stream, layer_index, params, query_tags, key_tags, positions):
    (
        gain_one,
        shift_one,
        mat_qkv,
        bias_qkv,
        mat_out,
        bias_out,
        gain_two,
        shift_two,
        mat_up,
        bias_up,
        mat_down,
        bias_down,
    ) = [item[layer_index] for item in params]
    rows_dev, lane_count, width = stream.shape
    features = mat_qkv.shape[2]
    head_count = features // HEAD_DIM
    frame_place, row_place, column_place = positions
    first = layer_norm(stream, gain_one, shift_one).astype(jnp.bfloat16)
    projected = (
        jnp.einsum("tbd,dcf->tbcf", first, mat_qkv, preferred_element_type=jnp.float32) + bias_qkv
    )
    split = projected.reshape(rows_dev, lane_count, 3, head_count, HEAD_DIM)
    query = (
        rotate(split[:, :, 0], frame_place, row_place, column_place)
        .reshape(rows_dev, lane_count, features)
        .astype(jnp.bfloat16)
    )
    keys = (
        rotate(split[:, :, 1], frame_place, row_place, column_place)
        .reshape(rows_dev, lane_count, features)
        .astype(jnp.bfloat16)
    )
    values = projected[:, :, 2].astype(jnp.bfloat16)
    keys_all, values_all = (
        lax.all_gather(keys, "seq", axis=0, tiled=True),
        lax.all_gather(values, "seq", axis=0, tiled=True),
    )
    mixed_full, log_total = attend_forward(query, keys_all, values_all, query_tags, key_tags)
    mixed = mixed_full.astype(jnp.bfloat16)
    middle = (
        stream
        + sum_heads(jnp.einsum("tbf,fd->tbd", mixed, mat_out, preferred_element_type=jnp.float32))
        + bias_out
    )
    second = layer_norm(middle, gain_two, shift_two).astype(jnp.bfloat16)
    hidden = jnp.einsum("tbd,df->tbf", second, mat_up, preferred_element_type=jnp.float32) + bias_up
    activation = gelu_exact(hidden).astype(jnp.bfloat16)
    return (
        first,
        query,
        keys_all,
        values_all,
        log_total,
        mixed,
        middle,
        second,
        hidden,
        activation,
        mixed_full,
    )


def layer_backward(stream, gradient, layer_index, params, query_tags, key_tags, positions):
    (
        gain_one,
        shift_one,
        mat_qkv,
        bias_qkv,
        mat_out,
        bias_out,
        gain_two,
        shift_two,
        mat_up,
        bias_up,
        mat_down,
        bias_down,
    ) = [item[layer_index] for item in params]
    (
        first,
        query,
        keys_all,
        values_all,
        log_total,
        mixed,
        middle,
        second,
        hidden,
        activation,
        mixed_full,
    ) = front(stream, layer_index, params, query_tags, key_tags, positions)
    frame_place, row_place, column_place = positions
    rows_dev, lane_count, width = stream.shape
    features = query.shape[2]
    head_count = features // HEAD_DIM
    grad_low = gradient.astype(jnp.bfloat16)
    grad_w_down = jnp.einsum(
        "tbf,tbd->fd", activation, grad_low, preferred_element_type=jnp.float32
    )
    grad_b_down = jnp.sum(gradient, axis=(0, 1))
    grad_activation = jnp.einsum(
        "tbd,fd->tbf", grad_low, mat_down, preferred_element_type=jnp.float32
    )
    grad_hidden = jax.vjp(gelu_exact, hidden)[1](grad_activation)[0].astype(jnp.bfloat16)
    grad_b_up = jnp.sum(grad_hidden.astype(jnp.float32), axis=(0, 1))
    grad_w_up = jnp.einsum("tbd,tbf->df", second, grad_hidden, preferred_element_type=jnp.float32)
    grad_second = sum_inputs(
        jnp.einsum("tbf,df->tbd", grad_hidden, mat_up, preferred_element_type=jnp.float32)
    )
    middle_pull = jax.vjp(layer_norm, middle, gain_two, shift_two)[1]
    grad_inner, grad_gain_two, grad_shift_two = middle_pull(grad_second)
    grad_middle = gradient + grad_inner
    grad_b_out = jnp.sum(grad_middle, axis=(0, 1))
    middle_low = grad_middle.astype(jnp.bfloat16)
    grad_w_out = jnp.einsum("tbf,tbd->fd", mixed, middle_low, preferred_element_type=jnp.float32)
    grad_mixed = jnp.einsum(
        "tbd,fd->tbf", middle_low, mat_out, preferred_element_type=jnp.float32
    ).astype(jnp.bfloat16)
    grad_query, key_terms = attend_backward(
        query, keys_all, values_all, log_total, grad_mixed, query_tags, key_tags
    )
    returned = lax.psum_scatter(key_terms, "seq", scatter_dimension=0, tiled=True)
    turned_query = rotate(
        grad_query.reshape(rows_dev, lane_count, head_count, HEAD_DIM),
        -frame_place,
        -row_place,
        -column_place,
    )
    turned_keys = rotate(
        returned[:, :, 0].reshape(rows_dev, lane_count, head_count, HEAD_DIM),
        -frame_place,
        -row_place,
        -column_place,
    )
    grad_projected = jnp.stack(
        [
            turned_query.reshape(rows_dev, lane_count, features),
            turned_keys.reshape(rows_dev, lane_count, features),
            returned[:, :, 1],
        ],
        axis=2,
    ).astype(jnp.bfloat16)
    grad_b_qkv = jnp.sum(grad_projected.astype(jnp.float32), axis=(0, 1))
    grad_w_qkv = jnp.einsum(
        "tbd,tbcf->dcf", first, grad_projected, preferred_element_type=jnp.float32
    )
    grad_first = sum_inputs(
        jnp.einsum("tbcf,dcf->tbd", grad_projected, mat_qkv, preferred_element_type=jnp.float32)
    )
    first_pull = jax.vjp(layer_norm, stream, gain_one, shift_one)[1]
    grad_entry, grad_gain_one, grad_shift_one = first_pull(grad_first)
    grads = (
        grad_gain_one,
        grad_shift_one,
        grad_w_qkv,
        grad_b_qkv,
        grad_w_out,
        grad_b_out,
        grad_gain_two,
        grad_shift_two,
        grad_w_up,
        grad_b_up,
        grad_w_down,
        grad_b_down,
    )
    return (grad_middle + grad_entry, grads)


def per_device(
    tokens,
    d_out,
    norm1_gain,
    norm1_shift,
    w_qkv,
    b_qkv,
    w_out,
    b_out,
    norm2_gain,
    norm2_shift,
    w_up,
    b_up,
    w_down,
    b_down,
    episode_frames,
    live,
):
    rows_dev = tokens.shape[0]
    lane_count = tokens.shape[1] // MICRO
    total_rows = rows_dev * lax.axis_size("seq")
    local_positions = lax.axis_index("seq") * rows_dev + jnp.arange(rows_dev, dtype=jnp.int32)
    key_positions = jnp.arange(total_rows, dtype=jnp.int32)
    tagger = jax.vmap(episode_tags, in_axes=(0, None), out_axes=1)
    query_episode, query_frame, query_row, query_column = tagger(episode_frames, local_positions)
    key_episode, key_frame, key_row, key_column = tagger(episode_frames, key_positions)
    live_keys = lax.all_gather(live, "seq", axis=0, tiled=True)
    params = (
        norm1_gain,
        norm1_shift,
        w_qkv,
        b_qkv,
        w_out,
        b_out,
        norm2_gain,
        norm2_shift,
        w_up,
        b_up,
        w_down,
        b_down,
    )
    layer_grads = [None] * LAYERS
    outputs = []
    grad_tokens = []
    for micro_index in range(MICRO):
        first_lane = micro_index * lane_count
        last_lane = first_lane + lane_count
        query_tags = (query_episode[:, first_lane:last_lane], query_frame[:, first_lane:last_lane])
        key_tags = (
            key_episode[:, first_lane:last_lane],
            key_frame[:, first_lane:last_lane],
            live_keys[:, first_lane:last_lane],
        )
        positions = (
            query_frame[:, first_lane:last_lane],
            query_row[:, first_lane:last_lane],
            query_column[:, first_lane:last_lane],
        )
        stream = tokens[:, first_lane:last_lane].astype(jnp.float32)
        inputs = []
        gathered = []
        for layer_index in range(LAYERS):
            inputs.append(stream)
            layer_state = front(stream, layer_index, params, query_tags, key_tags, positions)
            gathered.append((layer_state[2], layer_state[3]))
            branch = jnp.einsum(
                "tbf,fd->tbd",
                layer_state[9],
                w_down[layer_index],
                preferred_element_type=jnp.float32,
            )
            stream = layer_state[6] + sum_heads(branch) + b_down[layer_index]
        outputs.append(stream)
        gradient = d_out[:, first_lane:last_lane]
        for layer_index in reversed(range(LAYERS)):
            gradient, grads = layer_backward(
                inputs[layer_index], gradient, layer_index, params, query_tags, key_tags, positions
            )
            if layer_grads[layer_index] is None:
                layer_grads[layer_index] = grads
            else:
                layer_grads[layer_index] = jax.tree.map(jnp.add, layer_grads[layer_index], grads)
        grad_tokens.append(gradient)
    stacked = [
        jnp.stack([layer_grads[layer_index][entry] for layer_index in range(LAYERS)])
        for entry in range(12)
    ]
    (
        grad_gain_one,
        grad_shift_one,
        grad_w_qkv,
        grad_b_qkv,
        grad_w_out,
        grad_b_out,
        grad_gain_two,
        grad_shift_two,
        grad_w_up,
        grad_b_up,
        grad_w_down,
        grad_b_down,
    ) = stacked
    in_sums = (
        lax.psum_scatter(grad_w_qkv, "seq", scatter_dimension=1, tiled=True),
        lax.psum_scatter(grad_w_up, "seq", scatter_dimension=1, tiled=True),
        lax.psum_scatter(grad_gain_one, "seq", scatter_dimension=1, tiled=True),
        lax.psum_scatter(grad_shift_one, "seq", scatter_dimension=1, tiled=True),
        lax.psum_scatter(grad_gain_two, "seq", scatter_dimension=1, tiled=True),
        lax.psum_scatter(grad_shift_two, "seq", scatter_dimension=1, tiled=True),
        lax.psum_scatter(grad_b_out, "seq", scatter_dimension=1, tiled=True),
        lax.psum_scatter(grad_b_down, "seq", scatter_dimension=1, tiled=True),
    )
    out_sums = (
        lax.psum_scatter(grad_w_out, "seq", scatter_dimension=2, tiled=True),
        lax.psum_scatter(grad_w_down, "seq", scatter_dimension=2, tiled=True),
    )
    bias_total = lax.psum((grad_b_qkv, grad_b_up), "seq")
    return (
        jnp.concatenate(outputs, axis=1),
        jnp.concatenate(grad_tokens, axis=1),
        in_sums[2],
        in_sums[3],
        in_sums[0],
        bias_total[0],
        out_sums[0],
        in_sums[6],
        in_sums[4],
        in_sums[5],
        in_sums[1],
        bias_total[1],
        out_sums[1],
        in_sums[7],
    )


MESH = pl.DeviceIdType.MESH
BF16 = jnp.bfloat16
F32 = jnp.float32
VMEM_BYTES = 60 * 1024 * 1024
PAIR = 128
VEC = 2048


def nn(left, right):
    return lax.dot_general(left, right, (((1,), (0,)), ((), ())), preferred_element_type=F32)


def nt(left, right):
    return lax.dot_general(left, right, (((1,), (1,)), ((), ())), preferred_element_type=F32)


def tn(left, right):
    return lax.dot_general(left, right, (((0,), (0,)), ((), ())), preferred_element_type=F32)


def at(start, size):
    return pl.ds(pl.multiple_of(start, size), size)


def remote(src, dst, send, recv, seq, tp):
    return pltpu.make_async_remote_copy(
        src_ref=src,
        dst_ref=dst,
        send_sem=send,
        recv_sem=recv,
        device_id=(seq, tp),
        device_id_type=MESH,
    )


def hello(partners):
    barrier = pltpu.get_barrier_semaphore()
    for seq, tp in partners:
        pl.semaphore_signal(barrier, inc=1, device_id=(seq, tp), device_id_type=MESH)


def met(partners):
    pl.semaphore_wait(pltpu.get_barrier_semaphore(), len(partners))


def whole(array):
    zeros = (0,) * array.ndim
    return pl.BlockSpec(array.shape, lambda s: zeros, pipeline_mode=pl.Buffered(1))


def whole_out(shape):
    zeros = (0,) * len(shape)
    return pl.BlockSpec(shape, lambda s: zeros)


ANYWHERE = pl.BlockSpec(memory_space=pl.ANY)


def turn_row(table, place, section):
    frequency = np.exp(np.arange(10, dtype=np.float32) * np.float32(-math.log(10000.0) / 10.0))
    angle = place.astype(np.float32)[:, None] * frequency
    for base in range(20 * section, PAIR, HEAD_DIM):
        table[0, :, base : base + 10] = np.cos(angle)
        table[0, :, base + 10 : base + 20] = np.cos(angle)
        table[1, :, base : base + 10] = -np.sin(angle)
        table[2, :, base + 10 : base + 20] = np.sin(angle)


def turn_constants(frames):
    within, ahead = np.zeros((3, FRAME, PAIR), np.float32), np.zeros((3, frames, PAIR), np.float32)
    turn_row(within, np.arange(FRAME) // GRID, 1)
    turn_row(within, np.arange(FRAME) % GRID, 2)
    for base in range(60, PAIR, HEAD_DIM):
        within[0, :, base : base + 4] = 1.0
    turn_row(ahead, np.arange(frames), 0)
    return jnp.asarray(within), jnp.asarray(ahead)


def turn(values, tables, back=False):
    cosine, lower, upper = tables
    pieces = []
    for start in range(0, values.shape[1], PAIR):
        slab = values[:, start : start + PAIR]
        moved = pltpu.roll(slab, PAIR - 10, 1) * lower + pltpu.roll(slab, 10, 1) * upper
        pieces.append(slab * cosine - moved if back else slab * cosine + moved)
    return jnp.concatenate(pieces, axis=1)


def tables_of(fixed_ref, frames_ref, chunk):
    return [fixed_ref[i] + frames_ref[i, pl.ds(chunk, 1), :] for i in range(3)]


def normed(stream):
    center = stream - jnp.mean(stream, axis=-1, keepdims=True)
    spread = jnp.mean(center * center, axis=-1, keepdims=True)
    scale = lax.rsqrt(spread + EPSILON)
    return center * scale, scale


def norm_pull(grad, gain, unit, scale):
    scaled = grad * gain
    return scale * (
        scaled
        - jnp.mean(scaled, axis=-1, keepdims=True)
        - unit * jnp.mean(scaled * unit, axis=-1, keepdims=True)
    )


def keep_norm(unit, scale, unit_ref, scale_ref):
    unit_ref[...] = unit.astype(BF16)
    scale_ref[...] = jnp.broadcast_to(scale, scale_ref.shape)


def kept_norm(unit_ref, scale_ref):
    copies = unit_ref.shape[1] // scale_ref.shape[1]
    return unit_ref[...].astype(F32), jnp.concatenate([scale_ref[...]] * copies, axis=1)


def column_sum(values):
    return jnp.sum(values, axis=0, keepdims=True)


def gelu_both(hidden):
    normal = 0.5 + 0.5 * lax.erf(hidden * math.sqrt(0.5))
    density = jnp.exp(hidden * hidden * -0.5) * (1.0 / math.sqrt(2.0 * math.pi))
    return hidden * normal, normal + hidden * density


def project(stream, chunk, layer, pair, refs, outs, first_full):
    gain, shift, weight, bias, fixed, frames = refs
    query_ref, key_ref, value_ref, first_ref, unit_ref, scale_ref = outs
    unit, scale = normed(stream)
    keep_norm(unit, scale, unit_ref, scale_ref)
    first = (unit * gain[layer : layer + 1, :] + shift[layer : layer + 1, :]).astype(BF16)
    first_full[...] = first
    first_ref[...] = first_full[:, at(pair * PAIR, PAIR)]
    tables = tables_of(fixed, frames, chunk)
    query = nn(first, weight[0]) + bias[0, layer : layer + 1, :]
    query_ref[...] = (turn(query, tables) * SCORE_SCALE).astype(BF16)
    key = nn(first, weight[1]) + bias[1, layer : layer + 1, :]
    key_ref[...] = turn(key, tables).astype(BF16)
    value = nn(first, weight[2]) + bias[2, layer : layer + 1, :]
    value_ref[...] = value.astype(BF16)


class Relay:
    sems = 6

    def __init__(self, n, rows, buffer, other, sems, lives=None, live_other=None):
        self.n, self.rows, self.buffer, self.other = n, rows, buffer, other
        self.lives, self.live_other = lives, live_other
        self.z_send, self.z_recv, self.y_send, self.y_recv, self.c_send, self.c_recv = sems
        self.planes = n // 4
        self.me, self.core = lax.axis_index("seq"), lax.axis_index("tp")
        me = self.me
        self.x, self.y, self.z = lax.rem(me, 2), lax.rem(me // 2, 2), me // 4
        self.across = me + 2 - 4 * self.y

    @staticmethod
    def scratch(n):
        dma, planes = pltpu.SemaphoreType.DMA, n // 4
        shapes = [(planes, 2, 2)] * 2 + [(planes, 2)] * 2 + [(2 * planes,)] * 2
        return [dma(shape) for shape in shapes]

    @property
    def events(self):
        return self.planes

    def plane(self, step):
        return lax.rem(self.z + step, self.planes)

    def place(self, plane, lane):
        return plane * 4 + self.y * 2 + lane

    def reached(self):
        return [(step, far) for step in range(self.planes) for far in (0, 1) if step or far]

    def hello(self):
        barrier = pltpu.get_barrier_semaphore()
        partners = [(self.across, self.core), (self.me, 1 - self.core)]
        for step, far in self.reached():
            lane = 1 - self.x if far else self.x
            partners.append((self.place(self.plane(step), lane), self.core))
        for seq, tp in partners:
            pl.semaphore_signal(barrier, inc=1, device_id=(seq, tp), device_id_type=MESH)

    def met(self):
        pl.semaphore_wait(pltpu.get_barrier_semaphore(), 2 + len(self.reached()))

    def rows_of(self, side, seq):
        return self.buffer.at[side, at(seq * self.rows, self.rows), :]

    def block(self, side, pair):
        return self.buffer.at[side, at(pair * 2 * self.rows, 2 * self.rows), :]

    def items(self, pair):
        found = [self.block(self.core, pair)]
        if self.lives is not None:
            found.append(self.lives.at[at(pair * 2, 2)])
        return found

    def each(self, copy, what):
        for index in range(1 if self.lives is None else 2):
            getattr(copy(index), what)()

    def z_copy(self, step, far):
        def copy(index):
            lane = 1 - self.x if far else self.x
            if index == 0:
                source = self.other.at[self.core] if far else self.rows_of(self.core, self.me)
                target = self.rows_of(self.core, self.me)
            else:
                source = self.live_other if far else self.lives.at[self.me]
                target = self.lives.at[self.me]
            return remote(
                source,
                target,
                self.z_send.at[step, far, index],
                self.z_recv.at[step, far, index],
                self.place(self.plane(step), lane),
                self.core,
            )

        return copy

    def y_copy(self, plane, row):
        def copy(index):
            item = self.items(plane * 2 + row)[index]
            return remote(
                item,
                item,
                self.y_send.at[plane, index],
                self.y_recv.at[plane, index],
                self.across,
                self.core,
            )

        return copy

    def c_copy(self, pair, side):
        item = self.block(side, pair)
        return remote(
            item, item, self.c_send.at[pair], self.c_recv.at[pair], self.me, 1 - self.core
        )

    def begin(self):
        for step, far in self.reached():
            self.each(self.z_copy(step, far), "start")

    def arrive(self, event):
        for far in (0, 1) if event else (1,):
            self.each(self.z_copy(event, far), "wait_recv")
        plane = self.plane(self.planes - event)
        self.each(self.y_copy(plane, self.y), "start")
        self.c_copy(plane * 2 + self.y, self.core).start()

    def complete(self, event):
        plane = self.plane(self.planes - event)
        self.each(self.y_copy(plane, 1 - self.y), "wait_recv")
        self.c_copy(plane * 2 + 1 - self.y, self.core).start()

    def wait_straight(self):
        for step, far in self.reached():
            self.each(self.z_copy(step, far), "wait_recv")
        for step, far in self.reached():
            self.each(self.z_copy(step, far), "wait_send")

    def cross(self):
        for plane in range(self.planes):
            self.each(self.y_copy(plane, self.y), "start")
            self.c_copy(plane * 2 + self.y, self.core).start()

    def crossed(self, plane):
        self.each(self.y_copy(plane, 1 - self.y), "wait_recv")
        self.c_copy(plane * 2 + 1 - self.y, self.core).start()

    def wait_crossed(self):
        for pair in range(2 * self.planes):
            self.c_copy(pair, 1 - self.core).wait_recv()
        for plane in range(self.planes):
            self.each(self.y_copy(plane, self.y), "wait_send")
        for pair in range(2 * self.planes):
            self.c_copy(pair, self.core).wait_send()

    def ready(self, event):
        plane = self.plane(self.planes - event)
        self.c_copy(plane * 2, 1 - self.core).wait_recv()
        self.c_copy(plane * 2 + 1, 1 - self.core).wait_recv()
        return plane

    def finish(self):
        for step, far in self.reached():
            self.each(self.z_copy(step, far), "wait_send")
        for plane in range(self.planes):
            self.each(self.y_copy(plane, self.y), "wait_send")
        for pair in range(2 * self.planes):
            self.c_copy(pair, self.core).wait_send()


def split_lanes(values, x, buffer, other, start, rows):
    half = values.shape[2] // 2
    zero, one = values[:, 0, :], values[:, 1, :]
    own, far = jnp.where(x == 0, zero, one), jnp.where(x == 0, one, zero)
    core = lax.axis_index("tp")
    own = jnp.where(core == 0, own[:, :half], own[:, half:]).astype(BF16)
    buffer[core, at(start, rows), :] = own
    for side in range(2):
        other[side] = far[:, side * half : (side + 1) * half].astype(BF16)


def gather_and_project(tokens, live, episode_frames, gain, shift, qkv, bias, fixed, ahead, n):
    rows, lanes, width = tokens.shape
    half = width // 2
    total = n * rows
    chunks = total // FRAME
    per_frame = FRAME // rows
    features = qkv.shape[3]
    slots = episode_frames.shape[1]

    def kernel(*refs):
        refs = list(refs)

        def take(count):
            taken = refs[:count]
            del refs[:count]
            return taken

        tokens_ref, live_ref, counts_ref, gain_ref, shift_ref, w_any, bias_ref = take(7)
        fixed_ref, ahead_ref = take(2)
        all_ref, mask_ref, frames_ref = take(3)
        projected = take(6)
        other, lives, live_other, weight, full, w_sem = take(6)
        relay = Relay(n, rows, all_ref, other, take(Relay.sems), lives, live_other)
        load = pltpu.make_async_copy(w_any.at[0], weight, w_sem)
        load.start()
        relay.hello()
        x, me = relay.x, relay.me
        split_lanes(tokens_ref[...].astype(F32), x, all_ref, other, me * rows, rows)
        lane = lax.broadcasted_iota(jnp.int32, (1, FRAME), 1)
        here = lane // rows == lax.rem(me, per_frame)
        tiles = []
        for index in range(lanes):
            alive = live_ref[index : index + 1, :].astype(F32)
            alive = jnp.where(here, jnp.concatenate([alive] * per_frame, axis=1), 0.0)
            tiles.append(jnp.broadcast_to(alive, (8, FRAME)))
        lives[me] = jnp.where(x == 0, tiles[0], tiles[1])
        live_other[...] = jnp.where(x == 0, tiles[1], tiles[0])
        relay.met()
        relay.begin()

        counts = [counts_ref[x, slot] for slot in range(slots)]
        episodes, openings = [], []
        for frame in range(chunks):
            end, episode, opening = 0, 0, 0
            for slot in range(slots):
                end = end + counts[slot]
                passed = frame >= end
                episode = episode + passed.astype(jnp.int32)
                opening = opening + jnp.where(passed, counts[slot], 0)
            episodes.append(episode)
            openings.append(frame - opening)
        for index in range(3):
            table = []
            for frame in range(chunks):
                line = jnp.zeros((1, PAIR), F32)
                for choice in range(chunks):
                    line = jnp.where(
                        openings[frame] == choice, ahead_ref[index, choice : choice + 1, :], line
                    )
                table.append(line)
            frames_ref[index] = jnp.concatenate(
                table + [jnp.zeros((8 - chunks, PAIR), F32)], axis=0
            )
        load.wait()

        def project_frame(frame):
            place = at(frame * FRAME, FRAME)
            stream = jnp.concatenate([all_ref[0, place, :], all_ref[1, place, :]], axis=1)
            project(
                stream.astype(F32),
                frame,
                0,
                me // 2,
                (gain_ref, shift_ref, weight, bias_ref, fixed_ref, frames_ref),
                [ref.at[place, :] for ref in projected],
                full,
            )

        for event in range(relay.events):
            relay.arrive(event)
            if event:
                relay.complete(event - 1)
            if event > 1:
                project_frame(relay.ready(event - 2))
        relay.complete(relay.events - 1)
        for event in range(max(0, relay.events - 2), relay.events):
            project_frame(relay.ready(event))
        relay.finish()

        for key_frame in range(chunks):
            alive = lives[key_frame * per_frame, 0:1, :]
            for part in range(1, per_frame):
                alive = alive + lives[key_frame * per_frame + part, 0:1, :]
            closed = (alive - 1.0) * -MASKED
            lines = []
            for query_frame in range(chunks):
                allowed = (episodes[query_frame] == episodes[key_frame]) & (
                    openings[key_frame] <= openings[query_frame]
                )
                lines.append(jnp.where(allowed, closed, MASKED))
            lines.append(jnp.zeros((PAIR - chunks, FRAME), F32))
            mask_ref[key_frame * FRAME : (key_frame + 1) * FRAME, :] = jnp.concatenate(
                lines, axis=0
            ).T.astype(BF16)

    in_vmem = pl.BlockSpec(memory_space=pltpu.VMEM)
    in_smem = pl.BlockSpec(memory_space=pltpu.SMEM)
    projected = jax.ShapeDtypeStruct((total, features), BF16)
    return pl.pallas_call(
        kernel,
        out_shape=(
            jax.ShapeDtypeStruct((2, total, half), BF16),
            jax.ShapeDtypeStruct((total, PAIR), BF16),
            jax.ShapeDtypeStruct((3, 8, PAIR), F32),
            projected,
            projected,
            projected,
            jax.ShapeDtypeStruct((total, PAIR), BF16),
            jax.ShapeDtypeStruct((total, width), BF16),
            jax.ShapeDtypeStruct((total, PAIR), F32),
        ),
        in_specs=[in_vmem, in_vmem, in_smem, in_vmem, in_vmem, ANYWHERE] + [in_vmem] * 3,
        out_specs=(in_vmem,) * 9,
        scratch_shapes=[
            pltpu.VMEM((2, rows, half), BF16),
            pltpu.VMEM((n, 8, FRAME), F32),
            pltpu.VMEM((8, FRAME), F32),
            pltpu.VMEM(qkv.shape[1:], BF16),
            pltpu.VMEM((FRAME, width), BF16),
            pltpu.SemaphoreType.DMA,
        ]
        + Relay.scratch(n),
        compiler_params=pltpu.CompilerParams(
            collective_id=0, has_side_effects=True, vmem_limit_bytes=VMEM_BYTES
        ),
        name="gather_and_project",
    )(tokens, live, episode_frames, gain, shift, qkv, bias, fixed, ahead)


def halves(ref):
    return jnp.concatenate([ref[0], ref[1]], axis=1).astype(F32)


def halves_spec(shape, chunks, behind, span=FRAME):
    return pl.BlockSpec(
        (2, span, shape[2]), lambda s: (0, jnp.clip(s - behind, 0, chunks - 1), 0)
    )


def attention_forward(query, key, value, key_mask, d_out, d_part, n, identity):
    total, features = query.shape
    chunks = total // FRAME
    heads = features // HEAD_DIM
    slabs = features // PAIR
    rows_here = total // n
    first_phase = d_out is not None
    carried = d_out if first_phase else d_part
    half = carried.shape[2] // 2 if first_phase else carried.shape[1]

    def kernel(q_ref, k_ref, v_ref, mask_ref, d_ref, *rest):
        p_refs = rest[:chunks]
        r_ref, mixed_ref, d_to, buffer, other, d_sem, *sems = rest[chunks:]
        step = pl.program_id(0)
        relay = Relay(n, rows_here, buffer, other, sems)
        core = relay.core

        @pl.when(step == 0)
        def _():
            if first_phase:
                relay.hello()
                split_lanes(d_ref, relay.x, buffer, other, relay.me * rows_here, rows_here)
                relay.met()
                relay.begin()
            else:
                fetch = pltpu.make_async_copy(d_ref, buffer.at[core], d_sem)
                fetch.start()
                fetch.wait()
                partners = [(relay.across, core), (relay.me, 1 - core)]
                hello(partners)
                met(partners)
                relay.cross()

        if not first_phase:

            @pl.when(step == slabs - 2)
            def _():
                for plane in range(relay.planes // 2):
                    relay.crossed(plane)

        lane = lax.broadcasted_iota(jnp.int32, (1, PAIR), 1)
        low_side = lane < HEAD_DIM
        sides = [low_side.astype(F32).astype(BF16), (lane >= HEAD_DIM).astype(F32).astype(BF16)]
        keys_wide = jnp.concatenate([k_ref[...], mask_ref[...]], axis=1)
        values = [v_ref[...] * sides[side] + sides[1 - side] for side in range(2)]

        def score(frame, side):
            own = slice(frame * FRAME, (frame + 1) * FRAME)
            asked = jnp.broadcast_to((lane == frame).astype(F32), (FRAME, PAIR)).astype(BF16)
            ask = jnp.concatenate([q_ref[own, :] * sides[side], asked], axis=1)
            return nt(ask, keys_wide[: (frame + 1) * FRAME])

        turns = [(frame, side) for frame in reversed(range(chunks)) for side in range(2)]
        scores, sums = score(*turns[0]), []
        for index, (frame, side) in enumerate(turns):
            keys = FRAME * (frame + 1)
            own = slice(frame * FRAME, keys)
            following = score(*turns[index + 1]) if index + 1 < len(turns) else None
            highest = jnp.max(scores, axis=1, keepdims=True)
            shifted = jnp.exp(scores - highest).astype(BF16)
            p_refs[frame][side] = shifted.T
            sums.append(nn(shifted, values[side][:keys]))
            scores = following
            if side == 1:
                one, two = sums[-2:]
                divisor = 1.0 / jnp.where(
                    low_side, pltpu.roll(one, HEAD_DIM, 1), pltpu.roll(two, HEAD_DIM, 1)
                )
                r_ref[own, :] = divisor
                mixed_ref[own, :] = (jnp.where(low_side, one, two) * divisor).astype(BF16)

        @pl.when(step == slabs - 1)
        def _():
            if first_phase:
                relay.wait_straight()
                source = buffer.at[core]
            else:
                for plane in range(relay.planes // 2, relay.planes):
                    relay.crossed(plane)
                relay.wait_crossed()
                source = buffer
            keep = pltpu.make_async_copy(source, d_to, d_sem)
            keep.start()
            keep.wait()

    slab = pl.BlockSpec((total, PAIR), lambda s: (0, s))
    seen = [FRAME * (frame + 1) for frame in range(chunks)]
    return pl.pallas_call(
        kernel,
        grid=(slabs,),
        out_shape=(
            *[jax.ShapeDtypeStruct((heads, rows, FRAME), BF16) for rows in seen],
            jax.ShapeDtypeStruct((total, features), F32),
            jax.ShapeDtypeStruct((total, features), BF16),
            jax.ShapeDtypeStruct((total, half) if first_phase else (2, total, half), BF16),
        ),
        in_specs=[slab] * 3 + [whole(key_mask), whole(carried) if first_phase else ANYWHERE],
        out_specs=(
            *[pl.BlockSpec((2, rows, FRAME), lambda s: (s, 0, 0)) for rows in seen],
            slab,
            slab,
            ANYWHERE,
        ),
        scratch_shapes=[
            pltpu.VMEM((2, total, half), BF16),
            pltpu.VMEM((2, rows_here, half), BF16),
            pltpu.SemaphoreType.DMA,
        ]
        + Relay.scratch(n),
        compiler_params=pltpu.CompilerParams(
            collective_id=identity, has_side_effects=True, vmem_limit_bytes=VMEM_BYTES
        ),
        name=f"attention_forward_{identity}",
    )(query, key, value, key_mask, carried)


def layer_forward(layer, mixed, stream, mats, rows_of, next_refs, identity):
    total, features = mixed.shape
    split = stream.ndim == 3
    width = mats[1].shape[1]
    hidden_units = mats[1].shape[2]
    chunks = total // FRAME
    columns = 256
    last = next_refs is None
    b_out, gain, shift, b_up, b_down = rows_of
    mat_out, mat_up, mat_down = mats

    def kernel(*refs):
        refs = list(refs)

        def take(count):
            taken = refs[:count]
            del refs[:count]
            return taken

        mixed_ref, x_ref = take(2)
        wo_any, wu_any, wd_any = take(3)
        bo_ref, gain_ref, shift_ref, bu_ref, bd_ref = take(5)
        if not last:
            wq_any, ngain, nshift, nbias, fixed, frames = take(6)
        unit_ref, scale_ref, second_ref, act_ref, gp_ref, x_out = take(6)
        if not last:
            next_outs = take(6)
        wo, wu, wd, mid, full, next_full = take(6)
        if not last:
            (wq,) = take(1)
        a_send, a_recv, b_send, b_recv, w_sem, send_sem, recv_sem = take(7)

        step = pl.program_id(0)
        me, core = lax.axis_index("seq"), lax.axis_index("tp")

        items = [(wo_any, wo), (wu_any, wu), (wd_any, wd)]
        if not last:
            items.append((wq_any, wq))

        def load(index):
            source, target = items[index]
            return pltpu.make_async_copy(
                source.at[layer if index < 3 else layer + 1], target, w_sem.at[index]
            )

        def exchange(kind, chunk):
            source, target = ((a_send, a_recv), (b_send, b_recv))[kind]
            return remote(
                source.at[chunk],
                target.at[chunk],
                send_sem.at[kind, chunk],
                recv_sem.at[kind, chunk],
                me,
                1 - core,
            )

        @pl.when(step == 0)
        def _():
            for index in range(len(items)):
                load(index).start()
            hello([(me, 1 - core)])

        @pl.when(step == 0)
        def _():
            load(0).wait()
            met([(me, 1 - core)])

        @pl.when(step < chunks)
        def _():
            a_send[step] = nn(mixed_ref[...], wo[...]).astype(BF16)
            exchange(0, step).start()

        def feed_forward():
            chunk = step - 1
            middle = (halves(x_ref) if split else x_ref[...]) + (
                a_send[chunk].astype(F32) + a_recv[chunk].astype(F32)
            )
            middle = middle + bo_ref[layer : layer + 1, :]
            mid[lax.rem(chunk, 2)] = middle
            unit, scale = normed(middle)
            keep_norm(unit, scale, unit_ref, scale_ref)
            second = (unit * gain_ref[layer : layer + 1, :] + shift_ref[layer : layer + 1, :]).astype(BF16)
            full[...] = second
            second_ref[...] = full[:, at((me // 2) * PAIR, PAIR)]
            parts = [slice(start, start + columns) for start in range(0, hidden_units, columns)]
            hidden = nn(second, wu[:, parts[0]])
            for index, part in enumerate(parts):
                following = nn(second, wu[:, parts[index + 1]]) if index + 1 < len(parts) else None
                act, slope = gelu_both(hidden + bu_ref[layer : layer + 1, part])
                act_ref[:, part] = act.astype(BF16)
                gp_ref[:, part] = slope.astype(BF16)
                hidden = following
            b_send[chunk] = nn(act_ref[...], wd[...]).astype(BF16)

        def close():
            chunk = step - 2
            result = mid[lax.rem(chunk, 2)] + (b_send[chunk].astype(F32) + b_recv[chunk].astype(F32))
            result = result + bd_ref[layer : layer + 1, :]
            x_out[...] = result
            if not last:
                project(
                    result,
                    chunk,
                    layer + 1,
                    me // 2,
                    (ngain, nshift, wq, nbias, fixed, frames),
                    next_outs,
                    next_full,
                )

        @pl.when(step == 1)
        def _():
            load(1).wait()
            load(2).wait()

        @pl.when((step >= 1) & (step <= chunks))
        def _():
            exchange(0, step - 1).wait_recv()
            feed_forward()
            exchange(1, step - 1).start()

        if not last:

            @pl.when(step == 2)
            def _():
                load(3).wait()

        @pl.when(step >= 2)
        def _():
            exchange(1, step - 2).wait_recv()
            close()

        @pl.when(step == chunks + 1)
        def _():
            for kind in range(2):
                for chunk in range(chunks):
                    exchange(kind, chunk).wait_send()

    def rows(columns, behind):
        return pl.BlockSpec(
            (FRAME, columns), lambda s: (jnp.clip(s - behind, 0, chunks - 1), 0)
        )

    in_specs = [rows(features, 0)]
    in_specs += [halves_spec(stream.shape, chunks, 1) if split else rows(width, 1)]
    in_specs += [ANYWHERE] * 3 + [whole(item) for item in rows_of]
    operands = [mixed, stream, *mats, *rows_of]
    if not last:
        in_specs += [ANYWHERE] + [whole(item) for item in next_refs[1:]]
        operands += list(next_refs)
    out_shape = [
        jax.ShapeDtypeStruct((total, width), BF16),
        jax.ShapeDtypeStruct((total, PAIR), F32),
        jax.ShapeDtypeStruct((total, PAIR), BF16),
        jax.ShapeDtypeStruct((total, hidden_units), BF16),
        jax.ShapeDtypeStruct((total, hidden_units), BF16),
        jax.ShapeDtypeStruct((total, width), F32),
    ]
    out_specs = [
        rows(width, 1),
        rows(PAIR, 1),
        rows(PAIR, 1),
        rows(hidden_units, 1),
        rows(hidden_units, 1),
        rows(width, 2),
    ]
    scratch = [
        pltpu.VMEM(mat_out.shape[1:], BF16),
        pltpu.VMEM(mat_up.shape[1:], BF16),
        pltpu.VMEM(mat_down.shape[1:], BF16),
        pltpu.VMEM((2, FRAME, width), F32),
        pltpu.VMEM((FRAME, width), BF16),
        pltpu.VMEM((FRAME, width), BF16),
    ]
    if not last:
        out_shape += [jax.ShapeDtypeStruct((total, features), BF16)] * 3
        out_shape += [jax.ShapeDtypeStruct((total, PAIR), BF16)]
        out_shape += [jax.ShapeDtypeStruct((total, width), BF16)]
        out_shape += [jax.ShapeDtypeStruct((total, PAIR), F32)]
        out_specs += [rows(features, 2)] * 3 + [rows(PAIR, 2), rows(width, 2), rows(PAIR, 2)]
        scratch += [pltpu.VMEM(next_refs[0].shape[1:], BF16)]
    scratch += [pltpu.VMEM((chunks, FRAME, width), BF16)] * 4
    scratch += [
        pltpu.SemaphoreType.DMA((4,)),
        pltpu.SemaphoreType.DMA((2, chunks)),
        pltpu.SemaphoreType.DMA((2, chunks)),
    ]
    return pl.pallas_call(
        kernel,
        grid=(chunks + 2,),
        out_shape=out_shape,
        in_specs=in_specs,
        out_specs=out_specs,
        scratch_shapes=scratch,
        compiler_params=pltpu.CompilerParams(
            collective_id=identity, has_side_effects=True, vmem_limit_bytes=VMEM_BYTES
        ),
        name=f"layer_forward_{layer}",
    )(*operands)


class Swap:
    def __init__(self, ships, lane_rows):
        self.ships, self.lane_rows = ships, lane_rows
        self.count = len(ships) + len(lane_rows)

    def operands(self):
        return [*self.ships, *[item for item, _ in self.lane_rows]]

    def in_specs(self):
        return [whole(item) for item in self.ships] + [ANYWHERE] * len(self.lane_rows)

    def outputs(self):
        shapes, specs = [], []
        for item in self.ships:
            shape = (item.shape[0] // 2, item.shape[1])
            shapes.append(jax.ShapeDtypeStruct(shape, F32))
            specs.append(whole_out(shape))
        for item, count in self.lane_rows:
            shapes.append(jax.ShapeDtypeStruct((count or item.shape[0], item.shape[1]), item.dtype))
            specs.append(ANYWHERE)
        return shapes, specs

    def scratch(self):
        if not self.count:
            return []
        buffers = [pltpu.VMEM((item.shape[0] // 2, item.shape[1]), BF16) for item in self.ships]
        return buffers * 2 + [pltpu.SemaphoreType.DMA((self.count,))] * 2

    def bind(self, sources, targets, scratch):
        ships = len(self.ships)
        me, core = lax.axis_index("seq"), lax.axis_index("tp")
        x = lax.rem(me, 2)
        beside = me + 1 - 2 * x
        half = PAIR // 2

        def copy(index):
            if index < ships:
                source, target = scratch[index], scratch[ships + index]
            else:
                source, target = sources[index], targets[index]
                count = self.lane_rows[index - ships][1]
                if count:
                    source = source.at[at(beside * count, count), :]
            send, recv = scratch[2 * ships].at[index], scratch[2 * ships + 1].at[index]
            return remote(source, target, send, recv, beside, core)

        def start():
            for index in range(self.count):
                if index < ships:
                    scratch[index][...] = sources[index][at((1 - x) * half, half), :].astype(BF16)
                copy(index).start()

        def finish():
            for index in range(self.count):
                copy(index).wait_recv()
                if index < ships:
                    own = sources[index][at(x * half, half), :]
                    targets[index][...] = own + scratch[ships + index][...].astype(F32)
            for index in range(self.count):
                copy(index).wait_send()

        return start, finish


def attention_backward(
    probs, divisor, mixed, query, key, value, grad_mixed, first, fixed, frames, swap, swap_qkv, identity
):
    total, features = query.shape
    chunks = total // FRAME
    slabs = features // PAIR
    half = PAIR // 2

    def kernel(*refs):
        refs = list(refs)

        def take(count):
            taken = refs[:count]
            del refs[:count]
            return taken

        p_refs = take(chunks)
        r_ref, o_ref, q_ref, k_ref, v_ref, g_ref, first_ref, fixed_ref, frames_ref = take(9)
        sources = take(swap.count)
        dq_ref, dk_ref, dv_ref, qkv_out = take(4)
        targets = take(swap.count)
        dk_sum, dv_sum, first_turned = take(3)
        if swap_qkv:
            qkv_own, qkv_send, qkv_recv, qkv_sems = take(4)
        start, finish = swap.bind(sources, targets, refs)

        step = pl.program_id(0)
        me, core = lax.axis_index("seq"), lax.axis_index("tp")
        x = lax.rem(me, 2)
        beside = me + 1 - 2 * x

        def qkv_copy(slab):
            return remote(
                qkv_send.at[slab],
                qkv_recv.at[slab],
                qkv_sems.at[0, slab],
                qkv_sems.at[1, slab],
                beside,
                core,
            )

        @pl.when(step == 0)
        def _():
            hello([(beside, core)])
            first_turned[...] = first_ref[...].T
            met([(beside, core)])
            start()

        lane = lax.broadcasted_iota(jnp.int32, (1, PAIR), 1)
        sides = [(lane < HEAD_DIM).astype(F32).astype(BF16), (lane >= HEAD_DIM).astype(F32).astype(BF16)]
        turned = k_ref[...].T
        ones = jnp.broadcast_to((lane < 2).astype(F32), (total, PAIR)).astype(BF16)
        values = jnp.concatenate([v_ref[...], ones], axis=1)

        def give(frame):
            keys = FRAME * (frame + 1)
            own = slice(frame * FRAME, keys)
            scaled = (g_ref[own, :].astype(F32) * r_ref[own, :]).astype(BF16)
            inner = scaled.astype(F32) * o_ref[own, :].astype(F32)
            grads, q_parts, g_parts = [], [], []
            for side in range(2):
                delta = jnp.sum(
                    jnp.where((lane < HEAD_DIM) == (side == 0), inner, 0.0), axis=1, keepdims=True
                )
                coarse = delta.astype(BF16).astype(F32)
                rest = jnp.where(lane == 0, -coarse, jnp.where(lane == 1, coarse - delta, 0.0))
                g2 = scaled * sides[side]
                grads.append(nt(values[:keys], jnp.concatenate([g2, rest.astype(BF16)], axis=1)))
                q_parts.append(q_ref[own, :] * sides[side])
                g_parts.append(g2)
            return grads, jnp.concatenate(q_parts, axis=0), jnp.concatenate(g_parts, axis=0)

        given = give(chunks - 1)
        for frame in reversed(range(chunks)):
            keys = FRAME * (frame + 1)
            own = slice(frame * FRAME, keys)
            tables = tables_of(fixed_ref, frames_ref, frame)
            grads, q_part, g_part = given
            given = give(frame - 1) if frame else None
            query_parts, score_parts, prob_parts = [], [], []
            for side in range(2):
                attention = p_refs[frame][side]
                grad_scores = (attention.astype(F32) * grads[side]).astype(BF16)
                query_parts.append(nn(turned[side * HEAD_DIM : (side + 1) * HEAD_DIM, :keys], grad_scores))
                score_parts.append(grad_scores)
                prob_parts.append(attention)
            grad_query = jnp.concatenate(query_parts, axis=0).T
            key_parts = nn(jnp.concatenate(score_parts, axis=1), q_part)
            value_parts = nn(jnp.concatenate(prob_parts, axis=1), g_part)
            dq_ref[own, :] = (turn(grad_query, tables, True) * SCORE_SCALE).astype(BF16)
            if frame == chunks - 1:
                dk_sum[...] = key_parts
                dv_sum[...] = value_parts
            else:
                dk_sum[:keys, :] += key_parts
                dv_sum[:keys, :] += value_parts
            dk_ref[own, :] = turn(dk_sum[own, :], tables, True).astype(BF16)
            dv_ref[own, :] = dv_sum[own, :].astype(BF16)

        for part, ref in enumerate((dq_ref, dk_ref, dv_ref)):
            piece = slice(part * PAIR, (part + 1) * PAIR)
            terms = nn(first_turned[...], ref[...])
            if swap_qkv:
                qkv_own[step, :, piece] = terms
                qkv_send[step, :, piece] = qkv_own[step, at((1 - x) * half, half), piece].astype(BF16)
            else:
                qkv_out[:, at(part * features + step * PAIR, PAIR)] = terms
        if swap_qkv:
            qkv_copy(step).start()

        @pl.when(step == slabs - 1)
        def _():
            finish()
            for slab in range(slabs if swap_qkv else 0):
                qkv_copy(slab).wait_recv()
                for part in range(3):
                    piece = slice(part * PAIR, (part + 1) * PAIR)
                    place = part * features + slab * PAIR
                    qkv_out[:, place : place + PAIR] = qkv_own[
                        slab, at(x * half, half), piece
                    ] + qkv_recv[slab, :, piece].astype(F32)
            for slab in range(slabs if swap_qkv else 0):
                qkv_copy(slab).wait_send()

    slab = pl.BlockSpec((total, PAIR), lambda s: (0, s))
    in_specs = [pl.BlockSpec((2, *item.shape[1:]), lambda s: (s, 0, 0)) for item in probs]
    in_specs += [slab] * 6 + [whole(first), whole(fixed), whole(frames)]
    in_specs += swap.in_specs()
    qkv_shape = (half if swap_qkv else PAIR, 3 * features)
    shapes, specs = swap.outputs()
    out_shape = [jax.ShapeDtypeStruct((total, features), BF16)] * 3
    out_shape += [jax.ShapeDtypeStruct(qkv_shape, F32)] + shapes
    out_specs = [slab] * 3 + [whole_out(qkv_shape)] + specs
    scratch = [pltpu.VMEM((total, PAIR), F32)] * 2 + [pltpu.VMEM((PAIR, total), BF16)]
    if swap_qkv:
        scratch += [pltpu.VMEM((slabs, PAIR, 3 * PAIR), F32)]
        scratch += [pltpu.VMEM((slabs, half, 3 * PAIR), BF16)] * 2
        scratch += [pltpu.SemaphoreType.DMA((2, slabs))]
    scratch += swap.scratch()
    return pl.pallas_call(
        kernel,
        grid=(slabs,),
        out_shape=out_shape,
        in_specs=in_specs,
        out_specs=out_specs,
        scratch_shapes=scratch,
        compiler_params=pltpu.CompilerParams(
            collective_id=identity, has_side_effects=True, vmem_limit_bytes=VMEM_BYTES
        ),
        name=f"attention_backward_{identity}",
    )(
        *probs,
        divisor,
        mixed,
        query,
        key,
        value,
        grad_mixed,
        first,
        fixed,
        frames,
        *swap.operands(),
    )


def rows_backward(entry, upper, identity, span, swap):
    top, bottom = len(entry) == 1, upper is None
    if not top:
        above, entry = entry[0], entry[1:]
    total = entry[0].shape[1] if top else entry[0].shape[0]
    chunks = total // span
    columns = 256
    ahead = 0 if top else 2 if bottom else 1
    if top:
        width = 2 * entry[0].shape[2]
    else:
        features, width = entry[0].shape[1], entry[5].shape[1]
    if not bottom:
        layer = upper[0]
        hidden_units, mixed_features = upper[1].shape[1], upper[6].shape[1]
    place_rows = total // lax.axis_size("seq")

    def kernel(*refs):
        refs = list(refs)

        def take(count):
            taken = refs[:count]
            del refs[:count]
            return taken

        if top:
            (d_out_ref,) = take(1)
        else:
            dq_ref, dk_ref, dv_ref, unit1, scale1, dm_ref, wq, gain1 = take(8)
        if not bottom:
            act_ref, gp_ref, unit2, scale2, second_ref, mixed_ref = take(6)
            wo_any, wu_any, wd_any, gain2 = take(4)
        sources = take(swap.count)
        if not top:
            (vec1,) = take(1)
        if not bottom:
            dmid_out, dmix_out, out_sum, up_sum, down_sum, vec2 = take(6)
        else:
            dx_out, dx_other, vec_other = take(3)
        targets = take(swap.count)
        if not top:
            a_send, a_recv = take(2)
        if not bottom:
            b_send, b_recv, grad_keep, hidden_keep, low_keep, last_keep, wo, wu, wd, w_sem = take(10)
        else:
            dx_keep, dx_send, dx_recv, vec_recv, x_send_sem, x_recv_sem = take(6)
        send_sem, recv_sem = take(2)
        start_swap, finish_swap = swap.bind(sources, targets, refs)

        step = pl.program_id(0)
        me, core = lax.axis_index("seq"), lax.axis_index("tp")
        pair = at((me // 2) * PAIR, PAIR)
        x = lax.rem(me, 2)
        beside = me + 1 - 2 * x

        def exchange(kind, chunk):
            source, target = (a_send, a_recv) if kind == 0 else (b_send, b_recv)
            return remote(
                source.at[chunk],
                target.at[chunk],
                send_sem.at[kind, chunk],
                recv_sem.at[kind, chunk],
                me,
                1 - core,
            )

        def load(index):
            source, target = ((wd_any, wd), (wu_any, wu), (wo_any, wo))[index]
            return pltpu.make_async_copy(source.at[layer], target, w_sem.at[index])

        partners = [(me, 1 - core)] + ([(beside, core)] if bottom or swap.count else [])

        @pl.when(step == 0)
        def _():
            if not bottom:
                for index in range(3):
                    load(index).start()
                out_sum[...] = jnp.zeros_like(out_sum)
                up_sum[...] = jnp.zeros_like(up_sum)
                down_sum[...] = jnp.zeros_like(down_sum)
                vec2[...] = jnp.zeros_like(vec2)
            if not top:
                vec1[...] = jnp.zeros_like(vec1)
            hello(partners)

        def meet():
            @pl.when(step == 0)
            def _():
                met(partners)
                start_swap()

        def entry_products():
            partial = None
            for part, ref in enumerate((dq_ref, dk_ref, dv_ref)):
                grad = ref[...]
                term = nt(grad, wq[0, part])
                partial = term if partial is None else partial + term
                vec1[part : part + 1, :] += column_sum(grad.astype(F32))
            a_send[step] = partial.astype(BF16)

        def entry_norm(chunk):
            if top:
                return halves(d_out_ref)
            grad_first = a_send[chunk].astype(F32) + a_recv[chunk].astype(F32)
            unit, scale = kept_norm(unit1, scale1)
            for start, sums in ((3, column_sum(grad_first * unit)), (5, column_sum(grad_first))):
                for side in range(width // features):
                    piece = slice(side * features, (side + 1) * features)
                    vec1[start + side : start + side + 1, :] += sums[:, piece]
            return dm_ref[...] + norm_pull(grad_first, gain1[above : above + 1, :], unit, scale)

        def feed_forward(between=None):
            chunk = step - ahead
            gradient = entry_norm(chunk)
            if bottom:
                dx_keep[at(chunk * span, span), :] = gradient
                return
            grad_keep[lax.rem(chunk, 2)] = gradient
            vec2[1:2, :width] += column_sum(gradient)
            low = gradient.astype(BF16)
            low_keep[...] = low
            low_columns = low_keep[:, pair]
            second = second_ref[...]
            parts = [slice(start, start + columns) for start in range(0, hidden_units, columns)]
            grad_act = nt(low, wd[parts[0], :])
            for index, part in enumerate(parts):
                following = nt(low, wd[parts[index + 1], :]) if index + 1 < len(parts) else None
                grad_hidden = grad_act * gp_ref[:, part].astype(F32)
                hidden_keep[:, part] = grad_hidden.astype(BF16)
                vec2[0:1, part] += column_sum(grad_hidden)
                grad_act = following
            if between is not None:
                between()
            b_send[chunk] = nt(hidden_keep[...], wu[...]).astype(BF16)
            down_sum[...] += tn(low_columns, act_ref[...])
            up_sum[...] += tn(second, hidden_keep[...])

        def close():
            chunk = step - ahead - 1
            grad_second = b_send[chunk].astype(F32) + b_recv[chunk].astype(F32)
            unit, scale = kept_norm(unit2, scale2)
            vec2[2:3, :width] += column_sum(grad_second * unit)
            vec2[3:4, :width] += column_sum(grad_second)
            grad_middle = grad_keep[lax.rem(chunk, 2)] + norm_pull(
                grad_second, gain2[layer : layer + 1, :], unit, scale
            )
            dmid_out[...] = grad_middle
            vec2[4:5, :width] += column_sum(grad_middle)
            low = grad_middle.astype(BF16)
            last_keep[...] = low
            out_sum[...] += tn(last_keep[:, pair], mixed_ref[...])
            dmix_out[...] = nt(low, wo[...]).astype(BF16)

        if not top:

            @pl.when(step < chunks)
            def _():
                entry_products()
                meet()
                exchange(0, step).start()

        @pl.when((step >= ahead) & (step < chunks + ahead))
        def _():
            if not top:
                exchange(0, step - ahead).wait_recv()
            if not bottom:

                @pl.when(step == ahead)
                def _():
                    load(0).wait()

            feed_forward(lambda: pl.when(step == ahead)(lambda: load(1).wait()))
            if not bottom:
                if top:
                    meet()
                exchange(1, step - ahead).start()

        if not bottom:

            @pl.when(step == ahead + 1)
            def _():
                load(2).wait()

            @pl.when(step >= ahead + 1)
            def _():
                exchange(1, step - ahead - 1).wait_recv()
                close()

        if bottom:

            def x_copy(index):
                source, target = ((dx_send, dx_recv), (vec1, vec_recv))[index]
                return remote(
                    source, target, x_send_sem.at[index], x_recv_sem.at[index], beside, core
                )

            @pl.when(step == chunks + 1)
            def _():
                dx_send[...] = dx_keep[at(beside * place_rows, place_rows), :].astype(BF16)
                x_copy(0).start()
                x_copy(1).start()
                dx_out[...] = dx_keep[at(me * place_rows, place_rows), :]
                x_copy(0).wait_recv()
                x_copy(1).wait_recv()
                dx_other[...] = dx_recv[...].astype(F32)
                vec_other[...] = vec_recv[...]
                x_copy(0).wait_send()
                x_copy(1).wait_send()

        @pl.when(step == pl.num_programs(0) - 1)
        def _():
            for kind in ([] if top else [0]) + ([] if bottom else [1]):
                for chunk in range(chunks):
                    exchange(kind, chunk).wait_send()
            finish_swap()

    def rows(columns, behind):
        return pl.BlockSpec(
            (span, columns), lambda s: (jnp.clip(s - behind, 0, chunks - 1), 0)
        )

    vec = jax.ShapeDtypeStruct((8, VEC), F32)
    operands, in_specs, out_shape, out_specs, scratch = [], [], [], [], []
    if top:
        operands += list(entry)
        in_specs += [halves_spec(entry[0].shape, chunks, 0, span)]
    else:
        operands += list(entry)
        in_specs += [rows(features, 0)] * 3
        in_specs += [rows(width, ahead), rows(PAIR, ahead), rows(width, ahead)]
        in_specs += [
            pl.BlockSpec(
                (1, *entry[6].shape[1:]),
                lambda s: (above, 0, 0, 0),
                pipeline_mode=pl.Buffered(1),
            ),
            whole(entry[7]),
        ]
        narrow = jax.ShapeDtypeStruct((8, features), F32)
        out_shape += [narrow]
        out_specs += [whole_out((8, features))]
        scratch += [pltpu.VMEM((chunks, span, width), BF16)] * 2
    if not bottom:
        operands += list(upper[1:])
        in_specs += [rows(hidden_units, ahead)] * 2
        in_specs += [rows(width, ahead + 1), rows(PAIR, ahead + 1), rows(PAIR, ahead)]
        in_specs += [rows(mixed_features, ahead + 1)] + [ANYWHERE] * 3 + [whole(upper[10])]
        sums = [mixed_features, hidden_units, hidden_units]
        out_shape += [
            jax.ShapeDtypeStruct((total, width), F32),
            jax.ShapeDtypeStruct((total, mixed_features), BF16),
        ]
        out_shape += [jax.ShapeDtypeStruct((PAIR, size), F32) for size in sums] + [vec]
        out_specs += [rows(width, ahead + 1), rows(mixed_features, ahead + 1)]
        out_specs += [whole_out((PAIR, size)) for size in sums] + [whole_out((8, VEC))]
        scratch += [pltpu.VMEM((chunks, span, width), BF16)] * 2
        scratch += [
            pltpu.VMEM((2, span, width), F32),
            pltpu.VMEM((span, hidden_units), BF16),
            pltpu.VMEM((span, width), BF16),
            pltpu.VMEM((span, width), BF16),
            pltpu.VMEM(upper[7].shape[1:], BF16),
            pltpu.VMEM(upper[8].shape[1:], BF16),
            pltpu.VMEM(upper[9].shape[1:], BF16),
            pltpu.SemaphoreType.DMA((3,)),
        ]
    else:
        out_shape += [
            jax.ShapeDtypeStruct((place_rows, width), F32),
            jax.ShapeDtypeStruct((place_rows, width), F32),
            narrow,
        ]
        out_specs += [whole_out((place_rows, width))] * 2 + [whole_out((8, features))]
        scratch += [
            pltpu.VMEM((total, width), F32),
            pltpu.VMEM((place_rows, width), BF16),
            pltpu.VMEM((place_rows, width), BF16),
            pltpu.VMEM((8, features), F32),
            pltpu.SemaphoreType.DMA((2,)),
            pltpu.SemaphoreType.DMA((2,)),
        ]
    scratch += [pltpu.SemaphoreType.DMA((2, chunks))] * 2
    operands += swap.operands()
    in_specs += swap.in_specs()
    shapes, specs = swap.outputs()
    out_shape += shapes
    out_specs += specs
    scratch += swap.scratch()
    return pl.pallas_call(
        kernel,
        grid=(chunks + (1 if top else 2),),
        out_shape=out_shape,
        in_specs=in_specs,
        out_specs=out_specs,
        scratch_shapes=scratch,
        compiler_params=pltpu.CompilerParams(
            collective_id=identity, has_side_effects=True, vmem_limit_bytes=VMEM_BYTES
        ),
        name=f"rows_backward_{identity}",
    )(*operands)


def assemble(sums, vecs, lanes, n, features, hidden_units):
    place = lanes[1].shape[0]
    width = lanes[1].shape[1]
    half = PAIR // 2

    def kernel(*refs):
        refs = list(refs)

        def take(count):
            taken = refs[:count]
            del refs[:count]
            return taken

        qkvs, outs, ups, downs = take(LAYERS), take(LAYERS), take(LAYERS), take(LAYERS)
        vec_refs = [take(4) for _ in range(LAYERS)]
        out_lane, out_other, dx_own, dx_other = take(4)
        out_ref, dx_ref, gain1, shift1, g_qkv, b_qkv, g_out, b_out = take(8)
        gain2, shift2, g_up, b_up, g_down, b_down = take(6)
        out_own, sem = refs
        me = lax.axis_index("seq")
        x = lax.rem(me, 2)
        fetch = pltpu.make_async_copy(out_lane.at[at(me * place, place), :], out_own, sem)
        fetch.start()

        for layer in range(LAYERS):
            for part in range(3):
                g_qkv[layer, part] = qkvs[layer][:, part * features : (part + 1) * features]
            for ref, target in ((outs, g_out), (ups, g_up), (downs, g_down)):
                target[layer] = ref[layer][...]

        for layer, (entry_own, entry_other, upper_own, upper_other) in enumerate(vec_refs):
            line = slice(layer, layer + 1)
            for part in range(3):
                row = slice(part, part + 1)
                b_qkv[part, line, :] = entry_own[row, :] + entry_other[row, :]
            b_up[line, :] = upper_own[0:1, :hidden_units] + upper_other[0:1, :hidden_units]

            def owned(mine, other, row):
                wide = mine.shape[1]
                place = (me // 2) * PAIR
                pair = at(lax.rem(place, wide), PAIR)
                both = mine[row : row + 1, pair] + other[row : row + 1, pair]
                for later in range(1, width // wide):
                    line = slice(row + later, row + later + 1)
                    both = jnp.where(place // wide == later, mine[line, pair] + other[line, pair], both)
                return jnp.where(x == 0, both[:, :half], both[:, half:])

            gain1[line, :] = owned(entry_own, entry_other, 3)
            shift1[line, :] = owned(entry_own, entry_other, 5)
            b_down[line, :] = owned(upper_own, upper_other, 1)
            gain2[line, :] = owned(upper_own, upper_other, 2)
            shift2[line, :] = owned(upper_own, upper_other, 3)
            b_out[line, :] = owned(upper_own, upper_other, 4)

        def both_lanes(target, mine, other):
            target[:, 0, :] = jnp.where(x == 0, mine, other)
            target[:, 1, :] = jnp.where(x == 0, other, mine)

        both_lanes(dx_ref, dx_own[...], dx_other[...])
        fetch.wait()
        both_lanes(out_ref, out_own[...], out_other[...])

    def f32(*shape):
        return jax.ShapeDtypeStruct(shape, F32)

    in_vmem = pl.BlockSpec(memory_space=pltpu.VMEM)
    flat = []
    for kind in range(4):
        flat += [sums[layer][kind] for layer in range(LAYERS)]
    for layer in range(LAYERS):
        flat += list(vecs[layer])
    flat += list(lanes)
    small = f32(LAYERS, width // n)
    return pl.pallas_call(
        kernel,
        out_shape=(
            f32(place, 2, width),
            f32(place, 2, width),
            small,
            small,
            f32(LAYERS, 3, half, features),
            f32(3, LAYERS, features),
            f32(LAYERS, half, features),
            small,
            small,
            small,
            f32(LAYERS, half, hidden_units),
            f32(LAYERS, hidden_units),
            f32(LAYERS, half, hidden_units),
            small,
        ),
        in_specs=[in_vmem] * (len(flat) - 4) + [ANYWHERE] + [in_vmem] * 3,
        out_specs=(in_vmem,) * 14,
        scratch_shapes=[pltpu.VMEM((place, width), F32), pltpu.SemaphoreType.DMA],
        compiler_params=pltpu.CompilerParams(vmem_limit_bytes=VMEM_BYTES),
        name="assemble",
    )(*flat)


def per_chip(
    tokens,
    d_out,
    norm1_gain,
    norm1_shift,
    w_qkv,
    b_qkv,
    w_out,
    b_out,
    norm2_gain,
    norm2_shift,
    w_up,
    b_up,
    w_down,
    b_down,
    episode_frames,
    live,
):
    n = lax.axis_size("seq")
    rows = tokens.shape[0]
    features = w_qkv.shape[3]
    fixed, ahead = turn_constants(rows * n // FRAME)
    qkv, qkv_bias = w_qkv.transpose(0, 2, 1, 3), b_qkv.transpose(1, 0, 2)

    gathered, key_bias, frames, *projected = gather_and_project(
        tokens, live.T, episode_frames, norm1_gain, norm1_shift, qkv, qkv_bias, fixed, ahead, n
    )
    streams, kept, d_part = [gathered], [], None
    for layer in range(LAYERS):
        following = None
        if layer + 1 < LAYERS:
            following = (qkv, norm1_gain, norm1_shift, qkv_bias, fixed, frames)
        *probs, divisor, mixed, d_part = attention_forward(
            *projected[:3],
            key_bias,
            d_out if layer == 0 else None,
            d_part,
            n,
            1 + 2 * layer,
        )
        results = layer_forward(
            layer,
            mixed,
            streams[layer],
            (w_out, w_up, w_down),
            (b_out, norm2_gain, norm2_shift, b_up, b_down),
            following,
            2 + 2 * layer,
        )
        kept.append((*projected, probs, divisor, mixed, *results[:5]))
        streams.append(results[5])
        projected = results[6:]
    d_lane = d_part

    sums = [[None] * 4 for _ in range(LAYERS)]
    vecs = [[None] * 4 for _ in range(LAYERS)]
    entry, later = (d_lane,), None
    for layer in reversed(range(LAYERS)):
        query, key, value, first, unit1, scale1, probs, divisor, mixed = kept[layer][:9]
        unit2, scale2, second, act, slope = kept[layer][9:]
        upper = (
            layer,
            act,
            slope,
            unit2,
            scale2,
            second,
            mixed,
            w_out,
            w_up,
            w_down,
            norm2_gain,
        )
        identity = 1 + 2 * LAYERS + 2 * (LAYERS - 1 - layer)
        if later is None:
            results = rows_backward(entry, upper, identity, FRAME, Swap([], []))
        else:
            swap = Swap(later[:2], [(later[2], 0), (streams[LAYERS], rows)])
            vec1, *results = rows_backward(entry, upper, identity, FRAME, swap)
            results, swapped = results[:6], results[6:]
            sums[layer + 1][3], sums[layer + 1][0] = swapped[:2]
            vecs[layer + 1][3], out_other = swapped[2:]
            vecs[layer + 1][0] = vec1
        grad_middle, grad_mixed, out_sum, up_sum, down_sum, vec2 = results
        vecs[layer][2] = vec2
        last = layer == 0
        if last:
            swap = Swap([out_sum, up_sum], [(vec2, 0), (vecs[layer + 1][0], 0)])
        else:
            swap = Swap([out_sum, up_sum], [])
        results = attention_backward(
            probs,
            divisor,
            mixed,
            query,
            key,
            value,
            grad_mixed,
            first,
            fixed,
            frames,
            swap,
            last,
            identity + 1,
        )
        grad_query, grad_key, grad_value, qkv_sum = results[:4]
        if last:
            sums[layer][:3] = [qkv_sum, *results[4:6]]
            vecs[layer][3], vecs[layer + 1][1] = results[6:8]
        else:
            sums[layer][1:3] = results[4:6]
            later = [down_sum, qkv_sum, vec2]
        entry = (
            layer,
            grad_query,
            grad_key,
            grad_value,
            unit1,
            scale1,
            grad_middle,
            qkv,
            norm1_gain,
        )
    vec1, dx_own, dx_other, vec_other, sums[0][3] = rows_backward(
        entry, None, 1 + 4 * LAYERS, FRAME, Swap([down_sum], [])
    )
    vecs[0][:2] = [vec1, vec_other]
    results = list(
        assemble(
            sums,
            vecs,
            (streams[LAYERS], out_other, dx_own, dx_other),
            n,
            features,
            w_up.shape[2],
        )
    )
    results[4] = results[4].transpose(0, 2, 1, 3)
    results[5] = results[5].transpose(1, 0, 2)
    results[6] = results[6].transpose(0, 2, 1)
    results[12] = results[12].transpose(0, 2, 1)
    return tuple(results)


def lane_fits(mesh, tokens):
    n = mesh.shape["seq"]
    positions, lanes, width = tokens.shape
    rows = positions // n
    return (
        lanes == 2
        and n % 4 == 0
        and positions <= 4 * FRAME
        and positions % FRAME == 0
        and FRAME % rows == 0
        and width // n * 2 == PAIR
        and mesh.shape["tp"] == 2
    )


def solution(mesh):
    placed = (
        P("seq", None, None),
        P("seq", None, None),
        P(),
        P(),
        P(None, None, None, "tp"),
        P(None, None, "tp"),
        P(None, "tp", None),
        P(),
        P(),
        P(),
        P(None, None, "tp"),
        P(None, "tp"),
        P(None, "tp", None),
        P(),
        P(),
        P("seq", None),
    )
    def mapped(body):
        return jax.shard_map(
            body,
            mesh=mesh,
            in_specs=placed,
            out_specs=(
                P("seq", None, None),
                P("seq", None, None),
                P(None, "seq"),
                P(None, "seq"),
                P(None, "seq", None, "tp"),
                P(None, None, "tp"),
                P(None, "tp", "seq"),
                P(None, "seq"),
                P(None, "seq"),
                P(None, "seq"),
                P(None, "seq", "tp"),
                P(None, "tp"),
                P(None, "tp", "seq"),
                P(None, "seq"),
            ),
            check_vma=False,
        )

    def run(tokens, *others):
        if lane_fits(mesh, tokens):
            return mapped(per_chip)(tokens, *others)
        return mapped(per_device)(tokens, *others)

    return run
```

```python
import math

import jax
import jax.numpy as jnp
import numpy as np
from jax import lax
from jax.experimental import pallas as pl
from jax.experimental.pallas import tpu as pltpu
from jax.sharding import PartitionSpec as P

HEAD_DIM = 64
GRID = 16
FRAME = 256
LAYERS = 2
MICRO = 2


EPSILON = 1e-06
MASKED = -1e30
SCORE_SCALE = 0.125


def layer_norm(stream, norm_gain, norm_shift):
    center = stream - jnp.mean(stream, axis=-1, keepdims=True)
    spread = jnp.mean(center * center, axis=-1, keepdims=True)
    return center * lax.rsqrt(spread + EPSILON) * norm_gain + norm_shift


def rotate(values, frame_place, row_place, column_place):
    frequency = jnp.exp(jnp.arange(10, dtype=jnp.float32) * (-math.log(10000.0) / 10.0))
    pieces = []
    for section, place in enumerate((frame_place, row_place, column_place)):
        lower = values[..., 20 * section : 20 * section + 10]
        upper = values[..., 20 * section + 10 : 20 * section + 20]
        angles = place.astype(jnp.float32)[..., None, None] * frequency
        cosine = jnp.cos(angles)
        sine_part = jnp.sin(angles)
        pieces.append(lower * cosine - upper * sine_part)
        pieces.append(lower * sine_part + upper * cosine)
    pieces.append(values[..., 60:])
    return jnp.concatenate(pieces, axis=-1)


def episode_tags(frame_counts, positions):
    endings = jnp.cumsum(frame_counts) * FRAME
    passed = (positions[:, None] >= endings[None, :]).astype(jnp.int32)
    episode = jnp.sum(passed, axis=1)
    opening = jnp.sum(passed * frame_counts[None, :], axis=1)
    frame_index = positions // FRAME - opening
    within = positions % FRAME
    return (episode, frame_index, within // GRID, within % GRID)


def gelu_exact(values):
    return jax.nn.gelu(values, approximate=False)


def sum_heads(partial_sum):
    return lax.psum(partial_sum.astype(jnp.bfloat16), "tp").astype(jnp.float32)


def sum_inputs(partial_sum):
    return lax.psum(partial_sum.astype(jnp.bfloat16), "tp").astype(jnp.float32)


def lane_scores(query, keys_all, lane_index, query_tags, key_tags):
    head_count = query.shape[2] // HEAD_DIM
    query_lane = lax.dynamic_index_in_dim(query, lane_index, 1, False).reshape(
        query.shape[0], head_count, HEAD_DIM
    )
    keys_lane = lax.dynamic_index_in_dim(keys_all, lane_index, 1, False).reshape(
        keys_all.shape[0], head_count, HEAD_DIM
    )
    query_episode, query_frame = [
        lax.dynamic_index_in_dim(item, lane_index, 1, False) for item in query_tags
    ]
    key_episode, key_frame, key_live = [
        lax.dynamic_index_in_dim(item, lane_index, 1, False) for item in key_tags
    ]
    allowed = (
        (query_episode[:, None] == key_episode[None, :])
        & (key_frame[None, :] <= query_frame[:, None])
        & (key_live[None, :] > 0)
    )
    scores = (
        jnp.einsum("qhd,khd->hqk", query_lane, keys_lane, preferred_element_type=jnp.float32)
        * SCORE_SCALE
    )
    return (jnp.where(allowed[None], scores, MASKED), query_lane, keys_lane)


def attend_forward(query, keys_all, values_all, query_tags, key_tags):
    rows_dev, lane_count, features = query.shape
    head_count = features // HEAD_DIM

    def one_lane(lane_index, carry):
        scores, query_lane, keys_lane = lane_scores(
            query, keys_all, lane_index, query_tags, key_tags
        )
        highest = jnp.max(scores, axis=-1, keepdims=True)
        shifted = jnp.exp(scores - highest)
        summed = jnp.sum(shifted, axis=-1, keepdims=True)
        attention = (shifted / summed).astype(jnp.bfloat16)
        values_lane = lax.dynamic_index_in_dim(values_all, lane_index, 1, False).reshape(
            values_all.shape[0], head_count, HEAD_DIM
        )
        result = jnp.einsum(
            "hqk,khd->qhd", attention, values_lane, preferred_element_type=jnp.float32
        ).reshape(rows_dev, 1, features)
        log_total = (highest + jnp.log(summed))[None, :, :, 0]
        return (result, log_total)

    initial = (
        jnp.zeros((rows_dev, lane_count, features), jnp.float32),
        jnp.zeros((lane_count, head_count, rows_dev), jnp.float32),
    )
    return lax.fori_loop(0, lane_count, one_lane, initial)


def attend_backward(query, keys_all, values_all, log_total, grad_mixed, query_tags, key_tags):
    rows_dev, lane_count, features = query.shape
    head_count = features // HEAD_DIM
    key_rows = keys_all.shape[0]

    def one_lane(lane_index, carry):
        scores, query_lane, keys_lane = lane_scores(
            query, keys_all, lane_index, query_tags, key_tags
        )
        values_lane = lax.dynamic_index_in_dim(values_all, lane_index, 1, False).reshape(
            key_rows, head_count, HEAD_DIM
        )
        grad_lane = lax.dynamic_index_in_dim(grad_mixed, lane_index, 1, False).reshape(
            rows_dev, head_count, HEAD_DIM
        )
        attention = jnp.exp(
            scores - lax.dynamic_index_in_dim(log_total, lane_index, 0, False)[:, :, None]
        )
        grad_attention = jnp.einsum(
            "qhd,khd->hqk", grad_lane, values_lane, preferred_element_type=jnp.float32
        )
        inner = jnp.sum(attention * grad_attention, axis=-1, keepdims=True)
        grad_scores = (attention * (grad_attention - inner)).astype(jnp.bfloat16)
        query_part = (
            jnp.einsum("hqk,khd->qhd", grad_scores, keys_lane, preferred_element_type=jnp.float32)
            * SCORE_SCALE
        )
        key_part = (
            jnp.einsum("hqk,qhd->khd", grad_scores, query_lane, preferred_element_type=jnp.float32)
            * SCORE_SCALE
        )
        value_part = jnp.einsum(
            "hqk,qhd->khd",
            attention.astype(jnp.bfloat16),
            grad_lane,
            preferred_element_type=jnp.float32,
        )
        stacked = jnp.stack(
            [key_part.reshape(key_rows, features), value_part.reshape(key_rows, features)], axis=1
        )
        key_terms = stacked[:, None]
        grad_query = query_part.reshape(rows_dev, 1, features)
        return (grad_query, key_terms)

    initial = (
        jnp.zeros((rows_dev, lane_count, features), jnp.float32),
        jnp.zeros((key_rows, lane_count, 2, features), jnp.float32),
    )
    return lax.fori_loop(0, lane_count, one_lane, initial)


def front(stream, layer_index, params, query_tags, key_tags, positions):
    (
        gain_one,
        shift_one,
        mat_qkv,
        bias_qkv,
        mat_out,
        bias_out,
        gain_two,
        shift_two,
        mat_up,
        bias_up,
        mat_down,
        bias_down,
    ) = [item[layer_index] for item in params]
    rows_dev, lane_count, width = stream.shape
    features = mat_qkv.shape[2]
    head_count = features // HEAD_DIM
    frame_place, row_place, column_place = positions
    first = layer_norm(stream, gain_one, shift_one).astype(jnp.bfloat16)
    projected = (
        jnp.einsum("tbd,dcf->tbcf", first, mat_qkv, preferred_element_type=jnp.float32) + bias_qkv
    )
    split = projected.reshape(rows_dev, lane_count, 3, head_count, HEAD_DIM)
    query = (
        rotate(split[:, :, 0], frame_place, row_place, column_place)
        .reshape(rows_dev, lane_count, features)
        .astype(jnp.bfloat16)
    )
    keys = (
        rotate(split[:, :, 1], frame_place, row_place, column_place)
        .reshape(rows_dev, lane_count, features)
        .astype(jnp.bfloat16)
    )
    values = projected[:, :, 2].astype(jnp.bfloat16)
    keys_all, values_all = (
        lax.all_gather(keys, "seq", axis=0, tiled=True),
        lax.all_gather(values, "seq", axis=0, tiled=True),
    )
    mixed_full, log_total = attend_forward(query, keys_all, values_all, query_tags, key_tags)
    mixed = mixed_full.astype(jnp.bfloat16)
    middle = (
        stream
        + sum_heads(jnp.einsum("tbf,fd->tbd", mixed, mat_out, preferred_element_type=jnp.float32))
        + bias_out
    )
    second = layer_norm(middle, gain_two, shift_two).astype(jnp.bfloat16)
    hidden = jnp.einsum("tbd,df->tbf", second, mat_up, preferred_element_type=jnp.float32) + bias_up
    activation = gelu_exact(hidden).astype(jnp.bfloat16)
    return (
        first,
        query,
        keys_all,
        values_all,
        log_total,
        mixed,
        middle,
        second,
        hidden,
        activation,
        mixed_full,
    )


def layer_backward(stream, gradient, layer_index, params, query_tags, key_tags, positions):
    (
        gain_one,
        shift_one,
        mat_qkv,
        bias_qkv,
        mat_out,
        bias_out,
        gain_two,
        shift_two,
        mat_up,
        bias_up,
        mat_down,
        bias_down,
    ) = [item[layer_index] for item in params]
    (
        first,
        query,
        keys_all,
        values_all,
        log_total,
        mixed,
        middle,
        second,
        hidden,
        activation,
        mixed_full,
    ) = front(stream, layer_index, params, query_tags, key_tags, positions)
    frame_place, row_place, column_place = positions
    rows_dev, lane_count, width = stream.shape
    features = query.shape[2]
    head_count = features // HEAD_DIM
    grad_low = gradient.astype(jnp.bfloat16)
    grad_w_down = jnp.einsum(
        "tbf,tbd->fd", activation, grad_low, preferred_element_type=jnp.float32
    )
    grad_b_down = jnp.sum(gradient, axis=(0, 1))
    grad_activation = jnp.einsum(
        "tbd,fd->tbf", grad_low, mat_down, preferred_element_type=jnp.float32
    )
    grad_hidden = jax.vjp(gelu_exact, hidden)[1](grad_activation)[0].astype(jnp.bfloat16)
    grad_b_up = jnp.sum(grad_hidden.astype(jnp.float32), axis=(0, 1))
    grad_w_up = jnp.einsum("tbd,tbf->df", second, grad_hidden, preferred_element_type=jnp.float32)
    grad_second = sum_inputs(
        jnp.einsum("tbf,df->tbd", grad_hidden, mat_up, preferred_element_type=jnp.float32)
    )
    middle_pull = jax.vjp(layer_norm, middle, gain_two, shift_two)[1]
    grad_inner, grad_gain_two, grad_shift_two = middle_pull(grad_second)
    grad_middle = gradient + grad_inner
    grad_b_out = jnp.sum(grad_middle, axis=(0, 1))
    middle_low = grad_middle.astype(jnp.bfloat16)
    grad_w_out = jnp.einsum("tbf,tbd->fd", mixed, middle_low, preferred_element_type=jnp.float32)
    grad_mixed = jnp.einsum(
        "tbd,fd->tbf", middle_low, mat_out, preferred_element_type=jnp.float32
    ).astype(jnp.bfloat16)
    grad_query, key_terms = attend_backward(
        query, keys_all, values_all, log_total, grad_mixed, query_tags, key_tags
    )
    returned = lax.psum_scatter(key_terms, "seq", scatter_dimension=0, tiled=True)
    turned_query = rotate(
        grad_query.reshape(rows_dev, lane_count, head_count, HEAD_DIM),
        -frame_place,
        -row_place,
        -column_place,
    )
    turned_keys = rotate(
        returned[:, :, 0].reshape(rows_dev, lane_count, head_count, HEAD_DIM),
        -frame_place,
        -row_place,
        -column_place,
    )
    grad_projected = jnp.stack(
        [
            turned_query.reshape(rows_dev, lane_count, features),
            turned_keys.reshape(rows_dev, lane_count, features),
            returned[:, :, 1],
        ],
        axis=2,
    ).astype(jnp.bfloat16)
    grad_b_qkv = jnp.sum(grad_projected.astype(jnp.float32), axis=(0, 1))
    grad_w_qkv = jnp.einsum(
        "tbd,tbcf->dcf", first, grad_projected, preferred_element_type=jnp.float32
    )
    grad_first = sum_inputs(
        jnp.einsum("tbcf,dcf->tbd", grad_projected, mat_qkv, preferred_element_type=jnp.float32)
    )
    first_pull = jax.vjp(layer_norm, stream, gain_one, shift_one)[1]
    grad_entry, grad_gain_one, grad_shift_one = first_pull(grad_first)
    grads = (
        grad_gain_one,
        grad_shift_one,
        grad_w_qkv,
        grad_b_qkv,
        grad_w_out,
        grad_b_out,
        grad_gain_two,
        grad_shift_two,
        grad_w_up,
        grad_b_up,
        grad_w_down,
        grad_b_down,
    )
    return (grad_middle + grad_entry, grads)


def per_device(
    tokens,
    d_out,
    norm1_gain,
    norm1_shift,
    w_qkv,
    b_qkv,
    w_out,
    b_out,
    norm2_gain,
    norm2_shift,
    w_up,
    b_up,
    w_down,
    b_down,
    episode_frames,
    live,
):
    rows_dev = tokens.shape[0]
    lane_count = tokens.shape[1] // MICRO
    total_rows = rows_dev * lax.axis_size("seq")
    local_positions = lax.axis_index("seq") * rows_dev + jnp.arange(rows_dev, dtype=jnp.int32)
    key_positions = jnp.arange(total_rows, dtype=jnp.int32)
    tagger = jax.vmap(episode_tags, in_axes=(0, None), out_axes=1)
    query_episode, query_frame, query_row, query_column = tagger(episode_frames, local_positions)
    key_episode, key_frame, key_row, key_column = tagger(episode_frames, key_positions)
    live_keys = lax.all_gather(live, "seq", axis=0, tiled=True)
    params = (
        norm1_gain,
        norm1_shift,
        w_qkv,
        b_qkv,
        w_out,
        b_out,
        norm2_gain,
        norm2_shift,
        w_up,
        b_up,
        w_down,
        b_down,
    )
    layer_grads = [None] * LAYERS
    outputs = []
    grad_tokens = []
    for micro_index in range(MICRO):
        first_lane = micro_index * lane_count
        last_lane = first_lane + lane_count
        query_tags = (query_episode[:, first_lane:last_lane], query_frame[:, first_lane:last_lane])
        key_tags = (
            key_episode[:, first_lane:last_lane],
            key_frame[:, first_lane:last_lane],
            live_keys[:, first_lane:last_lane],
        )
        positions = (
            query_frame[:, first_lane:last_lane],
            query_row[:, first_lane:last_lane],
            query_column[:, first_lane:last_lane],
        )
        stream = tokens[:, first_lane:last_lane].astype(jnp.float32)
        inputs = []
        gathered = []
        for layer_index in range(LAYERS):
            inputs.append(stream)
            layer_state = front(stream, layer_index, params, query_tags, key_tags, positions)
            gathered.append((layer_state[2], layer_state[3]))
            branch = jnp.einsum(
                "tbf,fd->tbd",
                layer_state[9],
                w_down[layer_index],
                preferred_element_type=jnp.float32,
            )
            stream = layer_state[6] + sum_heads(branch) + b_down[layer_index]
        outputs.append(stream)
        gradient = d_out[:, first_lane:last_lane]
        for layer_index in reversed(range(LAYERS)):
            gradient, grads = layer_backward(
                inputs[layer_index], gradient, layer_index, params, query_tags, key_tags, positions
            )
            if layer_grads[layer_index] is None:
                layer_grads[layer_index] = grads
            else:
                layer_grads[layer_index] = jax.tree.map(jnp.add, layer_grads[layer_index], grads)
        grad_tokens.append(gradient)
    stacked = [
        jnp.stack([layer_grads[layer_index][entry] for layer_index in range(LAYERS)])
        for entry in range(12)
    ]
    (
        grad_gain_one,
        grad_shift_one,
        grad_w_qkv,
        grad_b_qkv,
        grad_w_out,
        grad_b_out,
        grad_gain_two,
        grad_shift_two,
        grad_w_up,
        grad_b_up,
        grad_w_down,
        grad_b_down,
    ) = stacked
    in_sums = (
        lax.psum_scatter(grad_w_qkv, "seq", scatter_dimension=1, tiled=True),
        lax.psum_scatter(grad_w_up, "seq", scatter_dimension=1, tiled=True),
        lax.psum_scatter(grad_gain_one, "seq", scatter_dimension=1, tiled=True),
        lax.psum_scatter(grad_shift_one, "seq", scatter_dimension=1, tiled=True),
        lax.psum_scatter(grad_gain_two, "seq", scatter_dimension=1, tiled=True),
        lax.psum_scatter(grad_shift_two, "seq", scatter_dimension=1, tiled=True),
        lax.psum_scatter(grad_b_out, "seq", scatter_dimension=1, tiled=True),
        lax.psum_scatter(grad_b_down, "seq", scatter_dimension=1, tiled=True),
    )
    out_sums = (
        lax.psum_scatter(grad_w_out, "seq", scatter_dimension=2, tiled=True),
        lax.psum_scatter(grad_w_down, "seq", scatter_dimension=2, tiled=True),
    )
    bias_total = lax.psum((grad_b_qkv, grad_b_up), "seq")
    return (
        jnp.concatenate(outputs, axis=1),
        jnp.concatenate(grad_tokens, axis=1),
        in_sums[2],
        in_sums[3],
        in_sums[0],
        bias_total[0],
        out_sums[0],
        in_sums[6],
        in_sums[4],
        in_sums[5],
        in_sums[1],
        bias_total[1],
        out_sums[1],
        in_sums[7],
    )


MESH = pl.DeviceIdType.MESH
BF16 = jnp.bfloat16
F32 = jnp.float32
VMEM_BYTES = 60 * 1024 * 1024
PAIR = 128
VEC = 2048


def nn(left, right):
    return lax.dot_general(left, right, (((1,), (0,)), ((), ())), preferred_element_type=F32)


def nt(left, right):
    return lax.dot_general(left, right, (((1,), (1,)), ((), ())), preferred_element_type=F32)


def tn(left, right):
    return lax.dot_general(left, right, (((0,), (0,)), ((), ())), preferred_element_type=F32)


def at(start, size):
    return pl.ds(pl.multiple_of(start, size), size)


def remote(src, dst, send, recv, seq, tp):
    return pltpu.make_async_remote_copy(
        src_ref=src,
        dst_ref=dst,
        send_sem=send,
        recv_sem=recv,
        device_id=(seq, tp),
        device_id_type=MESH,
    )


def hello(partners):
    barrier = pltpu.get_barrier_semaphore()
    for seq, tp in partners:
        pl.semaphore_signal(barrier, inc=1, device_id=(seq, tp), device_id_type=MESH)


def met(partners):
    pl.semaphore_wait(pltpu.get_barrier_semaphore(), len(partners))


class Exchange:
    pieces = 4

    def __init__(self, source, target, send, recv, me, core):
        rows = source.shape[0] // self.pieces
        self.copies = []
        for piece in range(self.pieces):
            part = pl.ds(piece * rows, rows)
            self.copies.append(
                (source.at[part, :], target.at[part, :], send.at[piece], recv.at[piece], me, 1 - core)
            )

    def start(self):
        for copy in self.copies:
            remote(*copy).start()

    def wait_recv(self):
        for copy in self.copies:
            remote(*copy).wait_recv()

    def wait_send(self):
        for copy in self.copies:
            remote(*copy).wait_send()


def whole(array):
    zeros = (0,) * array.ndim
    return pl.BlockSpec(array.shape, lambda s: zeros, pipeline_mode=pl.Buffered(1))


def whole_out(shape):
    zeros = (0,) * len(shape)
    return pl.BlockSpec(shape, lambda s: zeros)


ANYWHERE = pl.BlockSpec(memory_space=pl.ANY)


def turn_row(table, place, section):
    frequency = np.exp(np.arange(10, dtype=np.float32) * np.float32(-math.log(10000.0) / 10.0))
    angle = place.astype(np.float32)[:, None] * frequency
    for base in range(20 * section, PAIR, HEAD_DIM):
        table[0, :, base : base + 10] = np.cos(angle)
        table[0, :, base + 10 : base + 20] = np.cos(angle)
        table[1, :, base : base + 10] = -np.sin(angle)
        table[2, :, base + 10 : base + 20] = np.sin(angle)


def turn_constants(frames):
    within, ahead = np.zeros((3, FRAME, PAIR), np.float32), np.zeros((3, frames, PAIR), np.float32)
    turn_row(within, np.arange(FRAME) // GRID, 1)
    turn_row(within, np.arange(FRAME) % GRID, 2)
    for base in range(60, PAIR, HEAD_DIM):
        within[0, :, base : base + 4] = 1.0
    turn_row(ahead, np.arange(frames), 0)
    return jnp.asarray(within), jnp.asarray(ahead)


def turn(values, tables, back=False):
    cosine, lower, upper = tables
    pieces = []
    for start in range(0, values.shape[1], PAIR):
        slab = values[:, start : start + PAIR]
        moved = pltpu.roll(slab, PAIR - 10, 1) * lower + pltpu.roll(slab, 10, 1) * upper
        pieces.append(slab * cosine - moved if back else slab * cosine + moved)
    return jnp.concatenate(pieces, axis=1)


def tables_of(fixed_ref, frames_ref, chunk):
    return [fixed_ref[i] + frames_ref[i, pl.ds(chunk, 1), :] for i in range(3)]


def normed(stream):
    center = stream - jnp.mean(stream, axis=-1, keepdims=True)
    spread = jnp.mean(center * center, axis=-1, keepdims=True)
    scale = lax.rsqrt(spread + EPSILON)
    return center * scale, scale


def norm_pull(grad, gain, unit, scale):
    scaled = grad * gain
    return scale * (
        scaled
        - jnp.mean(scaled, axis=-1, keepdims=True)
        - unit * jnp.mean(scaled * unit, axis=-1, keepdims=True)
    )


def keep_norm(unit, scale, unit_ref, scale_ref):
    unit_ref[...] = unit.astype(BF16)
    scale_ref[...] = jnp.broadcast_to(scale, scale_ref.shape)


def kept_norm(unit_ref, scale_ref):
    copies = unit_ref.shape[1] // scale_ref.shape[1]
    return unit_ref[...].astype(F32), jnp.concatenate([scale_ref[...]] * copies, axis=1)


def column_sum(values):
    return jnp.sum(values, axis=0, keepdims=True)


def gelu_both(hidden):
    normal = 0.5 + 0.5 * lax.erf(hidden * math.sqrt(0.5))
    density = jnp.exp(hidden * hidden * -0.5) * (1.0 / math.sqrt(2.0 * math.pi))
    return hidden * normal, normal + hidden * density


def project(stream, chunk, layer, pair, refs, outs, first_full):
    gain, shift, weight, bias, fixed, frames = refs
    query_ref, key_ref, value_ref, first_ref, unit_ref, scale_ref = outs
    unit, scale = normed(stream)
    keep_norm(unit, scale, unit_ref, scale_ref)
    first = (unit * gain[layer : layer + 1, :] + shift[layer : layer + 1, :]).astype(BF16)
    first_full[...] = first
    first_ref[...] = first_full[:, at(pair * PAIR, PAIR)]
    tables = tables_of(fixed, frames, chunk)
    query = nn(first, weight[0]) + bias[0, layer : layer + 1, :]
    query_ref[...] = (turn(query, tables) * SCORE_SCALE).astype(BF16)
    key = nn(first, weight[1]) + bias[1, layer : layer + 1, :]
    key_ref[...] = turn(key, tables).astype(BF16)
    value = nn(first, weight[2]) + bias[2, layer : layer + 1, :]
    value_ref[...] = value.astype(BF16)


class Relay:
    sems = 6

    def __init__(self, n, rows, buffer, other, sems, lives=None, live_other=None):
        self.n, self.rows, self.buffer, self.other = n, rows, buffer, other
        self.lives, self.live_other = lives, live_other
        self.z_send, self.z_recv, self.y_send, self.y_recv, self.c_send, self.c_recv = sems
        self.planes = n // 4
        self.me, self.core = lax.axis_index("seq"), lax.axis_index("tp")
        me = self.me
        self.x, self.y, self.z = lax.rem(me, 2), lax.rem(me // 2, 2), me // 4
        self.across = me + 2 - 4 * self.y

    @staticmethod
    def scratch(n):
        dma, planes = pltpu.SemaphoreType.DMA, n // 4
        shapes = [(planes, 2, 2)] * 2 + [(planes, 2)] * 2 + [(2 * planes,)] * 2
        return [dma(shape) for shape in shapes]

    @property
    def events(self):
        return self.planes

    def plane(self, step):
        return lax.rem(self.z + step, self.planes)

    def place(self, plane, lane):
        return plane * 4 + self.y * 2 + lane

    def reached(self):
        return [(step, far) for step in range(self.planes) for far in (0, 1) if step or far]

    def hello(self):
        barrier = pltpu.get_barrier_semaphore()
        partners = [(self.across, self.core), (self.me, 1 - self.core)]
        for step, far in self.reached():
            lane = 1 - self.x if far else self.x
            partners.append((self.place(self.plane(step), lane), self.core))
        for seq, tp in partners:
            pl.semaphore_signal(barrier, inc=1, device_id=(seq, tp), device_id_type=MESH)

    def met(self):
        pl.semaphore_wait(pltpu.get_barrier_semaphore(), 2 + len(self.reached()))

    def rows_of(self, side, seq):
        return self.buffer.at[side, at(seq * self.rows, self.rows), :]

    def block(self, side, pair):
        return self.buffer.at[side, at(pair * 2 * self.rows, 2 * self.rows), :]

    def items(self, pair):
        found = [self.block(self.core, pair)]
        if self.lives is not None:
            found.append(self.lives.at[at(pair * 2, 2)])
        return found

    def each(self, copy, what):
        for index in range(1 if self.lives is None else 2):
            getattr(copy(index), what)()

    def z_copy(self, step, far):
        def copy(index):
            lane = 1 - self.x if far else self.x
            if index == 0:
                source = self.other.at[self.core] if far else self.rows_of(self.core, self.me)
                target = self.rows_of(self.core, self.me)
            else:
                source = self.live_other if far else self.lives.at[self.me]
                target = self.lives.at[self.me]
            return remote(
                source,
                target,
                self.z_send.at[step, far, index],
                self.z_recv.at[step, far, index],
                self.place(self.plane(step), lane),
                self.core,
            )

        return copy

    def y_copy(self, plane, row):
        def copy(index):
            item = self.items(plane * 2 + row)[index]
            return remote(
                item,
                item,
                self.y_send.at[plane, index],
                self.y_recv.at[plane, index],
                self.across,
                self.core,
            )

        return copy

    def c_copy(self, pair, side):
        item = self.block(side, pair)
        return remote(
            item, item, self.c_send.at[pair], self.c_recv.at[pair], self.me, 1 - self.core
        )

    def begin(self):
        for step, far in self.reached():
            self.each(self.z_copy(step, far), "start")

    def arrive(self, event):
        for far in (0, 1) if event else (1,):
            self.each(self.z_copy(event, far), "wait_recv")
        plane = self.plane(self.planes - event)
        self.each(self.y_copy(plane, self.y), "start")
        self.c_copy(plane * 2 + self.y, self.core).start()

    def complete(self, event):
        plane = self.plane(self.planes - event)
        self.each(self.y_copy(plane, 1 - self.y), "wait_recv")
        self.c_copy(plane * 2 + 1 - self.y, self.core).start()

    def wait_straight(self):
        for step, far in self.reached():
            self.each(self.z_copy(step, far), "wait_recv")
        for step, far in self.reached():
            self.each(self.z_copy(step, far), "wait_send")

    def cross(self, plane):
        self.each(self.y_copy(plane, self.y), "start")
        self.c_copy(plane * 2 + self.y, self.core).start()

    def straight(self, some):
        for step, far in self.reached()[some]:
            self.each(self.z_copy(step, far), "start")

    def crossed(self, plane):
        self.each(self.y_copy(plane, 1 - self.y), "wait_recv")
        self.c_copy(plane * 2 + 1 - self.y, self.core).start()

    def wait_crossed(self):
        for pair in range(2 * self.planes):
            self.c_copy(pair, 1 - self.core).wait_recv()
        for plane in range(self.planes):
            self.each(self.y_copy(plane, self.y), "wait_send")
        for pair in range(2 * self.planes):
            self.c_copy(pair, self.core).wait_send()

    def ready(self, event):
        plane = self.plane(self.planes - event)
        self.c_copy(plane * 2, 1 - self.core).wait_recv()
        self.c_copy(plane * 2 + 1, 1 - self.core).wait_recv()
        return plane

    def finish(self):
        for step, far in self.reached():
            self.each(self.z_copy(step, far), "wait_send")
        for plane in range(self.planes):
            self.each(self.y_copy(plane, self.y), "wait_send")
        for pair in range(2 * self.planes):
            self.c_copy(pair, self.core).wait_send()


def split_lanes(values, x, buffer, other, start, rows):
    half = values.shape[2] // 2
    zero, one = values[:, 0, :], values[:, 1, :]
    own, far = jnp.where(x == 0, zero, one), jnp.where(x == 0, one, zero)
    core = lax.axis_index("tp")
    own = jnp.where(core == 0, own[:, :half], own[:, half:]).astype(BF16)
    buffer[core, at(start, rows), :] = own
    for side in range(2):
        other[side] = far[:, side * half : (side + 1) * half].astype(BF16)


def gather_and_project(tokens, live, episode_frames, gain, shift, qkv, bias, fixed, ahead, n):
    rows, lanes, width = tokens.shape
    half = width // 2
    total = n * rows
    chunks = total // FRAME
    per_frame = FRAME // rows
    features = qkv.shape[3]
    slots = episode_frames.shape[1]

    def kernel(*refs):
        refs = list(refs)

        def take(count):
            taken = refs[:count]
            del refs[:count]
            return taken

        tokens_ref, live_ref, counts_ref, gain_ref, shift_ref, w_any, bias_ref = take(7)
        fixed_ref, ahead_ref = take(2)
        all_ref, mask_ref, frames_ref = take(3)
        projected = take(6)
        other, lives, live_other, weight, full, w_sem = take(6)
        relay = Relay(n, rows, all_ref, other, take(Relay.sems), lives, live_other)
        load = pltpu.make_async_copy(w_any.at[0], weight, w_sem)
        load.start()
        relay.hello()
        x, me = relay.x, relay.me
        split_lanes(tokens_ref[...].astype(F32), x, all_ref, other, me * rows, rows)
        lane = lax.broadcasted_iota(jnp.int32, (1, FRAME), 1)
        here = lane // rows == lax.rem(me, per_frame)
        tiles = []
        for index in range(lanes):
            alive = live_ref[index : index + 1, :].astype(F32)
            alive = jnp.where(here, jnp.concatenate([alive] * per_frame, axis=1), 0.0)
            tiles.append(jnp.broadcast_to(alive, (8, FRAME)))
        lives[me] = jnp.where(x == 0, tiles[0], tiles[1])
        live_other[...] = jnp.where(x == 0, tiles[1], tiles[0])
        relay.met()
        relay.begin()

        counts = [counts_ref[x, slot] for slot in range(slots)]
        episodes, openings = [], []
        for frame in range(chunks):
            end, episode, opening = 0, 0, 0
            for slot in range(slots):
                end = end + counts[slot]
                passed = frame >= end
                episode = episode + passed.astype(jnp.int32)
                opening = opening + jnp.where(passed, counts[slot], 0)
            episodes.append(episode)
            openings.append(frame - opening)
        for index in range(3):
            table = []
            for frame in range(chunks):
                line = jnp.zeros((1, PAIR), F32)
                for choice in range(chunks):
                    line = jnp.where(
                        openings[frame] == choice, ahead_ref[index, choice : choice + 1, :], line
                    )
                table.append(line)
            frames_ref[index] = jnp.concatenate(
                table + [jnp.zeros((8 - chunks, PAIR), F32)], axis=0
            )
        load.wait()

        def project_frame(frame):
            place = at(frame * FRAME, FRAME)
            stream = jnp.concatenate([all_ref[0, place, :], all_ref[1, place, :]], axis=1)
            project(
                stream.astype(F32),
                frame,
                0,
                me // 2,
                (gain_ref, shift_ref, weight, bias_ref, fixed_ref, frames_ref),
                [ref.at[place, :] for ref in projected],
                full,
            )

        for event in range(relay.events):
            relay.arrive(event)
            if event:
                relay.complete(event - 1)
            if event > 1:
                project_frame(relay.ready(event - 2))
        relay.complete(relay.events - 1)
        for event in range(max(0, relay.events - 2), relay.events):
            project_frame(relay.ready(event))
        relay.finish()

        for key_frame in range(chunks):
            alive = lives[key_frame * per_frame, 0:1, :]
            for part in range(1, per_frame):
                alive = alive + lives[key_frame * per_frame + part, 0:1, :]
            closed = (alive - 1.0) * -MASKED
            lines = []
            for query_frame in range(chunks):
                allowed = (episodes[query_frame] == episodes[key_frame]) & (
                    openings[key_frame] <= openings[query_frame]
                )
                lines.append(jnp.where(allowed, closed, MASKED))
            lines.append(jnp.zeros((PAIR - chunks, FRAME), F32))
            mask_ref[key_frame * FRAME : (key_frame + 1) * FRAME, :] = jnp.concatenate(
                lines, axis=0
            ).T.astype(BF16)

    in_vmem = pl.BlockSpec(memory_space=pltpu.VMEM)
    in_smem = pl.BlockSpec(memory_space=pltpu.SMEM)
    projected = jax.ShapeDtypeStruct((total, features), BF16)
    return pl.pallas_call(
        kernel,
        out_shape=(
            jax.ShapeDtypeStruct((2, total, half), BF16),
            jax.ShapeDtypeStruct((total, PAIR), BF16),
            jax.ShapeDtypeStruct((3, 8, PAIR), F32),
            projected,
            projected,
            projected,
            jax.ShapeDtypeStruct((total, PAIR), BF16),
            jax.ShapeDtypeStruct((total, width), BF16),
            jax.ShapeDtypeStruct((total, PAIR), F32),
        ),
        in_specs=[in_vmem, in_vmem, in_smem, in_vmem, in_vmem, ANYWHERE] + [in_vmem] * 3,
        out_specs=(in_vmem,) * 9,
        scratch_shapes=[
            pltpu.VMEM((2, rows, half), BF16),
            pltpu.VMEM((n, 8, FRAME), F32),
            pltpu.VMEM((8, FRAME), F32),
            pltpu.VMEM(qkv.shape[1:], BF16),
            pltpu.VMEM((FRAME, width), BF16),
            pltpu.SemaphoreType.DMA,
        ]
        + Relay.scratch(n),
        compiler_params=pltpu.CompilerParams(
            collective_id=0, has_side_effects=True, vmem_limit_bytes=VMEM_BYTES
        ),
        name="gather_and_project",
    )(tokens, live, episode_frames, gain, shift, qkv, bias, fixed, ahead)


def halves(ref):
    return jnp.concatenate([ref[0], ref[1]], axis=1).astype(F32)


def halves_spec(shape, chunks, behind, span=FRAME):
    return pl.BlockSpec(
        (2, span, shape[2]), lambda s: (0, jnp.clip(s - behind, 0, chunks - 1), 0)
    )


def layer_forward(layer, query, key, value, key_bias, stream, mats, rows_of, next_refs, d_out, d_part, n, identity):
    first_phase = d_out is not None
    carried = d_out if first_phase else d_part
    total, features = query.shape
    split = stream.ndim == 3
    width = mats[1].shape[1]
    rows_here = total // n
    hidden_units = mats[1].shape[2]
    chunks = total // FRAME
    heads = features // HEAD_DIM
    slabs = features // PAIR
    columns = 256
    last = next_refs is None
    b_out, gain, shift, b_up, b_down = rows_of
    mat_out, mat_up, mat_down = mats

    def kernel(*refs):
        refs = list(refs)

        def take(count):
            taken = refs[:count]
            del refs[:count]
            return taken

        q_ref, k_ref, v_ref, kb_ref, x_ref = take(5)
        wo_any, wu_any, wd_any = take(3)
        bo_ref, gain_ref, shift_ref, bu_ref, bd_ref = take(5)
        if not last:
            wq_any, ngain, nshift, nbias, fixed, frames = take(6)
        (d_ref,) = take(1)
        p_ref, r_ref, mixed_ref, unit_ref, scale_ref, second_ref, act_ref, gp_ref, x_out = take(9)
        if not last:
            next_outs = take(6)
        (d_to,) = take(1)
        wo, wu, wd, mid, full, next_full = take(6)
        if not last:
            (wq,) = take(1)
        a_send, a_recv, b_send, b_recv, w_sem, send_sem, recv_sem = take(7)
        buffer, other, d_sem = take(3)
        relay = Relay(n, rows_here, buffer, other, take(Relay.sems))

        step = pl.program_id(0)
        me, core = lax.axis_index("seq"), lax.axis_index("tp")

        items = [(wo_any, wo), (wu_any, wu), (wd_any, wd)]
        if not last:
            items.append((wq_any, wq))

        def load(index):
            source, target = items[index]
            return pltpu.make_async_copy(
                source.at[layer if index < 3 else layer + 1], target, w_sem.at[index]
            )

        def exchange(kind, chunk):
            source, target = ((a_send, a_recv), (b_send, b_recv))[kind]
            return Exchange(
                source.at[chunk],
                target.at[chunk],
                send_sem.at[kind, chunk],
                recv_sem.at[kind, chunk],
                me,
                core,
            )

        partners = [(relay.across, core), (me, 1 - core)]

        @pl.when(step == 0)
        def _():
            for index in range(len(items)):
                load(index).start()
            if first_phase:
                relay.hello()
                split_lanes(d_ref[...], relay.x, buffer, other, me * rows_here, rows_here)
            else:
                fetch = pltpu.make_async_copy(d_ref, buffer.at[core], d_sem)
                fetch.start()
                fetch.wait()
                hello(partners)

        lane = lax.broadcasted_iota(jnp.int32, (1, PAIR), 1)
        sides = [(lane < HEAD_DIM).astype(F32).astype(BF16), (lane >= HEAD_DIM).astype(F32).astype(BF16)]
        for frame in range(chunks):

            @pl.when(step == frame)
            def _():
                keys = FRAME * (frame + 1)
                mask = kb_ref[:keys, :]
                asked = jnp.broadcast_to((lane == frame).astype(F32), (FRAME, PAIR)).astype(BF16)

                slab_lanes = [slice(slab * PAIR, (slab + 1) * PAIR) for slab in range(slabs)]

                def score(head):
                    lanes, side = slab_lanes[head // 2], head % 2
                    key = jnp.concatenate([k_ref[:keys, lanes], mask], axis=1)
                    return nt(jnp.concatenate([q_ref[:, lanes] * sides[side], asked], axis=1), key)

                scores, sums = score(0), []
                for head in range(heads):
                    lanes, side = slab_lanes[head // 2], head % 2
                    following = score(head + 1) if head + 1 < heads else None
                    highest = jnp.max(scores, axis=1, keepdims=True)
                    shifted = jnp.exp(scores - highest).astype(BF16)
                    p_ref[0, head, :keys, :] = shifted.T
                    sums.append(nn(shifted, v_ref[:keys, lanes] * sides[side] + sides[1 - side]))
                    scores = following
                    if side == 1:
                        one, two = sums[head - 1 :]
                        low_side = lane < HEAD_DIM
                        divisor = 1.0 / jnp.where(
                            low_side, pltpu.roll(one, HEAD_DIM, 1), pltpu.roll(two, HEAD_DIM, 1)
                        )
                        r_ref[:, lanes] = divisor
                        mixed_ref[:, lanes] = (jnp.where(low_side, one, two) * divisor).astype(BF16)

        @pl.when(step == 0)
        def _():
            load(0).wait()
            if first_phase:
                relay.met()
            else:
                met(partners)

        @pl.when(step < chunks)
        def _():
            a_send[step] = nn(mixed_ref[...], wo[...]).astype(BF16)
            exchange(0, step).start()

        def feed_forward():
            chunk = step - 1
            middle = (halves(x_ref) if split else x_ref[...]) + (
                a_send[chunk].astype(F32) + a_recv[chunk].astype(F32)
            )
            middle = middle + bo_ref[layer : layer + 1, :]
            mid[lax.rem(chunk, 2)] = middle
            unit, scale = normed(middle)
            keep_norm(unit, scale, unit_ref, scale_ref)
            second = (unit * gain_ref[layer : layer + 1, :] + shift_ref[layer : layer + 1, :]).astype(BF16)
            full[...] = second
            second_ref[...] = full[:, at((me // 2) * PAIR, PAIR)]
            parts = [slice(start, start + columns) for start in range(0, hidden_units, columns)]
            hidden = nn(second, wu[:, parts[0]])
            for index, part in enumerate(parts):
                following = nn(second, wu[:, parts[index + 1]]) if index + 1 < len(parts) else None
                act, slope = gelu_both(hidden + bu_ref[layer : layer + 1, part])
                act_ref[:, part] = act.astype(BF16)
                gp_ref[:, part] = slope.astype(BF16)
                hidden = following
            b_send[chunk] = nn(act_ref[...], wd[...]).astype(BF16)

        def close():
            chunk = step - 2
            result = mid[lax.rem(chunk, 2)] + (b_send[chunk].astype(F32) + b_recv[chunk].astype(F32))
            result = result + bd_ref[layer : layer + 1, :]
            x_out[...] = result
            if not last:
                project(
                    result,
                    chunk,
                    layer + 1,
                    me // 2,
                    (ngain, nshift, wq, nbias, fixed, frames),
                    next_outs,
                    next_full,
                )

        @pl.when(step == 1)
        def _():
            load(1).wait()
            load(2).wait()

        @pl.when((step >= 1) & (step <= chunks))
        def _():
            exchange(0, step - 1).wait_recv()
            feed_forward()
            exchange(1, step - 1).start()

        sends = len(relay.reached())
        for index in range(chunks - 1):

            @pl.when(step == index)
            def _():
                if first_phase:
                    relay.straight(slice(sends * index // (chunks - 1), sends * (index + 1) // (chunks - 1)))
                else:
                    planes = relay.planes
                    for plane in range(planes * index // (chunks - 1), planes * (index + 1) // (chunks - 1)):
                        relay.cross(plane)

        if not first_phase:

            @pl.when(step == chunks)
            def _():
                for plane in range(relay.planes):
                    relay.crossed(plane)

        if not last:

            @pl.when(step == 2)
            def _():
                load(3).wait()

        @pl.when(step >= 2)
        def _():
            exchange(1, step - 2).wait_recv()
            close()

        @pl.when(step == chunks + 1)
        def _():
            if first_phase:
                relay.wait_straight()
            else:
                relay.wait_crossed()
            keep = pltpu.make_async_copy(buffer.at[core] if first_phase else buffer, d_to, d_sem)
            keep.start()
            keep.wait()
            for kind in range(2):
                for chunk in range(chunks):
                    exchange(kind, chunk).wait_send()

    def rows(columns, behind):
        return pl.BlockSpec(
            (FRAME, columns), lambda s: (jnp.clip(s - behind, 0, chunks - 1), 0)
        )

    in_specs = [rows(features, 0), whole(key), whole(value), whole(key_bias)]
    in_specs += [halves_spec(stream.shape, chunks, 1) if split else rows(width, 1)]
    in_specs += [ANYWHERE] * 3 + [whole(item) for item in rows_of]
    operands = [query, key, value, key_bias, stream, *mats, *rows_of]
    if not last:
        in_specs += [ANYWHERE] + [whole(item) for item in next_refs[1:]]
        operands += list(next_refs)
    in_specs += [whole(carried) if first_phase else ANYWHERE]
    operands += [carried]
    out_shape = [
        jax.ShapeDtypeStruct((chunks, heads, total, FRAME), BF16),
        jax.ShapeDtypeStruct((total, features), F32),
        jax.ShapeDtypeStruct((total, features), BF16),
        jax.ShapeDtypeStruct((total, width), BF16),
        jax.ShapeDtypeStruct((total, PAIR), F32),
        jax.ShapeDtypeStruct((total, PAIR), BF16),
        jax.ShapeDtypeStruct((total, hidden_units), BF16),
        jax.ShapeDtypeStruct((total, hidden_units), BF16),
        jax.ShapeDtypeStruct((total, width), F32),
    ]
    out_specs = [
        pl.BlockSpec((1, heads, total, FRAME), lambda s: (jnp.minimum(s, chunks - 1), 0, 0, 0)),
        rows(features, 0),
        rows(features, 0),
        rows(width, 1),
        rows(PAIR, 1),
        rows(PAIR, 1),
        rows(hidden_units, 1),
        rows(hidden_units, 1),
        rows(width, 2),
    ]
    scratch = [
        pltpu.VMEM(mat_out.shape[1:], BF16),
        pltpu.VMEM(mat_up.shape[1:], BF16),
        pltpu.VMEM(mat_down.shape[1:], BF16),
        pltpu.VMEM((2, FRAME, width), F32),
        pltpu.VMEM((FRAME, width), BF16),
        pltpu.VMEM((FRAME, width), BF16),
    ]
    if not last:
        out_shape += [jax.ShapeDtypeStruct((total, features), BF16)] * 3
        out_shape += [jax.ShapeDtypeStruct((total, PAIR), BF16)]
        out_shape += [jax.ShapeDtypeStruct((total, width), BF16)]
        out_shape += [jax.ShapeDtypeStruct((total, PAIR), F32)]
        out_specs += [rows(features, 2)] * 3 + [rows(PAIR, 2), rows(width, 2), rows(PAIR, 2)]
        scratch += [pltpu.VMEM(next_refs[0].shape[1:], BF16)]
    d_shape = (total, width // 2) if first_phase else (2, total, width // 2)
    out_shape += [jax.ShapeDtypeStruct(d_shape, BF16)]
    out_specs += [ANYWHERE]
    scratch += [pltpu.VMEM((chunks, FRAME, width), BF16)] * 4
    scratch += [
        pltpu.SemaphoreType.DMA((4,)),
        pltpu.SemaphoreType.DMA((2, chunks, Exchange.pieces)),
        pltpu.SemaphoreType.DMA((2, chunks, Exchange.pieces)),
    ]
    scratch += [
        pltpu.VMEM((2, total, width // 2), BF16),
        pltpu.VMEM((2, rows_here, width // 2), BF16),
        pltpu.SemaphoreType.DMA,
    ]
    scratch += Relay.scratch(n)
    return pl.pallas_call(
        kernel,
        grid=(chunks + 2,),
        out_shape=out_shape,
        in_specs=in_specs,
        out_specs=out_specs,
        scratch_shapes=scratch,
        compiler_params=pltpu.CompilerParams(
            collective_id=identity, has_side_effects=True, vmem_limit_bytes=VMEM_BYTES
        ),
        name=f"layer_forward_{layer}",
    )(*operands)


class Swap:
    def __init__(self, ships, lane_rows):
        self.ships, self.lane_rows = ships, lane_rows
        self.count = len(ships) + len(lane_rows)

    def operands(self):
        return [*self.ships, *[item for item, _ in self.lane_rows]]

    def in_specs(self):
        return [whole(item) for item in self.ships] + [ANYWHERE] * len(self.lane_rows)

    def outputs(self):
        shapes, specs = [], []
        for item in self.ships:
            shape = (item.shape[0] // 2, item.shape[1])
            shapes.append(jax.ShapeDtypeStruct(shape, F32))
            specs.append(whole_out(shape))
        for item, count in self.lane_rows:
            shapes.append(jax.ShapeDtypeStruct((count or item.shape[0], item.shape[1]), item.dtype))
            specs.append(ANYWHERE)
        return shapes, specs

    def scratch(self):
        if not self.count:
            return []
        buffers = [pltpu.VMEM((item.shape[0] // 2, item.shape[1]), BF16) for item in self.ships]
        return buffers * 2 + [pltpu.SemaphoreType.DMA((self.count,))] * 2

    def bind(self, sources, targets, scratch):
        ships = len(self.ships)
        me, core = lax.axis_index("seq"), lax.axis_index("tp")
        x = lax.rem(me, 2)
        beside = me + 1 - 2 * x
        half = PAIR // 2

        def copy(index):
            if index < ships:
                source, target = scratch[index], scratch[ships + index]
            else:
                source, target = sources[index], targets[index]
                count = self.lane_rows[index - ships][1]
                if count:
                    source = source.at[at(beside * count, count), :]
            send, recv = scratch[2 * ships].at[index], scratch[2 * ships + 1].at[index]
            return remote(source, target, send, recv, beside, core)

        def start():
            for index in range(self.count):
                if index < ships:
                    scratch[index][...] = sources[index][at((1 - x) * half, half), :].astype(BF16)
                copy(index).start()

        def finish():
            for index in range(self.count):
                copy(index).wait_recv()
                if index < ships:
                    own = sources[index][at(x * half, half), :]
                    targets[index][...] = own + scratch[ships + index][...].astype(F32)
            for index in range(self.count):
                copy(index).wait_send()

        return start, finish


def attention_backward(
    probs, divisor, mixed, query, key, value, grad_mixed, first, fixed, frames, swap, swap_qkv, identity
):
    total, features = query.shape
    chunks = total // FRAME
    slabs = features // PAIR
    half = PAIR // 2

    def kernel(*refs):
        refs = list(refs)

        def take(count):
            taken = refs[:count]
            del refs[:count]
            return taken

        p_ref, r_ref, o_ref, q_ref, k_ref, v_ref, g_ref, first_ref, fixed_ref, frames_ref = take(10)
        sources = take(swap.count)
        dq_ref, dk_ref, dv_ref, qkv_out = take(4)
        targets = take(swap.count)
        dk_sum, dv_sum, first_turned = take(3)
        if swap_qkv:
            qkv_own, qkv_send, qkv_recv, qkv_sems = take(4)
        start, finish = swap.bind(sources, targets, refs)

        step = pl.program_id(0)
        me, core = lax.axis_index("seq"), lax.axis_index("tp")
        x = lax.rem(me, 2)
        beside = me + 1 - 2 * x

        def qkv_copy(slab):
            return remote(
                qkv_send.at[slab],
                qkv_recv.at[slab],
                qkv_sems.at[0, slab],
                qkv_sems.at[1, slab],
                beside,
                core,
            )

        @pl.when(step == 0)
        def _():
            hello([(beside, core)])
            first_turned[...] = first_ref[...].T
            met([(beside, core)])
            start()

        lane = lax.broadcasted_iota(jnp.int32, (1, PAIR), 1)
        sides = [(lane < HEAD_DIM).astype(F32).astype(BF16), (lane >= HEAD_DIM).astype(F32).astype(BF16)]
        turned = k_ref[...].T
        ones = jnp.broadcast_to((lane < 2).astype(F32), (total, PAIR)).astype(BF16)
        values = jnp.concatenate([v_ref[...], ones], axis=1)

        def give(frame):
            keys = FRAME * (frame + 1)
            own = slice(frame * FRAME, keys)
            scaled = (g_ref[own, :].astype(F32) * r_ref[own, :]).astype(BF16)
            inner = scaled.astype(F32) * o_ref[own, :].astype(F32)
            grads, q_parts, g_parts = [], [], []
            for side in range(2):
                delta = jnp.sum(
                    jnp.where((lane < HEAD_DIM) == (side == 0), inner, 0.0), axis=1, keepdims=True
                )
                coarse = delta.astype(BF16).astype(F32)
                rest = jnp.where(lane == 0, -coarse, jnp.where(lane == 1, coarse - delta, 0.0))
                g2 = scaled * sides[side]
                grads.append(nt(values[:keys], jnp.concatenate([g2, rest.astype(BF16)], axis=1)))
                q_parts.append(q_ref[own, :] * sides[side])
                g_parts.append(g2)
            return grads, jnp.concatenate(q_parts, axis=0), jnp.concatenate(g_parts, axis=0)

        given = give(chunks - 1)
        for frame in reversed(range(chunks)):
            keys = FRAME * (frame + 1)
            own = slice(frame * FRAME, keys)
            tables = tables_of(fixed_ref, frames_ref, frame)
            grads, q_part, g_part = given
            given = give(frame - 1) if frame else None
            query_parts, score_parts, prob_parts = [], [], []
            for side in range(2):
                attention = p_ref[frame, side, :keys, :]
                grad_scores = (attention.astype(F32) * grads[side]).astype(BF16)
                query_parts.append(nn(turned[side * HEAD_DIM : (side + 1) * HEAD_DIM, :keys], grad_scores))
                score_parts.append(grad_scores)
                prob_parts.append(attention)
            grad_query = jnp.concatenate(query_parts, axis=0).T
            key_parts = nn(jnp.concatenate(score_parts, axis=1), q_part)
            value_parts = nn(jnp.concatenate(prob_parts, axis=1), g_part)
            dq_ref[own, :] = (turn(grad_query, tables, True) * SCORE_SCALE).astype(BF16)
            if frame == chunks - 1:
                dk_sum[...] = key_parts
                dv_sum[...] = value_parts
            else:
                dk_sum[:keys, :] += key_parts
                dv_sum[:keys, :] += value_parts
            dk_ref[own, :] = turn(dk_sum[own, :], tables, True).astype(BF16)
            dv_ref[own, :] = dv_sum[own, :].astype(BF16)

        for part, ref in enumerate((dq_ref, dk_ref, dv_ref)):
            piece = slice(part * PAIR, (part + 1) * PAIR)
            terms = nn(first_turned[...], ref[...])
            if swap_qkv:
                qkv_own[step, :, piece] = terms
                qkv_send[step, :, piece] = qkv_own[step, at((1 - x) * half, half), piece].astype(BF16)
            else:
                qkv_out[:, at(part * features + step * PAIR, PAIR)] = terms
        if swap_qkv:
            qkv_copy(step).start()

        @pl.when(step == slabs - 1)
        def _():
            finish()
            for slab in range(slabs if swap_qkv else 0):
                qkv_copy(slab).wait_recv()
                for part in range(3):
                    piece = slice(part * PAIR, (part + 1) * PAIR)
                    place = part * features + slab * PAIR
                    qkv_out[:, place : place + PAIR] = qkv_own[
                        slab, at(x * half, half), piece
                    ] + qkv_recv[slab, :, piece].astype(F32)
            for slab in range(slabs if swap_qkv else 0):
                qkv_copy(slab).wait_send()

    slab = pl.BlockSpec((total, PAIR), lambda s: (0, s))
    in_specs = [pl.BlockSpec((chunks, 2, total, FRAME), lambda s: (0, s, 0, 0))]
    in_specs += [slab] * 6 + [whole(first), whole(fixed), whole(frames)]
    in_specs += swap.in_specs()
    qkv_shape = (half if swap_qkv else PAIR, 3 * features)
    shapes, specs = swap.outputs()
    out_shape = [jax.ShapeDtypeStruct((total, features), BF16)] * 3
    out_shape += [jax.ShapeDtypeStruct(qkv_shape, F32)] + shapes
    out_specs = [slab] * 3 + [whole_out(qkv_shape)] + specs
    scratch = [pltpu.VMEM((total, PAIR), F32)] * 2 + [pltpu.VMEM((PAIR, total), BF16)]
    if swap_qkv:
        scratch += [pltpu.VMEM((slabs, PAIR, 3 * PAIR), F32)]
        scratch += [pltpu.VMEM((slabs, half, 3 * PAIR), BF16)] * 2
        scratch += [pltpu.SemaphoreType.DMA((2, slabs))]
    scratch += swap.scratch()
    return pl.pallas_call(
        kernel,
        grid=(slabs,),
        out_shape=out_shape,
        in_specs=in_specs,
        out_specs=out_specs,
        scratch_shapes=scratch,
        compiler_params=pltpu.CompilerParams(
            collective_id=identity, has_side_effects=True, vmem_limit_bytes=VMEM_BYTES
        ),
        name=f"attention_backward_{identity}",
    )(
        probs,
        divisor,
        mixed,
        query,
        key,
        value,
        grad_mixed,
        first,
        fixed,
        frames,
        *swap.operands(),
    )


def rows_backward(entry, upper, identity, span, swap):
    top, bottom = len(entry) == 1, upper is None
    if not top:
        above, entry = entry[0], entry[1:]
    total = entry[0].shape[1] if top else entry[0].shape[0]
    chunks = total // span
    columns = 256
    ahead = 0 if top else 2 if bottom else 1
    if top:
        width = 2 * entry[0].shape[2]
    else:
        features, width = entry[0].shape[1], entry[5].shape[1]
    if not bottom:
        layer = upper[0]
        hidden_units, mixed_features = upper[1].shape[1], upper[6].shape[1]
    place_rows = total // lax.axis_size("seq")

    def kernel(*refs):
        refs = list(refs)

        def take(count):
            taken = refs[:count]
            del refs[:count]
            return taken

        if top:
            (d_out_ref,) = take(1)
        else:
            dq_ref, dk_ref, dv_ref, unit1, scale1, dm_ref, wq, gain1 = take(8)
        if not bottom:
            act_ref, gp_ref, unit2, scale2, second_ref, mixed_ref = take(6)
            wo_any, wu_any, wd_any, gain2 = take(4)
        sources = take(swap.count)
        if not top:
            (vec1,) = take(1)
        if not bottom:
            dmid_out, dmix_out, out_sum, up_sum, down_sum, vec2 = take(6)
        else:
            dx_out, dx_other, vec_other = take(3)
        targets = take(swap.count)
        if not top:
            a_send, a_recv = take(2)
        if not bottom:
            b_send, b_recv, grad_keep, hidden_keep, low_keep, last_keep, wo, wu, wd, w_sem = take(10)
        else:
            dx_keep, dx_send, dx_recv, vec_recv, x_send_sem, x_recv_sem = take(6)
        send_sem, recv_sem = take(2)
        start_swap, finish_swap = swap.bind(sources, targets, refs)

        step = pl.program_id(0)
        me, core = lax.axis_index("seq"), lax.axis_index("tp")
        pair = at((me // 2) * PAIR, PAIR)
        x = lax.rem(me, 2)
        beside = me + 1 - 2 * x

        def exchange(kind, chunk):
            source, target = (a_send, a_recv) if kind == 0 else (b_send, b_recv)
            return Exchange(
                source.at[chunk],
                target.at[chunk],
                send_sem.at[kind, chunk],
                recv_sem.at[kind, chunk],
                me,
                core,
            )

        def load(index):
            source, target = ((wd_any, wd), (wu_any, wu), (wo_any, wo))[index]
            return pltpu.make_async_copy(source.at[layer], target, w_sem.at[index])

        partners = [(me, 1 - core)] + ([(beside, core)] if bottom or swap.count else [])

        @pl.when(step == 0)
        def _():
            if not bottom:
                for index in range(3):
                    load(index).start()
                out_sum[...] = jnp.zeros_like(out_sum)
                up_sum[...] = jnp.zeros_like(up_sum)
                down_sum[...] = jnp.zeros_like(down_sum)
                vec2[...] = jnp.zeros_like(vec2)
            if not top:
                vec1[...] = jnp.zeros_like(vec1)
            hello(partners)

        def meet():
            @pl.when(step == 0)
            def _():
                met(partners)
                start_swap()

        def entry_products():
            partial = None
            for part, ref in enumerate((dq_ref, dk_ref, dv_ref)):
                grad = ref[...]
                term = nt(grad, wq[0, part])
                partial = term if partial is None else partial + term
                vec1[part : part + 1, :] += column_sum(grad.astype(F32))
            a_send[step] = partial.astype(BF16)

        def entry_norm(chunk):
            if top:
                return halves(d_out_ref)
            grad_first = a_send[chunk].astype(F32) + a_recv[chunk].astype(F32)
            unit, scale = kept_norm(unit1, scale1)
            for start, sums in ((3, column_sum(grad_first * unit)), (5, column_sum(grad_first))):
                for side in range(width // features):
                    piece = slice(side * features, (side + 1) * features)
                    vec1[start + side : start + side + 1, :] += sums[:, piece]
            return dm_ref[...] + norm_pull(grad_first, gain1[above : above + 1, :], unit, scale)

        def feed_forward(between=None):
            chunk = step - ahead
            gradient = entry_norm(chunk)
            if bottom:
                dx_keep[at(chunk * span, span), :] = gradient
                return
            grad_keep[lax.rem(chunk, 2)] = gradient
            vec2[1:2, :width] += column_sum(gradient)
            low = gradient.astype(BF16)
            low_keep[...] = low
            low_columns = low_keep[:, pair]
            second = second_ref[...]
            parts = [slice(start, start + columns) for start in range(0, hidden_units, columns)]
            grad_act = nt(low, wd[parts[0], :])
            for index, part in enumerate(parts):
                following = nt(low, wd[parts[index + 1], :]) if index + 1 < len(parts) else None
                grad_hidden = grad_act * gp_ref[:, part].astype(F32)
                hidden_keep[:, part] = grad_hidden.astype(BF16)
                vec2[0:1, part] += column_sum(grad_hidden)
                grad_act = following
            if between is not None:
                between()
            b_send[chunk] = nt(hidden_keep[...], wu[...]).astype(BF16)
            down_sum[...] += tn(low_columns, act_ref[...])
            up_sum[...] += tn(second, hidden_keep[...])

        def close():
            chunk = step - ahead - 1
            grad_second = b_send[chunk].astype(F32) + b_recv[chunk].astype(F32)
            unit, scale = kept_norm(unit2, scale2)
            vec2[2:3, :width] += column_sum(grad_second * unit)
            vec2[3:4, :width] += column_sum(grad_second)
            grad_middle = grad_keep[lax.rem(chunk, 2)] + norm_pull(
                grad_second, gain2[layer : layer + 1, :], unit, scale
            )
            dmid_out[...] = grad_middle
            vec2[4:5, :width] += column_sum(grad_middle)
            low = grad_middle.astype(BF16)
            last_keep[...] = low
            out_sum[...] += tn(last_keep[:, pair], mixed_ref[...])
            dmix_out[...] = nt(low, wo[...]).astype(BF16)

        if not top:

            @pl.when(step < chunks)
            def _():
                entry_products()
                meet()
                exchange(0, step).start()

        @pl.when((step >= ahead) & (step < chunks + ahead))
        def _():
            if not top:
                exchange(0, step - ahead).wait_recv()
            if not bottom:

                @pl.when(step == ahead)
                def _():
                    load(0).wait()

            feed_forward(lambda: pl.when(step == ahead)(lambda: load(1).wait()))
            if not bottom:
                if top:
                    meet()
                exchange(1, step - ahead).start()

        if not bottom:

            @pl.when(step == ahead + 1)
            def _():
                load(2).wait()

            @pl.when(step >= ahead + 1)
            def _():
                exchange(1, step - ahead - 1).wait_recv()
                close()

        if bottom:

            def x_copy(index):
                source, target = ((dx_send, dx_recv), (vec1, vec_recv))[index]
                return remote(
                    source, target, x_send_sem.at[index], x_recv_sem.at[index], beside, core
                )

            @pl.when(step == chunks + 1)
            def _():
                dx_send[...] = dx_keep[at(beside * place_rows, place_rows), :].astype(BF16)
                x_copy(0).start()
                x_copy(1).start()
                dx_out[...] = dx_keep[at(me * place_rows, place_rows), :]
                x_copy(0).wait_recv()
                x_copy(1).wait_recv()
                dx_other[...] = dx_recv[...].astype(F32)
                vec_other[...] = vec_recv[...]
                x_copy(0).wait_send()
                x_copy(1).wait_send()

        @pl.when(step == pl.num_programs(0) - 1)
        def _():
            for kind in ([] if top else [0]) + ([] if bottom else [1]):
                for chunk in range(chunks):
                    exchange(kind, chunk).wait_send()
            finish_swap()

    def rows(columns, behind):
        return pl.BlockSpec(
            (span, columns), lambda s: (jnp.clip(s - behind, 0, chunks - 1), 0)
        )

    vec = jax.ShapeDtypeStruct((8, VEC), F32)
    operands, in_specs, out_shape, out_specs, scratch = [], [], [], [], []
    if top:
        operands += list(entry)
        in_specs += [halves_spec(entry[0].shape, chunks, 0, span)]
    else:
        operands += list(entry)
        in_specs += [rows(features, 0)] * 3
        in_specs += [rows(width, ahead), rows(PAIR, ahead), rows(width, ahead)]
        in_specs += [
            pl.BlockSpec(
                (1, *entry[6].shape[1:]),
                lambda s: (above, 0, 0, 0),
                pipeline_mode=pl.Buffered(1),
            ),
            whole(entry[7]),
        ]
        narrow = jax.ShapeDtypeStruct((8, features), F32)
        out_shape += [narrow]
        out_specs += [whole_out((8, features))]
        scratch += [pltpu.VMEM((chunks, span, width), BF16)] * 2
    if not bottom:
        operands += list(upper[1:])
        in_specs += [rows(hidden_units, ahead)] * 2
        in_specs += [rows(width, ahead + 1), rows(PAIR, ahead + 1), rows(PAIR, ahead)]
        in_specs += [rows(mixed_features, ahead + 1)] + [ANYWHERE] * 3 + [whole(upper[10])]
        sums = [mixed_features, hidden_units, hidden_units]
        out_shape += [
            jax.ShapeDtypeStruct((total, width), F32),
            jax.ShapeDtypeStruct((total, mixed_features), BF16),
        ]
        out_shape += [jax.ShapeDtypeStruct((PAIR, size), F32) for size in sums] + [vec]
        out_specs += [rows(width, ahead + 1), rows(mixed_features, ahead + 1)]
        out_specs += [whole_out((PAIR, size)) for size in sums] + [whole_out((8, VEC))]
        scratch += [pltpu.VMEM((chunks, span, width), BF16)] * 2
        scratch += [
            pltpu.VMEM((2, span, width), F32),
            pltpu.VMEM((span, hidden_units), BF16),
            pltpu.VMEM((span, width), BF16),
            pltpu.VMEM((span, width), BF16),
            pltpu.VMEM(upper[7].shape[1:], BF16),
            pltpu.VMEM(upper[8].shape[1:], BF16),
            pltpu.VMEM(upper[9].shape[1:], BF16),
            pltpu.SemaphoreType.DMA((3,)),
        ]
    else:
        out_shape += [
            jax.ShapeDtypeStruct((place_rows, width), F32),
            jax.ShapeDtypeStruct((place_rows, width), F32),
            narrow,
        ]
        out_specs += [whole_out((place_rows, width))] * 2 + [whole_out((8, features))]
        scratch += [
            pltpu.VMEM((total, width), F32),
            pltpu.VMEM((place_rows, width), BF16),
            pltpu.VMEM((place_rows, width), BF16),
            pltpu.VMEM((8, features), F32),
            pltpu.SemaphoreType.DMA((2,)),
            pltpu.SemaphoreType.DMA((2,)),
        ]
    scratch += [pltpu.SemaphoreType.DMA((2, chunks, Exchange.pieces))] * 2
    operands += swap.operands()
    in_specs += swap.in_specs()
    shapes, specs = swap.outputs()
    out_shape += shapes
    out_specs += specs
    scratch += swap.scratch()
    return pl.pallas_call(
        kernel,
        grid=(chunks + (1 if top else 2),),
        out_shape=out_shape,
        in_specs=in_specs,
        out_specs=out_specs,
        scratch_shapes=scratch,
        compiler_params=pltpu.CompilerParams(
            collective_id=identity, has_side_effects=True, vmem_limit_bytes=VMEM_BYTES
        ),
        name=f"rows_backward_{identity}",
    )(*operands)


def assemble(sums, vecs, lanes, n, features, hidden_units):
    place = lanes[1].shape[0]
    width = lanes[1].shape[1]
    half = PAIR // 2

    def kernel(*refs):
        refs = list(refs)

        def take(count):
            taken = refs[:count]
            del refs[:count]
            return taken

        qkvs, outs, ups, downs = take(LAYERS), take(LAYERS), take(LAYERS), take(LAYERS)
        vec_refs = [take(4) for _ in range(LAYERS)]
        out_lane, out_other, dx_own, dx_other = take(4)
        out_ref, dx_ref, gain1, shift1, g_qkv, b_qkv, g_out, b_out = take(8)
        gain2, shift2, g_up, b_up, g_down, b_down = take(6)
        out_own, sem = refs
        me = lax.axis_index("seq")
        x = lax.rem(me, 2)
        fetch = pltpu.make_async_copy(out_lane.at[at(me * place, place), :], out_own, sem)
        fetch.start()

        for layer in range(LAYERS):
            for part in range(3):
                g_qkv[layer, part] = qkvs[layer][:, part * features : (part + 1) * features]
            for ref, target in ((outs, g_out), (ups, g_up), (downs, g_down)):
                target[layer] = ref[layer][...]

        for layer, (entry_own, entry_other, upper_own, upper_other) in enumerate(vec_refs):
            line = slice(layer, layer + 1)
            for part in range(3):
                row = slice(part, part + 1)
                b_qkv[part, line, :] = entry_own[row, :] + entry_other[row, :]
            b_up[line, :] = upper_own[0:1, :hidden_units] + upper_other[0:1, :hidden_units]

            def owned(mine, other, row):
                wide = mine.shape[1]
                place = (me // 2) * PAIR
                pair = at(lax.rem(place, wide), PAIR)
                both = mine[row : row + 1, pair] + other[row : row + 1, pair]
                for later in range(1, width // wide):
                    line = slice(row + later, row + later + 1)
                    both = jnp.where(place // wide == later, mine[line, pair] + other[line, pair], both)
                return jnp.where(x == 0, both[:, :half], both[:, half:])

            gain1[line, :] = owned(entry_own, entry_other, 3)
            shift1[line, :] = owned(entry_own, entry_other, 5)
            b_down[line, :] = owned(upper_own, upper_other, 1)
            gain2[line, :] = owned(upper_own, upper_other, 2)
            shift2[line, :] = owned(upper_own, upper_other, 3)
            b_out[line, :] = owned(upper_own, upper_other, 4)

        def both_lanes(target, mine, other):
            target[:, 0, :] = jnp.where(x == 0, mine, other)
            target[:, 1, :] = jnp.where(x == 0, other, mine)

        both_lanes(dx_ref, dx_own[...], dx_other[...])
        fetch.wait()
        both_lanes(out_ref, out_own[...], out_other[...])

    def f32(*shape):
        return jax.ShapeDtypeStruct(shape, F32)

    in_vmem = pl.BlockSpec(memory_space=pltpu.VMEM)
    flat = []
    for kind in range(4):
        flat += [sums[layer][kind] for layer in range(LAYERS)]
    for layer in range(LAYERS):
        flat += list(vecs[layer])
    flat += list(lanes)
    small = f32(LAYERS, width // n)
    return pl.pallas_call(
        kernel,
        out_shape=(
            f32(place, 2, width),
            f32(place, 2, width),
            small,
            small,
            f32(LAYERS, 3, half, features),
            f32(3, LAYERS, features),
            f32(LAYERS, half, features),
            small,
            small,
            small,
            f32(LAYERS, half, hidden_units),
            f32(LAYERS, hidden_units),
            f32(LAYERS, half, hidden_units),
            small,
        ),
        in_specs=[in_vmem] * (len(flat) - 4) + [ANYWHERE] + [in_vmem] * 3,
        out_specs=(in_vmem,) * 14,
        scratch_shapes=[pltpu.VMEM((place, width), F32), pltpu.SemaphoreType.DMA],
        compiler_params=pltpu.CompilerParams(vmem_limit_bytes=VMEM_BYTES),
        name="assemble",
    )(*flat)


def per_chip(
    tokens,
    d_out,
    norm1_gain,
    norm1_shift,
    w_qkv,
    b_qkv,
    w_out,
    b_out,
    norm2_gain,
    norm2_shift,
    w_up,
    b_up,
    w_down,
    b_down,
    episode_frames,
    live,
):
    n = lax.axis_size("seq")
    rows = tokens.shape[0]
    features = w_qkv.shape[3]
    fixed, ahead = turn_constants(rows * n // FRAME)
    qkv, qkv_bias = w_qkv.transpose(0, 2, 1, 3), b_qkv.transpose(1, 0, 2)

    gathered, key_bias, frames, *projected = gather_and_project(
        tokens, live.T, episode_frames, norm1_gain, norm1_shift, qkv, qkv_bias, fixed, ahead, n
    )
    streams, kept, d_part = [gathered], [], None
    for layer in range(LAYERS):
        following = None
        if layer + 1 < LAYERS:
            following = (qkv, norm1_gain, norm1_shift, qkv_bias, fixed, frames)
        results = layer_forward(
            layer,
            *projected[:3],
            key_bias,
            streams[layer],
            (w_out, w_up, w_down),
            (b_out, norm2_gain, norm2_shift, b_up, b_down),
            following,
            d_out if layer == 0 else None,
            d_part,
            n,
            1 + layer,
        )
        kept.append((*projected, *results[:8]))
        streams.append(results[8])
        if following is not None:
            projected = results[9:15]
        d_part = results[-1]

    sums = [[None] * 4 for _ in range(LAYERS)]
    vecs = [[None] * 4 for _ in range(LAYERS)]
    entry, later = (d_part,), None
    for layer in reversed(range(LAYERS)):
        query, key, value, first, unit1, scale1, probs, divisor, mixed = kept[layer][:9]
        unit2, scale2, second, act, slope = kept[layer][9:]
        upper = (
            layer,
            act,
            slope,
            unit2,
            scale2,
            second,
            mixed,
            w_out,
            w_up,
            w_down,
            norm2_gain,
        )
        identity = 1 + LAYERS + 2 * (LAYERS - 1 - layer)
        results = rows_backward(entry, upper, identity, FRAME, Swap([], []))
        if later is not None:
            vecs[layer + 1][0], *results = results
        grad_middle, grad_mixed, out_sum, up_sum, down_sum, vec2 = results
        vecs[layer][2] = vec2
        last = layer == 0
        if last:
            swap = Swap(
                [later[0], out_sum, up_sum, down_sum], [(later[1], 0), (vec2, 0), (vecs[layer + 1][0], 0)]
            )
        else:
            swap = Swap([out_sum, up_sum, down_sum], [(streams[LAYERS], rows)])
        results = attention_backward(
            probs,
            divisor,
            mixed,
            query,
            key,
            value,
            grad_mixed,
            first,
            fixed,
            frames,
            swap,
            last,
            identity + 1,
        )
        grad_query, grad_key, grad_value, qkv_sum = results[:4]
        sums[layer][0] = qkv_sum
        if last:
            sums[layer + 1][0] = results[4]
            sums[layer][1:] = results[5:8]
            vecs[layer + 1][3], vecs[layer][3], vecs[layer + 1][1] = results[8:]
        else:
            sums[layer][1:] = results[4:7]
            (out_other,) = results[7:]
            later = [qkv_sum, vec2]
        entry = (
            layer,
            grad_query,
            grad_key,
            grad_value,
            unit1,
            scale1,
            grad_middle,
            qkv,
            norm1_gain,
        )
    vec1, dx_own, dx_other, vec_other = rows_backward(
        entry, None, 1 + 3 * LAYERS, FRAME, Swap([], [])
    )
    vecs[0][:2] = [vec1, vec_other]
    results = list(
        assemble(
            sums,
            vecs,
            (streams[LAYERS], out_other, dx_own, dx_other),
            n,
            features,
            w_up.shape[2],
        )
    )
    results[4] = results[4].transpose(0, 2, 1, 3)
    results[5] = results[5].transpose(1, 0, 2)
    results[6] = results[6].transpose(0, 2, 1)
    results[12] = results[12].transpose(0, 2, 1)
    return tuple(results)


def lane_fits(mesh, tokens):
    n = mesh.shape["seq"]
    positions, lanes, width = tokens.shape
    rows = positions // n
    return (
        lanes == 2
        and n % 4 == 0
        and positions <= 4 * FRAME
        and positions % FRAME == 0
        and FRAME % rows == 0
        and width // n * 2 == PAIR
        and mesh.shape["tp"] == 2
    )


def solution(mesh):
    placed = (
        P("seq", None, None),
        P("seq", None, None),
        P(),
        P(),
        P(None, None, None, "tp"),
        P(None, None, "tp"),
        P(None, "tp", None),
        P(),
        P(),
        P(),
        P(None, None, "tp"),
        P(None, "tp"),
        P(None, "tp", None),
        P(),
        P(),
        P("seq", None),
    )
    def mapped(body):
        return jax.shard_map(
            body,
            mesh=mesh,
            in_specs=placed,
            out_specs=(
                P("seq", None, None),
                P("seq", None, None),
                P(None, "seq"),
                P(None, "seq"),
                P(None, "seq", None, "tp"),
                P(None, None, "tp"),
                P(None, "tp", "seq"),
                P(None, "seq"),
                P(None, "seq"),
                P(None, "seq"),
                P(None, "seq", "tp"),
                P(None, "tp"),
                P(None, "tp", "seq"),
                P(None, "seq"),
            ),
            check_vma=False,
        )

    def run(tokens, *others):
        if lane_fits(mesh, tokens):
            return mapped(per_chip)(tokens, *others)
        return mapped(per_device)(tokens, *others)

    return run
```

```python
import math

import jax
import jax.numpy as jnp
import numpy as np
from jax import lax
from jax.experimental import pallas as pl
from jax.experimental.pallas import tpu as pltpu
from jax.sharding import PartitionSpec as P

HEAD_DIM = 64
GRID = 16
FRAME = 256
LAYERS = 2
MICRO = 2


EPSILON = 1e-06
MASKED = -1e30
SCORE_SCALE = 0.125


def layer_norm(stream, norm_gain, norm_shift):
    center = stream - jnp.mean(stream, axis=-1, keepdims=True)
    spread = jnp.mean(center * center, axis=-1, keepdims=True)
    return center * lax.rsqrt(spread + EPSILON) * norm_gain + norm_shift


def rotate(values, frame_place, row_place, column_place):
    frequency = jnp.exp(jnp.arange(10, dtype=jnp.float32) * (-math.log(10000.0) / 10.0))
    pieces = []
    for section, place in enumerate((frame_place, row_place, column_place)):
        lower = values[..., 20 * section : 20 * section + 10]
        upper = values[..., 20 * section + 10 : 20 * section + 20]
        angles = place.astype(jnp.float32)[..., None, None] * frequency
        cosine = jnp.cos(angles)
        sine_part = jnp.sin(angles)
        pieces.append(lower * cosine - upper * sine_part)
        pieces.append(lower * sine_part + upper * cosine)
    pieces.append(values[..., 60:])
    return jnp.concatenate(pieces, axis=-1)


def episode_tags(frame_counts, positions):
    endings = jnp.cumsum(frame_counts) * FRAME
    passed = (positions[:, None] >= endings[None, :]).astype(jnp.int32)
    episode = jnp.sum(passed, axis=1)
    opening = jnp.sum(passed * frame_counts[None, :], axis=1)
    frame_index = positions // FRAME - opening
    within = positions % FRAME
    return (episode, frame_index, within // GRID, within % GRID)


def gelu_exact(values):
    return jax.nn.gelu(values, approximate=False)


def sum_heads(partial_sum):
    return lax.psum(partial_sum.astype(jnp.bfloat16), "tp").astype(jnp.float32)


def sum_inputs(partial_sum):
    return lax.psum(partial_sum.astype(jnp.bfloat16), "tp").astype(jnp.float32)


def lane_scores(query, keys_all, lane_index, query_tags, key_tags):
    head_count = query.shape[2] // HEAD_DIM
    query_lane = lax.dynamic_index_in_dim(query, lane_index, 1, False).reshape(
        query.shape[0], head_count, HEAD_DIM
    )
    keys_lane = lax.dynamic_index_in_dim(keys_all, lane_index, 1, False).reshape(
        keys_all.shape[0], head_count, HEAD_DIM
    )
    query_episode, query_frame = [
        lax.dynamic_index_in_dim(item, lane_index, 1, False) for item in query_tags
    ]
    key_episode, key_frame, key_live = [
        lax.dynamic_index_in_dim(item, lane_index, 1, False) for item in key_tags
    ]
    allowed = (
        (query_episode[:, None] == key_episode[None, :])
        & (key_frame[None, :] <= query_frame[:, None])
        & (key_live[None, :] > 0)
    )
    scores = (
        jnp.einsum("qhd,khd->hqk", query_lane, keys_lane, preferred_element_type=jnp.float32)
        * SCORE_SCALE
    )
    return (jnp.where(allowed[None], scores, MASKED), query_lane, keys_lane)


def attend_forward(query, keys_all, values_all, query_tags, key_tags):
    rows_dev, lane_count, features = query.shape
    head_count = features // HEAD_DIM

    def one_lane(lane_index, carry):
        scores, query_lane, keys_lane = lane_scores(
            query, keys_all, lane_index, query_tags, key_tags
        )
        highest = jnp.max(scores, axis=-1, keepdims=True)
        shifted = jnp.exp(scores - highest)
        summed = jnp.sum(shifted, axis=-1, keepdims=True)
        attention = (shifted / summed).astype(jnp.bfloat16)
        values_lane = lax.dynamic_index_in_dim(values_all, lane_index, 1, False).reshape(
            values_all.shape[0], head_count, HEAD_DIM
        )
        result = jnp.einsum(
            "hqk,khd->qhd", attention, values_lane, preferred_element_type=jnp.float32
        ).reshape(rows_dev, 1, features)
        log_total = (highest + jnp.log(summed))[None, :, :, 0]
        return (result, log_total)

    initial = (
        jnp.zeros((rows_dev, lane_count, features), jnp.float32),
        jnp.zeros((lane_count, head_count, rows_dev), jnp.float32),
    )
    return lax.fori_loop(0, lane_count, one_lane, initial)


def attend_backward(query, keys_all, values_all, log_total, grad_mixed, query_tags, key_tags):
    rows_dev, lane_count, features = query.shape
    head_count = features // HEAD_DIM
    key_rows = keys_all.shape[0]

    def one_lane(lane_index, carry):
        scores, query_lane, keys_lane = lane_scores(
            query, keys_all, lane_index, query_tags, key_tags
        )
        values_lane = lax.dynamic_index_in_dim(values_all, lane_index, 1, False).reshape(
            key_rows, head_count, HEAD_DIM
        )
        grad_lane = lax.dynamic_index_in_dim(grad_mixed, lane_index, 1, False).reshape(
            rows_dev, head_count, HEAD_DIM
        )
        attention = jnp.exp(
            scores - lax.dynamic_index_in_dim(log_total, lane_index, 0, False)[:, :, None]
        )
        grad_attention = jnp.einsum(
            "qhd,khd->hqk", grad_lane, values_lane, preferred_element_type=jnp.float32
        )
        inner = jnp.sum(attention * grad_attention, axis=-1, keepdims=True)
        grad_scores = (attention * (grad_attention - inner)).astype(jnp.bfloat16)
        query_part = (
            jnp.einsum("hqk,khd->qhd", grad_scores, keys_lane, preferred_element_type=jnp.float32)
            * SCORE_SCALE
        )
        key_part = (
            jnp.einsum("hqk,qhd->khd", grad_scores, query_lane, preferred_element_type=jnp.float32)
            * SCORE_SCALE
        )
        value_part = jnp.einsum(
            "hqk,qhd->khd",
            attention.astype(jnp.bfloat16),
            grad_lane,
            preferred_element_type=jnp.float32,
        )
        stacked = jnp.stack(
            [key_part.reshape(key_rows, features), value_part.reshape(key_rows, features)], axis=1
        )
        key_terms = stacked[:, None]
        grad_query = query_part.reshape(rows_dev, 1, features)
        return (grad_query, key_terms)

    initial = (
        jnp.zeros((rows_dev, lane_count, features), jnp.float32),
        jnp.zeros((key_rows, lane_count, 2, features), jnp.float32),
    )
    return lax.fori_loop(0, lane_count, one_lane, initial)


def front(stream, layer_index, params, query_tags, key_tags, positions):
    (
        gain_one,
        shift_one,
        mat_qkv,
        bias_qkv,
        mat_out,
        bias_out,
        gain_two,
        shift_two,
        mat_up,
        bias_up,
        mat_down,
        bias_down,
    ) = [item[layer_index] for item in params]
    rows_dev, lane_count, width = stream.shape
    features = mat_qkv.shape[2]
    head_count = features // HEAD_DIM
    frame_place, row_place, column_place = positions
    first = layer_norm(stream, gain_one, shift_one).astype(jnp.bfloat16)
    projected = (
        jnp.einsum("tbd,dcf->tbcf", first, mat_qkv, preferred_element_type=jnp.float32) + bias_qkv
    )
    split = projected.reshape(rows_dev, lane_count, 3, head_count, HEAD_DIM)
    query = (
        rotate(split[:, :, 0], frame_place, row_place, column_place)
        .reshape(rows_dev, lane_count, features)
        .astype(jnp.bfloat16)
    )
    keys = (
        rotate(split[:, :, 1], frame_place, row_place, column_place)
        .reshape(rows_dev, lane_count, features)
        .astype(jnp.bfloat16)
    )
    values = projected[:, :, 2].astype(jnp.bfloat16)
    keys_all, values_all = (
        lax.all_gather(keys, "seq", axis=0, tiled=True),
        lax.all_gather(values, "seq", axis=0, tiled=True),
    )
    mixed_full, log_total = attend_forward(query, keys_all, values_all, query_tags, key_tags)
    mixed = mixed_full.astype(jnp.bfloat16)
    middle = (
        stream
        + sum_heads(jnp.einsum("tbf,fd->tbd", mixed, mat_out, preferred_element_type=jnp.float32))
        + bias_out
    )
    second = layer_norm(middle, gain_two, shift_two).astype(jnp.bfloat16)
    hidden = jnp.einsum("tbd,df->tbf", second, mat_up, preferred_element_type=jnp.float32) + bias_up
    activation = gelu_exact(hidden).astype(jnp.bfloat16)
    return (
        first,
        query,
        keys_all,
        values_all,
        log_total,
        mixed,
        middle,
        second,
        hidden,
        activation,
        mixed_full,
    )


def layer_backward(stream, gradient, layer_index, params, query_tags, key_tags, positions):
    (
        gain_one,
        shift_one,
        mat_qkv,
        bias_qkv,
        mat_out,
        bias_out,
        gain_two,
        shift_two,
        mat_up,
        bias_up,
        mat_down,
        bias_down,
    ) = [item[layer_index] for item in params]
    (
        first,
        query,
        keys_all,
        values_all,
        log_total,
        mixed,
        middle,
        second,
        hidden,
        activation,
        mixed_full,
    ) = front(stream, layer_index, params, query_tags, key_tags, positions)
    frame_place, row_place, column_place = positions
    rows_dev, lane_count, width = stream.shape
    features = query.shape[2]
    head_count = features // HEAD_DIM
    grad_low = gradient.astype(jnp.bfloat16)
    grad_w_down = jnp.einsum(
        "tbf,tbd->fd", activation, grad_low, preferred_element_type=jnp.float32
    )
    grad_b_down = jnp.sum(gradient, axis=(0, 1))
    grad_activation = jnp.einsum(
        "tbd,fd->tbf", grad_low, mat_down, preferred_element_type=jnp.float32
    )
    grad_hidden = jax.vjp(gelu_exact, hidden)[1](grad_activation)[0].astype(jnp.bfloat16)
    grad_b_up = jnp.sum(grad_hidden.astype(jnp.float32), axis=(0, 1))
    grad_w_up = jnp.einsum("tbd,tbf->df", second, grad_hidden, preferred_element_type=jnp.float32)
    grad_second = sum_inputs(
        jnp.einsum("tbf,df->tbd", grad_hidden, mat_up, preferred_element_type=jnp.float32)
    )
    middle_pull = jax.vjp(layer_norm, middle, gain_two, shift_two)[1]
    grad_inner, grad_gain_two, grad_shift_two = middle_pull(grad_second)
    grad_middle = gradient + grad_inner
    grad_b_out = jnp.sum(grad_middle, axis=(0, 1))
    middle_low = grad_middle.astype(jnp.bfloat16)
    grad_w_out = jnp.einsum("tbf,tbd->fd", mixed, middle_low, preferred_element_type=jnp.float32)
    grad_mixed = jnp.einsum(
        "tbd,fd->tbf", middle_low, mat_out, preferred_element_type=jnp.float32
    ).astype(jnp.bfloat16)
    grad_query, key_terms = attend_backward(
        query, keys_all, values_all, log_total, grad_mixed, query_tags, key_tags
    )
    returned = lax.psum_scatter(key_terms, "seq", scatter_dimension=0, tiled=True)
    turned_query = rotate(
        grad_query.reshape(rows_dev, lane_count, head_count, HEAD_DIM),
        -frame_place,
        -row_place,
        -column_place,
    )
    turned_keys = rotate(
        returned[:, :, 0].reshape(rows_dev, lane_count, head_count, HEAD_DIM),
        -frame_place,
        -row_place,
        -column_place,
    )
    grad_projected = jnp.stack(
        [
            turned_query.reshape(rows_dev, lane_count, features),
            turned_keys.reshape(rows_dev, lane_count, features),
            returned[:, :, 1],
        ],
        axis=2,
    ).astype(jnp.bfloat16)
    grad_b_qkv = jnp.sum(grad_projected.astype(jnp.float32), axis=(0, 1))
    grad_w_qkv = jnp.einsum(
        "tbd,tbcf->dcf", first, grad_projected, preferred_element_type=jnp.float32
    )
    grad_first = sum_inputs(
        jnp.einsum("tbcf,dcf->tbd", grad_projected, mat_qkv, preferred_element_type=jnp.float32)
    )
    first_pull = jax.vjp(layer_norm, stream, gain_one, shift_one)[1]
    grad_entry, grad_gain_one, grad_shift_one = first_pull(grad_first)
    grads = (
        grad_gain_one,
        grad_shift_one,
        grad_w_qkv,
        grad_b_qkv,
        grad_w_out,
        grad_b_out,
        grad_gain_two,
        grad_shift_two,
        grad_w_up,
        grad_b_up,
        grad_w_down,
        grad_b_down,
    )
    return (grad_middle + grad_entry, grads)


def per_device(
    tokens,
    d_out,
    norm1_gain,
    norm1_shift,
    w_qkv,
    b_qkv,
    w_out,
    b_out,
    norm2_gain,
    norm2_shift,
    w_up,
    b_up,
    w_down,
    b_down,
    episode_frames,
    live,
):
    rows_dev = tokens.shape[0]
    lane_count = tokens.shape[1] // MICRO
    total_rows = rows_dev * lax.axis_size("seq")
    local_positions = lax.axis_index("seq") * rows_dev + jnp.arange(rows_dev, dtype=jnp.int32)
    key_positions = jnp.arange(total_rows, dtype=jnp.int32)
    tagger = jax.vmap(episode_tags, in_axes=(0, None), out_axes=1)
    query_episode, query_frame, query_row, query_column = tagger(episode_frames, local_positions)
    key_episode, key_frame, key_row, key_column = tagger(episode_frames, key_positions)
    live_keys = lax.all_gather(live, "seq", axis=0, tiled=True)
    params = (
        norm1_gain,
        norm1_shift,
        w_qkv,
        b_qkv,
        w_out,
        b_out,
        norm2_gain,
        norm2_shift,
        w_up,
        b_up,
        w_down,
        b_down,
    )
    layer_grads = [None] * LAYERS
    outputs = []
    grad_tokens = []
    for micro_index in range(MICRO):
        first_lane = micro_index * lane_count
        last_lane = first_lane + lane_count
        query_tags = (query_episode[:, first_lane:last_lane], query_frame[:, first_lane:last_lane])
        key_tags = (
            key_episode[:, first_lane:last_lane],
            key_frame[:, first_lane:last_lane],
            live_keys[:, first_lane:last_lane],
        )
        positions = (
            query_frame[:, first_lane:last_lane],
            query_row[:, first_lane:last_lane],
            query_column[:, first_lane:last_lane],
        )
        stream = tokens[:, first_lane:last_lane].astype(jnp.float32)
        inputs = []
        gathered = []
        for layer_index in range(LAYERS):
            inputs.append(stream)
            layer_state = front(stream, layer_index, params, query_tags, key_tags, positions)
            gathered.append((layer_state[2], layer_state[3]))
            branch = jnp.einsum(
                "tbf,fd->tbd",
                layer_state[9],
                w_down[layer_index],
                preferred_element_type=jnp.float32,
            )
            stream = layer_state[6] + sum_heads(branch) + b_down[layer_index]
        outputs.append(stream)
        gradient = d_out[:, first_lane:last_lane]
        for layer_index in reversed(range(LAYERS)):
            gradient, grads = layer_backward(
                inputs[layer_index], gradient, layer_index, params, query_tags, key_tags, positions
            )
            if layer_grads[layer_index] is None:
                layer_grads[layer_index] = grads
            else:
                layer_grads[layer_index] = jax.tree.map(jnp.add, layer_grads[layer_index], grads)
        grad_tokens.append(gradient)
    stacked = [
        jnp.stack([layer_grads[layer_index][entry] for layer_index in range(LAYERS)])
        for entry in range(12)
    ]
    (
        grad_gain_one,
        grad_shift_one,
        grad_w_qkv,
        grad_b_qkv,
        grad_w_out,
        grad_b_out,
        grad_gain_two,
        grad_shift_two,
        grad_w_up,
        grad_b_up,
        grad_w_down,
        grad_b_down,
    ) = stacked
    in_sums = (
        lax.psum_scatter(grad_w_qkv, "seq", scatter_dimension=1, tiled=True),
        lax.psum_scatter(grad_w_up, "seq", scatter_dimension=1, tiled=True),
        lax.psum_scatter(grad_gain_one, "seq", scatter_dimension=1, tiled=True),
        lax.psum_scatter(grad_shift_one, "seq", scatter_dimension=1, tiled=True),
        lax.psum_scatter(grad_gain_two, "seq", scatter_dimension=1, tiled=True),
        lax.psum_scatter(grad_shift_two, "seq", scatter_dimension=1, tiled=True),
        lax.psum_scatter(grad_b_out, "seq", scatter_dimension=1, tiled=True),
        lax.psum_scatter(grad_b_down, "seq", scatter_dimension=1, tiled=True),
    )
    out_sums = (
        lax.psum_scatter(grad_w_out, "seq", scatter_dimension=2, tiled=True),
        lax.psum_scatter(grad_w_down, "seq", scatter_dimension=2, tiled=True),
    )
    bias_total = lax.psum((grad_b_qkv, grad_b_up), "seq")
    return (
        jnp.concatenate(outputs, axis=1),
        jnp.concatenate(grad_tokens, axis=1),
        in_sums[2],
        in_sums[3],
        in_sums[0],
        bias_total[0],
        out_sums[0],
        in_sums[6],
        in_sums[4],
        in_sums[5],
        in_sums[1],
        bias_total[1],
        out_sums[1],
        in_sums[7],
    )


MESH = pl.DeviceIdType.MESH
BF16 = jnp.bfloat16
F32 = jnp.float32
VMEM_BYTES = 60 * 1024 * 1024
PAIR = 128
VEC = 2048


def nn(left, right):
    return lax.dot_general(left, right, (((1,), (0,)), ((), ())), preferred_element_type=F32)


def nt(left, right):
    return lax.dot_general(left, right, (((1,), (1,)), ((), ())), preferred_element_type=F32)


def tn(left, right):
    return lax.dot_general(left, right, (((0,), (0,)), ((), ())), preferred_element_type=F32)


def at(start, size):
    return pl.ds(pl.multiple_of(start, size), size)


def repeat(count, body):
    def one(index, carry):
        body(index)
        return carry

    lax.fori_loop(0, count, one, 0)


def remote(src, dst, send, recv, seq, tp):
    return pltpu.make_async_remote_copy(
        src_ref=src,
        dst_ref=dst,
        send_sem=send,
        recv_sem=recv,
        device_id=(seq, tp),
        device_id_type=MESH,
    )


def hello(partners):
    barrier = pltpu.get_barrier_semaphore()
    for seq, tp in partners:
        pl.semaphore_signal(barrier, inc=1, device_id=(seq, tp), device_id_type=MESH)


def met(partners):
    pl.semaphore_wait(pltpu.get_barrier_semaphore(), len(partners))


def whole(array):
    zeros = (0,) * array.ndim
    return pl.BlockSpec(array.shape, lambda s: zeros, pipeline_mode=pl.Buffered(1))


def whole_out(shape):
    zeros = (0,) * len(shape)
    return pl.BlockSpec(shape, lambda s: zeros)


ANYWHERE = pl.BlockSpec(memory_space=pl.ANY)


def turn_row(table, place, section):
    frequency = np.exp(np.arange(10, dtype=np.float32) * np.float32(-math.log(10000.0) / 10.0))
    angle = place.astype(np.float32)[:, None] * frequency
    for base in range(20 * section, PAIR, HEAD_DIM):
        table[0, :, base : base + 10] = np.cos(angle)
        table[0, :, base + 10 : base + 20] = np.cos(angle)
        table[1, :, base : base + 10] = -np.sin(angle)
        table[2, :, base + 10 : base + 20] = np.sin(angle)


def turn_constants(frames):
    within, ahead = np.zeros((3, FRAME, PAIR), np.float32), np.zeros((3, frames, PAIR), np.float32)
    turn_row(within, np.arange(FRAME) // GRID, 1)
    turn_row(within, np.arange(FRAME) % GRID, 2)
    for base in range(60, PAIR, HEAD_DIM):
        within[0, :, base : base + 4] = 1.0
    turn_row(ahead, np.arange(frames), 0)
    return jnp.asarray(within), jnp.asarray(ahead)


def turn(values, tables, back=False):
    cosine, lower, upper = tables
    pieces = []
    for start in range(0, values.shape[1], PAIR):
        slab = values[:, start : start + PAIR]
        moved = pltpu.roll(slab, PAIR - 10, 1) * lower + pltpu.roll(slab, 10, 1) * upper
        pieces.append(slab * cosine - moved if back else slab * cosine + moved)
    return jnp.concatenate(pieces, axis=1)


def tables_of(fixed_ref, frames_ref, chunk):
    return [fixed_ref[i] + frames_ref[i, pl.ds(chunk, 1), :] for i in range(3)]


def normed(stream):
    center = stream - jnp.mean(stream, axis=-1, keepdims=True)
    spread = jnp.mean(center * center, axis=-1, keepdims=True)
    scale = lax.rsqrt(spread + EPSILON)
    return center * scale, scale


def norm_pull(grad, gain, unit, scale):
    scaled = grad * gain
    return scale * (
        scaled
        - jnp.mean(scaled, axis=-1, keepdims=True)
        - unit * jnp.mean(scaled * unit, axis=-1, keepdims=True)
    )


def keep_norm(unit, scale, unit_ref, scale_ref):
    unit_ref[...] = unit.astype(BF16)
    scale_ref[...] = jnp.broadcast_to(scale, scale_ref.shape)


def kept_norm(unit_ref, scale_ref):
    copies = unit_ref.shape[1] // scale_ref.shape[1]
    return unit_ref[...].astype(F32), jnp.concatenate([scale_ref[...]] * copies, axis=1)


def column_sum(values):
    return jnp.sum(values, axis=0, keepdims=True)


def gelu_both(hidden):
    normal = 0.5 + 0.5 * lax.erf(hidden * math.sqrt(0.5))
    density = jnp.exp(hidden * hidden * -0.5) * (1.0 / math.sqrt(2.0 * math.pi))
    return hidden * normal, normal + hidden * density


def project(stream, chunk, layer, pair, refs, outs, first_full):
    gain, shift, weight, bias, fixed, frames = refs
    qkv_ref, first_ref, unit_ref, scale_ref = outs
    unit, scale = normed(stream)
    keep_norm(unit, scale, unit_ref, scale_ref)
    first_full[...] = (unit * gain[layer : layer + 1, :] + shift[layer : layer + 1, :]).astype(BF16)
    first_ref[...] = first_full[:, at(pair * PAIR, PAIR)]
    cosine, lower, upper = tables_of(fixed, frames, chunk)

    def one(part):
        still = part == 2
        tables = (
            jnp.where(still, 1.0, cosine),
            jnp.where(still, 0.0, lower),
            jnp.where(still, 0.0, upper),
        )
        values = nn(first_full[...], weight[part]) + bias[part, layer : layer + 1, :]
        qkv_ref[part] = (turn(values, tables) * jnp.where(part == 0, SCORE_SCALE, 1.0)).astype(BF16)

    repeat(3, one)


class Relay:
    sems = 6

    def __init__(self, n, rows, buffer, other, sems, lives=None, live_other=None):
        self.n, self.rows, self.buffer, self.other = n, rows, buffer, other
        self.lives, self.live_other = lives, live_other
        self.z_send, self.z_recv, self.y_send, self.y_recv, self.c_send, self.c_recv = sems
        self.planes = n // 4
        self.me, self.core = lax.axis_index("seq"), lax.axis_index("tp")
        me = self.me
        self.x, self.y, self.z = lax.rem(me, 2), lax.rem(me // 2, 2), me // 4
        self.across = me + 2 - 4 * self.y

    @staticmethod
    def scratch(n):
        dma, planes = pltpu.SemaphoreType.DMA, n // 4
        shapes = [(planes, 2, 2)] * 2 + [(planes, 2)] * 2 + [(2 * planes,)] * 2
        return [dma(shape) for shape in shapes]

    @property
    def events(self):
        return self.planes

    def plane(self, step):
        return lax.rem(self.z + step, self.planes)

    def place(self, plane, lane):
        return plane * 4 + self.y * 2 + lane

    def reached(self):
        return [(step, far) for step in range(self.planes) for far in (0, 1) if step or far]

    def hello(self):
        barrier = pltpu.get_barrier_semaphore()
        partners = [(self.across, self.core), (self.me, 1 - self.core)]
        for step, far in self.reached():
            lane = 1 - self.x if far else self.x
            partners.append((self.place(self.plane(step), lane), self.core))
        for seq, tp in partners:
            pl.semaphore_signal(barrier, inc=1, device_id=(seq, tp), device_id_type=MESH)

    def met(self):
        pl.semaphore_wait(pltpu.get_barrier_semaphore(), 2 + len(self.reached()))

    def rows_of(self, side, seq):
        return self.buffer.at[side, at(seq * self.rows, self.rows), :]

    def block(self, side, pair):
        return self.buffer.at[side, at(pair * 2 * self.rows, 2 * self.rows), :]

    def items(self, pair):
        found = [self.block(self.core, pair)]
        if self.lives is not None:
            found.append(self.lives.at[at(pair * 2, 2)])
        return found

    def each(self, copy, what):
        for index in range(1 if self.lives is None else 2):
            getattr(copy(index), what)()

    def z_copy(self, step, far):
        def copy(index):
            lane = 1 - self.x if far else self.x
            if index == 0:
                source = self.other.at[self.core] if far else self.rows_of(self.core, self.me)
                target = self.rows_of(self.core, self.me)
            else:
                source = self.live_other if far else self.lives.at[self.me]
                target = self.lives.at[self.me]
            return remote(
                source,
                target,
                self.z_send.at[step, far, index],
                self.z_recv.at[step, far, index],
                self.place(self.plane(step), lane),
                self.core,
            )

        return copy

    def y_copy(self, plane, row):
        def copy(index):
            item = self.items(plane * 2 + row)[index]
            return remote(
                item,
                item,
                self.y_send.at[plane, index],
                self.y_recv.at[plane, index],
                self.across,
                self.core,
            )

        return copy

    def c_copy(self, pair, side):
        item = self.block(side, pair)
        return remote(
            item, item, self.c_send.at[pair], self.c_recv.at[pair], self.me, 1 - self.core
        )

    def begin(self):
        for step, far in self.reached():
            self.each(self.z_copy(step, far), "start")

    def arrive(self, event):
        for far in (0, 1) if event else (1,):
            self.each(self.z_copy(event, far), "wait_recv")
        plane = self.plane(self.planes - event)
        self.each(self.y_copy(plane, self.y), "start")
        self.c_copy(plane * 2 + self.y, self.core).start()

    def complete(self, event):
        plane = self.plane(self.planes - event)
        self.each(self.y_copy(plane, 1 - self.y), "wait_recv")
        self.c_copy(plane * 2 + 1 - self.y, self.core).start()

    def ready(self, event):
        plane = self.plane(self.planes - event)
        self.c_copy(plane * 2, 1 - self.core).wait_recv()
        self.c_copy(plane * 2 + 1, 1 - self.core).wait_recv()
        return plane

    def finish(self):
        for step, far in self.reached():
            self.each(self.z_copy(step, far), "wait_send")
        for plane in range(self.planes):
            self.each(self.y_copy(plane, self.y), "wait_send")
        for pair in range(2 * self.planes):
            self.c_copy(pair, self.core).wait_send()


def split_lanes(values, x, buffer, other, start, rows):
    half = values.shape[2] // 2
    zero, one = values[:, 0, :], values[:, 1, :]
    own, far = jnp.where(x == 0, zero, one), jnp.where(x == 0, one, zero)
    core = lax.axis_index("tp")
    own = jnp.where(core == 0, own[:, :half], own[:, half:]).astype(BF16)
    buffer[core, at(start, rows), :] = own
    for side in range(2):
        other[side] = far[:, side * half : (side + 1) * half].astype(BF16)


def gather_and_project(tokens, live, episode_frames, gain, shift, qkv, bias, fixed, ahead, n):
    rows, lanes, width = tokens.shape
    half = width // 2
    total = n * rows
    chunks = total // FRAME
    per_frame = FRAME // rows
    features = qkv.shape[3]
    slots = episode_frames.shape[1]

    def kernel(*refs):
        refs = list(refs)

        def take(count):
            taken = refs[:count]
            del refs[:count]
            return taken

        tokens_ref, live_ref, counts_ref, gain_ref, shift_ref, w_any, bias_ref = take(7)
        fixed_ref, ahead_ref = take(2)
        all_ref, mask_ref, frames_ref = take(3)
        qkv_ref, *projected = take(4)
        other, lives, live_other, weight, full, w_sem = take(6)
        relay = Relay(n, rows, all_ref, other, take(Relay.sems), lives, live_other)
        load = pltpu.make_async_copy(w_any.at[0], weight, w_sem)
        load.start()
        relay.hello()
        x, me = relay.x, relay.me
        split_lanes(tokens_ref[...].astype(F32), x, all_ref, other, me * rows, rows)
        lane = lax.broadcasted_iota(jnp.int32, (1, FRAME), 1)
        here = lane // rows == lax.rem(me, per_frame)
        tiles = []
        for index in range(lanes):
            alive = live_ref[index : index + 1, :].astype(F32)
            alive = jnp.where(here, jnp.concatenate([alive] * per_frame, axis=1), 0.0)
            tiles.append(jnp.broadcast_to(alive, (8, FRAME)))
        lives[me] = jnp.where(x == 0, tiles[0], tiles[1])
        live_other[...] = jnp.where(x == 0, tiles[1], tiles[0])
        relay.met()
        relay.begin()

        counts = [counts_ref[x, slot] for slot in range(slots)]
        episodes, openings = [], []
        for frame in range(chunks):
            end, episode, opening = 0, 0, 0
            for slot in range(slots):
                end = end + counts[slot]
                passed = frame >= end
                episode = episode + passed.astype(jnp.int32)
                opening = opening + jnp.where(passed, counts[slot], 0)
            episodes.append(episode)
            openings.append(frame - opening)
        for index in range(3):
            table = []
            for frame in range(chunks):
                line = jnp.zeros((1, PAIR), F32)
                for choice in range(chunks):
                    line = jnp.where(
                        openings[frame] == choice, ahead_ref[index, choice : choice + 1, :], line
                    )
                table.append(line)
            frames_ref[index] = jnp.concatenate(
                table + [jnp.zeros((8 - chunks, PAIR), F32)], axis=0
            )
        load.wait()

        def project_frame(frame):
            place = at(frame * FRAME, FRAME)
            stream = jnp.concatenate([all_ref[0, place, :], all_ref[1, place, :]], axis=1)
            project(
                stream.astype(F32),
                frame,
                0,
                me // 2,
                (gain_ref, shift_ref, weight, bias_ref, fixed_ref, frames_ref),
                [qkv_ref.at[:, place, :]] + [ref.at[place, :] for ref in projected],
                full,
            )

        for event in range(relay.events):
            relay.arrive(event)
            if event:
                relay.complete(event - 1)
            if event > 1:
                project_frame(relay.ready(event - 2))
        relay.complete(relay.events - 1)
        for event in range(max(0, relay.events - 2), relay.events):
            project_frame(relay.ready(event))
        relay.finish()

        for key_frame in range(chunks):
            alive = lives[key_frame * per_frame, 0:1, :]
            for part in range(1, per_frame):
                alive = alive + lives[key_frame * per_frame + part, 0:1, :]
            closed = (alive - 1.0) * -MASKED
            lines = []
            for query_frame in range(chunks):
                allowed = (episodes[query_frame] == episodes[key_frame]) & (
                    openings[key_frame] <= openings[query_frame]
                )
                lines.append(jnp.where(allowed, closed, MASKED))
            lines.append(jnp.zeros((PAIR - chunks, FRAME), F32))
            mask_ref[key_frame * FRAME : (key_frame + 1) * FRAME, :] = jnp.concatenate(
                lines, axis=0
            ).T.astype(BF16)

    in_vmem = pl.BlockSpec(memory_space=pltpu.VMEM)
    in_smem = pl.BlockSpec(memory_space=pltpu.SMEM)
    return pl.pallas_call(
        kernel,
        out_shape=(
            jax.ShapeDtypeStruct((2, total, half), BF16),
            jax.ShapeDtypeStruct((total, PAIR), BF16),
            jax.ShapeDtypeStruct((3, 8, PAIR), F32),
            jax.ShapeDtypeStruct((3, total, features), BF16),
            jax.ShapeDtypeStruct((total, PAIR), BF16),
            jax.ShapeDtypeStruct((total, width), BF16),
            jax.ShapeDtypeStruct((total, PAIR), F32),
        ),
        in_specs=[in_vmem, in_vmem, in_smem, in_vmem, in_vmem, ANYWHERE] + [in_vmem] * 3,
        out_specs=(in_vmem,) * 7,
        scratch_shapes=[
            pltpu.VMEM((2, rows, half), BF16),
            pltpu.VMEM((n, 8, FRAME), F32),
            pltpu.VMEM((8, FRAME), F32),
            pltpu.VMEM(qkv.shape[1:], BF16),
            pltpu.VMEM((FRAME, width), BF16),
            pltpu.SemaphoreType.DMA,
        ]
        + Relay.scratch(n),
        compiler_params=pltpu.CompilerParams(
            collective_id=0, has_side_effects=True, vmem_limit_bytes=VMEM_BYTES
        ),
        name="gather_and_project",
    )(tokens, live, episode_frames, gain, shift, qkv, bias, fixed, ahead)


def halves(ref):
    return jnp.concatenate([ref[0], ref[1]], axis=1).astype(F32)


def halves_spec(shape, chunks, behind, span=FRAME):
    return pl.BlockSpec(
        (2, span, shape[2]), lambda s: (0, jnp.clip(s - behind, 0, chunks - 1), 0)
    )


def layer_forward(layer, turned, key_bias, stream, mats, rows_of, next_refs, d_out, n, identity):
    _, total, features = turned.shape
    split = stream.ndim == 3
    width = mats[1].shape[1]
    rows_here = total // n
    hidden_units = mats[1].shape[2]
    chunks = total // FRAME
    heads = features // HEAD_DIM
    slabs = features // PAIR
    columns = 256
    last = next_refs is None
    b_out, gain, shift, b_up, b_down = rows_of
    mat_out, mat_up, mat_down = mats

    def kernel(*refs):
        refs = list(refs)

        def take(count):
            taken = refs[:count]
            del refs[:count]
            return taken

        q_ref, k_ref, v_ref, kb_ref, x_ref = take(5)
        wo_any, wu_any, wd_any = take(3)
        bo_ref, gain_ref, shift_ref, bu_ref, bd_ref = take(5)
        if not last:
            wq_any, ngain, nshift, nbias, fixed, frames = take(6)
        if d_out is not None:
            (d_ref,) = take(1)
        p_ref, r_ref, mixed_ref, unit_ref, scale_ref, second_ref, act_ref, gp_ref, x_out = take(9)
        if not last:
            next_outs = take(4)
        if d_out is not None:
            (d_all,) = take(1)
        wo, wu, wd, mid, full, next_full = take(6)
        if not last:
            (wq,) = take(1)
        a_send, a_recv, b_send, b_recv, w_sem, send_sem, recv_sem = take(7)
        relay = None
        if d_out is not None:
            buffer, other, d_sem = take(3)
            relay = Relay(n, rows_here, buffer, other, take(Relay.sems))

        step = pl.program_id(0)
        me, core = lax.axis_index("seq"), lax.axis_index("tp")

        items = [(wo_any, wo), (wu_any, wu), (wd_any, wd)]
        if not last:
            items.append((wq_any, wq))

        def load(index):
            source, target = items[index]
            return pltpu.make_async_copy(
                source.at[layer if index < 3 else layer + 1], target, w_sem.at[index]
            )

        def exchange(kind, chunk):
            source, target = ((a_send, a_recv), (b_send, b_recv))[kind]
            return remote(
                source.at[chunk],
                target.at[chunk],
                send_sem.at[kind, chunk],
                recv_sem.at[kind, chunk],
                me,
                1 - core,
            )

        @pl.when(step == 0)
        def _():
            for index in range(len(items)):
                load(index).start()
            if relay is None:
                hello([(me, 1 - core)])
            else:
                relay.hello()
                split_lanes(d_ref[...], relay.x, buffer, other, me * rows_here, rows_here)

        lane = lax.broadcasted_iota(jnp.int32, (1, PAIR), 1)
        sides = [(lane < HEAD_DIM).astype(F32).astype(BF16), (lane >= HEAD_DIM).astype(F32).astype(BF16)]
        for frame in range(chunks):

            @pl.when(step == frame)
            def _():
                keys = FRAME * (frame + 1)
                mask = kb_ref[:keys, :]
                asked = jnp.broadcast_to((lane == frame).astype(F32), (FRAME, PAIR)).astype(BF16)

                def two_slabs(couple):
                    def lanes_of(head):
                        return at((couple * 2 + head // 2) * PAIR, PAIR)

                    def score(head):
                        key = jnp.concatenate([k_ref[0, :keys, lanes_of(head)], mask], axis=1)
                        ask = q_ref[0, :, lanes_of(head)] * sides[head % 2]
                        return nt(jnp.concatenate([ask, asked], axis=1), key)

                    scores, sums = score(0), []
                    for head in range(4):
                        lanes, side = lanes_of(head), head % 2
                        following = score(head + 1) if head < 3 else None
                        highest = jnp.max(scores, axis=1, keepdims=True)
                        shifted = jnp.exp(scores - highest).astype(BF16)
                        p_ref[0, couple * 4 + head, :keys, :] = shifted.T
                        sums.append(nn(shifted, v_ref[0, :keys, lanes] * sides[side] + sides[1 - side]))
                        scores = following
                        if side == 1:
                            one, two = sums[head - 1 :]
                            low_side = lane < HEAD_DIM
                            divisor = 1.0 / jnp.where(
                                low_side, pltpu.roll(one, HEAD_DIM, 1), pltpu.roll(two, HEAD_DIM, 1)
                            )
                            r_ref[:, lanes] = divisor
                            mixed_ref[:, lanes] = (jnp.where(low_side, one, two) * divisor).astype(BF16)

                repeat(slabs // 2, two_slabs)

        @pl.when(step == 0)
        def _():
            load(0).wait()
            if relay is None:
                met([(me, 1 - core)])
            else:
                relay.met()
                relay.begin()

        @pl.when(step < chunks)
        def _():
            a_send[step] = nn(mixed_ref[...], wo[...]).astype(BF16)
            exchange(0, step).start()

        if relay is not None:
            for event in range(relay.events):

                @pl.when(step == 2 + event // 2)
                def _():
                    relay.arrive(event)

                @pl.when(step == 3 + event // 2)
                def _():
                    relay.complete(event)

            @pl.when(step == chunks + 1)
            def _():
                for event in range(relay.events):
                    relay.ready(event)
                relay.finish()
                pltpu.make_async_copy(buffer, d_all, d_sem).start()

        def feed_forward():
            chunk = step - 1
            middle = (halves(x_ref) if split else x_ref[...]) + (
                a_send[chunk].astype(F32) + a_recv[chunk].astype(F32)
            )
            middle = middle + bo_ref[layer : layer + 1, :]
            mid[lax.rem(chunk, 2)] = middle
            unit, scale = normed(middle)
            keep_norm(unit, scale, unit_ref, scale_ref)
            second = (unit * gain_ref[layer : layer + 1, :] + shift_ref[layer : layer + 1, :]).astype(BF16)
            full[...] = second
            second_ref[...] = full[:, at((me // 2) * PAIR, PAIR)]
            parts = [slice(start, start + columns) for start in range(0, hidden_units, columns)]
            hidden = nn(second, wu[:, parts[0]])
            for index, part in enumerate(parts):
                following = nn(second, wu[:, parts[index + 1]]) if index + 1 < len(parts) else None
                act, slope = gelu_both(hidden + bu_ref[layer : layer + 1, part])
                act_ref[:, part] = act.astype(BF16)
                gp_ref[:, part] = slope.astype(BF16)
                hidden = following
            b_send[chunk] = nn(act_ref[...], wd[...]).astype(BF16)

        def close():
            chunk = step - 2
            result = mid[lax.rem(chunk, 2)] + (b_send[chunk].astype(F32) + b_recv[chunk].astype(F32))
            result = result + bd_ref[layer : layer + 1, :]
            x_out[...] = result
            if not last:
                project(
                    result,
                    chunk,
                    layer + 1,
                    me // 2,
                    (ngain, nshift, wq, nbias, fixed, frames),
                    next_outs,
                    next_full,
                )

        @pl.when(step == 1)
        def _():
            load(1).wait()
            load(2).wait()

        @pl.when((step >= 1) & (step <= chunks))
        def _():
            exchange(0, step - 1).wait_recv()
            feed_forward()
            exchange(1, step - 1).start()

        if not last:

            @pl.when(step == 2)
            def _():
                load(3).wait()

        @pl.when(step >= 2)
        def _():
            exchange(1, step - 2).wait_recv()
            close()

        @pl.when(step == chunks + 1)
        def _():
            for kind in range(2):
                for chunk in range(chunks):
                    exchange(kind, chunk).wait_send()
            if relay is not None:
                pltpu.make_async_copy(buffer, d_all, d_sem).wait()

    def rows(columns, behind):
        return pl.BlockSpec(
            (FRAME, columns), lambda s: (jnp.clip(s - behind, 0, chunks - 1), 0)
        )

    def part_of(part):
        return pl.BlockSpec(
            (1, total, features), lambda s: (part, 0, 0), pipeline_mode=pl.Buffered(1)
        )

    in_specs = [
        pl.BlockSpec((1, FRAME, features), lambda s: (0, jnp.minimum(s, chunks - 1), 0)),
        part_of(1),
        part_of(2),
        whole(key_bias),
    ]
    in_specs += [halves_spec(stream.shape, chunks, 1) if split else rows(width, 1)]
    in_specs += [ANYWHERE] * 3 + [whole(item) for item in rows_of]
    operands = [turned, turned, turned, key_bias, stream, *mats, *rows_of]
    if not last:
        in_specs += [ANYWHERE] + [whole(item) for item in next_refs[1:]]
        operands += list(next_refs)
    if d_out is not None:
        in_specs += [whole(d_out)]
        operands += [d_out]
    out_shape = [
        jax.ShapeDtypeStruct((chunks, heads, total, FRAME), BF16),
        jax.ShapeDtypeStruct((total, features), F32),
        jax.ShapeDtypeStruct((total, features), BF16),
        jax.ShapeDtypeStruct((total, width), BF16),
        jax.ShapeDtypeStruct((total, PAIR), F32),
        jax.ShapeDtypeStruct((total, PAIR), BF16),
        jax.ShapeDtypeStruct((total, hidden_units), BF16),
        jax.ShapeDtypeStruct((total, hidden_units), BF16),
        jax.ShapeDtypeStruct((total, width), F32),
    ]
    out_specs = [
        pl.BlockSpec((1, heads, total, FRAME), lambda s: (jnp.minimum(s, chunks - 1), 0, 0, 0)),
        rows(features, 0),
        rows(features, 0),
        rows(width, 1),
        rows(PAIR, 1),
        rows(PAIR, 1),
        rows(hidden_units, 1),
        rows(hidden_units, 1),
        rows(width, 2),
    ]
    scratch = [
        pltpu.VMEM(mat_out.shape[1:], BF16),
        pltpu.VMEM(mat_up.shape[1:], BF16),
        pltpu.VMEM(mat_down.shape[1:], BF16),
        pltpu.VMEM((2, FRAME, width), F32),
        pltpu.VMEM((FRAME, width), BF16),
        pltpu.VMEM((FRAME, width), BF16),
    ]
    if not last:
        out_shape += [jax.ShapeDtypeStruct((3, total, features), BF16)]
        out_shape += [jax.ShapeDtypeStruct((total, PAIR), BF16)]
        out_shape += [jax.ShapeDtypeStruct((total, width), BF16)]
        out_shape += [jax.ShapeDtypeStruct((total, PAIR), F32)]
        out_specs += [
            pl.BlockSpec((3, FRAME, features), lambda s: (0, jnp.clip(s - 2, 0, chunks - 1), 0))
        ]
        out_specs += [rows(PAIR, 2), rows(width, 2), rows(PAIR, 2)]
    if d_out is not None:
        out_shape += [jax.ShapeDtypeStruct((2, total, width // 2), BF16)]
        out_specs += [ANYWHERE]
        scratch += [pltpu.VMEM(next_refs[0].shape[1:], BF16)]
    scratch += [pltpu.VMEM((chunks, FRAME, width), BF16)] * 4
    scratch += [
        pltpu.SemaphoreType.DMA((4,)),
        pltpu.SemaphoreType.DMA((2, chunks)),
        pltpu.SemaphoreType.DMA((2, chunks)),
    ]
    if d_out is not None:
        scratch += [
            pltpu.VMEM((2, total, width // 2), BF16),
            pltpu.VMEM((2, rows_here, width // 2), BF16),
            pltpu.SemaphoreType.DMA,
        ]
        scratch += Relay.scratch(n)
    return pl.pallas_call(
        kernel,
        grid=(chunks + 2,),
        out_shape=out_shape,
        in_specs=in_specs,
        out_specs=out_specs,
        scratch_shapes=scratch,
        compiler_params=pltpu.CompilerParams(
            collective_id=identity, has_side_effects=True, vmem_limit_bytes=VMEM_BYTES
        ),
        name=f"layer_forward_{layer}",
    )(*operands)


class Swap:
    def __init__(self, ships, lane_rows):
        self.ships, self.lane_rows = ships, lane_rows
        self.count = len(ships) + len(lane_rows)

    def operands(self):
        return [*self.ships, *[item for item, _ in self.lane_rows]]

    def in_specs(self):
        return [whole(item) for item in self.ships] + [ANYWHERE] * len(self.lane_rows)

    def outputs(self):
        shapes, specs = [], []
        for item in self.ships:
            shape = (item.shape[0] // 2, item.shape[1])
            shapes.append(jax.ShapeDtypeStruct(shape, F32))
            specs.append(whole_out(shape))
        for item, count in self.lane_rows:
            shapes.append(jax.ShapeDtypeStruct((count or item.shape[0], item.shape[1]), item.dtype))
            specs.append(ANYWHERE)
        return shapes, specs

    def scratch(self):
        if not self.count:
            return []
        buffers = [pltpu.VMEM((item.shape[0] // 2, item.shape[1]), BF16) for item in self.ships]
        return buffers * 2 + [pltpu.SemaphoreType.DMA((self.count,))] * 2

    def bind(self, sources, targets, scratch):
        ships = len(self.ships)
        me, core = lax.axis_index("seq"), lax.axis_index("tp")
        x = lax.rem(me, 2)
        beside = me + 1 - 2 * x
        half = PAIR // 2

        def copy(index):
            if index < ships:
                source, target = scratch[index], scratch[ships + index]
            else:
                source, target = sources[index], targets[index]
                count = self.lane_rows[index - ships][1]
                if count:
                    source = source.at[at(beside * count, count), :]
            send, recv = scratch[2 * ships].at[index], scratch[2 * ships + 1].at[index]
            return remote(source, target, send, recv, beside, core)

        def start():
            for index in range(self.count):
                if index < ships:
                    scratch[index][...] = sources[index][at((1 - x) * half, half), :].astype(BF16)
                copy(index).start()

        def finish():
            for index in range(self.count):
                copy(index).wait_recv()
                if index < ships:
                    own = sources[index][at(x * half, half), :]
                    targets[index][...] = own + scratch[ships + index][...].astype(F32)
            for index in range(self.count):
                copy(index).wait_send()

        return start, finish


def attention_backward(
    probs, divisor, mixed, turned_qkv, grad_mixed, first, fixed, frames, swap, swap_qkv, identity
):
    _, total, features = turned_qkv.shape
    chunks = total // FRAME
    slabs = features // PAIR
    half = PAIR // 2

    def kernel(*refs):
        refs = list(refs)

        def take(count):
            taken = refs[:count]
            del refs[:count]
            return taken

        p_ref, r_ref, o_ref, q_ref, k_ref, v_ref, g_ref, first_ref, fixed_ref, frames_ref = take(10)
        sources = take(swap.count)
        dq_ref, dk_ref, dv_ref, qkv_out = take(4)
        targets = take(swap.count)
        dk_sum, dv_sum, first_turned = take(3)
        if swap_qkv:
            qkv_own, qkv_send, qkv_recv, qkv_sems = take(4)
        start, finish = swap.bind(sources, targets, refs)

        step = pl.program_id(0)
        me, core = lax.axis_index("seq"), lax.axis_index("tp")
        x = lax.rem(me, 2)
        beside = me + 1 - 2 * x

        def qkv_copy(slab):
            return remote(
                qkv_send.at[slab],
                qkv_recv.at[slab],
                qkv_sems.at[0, slab],
                qkv_sems.at[1, slab],
                beside,
                core,
            )

        @pl.when(step == 0)
        def _():
            hello([(beside, core)])
            first_turned[...] = first_ref[...].T
            met([(beside, core)])
            start()

        lane = lax.broadcasted_iota(jnp.int32, (1, PAIR), 1)
        sides = [(lane < HEAD_DIM).astype(F32).astype(BF16), (lane >= HEAD_DIM).astype(F32).astype(BF16)]
        turned = k_ref[0].T
        ones = jnp.broadcast_to((lane < 2).astype(F32), (total, PAIR)).astype(BF16)
        values = jnp.concatenate([v_ref[0], ones], axis=1)

        def give(frame):
            keys = FRAME * (frame + 1)
            own = slice(frame * FRAME, keys)
            scaled = (g_ref[own, :].astype(F32) * r_ref[own, :]).astype(BF16)
            inner = scaled.astype(F32) * o_ref[own, :].astype(F32)
            grads, q_parts, g_parts = [], [], []
            for side in range(2):
                delta = jnp.sum(
                    jnp.where((lane < HEAD_DIM) == (side == 0), inner, 0.0), axis=1, keepdims=True
                )
                coarse = delta.astype(BF16).astype(F32)
                rest = jnp.where(lane == 0, -coarse, jnp.where(lane == 1, coarse - delta, 0.0))
                g2 = scaled * sides[side]
                grads.append(nt(values[:keys], jnp.concatenate([g2, rest.astype(BF16)], axis=1)))
                q_parts.append(q_ref[0, own, :] * sides[side])
                g_parts.append(g2)
            return grads, jnp.concatenate(q_parts, axis=0), jnp.concatenate(g_parts, axis=0)

        given = give(chunks - 1)
        for frame in reversed(range(chunks)):
            keys = FRAME * (frame + 1)
            own = slice(frame * FRAME, keys)
            tables = tables_of(fixed_ref, frames_ref, frame)
            grads, q_part, g_part = given
            given = give(frame - 1) if frame else None
            query_parts, score_parts, prob_parts = [], [], []
            for side in range(2):
                attention = p_ref[frame, side, :keys, :]
                grad_scores = (attention.astype(F32) * grads[side]).astype(BF16)
                query_parts.append(nn(turned[side * HEAD_DIM : (side + 1) * HEAD_DIM, :keys], grad_scores))
                score_parts.append(grad_scores)
                prob_parts.append(attention)
            grad_query = jnp.concatenate(query_parts, axis=0).T
            key_parts = nn(jnp.concatenate(score_parts, axis=1), q_part)
            value_parts = nn(jnp.concatenate(prob_parts, axis=1), g_part)
            dq_ref[own, :] = (turn(grad_query, tables, True) * SCORE_SCALE).astype(BF16)
            if frame == chunks - 1:
                dk_sum[...] = key_parts
                dv_sum[...] = value_parts
            else:
                dk_sum[:keys, :] += key_parts
                dv_sum[:keys, :] += value_parts
            dk_ref[own, :] = turn(dk_sum[own, :], tables, True).astype(BF16)
            dv_ref[own, :] = dv_sum[own, :].astype(BF16)

        for part, ref in enumerate((dq_ref, dk_ref, dv_ref)):
            piece = slice(part * PAIR, (part + 1) * PAIR)
            terms = nn(first_turned[...], ref[...])
            if swap_qkv:
                qkv_own[step, :, piece] = terms
                qkv_send[step, :, piece] = qkv_own[step, at((1 - x) * half, half), piece].astype(BF16)
            else:
                qkv_out[:, at(part * features + step * PAIR, PAIR)] = terms
        if swap_qkv:
            qkv_copy(step).start()

        @pl.when(step == slabs - 1)
        def _():
            finish()
            for slab in range(slabs if swap_qkv else 0):
                qkv_copy(slab).wait_recv()
                for part in range(3):
                    piece = slice(part * PAIR, (part + 1) * PAIR)
                    place = part * features + slab * PAIR
                    qkv_out[:, place : place + PAIR] = qkv_own[
                        slab, at(x * half, half), piece
                    ] + qkv_recv[slab, :, piece].astype(F32)
            for slab in range(slabs if swap_qkv else 0):
                qkv_copy(slab).wait_send()

    slab = pl.BlockSpec((total, PAIR), lambda s: (0, s))
    in_specs = [pl.BlockSpec((chunks, 2, total, FRAME), lambda s: (0, s, 0, 0))]
    in_specs += [slab] * 2
    for part in range(3):
        in_specs.append(pl.BlockSpec((1, total, PAIR), lambda s, part=part: (part, 0, s)))
    in_specs += [slab] + [whole(first), whole(fixed), whole(frames)]
    in_specs += swap.in_specs()
    qkv_shape = (half if swap_qkv else PAIR, 3 * features)
    shapes, specs = swap.outputs()
    out_shape = [jax.ShapeDtypeStruct((total, features), BF16)] * 3
    out_shape += [jax.ShapeDtypeStruct(qkv_shape, F32)] + shapes
    out_specs = [slab] * 3 + [whole_out(qkv_shape)] + specs
    scratch = [pltpu.VMEM((total, PAIR), F32)] * 2 + [pltpu.VMEM((PAIR, total), BF16)]
    if swap_qkv:
        scratch += [pltpu.VMEM((slabs, PAIR, 3 * PAIR), F32)]
        scratch += [pltpu.VMEM((slabs, half, 3 * PAIR), BF16)] * 2
        scratch += [pltpu.SemaphoreType.DMA((2, slabs))]
    scratch += swap.scratch()
    return pl.pallas_call(
        kernel,
        grid=(slabs,),
        out_shape=out_shape,
        in_specs=in_specs,
        out_specs=out_specs,
        scratch_shapes=scratch,
        compiler_params=pltpu.CompilerParams(
            collective_id=identity, has_side_effects=True, vmem_limit_bytes=VMEM_BYTES
        ),
        name=f"attention_backward_{identity}",
    )(
        probs,
        divisor,
        mixed,
        turned_qkv,
        turned_qkv,
        turned_qkv,
        grad_mixed,
        first,
        fixed,
        frames,
        *swap.operands(),
    )


def rows_backward(entry, upper, identity, span, swap):
    top, bottom = len(entry) == 1, upper is None
    if not top:
        above, entry = entry[0], entry[1:]
    total = entry[0].shape[1] if top else entry[0].shape[0]
    chunks = total // span
    columns = 256
    ahead = 0 if top else 2 if bottom else 1
    if top:
        width = 2 * entry[0].shape[2]
    else:
        features, width = entry[0].shape[1], entry[5].shape[1]
    if not bottom:
        layer = upper[0]
        hidden_units, mixed_features = upper[1].shape[1], upper[6].shape[1]
    place_rows = total // lax.axis_size("seq")

    def kernel(*refs):
        refs = list(refs)

        def take(count):
            taken = refs[:count]
            del refs[:count]
            return taken

        if top:
            (d_out_ref,) = take(1)
        else:
            dq_ref, dk_ref, dv_ref, unit1, scale1, dm_ref, wq, gain1 = take(8)
        if not bottom:
            act_ref, gp_ref, unit2, scale2, second_ref, mixed_ref = take(6)
            wo_any, wu_any, wd_any, gain2 = take(4)
        sources = take(swap.count)
        if not top:
            (vec1,) = take(1)
        if not bottom:
            dmid_out, dmix_out, out_sum, up_sum, down_sum, vec2 = take(6)
        else:
            dx_out, dx_other, vec_other = take(3)
        targets = take(swap.count)
        if not top:
            a_send, a_recv = take(2)
        if not bottom:
            b_send, b_recv, grad_keep, hidden_keep, low_keep, last_keep, wo, wu, wd, w_sem = take(10)
        else:
            dx_keep, dx_send, dx_recv, vec_recv, x_send_sem, x_recv_sem = take(6)
        send_sem, recv_sem = take(2)
        start_swap, finish_swap = swap.bind(sources, targets, refs)

        step = pl.program_id(0)
        me, core = lax.axis_index("seq"), lax.axis_index("tp")
        pair = at((me // 2) * PAIR, PAIR)
        x = lax.rem(me, 2)
        beside = me + 1 - 2 * x

        def exchange(kind, chunk):
            source, target = (a_send, a_recv) if kind == 0 else (b_send, b_recv)
            return remote(
                source.at[chunk],
                target.at[chunk],
                send_sem.at[kind, chunk],
                recv_sem.at[kind, chunk],
                me,
                1 - core,
            )

        def load(index):
            source, target = ((wd_any, wd), (wu_any, wu), (wo_any, wo))[index]
            return pltpu.make_async_copy(source.at[layer], target, w_sem.at[index])

        partners = [(me, 1 - core)] + ([(beside, core)] if bottom or swap.count else [])

        @pl.when(step == 0)
        def _():
            if not bottom:
                for index in range(3):
                    load(index).start()
                out_sum[...] = jnp.zeros_like(out_sum)
                up_sum[...] = jnp.zeros_like(up_sum)
                down_sum[...] = jnp.zeros_like(down_sum)
                vec2[...] = jnp.zeros_like(vec2)
            if not top:
                vec1[...] = jnp.zeros_like(vec1)
            hello(partners)

        def meet():
            @pl.when(step == 0)
            def _():
                met(partners)
                start_swap()

        def entry_products():
            partial = None
            for part, ref in enumerate((dq_ref, dk_ref, dv_ref)):
                grad = ref[...]
                term = nt(grad, wq[0, part])
                partial = term if partial is None else partial + term
                vec1[part : part + 1, :] += column_sum(grad.astype(F32))
            a_send[step] = partial.astype(BF16)

        def entry_norm(chunk):
            if top:
                return halves(d_out_ref)
            grad_first = a_send[chunk].astype(F32) + a_recv[chunk].astype(F32)
            unit, scale = kept_norm(unit1, scale1)
            for start, sums in ((3, column_sum(grad_first * unit)), (5, column_sum(grad_first))):
                for side in range(width // features):
                    piece = slice(side * features, (side + 1) * features)
                    vec1[start + side : start + side + 1, :] += sums[:, piece]
            return dm_ref[...] + norm_pull(grad_first, gain1[above : above + 1, :], unit, scale)

        def feed_forward(between=None):
            chunk = step - ahead
            gradient = entry_norm(chunk)
            if bottom:
                dx_keep[at(chunk * span, span), :] = gradient
                return
            grad_keep[lax.rem(chunk, 2)] = gradient
            vec2[1:2, :width] += column_sum(gradient)
            low = gradient.astype(BF16)
            low_keep[...] = low
            low_columns = low_keep[:, pair]
            second = second_ref[...]
            parts = [slice(start, start + columns) for start in range(0, hidden_units, columns)]
            grad_act = nt(low, wd[parts[0], :])
            for index, part in enumerate(parts):
                following = nt(low, wd[parts[index + 1], :]) if index + 1 < len(parts) else None
                grad_hidden = grad_act * gp_ref[:, part].astype(F32)
                hidden_keep[:, part] = grad_hidden.astype(BF16)
                vec2[0:1, part] += column_sum(grad_hidden)
                grad_act = following
            if between is not None:
                between()
            b_send[chunk] = nt(hidden_keep[...], wu[...]).astype(BF16)
            down_sum[...] += tn(low_columns, act_ref[...])
            up_sum[...] += tn(second, hidden_keep[...])

        def close():
            chunk = step - ahead - 1
            grad_second = b_send[chunk].astype(F32) + b_recv[chunk].astype(F32)
            unit, scale = kept_norm(unit2, scale2)
            vec2[2:3, :width] += column_sum(grad_second * unit)
            vec2[3:4, :width] += column_sum(grad_second)
            grad_middle = grad_keep[lax.rem(chunk, 2)] + norm_pull(
                grad_second, gain2[layer : layer + 1, :], unit, scale
            )
            dmid_out[...] = grad_middle
            vec2[4:5, :width] += column_sum(grad_middle)
            low = grad_middle.astype(BF16)
            last_keep[...] = low
            out_sum[...] += tn(last_keep[:, pair], mixed_ref[...])
            dmix_out[...] = nt(low, wo[...]).astype(BF16)

        if not top:

            @pl.when(step < chunks)
            def _():
                entry_products()
                meet()
                exchange(0, step).start()

        @pl.when((step >= ahead) & (step < chunks + ahead))
        def _():
            if not top:
                exchange(0, step - ahead).wait_recv()
            if not bottom:

                @pl.when(step == ahead)
                def _():
                    load(0).wait()

            feed_forward(lambda: pl.when(step == ahead)(lambda: load(1).wait()))
            if not bottom:
                if top:
                    meet()
                exchange(1, step - ahead).start()

        if not bottom:

            @pl.when(step == ahead + 1)
            def _():
                load(2).wait()

            @pl.when(step >= ahead + 1)
            def _():
                exchange(1, step - ahead - 1).wait_recv()
                close()

        if bottom:

            def x_copy(index):
                source, target = ((dx_send, dx_recv), (vec1, vec_recv))[index]
                return remote(
                    source, target, x_send_sem.at[index], x_recv_sem.at[index], beside, core
                )

            @pl.when(step == chunks + 1)
            def _():
                dx_send[...] = dx_keep[at(beside * place_rows, place_rows), :].astype(BF16)
                x_copy(0).start()
                x_copy(1).start()
                dx_out[...] = dx_keep[at(me * place_rows, place_rows), :]
                x_copy(0).wait_recv()
                x_copy(1).wait_recv()
                dx_other[...] = dx_recv[...].astype(F32)
                vec_other[...] = vec_recv[...]
                x_copy(0).wait_send()
                x_copy(1).wait_send()

        @pl.when(step == pl.num_programs(0) - 1)
        def _():
            for kind in ([] if top else [0]) + ([] if bottom else [1]):
                for chunk in range(chunks):
                    exchange(kind, chunk).wait_send()
            finish_swap()

    def rows(columns, behind):
        return pl.BlockSpec(
            (span, columns), lambda s: (jnp.clip(s - behind, 0, chunks - 1), 0)
        )

    vec = jax.ShapeDtypeStruct((8, VEC), F32)
    operands, in_specs, out_shape, out_specs, scratch = [], [], [], [], []
    if top:
        operands += list(entry)
        in_specs += [halves_spec(entry[0].shape, chunks, 0, span)]
    else:
        operands += list(entry)
        in_specs += [rows(features, 0)] * 3
        in_specs += [rows(width, ahead), rows(PAIR, ahead), rows(width, ahead)]
        in_specs += [
            pl.BlockSpec(
                (1, *entry[6].shape[1:]),
                lambda s: (above, 0, 0, 0),
                pipeline_mode=pl.Buffered(1),
            ),
            whole(entry[7]),
        ]
        narrow = jax.ShapeDtypeStruct((8, features), F32)
        out_shape += [narrow]
        out_specs += [whole_out((8, features))]
        scratch += [pltpu.VMEM((chunks, span, width), BF16)] * 2
    if not bottom:
        operands += list(upper[1:])
        in_specs += [rows(hidden_units, ahead)] * 2
        in_specs += [rows(width, ahead + 1), rows(PAIR, ahead + 1), rows(PAIR, ahead)]
        in_specs += [rows(mixed_features, ahead + 1)] + [ANYWHERE] * 3 + [whole(upper[10])]
        sums = [mixed_features, hidden_units, hidden_units]
        out_shape += [
            jax.ShapeDtypeStruct((total, width), F32),
            jax.ShapeDtypeStruct((total, mixed_features), BF16),
        ]
        out_shape += [jax.ShapeDtypeStruct((PAIR, size), F32) for size in sums] + [vec]
        out_specs += [rows(width, ahead + 1), rows(mixed_features, ahead + 1)]
        out_specs += [whole_out((PAIR, size)) for size in sums] + [whole_out((8, VEC))]
        scratch += [pltpu.VMEM((chunks, span, width), BF16)] * 2
        scratch += [
            pltpu.VMEM((2, span, width), F32),
            pltpu.VMEM((span, hidden_units), BF16),
            pltpu.VMEM((span, width), BF16),
            pltpu.VMEM((span, width), BF16),
            pltpu.VMEM(upper[7].shape[1:], BF16),
            pltpu.VMEM(upper[8].shape[1:], BF16),
            pltpu.VMEM(upper[9].shape[1:], BF16),
            pltpu.SemaphoreType.DMA((3,)),
        ]
    else:
        out_shape += [
            jax.ShapeDtypeStruct((place_rows, width), F32),
            jax.ShapeDtypeStruct((place_rows, width), F32),
            narrow,
        ]
        out_specs += [whole_out((place_rows, width))] * 2 + [whole_out((8, features))]
        scratch += [
            pltpu.VMEM((total, width), F32),
            pltpu.VMEM((place_rows, width), BF16),
            pltpu.VMEM((place_rows, width), BF16),
            pltpu.VMEM((8, features), F32),
            pltpu.SemaphoreType.DMA((2,)),
            pltpu.SemaphoreType.DMA((2,)),
        ]
    scratch += [pltpu.SemaphoreType.DMA((2, chunks))] * 2
    operands += swap.operands()
    in_specs += swap.in_specs()
    shapes, specs = swap.outputs()
    out_shape += shapes
    out_specs += specs
    scratch += swap.scratch()
    return pl.pallas_call(
        kernel,
        grid=(chunks + (1 if top else 2),),
        out_shape=out_shape,
        in_specs=in_specs,
        out_specs=out_specs,
        scratch_shapes=scratch,
        compiler_params=pltpu.CompilerParams(
            collective_id=identity, has_side_effects=True, vmem_limit_bytes=VMEM_BYTES
        ),
        name=f"rows_backward_{identity}",
    )(*operands)


def assemble(sums, vecs, lanes, n, features, hidden_units):
    place = lanes[1].shape[0]
    width = lanes[1].shape[1]
    half = PAIR // 2

    def kernel(*refs):
        refs = list(refs)

        def take(count):
            taken = refs[:count]
            del refs[:count]
            return taken

        qkvs, outs, ups, downs = take(LAYERS), take(LAYERS), take(LAYERS), take(LAYERS)
        vec_refs = [take(4) for _ in range(LAYERS)]
        out_lane, out_other, dx_own, dx_other = take(4)
        out_ref, dx_ref, gain1, shift1, g_qkv, b_qkv, g_out, b_out = take(8)
        gain2, shift2, g_up, b_up, g_down, b_down = take(6)
        out_own, sem = refs
        me = lax.axis_index("seq")
        x = lax.rem(me, 2)
        fetch = pltpu.make_async_copy(out_lane.at[at(me * place, place), :], out_own, sem)
        fetch.start()

        for layer in range(LAYERS):
            for part in range(3):
                g_qkv[layer, part] = qkvs[layer][:, part * features : (part + 1) * features]
            for ref, target in ((outs, g_out), (ups, g_up), (downs, g_down)):
                target[layer] = ref[layer][...]

        for layer, (entry_own, entry_other, upper_own, upper_other) in enumerate(vec_refs):
            line = slice(layer, layer + 1)
            for part in range(3):
                row = slice(part, part + 1)
                b_qkv[part, line, :] = entry_own[row, :] + entry_other[row, :]
            b_up[line, :] = upper_own[0:1, :hidden_units] + upper_other[0:1, :hidden_units]

            def owned(mine, other, row):
                wide = mine.shape[1]
                place = (me // 2) * PAIR
                pair = at(lax.rem(place, wide), PAIR)
                both = mine[row : row + 1, pair] + other[row : row + 1, pair]
                for later in range(1, width // wide):
                    line = slice(row + later, row + later + 1)
                    both = jnp.where(place // wide == later, mine[line, pair] + other[line, pair], both)
                return jnp.where(x == 0, both[:, :half], both[:, half:])

            gain1[line, :] = owned(entry_own, entry_other, 3)
            shift1[line, :] = owned(entry_own, entry_other, 5)
            b_down[line, :] = owned(upper_own, upper_other, 1)
            gain2[line, :] = owned(upper_own, upper_other, 2)
            shift2[line, :] = owned(upper_own, upper_other, 3)
            b_out[line, :] = owned(upper_own, upper_other, 4)

        def both_lanes(target, mine, other):
            target[:, 0, :] = jnp.where(x == 0, mine, other)
            target[:, 1, :] = jnp.where(x == 0, other, mine)

        both_lanes(dx_ref, dx_own[...], dx_other[...])
        fetch.wait()
        both_lanes(out_ref, out_own[...], out_other[...])

    def f32(*shape):
        return jax.ShapeDtypeStruct(shape, F32)

    in_vmem = pl.BlockSpec(memory_space=pltpu.VMEM)
    flat = []
    for kind in range(4):
        flat += [sums[layer][kind] for layer in range(LAYERS)]
    for layer in range(LAYERS):
        flat += list(vecs[layer])
    flat += list(lanes)
    small = f32(LAYERS, width // n)
    return pl.pallas_call(
        kernel,
        out_shape=(
            f32(place, 2, width),
            f32(place, 2, width),
            small,
            small,
            f32(LAYERS, 3, half, features),
            f32(3, LAYERS, features),
            f32(LAYERS, half, features),
            small,
            small,
            small,
            f32(LAYERS, half, hidden_units),
            f32(LAYERS, hidden_units),
            f32(LAYERS, half, hidden_units),
            small,
        ),
        in_specs=[in_vmem] * (len(flat) - 4) + [ANYWHERE] + [in_vmem] * 3,
        out_specs=(in_vmem,) * 14,
        scratch_shapes=[pltpu.VMEM((place, width), F32), pltpu.SemaphoreType.DMA],
        compiler_params=pltpu.CompilerParams(vmem_limit_bytes=VMEM_BYTES),
        name="assemble",
    )(*flat)


def per_chip(
    tokens,
    d_out,
    norm1_gain,
    norm1_shift,
    w_qkv,
    b_qkv,
    w_out,
    b_out,
    norm2_gain,
    norm2_shift,
    w_up,
    b_up,
    w_down,
    b_down,
    episode_frames,
    live,
):
    n = lax.axis_size("seq")
    rows = tokens.shape[0]
    features = w_qkv.shape[3]
    fixed, ahead = turn_constants(rows * n // FRAME)
    qkv, qkv_bias = w_qkv.transpose(0, 2, 1, 3), b_qkv.transpose(1, 0, 2)

    gathered, key_bias, frames, *projected = gather_and_project(
        tokens, live.T, episode_frames, norm1_gain, norm1_shift, qkv, qkv_bias, fixed, ahead, n
    )
    streams, kept, d_lane = [gathered], [], None
    for layer in range(LAYERS):
        following = None
        if layer + 1 < LAYERS:
            following = (qkv, norm1_gain, norm1_shift, qkv_bias, fixed, frames)
        results = layer_forward(
            layer,
            projected[0],
            key_bias,
            streams[layer],
            (w_out, w_up, w_down),
            (b_out, norm2_gain, norm2_shift, b_up, b_down),
            following,
            d_out if layer == 0 else None,
            n,
            1 + layer,
        )
        kept.append((*projected, *results[:8]))
        streams.append(results[8])
        if following is not None:
            projected = results[9:13]
        if layer == 0:
            d_lane = results[-1]

    sums = [[None] * 4 for _ in range(LAYERS)]
    vecs = [[None] * 4 for _ in range(LAYERS)]
    entry, later = (d_lane,), None
    for layer in reversed(range(LAYERS)):
        turned, first, unit1, scale1, probs, divisor, mixed = kept[layer][:7]
        unit2, scale2, second, act, slope = kept[layer][7:]
        upper = (
            layer,
            act,
            slope,
            unit2,
            scale2,
            second,
            mixed,
            w_out,
            w_up,
            w_down,
            norm2_gain,
        )
        identity = 1 + LAYERS + 2 * (LAYERS - 1 - layer)
        if later is None:
            results = rows_backward(entry, upper, identity, FRAME, Swap([], []))
        else:
            swap = Swap(later[:2], [(later[2], 0), (streams[LAYERS], rows)])
            vec1, *results = rows_backward(entry, upper, identity, FRAME, swap)
            results, swapped = results[:6], results[6:]
            sums[layer + 1][3], sums[layer + 1][0] = swapped[:2]
            vecs[layer + 1][3], out_other = swapped[2:]
            vecs[layer + 1][0] = vec1
        grad_middle, grad_mixed, out_sum, up_sum, down_sum, vec2 = results
        vecs[layer][2] = vec2
        last = layer == 0
        if last:
            swap = Swap([out_sum, up_sum], [(vec2, 0), (vecs[layer + 1][0], 0)])
        else:
            swap = Swap([out_sum, up_sum], [])
        results = attention_backward(
            probs,
            divisor,
            mixed,
            turned,
            grad_mixed,
            first,
            fixed,
            frames,
            swap,
            last,
            identity + 1,
        )
        grad_query, grad_key, grad_value, qkv_sum = results[:4]
        if last:
            sums[layer][:3] = [qkv_sum, *results[4:6]]
            vecs[layer][3], vecs[layer + 1][1] = results[6:8]
        else:
            sums[layer][1:3] = results[4:6]
            later = [down_sum, qkv_sum, vec2]
        entry = (
            layer,
            grad_query,
            grad_key,
            grad_value,
            unit1,
            scale1,
            grad_middle,
            qkv,
            norm1_gain,
        )
    vec1, dx_own, dx_other, vec_other, sums[0][3] = rows_backward(
        entry, None, 1 + 3 * LAYERS, FRAME, Swap([down_sum], [])
    )
    vecs[0][:2] = [vec1, vec_other]
    results = list(
        assemble(
            sums,
            vecs,
            (streams[LAYERS], out_other, dx_own, dx_other),
            n,
            features,
            w_up.shape[2],
        )
    )
    results[4] = results[4].transpose(0, 2, 1, 3)
    results[5] = results[5].transpose(1, 0, 2)
    results[6] = results[6].transpose(0, 2, 1)
    results[12] = results[12].transpose(0, 2, 1)
    return tuple(results)


def lane_fits(mesh, tokens):
    n = mesh.shape["seq"]
    positions, lanes, width = tokens.shape
    rows = positions // n
    return (
        lanes == 2
        and n % 4 == 0
        and positions <= 4 * FRAME
        and positions % FRAME == 0
        and FRAME % rows == 0
        and width // n * 2 == PAIR
        and mesh.shape["tp"] == 2
    )


def solution(mesh):
    placed = (
        P("seq", None, None),
        P("seq", None, None),
        P(),
        P(),
        P(None, None, None, "tp"),
        P(None, None, "tp"),
        P(None, "tp", None),
        P(),
        P(),
        P(),
        P(None, None, "tp"),
        P(None, "tp"),
        P(None, "tp", None),
        P(),
        P(),
        P("seq", None),
    )
    def mapped(body):
        return jax.shard_map(
            body,
            mesh=mesh,
            in_specs=placed,
            out_specs=(
                P("seq", None, None),
                P("seq", None, None),
                P(None, "seq"),
                P(None, "seq"),
                P(None, "seq", None, "tp"),
                P(None, None, "tp"),
                P(None, "tp", "seq"),
                P(None, "seq"),
                P(None, "seq"),
                P(None, "seq"),
                P(None, "seq", "tp"),
                P(None, "tp"),
                P(None, "tp", "seq"),
                P(None, "seq"),
            ),
            check_vma=False,
        )

    def run(tokens, *others):
        if lane_fits(mesh, tokens):
            return mapped(per_chip)(tokens, *others)
        return mapped(per_device)(tokens, *others)

    return run
```

```python
import math

import jax
import jax.numpy as jnp
import numpy as np
from jax import lax
from jax.experimental import pallas as pl
from jax.experimental.pallas import tpu as pltpu
from jax.sharding import PartitionSpec as P

HEAD_DIM = 64
GRID = 16
FRAME = 256
LAYERS = 2
MICRO = 2


EPSILON = 1e-06
MASKED = -1e30
SCORE_SCALE = 0.125


def layer_norm(stream, norm_gain, norm_shift):
    center = stream - jnp.mean(stream, axis=-1, keepdims=True)
    spread = jnp.mean(center * center, axis=-1, keepdims=True)
    return center * lax.rsqrt(spread + EPSILON) * norm_gain + norm_shift


def rotate(values, frame_place, row_place, column_place):
    frequency = jnp.exp(jnp.arange(10, dtype=jnp.float32) * (-math.log(10000.0) / 10.0))
    pieces = []
    for section, place in enumerate((frame_place, row_place, column_place)):
        lower = values[..., 20 * section : 20 * section + 10]
        upper = values[..., 20 * section + 10 : 20 * section + 20]
        angles = place.astype(jnp.float32)[..., None, None] * frequency
        cosine = jnp.cos(angles)
        sine_part = jnp.sin(angles)
        pieces.append(lower * cosine - upper * sine_part)
        pieces.append(lower * sine_part + upper * cosine)
    pieces.append(values[..., 60:])
    return jnp.concatenate(pieces, axis=-1)


def episode_tags(frame_counts, positions):
    endings = jnp.cumsum(frame_counts) * FRAME
    passed = (positions[:, None] >= endings[None, :]).astype(jnp.int32)
    episode = jnp.sum(passed, axis=1)
    opening = jnp.sum(passed * frame_counts[None, :], axis=1)
    frame_index = positions // FRAME - opening
    within = positions % FRAME
    return (episode, frame_index, within // GRID, within % GRID)


def gelu_exact(values):
    return jax.nn.gelu(values, approximate=False)


def sum_heads(partial_sum):
    return lax.psum(partial_sum.astype(jnp.bfloat16), "tp").astype(jnp.float32)


def sum_inputs(partial_sum):
    return lax.psum(partial_sum.astype(jnp.bfloat16), "tp").astype(jnp.float32)


def lane_scores(query, keys_all, lane_index, query_tags, key_tags):
    head_count = query.shape[2] // HEAD_DIM
    query_lane = lax.dynamic_index_in_dim(query, lane_index, 1, False).reshape(
        query.shape[0], head_count, HEAD_DIM
    )
    keys_lane = lax.dynamic_index_in_dim(keys_all, lane_index, 1, False).reshape(
        keys_all.shape[0], head_count, HEAD_DIM
    )
    query_episode, query_frame = [
        lax.dynamic_index_in_dim(item, lane_index, 1, False) for item in query_tags
    ]
    key_episode, key_frame, key_live = [
        lax.dynamic_index_in_dim(item, lane_index, 1, False) for item in key_tags
    ]
    allowed = (
        (query_episode[:, None] == key_episode[None, :])
        & (key_frame[None, :] <= query_frame[:, None])
        & (key_live[None, :] > 0)
    )
    scores = (
        jnp.einsum("qhd,khd->hqk", query_lane, keys_lane, preferred_element_type=jnp.float32)
        * SCORE_SCALE
    )
    return (jnp.where(allowed[None], scores, MASKED), query_lane, keys_lane)


def attend_forward(query, keys_all, values_all, query_tags, key_tags):
    rows_dev, lane_count, features = query.shape
    head_count = features // HEAD_DIM

    def one_lane(lane_index, carry):
        scores, query_lane, keys_lane = lane_scores(
            query, keys_all, lane_index, query_tags, key_tags
        )
        highest = jnp.max(scores, axis=-1, keepdims=True)
        shifted = jnp.exp(scores - highest)
        summed = jnp.sum(shifted, axis=-1, keepdims=True)
        attention = (shifted / summed).astype(jnp.bfloat16)
        values_lane = lax.dynamic_index_in_dim(values_all, lane_index, 1, False).reshape(
            values_all.shape[0], head_count, HEAD_DIM
        )
        result = jnp.einsum(
            "hqk,khd->qhd", attention, values_lane, preferred_element_type=jnp.float32
        ).reshape(rows_dev, 1, features)
        log_total = (highest + jnp.log(summed))[None, :, :, 0]
        return (result, log_total)

    initial = (
        jnp.zeros((rows_dev, lane_count, features), jnp.float32),
        jnp.zeros((lane_count, head_count, rows_dev), jnp.float32),
    )
    return lax.fori_loop(0, lane_count, one_lane, initial)


def attend_backward(query, keys_all, values_all, log_total, grad_mixed, query_tags, key_tags):
    rows_dev, lane_count, features = query.shape
    head_count = features // HEAD_DIM
    key_rows = keys_all.shape[0]

    def one_lane(lane_index, carry):
        scores, query_lane, keys_lane = lane_scores(
            query, keys_all, lane_index, query_tags, key_tags
        )
        values_lane = lax.dynamic_index_in_dim(values_all, lane_index, 1, False).reshape(
            key_rows, head_count, HEAD_DIM
        )
        grad_lane = lax.dynamic_index_in_dim(grad_mixed, lane_index, 1, False).reshape(
            rows_dev, head_count, HEAD_DIM
        )
        attention = jnp.exp(
            scores - lax.dynamic_index_in_dim(log_total, lane_index, 0, False)[:, :, None]
        )
        grad_attention = jnp.einsum(
            "qhd,khd->hqk", grad_lane, values_lane, preferred_element_type=jnp.float32
        )
        inner = jnp.sum(attention * grad_attention, axis=-1, keepdims=True)
        grad_scores = (attention * (grad_attention - inner)).astype(jnp.bfloat16)
        query_part = (
            jnp.einsum("hqk,khd->qhd", grad_scores, keys_lane, preferred_element_type=jnp.float32)
            * SCORE_SCALE
        )
        key_part = (
            jnp.einsum("hqk,qhd->khd", grad_scores, query_lane, preferred_element_type=jnp.float32)
            * SCORE_SCALE
        )
        value_part = jnp.einsum(
            "hqk,qhd->khd",
            attention.astype(jnp.bfloat16),
            grad_lane,
            preferred_element_type=jnp.float32,
        )
        stacked = jnp.stack(
            [key_part.reshape(key_rows, features), value_part.reshape(key_rows, features)], axis=1
        )
        key_terms = stacked[:, None]
        grad_query = query_part.reshape(rows_dev, 1, features)
        return (grad_query, key_terms)

    initial = (
        jnp.zeros((rows_dev, lane_count, features), jnp.float32),
        jnp.zeros((key_rows, lane_count, 2, features), jnp.float32),
    )
    return lax.fori_loop(0, lane_count, one_lane, initial)


def front(stream, layer_index, params, query_tags, key_tags, positions):
    (
        gain_one,
        shift_one,
        mat_qkv,
        bias_qkv,
        mat_out,
        bias_out,
        gain_two,
        shift_two,
        mat_up,
        bias_up,
        mat_down,
        bias_down,
    ) = [item[layer_index] for item in params]
    rows_dev, lane_count, width = stream.shape
    features = mat_qkv.shape[2]
    head_count = features // HEAD_DIM
    frame_place, row_place, column_place = positions
    first = layer_norm(stream, gain_one, shift_one).astype(jnp.bfloat16)
    projected = (
        jnp.einsum("tbd,dcf->tbcf", first, mat_qkv, preferred_element_type=jnp.float32) + bias_qkv
    )
    split = projected.reshape(rows_dev, lane_count, 3, head_count, HEAD_DIM)
    query = (
        rotate(split[:, :, 0], frame_place, row_place, column_place)
        .reshape(rows_dev, lane_count, features)
        .astype(jnp.bfloat16)
    )
    keys = (
        rotate(split[:, :, 1], frame_place, row_place, column_place)
        .reshape(rows_dev, lane_count, features)
        .astype(jnp.bfloat16)
    )
    values = projected[:, :, 2].astype(jnp.bfloat16)
    keys_all, values_all = (
        lax.all_gather(keys, "seq", axis=0, tiled=True),
        lax.all_gather(values, "seq", axis=0, tiled=True),
    )
    mixed_full, log_total = attend_forward(query, keys_all, values_all, query_tags, key_tags)
    mixed = mixed_full.astype(jnp.bfloat16)
    middle = (
        stream
        + sum_heads(jnp.einsum("tbf,fd->tbd", mixed, mat_out, preferred_element_type=jnp.float32))
        + bias_out
    )
    second = layer_norm(middle, gain_two, shift_two).astype(jnp.bfloat16)
    hidden = jnp.einsum("tbd,df->tbf", second, mat_up, preferred_element_type=jnp.float32) + bias_up
    activation = gelu_exact(hidden).astype(jnp.bfloat16)
    return (
        first,
        query,
        keys_all,
        values_all,
        log_total,
        mixed,
        middle,
        second,
        hidden,
        activation,
        mixed_full,
    )


def layer_backward(stream, gradient, layer_index, params, query_tags, key_tags, positions):
    (
        gain_one,
        shift_one,
        mat_qkv,
        bias_qkv,
        mat_out,
        bias_out,
        gain_two,
        shift_two,
        mat_up,
        bias_up,
        mat_down,
        bias_down,
    ) = [item[layer_index] for item in params]
    (
        first,
        query,
        keys_all,
        values_all,
        log_total,
        mixed,
        middle,
        second,
        hidden,
        activation,
        mixed_full,
    ) = front(stream, layer_index, params, query_tags, key_tags, positions)
    frame_place, row_place, column_place = positions
    rows_dev, lane_count, width = stream.shape
    features = query.shape[2]
    head_count = features // HEAD_DIM
    grad_low = gradient.astype(jnp.bfloat16)
    grad_w_down = jnp.einsum(
        "tbf,tbd->fd", activation, grad_low, preferred_element_type=jnp.float32
    )
    grad_b_down = jnp.sum(gradient, axis=(0, 1))
    grad_activation = jnp.einsum(
        "tbd,fd->tbf", grad_low, mat_down, preferred_element_type=jnp.float32
    )
    grad_hidden = jax.vjp(gelu_exact, hidden)[1](grad_activation)[0].astype(jnp.bfloat16)
    grad_b_up = jnp.sum(grad_hidden.astype(jnp.float32), axis=(0, 1))
    grad_w_up = jnp.einsum("tbd,tbf->df", second, grad_hidden, preferred_element_type=jnp.float32)
    grad_second = sum_inputs(
        jnp.einsum("tbf,df->tbd", grad_hidden, mat_up, preferred_element_type=jnp.float32)
    )
    middle_pull = jax.vjp(layer_norm, middle, gain_two, shift_two)[1]
    grad_inner, grad_gain_two, grad_shift_two = middle_pull(grad_second)
    grad_middle = gradient + grad_inner
    grad_b_out = jnp.sum(grad_middle, axis=(0, 1))
    middle_low = grad_middle.astype(jnp.bfloat16)
    grad_w_out = jnp.einsum("tbf,tbd->fd", mixed, middle_low, preferred_element_type=jnp.float32)
    grad_mixed = jnp.einsum(
        "tbd,fd->tbf", middle_low, mat_out, preferred_element_type=jnp.float32
    ).astype(jnp.bfloat16)
    grad_query, key_terms = attend_backward(
        query, keys_all, values_all, log_total, grad_mixed, query_tags, key_tags
    )
    returned = lax.psum_scatter(key_terms, "seq", scatter_dimension=0, tiled=True)
    turned_query = rotate(
        grad_query.reshape(rows_dev, lane_count, head_count, HEAD_DIM),
        -frame_place,
        -row_place,
        -column_place,
    )
    turned_keys = rotate(
        returned[:, :, 0].reshape(rows_dev, lane_count, head_count, HEAD_DIM),
        -frame_place,
        -row_place,
        -column_place,
    )
    grad_projected = jnp.stack(
        [
            turned_query.reshape(rows_dev, lane_count, features),
            turned_keys.reshape(rows_dev, lane_count, features),
            returned[:, :, 1],
        ],
        axis=2,
    ).astype(jnp.bfloat16)
    grad_b_qkv = jnp.sum(grad_projected.astype(jnp.float32), axis=(0, 1))
    grad_w_qkv = jnp.einsum(
        "tbd,tbcf->dcf", first, grad_projected, preferred_element_type=jnp.float32
    )
    grad_first = sum_inputs(
        jnp.einsum("tbcf,dcf->tbd", grad_projected, mat_qkv, preferred_element_type=jnp.float32)
    )
    first_pull = jax.vjp(layer_norm, stream, gain_one, shift_one)[1]
    grad_entry, grad_gain_one, grad_shift_one = first_pull(grad_first)
    grads = (
        grad_gain_one,
        grad_shift_one,
        grad_w_qkv,
        grad_b_qkv,
        grad_w_out,
        grad_b_out,
        grad_gain_two,
        grad_shift_two,
        grad_w_up,
        grad_b_up,
        grad_w_down,
        grad_b_down,
    )
    return (grad_middle + grad_entry, grads)


def per_device(
    tokens,
    d_out,
    norm1_gain,
    norm1_shift,
    w_qkv,
    b_qkv,
    w_out,
    b_out,
    norm2_gain,
    norm2_shift,
    w_up,
    b_up,
    w_down,
    b_down,
    episode_frames,
    live,
):
    rows_dev = tokens.shape[0]
    lane_count = tokens.shape[1] // MICRO
    total_rows = rows_dev * lax.axis_size("seq")
    local_positions = lax.axis_index("seq") * rows_dev + jnp.arange(rows_dev, dtype=jnp.int32)
    key_positions = jnp.arange(total_rows, dtype=jnp.int32)
    tagger = jax.vmap(episode_tags, in_axes=(0, None), out_axes=1)
    query_episode, query_frame, query_row, query_column = tagger(episode_frames, local_positions)
    key_episode, key_frame, key_row, key_column = tagger(episode_frames, key_positions)
    live_keys = lax.all_gather(live, "seq", axis=0, tiled=True)
    params = (
        norm1_gain,
        norm1_shift,
        w_qkv,
        b_qkv,
        w_out,
        b_out,
        norm2_gain,
        norm2_shift,
        w_up,
        b_up,
        w_down,
        b_down,
    )
    layer_grads = [None] * LAYERS
    outputs = []
    grad_tokens = []
    for micro_index in range(MICRO):
        first_lane = micro_index * lane_count
        last_lane = first_lane + lane_count
        query_tags = (query_episode[:, first_lane:last_lane], query_frame[:, first_lane:last_lane])
        key_tags = (
            key_episode[:, first_lane:last_lane],
            key_frame[:, first_lane:last_lane],
            live_keys[:, first_lane:last_lane],
        )
        positions = (
            query_frame[:, first_lane:last_lane],
            query_row[:, first_lane:last_lane],
            query_column[:, first_lane:last_lane],
        )
        stream = tokens[:, first_lane:last_lane].astype(jnp.float32)
        inputs = []
        gathered = []
        for layer_index in range(LAYERS):
            inputs.append(stream)
            layer_state = front(stream, layer_index, params, query_tags, key_tags, positions)
            gathered.append((layer_state[2], layer_state[3]))
            branch = jnp.einsum(
                "tbf,fd->tbd",
                layer_state[9],
                w_down[layer_index],
                preferred_element_type=jnp.float32,
            )
            stream = layer_state[6] + sum_heads(branch) + b_down[layer_index]
        outputs.append(stream)
        gradient = d_out[:, first_lane:last_lane]
        for layer_index in reversed(range(LAYERS)):
            gradient, grads = layer_backward(
                inputs[layer_index], gradient, layer_index, params, query_tags, key_tags, positions
            )
            if layer_grads[layer_index] is None:
                layer_grads[layer_index] = grads
            else:
                layer_grads[layer_index] = jax.tree.map(jnp.add, layer_grads[layer_index], grads)
        grad_tokens.append(gradient)
    stacked = [
        jnp.stack([layer_grads[layer_index][entry] for layer_index in range(LAYERS)])
        for entry in range(12)
    ]
    (
        grad_gain_one,
        grad_shift_one,
        grad_w_qkv,
        grad_b_qkv,
        grad_w_out,
        grad_b_out,
        grad_gain_two,
        grad_shift_two,
        grad_w_up,
        grad_b_up,
        grad_w_down,
        grad_b_down,
    ) = stacked
    in_sums = (
        lax.psum_scatter(grad_w_qkv, "seq", scatter_dimension=1, tiled=True),
        lax.psum_scatter(grad_w_up, "seq", scatter_dimension=1, tiled=True),
        lax.psum_scatter(grad_gain_one, "seq", scatter_dimension=1, tiled=True),
        lax.psum_scatter(grad_shift_one, "seq", scatter_dimension=1, tiled=True),
        lax.psum_scatter(grad_gain_two, "seq", scatter_dimension=1, tiled=True),
        lax.psum_scatter(grad_shift_two, "seq", scatter_dimension=1, tiled=True),
        lax.psum_scatter(grad_b_out, "seq", scatter_dimension=1, tiled=True),
        lax.psum_scatter(grad_b_down, "seq", scatter_dimension=1, tiled=True),
    )
    out_sums = (
        lax.psum_scatter(grad_w_out, "seq", scatter_dimension=2, tiled=True),
        lax.psum_scatter(grad_w_down, "seq", scatter_dimension=2, tiled=True),
    )
    bias_total = lax.psum((grad_b_qkv, grad_b_up), "seq")
    return (
        jnp.concatenate(outputs, axis=1),
        jnp.concatenate(grad_tokens, axis=1),
        in_sums[2],
        in_sums[3],
        in_sums[0],
        bias_total[0],
        out_sums[0],
        in_sums[6],
        in_sums[4],
        in_sums[5],
        in_sums[1],
        bias_total[1],
        out_sums[1],
        in_sums[7],
    )


MESH = pl.DeviceIdType.MESH
BF16 = jnp.bfloat16
F32 = jnp.float32
VMEM_BYTES = 60 * 1024 * 1024
PAIR = 128
VEC = 2048


def nn(left, right):
    return lax.dot_general(left, right, (((1,), (0,)), ((), ())), preferred_element_type=F32)


def nt(left, right):
    return lax.dot_general(left, right, (((1,), (1,)), ((), ())), preferred_element_type=F32)


def tn(left, right):
    return lax.dot_general(left, right, (((0,), (0,)), ((), ())), preferred_element_type=F32)


def at(start, size):
    return pl.ds(pl.multiple_of(start, size), size)


def repeat(count, body):
    def one(index, carry):
        body(index)
        return carry

    lax.fori_loop(0, count, one, 0)


def remote(src, dst, send, recv, seq, tp):
    return pltpu.make_async_remote_copy(
        src_ref=src,
        dst_ref=dst,
        send_sem=send,
        recv_sem=recv,
        device_id=(seq, tp),
        device_id_type=MESH,
    )


def hello(partners):
    barrier = pltpu.get_barrier_semaphore()
    for seq, tp in partners:
        pl.semaphore_signal(barrier, inc=1, device_id=(seq, tp), device_id_type=MESH)


def met(partners):
    pl.semaphore_wait(pltpu.get_barrier_semaphore(), len(partners))


def whole(array):
    zeros = (0,) * array.ndim
    return pl.BlockSpec(array.shape, lambda s: zeros, pipeline_mode=pl.Buffered(1))


def whole_out(shape):
    zeros = (0,) * len(shape)
    return pl.BlockSpec(shape, lambda s: zeros)


ANYWHERE = pl.BlockSpec(memory_space=pl.ANY)


def turn_row(table, place, section):
    frequency = np.exp(np.arange(10, dtype=np.float32) * np.float32(-math.log(10000.0) / 10.0))
    angle = place.astype(np.float32)[:, None] * frequency
    for base in range(20 * section, PAIR, HEAD_DIM):
        table[0, :, base : base + 10] = np.cos(angle)
        table[0, :, base + 10 : base + 20] = np.cos(angle)
        table[1, :, base : base + 10] = -np.sin(angle)
        table[2, :, base + 10 : base + 20] = np.sin(angle)


def turn_constants(frames):
    within, ahead = np.zeros((3, FRAME, PAIR), np.float32), np.zeros((3, frames, PAIR), np.float32)
    turn_row(within, np.arange(FRAME) // GRID, 1)
    turn_row(within, np.arange(FRAME) % GRID, 2)
    for base in range(60, PAIR, HEAD_DIM):
        within[0, :, base : base + 4] = 1.0
    turn_row(ahead, np.arange(frames), 0)
    return jnp.asarray(within), jnp.asarray(ahead)


def turn(values, tables, back=False):
    cosine, lower, upper = tables
    pieces = []
    for start in range(0, values.shape[1], PAIR):
        slab = values[:, start : start + PAIR]
        moved = pltpu.roll(slab, PAIR - 10, 1) * lower + pltpu.roll(slab, 10, 1) * upper
        pieces.append(slab * cosine - moved if back else slab * cosine + moved)
    return jnp.concatenate(pieces, axis=1)


def tables_of(fixed_ref, frames_ref, chunk):
    return [fixed_ref[i] + frames_ref[i, pl.ds(chunk, 1), :] for i in range(3)]


def normed(stream):
    center = stream - jnp.mean(stream, axis=-1, keepdims=True)
    spread = jnp.mean(center * center, axis=-1, keepdims=True)
    scale = lax.rsqrt(spread + EPSILON)
    return center * scale, scale


def norm_pull(grad, gain, unit, scale):
    scaled = grad * gain
    return scale * (
        scaled
        - jnp.mean(scaled, axis=-1, keepdims=True)
        - unit * jnp.mean(scaled * unit, axis=-1, keepdims=True)
    )


def keep_norm(unit, scale, unit_ref, scale_ref):
    unit_ref[...] = unit.astype(BF16)
    scale_ref[...] = jnp.broadcast_to(scale, scale_ref.shape)


def kept_norm(unit_ref, scale_ref):
    copies = unit_ref.shape[1] // scale_ref.shape[1]
    return unit_ref[...].astype(F32), jnp.concatenate([scale_ref[...]] * copies, axis=1)


def column_sum(values):
    return jnp.sum(values, axis=0, keepdims=True)


def gelu_both(hidden):
    normal = 0.5 + 0.5 * lax.erf(hidden * math.sqrt(0.5))
    density = jnp.exp(hidden * hidden * -0.5) * (1.0 / math.sqrt(2.0 * math.pi))
    return hidden * normal, normal + hidden * density


def project(stream, chunk, layer, pair, refs, outs, first_full):
    gain, shift, weight, bias, fixed, frames = refs
    qkv_ref, first_ref, unit_ref, scale_ref = outs
    unit, scale = normed(stream)
    keep_norm(unit, scale, unit_ref, scale_ref)
    first_full[...] = (unit * gain[layer : layer + 1, :] + shift[layer : layer + 1, :]).astype(BF16)
    first_ref[...] = first_full[:, at(pair * PAIR, PAIR)]
    cosine, lower, upper = tables_of(fixed, frames, chunk)

    def one(part):
        still = part == 2
        tables = (
            jnp.where(still, 1.0, cosine),
            jnp.where(still, 0.0, lower),
            jnp.where(still, 0.0, upper),
        )
        values = nn(first_full[...], weight[part]) + bias[part, layer : layer + 1, :]
        qkv_ref[part] = (turn(values, tables) * jnp.where(part == 0, SCORE_SCALE, 1.0)).astype(BF16)

    repeat(3, one)


class Relay:
    sems = 6

    def __init__(self, n, rows, buffer, other, sems, lives=None, live_other=None):
        self.n, self.rows, self.buffer, self.other = n, rows, buffer, other
        self.lives, self.live_other = lives, live_other
        self.z_send, self.z_recv, self.y_send, self.y_recv, self.c_send, self.c_recv = sems
        self.planes = n // 4
        self.me, self.core = lax.axis_index("seq"), lax.axis_index("tp")
        me = self.me
        self.x, self.y, self.z = lax.rem(me, 2), lax.rem(me // 2, 2), me // 4
        self.across = me + 2 - 4 * self.y

    @staticmethod
    def scratch(n):
        dma, planes = pltpu.SemaphoreType.DMA, n // 4
        shapes = [(planes, 2, 2)] * 2 + [(planes, 2)] * 2 + [(2 * planes,)] * 2
        return [dma(shape) for shape in shapes]

    @property
    def events(self):
        return self.planes

    def plane(self, step):
        return lax.rem(self.z + step, self.planes)

    def place(self, plane, lane):
        return plane * 4 + self.y * 2 + lane

    def reached(self):
        return [(step, far) for step in range(self.planes) for far in (0, 1) if step or far]

    def hello(self):
        barrier = pltpu.get_barrier_semaphore()
        partners = [(self.across, self.core), (self.me, 1 - self.core)]
        for step, far in self.reached():
            lane = 1 - self.x if far else self.x
            partners.append((self.place(self.plane(step), lane), self.core))
        for seq, tp in partners:
            pl.semaphore_signal(barrier, inc=1, device_id=(seq, tp), device_id_type=MESH)

    def met(self):
        pl.semaphore_wait(pltpu.get_barrier_semaphore(), 2 + len(self.reached()))

    def rows_of(self, side, seq):
        return self.buffer.at[side, at(seq * self.rows, self.rows), :]

    def block(self, side, pair):
        return self.buffer.at[side, at(pair * 2 * self.rows, 2 * self.rows), :]

    def items(self, pair):
        found = [self.block(self.core, pair)]
        if self.lives is not None:
            found.append(self.lives.at[at(pair * 2, 2)])
        return found

    def each(self, copy, what):
        for index in range(1 if self.lives is None else 2):
            getattr(copy(index), what)()

    def z_copy(self, step, far):
        def copy(index):
            lane = 1 - self.x if far else self.x
            if index == 0:
                source = self.other.at[self.core] if far else self.rows_of(self.core, self.me)
                target = self.rows_of(self.core, self.me)
            else:
                source = self.live_other if far else self.lives.at[self.me]
                target = self.lives.at[self.me]
            return remote(
                source,
                target,
                self.z_send.at[step, far, index],
                self.z_recv.at[step, far, index],
                self.place(self.plane(step), lane),
                self.core,
            )

        return copy

    def y_copy(self, plane, row):
        def copy(index):
            item = self.items(plane * 2 + row)[index]
            return remote(
                item,
                item,
                self.y_send.at[plane, index],
                self.y_recv.at[plane, index],
                self.across,
                self.core,
            )

        return copy

    def c_copy(self, pair, side):
        item = self.block(side, pair)
        return remote(
            item, item, self.c_send.at[pair], self.c_recv.at[pair], self.me, 1 - self.core
        )

    def begin(self):
        for step, far in self.reached():
            self.each(self.z_copy(step, far), "start")

    def arrive(self, event):
        for far in (0, 1) if event else (1,):
            self.each(self.z_copy(event, far), "wait_recv")
        plane = self.plane(self.planes - event)
        self.each(self.y_copy(plane, self.y), "start")
        self.c_copy(plane * 2 + self.y, self.core).start()

    def complete(self, event):
        plane = self.plane(self.planes - event)
        self.each(self.y_copy(plane, 1 - self.y), "wait_recv")
        self.c_copy(plane * 2 + 1 - self.y, self.core).start()

    def ready(self, event):
        plane = self.plane(self.planes - event)
        self.c_copy(plane * 2, 1 - self.core).wait_recv()
        self.c_copy(plane * 2 + 1, 1 - self.core).wait_recv()
        return plane

    def finish(self):
        for step, far in self.reached():
            self.each(self.z_copy(step, far), "wait_send")
        for plane in range(self.planes):
            self.each(self.y_copy(plane, self.y), "wait_send")
        for pair in range(2 * self.planes):
            self.c_copy(pair, self.core).wait_send()


def split_lanes(values, x, buffer, other, start, rows):
    half = values.shape[2] // 2
    zero, one = values[:, 0, :], values[:, 1, :]
    own, far = jnp.where(x == 0, zero, one), jnp.where(x == 0, one, zero)
    core = lax.axis_index("tp")
    own = jnp.where(core == 0, own[:, :half], own[:, half:]).astype(BF16)
    buffer[core, at(start, rows), :] = own
    for side in range(2):
        other[side] = far[:, side * half : (side + 1) * half].astype(BF16)


def gather_and_project(tokens, live, episode_frames, gain, shift, qkv, bias, fixed, ahead, n):
    rows, lanes, width = tokens.shape
    half = width // 2
    total = n * rows
    chunks = total // FRAME
    per_frame = FRAME // rows
    features = qkv.shape[3]
    slots = episode_frames.shape[1]

    def kernel(*refs):
        refs = list(refs)

        def take(count):
            taken = refs[:count]
            del refs[:count]
            return taken

        tokens_ref, live_ref, counts_ref, gain_ref, shift_ref, w_any, bias_ref = take(7)
        fixed_ref, ahead_ref = take(2)
        all_ref, mask_ref, frames_ref = take(3)
        qkv_ref, *projected = take(4)
        other, lives, live_other, weight, full, w_sem = take(6)
        relay = Relay(n, rows, all_ref, other, take(Relay.sems), lives, live_other)
        load = pltpu.make_async_copy(w_any.at[0], weight, w_sem)
        load.start()
        relay.hello()
        x, me = relay.x, relay.me
        split_lanes(tokens_ref[...].astype(F32), x, all_ref, other, me * rows, rows)
        lane = lax.broadcasted_iota(jnp.int32, (1, FRAME), 1)
        here = lane // rows == lax.rem(me, per_frame)
        tiles = []
        for index in range(lanes):
            alive = live_ref[index : index + 1, :].astype(F32)
            alive = jnp.where(here, jnp.concatenate([alive] * per_frame, axis=1), 0.0)
            tiles.append(jnp.broadcast_to(alive, (8, FRAME)))
        lives[me] = jnp.where(x == 0, tiles[0], tiles[1])
        live_other[...] = jnp.where(x == 0, tiles[1], tiles[0])
        relay.met()
        relay.begin()

        counts = [counts_ref[x, slot] for slot in range(slots)]
        episodes, openings = [], []
        for frame in range(chunks):
            end, episode, opening = 0, 0, 0
            for slot in range(slots):
                end = end + counts[slot]
                passed = frame >= end
                episode = episode + passed.astype(jnp.int32)
                opening = opening + jnp.where(passed, counts[slot], 0)
            episodes.append(episode)
            openings.append(frame - opening)
        for index in range(3):
            table = []
            for frame in range(chunks):
                line = jnp.zeros((1, PAIR), F32)
                for choice in range(chunks):
                    line = jnp.where(
                        openings[frame] == choice, ahead_ref[index, choice : choice + 1, :], line
                    )
                table.append(line)
            frames_ref[index] = jnp.concatenate(
                table + [jnp.zeros((8 - chunks, PAIR), F32)], axis=0
            )
        load.wait()

        def project_frame(frame):
            place = at(frame * FRAME, FRAME)
            stream = jnp.concatenate([all_ref[0, place, :], all_ref[1, place, :]], axis=1)
            project(
                stream.astype(F32),
                frame,
                0,
                me // 2,
                (gain_ref, shift_ref, weight, bias_ref, fixed_ref, frames_ref),
                [qkv_ref.at[:, place, :]] + [ref.at[place, :] for ref in projected],
                full,
            )

        for event in range(relay.events):
            relay.arrive(event)
        for event in range(relay.events):
            relay.complete(event)
            if event:
                project_frame(relay.ready(event - 1))
        project_frame(relay.ready(relay.events - 1))
        relay.finish()

        for key_frame in range(chunks):
            alive = lives[key_frame * per_frame, 0:1, :]
            for part in range(1, per_frame):
                alive = alive + lives[key_frame * per_frame + part, 0:1, :]
            closed = (alive - 1.0) * -MASKED
            lines = []
            for query_frame in range(chunks):
                allowed = (episodes[query_frame] == episodes[key_frame]) & (
                    openings[key_frame] <= openings[query_frame]
                )
                lines.append(jnp.where(allowed, closed, MASKED))
            lines.append(jnp.zeros((PAIR - chunks, FRAME), F32))
            mask_ref[key_frame * FRAME : (key_frame + 1) * FRAME, :] = jnp.concatenate(
                lines, axis=0
            ).T.astype(BF16)

    in_vmem = pl.BlockSpec(memory_space=pltpu.VMEM)
    in_smem = pl.BlockSpec(memory_space=pltpu.SMEM)
    return pl.pallas_call(
        kernel,
        out_shape=(
            jax.ShapeDtypeStruct((2, total, half), BF16),
            jax.ShapeDtypeStruct((total, PAIR), BF16),
            jax.ShapeDtypeStruct((3, 8, PAIR), F32),
            jax.ShapeDtypeStruct((3, total, features), BF16),
            jax.ShapeDtypeStruct((total, PAIR), BF16),
            jax.ShapeDtypeStruct((total, width), BF16),
            jax.ShapeDtypeStruct((total, PAIR), F32),
        ),
        in_specs=[in_vmem, in_vmem, in_smem, in_vmem, in_vmem, ANYWHERE] + [in_vmem] * 3,
        out_specs=(in_vmem,) * 7,
        scratch_shapes=[
            pltpu.VMEM((2, rows, half), BF16),
            pltpu.VMEM((n, 8, FRAME), F32),
            pltpu.VMEM((8, FRAME), F32),
            pltpu.VMEM(qkv.shape[1:], BF16),
            pltpu.VMEM((FRAME, width), BF16),
            pltpu.SemaphoreType.DMA,
        ]
        + Relay.scratch(n),
        compiler_params=pltpu.CompilerParams(
            collective_id=0, has_side_effects=True, vmem_limit_bytes=VMEM_BYTES
        ),
        name="gather_and_project",
    )(tokens, live, episode_frames, gain, shift, qkv, bias, fixed, ahead)


def halves(ref):
    return jnp.concatenate([ref[0], ref[1]], axis=1).astype(F32)


def halves_spec(shape, chunks, behind, span=FRAME):
    return pl.BlockSpec(
        (2, span, shape[2]), lambda s: (0, jnp.clip(s - behind, 0, chunks - 1), 0)
    )


def layer_forward(layer, turned, key_bias, stream, mats, rows_of, next_refs, d_out, n, identity):
    _, total, features = turned.shape
    split = stream.ndim == 3
    width = mats[1].shape[1]
    rows_here = total // n
    hidden_units = mats[1].shape[2]
    chunks = total // FRAME
    heads = features // HEAD_DIM
    slabs = features // PAIR
    columns = 256
    last = next_refs is None
    b_out, gain, shift, b_up, b_down = rows_of
    mat_out, mat_up, mat_down = mats

    def kernel(*refs):
        refs = list(refs)

        def take(count):
            taken = refs[:count]
            del refs[:count]
            return taken

        q_ref, k_ref, v_ref, kb_ref, x_ref = take(5)
        wo_any, wu_any, wd_any = take(3)
        bo_ref, gain_ref, shift_ref, bu_ref, bd_ref = take(5)
        if not last:
            wq_any, ngain, nshift, nbias, fixed, frames = take(6)
        if d_out is not None:
            (d_ref,) = take(1)
        p_ref, r_ref, mixed_ref, unit_ref, scale_ref, second_ref, act_ref, gp_ref, x_out = take(9)
        if not last:
            next_outs = take(4)
        if d_out is not None:
            (d_all,) = take(1)
        wo, wu, wd, mid, full, next_full = take(6)
        if not last:
            (wq,) = take(1)
        a_send, a_recv, b_send, b_recv, w_sem, send_sem, recv_sem = take(7)
        relay = None
        if d_out is not None:
            buffer, other, d_sem = take(3)
            relay = Relay(n, rows_here, buffer, other, take(Relay.sems))

        step = pl.program_id(0)
        me, core = lax.axis_index("seq"), lax.axis_index("tp")

        items = [(wo_any, wo), (wu_any, wu), (wd_any, wd)]
        if not last:
            items.append((wq_any, wq))

        def load(index):
            source, target = items[index]
            return pltpu.make_async_copy(
                source.at[layer if index < 3 else layer + 1], target, w_sem.at[index]
            )

        def exchange(kind, chunk):
            source, target = ((a_send, a_recv), (b_send, b_recv))[kind]
            return remote(
                source.at[chunk],
                target.at[chunk],
                send_sem.at[kind, chunk],
                recv_sem.at[kind, chunk],
                me,
                1 - core,
            )

        @pl.when(step == 0)
        def _():
            for index in range(len(items)):
                load(index).start()
            if relay is None:
                hello([(me, 1 - core)])
            else:
                relay.hello()
                split_lanes(d_ref[...], relay.x, buffer, other, me * rows_here, rows_here)

        lane = lax.broadcasted_iota(jnp.int32, (1, PAIR), 1)
        sides = [(lane < HEAD_DIM).astype(F32).astype(BF16), (lane >= HEAD_DIM).astype(F32).astype(BF16)]
        for frame in range(chunks):

            @pl.when(step == frame)
            def _():
                keys = FRAME * (frame + 1)
                mask = kb_ref[:keys, :]
                asked = jnp.broadcast_to((lane == frame).astype(F32), (FRAME, PAIR)).astype(BF16)

                def two_slabs(couple):
                    def lanes_of(head):
                        return at((couple * 2 + head // 2) * PAIR, PAIR)

                    def score(head):
                        key = jnp.concatenate([k_ref[0, :keys, lanes_of(head)], mask], axis=1)
                        ask = q_ref[0, :, lanes_of(head)] * sides[head % 2]
                        return nt(jnp.concatenate([ask, asked], axis=1), key)

                    scores, sums = score(0), []
                    for head in range(4):
                        lanes, side = lanes_of(head), head % 2
                        following = score(head + 1) if head < 3 else None
                        highest = jnp.max(scores, axis=1, keepdims=True)
                        shifted = jnp.exp(scores - highest).astype(BF16)
                        p_ref[0, couple * 4 + head, :keys, :] = shifted.T
                        sums.append(nn(shifted, v_ref[0, :keys, lanes] * sides[side] + sides[1 - side]))
                        scores = following
                        if side == 1:
                            one, two = sums[head - 1 :]
                            low_side = lane < HEAD_DIM
                            divisor = 1.0 / jnp.where(
                                low_side, pltpu.roll(one, HEAD_DIM, 1), pltpu.roll(two, HEAD_DIM, 1)
                            )
                            r_ref[:, lanes] = divisor
                            mixed_ref[:, lanes] = (jnp.where(low_side, one, two) * divisor).astype(BF16)

                repeat(slabs // 2, two_slabs)

        @pl.when(step == 0)
        def _():
            load(0).wait()
            if relay is None:
                met([(me, 1 - core)])
            else:
                relay.met()
                relay.begin()

        @pl.when(step < chunks)
        def _():
            a_send[step] = nn(mixed_ref[...], wo[...]).astype(BF16)
            exchange(0, step).start()

        def feed_forward():
            chunk = step - 1
            middle = (halves(x_ref) if split else x_ref[...]) + (
                a_send[chunk].astype(F32) + a_recv[chunk].astype(F32)
            )
            middle = middle + bo_ref[layer : layer + 1, :]
            mid[lax.rem(chunk, 2)] = middle
            unit, scale = normed(middle)
            keep_norm(unit, scale, unit_ref, scale_ref)
            second = (unit * gain_ref[layer : layer + 1, :] + shift_ref[layer : layer + 1, :]).astype(BF16)
            full[...] = second
            second_ref[...] = full[:, at((me // 2) * PAIR, PAIR)]
            parts = [slice(start, start + columns) for start in range(0, hidden_units, columns)]
            hidden = nn(second, wu[:, parts[0]])
            for index, part in enumerate(parts):
                following = nn(second, wu[:, parts[index + 1]]) if index + 1 < len(parts) else None
                act, slope = gelu_both(hidden + bu_ref[layer : layer + 1, part])
                act_ref[:, part] = act.astype(BF16)
                gp_ref[:, part] = slope.astype(BF16)
                hidden = following
            b_send[chunk] = nn(act_ref[...], wd[...]).astype(BF16)

        def close():
            chunk = step - 2
            result = mid[lax.rem(chunk, 2)] + (b_send[chunk].astype(F32) + b_recv[chunk].astype(F32))
            result = result + bd_ref[layer : layer + 1, :]
            x_out[...] = result
            if not last:
                project(
                    result,
                    chunk,
                    layer + 1,
                    me // 2,
                    (ngain, nshift, wq, nbias, fixed, frames),
                    next_outs,
                    next_full,
                )

        @pl.when(step == 1)
        def _():
            load(1).wait()
            load(2).wait()

        @pl.when((step >= 1) & (step <= chunks))
        def _():
            exchange(0, step - 1).wait_recv()
            feed_forward()
            exchange(1, step - 1).start()

        if not last:

            @pl.when(step == 2)
            def _():
                load(3).wait()

        @pl.when(step >= 2)
        def _():
            exchange(1, step - 2).wait_recv()
            close()

        if relay is not None:
            for event in range(relay.events):

                @pl.when(step == 1 + event // 2)
                def _():
                    relay.arrive(event)

                @pl.when(step == 2 + event // 2)
                def _():
                    relay.complete(event)

            @pl.when(step == chunks + 1)
            def _():
                for event in range(relay.events):
                    relay.ready(event)
                relay.finish()
                pltpu.make_async_copy(buffer, d_all, d_sem).start()

        @pl.when(step == chunks + 1)
        def _():
            for kind in range(2):
                for chunk in range(chunks):
                    exchange(kind, chunk).wait_send()
            if relay is not None:
                pltpu.make_async_copy(buffer, d_all, d_sem).wait()

    def rows(columns, behind):
        return pl.BlockSpec(
            (FRAME, columns), lambda s: (jnp.clip(s - behind, 0, chunks - 1), 0)
        )

    def part_of(part):
        return pl.BlockSpec(
            (1, total, features), lambda s: (part, 0, 0), pipeline_mode=pl.Buffered(1)
        )

    in_specs = [
        pl.BlockSpec((1, FRAME, features), lambda s: (0, jnp.minimum(s, chunks - 1), 0)),
        part_of(1),
        part_of(2),
        whole(key_bias),
    ]
    in_specs += [halves_spec(stream.shape, chunks, 1) if split else rows(width, 1)]
    in_specs += [ANYWHERE] * 3 + [whole(item) for item in rows_of]
    operands = [turned, turned, turned, key_bias, stream, *mats, *rows_of]
    if not last:
        in_specs += [ANYWHERE] + [whole(item) for item in next_refs[1:]]
        operands += list(next_refs)
    if d_out is not None:
        in_specs += [whole(d_out)]
        operands += [d_out]
    out_shape = [
        jax.ShapeDtypeStruct((chunks, heads, total, FRAME), BF16),
        jax.ShapeDtypeStruct((total, features), F32),
        jax.ShapeDtypeStruct((total, features), BF16),
        jax.ShapeDtypeStruct((total, width), BF16),
        jax.ShapeDtypeStruct((total, PAIR), F32),
        jax.ShapeDtypeStruct((total, PAIR), BF16),
        jax.ShapeDtypeStruct((total, hidden_units), BF16),
        jax.ShapeDtypeStruct((total, hidden_units), BF16),
        jax.ShapeDtypeStruct((total, width), F32),
    ]
    out_specs = [
        pl.BlockSpec((1, heads, total, FRAME), lambda s: (jnp.minimum(s, chunks - 1), 0, 0, 0)),
        rows(features, 0),
        rows(features, 0),
        rows(width, 1),
        rows(PAIR, 1),
        rows(PAIR, 1),
        rows(hidden_units, 1),
        rows(hidden_units, 1),
        rows(width, 2),
    ]
    scratch = [
        pltpu.VMEM(mat_out.shape[1:], BF16),
        pltpu.VMEM(mat_up.shape[1:], BF16),
        pltpu.VMEM(mat_down.shape[1:], BF16),
        pltpu.VMEM((2, FRAME, width), F32),
        pltpu.VMEM((FRAME, width), BF16),
        pltpu.VMEM((FRAME, width), BF16),
    ]
    if not last:
        out_shape += [jax.ShapeDtypeStruct((3, total, features), BF16)]
        out_shape += [jax.ShapeDtypeStruct((total, PAIR), BF16)]
        out_shape += [jax.ShapeDtypeStruct((total, width), BF16)]
        out_shape += [jax.ShapeDtypeStruct((total, PAIR), F32)]
        out_specs += [
            pl.BlockSpec((3, FRAME, features), lambda s: (0, jnp.clip(s - 2, 0, chunks - 1), 0))
        ]
        out_specs += [rows(PAIR, 2), rows(width, 2), rows(PAIR, 2)]
    if d_out is not None:
        out_shape += [jax.ShapeDtypeStruct((2, total, width // 2), BF16)]
        out_specs += [ANYWHERE]
        scratch += [pltpu.VMEM(next_refs[0].shape[1:], BF16)]
    scratch += [pltpu.VMEM((chunks, FRAME, width), BF16)] * 4
    scratch += [
        pltpu.SemaphoreType.DMA((4,)),
        pltpu.SemaphoreType.DMA((2, chunks)),
        pltpu.SemaphoreType.DMA((2, chunks)),
    ]
    if d_out is not None:
        scratch += [
            pltpu.VMEM((2, total, width // 2), BF16),
            pltpu.VMEM((2, rows_here, width // 2), BF16),
            pltpu.SemaphoreType.DMA,
        ]
        scratch += Relay.scratch(n)
    return pl.pallas_call(
        kernel,
        grid=(chunks + 2,),
        out_shape=out_shape,
        in_specs=in_specs,
        out_specs=out_specs,
        scratch_shapes=scratch,
        compiler_params=pltpu.CompilerParams(
            collective_id=identity, has_side_effects=True, vmem_limit_bytes=VMEM_BYTES
        ),
        name=f"layer_forward_{layer}",
    )(*operands)


class Swap:
    def __init__(self, ships, lane_rows):
        self.ships, self.lane_rows = ships, lane_rows
        self.count = len(ships) + len(lane_rows)

    def operands(self):
        return [*self.ships, *[item for item, _ in self.lane_rows]]

    def in_specs(self):
        return [whole(item) for item in self.ships] + [ANYWHERE] * len(self.lane_rows)

    def outputs(self):
        shapes, specs = [], []
        for item in self.ships:
            shape = (item.shape[0] // 2, item.shape[1])
            shapes.append(jax.ShapeDtypeStruct(shape, F32))
            specs.append(whole_out(shape))
        for item, count in self.lane_rows:
            shapes.append(jax.ShapeDtypeStruct((count or item.shape[0], item.shape[1]), item.dtype))
            specs.append(ANYWHERE)
        return shapes, specs

    def scratch(self):
        if not self.count:
            return []
        buffers = [pltpu.VMEM((item.shape[0] // 2, item.shape[1]), BF16) for item in self.ships]
        return buffers * 2 + [pltpu.SemaphoreType.DMA((self.count,))] * 2

    def bind(self, sources, targets, scratch):
        ships = len(self.ships)
        me, core = lax.axis_index("seq"), lax.axis_index("tp")
        x = lax.rem(me, 2)
        beside = me + 1 - 2 * x
        half = PAIR // 2

        def copy(index):
            if index < ships:
                source, target = scratch[index], scratch[ships + index]
            else:
                source, target = sources[index], targets[index]
                count = self.lane_rows[index - ships][1]
                if count:
                    source = source.at[at(beside * count, count), :]
            send, recv = scratch[2 * ships].at[index], scratch[2 * ships + 1].at[index]
            return remote(source, target, send, recv, beside, core)

        def start():
            for index in range(self.count):
                if index < ships:
                    scratch[index][...] = sources[index][at((1 - x) * half, half), :].astype(BF16)
                copy(index).start()

        def finish():
            for index in range(self.count):
                copy(index).wait_recv()
                if index < ships:
                    own = sources[index][at(x * half, half), :]
                    targets[index][...] = own + scratch[ships + index][...].astype(F32)
            for index in range(self.count):
                copy(index).wait_send()

        return start, finish


def attention_backward(
    probs, divisor, mixed, turned_qkv, grad_mixed, first, fixed, frames, swap, swap_qkv, identity
):
    _, total, features = turned_qkv.shape
    chunks = total // FRAME
    slabs = features // PAIR
    half = PAIR // 2

    def kernel(*refs):
        refs = list(refs)

        def take(count):
            taken = refs[:count]
            del refs[:count]
            return taken

        p_ref, r_ref, o_ref, q_ref, k_ref, v_ref, g_ref, first_ref, fixed_ref, frames_ref = take(10)
        sources = take(swap.count)
        dq_ref, dk_ref, dv_ref, qkv_out = take(4)
        targets = take(swap.count)
        dk_sum, dv_sum, first_turned = take(3)
        if swap_qkv:
            qkv_own, qkv_send, qkv_recv, qkv_sems = take(4)
        start, finish = swap.bind(sources, targets, refs)

        step = pl.program_id(0)
        me, core = lax.axis_index("seq"), lax.axis_index("tp")
        x = lax.rem(me, 2)
        beside = me + 1 - 2 * x

        def qkv_copy(slab):
            return remote(
                qkv_send.at[slab],
                qkv_recv.at[slab],
                qkv_sems.at[0, slab],
                qkv_sems.at[1, slab],
                beside,
                core,
            )

        @pl.when(step == 0)
        def _():
            hello([(beside, core)])
            first_turned[...] = first_ref[...].T
            met([(beside, core)])
            start()

        lane = lax.broadcasted_iota(jnp.int32, (1, PAIR), 1)
        sides = [(lane < HEAD_DIM).astype(F32).astype(BF16), (lane >= HEAD_DIM).astype(F32).astype(BF16)]
        turned = k_ref[0].T
        ones = jnp.broadcast_to((lane < 2).astype(F32), (total, PAIR)).astype(BF16)
        values = jnp.concatenate([v_ref[0], ones], axis=1)

        def give(frame):
            keys = FRAME * (frame + 1)
            own = slice(frame * FRAME, keys)
            scaled = (g_ref[own, :].astype(F32) * r_ref[own, :]).astype(BF16)
            inner = scaled.astype(F32) * o_ref[own, :].astype(F32)
            grads, q_parts, g_parts = [], [], []
            for side in range(2):
                delta = jnp.sum(
                    jnp.where((lane < HEAD_DIM) == (side == 0), inner, 0.0), axis=1, keepdims=True
                )
                coarse = delta.astype(BF16).astype(F32)
                rest = jnp.where(lane == 0, -coarse, jnp.where(lane == 1, coarse - delta, 0.0))
                g2 = scaled * sides[side]
                grads.append(nt(values[:keys], jnp.concatenate([g2, rest.astype(BF16)], axis=1)))
                q_parts.append(q_ref[0, own, :] * sides[side])
                g_parts.append(g2)
            return grads, jnp.concatenate(q_parts, axis=0), jnp.concatenate(g_parts, axis=0)

        given = give(chunks - 1)
        for frame in reversed(range(chunks)):
            keys = FRAME * (frame + 1)
            own = slice(frame * FRAME, keys)
            tables = tables_of(fixed_ref, frames_ref, frame)
            grads, q_part, g_part = given
            given = give(frame - 1) if frame else None
            query_parts, score_parts, prob_parts = [], [], []
            for side in range(2):
                attention = p_ref[frame, side, :keys, :]
                grad_scores = (attention.astype(F32) * grads[side]).astype(BF16)
                query_parts.append(nn(turned[side * HEAD_DIM : (side + 1) * HEAD_DIM, :keys], grad_scores))
                score_parts.append(grad_scores)
                prob_parts.append(attention)
            grad_query = jnp.concatenate(query_parts, axis=0).T
            key_parts = nn(jnp.concatenate(score_parts, axis=1), q_part)
            value_parts = nn(jnp.concatenate(prob_parts, axis=1), g_part)
            dq_ref[own, :] = (turn(grad_query, tables, True) * SCORE_SCALE).astype(BF16)
            if frame == chunks - 1:
                dk_sum[...] = key_parts
                dv_sum[...] = value_parts
            else:
                dk_sum[:keys, :] += key_parts
                dv_sum[:keys, :] += value_parts
            dk_ref[own, :] = turn(dk_sum[own, :], tables, True).astype(BF16)
            dv_ref[own, :] = dv_sum[own, :].astype(BF16)

        for part, ref in enumerate((dq_ref, dk_ref, dv_ref)):
            piece = slice(part * PAIR, (part + 1) * PAIR)
            terms = nn(first_turned[...], ref[...])
            if swap_qkv:
                qkv_own[step, :, piece] = terms
                qkv_send[step, :, piece] = qkv_own[step, at((1 - x) * half, half), piece].astype(BF16)
            else:
                qkv_out[:, at(part * features + step * PAIR, PAIR)] = terms
        if swap_qkv:
            qkv_copy(step).start()

        @pl.when(step == slabs - 1)
        def _():
            finish()
            for slab in range(slabs if swap_qkv else 0):
                qkv_copy(slab).wait_recv()
                for part in range(3):
                    piece = slice(part * PAIR, (part + 1) * PAIR)
                    place = part * features + slab * PAIR
                    qkv_out[:, place : place + PAIR] = qkv_own[
                        slab, at(x * half, half), piece
                    ] + qkv_recv[slab, :, piece].astype(F32)
            for slab in range(slabs if swap_qkv else 0):
                qkv_copy(slab).wait_send()

    slab = pl.BlockSpec((total, PAIR), lambda s: (0, s))
    in_specs = [pl.BlockSpec((chunks, 2, total, FRAME), lambda s: (0, s, 0, 0))]
    in_specs += [slab] * 2
    for part in range(3):
        in_specs.append(pl.BlockSpec((1, total, PAIR), lambda s, part=part: (part, 0, s)))
    in_specs += [slab] + [whole(first), whole(fixed), whole(frames)]
    in_specs += swap.in_specs()
    qkv_shape = (half if swap_qkv else PAIR, 3 * features)
    shapes, specs = swap.outputs()
    out_shape = [jax.ShapeDtypeStruct((total, features), BF16)] * 3
    out_shape += [jax.ShapeDtypeStruct(qkv_shape, F32)] + shapes
    out_specs = [slab] * 3 + [whole_out(qkv_shape)] + specs
    scratch = [pltpu.VMEM((total, PAIR), F32)] * 2 + [pltpu.VMEM((PAIR, total), BF16)]
    if swap_qkv:
        scratch += [pltpu.VMEM((slabs, PAIR, 3 * PAIR), F32)]
        scratch += [pltpu.VMEM((slabs, half, 3 * PAIR), BF16)] * 2
        scratch += [pltpu.SemaphoreType.DMA((2, slabs))]
    scratch += swap.scratch()
    return pl.pallas_call(
        kernel,
        grid=(slabs,),
        out_shape=out_shape,
        in_specs=in_specs,
        out_specs=out_specs,
        scratch_shapes=scratch,
        compiler_params=pltpu.CompilerParams(
            collective_id=identity, has_side_effects=True, vmem_limit_bytes=VMEM_BYTES
        ),
        name=f"attention_backward_{identity}",
    )(
        probs,
        divisor,
        mixed,
        turned_qkv,
        turned_qkv,
        turned_qkv,
        grad_mixed,
        first,
        fixed,
        frames,
        *swap.operands(),
    )


def rows_backward(entry, upper, identity, span, swap):
    top, bottom = len(entry) == 1, upper is None
    if not top:
        above, entry = entry[0], entry[1:]
    total = entry[0].shape[1] if top else entry[0].shape[0]
    chunks = total // span
    columns = 256
    ahead = 0 if top else 2 if bottom else 1
    if top:
        width = 2 * entry[0].shape[2]
    else:
        features, width = entry[0].shape[1], entry[5].shape[1]
    if not bottom:
        layer = upper[0]
        hidden_units, mixed_features = upper[1].shape[1], upper[6].shape[1]
    place_rows = total // lax.axis_size("seq")

    def kernel(*refs):
        refs = list(refs)

        def take(count):
            taken = refs[:count]
            del refs[:count]
            return taken

        if top:
            (d_out_ref,) = take(1)
        else:
            dq_ref, dk_ref, dv_ref, unit1, scale1, dm_ref, wq, gain1 = take(8)
        if not bottom:
            act_ref, gp_ref, unit2, scale2, second_ref, mixed_ref = take(6)
            wo_any, wu_any, wd_any, gain2 = take(4)
        sources = take(swap.count)
        if not top:
            (vec1,) = take(1)
        if not bottom:
            dmid_out, dmix_out, out_sum, up_sum, down_sum, vec2 = take(6)
        else:
            dx_out, dx_other, vec_other = take(3)
        targets = take(swap.count)
        if not top:
            a_send, a_recv = take(2)
        if not bottom:
            b_send, b_recv, grad_keep, hidden_keep, low_keep, last_keep, wo, wu, wd, w_sem = take(10)
        else:
            dx_keep, dx_send, dx_recv, vec_recv, x_send_sem, x_recv_sem = take(6)
        send_sem, recv_sem = take(2)
        start_swap, finish_swap = swap.bind(sources, targets, refs)

        step = pl.program_id(0)
        me, core = lax.axis_index("seq"), lax.axis_index("tp")
        pair = at((me // 2) * PAIR, PAIR)
        x = lax.rem(me, 2)
        beside = me + 1 - 2 * x

        def exchange(kind, chunk):
            source, target = (a_send, a_recv) if kind == 0 else (b_send, b_recv)
            return remote(
                source.at[chunk],
                target.at[chunk],
                send_sem.at[kind, chunk],
                recv_sem.at[kind, chunk],
                me,
                1 - core,
            )

        def load(index):
            source, target = ((wd_any, wd), (wu_any, wu), (wo_any, wo))[index]
            return pltpu.make_async_copy(source.at[layer], target, w_sem.at[index])

        partners = [(me, 1 - core)] + ([(beside, core)] if bottom or swap.count else [])

        @pl.when(step == 0)
        def _():
            if not bottom:
                for index in range(3):
                    load(index).start()
                out_sum[...] = jnp.zeros_like(out_sum)
                up_sum[...] = jnp.zeros_like(up_sum)
                down_sum[...] = jnp.zeros_like(down_sum)
                vec2[...] = jnp.zeros_like(vec2)
            if not top:
                vec1[...] = jnp.zeros_like(vec1)
            hello(partners)

        def meet():
            @pl.when(step == 0)
            def _():
                met(partners)
                start_swap()

        def entry_products():
            partial = None
            for part, ref in enumerate((dq_ref, dk_ref, dv_ref)):
                grad = ref[...]
                term = nt(grad, wq[0, part])
                partial = term if partial is None else partial + term
                vec1[part : part + 1, :] += column_sum(grad.astype(F32))
            a_send[step] = partial.astype(BF16)

        def entry_norm(chunk):
            if top:
                return halves(d_out_ref)
            grad_first = a_send[chunk].astype(F32) + a_recv[chunk].astype(F32)
            unit, scale = kept_norm(unit1, scale1)
            for start, sums in ((3, column_sum(grad_first * unit)), (5, column_sum(grad_first))):
                for side in range(width // features):
                    piece = slice(side * features, (side + 1) * features)
                    vec1[start + side : start + side + 1, :] += sums[:, piece]
            return dm_ref[...] + norm_pull(grad_first, gain1[above : above + 1, :], unit, scale)

        def feed_forward(between=None):
            chunk = step - ahead
            gradient = entry_norm(chunk)
            if bottom:
                dx_keep[at(chunk * span, span), :] = gradient
                return
            grad_keep[lax.rem(chunk, 2)] = gradient
            vec2[1:2, :width] += column_sum(gradient)
            low = gradient.astype(BF16)
            low_keep[...] = low
            low_columns = low_keep[:, pair]
            second = second_ref[...]
            parts = [slice(start, start + columns) for start in range(0, hidden_units, columns)]
            if not top:
                wide = 4 * columns

                def some(index):
                    start = index * wide
                    places = [pl.ds(pl.multiple_of(start + k * columns, columns), columns) for k in range(4)]
                    grad_act = nt(low_keep[...], wd[places[0], :])
                    for k, part in enumerate(places):
                        following = nt(low_keep[...], wd[places[k + 1], :]) if k < 3 else None
                        grad_hidden = grad_act * gp_ref[:, part].astype(F32)
                        hidden_keep[:, part] = grad_hidden.astype(BF16)
                        vec2[0:1, part] += column_sum(grad_hidden)
                        grad_act = following

                repeat(hidden_units // wide, some)
            else:
                grad_act = nt(low, wd[parts[0], :])
                for index, part in enumerate(parts):
                    following = nt(low, wd[parts[index + 1], :]) if index + 1 < len(parts) else None
                    grad_hidden = grad_act * gp_ref[:, part].astype(F32)
                    hidden_keep[:, part] = grad_hidden.astype(BF16)
                    vec2[0:1, part] += column_sum(grad_hidden)
                    grad_act = following

            if between is not None:
                between()
            b_send[chunk] = nt(hidden_keep[...], wu[...]).astype(BF16)
            down_sum[...] += tn(low_columns, act_ref[...])
            up_sum[...] += tn(second, hidden_keep[...])

        def close():
            chunk = step - ahead - 1
            grad_second = b_send[chunk].astype(F32) + b_recv[chunk].astype(F32)
            unit, scale = kept_norm(unit2, scale2)
            vec2[2:3, :width] += column_sum(grad_second * unit)
            vec2[3:4, :width] += column_sum(grad_second)
            grad_middle = grad_keep[lax.rem(chunk, 2)] + norm_pull(
                grad_second, gain2[layer : layer + 1, :], unit, scale
            )
            dmid_out[...] = grad_middle
            vec2[4:5, :width] += column_sum(grad_middle)
            low = grad_middle.astype(BF16)
            last_keep[...] = low
            out_sum[...] += tn(last_keep[:, pair], mixed_ref[...])
            dmix_out[...] = nt(low, wo[...]).astype(BF16)

        if not top:

            @pl.when(step < chunks)
            def _():
                entry_products()
                meet()
                exchange(0, step).start()

        @pl.when((step >= ahead) & (step < chunks + ahead))
        def _():
            if not top:
                exchange(0, step - ahead).wait_recv()
            if not bottom:

                @pl.when(step == ahead)
                def _():
                    load(0).wait()

            feed_forward(lambda: pl.when(step == ahead)(lambda: load(1).wait()))
            if not bottom:
                if top:
                    meet()
                exchange(1, step - ahead).start()

        if not bottom:

            @pl.when(step == ahead + 1)
            def _():
                load(2).wait()

            @pl.when(step >= ahead + 1)
            def _():
                exchange(1, step - ahead - 1).wait_recv()
                close()

        if bottom:

            def x_copy(index):
                source, target = ((dx_send, dx_recv), (vec1, vec_recv))[index]
                return remote(
                    source, target, x_send_sem.at[index], x_recv_sem.at[index], beside, core
                )

            @pl.when(step == chunks + 1)
            def _():
                dx_send[...] = dx_keep[at(beside * place_rows, place_rows), :].astype(BF16)
                x_copy(0).start()
                x_copy(1).start()
                dx_out[...] = dx_keep[at(me * place_rows, place_rows), :]
                x_copy(0).wait_recv()
                x_copy(1).wait_recv()
                dx_other[...] = dx_recv[...].astype(F32)
                vec_other[...] = vec_recv[...]
                x_copy(0).wait_send()
                x_copy(1).wait_send()

        @pl.when(step == pl.num_programs(0) - 1)
        def _():
            for kind in ([] if top else [0]) + ([] if bottom else [1]):
                for chunk in range(chunks):
                    exchange(kind, chunk).wait_send()
            finish_swap()

    def rows(columns, behind):
        return pl.BlockSpec(
            (span, columns), lambda s: (jnp.clip(s - behind, 0, chunks - 1), 0)
        )

    vec = jax.ShapeDtypeStruct((8, VEC), F32)
    operands, in_specs, out_shape, out_specs, scratch = [], [], [], [], []
    if top:
        operands += list(entry)
        in_specs += [halves_spec(entry[0].shape, chunks, 0, span)]
    else:
        operands += list(entry)
        in_specs += [rows(features, 0)] * 3
        in_specs += [rows(width, ahead), rows(PAIR, ahead), rows(width, ahead)]
        in_specs += [
            pl.BlockSpec(
                (1, *entry[6].shape[1:]),
                lambda s: (above, 0, 0, 0),
                pipeline_mode=pl.Buffered(1),
            ),
            whole(entry[7]),
        ]
        narrow = jax.ShapeDtypeStruct((8, features), F32)
        out_shape += [narrow]
        out_specs += [whole_out((8, features))]
        scratch += [pltpu.VMEM((chunks, span, width), BF16)] * 2
    if not bottom:
        operands += list(upper[1:])
        in_specs += [rows(hidden_units, ahead)] * 2
        in_specs += [rows(width, ahead + 1), rows(PAIR, ahead + 1), rows(PAIR, ahead)]
        in_specs += [rows(mixed_features, ahead + 1)] + [ANYWHERE] * 3 + [whole(upper[10])]
        sums = [mixed_features, hidden_units, hidden_units]
        out_shape += [
            jax.ShapeDtypeStruct((total, width), F32),
            jax.ShapeDtypeStruct((total, mixed_features), BF16),
        ]
        out_shape += [jax.ShapeDtypeStruct((PAIR, size), F32) for size in sums] + [vec]
        out_specs += [rows(width, ahead + 1), rows(mixed_features, ahead + 1)]
        out_specs += [whole_out((PAIR, size)) for size in sums] + [whole_out((8, VEC))]
        scratch += [pltpu.VMEM((chunks, span, width), BF16)] * 2
        scratch += [
            pltpu.VMEM((2, span, width), F32),
            pltpu.VMEM((span, hidden_units), BF16),
            pltpu.VMEM((span, width), BF16),
            pltpu.VMEM((span, width), BF16),
            pltpu.VMEM(upper[7].shape[1:], BF16),
            pltpu.VMEM(upper[8].shape[1:], BF16),
            pltpu.VMEM(upper[9].shape[1:], BF16),
            pltpu.SemaphoreType.DMA((3,)),
        ]
    else:
        out_shape += [
            jax.ShapeDtypeStruct((place_rows, width), F32),
            jax.ShapeDtypeStruct((place_rows, width), F32),
            narrow,
        ]
        out_specs += [whole_out((place_rows, width))] * 2 + [whole_out((8, features))]
        scratch += [
            pltpu.VMEM((total, width), F32),
            pltpu.VMEM((place_rows, width), BF16),
            pltpu.VMEM((place_rows, width), BF16),
            pltpu.VMEM((8, features), F32),
            pltpu.SemaphoreType.DMA((2,)),
            pltpu.SemaphoreType.DMA((2,)),
        ]
    scratch += [pltpu.SemaphoreType.DMA((2, chunks))] * 2
    operands += swap.operands()
    in_specs += swap.in_specs()
    shapes, specs = swap.outputs()
    out_shape += shapes
    out_specs += specs
    scratch += swap.scratch()
    return pl.pallas_call(
        kernel,
        grid=(chunks + (1 if top else 2),),
        out_shape=out_shape,
        in_specs=in_specs,
        out_specs=out_specs,
        scratch_shapes=scratch,
        compiler_params=pltpu.CompilerParams(
            collective_id=identity, has_side_effects=True, vmem_limit_bytes=VMEM_BYTES
        ),
        name=f"rows_backward_{identity}",
    )(*operands)


def assemble(sums, vecs, lanes, n, features, hidden_units):
    place = lanes[1].shape[0]
    width = lanes[1].shape[1]
    half = PAIR // 2

    def kernel(*refs):
        refs = list(refs)

        def take(count):
            taken = refs[:count]
            del refs[:count]
            return taken

        qkvs, outs, ups, downs = take(LAYERS), take(LAYERS), take(LAYERS), take(LAYERS)
        vec_refs = [take(4) for _ in range(LAYERS)]
        out_lane, out_other, dx_own, dx_other = take(4)
        out_ref, dx_ref, gain1, shift1, g_qkv, b_qkv, g_out, b_out = take(8)
        gain2, shift2, g_up, b_up, g_down, b_down = take(6)
        out_own, sem, lane_sems = refs
        me = lax.axis_index("seq")
        x = lax.rem(me, 2)
        fetch = pltpu.make_async_copy(out_lane.at[at(me * place, place), :], out_own, sem)
        fetch.start()

        for layer in range(LAYERS):
            for part in range(3):
                g_qkv[layer, part] = qkvs[layer][:, part * features : (part + 1) * features]
            for ref, target in ((outs, g_out), (ups, g_up), (downs, g_down)):
                target[layer] = ref[layer][...]

        for layer, (entry_own, entry_other, upper_own, upper_other) in enumerate(vec_refs):
            line = slice(layer, layer + 1)
            for part in range(3):
                row = slice(part, part + 1)
                b_qkv[part, line, :] = entry_own[row, :] + entry_other[row, :]
            b_up[line, :] = upper_own[0:1, :hidden_units] + upper_other[0:1, :hidden_units]

            def owned(mine, other, row):
                wide = mine.shape[1]
                place = (me // 2) * PAIR
                pair = at(lax.rem(place, wide), PAIR)
                both = mine[row : row + 1, pair] + other[row : row + 1, pair]
                for later in range(1, width // wide):
                    line = slice(row + later, row + later + 1)
                    both = jnp.where(place // wide == later, mine[line, pair] + other[line, pair], both)
                return jnp.where(x == 0, both[:, :half], both[:, half:])

            gain1[line, :] = owned(entry_own, entry_other, 3)
            shift1[line, :] = owned(entry_own, entry_other, 5)
            b_down[line, :] = owned(upper_own, upper_other, 1)
            gain2[line, :] = owned(upper_own, upper_other, 2)
            shift2[line, :] = owned(upper_own, upper_other, 3)
            b_out[line, :] = owned(upper_own, upper_other, 4)

        fetch.wait()

        def lane_copies(lane):
            return [
                pltpu.make_async_copy(source, target.at[:, place_of, :], lane_sems.at[index])
                for index, (source, target, place_of) in enumerate(
                    (
                        (out_own, out_ref, lane),
                        (out_other, out_ref, 1 - lane),
                        (dx_own, dx_ref, lane),
                        (dx_other, dx_ref, 1 - lane),
                    )
                )
            ]

        for lane in range(2):

            @pl.when(x == lane)
            def _():
                for copy in lane_copies(lane):
                    copy.start()
                for copy in lane_copies(lane):
                    copy.wait()

    def f32(*shape):
        return jax.ShapeDtypeStruct(shape, F32)

    in_vmem = pl.BlockSpec(memory_space=pltpu.VMEM)
    flat = []
    for kind in range(4):
        flat += [sums[layer][kind] for layer in range(LAYERS)]
    for layer in range(LAYERS):
        flat += list(vecs[layer])
    flat += list(lanes)
    small = f32(LAYERS, width // n)
    return pl.pallas_call(
        kernel,
        out_shape=(
            f32(place, 2, width),
            f32(place, 2, width),
            small,
            small,
            f32(LAYERS, 3, half, features),
            f32(3, LAYERS, features),
            f32(LAYERS, half, features),
            small,
            small,
            small,
            f32(LAYERS, half, hidden_units),
            f32(LAYERS, hidden_units),
            f32(LAYERS, half, hidden_units),
            small,
        ),
        in_specs=[in_vmem] * (len(flat) - 4) + [ANYWHERE] + [in_vmem] * 3,
        out_specs=(ANYWHERE,) * 2 + (in_vmem,) * 12,
        scratch_shapes=[
            pltpu.VMEM((place, width), F32),
            pltpu.SemaphoreType.DMA,
            pltpu.SemaphoreType.DMA((4,)),
        ],
        compiler_params=pltpu.CompilerParams(vmem_limit_bytes=VMEM_BYTES),
        name="assemble",
    )(*flat)


def per_chip(
    tokens,
    d_out,
    norm1_gain,
    norm1_shift,
    w_qkv,
    b_qkv,
    w_out,
    b_out,
    norm2_gain,
    norm2_shift,
    w_up,
    b_up,
    w_down,
    b_down,
    episode_frames,
    live,
):
    n = lax.axis_size("seq")
    rows = tokens.shape[0]
    features = w_qkv.shape[3]
    fixed, ahead = turn_constants(rows * n // FRAME)
    qkv, qkv_bias = w_qkv.transpose(0, 2, 1, 3), b_qkv.transpose(1, 0, 2)

    gathered, key_bias, frames, *projected = gather_and_project(
        tokens, live.T, episode_frames, norm1_gain, norm1_shift, qkv, qkv_bias, fixed, ahead, n
    )
    streams, kept, d_lane = [gathered], [], None
    for layer in range(LAYERS):
        following = None
        if layer + 1 < LAYERS:
            following = (qkv, norm1_gain, norm1_shift, qkv_bias, fixed, frames)
        results = layer_forward(
            layer,
            projected[0],
            key_bias,
            streams[layer],
            (w_out, w_up, w_down),
            (b_out, norm2_gain, norm2_shift, b_up, b_down),
            following,
            d_out if layer == 0 else None,
            n,
            1 + layer,
        )
        kept.append((*projected, *results[:8]))
        streams.append(results[8])
        if following is not None:
            projected = results[9:13]
        if layer == 0:
            d_lane = results[-1]

    sums = [[None] * 4 for _ in range(LAYERS)]
    vecs = [[None] * 4 for _ in range(LAYERS)]
    entry, later = (d_lane,), None
    for layer in reversed(range(LAYERS)):
        turned, first, unit1, scale1, probs, divisor, mixed = kept[layer][:7]
        unit2, scale2, second, act, slope = kept[layer][7:]
        upper = (
            layer,
            act,
            slope,
            unit2,
            scale2,
            second,
            mixed,
            w_out,
            w_up,
            w_down,
            norm2_gain,
        )
        identity = 1 + LAYERS + 2 * (LAYERS - 1 - layer)
        if later is None:
            results = rows_backward(entry, upper, identity, FRAME, Swap([], []))
        else:
            swap = Swap(later[:2], [(later[2], 0), (streams[LAYERS], rows)])
            vec1, *results = rows_backward(entry, upper, identity, FRAME, swap)
            results, swapped = results[:6], results[6:]
            sums[layer + 1][3], sums[layer + 1][0] = swapped[:2]
            vecs[layer + 1][3], out_other = swapped[2:]
            vecs[layer + 1][0] = vec1
        grad_middle, grad_mixed, out_sum, up_sum, down_sum, vec2 = results
        vecs[layer][2] = vec2
        last = layer == 0
        if last:
            swap = Swap([out_sum, up_sum], [(vec2, 0), (vecs[layer + 1][0], 0)])
        else:
            swap = Swap([out_sum, up_sum], [])
        results = attention_backward(
            probs,
            divisor,
            mixed,
            turned,
            grad_mixed,
            first,
            fixed,
            frames,
            swap,
            last,
            identity + 1,
        )
        grad_query, grad_key, grad_value, qkv_sum = results[:4]
        if last:
            sums[layer][:3] = [qkv_sum, *results[4:6]]
            vecs[layer][3], vecs[layer + 1][1] = results[6:8]
        else:
            sums[layer][1:3] = results[4:6]
            later = [down_sum, qkv_sum, vec2]
        entry = (
            layer,
            grad_query,
            grad_key,
            grad_value,
            unit1,
            scale1,
            grad_middle,
            qkv,
            norm1_gain,
        )
    vec1, dx_own, dx_other, vec_other, sums[0][3] = rows_backward(
        entry, None, 1 + 3 * LAYERS, FRAME, Swap([down_sum], [])
    )
    vecs[0][:2] = [vec1, vec_other]
    results = list(
        assemble(
            sums,
            vecs,
            (streams[LAYERS], out_other, dx_own, dx_other),
            n,
            features,
            w_up.shape[2],
        )
    )
    results[4] = results[4].transpose(0, 2, 1, 3)
    results[5] = results[5].transpose(1, 0, 2)
    results[6] = results[6].transpose(0, 2, 1)
    results[12] = results[12].transpose(0, 2, 1)
    return tuple(results)


def lane_fits(mesh, tokens):
    n = mesh.shape["seq"]
    positions, lanes, width = tokens.shape
    rows = positions // n
    return (
        lanes == 2
        and n % 4 == 0
        and positions <= 4 * FRAME
        and positions % FRAME == 0
        and FRAME % rows == 0
        and width // n * 2 == PAIR
        and mesh.shape["tp"] == 2
    )


def solution(mesh):
    placed = (
        P("seq", None, None),
        P("seq", None, None),
        P(),
        P(),
        P(None, None, None, "tp"),
        P(None, None, "tp"),
        P(None, "tp", None),
        P(),
        P(),
        P(),
        P(None, None, "tp"),
        P(None, "tp"),
        P(None, "tp", None),
        P(),
        P(),
        P("seq", None),
    )
    def mapped(body):
        return jax.shard_map(
            body,
            mesh=mesh,
            in_specs=placed,
            out_specs=(
                P("seq", None, None),
                P("seq", None, None),
                P(None, "seq"),
                P(None, "seq"),
                P(None, "seq", None, "tp"),
                P(None, None, "tp"),
                P(None, "tp", "seq"),
                P(None, "seq"),
                P(None, "seq"),
                P(None, "seq"),
                P(None, "seq", "tp"),
                P(None, "tp"),
                P(None, "tp", "seq"),
                P(None, "seq"),
            ),
            check_vma=False,
        )

    def run(tokens, *others):
        if lane_fits(mesh, tokens):
            return mapped(per_chip)(tokens, *others)
        return mapped(per_device)(tokens, *others)

    return run
```

```python
import math

import jax
import jax.numpy as jnp
import numpy as np
from jax import lax
from jax.experimental import pallas as pl
from jax.experimental.pallas import tpu as pltpu
from jax.sharding import PartitionSpec as P

HEAD_DIM = 64
GRID = 16
FRAME = 256
LAYERS = 2
MICRO = 2


EPSILON = 1e-06
MASKED = -1e30
SCORE_SCALE = 0.125


def layer_norm(stream, norm_gain, norm_shift):
    center = stream - jnp.mean(stream, axis=-1, keepdims=True)
    spread = jnp.mean(center * center, axis=-1, keepdims=True)
    return center * lax.rsqrt(spread + EPSILON) * norm_gain + norm_shift


def rotate(values, frame_place, row_place, column_place):
    frequency = jnp.exp(jnp.arange(10, dtype=jnp.float32) * (-math.log(10000.0) / 10.0))
    pieces = []
    for section, place in enumerate((frame_place, row_place, column_place)):
        lower = values[..., 20 * section : 20 * section + 10]
        upper = values[..., 20 * section + 10 : 20 * section + 20]
        angles = place.astype(jnp.float32)[..., None, None] * frequency
        cosine = jnp.cos(angles)
        sine_part = jnp.sin(angles)
        pieces.append(lower * cosine - upper * sine_part)
        pieces.append(lower * sine_part + upper * cosine)
    pieces.append(values[..., 60:])
    return jnp.concatenate(pieces, axis=-1)


def episode_tags(frame_counts, positions):
    endings = jnp.cumsum(frame_counts) * FRAME
    passed = (positions[:, None] >= endings[None, :]).astype(jnp.int32)
    episode = jnp.sum(passed, axis=1)
    opening = jnp.sum(passed * frame_counts[None, :], axis=1)
    frame_index = positions // FRAME - opening
    within = positions % FRAME
    return (episode, frame_index, within // GRID, within % GRID)


def gelu_exact(values):
    return jax.nn.gelu(values, approximate=False)


def sum_heads(partial_sum):
    return lax.psum(partial_sum.astype(jnp.bfloat16), "tp").astype(jnp.float32)


def sum_inputs(partial_sum):
    return lax.psum(partial_sum.astype(jnp.bfloat16), "tp").astype(jnp.float32)


def lane_scores(query, keys_all, lane_index, query_tags, key_tags):
    head_count = query.shape[2] // HEAD_DIM
    query_lane = lax.dynamic_index_in_dim(query, lane_index, 1, False).reshape(
        query.shape[0], head_count, HEAD_DIM
    )
    keys_lane = lax.dynamic_index_in_dim(keys_all, lane_index, 1, False).reshape(
        keys_all.shape[0], head_count, HEAD_DIM
    )
    query_episode, query_frame = [
        lax.dynamic_index_in_dim(item, lane_index, 1, False) for item in query_tags
    ]
    key_episode, key_frame, key_live = [
        lax.dynamic_index_in_dim(item, lane_index, 1, False) for item in key_tags
    ]
    allowed = (
        (query_episode[:, None] == key_episode[None, :])
        & (key_frame[None, :] <= query_frame[:, None])
        & (key_live[None, :] > 0)
    )
    scores = (
        jnp.einsum("qhd,khd->hqk", query_lane, keys_lane, preferred_element_type=jnp.float32)
        * SCORE_SCALE
    )
    return (jnp.where(allowed[None], scores, MASKED), query_lane, keys_lane)


def attend_forward(query, keys_all, values_all, query_tags, key_tags):
    rows_dev, lane_count, features = query.shape
    head_count = features // HEAD_DIM

    def one_lane(lane_index, carry):
        scores, query_lane, keys_lane = lane_scores(
            query, keys_all, lane_index, query_tags, key_tags
        )
        highest = jnp.max(scores, axis=-1, keepdims=True)
        shifted = jnp.exp(scores - highest)
        summed = jnp.sum(shifted, axis=-1, keepdims=True)
        attention = (shifted / summed).astype(jnp.bfloat16)
        values_lane = lax.dynamic_index_in_dim(values_all, lane_index, 1, False).reshape(
            values_all.shape[0], head_count, HEAD_DIM
        )
        result = jnp.einsum(
            "hqk,khd->qhd", attention, values_lane, preferred_element_type=jnp.float32
        ).reshape(rows_dev, 1, features)
        log_total = (highest + jnp.log(summed))[None, :, :, 0]
        return (result, log_total)

    initial = (
        jnp.zeros((rows_dev, lane_count, features), jnp.float32),
        jnp.zeros((lane_count, head_count, rows_dev), jnp.float32),
    )
    return lax.fori_loop(0, lane_count, one_lane, initial)


def attend_backward(query, keys_all, values_all, log_total, grad_mixed, query_tags, key_tags):
    rows_dev, lane_count, features = query.shape
    head_count = features // HEAD_DIM
    key_rows = keys_all.shape[0]

    def one_lane(lane_index, carry):
        scores, query_lane, keys_lane = lane_scores(
            query, keys_all, lane_index, query_tags, key_tags
        )
        values_lane = lax.dynamic_index_in_dim(values_all, lane_index, 1, False).reshape(
            key_rows, head_count, HEAD_DIM
        )
        grad_lane = lax.dynamic_index_in_dim(grad_mixed, lane_index, 1, False).reshape(
            rows_dev, head_count, HEAD_DIM
        )
        attention = jnp.exp(
            scores - lax.dynamic_index_in_dim(log_total, lane_index, 0, False)[:, :, None]
        )
        grad_attention = jnp.einsum(
            "qhd,khd->hqk", grad_lane, values_lane, preferred_element_type=jnp.float32
        )
        inner = jnp.sum(attention * grad_attention, axis=-1, keepdims=True)
        grad_scores = (attention * (grad_attention - inner)).astype(jnp.bfloat16)
        query_part = (
            jnp.einsum("hqk,khd->qhd", grad_scores, keys_lane, preferred_element_type=jnp.float32)
            * SCORE_SCALE
        )
        key_part = (
            jnp.einsum("hqk,qhd->khd", grad_scores, query_lane, preferred_element_type=jnp.float32)
            * SCORE_SCALE
        )
        value_part = jnp.einsum(
            "hqk,qhd->khd",
            attention.astype(jnp.bfloat16),
            grad_lane,
            preferred_element_type=jnp.float32,
        )
        stacked = jnp.stack(
            [key_part.reshape(key_rows, features), value_part.reshape(key_rows, features)], axis=1
        )
        key_terms = stacked[:, None]
        grad_query = query_part.reshape(rows_dev, 1, features)
        return (grad_query, key_terms)

    initial = (
        jnp.zeros((rows_dev, lane_count, features), jnp.float32),
        jnp.zeros((key_rows, lane_count, 2, features), jnp.float32),
    )
    return lax.fori_loop(0, lane_count, one_lane, initial)


def front(stream, layer_index, params, query_tags, key_tags, positions):
    (
        gain_one,
        shift_one,
        mat_qkv,
        bias_qkv,
        mat_out,
        bias_out,
        gain_two,
        shift_two,
        mat_up,
        bias_up,
        mat_down,
        bias_down,
    ) = [item[layer_index] for item in params]
    rows_dev, lane_count, width = stream.shape
    features = mat_qkv.shape[2]
    head_count = features // HEAD_DIM
    frame_place, row_place, column_place = positions
    first = layer_norm(stream, gain_one, shift_one).astype(jnp.bfloat16)
    projected = (
        jnp.einsum("tbd,dcf->tbcf", first, mat_qkv, preferred_element_type=jnp.float32) + bias_qkv
    )
    split = projected.reshape(rows_dev, lane_count, 3, head_count, HEAD_DIM)
    query = (
        rotate(split[:, :, 0], frame_place, row_place, column_place)
        .reshape(rows_dev, lane_count, features)
        .astype(jnp.bfloat16)
    )
    keys = (
        rotate(split[:, :, 1], frame_place, row_place, column_place)
        .reshape(rows_dev, lane_count, features)
        .astype(jnp.bfloat16)
    )
    values = projected[:, :, 2].astype(jnp.bfloat16)
    keys_all, values_all = (
        lax.all_gather(keys, "seq", axis=0, tiled=True),
        lax.all_gather(values, "seq", axis=0, tiled=True),
    )
    mixed_full, log_total = attend_forward(query, keys_all, values_all, query_tags, key_tags)
    mixed = mixed_full.astype(jnp.bfloat16)
    middle = (
        stream
        + sum_heads(jnp.einsum("tbf,fd->tbd", mixed, mat_out, preferred_element_type=jnp.float32))
        + bias_out
    )
    second = layer_norm(middle, gain_two, shift_two).astype(jnp.bfloat16)
    hidden = jnp.einsum("tbd,df->tbf", second, mat_up, preferred_element_type=jnp.float32) + bias_up
    activation = gelu_exact(hidden).astype(jnp.bfloat16)
    return (
        first,
        query,
        keys_all,
        values_all,
        log_total,
        mixed,
        middle,
        second,
        hidden,
        activation,
        mixed_full,
    )


def layer_backward(stream, gradient, layer_index, params, query_tags, key_tags, positions):
    (
        gain_one,
        shift_one,
        mat_qkv,
        bias_qkv,
        mat_out,
        bias_out,
        gain_two,
        shift_two,
        mat_up,
        bias_up,
        mat_down,
        bias_down,
    ) = [item[layer_index] for item in params]
    (
        first,
        query,
        keys_all,
        values_all,
        log_total,
        mixed,
        middle,
        second,
        hidden,
        activation,
        mixed_full,
    ) = front(stream, layer_index, params, query_tags, key_tags, positions)
    frame_place, row_place, column_place = positions
    rows_dev, lane_count, width = stream.shape
    features = query.shape[2]
    head_count = features // HEAD_DIM
    grad_low = gradient.astype(jnp.bfloat16)
    grad_w_down = jnp.einsum(
        "tbf,tbd->fd", activation, grad_low, preferred_element_type=jnp.float32
    )
    grad_b_down = jnp.sum(gradient, axis=(0, 1))
    grad_activation = jnp.einsum(
        "tbd,fd->tbf", grad_low, mat_down, preferred_element_type=jnp.float32
    )
    grad_hidden = jax.vjp(gelu_exact, hidden)[1](grad_activation)[0].astype(jnp.bfloat16)
    grad_b_up = jnp.sum(grad_hidden.astype(jnp.float32), axis=(0, 1))
    grad_w_up = jnp.einsum("tbd,tbf->df", second, grad_hidden, preferred_element_type=jnp.float32)
    grad_second = sum_inputs(
        jnp.einsum("tbf,df->tbd", grad_hidden, mat_up, preferred_element_type=jnp.float32)
    )
    middle_pull = jax.vjp(layer_norm, middle, gain_two, shift_two)[1]
    grad_inner, grad_gain_two, grad_shift_two = middle_pull(grad_second)
    grad_middle = gradient + grad_inner
    grad_b_out = jnp.sum(grad_middle, axis=(0, 1))
    middle_low = grad_middle.astype(jnp.bfloat16)
    grad_w_out = jnp.einsum("tbf,tbd->fd", mixed, middle_low, preferred_element_type=jnp.float32)
    grad_mixed = jnp.einsum(
        "tbd,fd->tbf", middle_low, mat_out, preferred_element_type=jnp.float32
    ).astype(jnp.bfloat16)
    grad_query, key_terms = attend_backward(
        query, keys_all, values_all, log_total, grad_mixed, query_tags, key_tags
    )
    returned = lax.psum_scatter(key_terms, "seq", scatter_dimension=0, tiled=True)
    turned_query = rotate(
        grad_query.reshape(rows_dev, lane_count, head_count, HEAD_DIM),
        -frame_place,
        -row_place,
        -column_place,
    )
    turned_keys = rotate(
        returned[:, :, 0].reshape(rows_dev, lane_count, head_count, HEAD_DIM),
        -frame_place,
        -row_place,
        -column_place,
    )
    grad_projected = jnp.stack(
        [
            turned_query.reshape(rows_dev, lane_count, features),
            turned_keys.reshape(rows_dev, lane_count, features),
            returned[:, :, 1],
        ],
        axis=2,
    ).astype(jnp.bfloat16)
    grad_b_qkv = jnp.sum(grad_projected.astype(jnp.float32), axis=(0, 1))
    grad_w_qkv = jnp.einsum(
        "tbd,tbcf->dcf", first, grad_projected, preferred_element_type=jnp.float32
    )
    grad_first = sum_inputs(
        jnp.einsum("tbcf,dcf->tbd", grad_projected, mat_qkv, preferred_element_type=jnp.float32)
    )
    first_pull = jax.vjp(layer_norm, stream, gain_one, shift_one)[1]
    grad_entry, grad_gain_one, grad_shift_one = first_pull(grad_first)
    grads = (
        grad_gain_one,
        grad_shift_one,
        grad_w_qkv,
        grad_b_qkv,
        grad_w_out,
        grad_b_out,
        grad_gain_two,
        grad_shift_two,
        grad_w_up,
        grad_b_up,
        grad_w_down,
        grad_b_down,
    )
    return (grad_middle + grad_entry, grads)


def per_device(
    tokens,
    d_out,
    norm1_gain,
    norm1_shift,
    w_qkv,
    b_qkv,
    w_out,
    b_out,
    norm2_gain,
    norm2_shift,
    w_up,
    b_up,
    w_down,
    b_down,
    episode_frames,
    live,
):
    rows_dev = tokens.shape[0]
    lane_count = tokens.shape[1] // MICRO
    total_rows = rows_dev * lax.axis_size("seq")
    local_positions = lax.axis_index("seq") * rows_dev + jnp.arange(rows_dev, dtype=jnp.int32)
    key_positions = jnp.arange(total_rows, dtype=jnp.int32)
    tagger = jax.vmap(episode_tags, in_axes=(0, None), out_axes=1)
    query_episode, query_frame, query_row, query_column = tagger(episode_frames, local_positions)
    key_episode, key_frame, key_row, key_column = tagger(episode_frames, key_positions)
    live_keys = lax.all_gather(live, "seq", axis=0, tiled=True)
    params = (
        norm1_gain,
        norm1_shift,
        w_qkv,
        b_qkv,
        w_out,
        b_out,
        norm2_gain,
        norm2_shift,
        w_up,
        b_up,
        w_down,
        b_down,
    )
    layer_grads = [None] * LAYERS
    outputs = []
    grad_tokens = []
    for micro_index in range(MICRO):
        first_lane = micro_index * lane_count
        last_lane = first_lane + lane_count
        query_tags = (query_episode[:, first_lane:last_lane], query_frame[:, first_lane:last_lane])
        key_tags = (
            key_episode[:, first_lane:last_lane],
            key_frame[:, first_lane:last_lane],
            live_keys[:, first_lane:last_lane],
        )
        positions = (
            query_frame[:, first_lane:last_lane],
            query_row[:, first_lane:last_lane],
            query_column[:, first_lane:last_lane],
        )
        stream = tokens[:, first_lane:last_lane].astype(jnp.float32)
        inputs = []
        gathered = []
        for layer_index in range(LAYERS):
            inputs.append(stream)
            layer_state = front(stream, layer_index, params, query_tags, key_tags, positions)
            gathered.append((layer_state[2], layer_state[3]))
            branch = jnp.einsum(
                "tbf,fd->tbd",
                layer_state[9],
                w_down[layer_index],
                preferred_element_type=jnp.float32,
            )
            stream = layer_state[6] + sum_heads(branch) + b_down[layer_index]
        outputs.append(stream)
        gradient = d_out[:, first_lane:last_lane]
        for layer_index in reversed(range(LAYERS)):
            gradient, grads = layer_backward(
                inputs[layer_index], gradient, layer_index, params, query_tags, key_tags, positions
            )
            if layer_grads[layer_index] is None:
                layer_grads[layer_index] = grads
            else:
                layer_grads[layer_index] = jax.tree.map(jnp.add, layer_grads[layer_index], grads)
        grad_tokens.append(gradient)
    stacked = [
        jnp.stack([layer_grads[layer_index][entry] for layer_index in range(LAYERS)])
        for entry in range(12)
    ]
    (
        grad_gain_one,
        grad_shift_one,
        grad_w_qkv,
        grad_b_qkv,
        grad_w_out,
        grad_b_out,
        grad_gain_two,
        grad_shift_two,
        grad_w_up,
        grad_b_up,
        grad_w_down,
        grad_b_down,
    ) = stacked
    in_sums = (
        lax.psum_scatter(grad_w_qkv, "seq", scatter_dimension=1, tiled=True),
        lax.psum_scatter(grad_w_up, "seq", scatter_dimension=1, tiled=True),
        lax.psum_scatter(grad_gain_one, "seq", scatter_dimension=1, tiled=True),
        lax.psum_scatter(grad_shift_one, "seq", scatter_dimension=1, tiled=True),
        lax.psum_scatter(grad_gain_two, "seq", scatter_dimension=1, tiled=True),
        lax.psum_scatter(grad_shift_two, "seq", scatter_dimension=1, tiled=True),
        lax.psum_scatter(grad_b_out, "seq", scatter_dimension=1, tiled=True),
        lax.psum_scatter(grad_b_down, "seq", scatter_dimension=1, tiled=True),
    )
    out_sums = (
        lax.psum_scatter(grad_w_out, "seq", scatter_dimension=2, tiled=True),
        lax.psum_scatter(grad_w_down, "seq", scatter_dimension=2, tiled=True),
    )
    bias_total = lax.psum((grad_b_qkv, grad_b_up), "seq")
    return (
        jnp.concatenate(outputs, axis=1),
        jnp.concatenate(grad_tokens, axis=1),
        in_sums[2],
        in_sums[3],
        in_sums[0],
        bias_total[0],
        out_sums[0],
        in_sums[6],
        in_sums[4],
        in_sums[5],
        in_sums[1],
        bias_total[1],
        out_sums[1],
        in_sums[7],
    )


MESH = pl.DeviceIdType.MESH
BF16 = jnp.bfloat16
F32 = jnp.float32
VMEM_BYTES = 60 * 1024 * 1024
PAIR = 128
VEC = 2048


def nn(left, right):
    return lax.dot_general(left, right, (((1,), (0,)), ((), ())), preferred_element_type=F32)


def nt(left, right):
    return lax.dot_general(left, right, (((1,), (1,)), ((), ())), preferred_element_type=F32)


def tn(left, right):
    return lax.dot_general(left, right, (((0,), (0,)), ((), ())), preferred_element_type=F32)


def at(start, size):
    return pl.ds(pl.multiple_of(start, size), size)


def repeat(count, body):
    def one(index, carry):
        body(index)
        return carry

    lax.fori_loop(0, count, one, 0)


def remote(src, dst, send, recv, seq, tp):
    return pltpu.make_async_remote_copy(
        src_ref=src,
        dst_ref=dst,
        send_sem=send,
        recv_sem=recv,
        device_id=(seq, tp),
        device_id_type=MESH,
    )


def hello(partners):
    barrier = pltpu.get_barrier_semaphore()
    for seq, tp in partners:
        pl.semaphore_signal(barrier, inc=1, device_id=(seq, tp), device_id_type=MESH)


def met(partners):
    pl.semaphore_wait(pltpu.get_barrier_semaphore(), len(partners))


def whole(array):
    zeros = (0,) * array.ndim
    return pl.BlockSpec(array.shape, lambda s: zeros, pipeline_mode=pl.Buffered(1))


def whole_out(shape):
    zeros = (0,) * len(shape)
    return pl.BlockSpec(shape, lambda s: zeros)


ANYWHERE = pl.BlockSpec(memory_space=pl.ANY)


def turn_row(table, place, section):
    frequency = np.exp(np.arange(10, dtype=np.float32) * np.float32(-math.log(10000.0) / 10.0))
    angle = place.astype(np.float32)[:, None] * frequency
    for base in range(20 * section, PAIR, HEAD_DIM):
        table[0, :, base : base + 10] = np.cos(angle)
        table[0, :, base + 10 : base + 20] = np.cos(angle)
        table[1, :, base : base + 10] = -np.sin(angle)
        table[2, :, base + 10 : base + 20] = np.sin(angle)


def turn_constants(frames):
    within, ahead = np.zeros((3, FRAME, PAIR), np.float32), np.zeros((3, frames, PAIR), np.float32)
    turn_row(within, np.arange(FRAME) // GRID, 1)
    turn_row(within, np.arange(FRAME) % GRID, 2)
    for base in range(60, PAIR, HEAD_DIM):
        within[0, :, base : base + 4] = 1.0
    turn_row(ahead, np.arange(frames), 0)
    return jnp.asarray(within), jnp.asarray(ahead)


def turn(values, tables, back=False):
    cosine, lower, upper = tables
    pieces = []
    for start in range(0, values.shape[1], PAIR):
        slab = values[:, start : start + PAIR]
        moved = pltpu.roll(slab, PAIR - 10, 1) * lower + pltpu.roll(slab, 10, 1) * upper
        pieces.append(slab * cosine - moved if back else slab * cosine + moved)
    return jnp.concatenate(pieces, axis=1)


def tables_of(fixed_ref, frames_ref, chunk):
    return [fixed_ref[i] + frames_ref[i, pl.ds(chunk, 1), :] for i in range(3)]


def normed(stream):
    center = stream - jnp.mean(stream, axis=-1, keepdims=True)
    spread = jnp.mean(center * center, axis=-1, keepdims=True)
    scale = lax.rsqrt(spread + EPSILON)
    return center * scale, scale


def norm_pull(grad, gain, unit, scale):
    scaled = grad * gain
    return scale * (
        scaled
        - jnp.mean(scaled, axis=-1, keepdims=True)
        - unit * jnp.mean(scaled * unit, axis=-1, keepdims=True)
    )


def keep_norm(unit, scale, unit_ref, scale_ref):
    unit_ref[...] = unit.astype(BF16)
    scale_ref[...] = jnp.broadcast_to(scale, scale_ref.shape)


def kept_norm(unit_ref, scale_ref):
    copies = unit_ref.shape[1] // scale_ref.shape[1]
    return unit_ref[...].astype(F32), jnp.concatenate([scale_ref[...]] * copies, axis=1)


def column_sum(values):
    return jnp.sum(values, axis=0, keepdims=True)


def gelu_both(hidden):
    normal = 0.5 + 0.5 * lax.erf(hidden * math.sqrt(0.5))
    density = jnp.exp(hidden * hidden * -0.5) * (1.0 / math.sqrt(2.0 * math.pi))
    return hidden * normal, normal + hidden * density


def project(stream, chunk, layer, pair, refs, outs, first_full, straight=False):
    gain, shift, weight, bias, fixed, frames = refs
    qkv_ref, first_ref, unit_ref, scale_ref = outs
    unit, scale = normed(stream)
    keep_norm(unit, scale, unit_ref, scale_ref)
    first_full[...] = (unit * gain[layer : layer + 1, :] + shift[layer : layer + 1, :]).astype(BF16)
    first_ref[...] = first_full[:, at(pair * PAIR, PAIR)]
    cosine, lower, upper = tables_of(fixed, frames, chunk)

    def one(part):
        still = part == 2
        tables = (
            jnp.where(still, 1.0, cosine),
            jnp.where(still, 0.0, lower),
            jnp.where(still, 0.0, upper),
        )
        values = nn(first_full[...], weight[part]) + bias[part, layer : layer + 1, :]
        qkv_ref[part] = (turn(values, tables) * jnp.where(part == 0, SCORE_SCALE, 1.0)).astype(BF16)

    if not straight:
        repeat(3, one)
        return
    for part in range(3):
        values = nn(first_full[...], weight[part]) + bias[part, layer : layer + 1, :]
        if part < 2:
            values = turn(values, (cosine, lower, upper))
        if part == 0:
            values = values * SCORE_SCALE
        qkv_ref[part] = values.astype(BF16)


class Relay:
    sems = 6

    def __init__(self, n, rows, buffer, other, sems, lives=None, live_other=None):
        self.n, self.rows, self.buffer, self.other = n, rows, buffer, other
        self.lives, self.live_other = lives, live_other
        self.z_send, self.z_recv, self.y_send, self.y_recv, self.c_send, self.c_recv = sems
        self.planes = n // 4
        self.me, self.core = lax.axis_index("seq"), lax.axis_index("tp")
        me = self.me
        self.x, self.y, self.z = lax.rem(me, 2), lax.rem(me // 2, 2), me // 4
        self.across = me + 2 - 4 * self.y

    @staticmethod
    def scratch(n):
        dma, planes = pltpu.SemaphoreType.DMA, n // 4
        shapes = [(planes, 2, 2)] * 2 + [(planes, 2)] * 2 + [(2 * planes,)] * 2
        return [dma(shape) for shape in shapes]

    @property
    def events(self):
        return self.planes

    def plane(self, step):
        return lax.rem(self.z + step, self.planes)

    def place(self, plane, lane):
        return plane * 4 + self.y * 2 + lane

    def reached(self):
        return [(step, far) for step in range(self.planes) for far in (0, 1) if step or far]

    def hello(self):
        barrier = pltpu.get_barrier_semaphore()
        partners = [(self.across, self.core), (self.me, 1 - self.core)]
        for step, far in self.reached():
            lane = 1 - self.x if far else self.x
            partners.append((self.place(self.plane(step), lane), self.core))
        for seq, tp in partners:
            pl.semaphore_signal(barrier, inc=1, device_id=(seq, tp), device_id_type=MESH)

    def met(self):
        pl.semaphore_wait(pltpu.get_barrier_semaphore(), 2 + len(self.reached()))

    def rows_of(self, side, seq):
        return self.buffer.at[side, at(seq * self.rows, self.rows), :]

    def block(self, side, pair):
        return self.buffer.at[side, at(pair * 2 * self.rows, 2 * self.rows), :]

    def items(self, pair):
        found = [self.block(self.core, pair)]
        if self.lives is not None:
            found.append(self.lives.at[at(pair * 2, 2)])
        return found

    def each(self, copy, what):
        for index in range(1 if self.lives is None else 2):
            getattr(copy(index), what)()

    def z_copy(self, step, far):
        def copy(index):
            lane = 1 - self.x if far else self.x
            if index == 0:
                source = self.other.at[self.core] if far else self.rows_of(self.core, self.me)
                target = self.rows_of(self.core, self.me)
            else:
                source = self.live_other if far else self.lives.at[self.me]
                target = self.lives.at[self.me]
            return remote(
                source,
                target,
                self.z_send.at[step, far, index],
                self.z_recv.at[step, far, index],
                self.place(self.plane(step), lane),
                self.core,
            )

        return copy

    def y_copy(self, plane, row):
        def copy(index):
            item = self.items(plane * 2 + row)[index]
            return remote(
                item,
                item,
                self.y_send.at[plane, index],
                self.y_recv.at[plane, index],
                self.across,
                self.core,
            )

        return copy

    def c_copy(self, pair, side):
        item = self.block(side, pair)
        return remote(
            item, item, self.c_send.at[pair], self.c_recv.at[pair], self.me, 1 - self.core
        )

    def begin(self):
        for step, far in self.reached():
            self.each(self.z_copy(step, far), "start")

    def arrive(self, event):
        for far in (0, 1) if event else (1,):
            self.each(self.z_copy(event, far), "wait_recv")
        plane = self.plane(self.planes - event)
        self.each(self.y_copy(plane, self.y), "start")
        self.c_copy(plane * 2 + self.y, self.core).start()

    def complete(self, event):
        plane = self.plane(self.planes - event)
        self.each(self.y_copy(plane, 1 - self.y), "wait_recv")
        self.c_copy(plane * 2 + 1 - self.y, self.core).start()

    def ready(self, event):
        plane = self.plane(self.planes - event)
        self.c_copy(plane * 2, 1 - self.core).wait_recv()
        self.c_copy(plane * 2 + 1, 1 - self.core).wait_recv()
        return plane

    def finish(self):
        for step, far in self.reached():
            self.each(self.z_copy(step, far), "wait_send")
        for plane in range(self.planes):
            self.each(self.y_copy(plane, self.y), "wait_send")
        for pair in range(2 * self.planes):
            self.c_copy(pair, self.core).wait_send()


def split_lanes(values, x, buffer, other, start, rows):
    half = values.shape[2] // 2
    zero, one = values[:, 0, :], values[:, 1, :]
    own, far = jnp.where(x == 0, zero, one), jnp.where(x == 0, one, zero)
    core = lax.axis_index("tp")
    own = jnp.where(core == 0, own[:, :half], own[:, half:]).astype(BF16)
    buffer[core, at(start, rows), :] = own
    for side in range(2):
        other[side] = far[:, side * half : (side + 1) * half].astype(BF16)


def gather_and_project(tokens, live, episode_frames, gain, shift, qkv, bias, fixed, ahead, n):
    rows, lanes, width = tokens.shape
    half = width // 2
    total = n * rows
    chunks = total // FRAME
    per_frame = FRAME // rows
    features = qkv.shape[3]
    slots = episode_frames.shape[1]

    def kernel(*refs):
        refs = list(refs)

        def take(count):
            taken = refs[:count]
            del refs[:count]
            return taken

        tokens_ref, live_ref, counts_ref, gain_ref, shift_ref, w_any, bias_ref = take(7)
        fixed_ref, ahead_ref = take(2)
        all_ref, mask_ref, frames_ref = take(3)
        qkv_ref, *projected = take(4)
        other, lives, live_other, weight, full, w_sem = take(6)
        relay = Relay(n, rows, all_ref, other, take(Relay.sems), lives, live_other)
        load = pltpu.make_async_copy(w_any.at[0], weight, w_sem)
        load.start()
        relay.hello()
        x, me = relay.x, relay.me
        split_lanes(tokens_ref[...].astype(F32), x, all_ref, other, me * rows, rows)
        lane = lax.broadcasted_iota(jnp.int32, (1, FRAME), 1)
        here = lane // rows == lax.rem(me, per_frame)
        tiles = []
        for index in range(lanes):
            alive = live_ref[index : index + 1, :].astype(F32)
            alive = jnp.where(here, jnp.concatenate([alive] * per_frame, axis=1), 0.0)
            tiles.append(jnp.broadcast_to(alive, (8, FRAME)))
        lives[me] = jnp.where(x == 0, tiles[0], tiles[1])
        live_other[...] = jnp.where(x == 0, tiles[1], tiles[0])
        relay.met()
        relay.begin()

        counts = [counts_ref[x, slot] for slot in range(slots)]
        episodes, openings = [], []
        for frame in range(chunks):
            end, episode, opening = 0, 0, 0
            for slot in range(slots):
                end = end + counts[slot]
                passed = frame >= end
                episode = episode + passed.astype(jnp.int32)
                opening = opening + jnp.where(passed, counts[slot], 0)
            episodes.append(episode)
            openings.append(frame - opening)
        for index in range(3):
            table = []
            for frame in range(chunks):
                line = jnp.zeros((1, PAIR), F32)
                for choice in range(chunks):
                    line = jnp.where(
                        openings[frame] == choice, ahead_ref[index, choice : choice + 1, :], line
                    )
                table.append(line)
            frames_ref[index] = jnp.concatenate(
                table + [jnp.zeros((8 - chunks, PAIR), F32)], axis=0
            )
        load.wait()

        def project_frame(frame):
            place = at(frame * FRAME, FRAME)
            stream = jnp.concatenate([all_ref[0, place, :], all_ref[1, place, :]], axis=1)
            project(
                stream.astype(F32),
                frame,
                0,
                me // 2,
                (gain_ref, shift_ref, weight, bias_ref, fixed_ref, frames_ref),
                [qkv_ref.at[:, place, :]] + [ref.at[place, :] for ref in projected],
                full,
                straight=True,
            )

        for event in range(relay.events):
            relay.arrive(event)
            if event:
                relay.complete(event - 1)
            if event > 1:
                project_frame(relay.ready(event - 2))
        relay.complete(relay.events - 1)
        for event in range(max(0, relay.events - 2), relay.events):
            project_frame(relay.ready(event))
        relay.finish()

        for key_frame in range(chunks):
            alive = lives[key_frame * per_frame, 0:1, :]
            for part in range(1, per_frame):
                alive = alive + lives[key_frame * per_frame + part, 0:1, :]
            closed = (alive - 1.0) * -MASKED
            lines = []
            for query_frame in range(chunks):
                allowed = (episodes[query_frame] == episodes[key_frame]) & (
                    openings[key_frame] <= openings[query_frame]
                )
                lines.append(jnp.where(allowed, closed, MASKED))
            lines.append(jnp.zeros((PAIR - chunks, FRAME), F32))
            mask_ref[key_frame * FRAME : (key_frame + 1) * FRAME, :] = jnp.concatenate(
                lines, axis=0
            ).T.astype(BF16)

    in_vmem = pl.BlockSpec(memory_space=pltpu.VMEM)
    in_smem = pl.BlockSpec(memory_space=pltpu.SMEM)
    return pl.pallas_call(
        kernel,
        out_shape=(
            jax.ShapeDtypeStruct((2, total, half), BF16),
            jax.ShapeDtypeStruct((total, PAIR), BF16),
            jax.ShapeDtypeStruct((3, 8, PAIR), F32),
            jax.ShapeDtypeStruct((3, total, features), BF16),
            jax.ShapeDtypeStruct((total, PAIR), BF16),
            jax.ShapeDtypeStruct((total, width), BF16),
            jax.ShapeDtypeStruct((total, PAIR), F32),
        ),
        in_specs=[in_vmem, in_vmem, in_smem, in_vmem, in_vmem, ANYWHERE] + [in_vmem] * 3,
        out_specs=(in_vmem,) * 7,
        scratch_shapes=[
            pltpu.VMEM((2, rows, half), BF16),
            pltpu.VMEM((n, 8, FRAME), F32),
            pltpu.VMEM((8, FRAME), F32),
            pltpu.VMEM(qkv.shape[1:], BF16),
            pltpu.VMEM((FRAME, width), BF16),
            pltpu.SemaphoreType.DMA,
        ]
        + Relay.scratch(n),
        compiler_params=pltpu.CompilerParams(
            collective_id=0, has_side_effects=True, vmem_limit_bytes=VMEM_BYTES
        ),
        name="gather_and_project",
    )(tokens, live, episode_frames, gain, shift, qkv, bias, fixed, ahead)


def halves(ref):
    return jnp.concatenate([ref[0], ref[1]], axis=1).astype(F32)


def halves_spec(shape, chunks, behind, span=FRAME):
    return pl.BlockSpec(
        (2, span, shape[2]), lambda s: (0, jnp.clip(s - behind, 0, chunks - 1), 0)
    )


def layer_forward(layer, turned, key_bias, stream, mats, rows_of, next_refs, d_out, n, identity):
    _, total, features = turned.shape
    split = stream.ndim == 3
    width = mats[1].shape[1]
    rows_here = total // n
    hidden_units = mats[1].shape[2]
    chunks = total // FRAME
    heads = features // HEAD_DIM
    slabs = features // PAIR
    columns = 256
    last = next_refs is None
    b_out, gain, shift, b_up, b_down = rows_of
    mat_out, mat_up, mat_down = mats

    def kernel(*refs):
        refs = list(refs)

        def take(count):
            taken = refs[:count]
            del refs[:count]
            return taken

        q_ref, k_ref, v_ref, kb_ref, x_ref = take(5)
        wo_any, wu_any, wd_any = take(3)
        bo_ref, gain_ref, shift_ref, bu_ref, bd_ref = take(5)
        if not last:
            wq_any, ngain, nshift, nbias, fixed, frames = take(6)
        if d_out is not None:
            (d_ref,) = take(1)
        p_ref, r_ref, mixed_ref, unit_ref, scale_ref, second_ref, act_ref, gp_ref, x_out = take(9)
        if not last:
            next_outs = take(4)
        if d_out is not None:
            (d_all,) = take(1)
        wo, wu, wd, mid, full, next_full = take(6)
        if not last:
            (wq,) = take(1)
        a_send, a_recv, b_send, b_recv, w_sem, send_sem, recv_sem = take(7)
        relay = None
        if d_out is not None:
            buffer, other, d_sem = take(3)
            relay = Relay(n, rows_here, buffer, other, take(Relay.sems))

        step = pl.program_id(0)
        me, core = lax.axis_index("seq"), lax.axis_index("tp")

        items = [(wo_any, wo), (wu_any, wu), (wd_any, wd)]
        if not last:
            items.append((wq_any, wq))

        def load(index):
            source, target = items[index]
            return pltpu.make_async_copy(
                source.at[layer if index < 3 else layer + 1], target, w_sem.at[index]
            )

        def exchange(kind, chunk):
            source, target = ((a_send, a_recv), (b_send, b_recv))[kind]
            return remote(
                source.at[chunk],
                target.at[chunk],
                send_sem.at[kind, chunk],
                recv_sem.at[kind, chunk],
                me,
                1 - core,
            )

        @pl.when(step == 0)
        def _():
            for index in range(len(items)):
                load(index).start()
            if relay is None:
                hello([(me, 1 - core)])
            else:
                relay.hello()
                split_lanes(d_ref[...], relay.x, buffer, other, me * rows_here, rows_here)

        lane = lax.broadcasted_iota(jnp.int32, (1, PAIR), 1)
        sides = [(lane < HEAD_DIM).astype(F32).astype(BF16), (lane >= HEAD_DIM).astype(F32).astype(BF16)]
        for frame in range(chunks):

            @pl.when(step == frame)
            def _():
                keys = FRAME * (frame + 1)
                mask = kb_ref[:keys, :]
                asked = jnp.broadcast_to((lane == frame).astype(F32), (FRAME, PAIR)).astype(BF16)

                def two_slabs(couple):
                    def lanes_of(head):
                        return at((couple * 2 + head // 2) * PAIR, PAIR)

                    def score(head):
                        key = jnp.concatenate([k_ref[0, :keys, lanes_of(head)], mask], axis=1)
                        ask = q_ref[0, :, lanes_of(head)] * sides[head % 2]
                        return nt(jnp.concatenate([ask, asked], axis=1), key)

                    scores, sums = score(0), []
                    for head in range(4):
                        lanes, side = lanes_of(head), head % 2
                        following = score(head + 1) if head < 3 else None
                        highest = jnp.max(scores, axis=1, keepdims=True)
                        shifted = jnp.exp(scores - highest).astype(BF16)
                        p_ref[0, couple * 4 + head, :keys, :] = shifted.T
                        sums.append(nn(shifted, v_ref[0, :keys, lanes] * sides[side] + sides[1 - side]))
                        scores = following
                        if side == 1:
                            one, two = sums[head - 1 :]
                            low_side = lane < HEAD_DIM
                            divisor = 1.0 / jnp.where(
                                low_side, pltpu.roll(one, HEAD_DIM, 1), pltpu.roll(two, HEAD_DIM, 1)
                            )
                            r_ref[:, lanes] = divisor
                            mixed_ref[:, lanes] = (jnp.where(low_side, one, two) * divisor).astype(BF16)

                repeat(slabs // 2, two_slabs)

        @pl.when(step == 0)
        def _():
            load(0).wait()
            if relay is None:
                met([(me, 1 - core)])
            else:
                relay.met()
                relay.begin()

        @pl.when(step < chunks)
        def _():
            a_send[step] = nn(mixed_ref[...], wo[...]).astype(BF16)
            exchange(0, step).start()

        if relay is not None:
            for event in range(relay.events):

                @pl.when(step == 2 + event // 2)
                def _():
                    relay.arrive(event)

                @pl.when(step == 3 + event // 2)
                def _():
                    relay.complete(event)

            @pl.when(step == chunks + 1)
            def _():
                for event in range(relay.events):
                    relay.ready(event)
                relay.finish()
                pltpu.make_async_copy(buffer, d_all, d_sem).start()

        def feed_forward():
            chunk = step - 1
            middle = (halves(x_ref) if split else x_ref[...]) + (
                a_send[chunk].astype(F32) + a_recv[chunk].astype(F32)
            )
            middle = middle + bo_ref[layer : layer + 1, :]
            mid[lax.rem(chunk, 2)] = middle
            unit, scale = normed(middle)
            keep_norm(unit, scale, unit_ref, scale_ref)
            second = (unit * gain_ref[layer : layer + 1, :] + shift_ref[layer : layer + 1, :]).astype(BF16)
            full[...] = second
            second_ref[...] = full[:, at((me // 2) * PAIR, PAIR)]
            parts = [slice(start, start + columns) for start in range(0, hidden_units, columns)]
            hidden = nn(second, wu[:, parts[0]])
            for index, part in enumerate(parts):
                following = nn(second, wu[:, parts[index + 1]]) if index + 1 < len(parts) else None
                act, slope = gelu_both(hidden + bu_ref[layer : layer + 1, part])
                act_ref[:, part] = act.astype(BF16)
                gp_ref[:, part] = slope.astype(BF16)
                hidden = following
            b_send[chunk] = nn(act_ref[...], wd[...]).astype(BF16)

        def close():
            chunk = step - 2
            result = mid[lax.rem(chunk, 2)] + (b_send[chunk].astype(F32) + b_recv[chunk].astype(F32))
            result = result + bd_ref[layer : layer + 1, :]
            x_out[...] = result
            if not last:
                project(
                    result,
                    chunk,
                    layer + 1,
                    me // 2,
                    (ngain, nshift, wq, nbias, fixed, frames),
                    next_outs,
                    next_full,
                )

        @pl.when(step == 1)
        def _():
            load(1).wait()
            load(2).wait()

        @pl.when((step >= 1) & (step <= chunks))
        def _():
            exchange(0, step - 1).wait_recv()
            feed_forward()
            exchange(1, step - 1).start()

        if not last:

            @pl.when(step == 2)
            def _():
                load(3).wait()

        @pl.when(step >= 2)
        def _():
            exchange(1, step - 2).wait_recv()
            close()

        @pl.when(step == chunks + 1)
        def _():
            for kind in range(2):
                for chunk in range(chunks):
                    exchange(kind, chunk).wait_send()
            if relay is not None:
                pltpu.make_async_copy(buffer, d_all, d_sem).wait()

    def rows(columns, behind):
        return pl.BlockSpec(
            (FRAME, columns), lambda s: (jnp.clip(s - behind, 0, chunks - 1), 0)
        )

    def part_of(part):
        return pl.BlockSpec(
            (1, total, features), lambda s: (part, 0, 0), pipeline_mode=pl.Buffered(1)
        )

    in_specs = [
        pl.BlockSpec((1, FRAME, features), lambda s: (0, jnp.minimum(s, chunks - 1), 0)),
        part_of(1),
        part_of(2),
        whole(key_bias),
    ]
    in_specs += [halves_spec(stream.shape, chunks, 1) if split else rows(width, 1)]
    in_specs += [ANYWHERE] * 3 + [whole(item) for item in rows_of]
    operands = [turned, turned, turned, key_bias, stream, *mats, *rows_of]
    if not last:
        in_specs += [ANYWHERE] + [whole(item) for item in next_refs[1:]]
        operands += list(next_refs)
    if d_out is not None:
        in_specs += [whole(d_out)]
        operands += [d_out]
    out_shape = [
        jax.ShapeDtypeStruct((chunks, heads, total, FRAME), BF16),
        jax.ShapeDtypeStruct((total, features), F32),
        jax.ShapeDtypeStruct((total, features), BF16),
        jax.ShapeDtypeStruct((total, width), BF16),
        jax.ShapeDtypeStruct((total, PAIR), F32),
        jax.ShapeDtypeStruct((total, PAIR), BF16),
        jax.ShapeDtypeStruct((total, hidden_units), BF16),
        jax.ShapeDtypeStruct((total, hidden_units), BF16),
        jax.ShapeDtypeStruct((total, width), F32),
    ]
    out_specs = [
        pl.BlockSpec((1, heads, total, FRAME), lambda s: (jnp.minimum(s, chunks - 1), 0, 0, 0)),
        rows(features, 0),
        rows(features, 0),
        rows(width, 1),
        rows(PAIR, 1),
        rows(PAIR, 1),
        rows(hidden_units, 1),
        rows(hidden_units, 1),
        rows(width, 2),
    ]
    scratch = [
        pltpu.VMEM(mat_out.shape[1:], BF16),
        pltpu.VMEM(mat_up.shape[1:], BF16),
        pltpu.VMEM(mat_down.shape[1:], BF16),
        pltpu.VMEM((2, FRAME, width), F32),
        pltpu.VMEM((FRAME, width), BF16),
        pltpu.VMEM((FRAME, width), BF16),
    ]
    if not last:
        out_shape += [jax.ShapeDtypeStruct((3, total, features), BF16)]
        out_shape += [jax.ShapeDtypeStruct((total, PAIR), BF16)]
        out_shape += [jax.ShapeDtypeStruct((total, width), BF16)]
        out_shape += [jax.ShapeDtypeStruct((total, PAIR), F32)]
        out_specs += [
            pl.BlockSpec((3, FRAME, features), lambda s: (0, jnp.clip(s - 2, 0, chunks - 1), 0))
        ]
        out_specs += [rows(PAIR, 2), rows(width, 2), rows(PAIR, 2)]
    if d_out is not None:
        out_shape += [jax.ShapeDtypeStruct((2, total, width // 2), BF16)]
        out_specs += [ANYWHERE]
        scratch += [pltpu.VMEM(next_refs[0].shape[1:], BF16)]
    scratch += [pltpu.VMEM((chunks, FRAME, width), BF16)] * 4
    scratch += [
        pltpu.SemaphoreType.DMA((4,)),
        pltpu.SemaphoreType.DMA((2, chunks)),
        pltpu.SemaphoreType.DMA((2, chunks)),
    ]
    if d_out is not None:
        scratch += [
            pltpu.VMEM((2, total, width // 2), BF16),
            pltpu.VMEM((2, rows_here, width // 2), BF16),
            pltpu.SemaphoreType.DMA,
        ]
        scratch += Relay.scratch(n)
    return pl.pallas_call(
        kernel,
        grid=(chunks + 2,),
        out_shape=out_shape,
        in_specs=in_specs,
        out_specs=out_specs,
        scratch_shapes=scratch,
        compiler_params=pltpu.CompilerParams(
            collective_id=identity, has_side_effects=True, vmem_limit_bytes=VMEM_BYTES
        ),
        name=f"layer_forward_{layer}",
    )(*operands)


class Swap:
    def __init__(self, ships, lane_rows):
        self.ships, self.lane_rows = ships, lane_rows
        self.count = len(ships) + len(lane_rows)

    def operands(self):
        return [*self.ships, *[item for item, _ in self.lane_rows]]

    def in_specs(self):
        return [whole(item) for item in self.ships] + [ANYWHERE] * len(self.lane_rows)

    def outputs(self):
        shapes, specs = [], []
        for item in self.ships:
            shape = (item.shape[0] // 2, item.shape[1])
            shapes.append(jax.ShapeDtypeStruct(shape, F32))
            specs.append(whole_out(shape))
        for item, count in self.lane_rows:
            shapes.append(jax.ShapeDtypeStruct((count or item.shape[0], item.shape[1]), item.dtype))
            specs.append(ANYWHERE)
        return shapes, specs

    def scratch(self):
        if not self.count:
            return []
        buffers = [pltpu.VMEM((item.shape[0] // 2, item.shape[1]), BF16) for item in self.ships]
        return buffers * 2 + [pltpu.SemaphoreType.DMA((self.count,))] * 2

    def bind(self, sources, targets, scratch):
        ships = len(self.ships)
        me, core = lax.axis_index("seq"), lax.axis_index("tp")
        x = lax.rem(me, 2)
        beside = me + 1 - 2 * x
        half = PAIR // 2

        def copy(index):
            if index < ships:
                source, target = scratch[index], scratch[ships + index]
            else:
                source, target = sources[index], targets[index]
                count = self.lane_rows[index - ships][1]
                if count:
                    source = source.at[at(beside * count, count), :]
            send, recv = scratch[2 * ships].at[index], scratch[2 * ships + 1].at[index]
            return remote(source, target, send, recv, beside, core)

        def start():
            for index in range(self.count):
                if index < ships:
                    scratch[index][...] = sources[index][at((1 - x) * half, half), :].astype(BF16)
                copy(index).start()

        def finish():
            for index in range(self.count):
                copy(index).wait_recv()
                if index < ships:
                    own = sources[index][at(x * half, half), :]
                    targets[index][...] = own + scratch[ships + index][...].astype(F32)
            for index in range(self.count):
                copy(index).wait_send()

        return start, finish


def attention_backward(
    probs, divisor, mixed, turned_qkv, grad_mixed, first, fixed, frames, swap, swap_qkv, identity
):
    _, total, features = turned_qkv.shape
    chunks = total // FRAME
    slabs = features // PAIR
    half = PAIR // 2

    def kernel(*refs):
        refs = list(refs)

        def take(count):
            taken = refs[:count]
            del refs[:count]
            return taken

        p_ref, r_ref, o_ref, q_ref, k_ref, v_ref, g_ref, first_ref, fixed_ref, frames_ref = take(10)
        sources = take(swap.count)
        dq_ref, dk_ref, dv_ref, qkv_out = take(4)
        targets = take(swap.count)
        dk_sum, dv_sum, first_turned = take(3)
        if swap_qkv:
            qkv_own, qkv_send, qkv_recv, qkv_sems = take(4)
        start, finish = swap.bind(sources, targets, refs)

        step = pl.program_id(0)
        me, core = lax.axis_index("seq"), lax.axis_index("tp")
        x = lax.rem(me, 2)
        beside = me + 1 - 2 * x

        def qkv_copy(slab):
            return remote(
                qkv_send.at[slab],
                qkv_recv.at[slab],
                qkv_sems.at[0, slab],
                qkv_sems.at[1, slab],
                beside,
                core,
            )

        @pl.when(step == 0)
        def _():
            hello([(beside, core)])
            first_turned[...] = first_ref[...].T
            met([(beside, core)])
            start()

        lane = lax.broadcasted_iota(jnp.int32, (1, PAIR), 1)
        sides = [(lane < HEAD_DIM).astype(F32).astype(BF16), (lane >= HEAD_DIM).astype(F32).astype(BF16)]
        turned = k_ref[0].T
        ones = jnp.broadcast_to((lane < 2).astype(F32), (total, PAIR)).astype(BF16)
        values = jnp.concatenate([v_ref[0], ones], axis=1)

        def give(frame):
            keys = FRAME * (frame + 1)
            own = slice(frame * FRAME, keys)
            scaled = (g_ref[own, :].astype(F32) * r_ref[own, :]).astype(BF16)
            inner = scaled.astype(F32) * o_ref[own, :].astype(F32)
            grads, q_parts, g_parts = [], [], []
            for side in range(2):
                delta = jnp.sum(
                    jnp.where((lane < HEAD_DIM) == (side == 0), inner, 0.0), axis=1, keepdims=True
                )
                coarse = delta.astype(BF16).astype(F32)
                rest = jnp.where(lane == 0, -coarse, jnp.where(lane == 1, coarse - delta, 0.0))
                g2 = scaled * sides[side]
                grads.append(nt(values[:keys], jnp.concatenate([g2, rest.astype(BF16)], axis=1)))
                q_parts.append(q_ref[0, own, :] * sides[side])
                g_parts.append(g2)
            return grads, jnp.concatenate(q_parts, axis=0), jnp.concatenate(g_parts, axis=0)

        given = give(chunks - 1)
        for frame in reversed(range(chunks)):
            keys = FRAME * (frame + 1)
            own = slice(frame * FRAME, keys)
            tables = tables_of(fixed_ref, frames_ref, frame)
            grads, q_part, g_part = given
            given = give(frame - 1) if frame else None
            query_parts, score_parts, prob_parts = [], [], []
            for side in range(2):
                attention = p_ref[frame, side, :keys, :]
                grad_scores = (attention.astype(F32) * grads[side]).astype(BF16)
                query_parts.append(nn(turned[side * HEAD_DIM : (side + 1) * HEAD_DIM, :keys], grad_scores))
                score_parts.append(grad_scores)
                prob_parts.append(attention)
            grad_query = jnp.concatenate(query_parts, axis=0).T
            key_parts = nn(jnp.concatenate(score_parts, axis=1), q_part)
            value_parts = nn(jnp.concatenate(prob_parts, axis=1), g_part)
            dq_ref[own, :] = (turn(grad_query, tables, True) * SCORE_SCALE).astype(BF16)
            if frame == chunks - 1:
                dk_sum[...] = key_parts
                dv_sum[...] = value_parts
            else:
                dk_sum[:keys, :] += key_parts
                dv_sum[:keys, :] += value_parts
            dk_ref[own, :] = turn(dk_sum[own, :], tables, True).astype(BF16)
            dv_ref[own, :] = dv_sum[own, :].astype(BF16)

        for part, ref in enumerate((dq_ref, dk_ref, dv_ref)):
            piece = slice(part * PAIR, (part + 1) * PAIR)
            terms = nn(first_turned[...], ref[...])
            if swap_qkv:
                qkv_own[step, :, piece] = terms
                qkv_send[step, :, piece] = qkv_own[step, at((1 - x) * half, half), piece].astype(BF16)
            else:
                qkv_out[:, at(part * features + step * PAIR, PAIR)] = terms
        if swap_qkv:
            qkv_copy(step).start()

        @pl.when(step == slabs - 1)
        def _():
            finish()
            for slab in range(slabs if swap_qkv else 0):
                qkv_copy(slab).wait_recv()
                for part in range(3):
                    piece = slice(part * PAIR, (part + 1) * PAIR)
                    place = part * features + slab * PAIR
                    qkv_out[:, place : place + PAIR] = qkv_own[
                        slab, at(x * half, half), piece
                    ] + qkv_recv[slab, :, piece].astype(F32)
            for slab in range(slabs if swap_qkv else 0):
                qkv_copy(slab).wait_send()

    slab = pl.BlockSpec((total, PAIR), lambda s: (0, s))
    in_specs = [pl.BlockSpec((chunks, 2, total, FRAME), lambda s: (0, s, 0, 0))]
    in_specs += [slab] * 2
    for part in range(3):
        in_specs.append(pl.BlockSpec((1, total, PAIR), lambda s, part=part: (part, 0, s)))
    in_specs += [slab] + [whole(first), whole(fixed), whole(frames)]
    in_specs += swap.in_specs()
    qkv_shape = (half if swap_qkv else PAIR, 3 * features)
    shapes, specs = swap.outputs()
    out_shape = [jax.ShapeDtypeStruct((total, features), BF16)] * 3
    out_shape += [jax.ShapeDtypeStruct(qkv_shape, F32)] + shapes
    out_specs = [slab] * 3 + [whole_out(qkv_shape)] + specs
    scratch = [pltpu.VMEM((total, PAIR), F32)] * 2 + [pltpu.VMEM((PAIR, total), BF16)]
    if swap_qkv:
        scratch += [pltpu.VMEM((slabs, PAIR, 3 * PAIR), F32)]
        scratch += [pltpu.VMEM((slabs, half, 3 * PAIR), BF16)] * 2
        scratch += [pltpu.SemaphoreType.DMA((2, slabs))]
    scratch += swap.scratch()
    return pl.pallas_call(
        kernel,
        grid=(slabs,),
        out_shape=out_shape,
        in_specs=in_specs,
        out_specs=out_specs,
        scratch_shapes=scratch,
        compiler_params=pltpu.CompilerParams(
            collective_id=identity, has_side_effects=True, vmem_limit_bytes=VMEM_BYTES
        ),
        name=f"attention_backward_{identity}",
    )(
        probs,
        divisor,
        mixed,
        turned_qkv,
        turned_qkv,
        turned_qkv,
        grad_mixed,
        first,
        fixed,
        frames,
        *swap.operands(),
    )


def rows_backward(entry, upper, identity, span, swap):
    top, bottom = len(entry) == 1, upper is None
    if not top:
        above, entry = entry[0], entry[1:]
    total = entry[0].shape[1] if top else entry[0].shape[0]
    chunks = total // span
    columns = 256
    ahead = 0 if top else 2 if bottom else 1
    if top:
        width = 2 * entry[0].shape[2]
    else:
        features, width = entry[0].shape[1], entry[5].shape[1]
    if not bottom:
        layer = upper[0]
        hidden_units, mixed_features = upper[1].shape[1], upper[6].shape[1]
    place_rows = total // lax.axis_size("seq")

    def kernel(*refs):
        refs = list(refs)

        def take(count):
            taken = refs[:count]
            del refs[:count]
            return taken

        if top:
            (d_out_ref,) = take(1)
        else:
            dq_ref, dk_ref, dv_ref, unit1, scale1, dm_ref, wq, gain1 = take(8)
        if not bottom:
            act_ref, gp_ref, unit2, scale2, second_ref, mixed_ref = take(6)
            wo_any, wu_any, wd_any, gain2 = take(4)
        sources = take(swap.count)
        if not top:
            (vec1,) = take(1)
        if not bottom:
            dmid_out, dmix_out, out_sum, up_sum, down_sum, vec2 = take(6)
        else:
            dx_out, dx_other, vec_other = take(3)
        targets = take(swap.count)
        if not top:
            a_send, a_recv = take(2)
        if not bottom:
            b_send, b_recv, grad_keep, hidden_keep, low_keep, last_keep, wo, wu, wd, w_sem = take(10)
        else:
            dx_keep, dx_send, dx_recv, vec_recv, x_send_sem, x_recv_sem = take(6)
        send_sem, recv_sem = take(2)
        start_swap, finish_swap = swap.bind(sources, targets, refs)

        step = pl.program_id(0)
        me, core = lax.axis_index("seq"), lax.axis_index("tp")
        pair = at((me // 2) * PAIR, PAIR)
        x = lax.rem(me, 2)
        beside = me + 1 - 2 * x

        def exchange(kind, chunk):
            source, target = (a_send, a_recv) if kind == 0 else (b_send, b_recv)
            return remote(
                source.at[chunk],
                target.at[chunk],
                send_sem.at[kind, chunk],
                recv_sem.at[kind, chunk],
                me,
                1 - core,
            )

        def load(index):
            source, target = ((wd_any, wd), (wu_any, wu), (wo_any, wo))[index]
            return pltpu.make_async_copy(source.at[layer], target, w_sem.at[index])

        partners = [(me, 1 - core)] + ([(beside, core)] if bottom or swap.count else [])

        @pl.when(step == 0)
        def _():
            if not bottom:
                for index in range(3):
                    load(index).start()
                out_sum[...] = jnp.zeros_like(out_sum)
                up_sum[...] = jnp.zeros_like(up_sum)
                down_sum[...] = jnp.zeros_like(down_sum)
                vec2[...] = jnp.zeros_like(vec2)
            if not top:
                vec1[...] = jnp.zeros_like(vec1)
            hello(partners)

        def meet():
            @pl.when(step == 0)
            def _():
                met(partners)
                start_swap()

        def entry_products():
            partial = None
            for part, ref in enumerate((dq_ref, dk_ref, dv_ref)):
                grad = ref[...]
                term = nt(grad, wq[0, part])
                partial = term if partial is None else partial + term
                vec1[part : part + 1, :] += column_sum(grad.astype(F32))
            a_send[step] = partial.astype(BF16)

        def entry_norm(chunk):
            if top:
                return halves(d_out_ref)
            grad_first = a_send[chunk].astype(F32) + a_recv[chunk].astype(F32)
            unit, scale = kept_norm(unit1, scale1)
            for start, sums in ((3, column_sum(grad_first * unit)), (5, column_sum(grad_first))):
                for side in range(width // features):
                    piece = slice(side * features, (side + 1) * features)
                    vec1[start + side : start + side + 1, :] += sums[:, piece]
            return dm_ref[...] + norm_pull(grad_first, gain1[above : above + 1, :], unit, scale)

        def feed_forward(between=None):
            chunk = step - ahead
            gradient = entry_norm(chunk)
            if bottom:
                dx_keep[at(chunk * span, span), :] = gradient
                return
            grad_keep[lax.rem(chunk, 2)] = gradient
            vec2[1:2, :width] += column_sum(gradient)
            low = gradient.astype(BF16)
            low_keep[...] = low
            low_columns = low_keep[:, pair]
            second = second_ref[...]
            parts = [slice(start, start + columns) for start in range(0, hidden_units, columns)]
            grad_act = nt(low, wd[parts[0], :])
            for index, part in enumerate(parts):
                following = nt(low, wd[parts[index + 1], :]) if index + 1 < len(parts) else None
                grad_hidden = grad_act * gp_ref[:, part].astype(F32)
                hidden_keep[:, part] = grad_hidden.astype(BF16)
                vec2[0:1, part] += column_sum(grad_hidden)
                grad_act = following
            if between is not None:
                between()
            b_send[chunk] = nt(hidden_keep[...], wu[...]).astype(BF16)
            down_sum[...] += tn(low_columns, act_ref[...])
            up_sum[...] += tn(second, hidden_keep[...])

        def close():
            chunk = step - ahead - 1
            grad_second = b_send[chunk].astype(F32) + b_recv[chunk].astype(F32)
            unit, scale = kept_norm(unit2, scale2)
            vec2[2:3, :width] += column_sum(grad_second * unit)
            vec2[3:4, :width] += column_sum(grad_second)
            grad_middle = grad_keep[lax.rem(chunk, 2)] + norm_pull(
                grad_second, gain2[layer : layer + 1, :], unit, scale
            )
            dmid_out[...] = grad_middle
            vec2[4:5, :width] += column_sum(grad_middle)
            low = grad_middle.astype(BF16)
            last_keep[...] = low
            out_sum[...] += tn(last_keep[:, pair], mixed_ref[...])
            dmix_out[...] = nt(low, wo[...]).astype(BF16)

        if not top:

            @pl.when(step < chunks)
            def _():
                entry_products()
                meet()
                exchange(0, step).start()

        @pl.when((step >= ahead) & (step < chunks + ahead))
        def _():
            if not top:
                exchange(0, step - ahead).wait_recv()
            if not bottom:

                @pl.when(step == ahead)
                def _():
                    load(0).wait()

            feed_forward(lambda: pl.when(step == ahead)(lambda: load(1).wait()))
            if not bottom:
                if top:
                    meet()
                exchange(1, step - ahead).start()

        if not bottom:

            @pl.when(step == ahead + 1)
            def _():
                load(2).wait()

            @pl.when(step >= ahead + 1)
            def _():
                exchange(1, step - ahead - 1).wait_recv()
                close()

        if bottom:

            def x_copy(index):
                source, target = ((dx_send, dx_recv), (vec1, vec_recv))[index]
                return remote(
                    source, target, x_send_sem.at[index], x_recv_sem.at[index], beside, core
                )

            @pl.when(step == chunks + 1)
            def _():
                dx_send[...] = dx_keep[at(beside * place_rows, place_rows), :].astype(BF16)
                x_copy(0).start()
                x_copy(1).start()
                dx_out[...] = dx_keep[at(me * place_rows, place_rows), :]
                x_copy(0).wait_recv()
                x_copy(1).wait_recv()
                dx_other[...] = dx_recv[...].astype(F32)
                vec_other[...] = vec_recv[...]
                x_copy(0).wait_send()
                x_copy(1).wait_send()

        @pl.when(step == pl.num_programs(0) - 1)
        def _():
            for kind in ([] if top else [0]) + ([] if bottom else [1]):
                for chunk in range(chunks):
                    exchange(kind, chunk).wait_send()
            finish_swap()

    def rows(columns, behind):
        return pl.BlockSpec(
            (span, columns), lambda s: (jnp.clip(s - behind, 0, chunks - 1), 0)
        )

    vec = jax.ShapeDtypeStruct((8, VEC), F32)
    operands, in_specs, out_shape, out_specs, scratch = [], [], [], [], []
    if top:
        operands += list(entry)
        in_specs += [halves_spec(entry[0].shape, chunks, 0, span)]
    else:
        operands += list(entry)
        in_specs += [rows(features, 0)] * 3
        in_specs += [rows(width, ahead), rows(PAIR, ahead), rows(width, ahead)]
        in_specs += [
            pl.BlockSpec(
                (1, *entry[6].shape[1:]),
                lambda s: (above, 0, 0, 0),
                pipeline_mode=pl.Buffered(1),
            ),
            whole(entry[7]),
        ]
        narrow = jax.ShapeDtypeStruct((8, features), F32)
        out_shape += [narrow]
        out_specs += [whole_out((8, features))]
        scratch += [pltpu.VMEM((chunks, span, width), BF16)] * 2
    if not bottom:
        operands += list(upper[1:])
        in_specs += [rows(hidden_units, ahead)] * 2
        in_specs += [rows(width, ahead + 1), rows(PAIR, ahead + 1), rows(PAIR, ahead)]
        in_specs += [rows(mixed_features, ahead + 1)] + [ANYWHERE] * 3 + [whole(upper[10])]
        sums = [mixed_features, hidden_units, hidden_units]
        out_shape += [
            jax.ShapeDtypeStruct((total, width), F32),
            jax.ShapeDtypeStruct((total, mixed_features), BF16),
        ]
        out_shape += [jax.ShapeDtypeStruct((PAIR, size), F32) for size in sums] + [vec]
        out_specs += [rows(width, ahead + 1), rows(mixed_features, ahead + 1)]
        out_specs += [whole_out((PAIR, size)) for size in sums] + [whole_out((8, VEC))]
        scratch += [pltpu.VMEM((chunks, span, width), BF16)] * 2
        scratch += [
            pltpu.VMEM((2, span, width), F32),
            pltpu.VMEM((span, hidden_units), BF16),
            pltpu.VMEM((span, width), BF16),
            pltpu.VMEM((span, width), BF16),
            pltpu.VMEM(upper[7].shape[1:], BF16),
            pltpu.VMEM(upper[8].shape[1:], BF16),
            pltpu.VMEM(upper[9].shape[1:], BF16),
            pltpu.SemaphoreType.DMA((3,)),
        ]
    else:
        out_shape += [
            jax.ShapeDtypeStruct((place_rows, width), F32),
            jax.ShapeDtypeStruct((place_rows, width), F32),
            narrow,
        ]
        out_specs += [whole_out((place_rows, width))] * 2 + [whole_out((8, features))]
        scratch += [
            pltpu.VMEM((total, width), F32),
            pltpu.VMEM((place_rows, width), BF16),
            pltpu.VMEM((place_rows, width), BF16),
            pltpu.VMEM((8, features), F32),
            pltpu.SemaphoreType.DMA((2,)),
            pltpu.SemaphoreType.DMA((2,)),
        ]
    scratch += [pltpu.SemaphoreType.DMA((2, chunks))] * 2
    operands += swap.operands()
    in_specs += swap.in_specs()
    shapes, specs = swap.outputs()
    out_shape += shapes
    out_specs += specs
    scratch += swap.scratch()
    return pl.pallas_call(
        kernel,
        grid=(chunks + (1 if top else 2),),
        out_shape=out_shape,
        in_specs=in_specs,
        out_specs=out_specs,
        scratch_shapes=scratch,
        compiler_params=pltpu.CompilerParams(
            collective_id=identity, has_side_effects=True, vmem_limit_bytes=VMEM_BYTES
        ),
        name=f"rows_backward_{identity}",
    )(*operands)


def assemble(sums, vecs, lanes, n, features, hidden_units):
    place = lanes[1].shape[0]
    width = lanes[1].shape[1]
    half = PAIR // 2

    def kernel(*refs):
        refs = list(refs)

        def take(count):
            taken = refs[:count]
            del refs[:count]
            return taken

        qkvs, outs, ups, downs = take(LAYERS), take(LAYERS), take(LAYERS), take(LAYERS)
        vec_refs = [take(4) for _ in range(LAYERS)]
        out_lane, out_other, dx_own, dx_other = take(4)
        out_ref, dx_ref, gain1, shift1, g_qkv, b_qkv, g_out, b_out = take(8)
        gain2, shift2, g_up, b_up, g_down, b_down = take(6)
        out_own, sem = refs
        me = lax.axis_index("seq")
        x = lax.rem(me, 2)
        fetch = pltpu.make_async_copy(out_lane.at[at(me * place, place), :], out_own, sem)
        fetch.start()

        for layer in range(LAYERS):
            for part in range(3):
                g_qkv[layer, part] = qkvs[layer][:, part * features : (part + 1) * features]
            for ref, target in ((outs, g_out), (ups, g_up), (downs, g_down)):
                target[layer] = ref[layer][...]

        for layer, (entry_own, entry_other, upper_own, upper_other) in enumerate(vec_refs):
            line = slice(layer, layer + 1)
            for part in range(3):
                row = slice(part, part + 1)
                b_qkv[part, line, :] = entry_own[row, :] + entry_other[row, :]
            b_up[line, :] = upper_own[0:1, :hidden_units] + upper_other[0:1, :hidden_units]

            def owned(mine, other, row):
                wide = mine.shape[1]
                place = (me // 2) * PAIR
                pair = at(lax.rem(place, wide), PAIR)
                both = mine[row : row + 1, pair] + other[row : row + 1, pair]
                for later in range(1, width // wide):
                    line = slice(row + later, row + later + 1)
                    both = jnp.where(place // wide == later, mine[line, pair] + other[line, pair], both)
                return jnp.where(x == 0, both[:, :half], both[:, half:])

            gain1[line, :] = owned(entry_own, entry_other, 3)
            shift1[line, :] = owned(entry_own, entry_other, 5)
            b_down[line, :] = owned(upper_own, upper_other, 1)
            gain2[line, :] = owned(upper_own, upper_other, 2)
            shift2[line, :] = owned(upper_own, upper_other, 3)
            b_out[line, :] = owned(upper_own, upper_other, 4)

        def both_lanes(target, mine, other):
            target[:, 0, :] = jnp.where(x == 0, mine, other)
            target[:, 1, :] = jnp.where(x == 0, other, mine)

        both_lanes(dx_ref, dx_own[...], dx_other[...])
        fetch.wait()
        both_lanes(out_ref, out_own[...], out_other[...])

    def f32(*shape):
        return jax.ShapeDtypeStruct(shape, F32)

    in_vmem = pl.BlockSpec(memory_space=pltpu.VMEM)
    flat = []
    for kind in range(4):
        flat += [sums[layer][kind] for layer in range(LAYERS)]
    for layer in range(LAYERS):
        flat += list(vecs[layer])
    flat += list(lanes)
    small = f32(LAYERS, width // n)
    return pl.pallas_call(
        kernel,
        out_shape=(
            f32(place, 2, width),
            f32(place, 2, width),
            small,
            small,
            f32(LAYERS, 3, half, features),
            f32(3, LAYERS, features),
            f32(LAYERS, half, features),
            small,
            small,
            small,
            f32(LAYERS, half, hidden_units),
            f32(LAYERS, hidden_units),
            f32(LAYERS, half, hidden_units),
            small,
        ),
        in_specs=[in_vmem] * (len(flat) - 4) + [ANYWHERE] + [in_vmem] * 3,
        out_specs=(in_vmem,) * 14,
        scratch_shapes=[pltpu.VMEM((place, width), F32), pltpu.SemaphoreType.DMA],
        compiler_params=pltpu.CompilerParams(vmem_limit_bytes=VMEM_BYTES),
        name="assemble",
    )(*flat)


def per_chip(
    tokens,
    d_out,
    norm1_gain,
    norm1_shift,
    w_qkv,
    b_qkv,
    w_out,
    b_out,
    norm2_gain,
    norm2_shift,
    w_up,
    b_up,
    w_down,
    b_down,
    episode_frames,
    live,
):
    n = lax.axis_size("seq")
    rows = tokens.shape[0]
    features = w_qkv.shape[3]
    fixed, ahead = turn_constants(rows * n // FRAME)
    qkv, qkv_bias = w_qkv.transpose(0, 2, 1, 3), b_qkv.transpose(1, 0, 2)

    gathered, key_bias, frames, *projected = gather_and_project(
        tokens, live.T, episode_frames, norm1_gain, norm1_shift, qkv, qkv_bias, fixed, ahead, n
    )
    streams, kept, d_lane = [gathered], [], None
    for layer in range(LAYERS):
        following = None
        if layer + 1 < LAYERS:
            following = (qkv, norm1_gain, norm1_shift, qkv_bias, fixed, frames)
        results = layer_forward(
            layer,
            projected[0],
            key_bias,
            streams[layer],
            (w_out, w_up, w_down),
            (b_out, norm2_gain, norm2_shift, b_up, b_down),
            following,
            d_out if layer == 0 else None,
            n,
            1 + layer,
        )
        kept.append((*projected, *results[:8]))
        streams.append(results[8])
        if following is not None:
            projected = results[9:13]
        if layer == 0:
            d_lane = results[-1]

    sums = [[None] * 4 for _ in range(LAYERS)]
    vecs = [[None] * 4 for _ in range(LAYERS)]
    entry, later = (d_lane,), None
    for layer in reversed(range(LAYERS)):
        turned, first, unit1, scale1, probs, divisor, mixed = kept[layer][:7]
        unit2, scale2, second, act, slope = kept[layer][7:]
        upper = (
            layer,
            act,
            slope,
            unit2,
            scale2,
            second,
            mixed,
            w_out,
            w_up,
            w_down,
            norm2_gain,
        )
        identity = 1 + LAYERS + 2 * (LAYERS - 1 - layer)
        if later is None:
            results = rows_backward(entry, upper, identity, FRAME, Swap([], []))
        else:
            swap = Swap(later[:2], [(later[2], 0), (streams[LAYERS], rows)])
            vec1, *results = rows_backward(entry, upper, identity, FRAME, swap)
            results, swapped = results[:6], results[6:]
            sums[layer + 1][3], sums[layer + 1][0] = swapped[:2]
            vecs[layer + 1][3], out_other = swapped[2:]
            vecs[layer + 1][0] = vec1
        grad_middle, grad_mixed, out_sum, up_sum, down_sum, vec2 = results
        vecs[layer][2] = vec2
        last = layer == 0
        if last:
            swap = Swap([out_sum, up_sum], [(vec2, 0), (vecs[layer + 1][0], 0)])
        else:
            swap = Swap([out_sum, up_sum], [])
        results = attention_backward(
            probs,
            divisor,
            mixed,
            turned,
            grad_mixed,
            first,
            fixed,
            frames,
            swap,
            False,
            identity + 1,
        )
        grad_query, grad_key, grad_value, qkv_sum = results[:4]
        if last:
            sums[layer][1:3] = results[4:6]
            vecs[layer][3], vecs[layer + 1][1] = results[6:8]
        else:
            sums[layer][1:3] = results[4:6]
            later = [down_sum, qkv_sum, vec2]
        entry = (
            layer,
            grad_query,
            grad_key,
            grad_value,
            unit1,
            scale1,
            grad_middle,
            qkv,
            norm1_gain,
        )
    vec1, dx_own, dx_other, vec_other, sums[0][3], sums[0][0] = rows_backward(
        entry, None, 1 + 3 * LAYERS, FRAME, Swap([down_sum, qkv_sum], [])
    )
    vecs[0][:2] = [vec1, vec_other]
    results = list(
        assemble(
            sums,
            vecs,
            (streams[LAYERS], out_other, dx_own, dx_other),
            n,
            features,
            w_up.shape[2],
        )
    )
    results[4] = results[4].transpose(0, 2, 1, 3)
    results[5] = results[5].transpose(1, 0, 2)
    results[6] = results[6].transpose(0, 2, 1)
    results[12] = results[12].transpose(0, 2, 1)
    return tuple(results)


def lane_fits(mesh, tokens):
    n = mesh.shape["seq"]
    positions, lanes, width = tokens.shape
    rows = positions // n
    return (
        lanes == 2
        and n % 4 == 0
        and positions <= 4 * FRAME
        and positions % FRAME == 0
        and FRAME % rows == 0
        and width // n * 2 == PAIR
        and mesh.shape["tp"] == 2
    )


def solution(mesh):
    placed = (
        P("seq", None, None),
        P("seq", None, None),
        P(),
        P(),
        P(None, None, None, "tp"),
        P(None, None, "tp"),
        P(None, "tp", None),
        P(),
        P(),
        P(),
        P(None, None, "tp"),
        P(None, "tp"),
        P(None, "tp", None),
        P(),
        P(),
        P("seq", None),
    )
    def mapped(body):
        return jax.shard_map(
            body,
            mesh=mesh,
            in_specs=placed,
            out_specs=(
                P("seq", None, None),
                P("seq", None, None),
                P(None, "seq"),
                P(None, "seq"),
                P(None, "seq", None, "tp"),
                P(None, None, "tp"),
                P(None, "tp", "seq"),
                P(None, "seq"),
                P(None, "seq"),
                P(None, "seq"),
                P(None, "seq", "tp"),
                P(None, "tp"),
                P(None, "tp", "seq"),
                P(None, "seq"),
            ),
            check_vma=False,
        )

    def run(tokens, *others):
        if lane_fits(mesh, tokens):
            return mapped(per_chip)(tokens, *others)
        return mapped(per_device)(tokens, *others)

    return run
```

```python
import math

import jax
import jax.numpy as jnp
import numpy as np
from jax import lax
from jax.experimental import pallas as pl
from jax.experimental.pallas import tpu as pltpu
from jax.sharding import PartitionSpec as P

HEAD_DIM = 64
GRID = 16
FRAME = 256
LAYERS = 2
MICRO = 2


EPSILON = 1e-06
MASKED = -1e30
SCORE_SCALE = 0.125


def layer_norm(stream, norm_gain, norm_shift):
    center = stream - jnp.mean(stream, axis=-1, keepdims=True)
    spread = jnp.mean(center * center, axis=-1, keepdims=True)
    return center * lax.rsqrt(spread + EPSILON) * norm_gain + norm_shift


def rotate(values, frame_place, row_place, column_place):
    frequency = jnp.exp(jnp.arange(10, dtype=jnp.float32) * (-math.log(10000.0) / 10.0))
    pieces = []
    for section, place in enumerate((frame_place, row_place, column_place)):
        lower = values[..., 20 * section : 20 * section + 10]
        upper = values[..., 20 * section + 10 : 20 * section + 20]
        angles = place.astype(jnp.float32)[..., None, None] * frequency
        cosine = jnp.cos(angles)
        sine_part = jnp.sin(angles)
        pieces.append(lower * cosine - upper * sine_part)
        pieces.append(lower * sine_part + upper * cosine)
    pieces.append(values[..., 60:])
    return jnp.concatenate(pieces, axis=-1)


def episode_tags(frame_counts, positions):
    endings = jnp.cumsum(frame_counts) * FRAME
    passed = (positions[:, None] >= endings[None, :]).astype(jnp.int32)
    episode = jnp.sum(passed, axis=1)
    opening = jnp.sum(passed * frame_counts[None, :], axis=1)
    frame_index = positions // FRAME - opening
    within = positions % FRAME
    return (episode, frame_index, within // GRID, within % GRID)


def gelu_exact(values):
    return jax.nn.gelu(values, approximate=False)


def sum_heads(partial_sum):
    return lax.psum(partial_sum.astype(jnp.bfloat16), "tp").astype(jnp.float32)


def sum_inputs(partial_sum):
    return lax.psum(partial_sum.astype(jnp.bfloat16), "tp").astype(jnp.float32)


def lane_scores(query, keys_all, lane_index, query_tags, key_tags):
    head_count = query.shape[2] // HEAD_DIM
    query_lane = lax.dynamic_index_in_dim(query, lane_index, 1, False).reshape(
        query.shape[0], head_count, HEAD_DIM
    )
    keys_lane = lax.dynamic_index_in_dim(keys_all, lane_index, 1, False).reshape(
        keys_all.shape[0], head_count, HEAD_DIM
    )
    query_episode, query_frame = [
        lax.dynamic_index_in_dim(item, lane_index, 1, False) for item in query_tags
    ]
    key_episode, key_frame, key_live = [
        lax.dynamic_index_in_dim(item, lane_index, 1, False) for item in key_tags
    ]
    allowed = (
        (query_episode[:, None] == key_episode[None, :])
        & (key_frame[None, :] <= query_frame[:, None])
        & (key_live[None, :] > 0)
    )
    scores = (
        jnp.einsum("qhd,khd->hqk", query_lane, keys_lane, preferred_element_type=jnp.float32)
        * SCORE_SCALE
    )
    return (jnp.where(allowed[None], scores, MASKED), query_lane, keys_lane)


def attend_forward(query, keys_all, values_all, query_tags, key_tags):
    rows_dev, lane_count, features = query.shape
    head_count = features // HEAD_DIM

    def one_lane(lane_index, carry):
        scores, query_lane, keys_lane = lane_scores(
            query, keys_all, lane_index, query_tags, key_tags
        )
        highest = jnp.max(scores, axis=-1, keepdims=True)
        shifted = jnp.exp(scores - highest)
        summed = jnp.sum(shifted, axis=-1, keepdims=True)
        attention = (shifted / summed).astype(jnp.bfloat16)
        values_lane = lax.dynamic_index_in_dim(values_all, lane_index, 1, False).reshape(
            values_all.shape[0], head_count, HEAD_DIM
        )
        result = jnp.einsum(
            "hqk,khd->qhd", attention, values_lane, preferred_element_type=jnp.float32
        ).reshape(rows_dev, 1, features)
        log_total = (highest + jnp.log(summed))[None, :, :, 0]
        return (result, log_total)

    initial = (
        jnp.zeros((rows_dev, lane_count, features), jnp.float32),
        jnp.zeros((lane_count, head_count, rows_dev), jnp.float32),
    )
    return lax.fori_loop(0, lane_count, one_lane, initial)


def attend_backward(query, keys_all, values_all, log_total, grad_mixed, query_tags, key_tags):
    rows_dev, lane_count, features = query.shape
    head_count = features // HEAD_DIM
    key_rows = keys_all.shape[0]

    def one_lane(lane_index, carry):
        scores, query_lane, keys_lane = lane_scores(
            query, keys_all, lane_index, query_tags, key_tags
        )
        values_lane = lax.dynamic_index_in_dim(values_all, lane_index, 1, False).reshape(
            key_rows, head_count, HEAD_DIM
        )
        grad_lane = lax.dynamic_index_in_dim(grad_mixed, lane_index, 1, False).reshape(
            rows_dev, head_count, HEAD_DIM
        )
        attention = jnp.exp(
            scores - lax.dynamic_index_in_dim(log_total, lane_index, 0, False)[:, :, None]
        )
        grad_attention = jnp.einsum(
            "qhd,khd->hqk", grad_lane, values_lane, preferred_element_type=jnp.float32
        )
        inner = jnp.sum(attention * grad_attention, axis=-1, keepdims=True)
        grad_scores = (attention * (grad_attention - inner)).astype(jnp.bfloat16)
        query_part = (
            jnp.einsum("hqk,khd->qhd", grad_scores, keys_lane, preferred_element_type=jnp.float32)
            * SCORE_SCALE
        )
        key_part = (
            jnp.einsum("hqk,qhd->khd", grad_scores, query_lane, preferred_element_type=jnp.float32)
            * SCORE_SCALE
        )
        value_part = jnp.einsum(
            "hqk,qhd->khd",
            attention.astype(jnp.bfloat16),
            grad_lane,
            preferred_element_type=jnp.float32,
        )
        stacked = jnp.stack(
            [key_part.reshape(key_rows, features), value_part.reshape(key_rows, features)], axis=1
        )
        key_terms = stacked[:, None]
        grad_query = query_part.reshape(rows_dev, 1, features)
        return (grad_query, key_terms)

    initial = (
        jnp.zeros((rows_dev, lane_count, features), jnp.float32),
        jnp.zeros((key_rows, lane_count, 2, features), jnp.float32),
    )
    return lax.fori_loop(0, lane_count, one_lane, initial)


def front(stream, layer_index, params, query_tags, key_tags, positions):
    (
        gain_one,
        shift_one,
        mat_qkv,
        bias_qkv,
        mat_out,
        bias_out,
        gain_two,
        shift_two,
        mat_up,
        bias_up,
        mat_down,
        bias_down,
    ) = [item[layer_index] for item in params]
    rows_dev, lane_count, width = stream.shape
    features = mat_qkv.shape[2]
    head_count = features // HEAD_DIM
    frame_place, row_place, column_place = positions
    first = layer_norm(stream, gain_one, shift_one).astype(jnp.bfloat16)
    projected = (
        jnp.einsum("tbd,dcf->tbcf", first, mat_qkv, preferred_element_type=jnp.float32) + bias_qkv
    )
    split = projected.reshape(rows_dev, lane_count, 3, head_count, HEAD_DIM)
    query = (
        rotate(split[:, :, 0], frame_place, row_place, column_place)
        .reshape(rows_dev, lane_count, features)
        .astype(jnp.bfloat16)
    )
    keys = (
        rotate(split[:, :, 1], frame_place, row_place, column_place)
        .reshape(rows_dev, lane_count, features)
        .astype(jnp.bfloat16)
    )
    values = projected[:, :, 2].astype(jnp.bfloat16)
    keys_all, values_all = (
        lax.all_gather(keys, "seq", axis=0, tiled=True),
        lax.all_gather(values, "seq", axis=0, tiled=True),
    )
    mixed_full, log_total = attend_forward(query, keys_all, values_all, query_tags, key_tags)
    mixed = mixed_full.astype(jnp.bfloat16)
    middle = (
        stream
        + sum_heads(jnp.einsum("tbf,fd->tbd", mixed, mat_out, preferred_element_type=jnp.float32))
        + bias_out
    )
    second = layer_norm(middle, gain_two, shift_two).astype(jnp.bfloat16)
    hidden = jnp.einsum("tbd,df->tbf", second, mat_up, preferred_element_type=jnp.float32) + bias_up
    activation = gelu_exact(hidden).astype(jnp.bfloat16)
    return (
        first,
        query,
        keys_all,
        values_all,
        log_total,
        mixed,
        middle,
        second,
        hidden,
        activation,
        mixed_full,
    )


def layer_backward(stream, gradient, layer_index, params, query_tags, key_tags, positions):
    (
        gain_one,
        shift_one,
        mat_qkv,
        bias_qkv,
        mat_out,
        bias_out,
        gain_two,
        shift_two,
        mat_up,
        bias_up,
        mat_down,
        bias_down,
    ) = [item[layer_index] for item in params]
    (
        first,
        query,
        keys_all,
        values_all,
        log_total,
        mixed,
        middle,
        second,
        hidden,
        activation,
        mixed_full,
    ) = front(stream, layer_index, params, query_tags, key_tags, positions)
    frame_place, row_place, column_place = positions
    rows_dev, lane_count, width = stream.shape
    features = query.shape[2]
    head_count = features // HEAD_DIM
    grad_low = gradient.astype(jnp.bfloat16)
    grad_w_down = jnp.einsum(
        "tbf,tbd->fd", activation, grad_low, preferred_element_type=jnp.float32
    )
    grad_b_down = jnp.sum(gradient, axis=(0, 1))
    grad_activation = jnp.einsum(
        "tbd,fd->tbf", grad_low, mat_down, preferred_element_type=jnp.float32
    )
    grad_hidden = jax.vjp(gelu_exact, hidden)[1](grad_activation)[0].astype(jnp.bfloat16)
    grad_b_up = jnp.sum(grad_hidden.astype(jnp.float32), axis=(0, 1))
    grad_w_up = jnp.einsum("tbd,tbf->df", second, grad_hidden, preferred_element_type=jnp.float32)
    grad_second = sum_inputs(
        jnp.einsum("tbf,df->tbd", grad_hidden, mat_up, preferred_element_type=jnp.float32)
    )
    middle_pull = jax.vjp(layer_norm, middle, gain_two, shift_two)[1]
    grad_inner, grad_gain_two, grad_shift_two = middle_pull(grad_second)
    grad_middle = gradient + grad_inner
    grad_b_out = jnp.sum(grad_middle, axis=(0, 1))
    middle_low = grad_middle.astype(jnp.bfloat16)
    grad_w_out = jnp.einsum("tbf,tbd->fd", mixed, middle_low, preferred_element_type=jnp.float32)
    grad_mixed = jnp.einsum(
        "tbd,fd->tbf", middle_low, mat_out, preferred_element_type=jnp.float32
    ).astype(jnp.bfloat16)
    grad_query, key_terms = attend_backward(
        query, keys_all, values_all, log_total, grad_mixed, query_tags, key_tags
    )
    returned = lax.psum_scatter(key_terms, "seq", scatter_dimension=0, tiled=True)
    turned_query = rotate(
        grad_query.reshape(rows_dev, lane_count, head_count, HEAD_DIM),
        -frame_place,
        -row_place,
        -column_place,
    )
    turned_keys = rotate(
        returned[:, :, 0].reshape(rows_dev, lane_count, head_count, HEAD_DIM),
        -frame_place,
        -row_place,
        -column_place,
    )
    grad_projected = jnp.stack(
        [
            turned_query.reshape(rows_dev, lane_count, features),
            turned_keys.reshape(rows_dev, lane_count, features),
            returned[:, :, 1],
        ],
        axis=2,
    ).astype(jnp.bfloat16)
    grad_b_qkv = jnp.sum(grad_projected.astype(jnp.float32), axis=(0, 1))
    grad_w_qkv = jnp.einsum(
        "tbd,tbcf->dcf", first, grad_projected, preferred_element_type=jnp.float32
    )
    grad_first = sum_inputs(
        jnp.einsum("tbcf,dcf->tbd", grad_projected, mat_qkv, preferred_element_type=jnp.float32)
    )
    first_pull = jax.vjp(layer_norm, stream, gain_one, shift_one)[1]
    grad_entry, grad_gain_one, grad_shift_one = first_pull(grad_first)
    grads = (
        grad_gain_one,
        grad_shift_one,
        grad_w_qkv,
        grad_b_qkv,
        grad_w_out,
        grad_b_out,
        grad_gain_two,
        grad_shift_two,
        grad_w_up,
        grad_b_up,
        grad_w_down,
        grad_b_down,
    )
    return (grad_middle + grad_entry, grads)


def per_device(
    tokens,
    d_out,
    norm1_gain,
    norm1_shift,
    w_qkv,
    b_qkv,
    w_out,
    b_out,
    norm2_gain,
    norm2_shift,
    w_up,
    b_up,
    w_down,
    b_down,
    episode_frames,
    live,
):
    rows_dev = tokens.shape[0]
    lane_count = tokens.shape[1] // MICRO
    total_rows = rows_dev * lax.axis_size("seq")
    local_positions = lax.axis_index("seq") * rows_dev + jnp.arange(rows_dev, dtype=jnp.int32)
    key_positions = jnp.arange(total_rows, dtype=jnp.int32)
    tagger = jax.vmap(episode_tags, in_axes=(0, None), out_axes=1)
    query_episode, query_frame, query_row, query_column = tagger(episode_frames, local_positions)
    key_episode, key_frame, key_row, key_column = tagger(episode_frames, key_positions)
    live_keys = lax.all_gather(live, "seq", axis=0, tiled=True)
    params = (
        norm1_gain,
        norm1_shift,
        w_qkv,
        b_qkv,
        w_out,
        b_out,
        norm2_gain,
        norm2_shift,
        w_up,
        b_up,
        w_down,
        b_down,
    )
    layer_grads = [None] * LAYERS
    outputs = []
    grad_tokens = []
    for micro_index in range(MICRO):
        first_lane = micro_index * lane_count
        last_lane = first_lane + lane_count
        query_tags = (query_episode[:, first_lane:last_lane], query_frame[:, first_lane:last_lane])
        key_tags = (
            key_episode[:, first_lane:last_lane],
            key_frame[:, first_lane:last_lane],
            live_keys[:, first_lane:last_lane],
        )
        positions = (
            query_frame[:, first_lane:last_lane],
            query_row[:, first_lane:last_lane],
            query_column[:, first_lane:last_lane],
        )
        stream = tokens[:, first_lane:last_lane].astype(jnp.float32)
        inputs = []
        gathered = []
        for layer_index in range(LAYERS):
            inputs.append(stream)
            layer_state = front(stream, layer_index, params, query_tags, key_tags, positions)
            gathered.append((layer_state[2], layer_state[3]))
            branch = jnp.einsum(
                "tbf,fd->tbd",
                layer_state[9],
                w_down[layer_index],
                preferred_element_type=jnp.float32,
            )
            stream = layer_state[6] + sum_heads(branch) + b_down[layer_index]
        outputs.append(stream)
        gradient = d_out[:, first_lane:last_lane]
        for layer_index in reversed(range(LAYERS)):
            gradient, grads = layer_backward(
                inputs[layer_index], gradient, layer_index, params, query_tags, key_tags, positions
            )
            if layer_grads[layer_index] is None:
                layer_grads[layer_index] = grads
            else:
                layer_grads[layer_index] = jax.tree.map(jnp.add, layer_grads[layer_index], grads)
        grad_tokens.append(gradient)
    stacked = [
        jnp.stack([layer_grads[layer_index][entry] for layer_index in range(LAYERS)])
        for entry in range(12)
    ]
    (
        grad_gain_one,
        grad_shift_one,
        grad_w_qkv,
        grad_b_qkv,
        grad_w_out,
        grad_b_out,
        grad_gain_two,
        grad_shift_two,
        grad_w_up,
        grad_b_up,
        grad_w_down,
        grad_b_down,
    ) = stacked
    in_sums = (
        lax.psum_scatter(grad_w_qkv, "seq", scatter_dimension=1, tiled=True),
        lax.psum_scatter(grad_w_up, "seq", scatter_dimension=1, tiled=True),
        lax.psum_scatter(grad_gain_one, "seq", scatter_dimension=1, tiled=True),
        lax.psum_scatter(grad_shift_one, "seq", scatter_dimension=1, tiled=True),
        lax.psum_scatter(grad_gain_two, "seq", scatter_dimension=1, tiled=True),
        lax.psum_scatter(grad_shift_two, "seq", scatter_dimension=1, tiled=True),
        lax.psum_scatter(grad_b_out, "seq", scatter_dimension=1, tiled=True),
        lax.psum_scatter(grad_b_down, "seq", scatter_dimension=1, tiled=True),
    )
    out_sums = (
        lax.psum_scatter(grad_w_out, "seq", scatter_dimension=2, tiled=True),
        lax.psum_scatter(grad_w_down, "seq", scatter_dimension=2, tiled=True),
    )
    bias_total = lax.psum((grad_b_qkv, grad_b_up), "seq")
    return (
        jnp.concatenate(outputs, axis=1),
        jnp.concatenate(grad_tokens, axis=1),
        in_sums[2],
        in_sums[3],
        in_sums[0],
        bias_total[0],
        out_sums[0],
        in_sums[6],
        in_sums[4],
        in_sums[5],
        in_sums[1],
        bias_total[1],
        out_sums[1],
        in_sums[7],
    )


MESH = pl.DeviceIdType.MESH
BF16 = jnp.bfloat16
F32 = jnp.float32
VMEM_BYTES = 60 * 1024 * 1024
PAIR = 128
VEC = 2048


def nn(left, right):
    return lax.dot_general(left, right, (((1,), (0,)), ((), ())), preferred_element_type=F32)


def nt(left, right):
    return lax.dot_general(left, right, (((1,), (1,)), ((), ())), preferred_element_type=F32)


def tn(left, right):
    return lax.dot_general(left, right, (((0,), (0,)), ((), ())), preferred_element_type=F32)


def at(start, size):
    return pl.ds(pl.multiple_of(start, size), size)


def repeat(count, body):
    def one(index, carry):
        body(index)
        return carry

    lax.fori_loop(0, count, one, 0)


def remote(src, dst, send, recv, seq, tp):
    return pltpu.make_async_remote_copy(
        src_ref=src,
        dst_ref=dst,
        send_sem=send,
        recv_sem=recv,
        device_id=(seq, tp),
        device_id_type=MESH,
    )


def hello(partners):
    barrier = pltpu.get_barrier_semaphore()
    for seq, tp in partners:
        pl.semaphore_signal(barrier, inc=1, device_id=(seq, tp), device_id_type=MESH)


def met(partners):
    pl.semaphore_wait(pltpu.get_barrier_semaphore(), len(partners))


def whole(array):
    zeros = (0,) * array.ndim
    return pl.BlockSpec(array.shape, lambda s: zeros, pipeline_mode=pl.Buffered(1))


def whole_out(shape):
    zeros = (0,) * len(shape)
    return pl.BlockSpec(shape, lambda s: zeros)


ANYWHERE = pl.BlockSpec(memory_space=pl.ANY)


def turn_row(table, place, section):
    frequency = np.exp(np.arange(10, dtype=np.float32) * np.float32(-math.log(10000.0) / 10.0))
    angle = place.astype(np.float32)[:, None] * frequency
    for base in range(20 * section, PAIR, HEAD_DIM):
        table[0, :, base : base + 10] = np.cos(angle)
        table[0, :, base + 10 : base + 20] = np.cos(angle)
        table[1, :, base : base + 10] = -np.sin(angle)
        table[2, :, base + 10 : base + 20] = np.sin(angle)


def turn_constants(frames):
    within, ahead = np.zeros((3, FRAME, PAIR), np.float32), np.zeros((3, frames, PAIR), np.float32)
    turn_row(within, np.arange(FRAME) // GRID, 1)
    turn_row(within, np.arange(FRAME) % GRID, 2)
    for base in range(60, PAIR, HEAD_DIM):
        within[0, :, base : base + 4] = 1.0
    turn_row(ahead, np.arange(frames), 0)
    return jnp.asarray(within), jnp.asarray(ahead)


def turn(values, tables, back=False):
    cosine, lower, upper = tables
    pieces = []
    for start in range(0, values.shape[1], PAIR):
        slab = values[:, start : start + PAIR]
        moved = pltpu.roll(slab, PAIR - 10, 1) * lower + pltpu.roll(slab, 10, 1) * upper
        pieces.append(slab * cosine - moved if back else slab * cosine + moved)
    return jnp.concatenate(pieces, axis=1)


def tables_of(fixed_ref, frames_ref, chunk):
    return [fixed_ref[i] + frames_ref[i, pl.ds(chunk, 1), :] for i in range(3)]


def normed(stream):
    center = stream - jnp.mean(stream, axis=-1, keepdims=True)
    spread = jnp.mean(center * center, axis=-1, keepdims=True)
    scale = lax.rsqrt(spread + EPSILON)
    return center * scale, scale


def norm_pull(grad, gain, unit, scale):
    scaled = grad * gain
    return scale * (
        scaled
        - jnp.mean(scaled, axis=-1, keepdims=True)
        - unit * jnp.mean(scaled * unit, axis=-1, keepdims=True)
    )


def keep_norm(unit, scale, unit_ref, scale_ref):
    unit_ref[...] = unit.astype(BF16)
    scale_ref[...] = jnp.broadcast_to(scale, scale_ref.shape)


def kept_norm(unit_ref, scale_ref):
    copies = unit_ref.shape[1] // scale_ref.shape[1]
    return unit_ref[...].astype(F32), jnp.concatenate([scale_ref[...]] * copies, axis=1)


def column_sum(values):
    return jnp.sum(values, axis=0, keepdims=True)


def gelu_both(hidden):
    normal = 0.5 + 0.5 * lax.erf(hidden * math.sqrt(0.5))
    density = jnp.exp(hidden * hidden * -0.5) * (1.0 / math.sqrt(2.0 * math.pi))
    return hidden * normal, normal + hidden * density


def project(stream, chunk, layer, pair, refs, outs, first_full, straight=False):
    gain, shift, weight, bias, fixed, frames = refs
    qkv_ref, first_ref, unit_ref, scale_ref = outs
    unit, scale = normed(stream)
    keep_norm(unit, scale, unit_ref, scale_ref)
    first_full[...] = (unit * gain[layer : layer + 1, :] + shift[layer : layer + 1, :]).astype(BF16)
    first_ref[...] = first_full[:, at(pair * PAIR, PAIR)]
    cosine, lower, upper = tables_of(fixed, frames, chunk)

    def one(part):
        still = part == 2
        tables = (
            jnp.where(still, 1.0, cosine),
            jnp.where(still, 0.0, lower),
            jnp.where(still, 0.0, upper),
        )
        values = nn(first_full[...], weight[part]) + bias[part, layer : layer + 1, :]
        qkv_ref[part] = (turn(values, tables) * jnp.where(part == 0, SCORE_SCALE, 1.0)).astype(BF16)

    if not straight:
        repeat(3, one)
        return
    for part in range(3):
        values = nn(first_full[...], weight[part]) + bias[part, layer : layer + 1, :]
        if part < 2:
            values = turn(values, (cosine, lower, upper))
        if part == 0:
            values = values * SCORE_SCALE
        qkv_ref[part] = values.astype(BF16)


class Relay:
    sems = 6

    def __init__(self, n, rows, buffer, other, sems, lives=None, live_other=None):
        self.n, self.rows, self.buffer, self.other = n, rows, buffer, other
        self.lives, self.live_other = lives, live_other
        self.z_send, self.z_recv, self.y_send, self.y_recv, self.c_send, self.c_recv = sems
        self.planes = n // 4
        self.me, self.core = lax.axis_index("seq"), lax.axis_index("tp")
        me = self.me
        self.x, self.y, self.z = lax.rem(me, 2), lax.rem(me // 2, 2), me // 4
        self.across = me + 2 - 4 * self.y

    @staticmethod
    def scratch(n):
        dma, planes = pltpu.SemaphoreType.DMA, n // 4
        shapes = [(planes, 2, 2)] * 2 + [(planes, 2)] * 2 + [(2 * planes,)] * 2
        return [dma(shape) for shape in shapes]

    @property
    def events(self):
        return self.planes

    def plane(self, step):
        return lax.rem(self.z + step, self.planes)

    def place(self, plane, lane):
        return plane * 4 + self.y * 2 + lane

    def reached(self):
        return [(step, far) for step in range(self.planes) for far in (0, 1) if step or far]

    def hello(self):
        barrier = pltpu.get_barrier_semaphore()
        partners = [(self.across, self.core), (self.me, 1 - self.core)]
        for step, far in self.reached():
            lane = 1 - self.x if far else self.x
            partners.append((self.place(self.plane(step), lane), self.core))
        for seq, tp in partners:
            pl.semaphore_signal(barrier, inc=1, device_id=(seq, tp), device_id_type=MESH)

    def met(self):
        pl.semaphore_wait(pltpu.get_barrier_semaphore(), 2 + len(self.reached()))

    def rows_of(self, side, seq):
        return self.buffer.at[side, at(seq * self.rows, self.rows), :]

    def block(self, side, pair):
        return self.buffer.at[side, at(pair * 2 * self.rows, 2 * self.rows), :]

    def items(self, pair):
        found = [self.block(self.core, pair)]
        if self.lives is not None:
            found.append(self.lives.at[at(pair * 2, 2)])
        return found

    def each(self, copy, what):
        for index in range(1 if self.lives is None else 2):
            getattr(copy(index), what)()

    def z_copy(self, step, far):
        def copy(index):
            lane = 1 - self.x if far else self.x
            if index == 0:
                source = self.other.at[self.core] if far else self.rows_of(self.core, self.me)
                target = self.rows_of(self.core, self.me)
            else:
                source = self.live_other if far else self.lives.at[self.me]
                target = self.lives.at[self.me]
            return remote(
                source,
                target,
                self.z_send.at[step, far, index],
                self.z_recv.at[step, far, index],
                self.place(self.plane(step), lane),
                self.core,
            )

        return copy

    def y_copy(self, plane, row):
        def copy(index):
            item = self.items(plane * 2 + row)[index]
            return remote(
                item,
                item,
                self.y_send.at[plane, index],
                self.y_recv.at[plane, index],
                self.across,
                self.core,
            )

        return copy

    def c_copy(self, pair, side):
        item = self.block(side, pair)
        return remote(
            item, item, self.c_send.at[pair], self.c_recv.at[pair], self.me, 1 - self.core
        )

    def begin(self):
        for step, far in self.reached():
            self.each(self.z_copy(step, far), "start")

    def arrive(self, event):
        for far in (0, 1) if event else (1,):
            self.each(self.z_copy(event, far), "wait_recv")
        plane = self.plane(self.planes - event)
        self.each(self.y_copy(plane, self.y), "start")
        self.c_copy(plane * 2 + self.y, self.core).start()

    def complete(self, event):
        plane = self.plane(self.planes - event)
        self.each(self.y_copy(plane, 1 - self.y), "wait_recv")
        self.c_copy(plane * 2 + 1 - self.y, self.core).start()

    def ready(self, event):
        plane = self.plane(self.planes - event)
        self.c_copy(plane * 2, 1 - self.core).wait_recv()
        self.c_copy(plane * 2 + 1, 1 - self.core).wait_recv()
        return plane

    def finish(self):
        for step, far in self.reached():
            self.each(self.z_copy(step, far), "wait_send")
        for plane in range(self.planes):
            self.each(self.y_copy(plane, self.y), "wait_send")
        for pair in range(2 * self.planes):
            self.c_copy(pair, self.core).wait_send()


def split_lanes(values, x, buffer, other, start, rows):
    half = values.shape[2] // 2
    zero, one = values[:, 0, :], values[:, 1, :]
    own, far = jnp.where(x == 0, zero, one), jnp.where(x == 0, one, zero)
    core = lax.axis_index("tp")
    own = jnp.where(core == 0, own[:, :half], own[:, half:]).astype(BF16)
    buffer[core, at(start, rows), :] = own
    for side in range(2):
        other[side] = far[:, side * half : (side + 1) * half].astype(BF16)


def gather_and_project(tokens, live, episode_frames, gain, shift, qkv, bias, fixed, ahead, n):
    rows, lanes, width = tokens.shape
    half = width // 2
    total = n * rows
    chunks = total // FRAME
    per_frame = FRAME // rows
    features = qkv.shape[3]
    slots = episode_frames.shape[1]

    def kernel(*refs):
        refs = list(refs)

        def take(count):
            taken = refs[:count]
            del refs[:count]
            return taken

        tokens_ref, live_ref, counts_ref, gain_ref, shift_ref, w_any, bias_ref = take(7)
        fixed_ref, ahead_ref = take(2)
        all_ref, mask_ref, frames_ref = take(3)
        qkv_ref, *projected = take(4)
        other, lives, live_other, weight, full, w_sem = take(6)
        relay = Relay(n, rows, all_ref, other, take(Relay.sems), lives, live_other)
        load = pltpu.make_async_copy(w_any.at[0], weight, w_sem)
        load.start()
        relay.hello()
        x, me = relay.x, relay.me
        split_lanes(tokens_ref[...].astype(F32), x, all_ref, other, me * rows, rows)
        lane = lax.broadcasted_iota(jnp.int32, (1, FRAME), 1)
        here = lane // rows == lax.rem(me, per_frame)
        tiles = []
        for index in range(lanes):
            alive = live_ref[index : index + 1, :].astype(F32)
            alive = jnp.where(here, jnp.concatenate([alive] * per_frame, axis=1), 0.0)
            tiles.append(jnp.broadcast_to(alive, (8, FRAME)))
        lives[me] = jnp.where(x == 0, tiles[0], tiles[1])
        live_other[...] = jnp.where(x == 0, tiles[1], tiles[0])
        relay.met()
        relay.begin()

        counts = [counts_ref[x, slot] for slot in range(slots)]
        episodes, openings = [], []
        for frame in range(chunks):
            end, episode, opening = 0, 0, 0
            for slot in range(slots):
                end = end + counts[slot]
                passed = frame >= end
                episode = episode + passed.astype(jnp.int32)
                opening = opening + jnp.where(passed, counts[slot], 0)
            episodes.append(episode)
            openings.append(frame - opening)
        for index in range(3):
            table = []
            for frame in range(chunks):
                line = jnp.zeros((1, PAIR), F32)
                for choice in range(chunks):
                    line = jnp.where(
                        openings[frame] == choice, ahead_ref[index, choice : choice + 1, :], line
                    )
                table.append(line)
            frames_ref[index] = jnp.concatenate(
                table + [jnp.zeros((8 - chunks, PAIR), F32)], axis=0
            )
        load.wait()

        def project_frame(frame):
            place = at(frame * FRAME, FRAME)
            stream = jnp.concatenate([all_ref[0, place, :], all_ref[1, place, :]], axis=1)
            project(
                stream.astype(F32),
                frame,
                0,
                me // 2,
                (gain_ref, shift_ref, weight, bias_ref, fixed_ref, frames_ref),
                [qkv_ref.at[:, place, :]] + [ref.at[place, :] for ref in projected],
                full,
                straight=True,
            )

        for event in range(relay.events):
            relay.arrive(event)
            if event:
                relay.complete(event - 1)
            if event > 1:
                project_frame(relay.ready(event - 2))
        relay.complete(relay.events - 1)
        for event in range(max(0, relay.events - 2), relay.events):
            project_frame(relay.ready(event))
        relay.finish()

        for key_frame in range(chunks):
            alive = lives[key_frame * per_frame, 0:1, :]
            for part in range(1, per_frame):
                alive = alive + lives[key_frame * per_frame + part, 0:1, :]
            closed = (alive - 1.0) * -MASKED
            lines = []
            for query_frame in range(chunks):
                allowed = (episodes[query_frame] == episodes[key_frame]) & (
                    openings[key_frame] <= openings[query_frame]
                )
                lines.append(jnp.where(allowed, closed, MASKED))
            lines.append(jnp.zeros((PAIR - chunks, FRAME), F32))
            mask_ref[key_frame * FRAME : (key_frame + 1) * FRAME, :] = jnp.concatenate(
                lines, axis=0
            ).T.astype(BF16)

    in_vmem = pl.BlockSpec(memory_space=pltpu.VMEM)
    in_smem = pl.BlockSpec(memory_space=pltpu.SMEM)
    return pl.pallas_call(
        kernel,
        out_shape=(
            jax.ShapeDtypeStruct((2, total, half), BF16),
            jax.ShapeDtypeStruct((total, PAIR), BF16),
            jax.ShapeDtypeStruct((3, 8, PAIR), F32),
            jax.ShapeDtypeStruct((3, total, features), BF16),
            jax.ShapeDtypeStruct((total, PAIR), BF16),
            jax.ShapeDtypeStruct((total, width), BF16),
            jax.ShapeDtypeStruct((total, PAIR), F32),
        ),
        in_specs=[in_vmem, in_vmem, in_smem, in_vmem, in_vmem, ANYWHERE] + [in_vmem] * 3,
        out_specs=(in_vmem,) * 7,
        scratch_shapes=[
            pltpu.VMEM((2, rows, half), BF16),
            pltpu.VMEM((n, 8, FRAME), F32),
            pltpu.VMEM((8, FRAME), F32),
            pltpu.VMEM(qkv.shape[1:], BF16),
            pltpu.VMEM((FRAME, width), BF16),
            pltpu.SemaphoreType.DMA,
        ]
        + Relay.scratch(n),
        compiler_params=pltpu.CompilerParams(
            collective_id=0, has_side_effects=True, vmem_limit_bytes=VMEM_BYTES
        ),
        name="gather_and_project",
    )(tokens, live, episode_frames, gain, shift, qkv, bias, fixed, ahead)


def halves(ref):
    return jnp.concatenate([ref[0], ref[1]], axis=1).astype(F32)


def halves_spec(shape, chunks, behind, span=FRAME):
    return pl.BlockSpec(
        (2, span, shape[2]), lambda s: (0, jnp.clip(s - behind, 0, chunks - 1), 0)
    )


def layer_forward(layer, turned, key_bias, stream, mats, rows_of, next_refs, d_out, n, identity):
    _, total, features = turned.shape
    split = stream.ndim == 3
    width = mats[1].shape[1]
    rows_here = total // n
    hidden_units = mats[1].shape[2]
    chunks = total // FRAME
    heads = features // HEAD_DIM
    slabs = features // PAIR
    columns = 256
    last = next_refs is None
    b_out, gain, shift, b_up, b_down = rows_of
    mat_out, mat_up, mat_down = mats

    def kernel(*refs):
        refs = list(refs)

        def take(count):
            taken = refs[:count]
            del refs[:count]
            return taken

        q_ref, k_ref, v_ref, kb_ref, x_ref = take(5)
        wo_any, wu_any, wd_any = take(3)
        bo_ref, gain_ref, shift_ref, bu_ref, bd_ref = take(5)
        if not last:
            wq_any, ngain, nshift, nbias, fixed, frames = take(6)
        if d_out is not None:
            (d_ref,) = take(1)
        p_ref, r_ref, mixed_ref, unit_ref, scale_ref, second_ref, act_ref, gp_ref, x_out = take(9)
        if not last:
            next_outs = take(4)
        if d_out is not None:
            (d_all,) = take(1)
        wo, wu, wd, mid, full, next_full = take(6)
        if not last:
            (wq,) = take(1)
        a_send, a_recv, b_send, b_recv, w_sem, send_sem, recv_sem = take(7)
        relay = None
        if d_out is not None:
            buffer, other, d_sem = take(3)
            relay = Relay(n, rows_here, buffer, other, take(Relay.sems))

        step = pl.program_id(0)
        me, core = lax.axis_index("seq"), lax.axis_index("tp")

        items = [(wo_any, wo), (wu_any, wu), (wd_any, wd)]
        if not last:
            items.append((wq_any, wq))

        def load(index):
            source, target = items[index]
            return pltpu.make_async_copy(
                source.at[layer if index < 3 else layer + 1], target, w_sem.at[index]
            )

        def exchange(kind, chunk):
            source, target = ((a_send, a_recv), (b_send, b_recv))[kind]
            return remote(
                source.at[chunk],
                target.at[chunk],
                send_sem.at[kind, chunk],
                recv_sem.at[kind, chunk],
                me,
                1 - core,
            )

        @pl.when(step == 0)
        def _():
            for index in range(len(items)):
                load(index).start()
            if relay is None:
                hello([(me, 1 - core)])
            else:
                relay.hello()
                split_lanes(d_ref[...], relay.x, buffer, other, me * rows_here, rows_here)

        lane = lax.broadcasted_iota(jnp.int32, (1, PAIR), 1)
        sides = [(lane < HEAD_DIM).astype(F32).astype(BF16), (lane >= HEAD_DIM).astype(F32).astype(BF16)]
        for frame in range(chunks):

            @pl.when(step == frame)
            def _():
                keys = FRAME * (frame + 1)
                mask = kb_ref[:keys, :]
                asked = jnp.broadcast_to((lane == frame).astype(F32), (FRAME, PAIR)).astype(BF16)

                def two_slabs(couple):
                    def lanes_of(head):
                        return at((couple * 2 + head // 2) * PAIR, PAIR)

                    def score(head):
                        key = jnp.concatenate([k_ref[0, :keys, lanes_of(head)], mask], axis=1)
                        ask = q_ref[0, :, lanes_of(head)] * sides[head % 2]
                        return nt(jnp.concatenate([ask, asked], axis=1), key)

                    scores, sums = score(0), []
                    for head in range(4):
                        lanes, side = lanes_of(head), head % 2
                        following = score(head + 1) if head < 3 else None
                        highest = jnp.max(scores, axis=1, keepdims=True)
                        shifted = jnp.exp(scores - highest).astype(BF16)
                        p_ref[0, couple * 4 + head, :keys, :] = shifted.T
                        sums.append(nn(shifted, v_ref[0, :keys, lanes] * sides[side] + sides[1 - side]))
                        scores = following
                        if side == 1:
                            one, two = sums[head - 1 :]
                            low_side = lane < HEAD_DIM
                            divisor = 1.0 / jnp.where(
                                low_side, pltpu.roll(one, HEAD_DIM, 1), pltpu.roll(two, HEAD_DIM, 1)
                            )
                            r_ref[:, lanes] = divisor
                            mixed_ref[:, lanes] = (jnp.where(low_side, one, two) * divisor).astype(BF16)

                repeat(slabs // 2, two_slabs)

        @pl.when(step == 0)
        def _():
            load(0).wait()
            if relay is None:
                met([(me, 1 - core)])
            else:
                relay.met()
                relay.begin()

        @pl.when(step < chunks)
        def _():
            a_send[step] = nn(mixed_ref[...], wo[...]).astype(BF16)
            exchange(0, step).start()

        if relay is not None:
            for event in range(relay.events):

                @pl.when(step == 2 + event // 2)
                def _():
                    relay.arrive(event)

                @pl.when(step == 3 + event // 2)
                def _():
                    relay.complete(event)

            @pl.when(step == chunks + 1)
            def _():
                for event in range(relay.events):
                    relay.ready(event)
                relay.finish()
                pltpu.make_async_copy(buffer, d_all, d_sem).start()

        def feed_forward():
            chunk = step - 1
            middle = (halves(x_ref) if split else x_ref[...]) + (
                a_send[chunk].astype(F32) + a_recv[chunk].astype(F32)
            )
            middle = middle + bo_ref[layer : layer + 1, :]
            mid[lax.rem(chunk, 2)] = middle
            unit, scale = normed(middle)
            keep_norm(unit, scale, unit_ref, scale_ref)
            second = (unit * gain_ref[layer : layer + 1, :] + shift_ref[layer : layer + 1, :]).astype(BF16)
            full[...] = second
            second_ref[...] = full[:, at((me // 2) * PAIR, PAIR)]
            parts = [slice(start, start + columns) for start in range(0, hidden_units, columns)]
            hidden = nn(second, wu[:, parts[0]])
            for index, part in enumerate(parts):
                following = nn(second, wu[:, parts[index + 1]]) if index + 1 < len(parts) else None
                act, slope = gelu_both(hidden + bu_ref[layer : layer + 1, part])
                act_ref[:, part] = act.astype(BF16)
                gp_ref[:, part] = slope.astype(BF16)
                hidden = following
            b_send[chunk] = nn(act_ref[...], wd[...]).astype(BF16)

        def close():
            chunk = step - 2
            result = mid[lax.rem(chunk, 2)] + (b_send[chunk].astype(F32) + b_recv[chunk].astype(F32))
            result = result + bd_ref[layer : layer + 1, :]
            x_out[...] = result
            if not last:
                project(
                    result,
                    chunk,
                    layer + 1,
                    me // 2,
                    (ngain, nshift, wq, nbias, fixed, frames),
                    next_outs,
                    next_full,
                )

        @pl.when(step == 1)
        def _():
            load(1).wait()
            load(2).wait()

        @pl.when((step >= 1) & (step <= chunks))
        def _():
            exchange(0, step - 1).wait_recv()
            feed_forward()
            exchange(1, step - 1).start()

        if not last:

            @pl.when(step == 2)
            def _():
                load(3).wait()

        @pl.when(step >= 2)
        def _():
            exchange(1, step - 2).wait_recv()
            close()

        @pl.when(step == chunks + 1)
        def _():
            for kind in range(2):
                for chunk in range(chunks):
                    exchange(kind, chunk).wait_send()
            if relay is not None:
                pltpu.make_async_copy(buffer, d_all, d_sem).wait()

    def rows(columns, behind):
        return pl.BlockSpec(
            (FRAME, columns), lambda s: (jnp.clip(s - behind, 0, chunks - 1), 0)
        )

    def part_of(part):
        return pl.BlockSpec(
            (1, total, features), lambda s: (part, 0, 0), pipeline_mode=pl.Buffered(1)
        )

    in_specs = [
        pl.BlockSpec((1, FRAME, features), lambda s: (0, jnp.minimum(s, chunks - 1), 0)),
        part_of(1),
        part_of(2),
        whole(key_bias),
    ]
    in_specs += [halves_spec(stream.shape, chunks, 1) if split else rows(width, 1)]
    in_specs += [ANYWHERE] * 3 + [whole(item) for item in rows_of]
    operands = [turned, turned, turned, key_bias, stream, *mats, *rows_of]
    if not last:
        in_specs += [ANYWHERE] + [whole(item) for item in next_refs[1:]]
        operands += list(next_refs)
    if d_out is not None:
        in_specs += [whole(d_out)]
        operands += [d_out]
    out_shape = [
        jax.ShapeDtypeStruct((chunks, heads, total, FRAME), BF16),
        jax.ShapeDtypeStruct((total, features), F32),
        jax.ShapeDtypeStruct((total, features), BF16),
        jax.ShapeDtypeStruct((total, width), BF16),
        jax.ShapeDtypeStruct((total, PAIR), F32),
        jax.ShapeDtypeStruct((total, PAIR), BF16),
        jax.ShapeDtypeStruct((total, hidden_units), BF16),
        jax.ShapeDtypeStruct((total, hidden_units), BF16),
        jax.ShapeDtypeStruct((total, width), F32),
    ]
    out_specs = [
        pl.BlockSpec((1, heads, total, FRAME), lambda s: (jnp.minimum(s, chunks - 1), 0, 0, 0)),
        rows(features, 0),
        rows(features, 0),
        rows(width, 1),
        rows(PAIR, 1),
        rows(PAIR, 1),
        rows(hidden_units, 1),
        rows(hidden_units, 1),
        rows(width, 2),
    ]
    scratch = [
        pltpu.VMEM(mat_out.shape[1:], BF16),
        pltpu.VMEM(mat_up.shape[1:], BF16),
        pltpu.VMEM(mat_down.shape[1:], BF16),
        pltpu.VMEM((2, FRAME, width), F32),
        pltpu.VMEM((FRAME, width), BF16),
        pltpu.VMEM((FRAME, width), BF16),
    ]
    if not last:
        out_shape += [jax.ShapeDtypeStruct((3, total, features), BF16)]
        out_shape += [jax.ShapeDtypeStruct((total, PAIR), BF16)]
        out_shape += [jax.ShapeDtypeStruct((total, width), BF16)]
        out_shape += [jax.ShapeDtypeStruct((total, PAIR), F32)]
        out_specs += [
            pl.BlockSpec((3, FRAME, features), lambda s: (0, jnp.clip(s - 2, 0, chunks - 1), 0))
        ]
        out_specs += [rows(PAIR, 2), rows(width, 2), rows(PAIR, 2)]
    if d_out is not None:
        out_shape += [jax.ShapeDtypeStruct((2, total, width // 2), BF16)]
        out_specs += [ANYWHERE]
        scratch += [pltpu.VMEM(next_refs[0].shape[1:], BF16)]
    scratch += [pltpu.VMEM((chunks, FRAME, width), BF16)] * 4
    scratch += [
        pltpu.SemaphoreType.DMA((4,)),
        pltpu.SemaphoreType.DMA((2, chunks)),
        pltpu.SemaphoreType.DMA((2, chunks)),
    ]
    if d_out is not None:
        scratch += [
            pltpu.VMEM((2, total, width // 2), BF16),
            pltpu.VMEM((2, rows_here, width // 2), BF16),
            pltpu.SemaphoreType.DMA,
        ]
        scratch += Relay.scratch(n)
    return pl.pallas_call(
        kernel,
        grid=(chunks + 2,),
        out_shape=out_shape,
        in_specs=in_specs,
        out_specs=out_specs,
        scratch_shapes=scratch,
        compiler_params=pltpu.CompilerParams(
            collective_id=identity, has_side_effects=True, vmem_limit_bytes=VMEM_BYTES
        ),
        name=f"layer_forward_{layer}",
    )(*operands)


class Swap:
    def __init__(self, ships, lane_rows):
        self.ships, self.lane_rows = ships, lane_rows
        self.count = len(ships) + len(lane_rows)

    def operands(self):
        return [*self.ships, *[item for item, _ in self.lane_rows]]

    def in_specs(self):
        return [whole(item) for item in self.ships] + [ANYWHERE] * len(self.lane_rows)

    def outputs(self):
        shapes, specs = [], []
        for item in self.ships:
            shape = (item.shape[0] // 2, item.shape[1])
            shapes.append(jax.ShapeDtypeStruct(shape, F32))
            specs.append(whole_out(shape))
        for item, count in self.lane_rows:
            shapes.append(jax.ShapeDtypeStruct((count or item.shape[0], item.shape[1]), item.dtype))
            specs.append(ANYWHERE)
        return shapes, specs

    def scratch(self):
        if not self.count:
            return []
        buffers = [pltpu.VMEM((item.shape[0] // 2, item.shape[1]), BF16) for item in self.ships]
        return buffers * 2 + [pltpu.SemaphoreType.DMA((self.count,))] * 2

    def bind(self, sources, targets, scratch):
        ships = len(self.ships)
        me, core = lax.axis_index("seq"), lax.axis_index("tp")
        x = lax.rem(me, 2)
        beside = me + 1 - 2 * x
        half = PAIR // 2

        def copy(index):
            if index < ships:
                source, target = scratch[index], scratch[ships + index]
            else:
                source, target = sources[index], targets[index]
                count = self.lane_rows[index - ships][1]
                if count:
                    source = source.at[at(beside * count, count), :]
            send, recv = scratch[2 * ships].at[index], scratch[2 * ships + 1].at[index]
            return remote(source, target, send, recv, beside, core)

        def start():
            for index in range(self.count):
                if index < ships:
                    scratch[index][...] = sources[index][at((1 - x) * half, half), :].astype(BF16)
                copy(index).start()

        def finish():
            for index in range(self.count):
                copy(index).wait_recv()
                if index < ships:
                    own = sources[index][at(x * half, half), :]
                    targets[index][...] = own + scratch[ships + index][...].astype(F32)
            for index in range(self.count):
                copy(index).wait_send()

        return start, finish


def attention_backward(
    probs, divisor, mixed, turned_qkv, grad_mixed, first, fixed, frames, swap, swap_qkv, identity
):
    _, total, features = turned_qkv.shape
    chunks = total // FRAME
    slabs = features // PAIR
    half = PAIR // 2

    def kernel(*refs):
        refs = list(refs)

        def take(count):
            taken = refs[:count]
            del refs[:count]
            return taken

        p_ref, r_ref, o_ref, q_ref, k_ref, v_ref, g_ref, first_ref, fixed_ref, frames_ref = take(10)
        sources = take(swap.count)
        dq_ref, dk_ref, dv_ref, qkv_out = take(4)
        targets = take(swap.count)
        dk_sum, dv_sum, first_turned = take(3)
        if swap_qkv:
            qkv_own, qkv_send, qkv_recv, qkv_sems = take(4)
        start, finish = swap.bind(sources, targets, refs)

        step = pl.program_id(0)
        me, core = lax.axis_index("seq"), lax.axis_index("tp")
        x = lax.rem(me, 2)
        beside = me + 1 - 2 * x

        def qkv_copy(slab):
            return remote(
                qkv_send.at[slab],
                qkv_recv.at[slab],
                qkv_sems.at[0, slab],
                qkv_sems.at[1, slab],
                beside,
                core,
            )

        @pl.when(step == 0)
        def _():
            hello([(beside, core)])
            first_turned[...] = first_ref[...].T
            met([(beside, core)])
            start()

        lane = lax.broadcasted_iota(jnp.int32, (1, PAIR), 1)
        sides = [(lane < HEAD_DIM).astype(F32).astype(BF16), (lane >= HEAD_DIM).astype(F32).astype(BF16)]
        turned = k_ref[0].T
        ones = jnp.broadcast_to((lane < 2).astype(F32), (total, PAIR)).astype(BF16)
        values = jnp.concatenate([v_ref[0], ones], axis=1)

        def give(frame):
            keys = FRAME * (frame + 1)
            own = slice(frame * FRAME, keys)
            scaled = (g_ref[own, :].astype(F32) * r_ref[own, :]).astype(BF16)
            inner = scaled.astype(F32) * o_ref[own, :].astype(F32)
            grads, q_parts, g_parts = [], [], []
            for side in range(2):
                delta = jnp.sum(
                    jnp.where((lane < HEAD_DIM) == (side == 0), inner, 0.0), axis=1, keepdims=True
                )
                coarse = delta.astype(BF16).astype(F32)
                rest = jnp.where(lane == 0, -coarse, jnp.where(lane == 1, coarse - delta, 0.0))
                g2 = scaled * sides[side]
                grads.append(nt(values[:keys], jnp.concatenate([g2, rest.astype(BF16)], axis=1)))
                q_parts.append(q_ref[0, own, :] * sides[side])
                g_parts.append(g2)
            return grads, jnp.concatenate(q_parts, axis=0), jnp.concatenate(g_parts, axis=0)

        given = give(chunks - 1)
        for frame in reversed(range(chunks)):
            keys = FRAME * (frame + 1)
            own = slice(frame * FRAME, keys)
            tables = tables_of(fixed_ref, frames_ref, frame)
            grads, q_part, g_part = given
            given = give(frame - 1) if frame else None
            query_parts, score_parts, prob_parts = [], [], []
            for side in range(2):
                attention = p_ref[frame, side, :keys, :]
                grad_scores = (attention.astype(F32) * grads[side]).astype(BF16)
                query_parts.append(nn(turned[side * HEAD_DIM : (side + 1) * HEAD_DIM, :keys], grad_scores))
                score_parts.append(grad_scores)
                prob_parts.append(attention)
            grad_query = jnp.concatenate(query_parts, axis=0).T
            key_parts = nn(jnp.concatenate(score_parts, axis=1), q_part)
            value_parts = nn(jnp.concatenate(prob_parts, axis=1), g_part)
            dq_ref[own, :] = (turn(grad_query, tables, True) * SCORE_SCALE).astype(BF16)
            if frame == chunks - 1:
                dk_sum[...] = key_parts
                dv_sum[...] = value_parts
            else:
                dk_sum[:keys, :] += key_parts
                dv_sum[:keys, :] += value_parts
            dk_ref[own, :] = turn(dk_sum[own, :], tables, True).astype(BF16)
            dv_ref[own, :] = dv_sum[own, :].astype(BF16)

        for part, ref in enumerate((dq_ref, dk_ref, dv_ref)):
            piece = slice(part * PAIR, (part + 1) * PAIR)
            terms = nn(first_turned[...], ref[...])
            if swap_qkv:
                qkv_own[step, :, piece] = terms
                qkv_send[step, :, piece] = qkv_own[step, at((1 - x) * half, half), piece].astype(BF16)
            else:
                qkv_out[:, at(part * features + step * PAIR, PAIR)] = terms
        if swap_qkv:
            qkv_copy(step).start()

        @pl.when(step == slabs - 1)
        def _():
            finish()
            for slab in range(slabs if swap_qkv else 0):
                qkv_copy(slab).wait_recv()
                for part in range(3):
                    piece = slice(part * PAIR, (part + 1) * PAIR)
                    place = part * features + slab * PAIR
                    qkv_out[:, place : place + PAIR] = qkv_own[
                        slab, at(x * half, half), piece
                    ] + qkv_recv[slab, :, piece].astype(F32)
            for slab in range(slabs if swap_qkv else 0):
                qkv_copy(slab).wait_send()

    slab = pl.BlockSpec((total, PAIR), lambda s: (0, s))
    in_specs = [pl.BlockSpec((chunks, 2, total, FRAME), lambda s: (0, s, 0, 0))]
    in_specs += [slab] * 2
    for part in range(3):
        in_specs.append(pl.BlockSpec((1, total, PAIR), lambda s, part=part: (part, 0, s)))
    in_specs += [slab] + [whole(first), whole(fixed), whole(frames)]
    in_specs += swap.in_specs()
    qkv_shape = (half if swap_qkv else PAIR, 3 * features)
    shapes, specs = swap.outputs()
    out_shape = [jax.ShapeDtypeStruct((total, features), BF16)] * 3
    out_shape += [jax.ShapeDtypeStruct(qkv_shape, F32)] + shapes
    out_specs = [slab] * 3 + [whole_out(qkv_shape)] + specs
    scratch = [pltpu.VMEM((total, PAIR), F32)] * 2 + [pltpu.VMEM((PAIR, total), BF16)]
    if swap_qkv:
        scratch += [pltpu.VMEM((slabs, PAIR, 3 * PAIR), F32)]
        scratch += [pltpu.VMEM((slabs, half, 3 * PAIR), BF16)] * 2
        scratch += [pltpu.SemaphoreType.DMA((2, slabs))]
    scratch += swap.scratch()
    return pl.pallas_call(
        kernel,
        grid=(slabs,),
        out_shape=out_shape,
        in_specs=in_specs,
        out_specs=out_specs,
        scratch_shapes=scratch,
        compiler_params=pltpu.CompilerParams(
            collective_id=identity, has_side_effects=True, vmem_limit_bytes=VMEM_BYTES
        ),
        name=f"attention_backward_{identity}",
    )(
        probs,
        divisor,
        mixed,
        turned_qkv,
        turned_qkv,
        turned_qkv,
        grad_mixed,
        first,
        fixed,
        frames,
        *swap.operands(),
    )


def rows_backward(entry, upper, identity, span, swap):
    top, bottom = len(entry) == 1, upper is None
    if not top:
        above, entry = entry[0], entry[1:]
    total = entry[0].shape[1] if top else entry[0].shape[0]
    chunks = total // span
    columns = 256
    ahead = 0 if top else 2 if bottom else 1
    if top:
        width = 2 * entry[0].shape[2]
    else:
        features, width = entry[0].shape[1], entry[5].shape[1]
    if not bottom:
        layer = upper[0]
        hidden_units, mixed_features = upper[1].shape[1], upper[6].shape[1]
    place_rows = total // lax.axis_size("seq")

    def kernel(*refs):
        refs = list(refs)

        def take(count):
            taken = refs[:count]
            del refs[:count]
            return taken

        if top:
            (d_out_ref,) = take(1)
        else:
            dq_ref, dk_ref, dv_ref, unit1, scale1, dm_ref, wq, gain1 = take(8)
        if not bottom:
            act_ref, gp_ref, unit2, scale2, second_ref, mixed_ref = take(6)
            wo_any, wu_any, wd_any, gain2 = take(4)
        sources = take(swap.count)
        if not top:
            (vec1,) = take(1)
        if not bottom:
            dmid_out, dmix_out, out_sum, up_sum, down_sum, vec2 = take(6)
        else:
            dx_out, dx_other, vec_other = take(3)
        targets = take(swap.count)
        if not top:
            a_send, a_recv = take(2)
        if not bottom:
            b_send, b_recv, grad_keep, hidden_keep, low_keep, last_keep, wo, wu, wd, w_sem = take(10)
        else:
            dx_keep, dx_send, dx_recv, vec_recv, x_send_sem, x_recv_sem = take(6)
        send_sem, recv_sem = take(2)
        start_swap, finish_swap = swap.bind(sources, targets, refs)

        step = pl.program_id(0)
        me, core = lax.axis_index("seq"), lax.axis_index("tp")
        pair = at((me // 2) * PAIR, PAIR)
        x = lax.rem(me, 2)
        beside = me + 1 - 2 * x

        def exchange(kind, chunk):
            source, target = (a_send, a_recv) if kind == 0 else (b_send, b_recv)
            return remote(
                source.at[chunk],
                target.at[chunk],
                send_sem.at[kind, chunk],
                recv_sem.at[kind, chunk],
                me,
                1 - core,
            )

        def load(index):
            source, target = ((wd_any, wd), (wu_any, wu), (wo_any, wo))[index]
            return pltpu.make_async_copy(source.at[layer], target, w_sem.at[index])

        partners = [(me, 1 - core)] + ([(beside, core)] if bottom or swap.count else [])

        @pl.when(step == 0)
        def _():
            if not bottom:
                for index in range(3):
                    load(index).start()
                out_sum[...] = jnp.zeros_like(out_sum)
                up_sum[...] = jnp.zeros_like(up_sum)
                down_sum[...] = jnp.zeros_like(down_sum)
                vec2[...] = jnp.zeros_like(vec2)
            if not top:
                vec1[...] = jnp.zeros_like(vec1)
            hello(partners)

        def meet():
            @pl.when(step == 0)
            def _():
                met(partners)
                start_swap()

        def entry_products():
            partial = None
            for part, ref in enumerate((dq_ref, dk_ref, dv_ref)):
                grad = ref[...]
                term = nt(grad, wq[0, part])
                partial = term if partial is None else partial + term
                vec1[part : part + 1, :] += column_sum(grad.astype(F32))
            a_send[step] = partial.astype(BF16)

        def entry_norm(chunk):
            if top:
                return halves(d_out_ref)
            grad_first = a_send[chunk].astype(F32) + a_recv[chunk].astype(F32)
            unit, scale = kept_norm(unit1, scale1)
            for start, sums in ((3, column_sum(grad_first * unit)), (5, column_sum(grad_first))):
                for side in range(width // features):
                    piece = slice(side * features, (side + 1) * features)
                    vec1[start + side : start + side + 1, :] += sums[:, piece]
            return dm_ref[...] + norm_pull(grad_first, gain1[above : above + 1, :], unit, scale)

        def feed_forward(between=None):
            chunk = step - ahead
            gradient = entry_norm(chunk)
            if bottom:
                dx_keep[at(chunk * span, span), :] = gradient
                return
            grad_keep[lax.rem(chunk, 2)] = gradient
            vec2[1:2, :width] += column_sum(gradient)
            low = gradient.astype(BF16)
            low_keep[...] = low
            low_columns = low_keep[:, pair]
            second = second_ref[...]
            parts = [slice(start, start + columns) for start in range(0, hidden_units, columns)]
            grad_act = nt(low, wd[parts[0], :])
            for index, part in enumerate(parts):
                following = nt(low, wd[parts[index + 1], :]) if index + 1 < len(parts) else None
                grad_hidden = grad_act * gp_ref[:, part].astype(F32)
                hidden_keep[:, part] = grad_hidden.astype(BF16)
                vec2[0:1, part] += column_sum(grad_hidden)
                grad_act = following
            if between is not None:
                between()
            b_send[chunk] = nt(hidden_keep[...], wu[...]).astype(BF16)
            down_sum[...] += tn(low_columns, act_ref[...])
            up_sum[...] += tn(second, hidden_keep[...])

        def close():
            chunk = step - ahead - 1
            grad_second = b_send[chunk].astype(F32) + b_recv[chunk].astype(F32)
            unit, scale = kept_norm(unit2, scale2)
            vec2[2:3, :width] += column_sum(grad_second * unit)
            vec2[3:4, :width] += column_sum(grad_second)
            grad_middle = grad_keep[lax.rem(chunk, 2)] + norm_pull(
                grad_second, gain2[layer : layer + 1, :], unit, scale
            )
            dmid_out[...] = grad_middle
            vec2[4:5, :width] += column_sum(grad_middle)
            low = grad_middle.astype(BF16)
            last_keep[...] = low
            out_sum[...] += tn(last_keep[:, pair], mixed_ref[...])
            dmix_out[...] = nt(low, wo[...]).astype(BF16)

        if not top:

            @pl.when(step < chunks)
            def _():
                entry_products()
                meet()
                exchange(0, step).start()

        @pl.when((step >= ahead) & (step < chunks + ahead))
        def _():
            if not top:
                exchange(0, step - ahead).wait_recv()
            if not bottom:

                @pl.when(step == ahead)
                def _():
                    load(0).wait()

            feed_forward(lambda: pl.when(step == ahead)(lambda: load(1).wait()))
            if not bottom:
                if top:
                    meet()
                exchange(1, step - ahead).start()

        if not bottom:

            @pl.when(step == ahead + 1)
            def _():
                load(2).wait()

            @pl.when(step >= ahead + 1)
            def _():
                exchange(1, step - ahead - 1).wait_recv()
                close()

        if bottom:

            def x_copy(index):
                source, target = ((dx_send, dx_recv), (vec1, vec_recv))[index]
                return remote(
                    source, target, x_send_sem.at[index], x_recv_sem.at[index], beside, core
                )

            @pl.when(step == chunks + 1)
            def _():
                dx_send[...] = dx_keep[at(beside * place_rows, place_rows), :].astype(BF16)
                x_copy(0).start()
                x_copy(1).start()
                dx_out[...] = dx_keep[at(me * place_rows, place_rows), :]
                x_copy(0).wait_recv()
                x_copy(1).wait_recv()
                dx_other[...] = dx_recv[...].astype(F32)
                vec_other[...] = vec_recv[...]
                x_copy(0).wait_send()
                x_copy(1).wait_send()

        @pl.when(step == pl.num_programs(0) - 1)
        def _():
            for kind in ([] if top else [0]) + ([] if bottom else [1]):
                for chunk in range(chunks):
                    exchange(kind, chunk).wait_send()
            finish_swap()

    def rows(columns, behind):
        return pl.BlockSpec(
            (span, columns), lambda s: (jnp.clip(s - behind, 0, chunks - 1), 0)
        )

    vec = jax.ShapeDtypeStruct((8, VEC), F32)
    operands, in_specs, out_shape, out_specs, scratch = [], [], [], [], []
    if top:
        operands += list(entry)
        in_specs += [halves_spec(entry[0].shape, chunks, 0, span)]
    else:
        operands += list(entry)
        in_specs += [rows(features, 0)] * 3
        in_specs += [rows(width, ahead), rows(PAIR, ahead), rows(width, ahead)]
        in_specs += [
            pl.BlockSpec(
                (1, *entry[6].shape[1:]),
                lambda s: (above, 0, 0, 0),
                pipeline_mode=pl.Buffered(1),
            ),
            whole(entry[7]),
        ]
        narrow = jax.ShapeDtypeStruct((8, features), F32)
        out_shape += [narrow]
        out_specs += [whole_out((8, features))]
        scratch += [pltpu.VMEM((chunks, span, width), BF16)] * 2
    if not bottom:
        operands += list(upper[1:])
        in_specs += [rows(hidden_units, ahead)] * 2
        in_specs += [rows(width, ahead + 1), rows(PAIR, ahead + 1), rows(PAIR, ahead)]
        in_specs += [rows(mixed_features, ahead + 1)] + [ANYWHERE] * 3 + [whole(upper[10])]
        sums = [mixed_features, hidden_units, hidden_units]
        out_shape += [
            jax.ShapeDtypeStruct((total, width), F32),
            jax.ShapeDtypeStruct((total, mixed_features), BF16),
        ]
        out_shape += [jax.ShapeDtypeStruct((PAIR, size), F32) for size in sums] + [vec]
        out_specs += [rows(width, ahead + 1), rows(mixed_features, ahead + 1)]
        out_specs += [whole_out((PAIR, size)) for size in sums] + [whole_out((8, VEC))]
        scratch += [pltpu.VMEM((chunks, span, width), BF16)] * 2
        scratch += [
            pltpu.VMEM((2, span, width), F32),
            pltpu.VMEM((span, hidden_units), BF16),
            pltpu.VMEM((span, width), BF16),
            pltpu.VMEM((span, width), BF16),
            pltpu.VMEM(upper[7].shape[1:], BF16),
            pltpu.VMEM(upper[8].shape[1:], BF16),
            pltpu.VMEM(upper[9].shape[1:], BF16),
            pltpu.SemaphoreType.DMA((3,)),
        ]
    else:
        out_shape += [
            jax.ShapeDtypeStruct((place_rows, width), F32),
            jax.ShapeDtypeStruct((place_rows, width), F32),
            narrow,
        ]
        out_specs += [whole_out((place_rows, width))] * 2 + [whole_out((8, features))]
        scratch += [
            pltpu.VMEM((total, width), F32),
            pltpu.VMEM((place_rows, width), BF16),
            pltpu.VMEM((place_rows, width), BF16),
            pltpu.VMEM((8, features), F32),
            pltpu.SemaphoreType.DMA((2,)),
            pltpu.SemaphoreType.DMA((2,)),
        ]
    scratch += [pltpu.SemaphoreType.DMA((2, chunks))] * 2
    operands += swap.operands()
    in_specs += swap.in_specs()
    shapes, specs = swap.outputs()
    out_shape += shapes
    out_specs += specs
    scratch += swap.scratch()
    return pl.pallas_call(
        kernel,
        grid=(chunks + (1 if top else 2),),
        out_shape=out_shape,
        in_specs=in_specs,
        out_specs=out_specs,
        scratch_shapes=scratch,
        compiler_params=pltpu.CompilerParams(
            collective_id=identity, has_side_effects=True, vmem_limit_bytes=VMEM_BYTES
        ),
        name=f"rows_backward_{identity}",
    )(*operands)


def assemble(sums, vecs, lanes, n, features, hidden_units):
    place = lanes[1].shape[0]
    width = lanes[1].shape[1]
    half = PAIR // 2

    def kernel(*refs):
        refs = list(refs)

        def take(count):
            taken = refs[:count]
            del refs[:count]
            return taken

        qkvs, outs, ups, downs = take(LAYERS), take(LAYERS), take(LAYERS), take(LAYERS)
        vec_refs = [take(4) for _ in range(LAYERS)]
        out_lane, out_other, dx_own, dx_other = take(4)
        out_ref, dx_ref, gain1, shift1, g_qkv, b_qkv, g_out, b_out = take(8)
        gain2, shift2, g_up, b_up, g_down, b_down = take(6)
        out_own, sem = refs
        me = lax.axis_index("seq")
        x = lax.rem(me, 2)
        fetch = pltpu.make_async_copy(out_lane.at[at(me * place, place), :], out_own, sem)
        fetch.start()

        for layer in range(LAYERS):
            for part in range(3):
                g_qkv[layer, part] = qkvs[layer][:, part * features : (part + 1) * features]
            for ref, target in ((outs, g_out), (ups, g_up), (downs, g_down)):
                target[layer] = ref[layer][...]

        for layer, (entry_own, entry_other, upper_own, upper_other) in enumerate(vec_refs):
            line = slice(layer, layer + 1)
            for part in range(3):
                row = slice(part, part + 1)
                b_qkv[part, line, :] = entry_own[row, :] + entry_other[row, :]
            b_up[line, :] = upper_own[0:1, :hidden_units] + upper_other[0:1, :hidden_units]

            def owned(mine, other, row):
                wide = mine.shape[1]
                place = (me // 2) * PAIR
                pair = at(lax.rem(place, wide), PAIR)
                both = mine[row : row + 1, pair] + other[row : row + 1, pair]
                for later in range(1, width // wide):
                    line = slice(row + later, row + later + 1)
                    both = jnp.where(place // wide == later, mine[line, pair] + other[line, pair], both)
                return jnp.where(x == 0, both[:, :half], both[:, half:])

            gain1[line, :] = owned(entry_own, entry_other, 3)
            shift1[line, :] = owned(entry_own, entry_other, 5)
            b_down[line, :] = owned(upper_own, upper_other, 1)
            gain2[line, :] = owned(upper_own, upper_other, 2)
            shift2[line, :] = owned(upper_own, upper_other, 3)
            b_out[line, :] = owned(upper_own, upper_other, 4)

        def both_lanes(target, mine, other):
            target[:, 0, :] = jnp.where(x == 0, mine, other)
            target[:, 1, :] = jnp.where(x == 0, other, mine)

        both_lanes(dx_ref, dx_own[...], dx_other[...])
        fetch.wait()
        both_lanes(out_ref, out_own[...], out_other[...])

    def f32(*shape):
        return jax.ShapeDtypeStruct(shape, F32)

    in_vmem = pl.BlockSpec(memory_space=pltpu.VMEM)
    flat = []
    for kind in range(4):
        flat += [sums[layer][kind] for layer in range(LAYERS)]
    for layer in range(LAYERS):
        flat += list(vecs[layer])
    flat += list(lanes)
    small = f32(LAYERS, width // n)
    return pl.pallas_call(
        kernel,
        out_shape=(
            f32(place, 2, width),
            f32(place, 2, width),
            small,
            small,
            f32(LAYERS, 3, half, features),
            f32(3, LAYERS, features),
            f32(LAYERS, half, features),
            small,
            small,
            small,
            f32(LAYERS, half, hidden_units),
            f32(LAYERS, hidden_units),
            f32(LAYERS, half, hidden_units),
            small,
        ),
        in_specs=[in_vmem] * (len(flat) - 4) + [ANYWHERE] + [in_vmem] * 3,
        out_specs=(in_vmem,) * 14,
        scratch_shapes=[pltpu.VMEM((place, width), F32), pltpu.SemaphoreType.DMA],
        compiler_params=pltpu.CompilerParams(vmem_limit_bytes=VMEM_BYTES),
        name="assemble",
    )(*flat)


def per_chip(
    tokens,
    d_out,
    norm1_gain,
    norm1_shift,
    w_qkv,
    b_qkv,
    w_out,
    b_out,
    norm2_gain,
    norm2_shift,
    w_up,
    b_up,
    w_down,
    b_down,
    episode_frames,
    live,
):
    n = lax.axis_size("seq")
    rows = tokens.shape[0]
    features = w_qkv.shape[3]
    fixed, ahead = turn_constants(rows * n // FRAME)
    qkv, qkv_bias = w_qkv.transpose(0, 2, 1, 3), b_qkv.transpose(1, 0, 2)

    gathered, key_bias, frames, *projected = gather_and_project(
        tokens, live.T, episode_frames, norm1_gain, norm1_shift, qkv, qkv_bias, fixed, ahead, n
    )
    streams, kept, d_lane = [gathered], [], None
    for layer in range(LAYERS):
        following = None
        if layer + 1 < LAYERS:
            following = (qkv, norm1_gain, norm1_shift, qkv_bias, fixed, frames)
        results = layer_forward(
            layer,
            projected[0],
            key_bias,
            streams[layer],
            (w_out, w_up, w_down),
            (b_out, norm2_gain, norm2_shift, b_up, b_down),
            following,
            d_out if layer == 0 else None,
            n,
            1 + layer,
        )
        kept.append((*projected, *results[:8]))
        streams.append(results[8])
        if following is not None:
            projected = results[9:13]
        if layer == 0:
            d_lane = results[-1]

    sums = [[None] * 4 for _ in range(LAYERS)]
    vecs = [[None] * 4 for _ in range(LAYERS)]
    entry, later = (d_lane,), None
    for layer in reversed(range(LAYERS)):
        turned, first, unit1, scale1, probs, divisor, mixed = kept[layer][:7]
        unit2, scale2, second, act, slope = kept[layer][7:]
        upper = (
            layer,
            act,
            slope,
            unit2,
            scale2,
            second,
            mixed,
            w_out,
            w_up,
            w_down,
            norm2_gain,
        )
        identity = 1 + LAYERS + 2 * (LAYERS - 1 - layer)
        if later is None:
            results = rows_backward(entry, upper, identity, FRAME, Swap([], []))
        else:
            swap = Swap(later[:2], [(later[2], 0), (streams[LAYERS], rows)])
            vec1, *results = rows_backward(entry, upper, identity, FRAME, swap)
            results, swapped = results[:6], results[6:]
            sums[layer + 1][3], sums[layer + 1][0] = swapped[:2]
            vecs[layer + 1][3], out_other = swapped[2:]
            vecs[layer + 1][0] = vec1
        grad_middle, grad_mixed, out_sum, up_sum, down_sum, vec2 = results
        vecs[layer][2] = vec2
        last = layer == 0
        if last:
            swap = Swap([out_sum, up_sum, down_sum], [(vec2, 0), (vecs[layer + 1][0], 0)])
        else:
            swap = Swap([out_sum, up_sum], [])
        results = attention_backward(
            probs,
            divisor,
            mixed,
            turned,
            grad_mixed,
            first,
            fixed,
            frames,
            swap,
            False,
            identity + 1,
        )
        grad_query, grad_key, grad_value, qkv_sum = results[:4]
        if last:
            sums[layer][1:] = results[4:7]
            vecs[layer][3], vecs[layer + 1][1] = results[7:9]
        else:
            sums[layer][1:3] = results[4:6]
            later = [down_sum, qkv_sum, vec2]
        entry = (
            layer,
            grad_query,
            grad_key,
            grad_value,
            unit1,
            scale1,
            grad_middle,
            qkv,
            norm1_gain,
        )
    vec1, dx_own, dx_other, vec_other, sums[0][0] = rows_backward(
        entry, None, 1 + 3 * LAYERS, FRAME, Swap([qkv_sum], [])
    )
    vecs[0][:2] = [vec1, vec_other]
    results = list(
        assemble(
            sums,
            vecs,
            (streams[LAYERS], out_other, dx_own, dx_other),
            n,
            features,
            w_up.shape[2],
        )
    )
    results[4] = results[4].transpose(0, 2, 1, 3)
    results[5] = results[5].transpose(1, 0, 2)
    results[6] = results[6].transpose(0, 2, 1)
    results[12] = results[12].transpose(0, 2, 1)
    return tuple(results)


def lane_fits(mesh, tokens):
    n = mesh.shape["seq"]
    positions, lanes, width = tokens.shape
    rows = positions // n
    return (
        lanes == 2
        and n % 4 == 0
        and positions <= 4 * FRAME
        and positions % FRAME == 0
        and FRAME % rows == 0
        and width // n * 2 == PAIR
        and mesh.shape["tp"] == 2
    )


def solution(mesh):
    placed = (
        P("seq", None, None),
        P("seq", None, None),
        P(),
        P(),
        P(None, None, None, "tp"),
        P(None, None, "tp"),
        P(None, "tp", None),
        P(),
        P(),
        P(),
        P(None, None, "tp"),
        P(None, "tp"),
        P(None, "tp", None),
        P(),
        P(),
        P("seq", None),
    )
    def mapped(body):
        return jax.shard_map(
            body,
            mesh=mesh,
            in_specs=placed,
            out_specs=(
                P("seq", None, None),
                P("seq", None, None),
                P(None, "seq"),
                P(None, "seq"),
                P(None, "seq", None, "tp"),
                P(None, None, "tp"),
                P(None, "tp", "seq"),
                P(None, "seq"),
                P(None, "seq"),
                P(None, "seq"),
                P(None, "seq", "tp"),
                P(None, "tp"),
                P(None, "tp", "seq"),
                P(None, "seq"),
            ),
            check_vma=False,
        )

    def run(tokens, *others):
        if lane_fits(mesh, tokens):
            return mapped(per_chip)(tokens, *others)
        return mapped(per_device)(tokens, *others)

    return run
```

```python
import math

import jax
import jax.numpy as jnp
import numpy as np
from jax import lax
from jax.experimental import pallas as pl
from jax.experimental.pallas import tpu as pltpu
from jax.sharding import PartitionSpec as P

HEAD_DIM = 64
GRID = 16
FRAME = 256
LAYERS = 2
MICRO = 2


EPSILON = 1e-06
MASKED = -1e30
SCORE_SCALE = 0.125


def layer_norm(stream, norm_gain, norm_shift):
    center = stream - jnp.mean(stream, axis=-1, keepdims=True)
    spread = jnp.mean(center * center, axis=-1, keepdims=True)
    return center * lax.rsqrt(spread + EPSILON) * norm_gain + norm_shift


def rotate(values, frame_place, row_place, column_place):
    frequency = jnp.exp(jnp.arange(10, dtype=jnp.float32) * (-math.log(10000.0) / 10.0))
    pieces = []
    for section, place in enumerate((frame_place, row_place, column_place)):
        lower = values[..., 20 * section : 20 * section + 10]
        upper = values[..., 20 * section + 10 : 20 * section + 20]
        angles = place.astype(jnp.float32)[..., None, None] * frequency
        cosine = jnp.cos(angles)
        sine_part = jnp.sin(angles)
        pieces.append(lower * cosine - upper * sine_part)
        pieces.append(lower * sine_part + upper * cosine)
    pieces.append(values[..., 60:])
    return jnp.concatenate(pieces, axis=-1)


def episode_tags(frame_counts, positions):
    endings = jnp.cumsum(frame_counts) * FRAME
    passed = (positions[:, None] >= endings[None, :]).astype(jnp.int32)
    episode = jnp.sum(passed, axis=1)
    opening = jnp.sum(passed * frame_counts[None, :], axis=1)
    frame_index = positions // FRAME - opening
    within = positions % FRAME
    return (episode, frame_index, within // GRID, within % GRID)


def gelu_exact(values):
    return jax.nn.gelu(values, approximate=False)


def sum_heads(partial_sum):
    return lax.psum(partial_sum.astype(jnp.bfloat16), "tp").astype(jnp.float32)


def sum_inputs(partial_sum):
    return lax.psum(partial_sum.astype(jnp.bfloat16), "tp").astype(jnp.float32)


def lane_scores(query, keys_all, lane_index, query_tags, key_tags):
    head_count = query.shape[2] // HEAD_DIM
    query_lane = lax.dynamic_index_in_dim(query, lane_index, 1, False).reshape(
        query.shape[0], head_count, HEAD_DIM
    )
    keys_lane = lax.dynamic_index_in_dim(keys_all, lane_index, 1, False).reshape(
        keys_all.shape[0], head_count, HEAD_DIM
    )
    query_episode, query_frame = [
        lax.dynamic_index_in_dim(item, lane_index, 1, False) for item in query_tags
    ]
    key_episode, key_frame, key_live = [
        lax.dynamic_index_in_dim(item, lane_index, 1, False) for item in key_tags
    ]
    allowed = (
        (query_episode[:, None] == key_episode[None, :])
        & (key_frame[None, :] <= query_frame[:, None])
        & (key_live[None, :] > 0)
    )
    scores = (
        jnp.einsum("qhd,khd->hqk", query_lane, keys_lane, preferred_element_type=jnp.float32)
        * SCORE_SCALE
    )
    return (jnp.where(allowed[None], scores, MASKED), query_lane, keys_lane)


def attend_forward(query, keys_all, values_all, query_tags, key_tags):
    rows_dev, lane_count, features = query.shape
    head_count = features // HEAD_DIM

    def one_lane(lane_index, carry):
        scores, query_lane, keys_lane = lane_scores(
            query, keys_all, lane_index, query_tags, key_tags
        )
        highest = jnp.max(scores, axis=-1, keepdims=True)
        shifted = jnp.exp(scores - highest)
        summed = jnp.sum(shifted, axis=-1, keepdims=True)
        attention = (shifted / summed).astype(jnp.bfloat16)
        values_lane = lax.dynamic_index_in_dim(values_all, lane_index, 1, False).reshape(
            values_all.shape[0], head_count, HEAD_DIM
        )
        result = jnp.einsum(
            "hqk,khd->qhd", attention, values_lane, preferred_element_type=jnp.float32
        ).reshape(rows_dev, 1, features)
        log_total = (highest + jnp.log(summed))[None, :, :, 0]
        return (result, log_total)

    initial = (
        jnp.zeros((rows_dev, lane_count, features), jnp.float32),
        jnp.zeros((lane_count, head_count, rows_dev), jnp.float32),
    )
    return lax.fori_loop(0, lane_count, one_lane, initial)


def attend_backward(query, keys_all, values_all, log_total, grad_mixed, query_tags, key_tags):
    rows_dev, lane_count, features = query.shape
    head_count = features // HEAD_DIM
    key_rows = keys_all.shape[0]

    def one_lane(lane_index, carry):
        scores, query_lane, keys_lane = lane_scores(
            query, keys_all, lane_index, query_tags, key_tags
        )
        values_lane = lax.dynamic_index_in_dim(values_all, lane_index, 1, False).reshape(
            key_rows, head_count, HEAD_DIM
        )
        grad_lane = lax.dynamic_index_in_dim(grad_mixed, lane_index, 1, False).reshape(
            rows_dev, head_count, HEAD_DIM
        )
        attention = jnp.exp(
            scores - lax.dynamic_index_in_dim(log_total, lane_index, 0, False)[:, :, None]
        )
        grad_attention = jnp.einsum(
            "qhd,khd->hqk", grad_lane, values_lane, preferred_element_type=jnp.float32
        )
        inner = jnp.sum(attention * grad_attention, axis=-1, keepdims=True)
        grad_scores = (attention * (grad_attention - inner)).astype(jnp.bfloat16)
        query_part = (
            jnp.einsum("hqk,khd->qhd", grad_scores, keys_lane, preferred_element_type=jnp.float32)
            * SCORE_SCALE
        )
        key_part = (
            jnp.einsum("hqk,qhd->khd", grad_scores, query_lane, preferred_element_type=jnp.float32)
            * SCORE_SCALE
        )
        value_part = jnp.einsum(
            "hqk,qhd->khd",
            attention.astype(jnp.bfloat16),
            grad_lane,
            preferred_element_type=jnp.float32,
        )
        stacked = jnp.stack(
            [key_part.reshape(key_rows, features), value_part.reshape(key_rows, features)], axis=1
        )
        key_terms = stacked[:, None]
        grad_query = query_part.reshape(rows_dev, 1, features)
        return (grad_query, key_terms)

    initial = (
        jnp.zeros((rows_dev, lane_count, features), jnp.float32),
        jnp.zeros((key_rows, lane_count, 2, features), jnp.float32),
    )
    return lax.fori_loop(0, lane_count, one_lane, initial)


def front(stream, layer_index, params, query_tags, key_tags, positions):
    (
        gain_one,
        shift_one,
        mat_qkv,
        bias_qkv,
        mat_out,
        bias_out,
        gain_two,
        shift_two,
        mat_up,
        bias_up,
        mat_down,
        bias_down,
    ) = [item[layer_index] for item in params]
    rows_dev, lane_count, width = stream.shape
    features = mat_qkv.shape[2]
    head_count = features // HEAD_DIM
    frame_place, row_place, column_place = positions
    first = layer_norm(stream, gain_one, shift_one).astype(jnp.bfloat16)
    projected = (
        jnp.einsum("tbd,dcf->tbcf", first, mat_qkv, preferred_element_type=jnp.float32) + bias_qkv
    )
    split = projected.reshape(rows_dev, lane_count, 3, head_count, HEAD_DIM)
    query = (
        rotate(split[:, :, 0], frame_place, row_place, column_place)
        .reshape(rows_dev, lane_count, features)
        .astype(jnp.bfloat16)
    )
    keys = (
        rotate(split[:, :, 1], frame_place, row_place, column_place)
        .reshape(rows_dev, lane_count, features)
        .astype(jnp.bfloat16)
    )
    values = projected[:, :, 2].astype(jnp.bfloat16)
    keys_all, values_all = (
        lax.all_gather(keys, "seq", axis=0, tiled=True),
        lax.all_gather(values, "seq", axis=0, tiled=True),
    )
    mixed_full, log_total = attend_forward(query, keys_all, values_all, query_tags, key_tags)
    mixed = mixed_full.astype(jnp.bfloat16)
    middle = (
        stream
        + sum_heads(jnp.einsum("tbf,fd->tbd", mixed, mat_out, preferred_element_type=jnp.float32))
        + bias_out
    )
    second = layer_norm(middle, gain_two, shift_two).astype(jnp.bfloat16)
    hidden = jnp.einsum("tbd,df->tbf", second, mat_up, preferred_element_type=jnp.float32) + bias_up
    activation = gelu_exact(hidden).astype(jnp.bfloat16)
    return (
        first,
        query,
        keys_all,
        values_all,
        log_total,
        mixed,
        middle,
        second,
        hidden,
        activation,
        mixed_full,
    )


def layer_backward(stream, gradient, layer_index, params, query_tags, key_tags, positions):
    (
        gain_one,
        shift_one,
        mat_qkv,
        bias_qkv,
        mat_out,
        bias_out,
        gain_two,
        shift_two,
        mat_up,
        bias_up,
        mat_down,
        bias_down,
    ) = [item[layer_index] for item in params]
    (
        first,
        query,
        keys_all,
        values_all,
        log_total,
        mixed,
        middle,
        second,
        hidden,
        activation,
        mixed_full,
    ) = front(stream, layer_index, params, query_tags, key_tags, positions)
    frame_place, row_place, column_place = positions
    rows_dev, lane_count, width = stream.shape
    features = query.shape[2]
    head_count = features // HEAD_DIM
    grad_low = gradient.astype(jnp.bfloat16)
    grad_w_down = jnp.einsum(
        "tbf,tbd->fd", activation, grad_low, preferred_element_type=jnp.float32
    )
    grad_b_down = jnp.sum(gradient, axis=(0, 1))
    grad_activation = jnp.einsum(
        "tbd,fd->tbf", grad_low, mat_down, preferred_element_type=jnp.float32
    )
    grad_hidden = jax.vjp(gelu_exact, hidden)[1](grad_activation)[0].astype(jnp.bfloat16)
    grad_b_up = jnp.sum(grad_hidden.astype(jnp.float32), axis=(0, 1))
    grad_w_up = jnp.einsum("tbd,tbf->df", second, grad_hidden, preferred_element_type=jnp.float32)
    grad_second = sum_inputs(
        jnp.einsum("tbf,df->tbd", grad_hidden, mat_up, preferred_element_type=jnp.float32)
    )
    middle_pull = jax.vjp(layer_norm, middle, gain_two, shift_two)[1]
    grad_inner, grad_gain_two, grad_shift_two = middle_pull(grad_second)
    grad_middle = gradient + grad_inner
    grad_b_out = jnp.sum(grad_middle, axis=(0, 1))
    middle_low = grad_middle.astype(jnp.bfloat16)
    grad_w_out = jnp.einsum("tbf,tbd->fd", mixed, middle_low, preferred_element_type=jnp.float32)
    grad_mixed = jnp.einsum(
        "tbd,fd->tbf", middle_low, mat_out, preferred_element_type=jnp.float32
    ).astype(jnp.bfloat16)
    grad_query, key_terms = attend_backward(
        query, keys_all, values_all, log_total, grad_mixed, query_tags, key_tags
    )
    returned = lax.psum_scatter(key_terms, "seq", scatter_dimension=0, tiled=True)
    turned_query = rotate(
        grad_query.reshape(rows_dev, lane_count, head_count, HEAD_DIM),
        -frame_place,
        -row_place,
        -column_place,
    )
    turned_keys = rotate(
        returned[:, :, 0].reshape(rows_dev, lane_count, head_count, HEAD_DIM),
        -frame_place,
        -row_place,
        -column_place,
    )
    grad_projected = jnp.stack(
        [
            turned_query.reshape(rows_dev, lane_count, features),
            turned_keys.reshape(rows_dev, lane_count, features),
            returned[:, :, 1],
        ],
        axis=2,
    ).astype(jnp.bfloat16)
    grad_b_qkv = jnp.sum(grad_projected.astype(jnp.float32), axis=(0, 1))
    grad_w_qkv = jnp.einsum(
        "tbd,tbcf->dcf", first, grad_projected, preferred_element_type=jnp.float32
    )
    grad_first = sum_inputs(
        jnp.einsum("tbcf,dcf->tbd", grad_projected, mat_qkv, preferred_element_type=jnp.float32)
    )
    first_pull = jax.vjp(layer_norm, stream, gain_one, shift_one)[1]
    grad_entry, grad_gain_one, grad_shift_one = first_pull(grad_first)
    grads = (
        grad_gain_one,
        grad_shift_one,
        grad_w_qkv,
        grad_b_qkv,
        grad_w_out,
        grad_b_out,
        grad_gain_two,
        grad_shift_two,
        grad_w_up,
        grad_b_up,
        grad_w_down,
        grad_b_down,
    )
    return (grad_middle + grad_entry, grads)


def per_device(
    tokens,
    d_out,
    norm1_gain,
    norm1_shift,
    w_qkv,
    b_qkv,
    w_out,
    b_out,
    norm2_gain,
    norm2_shift,
    w_up,
    b_up,
    w_down,
    b_down,
    episode_frames,
    live,
):
    rows_dev = tokens.shape[0]
    lane_count = tokens.shape[1] // MICRO
    total_rows = rows_dev * lax.axis_size("seq")
    local_positions = lax.axis_index("seq") * rows_dev + jnp.arange(rows_dev, dtype=jnp.int32)
    key_positions = jnp.arange(total_rows, dtype=jnp.int32)
    tagger = jax.vmap(episode_tags, in_axes=(0, None), out_axes=1)
    query_episode, query_frame, query_row, query_column = tagger(episode_frames, local_positions)
    key_episode, key_frame, key_row, key_column = tagger(episode_frames, key_positions)
    live_keys = lax.all_gather(live, "seq", axis=0, tiled=True)
    params = (
        norm1_gain,
        norm1_shift,
        w_qkv,
        b_qkv,
        w_out,
        b_out,
        norm2_gain,
        norm2_shift,
        w_up,
        b_up,
        w_down,
        b_down,
    )
    layer_grads = [None] * LAYERS
    outputs = []
    grad_tokens = []
    for micro_index in range(MICRO):
        first_lane = micro_index * lane_count
        last_lane = first_lane + lane_count
        query_tags = (query_episode[:, first_lane:last_lane], query_frame[:, first_lane:last_lane])
        key_tags = (
            key_episode[:, first_lane:last_lane],
            key_frame[:, first_lane:last_lane],
            live_keys[:, first_lane:last_lane],
        )
        positions = (
            query_frame[:, first_lane:last_lane],
            query_row[:, first_lane:last_lane],
            query_column[:, first_lane:last_lane],
        )
        stream = tokens[:, first_lane:last_lane].astype(jnp.float32)
        inputs = []
        gathered = []
        for layer_index in range(LAYERS):
            inputs.append(stream)
            layer_state = front(stream, layer_index, params, query_tags, key_tags, positions)
            gathered.append((layer_state[2], layer_state[3]))
            branch = jnp.einsum(
                "tbf,fd->tbd",
                layer_state[9],
                w_down[layer_index],
                preferred_element_type=jnp.float32,
            )
            stream = layer_state[6] + sum_heads(branch) + b_down[layer_index]
        outputs.append(stream)
        gradient = d_out[:, first_lane:last_lane]
        for layer_index in reversed(range(LAYERS)):
            gradient, grads = layer_backward(
                inputs[layer_index], gradient, layer_index, params, query_tags, key_tags, positions
            )
            if layer_grads[layer_index] is None:
                layer_grads[layer_index] = grads
            else:
                layer_grads[layer_index] = jax.tree.map(jnp.add, layer_grads[layer_index], grads)
        grad_tokens.append(gradient)
    stacked = [
        jnp.stack([layer_grads[layer_index][entry] for layer_index in range(LAYERS)])
        for entry in range(12)
    ]
    (
        grad_gain_one,
        grad_shift_one,
        grad_w_qkv,
        grad_b_qkv,
        grad_w_out,
        grad_b_out,
        grad_gain_two,
        grad_shift_two,
        grad_w_up,
        grad_b_up,
        grad_w_down,
        grad_b_down,
    ) = stacked
    in_sums = (
        lax.psum_scatter(grad_w_qkv, "seq", scatter_dimension=1, tiled=True),
        lax.psum_scatter(grad_w_up, "seq", scatter_dimension=1, tiled=True),
        lax.psum_scatter(grad_gain_one, "seq", scatter_dimension=1, tiled=True),
        lax.psum_scatter(grad_shift_one, "seq", scatter_dimension=1, tiled=True),
        lax.psum_scatter(grad_gain_two, "seq", scatter_dimension=1, tiled=True),
        lax.psum_scatter(grad_shift_two, "seq", scatter_dimension=1, tiled=True),
        lax.psum_scatter(grad_b_out, "seq", scatter_dimension=1, tiled=True),
        lax.psum_scatter(grad_b_down, "seq", scatter_dimension=1, tiled=True),
    )
    out_sums = (
        lax.psum_scatter(grad_w_out, "seq", scatter_dimension=2, tiled=True),
        lax.psum_scatter(grad_w_down, "seq", scatter_dimension=2, tiled=True),
    )
    bias_total = lax.psum((grad_b_qkv, grad_b_up), "seq")
    return (
        jnp.concatenate(outputs, axis=1),
        jnp.concatenate(grad_tokens, axis=1),
        in_sums[2],
        in_sums[3],
        in_sums[0],
        bias_total[0],
        out_sums[0],
        in_sums[6],
        in_sums[4],
        in_sums[5],
        in_sums[1],
        bias_total[1],
        out_sums[1],
        in_sums[7],
    )


MESH = pl.DeviceIdType.MESH
BF16 = jnp.bfloat16
F32 = jnp.float32
VMEM_BYTES = 60 * 1024 * 1024
PAIR = 128
VEC = 2048


def nn(left, right):
    return lax.dot_general(left, right, (((1,), (0,)), ((), ())), preferred_element_type=F32)


def nt(left, right):
    return lax.dot_general(left, right, (((1,), (1,)), ((), ())), preferred_element_type=F32)


def tn(left, right):
    return lax.dot_general(left, right, (((0,), (0,)), ((), ())), preferred_element_type=F32)


def at(start, size):
    return pl.ds(pl.multiple_of(start, size), size)


def repeat(count, body):
    def one(index, carry):
        body(index)
        return carry

    lax.fori_loop(0, count, one, 0)


def remote(src, dst, send, recv, seq, tp):
    return pltpu.make_async_remote_copy(
        src_ref=src,
        dst_ref=dst,
        send_sem=send,
        recv_sem=recv,
        device_id=(seq, tp),
        device_id_type=MESH,
    )


def hello(partners):
    barrier = pltpu.get_barrier_semaphore()
    for seq, tp in partners:
        pl.semaphore_signal(barrier, inc=1, device_id=(seq, tp), device_id_type=MESH)


def met(partners):
    pl.semaphore_wait(pltpu.get_barrier_semaphore(), len(partners))


def whole(array):
    zeros = (0,) * array.ndim
    return pl.BlockSpec(array.shape, lambda s: zeros, pipeline_mode=pl.Buffered(1))


def whole_out(shape):
    zeros = (0,) * len(shape)
    return pl.BlockSpec(shape, lambda s: zeros)


ANYWHERE = pl.BlockSpec(memory_space=pl.ANY)


def turn_row(table, place, section):
    frequency = np.exp(np.arange(10, dtype=np.float32) * np.float32(-math.log(10000.0) / 10.0))
    angle = place.astype(np.float32)[:, None] * frequency
    for base in range(20 * section, PAIR, HEAD_DIM):
        table[0, :, base : base + 10] = np.cos(angle)
        table[0, :, base + 10 : base + 20] = np.cos(angle)
        table[1, :, base : base + 10] = -np.sin(angle)
        table[2, :, base + 10 : base + 20] = np.sin(angle)


def turn_constants(frames):
    within, ahead = np.zeros((3, FRAME, PAIR), np.float32), np.zeros((3, frames, PAIR), np.float32)
    turn_row(within, np.arange(FRAME) // GRID, 1)
    turn_row(within, np.arange(FRAME) % GRID, 2)
    for base in range(60, PAIR, HEAD_DIM):
        within[0, :, base : base + 4] = 1.0
    turn_row(ahead, np.arange(frames), 0)
    return jnp.asarray(within), jnp.asarray(ahead)


def turn(values, tables, back=False):
    cosine, lower, upper = tables
    pieces = []
    for start in range(0, values.shape[1], PAIR):
        slab = values[:, start : start + PAIR]
        moved = pltpu.roll(slab, PAIR - 10, 1) * lower + pltpu.roll(slab, 10, 1) * upper
        pieces.append(slab * cosine - moved if back else slab * cosine + moved)
    return jnp.concatenate(pieces, axis=1)


def tables_of(fixed_ref, frames_ref, chunk):
    return [fixed_ref[i] + frames_ref[i, pl.ds(chunk, 1), :] for i in range(3)]


def normed(stream):
    center = stream - jnp.mean(stream, axis=-1, keepdims=True)
    spread = jnp.mean(center * center, axis=-1, keepdims=True)
    scale = lax.rsqrt(spread + EPSILON)
    return center * scale, scale


def norm_pull(grad, gain, unit, scale):
    scaled = grad * gain
    return scale * (
        scaled
        - jnp.mean(scaled, axis=-1, keepdims=True)
        - unit * jnp.mean(scaled * unit, axis=-1, keepdims=True)
    )


def keep_norm(unit, scale, unit_ref, scale_ref):
    unit_ref[...] = unit.astype(BF16)
    scale_ref[...] = jnp.broadcast_to(scale, scale_ref.shape)


def kept_norm(unit_ref, scale_ref):
    copies = unit_ref.shape[1] // scale_ref.shape[1]
    return unit_ref[...].astype(F32), jnp.concatenate([scale_ref[...]] * copies, axis=1)


def column_sum(values):
    return jnp.sum(values, axis=0, keepdims=True)


def gelu_both(hidden):
    normal = 0.5 + 0.5 * lax.erf(hidden * math.sqrt(0.5))
    density = jnp.exp(hidden * hidden * -0.5) * (1.0 / math.sqrt(2.0 * math.pi))
    return hidden * normal, normal + hidden * density


def project(stream, chunk, layer, pair, refs, outs, first_full, straight=False):
    gain, shift, weight, bias, fixed, frames = refs
    qkv_ref, first_ref, unit_ref, scale_ref = outs
    unit, scale = normed(stream)
    keep_norm(unit, scale, unit_ref, scale_ref)
    first_full[...] = (unit * gain[layer : layer + 1, :] + shift[layer : layer + 1, :]).astype(BF16)
    first_ref[...] = first_full[:, at(pair * PAIR, PAIR)]
    cosine, lower, upper = tables_of(fixed, frames, chunk)

    def one(part):
        still = part == 2
        tables = (
            jnp.where(still, 1.0, cosine),
            jnp.where(still, 0.0, lower),
            jnp.where(still, 0.0, upper),
        )
        values = nn(first_full[...], weight[part]) + bias[part, layer : layer + 1, :]
        qkv_ref[part] = (turn(values, tables) * jnp.where(part == 0, SCORE_SCALE, 1.0)).astype(BF16)

    if not straight:
        repeat(3, one)
        return
    for part in range(3):
        values = nn(first_full[...], weight[part]) + bias[part, layer : layer + 1, :]
        if part < 2:
            values = turn(values, (cosine, lower, upper))
        if part == 0:
            values = values * SCORE_SCALE
        qkv_ref[part] = values.astype(BF16)


class Relay:
    sems = 6

    def __init__(self, n, rows, buffer, other, sems, lives=None, live_other=None):
        self.n, self.rows, self.buffer, self.other = n, rows, buffer, other
        self.lives, self.live_other = lives, live_other
        self.z_send, self.z_recv, self.y_send, self.y_recv, self.c_send, self.c_recv = sems
        self.planes = n // 4
        self.me, self.core = lax.axis_index("seq"), lax.axis_index("tp")
        me = self.me
        self.x, self.y, self.z = lax.rem(me, 2), lax.rem(me // 2, 2), me // 4
        self.across = me + 2 - 4 * self.y

    @staticmethod
    def scratch(n):
        dma, planes = pltpu.SemaphoreType.DMA, n // 4
        shapes = [(planes, 2, 2)] * 2 + [(planes, 2)] * 2 + [(2 * planes,)] * 2
        return [dma(shape) for shape in shapes]

    @property
    def events(self):
        return self.planes

    def plane(self, step):
        return lax.rem(self.z + step, self.planes)

    def place(self, plane, lane):
        return plane * 4 + self.y * 2 + lane

    def reached(self):
        return [(step, far) for step in range(self.planes) for far in (0, 1) if step or far]

    def hello(self):
        barrier = pltpu.get_barrier_semaphore()
        partners = [(self.across, self.core), (self.me, 1 - self.core)]
        for step, far in self.reached():
            lane = 1 - self.x if far else self.x
            partners.append((self.place(self.plane(step), lane), self.core))
        for seq, tp in partners:
            pl.semaphore_signal(barrier, inc=1, device_id=(seq, tp), device_id_type=MESH)

    def met(self):
        pl.semaphore_wait(pltpu.get_barrier_semaphore(), 2 + len(self.reached()))

    def rows_of(self, side, seq):
        return self.buffer.at[side, at(seq * self.rows, self.rows), :]

    def block(self, side, pair):
        return self.buffer.at[side, at(pair * 2 * self.rows, 2 * self.rows), :]

    def items(self, pair):
        found = [self.block(self.core, pair)]
        if self.lives is not None:
            found.append(self.lives.at[at(pair * 2, 2)])
        return found

    def each(self, copy, what):
        for index in range(1 if self.lives is None else 2):
            getattr(copy(index), what)()

    def z_copy(self, step, far):
        def copy(index):
            lane = 1 - self.x if far else self.x
            if index == 0:
                source = self.other.at[self.core] if far else self.rows_of(self.core, self.me)
                target = self.rows_of(self.core, self.me)
            else:
                source = self.live_other if far else self.lives.at[self.me]
                target = self.lives.at[self.me]
            return remote(
                source,
                target,
                self.z_send.at[step, far, index],
                self.z_recv.at[step, far, index],
                self.place(self.plane(step), lane),
                self.core,
            )

        return copy

    def y_copy(self, plane, row):
        def copy(index):
            item = self.items(plane * 2 + row)[index]
            return remote(
                item,
                item,
                self.y_send.at[plane, index],
                self.y_recv.at[plane, index],
                self.across,
                self.core,
            )

        return copy

    def c_copy(self, pair, side):
        item = self.block(side, pair)
        return remote(
            item, item, self.c_send.at[pair], self.c_recv.at[pair], self.me, 1 - self.core
        )

    def begin(self):
        for step, far in self.reached():
            self.each(self.z_copy(step, far), "start")

    def arrive(self, event):
        for far in (0, 1) if event else (1,):
            self.each(self.z_copy(event, far), "wait_recv")
        plane = self.plane(self.planes - event)
        self.each(self.y_copy(plane, self.y), "start")
        self.c_copy(plane * 2 + self.y, self.core).start()

    def complete(self, event):
        plane = self.plane(self.planes - event)
        self.each(self.y_copy(plane, 1 - self.y), "wait_recv")
        self.c_copy(plane * 2 + 1 - self.y, self.core).start()

    def ready(self, event):
        plane = self.plane(self.planes - event)
        self.c_copy(plane * 2, 1 - self.core).wait_recv()
        self.c_copy(plane * 2 + 1, 1 - self.core).wait_recv()
        return plane

    def finish(self):
        for step, far in self.reached():
            self.each(self.z_copy(step, far), "wait_send")
        for plane in range(self.planes):
            self.each(self.y_copy(plane, self.y), "wait_send")
        for pair in range(2 * self.planes):
            self.c_copy(pair, self.core).wait_send()


def split_lanes(values, x, buffer, other, start, rows):
    half = values.shape[2] // 2
    zero, one = values[:, 0, :], values[:, 1, :]
    own, far = jnp.where(x == 0, zero, one), jnp.where(x == 0, one, zero)
    core = lax.axis_index("tp")
    own = jnp.where(core == 0, own[:, :half], own[:, half:]).astype(BF16)
    buffer[core, at(start, rows), :] = own
    for side in range(2):
        other[side] = far[:, side * half : (side + 1) * half].astype(BF16)


def gather_and_project(tokens, live, episode_frames, gain, shift, qkv, bias, fixed, ahead, n):
    rows, lanes, width = tokens.shape
    half = width // 2
    total = n * rows
    chunks = total // FRAME
    per_frame = FRAME // rows
    features = qkv.shape[3]
    slots = episode_frames.shape[1]

    def kernel(*refs):
        refs = list(refs)

        def take(count):
            taken = refs[:count]
            del refs[:count]
            return taken

        tokens_ref, live_ref, counts_ref, gain_ref, shift_ref, w_any, bias_ref = take(7)
        fixed_ref, ahead_ref = take(2)
        all_ref, mask_ref, frames_ref = take(3)
        qkv_ref, *projected = take(4)
        other, lives, live_other, weight, full, w_sem = take(6)
        relay = Relay(n, rows, all_ref, other, take(Relay.sems), lives, live_other)
        load = pltpu.make_async_copy(w_any.at[0], weight, w_sem)
        load.start()
        relay.hello()
        x, me = relay.x, relay.me
        split_lanes(tokens_ref[...].astype(F32), x, all_ref, other, me * rows, rows)
        lane = lax.broadcasted_iota(jnp.int32, (1, FRAME), 1)
        here = lane // rows == lax.rem(me, per_frame)
        tiles = []
        for index in range(lanes):
            alive = live_ref[index : index + 1, :].astype(F32)
            alive = jnp.where(here, jnp.concatenate([alive] * per_frame, axis=1), 0.0)
            tiles.append(jnp.broadcast_to(alive, (8, FRAME)))
        lives[me] = jnp.where(x == 0, tiles[0], tiles[1])
        live_other[...] = jnp.where(x == 0, tiles[1], tiles[0])
        relay.met()
        relay.begin()

        counts = [counts_ref[x, slot] for slot in range(slots)]
        episodes, openings = [], []
        for frame in range(chunks):
            end, episode, opening = 0, 0, 0
            for slot in range(slots):
                end = end + counts[slot]
                passed = frame >= end
                episode = episode + passed.astype(jnp.int32)
                opening = opening + jnp.where(passed, counts[slot], 0)
            episodes.append(episode)
            openings.append(frame - opening)
        for index in range(3):
            table = []
            for frame in range(chunks):
                line = jnp.zeros((1, PAIR), F32)
                for choice in range(chunks):
                    line = jnp.where(
                        openings[frame] == choice, ahead_ref[index, choice : choice + 1, :], line
                    )
                table.append(line)
            frames_ref[index] = jnp.concatenate(
                table + [jnp.zeros((8 - chunks, PAIR), F32)], axis=0
            )
        load.wait()

        def project_frame(frame):
            place = at(frame * FRAME, FRAME)
            stream = jnp.concatenate([all_ref[0, place, :], all_ref[1, place, :]], axis=1)
            project(
                stream.astype(F32),
                frame,
                0,
                me // 2,
                (gain_ref, shift_ref, weight, bias_ref, fixed_ref, frames_ref),
                [qkv_ref.at[:, place, :]] + [ref.at[place, :] for ref in projected],
                full,
                straight=True,
            )

        for event in range(relay.events):
            relay.arrive(event)
            if event:
                relay.complete(event - 1)
            if event > 1:
                project_frame(relay.ready(event - 2))
        relay.complete(relay.events - 1)
        for event in range(max(0, relay.events - 2), relay.events):
            project_frame(relay.ready(event))
        relay.finish()

        for key_frame in range(chunks):
            alive = lives[key_frame * per_frame, 0:1, :]
            for part in range(1, per_frame):
                alive = alive + lives[key_frame * per_frame + part, 0:1, :]
            closed = (alive - 1.0) * -MASKED
            lines = []
            for query_frame in range(chunks):
                allowed = (episodes[query_frame] == episodes[key_frame]) & (
                    openings[key_frame] <= openings[query_frame]
                )
                lines.append(jnp.where(allowed, closed, MASKED))
            lines.append(jnp.zeros((PAIR - chunks, FRAME), F32))
            mask_ref[key_frame * FRAME : (key_frame + 1) * FRAME, :] = jnp.concatenate(
                lines, axis=0
            ).T.astype(BF16)

    in_vmem = pl.BlockSpec(memory_space=pltpu.VMEM)
    in_smem = pl.BlockSpec(memory_space=pltpu.SMEM)
    return pl.pallas_call(
        kernel,
        out_shape=(
            jax.ShapeDtypeStruct((2, total, half), BF16),
            jax.ShapeDtypeStruct((total, PAIR), BF16),
            jax.ShapeDtypeStruct((3, 8, PAIR), F32),
            jax.ShapeDtypeStruct((3, total, features), BF16),
            jax.ShapeDtypeStruct((total, PAIR), BF16),
            jax.ShapeDtypeStruct((total, width), BF16),
            jax.ShapeDtypeStruct((total, PAIR), F32),
        ),
        in_specs=[in_vmem, in_vmem, in_smem, in_vmem, in_vmem, ANYWHERE] + [in_vmem] * 3,
        out_specs=(in_vmem,) * 7,
        scratch_shapes=[
            pltpu.VMEM((2, rows, half), BF16),
            pltpu.VMEM((n, 8, FRAME), F32),
            pltpu.VMEM((8, FRAME), F32),
            pltpu.VMEM(qkv.shape[1:], BF16),
            pltpu.VMEM((FRAME, width), BF16),
            pltpu.SemaphoreType.DMA,
        ]
        + Relay.scratch(n),
        compiler_params=pltpu.CompilerParams(
            collective_id=0, has_side_effects=True, vmem_limit_bytes=VMEM_BYTES
        ),
        name="gather_and_project",
    )(tokens, live, episode_frames, gain, shift, qkv, bias, fixed, ahead)


def halves(ref):
    return jnp.concatenate([ref[0], ref[1]], axis=1).astype(F32)


def halves_spec(shape, chunks, behind, span=FRAME):
    return pl.BlockSpec(
        (2, span, shape[2]), lambda s: (0, jnp.clip(s - behind, 0, chunks - 1), 0)
    )


def layer_forward(layer, turned, key_bias, stream, mats, rows_of, next_refs, d_out, n, identity):
    _, total, features = turned.shape
    split = stream.ndim == 3
    width = mats[1].shape[1]
    rows_here = total // n
    hidden_units = mats[1].shape[2]
    chunks = total // FRAME
    heads = features // HEAD_DIM
    slabs = features // PAIR
    columns = 256
    last = next_refs is None
    b_out, gain, shift, b_up, b_down = rows_of
    mat_out, mat_up, mat_down = mats

    def kernel(*refs):
        refs = list(refs)

        def take(count):
            taken = refs[:count]
            del refs[:count]
            return taken

        q_ref, k_ref, v_ref, kb_ref, x_ref = take(5)
        wo_any, wu_any, wd_any = take(3)
        bo_ref, gain_ref, shift_ref, bu_ref, bd_ref = take(5)
        if not last:
            wq_any, ngain, nshift, nbias, fixed, frames = take(6)
        if d_out is not None:
            (d_ref,) = take(1)
        p_ref, r_ref, mixed_ref, unit_ref, scale_ref, second_ref, act_ref, gp_ref, x_out = take(9)
        if not last:
            next_outs = take(4)
        if d_out is not None:
            (d_all,) = take(1)
        wo, wu, wd, mid, full, next_full = take(6)
        if not last:
            (wq,) = take(1)
        a_send, a_recv, b_send, b_recv, w_sem, send_sem, recv_sem = take(7)
        relay = None
        if d_out is not None:
            buffer, other, d_sem = take(3)
            relay = Relay(n, rows_here, buffer, other, take(Relay.sems))

        step = pl.program_id(0)
        me, core = lax.axis_index("seq"), lax.axis_index("tp")

        items = [(wo_any, wo), (wu_any, wu), (wd_any, wd)]
        if not last:
            items.append((wq_any, wq))

        def load(index):
            source, target = items[index]
            return pltpu.make_async_copy(
                source.at[layer if index < 3 else layer + 1], target, w_sem.at[index]
            )

        def exchange(kind, chunk):
            source, target = ((a_send, a_recv), (b_send, b_recv))[kind]
            return remote(
                source.at[chunk],
                target.at[chunk],
                send_sem.at[kind, chunk],
                recv_sem.at[kind, chunk],
                me,
                1 - core,
            )

        @pl.when(step == 0)
        def _():
            for index in range(len(items)):
                load(index).start()
            if relay is None:
                hello([(me, 1 - core)])
            else:
                relay.hello()
                split_lanes(d_ref[...], relay.x, buffer, other, me * rows_here, rows_here)

        lane = lax.broadcasted_iota(jnp.int32, (1, PAIR), 1)
        sides = [(lane < HEAD_DIM).astype(F32).astype(BF16), (lane >= HEAD_DIM).astype(F32).astype(BF16)]
        for frame in range(chunks):

            @pl.when(step == frame)
            def _():
                keys = FRAME * (frame + 1)
                mask = kb_ref[:keys, :]
                asked = jnp.broadcast_to((lane == frame).astype(F32), (FRAME, PAIR)).astype(BF16)

                def two_slabs(couple):
                    def lanes_of(head):
                        return at((couple * 2 + head // 2) * PAIR, PAIR)

                    def score(head):
                        key = jnp.concatenate([k_ref[0, :keys, lanes_of(head)], mask], axis=1)
                        ask = q_ref[0, :, lanes_of(head)] * sides[head % 2]
                        return nt(jnp.concatenate([ask, asked], axis=1), key)

                    scores, sums = score(0), []
                    for head in range(4):
                        lanes, side = lanes_of(head), head % 2
                        following = score(head + 1) if head < 3 else None
                        highest = jnp.max(scores, axis=1, keepdims=True)
                        shifted = jnp.exp(scores - highest).astype(BF16)
                        p_ref[0, couple * 4 + head, :keys, :] = shifted.T
                        sums.append(nn(shifted, v_ref[0, :keys, lanes] * sides[side] + sides[1 - side]))
                        scores = following
                        if side == 1:
                            one, two = sums[head - 1 :]
                            low_side = lane < HEAD_DIM
                            divisor = 1.0 / jnp.where(
                                low_side, pltpu.roll(one, HEAD_DIM, 1), pltpu.roll(two, HEAD_DIM, 1)
                            )
                            r_ref[:, lanes] = divisor
                            mixed_ref[:, lanes] = (jnp.where(low_side, one, two) * divisor).astype(BF16)

                repeat(slabs // 2, two_slabs)

        @pl.when(step == 0)
        def _():
            load(0).wait()
            if relay is None:
                met([(me, 1 - core)])
            else:
                relay.met()
                relay.begin()

        @pl.when(step < chunks)
        def _():
            a_send[step] = nn(mixed_ref[...], wo[...]).astype(BF16)
            exchange(0, step).start()

        if relay is not None:
            for event in range(relay.events):

                @pl.when(step == 2 + event // 2)
                def _():
                    relay.arrive(event)

                @pl.when(step == 3 + event // 2)
                def _():
                    relay.complete(event)

            @pl.when(step == chunks + 1)
            def _():
                for event in range(relay.events):
                    relay.ready(event)
                relay.finish()
                pltpu.make_async_copy(buffer, d_all, d_sem).start()

        def feed_forward():
            chunk = step - 1
            middle = (halves(x_ref) if split else x_ref[...]) + (
                a_send[chunk].astype(F32) + a_recv[chunk].astype(F32)
            )
            middle = middle + bo_ref[layer : layer + 1, :]
            mid[lax.rem(chunk, 2)] = middle
            unit, scale = normed(middle)
            keep_norm(unit, scale, unit_ref, scale_ref)
            second = (unit * gain_ref[layer : layer + 1, :] + shift_ref[layer : layer + 1, :]).astype(BF16)
            full[...] = second
            second_ref[...] = full[:, at((me // 2) * PAIR, PAIR)]
            parts = [slice(start, start + columns) for start in range(0, hidden_units, columns)]
            hidden = nn(second, wu[:, parts[0]])
            for index, part in enumerate(parts):
                following = nn(second, wu[:, parts[index + 1]]) if index + 1 < len(parts) else None
                act, slope = gelu_both(hidden + bu_ref[layer : layer + 1, part])
                act_ref[:, part] = act.astype(BF16)
                gp_ref[:, part] = slope.astype(BF16)
                hidden = following
            b_send[chunk] = nn(act_ref[...], wd[...]).astype(BF16)

        def close():
            chunk = step - 2
            result = mid[lax.rem(chunk, 2)] + (b_send[chunk].astype(F32) + b_recv[chunk].astype(F32))
            result = result + bd_ref[layer : layer + 1, :]
            x_out[...] = result
            if not last:
                project(
                    result,
                    chunk,
                    layer + 1,
                    me // 2,
                    (ngain, nshift, wq, nbias, fixed, frames),
                    next_outs,
                    next_full,
                )

        @pl.when(step == 1)
        def _():
            load(1).wait()
            load(2).wait()

        @pl.when((step >= 1) & (step <= chunks))
        def _():
            exchange(0, step - 1).wait_recv()
            feed_forward()
            exchange(1, step - 1).start()

        if not last:

            @pl.when(step == 2)
            def _():
                load(3).wait()

        @pl.when(step >= 2)
        def _():
            exchange(1, step - 2).wait_recv()
            close()

        @pl.when(step == chunks + 1)
        def _():
            for kind in range(2):
                for chunk in range(chunks):
                    exchange(kind, chunk).wait_send()
            if relay is not None:
                pltpu.make_async_copy(buffer, d_all, d_sem).wait()

    def rows(columns, behind):
        return pl.BlockSpec(
            (FRAME, columns), lambda s: (jnp.clip(s - behind, 0, chunks - 1), 0)
        )

    def part_of(part):
        return pl.BlockSpec(
            (1, total, features), lambda s: (part, 0, 0), pipeline_mode=pl.Buffered(1)
        )

    in_specs = [
        pl.BlockSpec((1, FRAME, features), lambda s: (0, jnp.minimum(s, chunks - 1), 0)),
        part_of(1),
        part_of(2),
        whole(key_bias),
    ]
    in_specs += [halves_spec(stream.shape, chunks, 1) if split else rows(width, 1)]
    in_specs += [ANYWHERE] * 3 + [whole(item) for item in rows_of]
    operands = [turned, turned, turned, key_bias, stream, *mats, *rows_of]
    if not last:
        in_specs += [ANYWHERE] + [whole(item) for item in next_refs[1:]]
        operands += list(next_refs)
    if d_out is not None:
        in_specs += [whole(d_out)]
        operands += [d_out]
    out_shape = [
        jax.ShapeDtypeStruct((chunks, heads, total, FRAME), BF16),
        jax.ShapeDtypeStruct((total, features), F32),
        jax.ShapeDtypeStruct((total, features), BF16),
        jax.ShapeDtypeStruct((total, width), BF16),
        jax.ShapeDtypeStruct((total, PAIR), F32),
        jax.ShapeDtypeStruct((total, PAIR), BF16),
        jax.ShapeDtypeStruct((total, hidden_units), BF16),
        jax.ShapeDtypeStruct((total, hidden_units), BF16),
        jax.ShapeDtypeStruct((total, width), F32),
    ]
    out_specs = [
        pl.BlockSpec((1, heads, total, FRAME), lambda s: (jnp.minimum(s, chunks - 1), 0, 0, 0)),
        rows(features, 0),
        rows(features, 0),
        rows(width, 1),
        rows(PAIR, 1),
        rows(PAIR, 1),
        rows(hidden_units, 1),
        rows(hidden_units, 1),
        rows(width, 2),
    ]
    scratch = [
        pltpu.VMEM(mat_out.shape[1:], BF16),
        pltpu.VMEM(mat_up.shape[1:], BF16),
        pltpu.VMEM(mat_down.shape[1:], BF16),
        pltpu.VMEM((2, FRAME, width), F32),
        pltpu.VMEM((FRAME, width), BF16),
        pltpu.VMEM((FRAME, width), BF16),
    ]
    if not last:
        out_shape += [jax.ShapeDtypeStruct((3, total, features), BF16)]
        out_shape += [jax.ShapeDtypeStruct((total, PAIR), BF16)]
        out_shape += [jax.ShapeDtypeStruct((total, width), BF16)]
        out_shape += [jax.ShapeDtypeStruct((total, PAIR), F32)]
        out_specs += [
            pl.BlockSpec((3, FRAME, features), lambda s: (0, jnp.clip(s - 2, 0, chunks - 1), 0))
        ]
        out_specs += [rows(PAIR, 2), rows(width, 2), rows(PAIR, 2)]
    if d_out is not None:
        out_shape += [jax.ShapeDtypeStruct((2, total, width // 2), BF16)]
        out_specs += [ANYWHERE]
        scratch += [pltpu.VMEM(next_refs[0].shape[1:], BF16)]
    scratch += [pltpu.VMEM((chunks, FRAME, width), BF16)] * 4
    scratch += [
        pltpu.SemaphoreType.DMA((4,)),
        pltpu.SemaphoreType.DMA((2, chunks)),
        pltpu.SemaphoreType.DMA((2, chunks)),
    ]
    if d_out is not None:
        scratch += [
            pltpu.VMEM((2, total, width // 2), BF16),
            pltpu.VMEM((2, rows_here, width // 2), BF16),
            pltpu.SemaphoreType.DMA,
        ]
        scratch += Relay.scratch(n)
    return pl.pallas_call(
        kernel,
        grid=(chunks + 2,),
        out_shape=out_shape,
        in_specs=in_specs,
        out_specs=out_specs,
        scratch_shapes=scratch,
        compiler_params=pltpu.CompilerParams(
            collective_id=identity, has_side_effects=True, vmem_limit_bytes=VMEM_BYTES
        ),
        name=f"layer_forward_{layer}",
    )(*operands)


class Swap:
    def __init__(self, ships, lane_rows):
        self.ships, self.lane_rows = ships, lane_rows
        self.count = len(ships) + len(lane_rows)

    def operands(self):
        return [*self.ships, *[item for item, _ in self.lane_rows]]

    def in_specs(self):
        return [whole(item) for item in self.ships] + [ANYWHERE] * len(self.lane_rows)

    def outputs(self):
        shapes, specs = [], []
        for item in self.ships:
            shape = (item.shape[0] // 2, item.shape[1])
            shapes.append(jax.ShapeDtypeStruct(shape, F32))
            specs.append(whole_out(shape))
        for item, count in self.lane_rows:
            shapes.append(jax.ShapeDtypeStruct((count or item.shape[0], item.shape[1]), item.dtype))
            specs.append(ANYWHERE)
        return shapes, specs

    def scratch(self):
        if not self.count:
            return []
        buffers = [pltpu.VMEM((item.shape[0] // 2, item.shape[1]), BF16) for item in self.ships]
        return buffers * 2 + [pltpu.SemaphoreType.DMA((self.count,))] * 2

    def bind(self, sources, targets, scratch):
        ships = len(self.ships)
        me, core = lax.axis_index("seq"), lax.axis_index("tp")
        x = lax.rem(me, 2)
        beside = me + 1 - 2 * x
        half = PAIR // 2

        def copy(index):
            if index < ships:
                source, target = scratch[index], scratch[ships + index]
            else:
                source, target = sources[index], targets[index]
                count = self.lane_rows[index - ships][1]
                if count:
                    source = source.at[at(beside * count, count), :]
            send, recv = scratch[2 * ships].at[index], scratch[2 * ships + 1].at[index]
            return remote(source, target, send, recv, beside, core)

        def start():
            for index in range(self.count):
                if index < ships:
                    scratch[index][...] = sources[index][at((1 - x) * half, half), :].astype(BF16)
                copy(index).start()

        def finish():
            for index in range(self.count):
                copy(index).wait_recv()
                if index < ships:
                    own = sources[index][at(x * half, half), :]
                    targets[index][...] = own + scratch[ships + index][...].astype(F32)
            for index in range(self.count):
                copy(index).wait_send()

        return start, finish


def attention_backward(
    probs, divisor, mixed, turned_qkv, grad_mixed, first, fixed, frames, swap, swap_qkv, identity
):
    _, total, features = turned_qkv.shape
    chunks = total // FRAME
    slabs = features // PAIR
    half = PAIR // 2

    def kernel(*refs):
        refs = list(refs)

        def take(count):
            taken = refs[:count]
            del refs[:count]
            return taken

        p_ref, r_ref, o_ref, q_ref, k_ref, v_ref, g_ref, first_ref, fixed_ref, frames_ref = take(10)
        sources = take(swap.count)
        dq_ref, dk_ref, dv_ref, qkv_out = take(4)
        targets = take(swap.count)
        dk_sum, dv_sum, first_turned = take(3)
        if swap_qkv:
            qkv_own, qkv_send, qkv_recv, qkv_sems = take(4)
        start, finish = swap.bind(sources, targets, refs)

        step = pl.program_id(0)
        me, core = lax.axis_index("seq"), lax.axis_index("tp")
        x = lax.rem(me, 2)
        beside = me + 1 - 2 * x

        def qkv_copy(slab):
            return remote(
                qkv_send.at[slab],
                qkv_recv.at[slab],
                qkv_sems.at[0, slab],
                qkv_sems.at[1, slab],
                beside,
                core,
            )

        @pl.when(step == 0)
        def _():
            hello([(beside, core)])
            first_turned[...] = first_ref[...].T
            met([(beside, core)])
            start()

        lane = lax.broadcasted_iota(jnp.int32, (1, PAIR), 1)
        sides = [(lane < HEAD_DIM).astype(F32).astype(BF16), (lane >= HEAD_DIM).astype(F32).astype(BF16)]
        turned = k_ref[0].T
        ones = jnp.broadcast_to((lane < 2).astype(F32), (total, PAIR)).astype(BF16)
        values = jnp.concatenate([v_ref[0], ones], axis=1)

        def give(frame):
            keys = FRAME * (frame + 1)
            own = slice(frame * FRAME, keys)
            scaled = (g_ref[own, :].astype(F32) * r_ref[own, :]).astype(BF16)
            inner = scaled.astype(F32) * o_ref[own, :].astype(F32)
            grads, q_parts, g_parts = [], [], []
            for side in range(2):
                delta = jnp.sum(
                    jnp.where((lane < HEAD_DIM) == (side == 0), inner, 0.0), axis=1, keepdims=True
                )
                coarse = delta.astype(BF16).astype(F32)
                rest = jnp.where(lane == 0, -coarse, jnp.where(lane == 1, coarse - delta, 0.0))
                g2 = scaled * sides[side]
                grads.append(nt(values[:keys], jnp.concatenate([g2, rest.astype(BF16)], axis=1)))
                q_parts.append(q_ref[0, own, :] * sides[side])
                g_parts.append(g2)
            return grads, jnp.concatenate(q_parts, axis=0), jnp.concatenate(g_parts, axis=0)

        given = give(chunks - 1)
        for frame in reversed(range(chunks)):
            keys = FRAME * (frame + 1)
            own = slice(frame * FRAME, keys)
            tables = tables_of(fixed_ref, frames_ref, frame)
            grads, q_part, g_part = given
            given = give(frame - 1) if frame else None
            query_parts, score_parts, prob_parts = [], [], []
            for side in range(2):
                attention = p_ref[frame, side, :keys, :]
                grad_scores = (attention.astype(F32) * grads[side]).astype(BF16)
                query_parts.append(nn(turned[side * HEAD_DIM : (side + 1) * HEAD_DIM, :keys], grad_scores))
                score_parts.append(grad_scores)
                prob_parts.append(attention)
            grad_query = jnp.concatenate(query_parts, axis=0).T
            key_parts = nn(jnp.concatenate(score_parts, axis=1), q_part)
            value_parts = nn(jnp.concatenate(prob_parts, axis=1), g_part)
            dq_ref[own, :] = (turn(grad_query, tables, True) * SCORE_SCALE).astype(BF16)
            if frame == chunks - 1:
                dk_sum[...] = key_parts
                dv_sum[...] = value_parts
            else:
                dk_sum[:keys, :] += key_parts
                dv_sum[:keys, :] += value_parts
            dk_ref[own, :] = turn(dk_sum[own, :], tables, True).astype(BF16)
            dv_ref[own, :] = dv_sum[own, :].astype(BF16)

        for part, ref in enumerate((dq_ref, dk_ref, dv_ref)):
            piece = slice(part * PAIR, (part + 1) * PAIR)
            terms = nn(first_turned[...], ref[...])
            if swap_qkv:
                qkv_own[step, :, piece] = terms
                qkv_send[step, :, piece] = qkv_own[step, at((1 - x) * half, half), piece].astype(BF16)
            else:
                qkv_out[:, at(part * features + step * PAIR, PAIR)] = terms
        if swap_qkv:
            qkv_copy(step).start()

        @pl.when(step == slabs - 1)
        def _():
            finish()
            for slab in range(slabs if swap_qkv else 0):
                qkv_copy(slab).wait_recv()
                for part in range(3):
                    piece = slice(part * PAIR, (part + 1) * PAIR)
                    place = part * features + slab * PAIR
                    qkv_out[:, place : place + PAIR] = qkv_own[
                        slab, at(x * half, half), piece
                    ] + qkv_recv[slab, :, piece].astype(F32)
            for slab in range(slabs if swap_qkv else 0):
                qkv_copy(slab).wait_send()

    slab = pl.BlockSpec((total, PAIR), lambda s: (0, s))
    in_specs = [pl.BlockSpec((chunks, 2, total, FRAME), lambda s: (0, s, 0, 0))]
    in_specs += [slab] * 2
    for part in range(3):
        in_specs.append(pl.BlockSpec((1, total, PAIR), lambda s, part=part: (part, 0, s)))
    in_specs += [slab] + [whole(first), whole(fixed), whole(frames)]
    in_specs += swap.in_specs()
    qkv_shape = (half if swap_qkv else PAIR, 3 * features)
    shapes, specs = swap.outputs()
    out_shape = [jax.ShapeDtypeStruct((total, features), BF16)] * 3
    out_shape += [jax.ShapeDtypeStruct(qkv_shape, F32)] + shapes
    out_specs = [slab] * 3 + [whole_out(qkv_shape)] + specs
    scratch = [pltpu.VMEM((total, PAIR), F32)] * 2 + [pltpu.VMEM((PAIR, total), BF16)]
    if swap_qkv:
        scratch += [pltpu.VMEM((slabs, PAIR, 3 * PAIR), F32)]
        scratch += [pltpu.VMEM((slabs, half, 3 * PAIR), BF16)] * 2
        scratch += [pltpu.SemaphoreType.DMA((2, slabs))]
    scratch += swap.scratch()
    return pl.pallas_call(
        kernel,
        grid=(slabs,),
        out_shape=out_shape,
        in_specs=in_specs,
        out_specs=out_specs,
        scratch_shapes=scratch,
        compiler_params=pltpu.CompilerParams(
            collective_id=identity, has_side_effects=True, vmem_limit_bytes=VMEM_BYTES
        ),
        name=f"attention_backward_{identity}",
    )(
        probs,
        divisor,
        mixed,
        turned_qkv,
        turned_qkv,
        turned_qkv,
        grad_mixed,
        first,
        fixed,
        frames,
        *swap.operands(),
    )


def rows_backward(entry, upper, identity, span, swap):
    top, bottom = len(entry) == 1, upper is None
    if not top:
        above, entry = entry[0], entry[1:]
    total = entry[0].shape[1] if top else entry[0].shape[0]
    chunks = total // span
    columns = 256
    ahead = 0 if top else 2 if bottom else 1
    if top:
        width = 2 * entry[0].shape[2]
    else:
        features, width = entry[0].shape[1], entry[5].shape[1]
    if not bottom:
        layer = upper[0]
        hidden_units, mixed_features = upper[1].shape[1], upper[6].shape[1]
    place_rows = total // lax.axis_size("seq")

    def kernel(*refs):
        refs = list(refs)

        def take(count):
            taken = refs[:count]
            del refs[:count]
            return taken

        if top:
            (d_out_ref,) = take(1)
        else:
            dq_ref, dk_ref, dv_ref, unit1, scale1, dm_ref, wq, gain1 = take(8)
        if not bottom:
            act_ref, gp_ref, unit2, scale2, second_ref, mixed_ref = take(6)
            wo_any, wu_any, wd_any, gain2 = take(4)
        sources = take(swap.count)
        if not top:
            (vec1,) = take(1)
        if not bottom:
            dmid_out, dmix_out, out_sum, up_sum, down_sum, vec2 = take(6)
        else:
            dx_out, dx_other, vec_other = take(3)
        targets = take(swap.count)
        if not top:
            a_send, a_recv = take(2)
        if not bottom:
            b_send, b_recv, grad_keep, hidden_keep, low_keep, last_keep, wo, wu, wd, w_sem = take(10)
        else:
            dx_keep, dx_send, dx_recv, vec_recv, x_send_sem, x_recv_sem = take(6)
        send_sem, recv_sem = take(2)
        start_swap, finish_swap = swap.bind(sources, targets, refs)

        step = pl.program_id(0)
        me, core = lax.axis_index("seq"), lax.axis_index("tp")
        pair = at((me // 2) * PAIR, PAIR)
        x = lax.rem(me, 2)
        beside = me + 1 - 2 * x

        def exchange(kind, chunk):
            source, target = (a_send, a_recv) if kind == 0 else (b_send, b_recv)
            return remote(
                source.at[chunk],
                target.at[chunk],
                send_sem.at[kind, chunk],
                recv_sem.at[kind, chunk],
                me,
                1 - core,
            )

        def load(index):
            source, target = ((wd_any, wd), (wu_any, wu), (wo_any, wo))[index]
            return pltpu.make_async_copy(source.at[layer], target, w_sem.at[index])

        partners = [(me, 1 - core)] + ([(beside, core)] if bottom or swap.count else [])

        @pl.when(step == 0)
        def _():
            if not bottom:
                for index in range(3):
                    load(index).start()
                out_sum[...] = jnp.zeros_like(out_sum)
                up_sum[...] = jnp.zeros_like(up_sum)
                down_sum[...] = jnp.zeros_like(down_sum)
                vec2[...] = jnp.zeros_like(vec2)
            if not top:
                vec1[...] = jnp.zeros_like(vec1)
            hello(partners)

        def meet():
            @pl.when(step == 0)
            def _():
                met(partners)
                start_swap()

        def entry_products():
            partial = None
            for part, ref in enumerate((dq_ref, dk_ref, dv_ref)):
                grad = ref[...]
                term = nt(grad, wq[0, part])
                partial = term if partial is None else partial + term
                vec1[part : part + 1, :] += column_sum(grad.astype(F32))
            a_send[step] = partial.astype(BF16)

        def entry_norm(chunk):
            if top:
                return halves(d_out_ref)
            grad_first = a_send[chunk].astype(F32) + a_recv[chunk].astype(F32)
            unit, scale = kept_norm(unit1, scale1)
            for start, sums in ((3, column_sum(grad_first * unit)), (5, column_sum(grad_first))):
                for side in range(width // features):
                    piece = slice(side * features, (side + 1) * features)
                    vec1[start + side : start + side + 1, :] += sums[:, piece]
            return dm_ref[...] + norm_pull(grad_first, gain1[above : above + 1, :], unit, scale)

        def feed_forward(between=None):
            chunk = step - ahead
            gradient = entry_norm(chunk)
            if bottom:
                dx_keep[at(chunk * span, span), :] = gradient
                return
            grad_keep[lax.rem(chunk, 2)] = gradient
            vec2[1:2, :width] += column_sum(gradient)
            low = gradient.astype(BF16)
            low_keep[...] = low
            low_columns = low_keep[:, pair]
            second = second_ref[...]
            parts = [slice(start, start + columns) for start in range(0, hidden_units, columns)]
            grad_act = nt(low, wd[parts[0], :])
            for index, part in enumerate(parts):
                following = nt(low, wd[parts[index + 1], :]) if index + 1 < len(parts) else None
                grad_hidden = grad_act * gp_ref[:, part].astype(F32)
                hidden_keep[:, part] = grad_hidden.astype(BF16)
                vec2[0:1, part] += column_sum(grad_hidden)
                grad_act = following
            if between is not None:
                between()
            b_send[chunk] = nt(hidden_keep[...], wu[...]).astype(BF16)
            down_sum[...] += tn(low_columns, act_ref[...])
            up_sum[...] += tn(second, hidden_keep[...])

        def close():
            chunk = step - ahead - 1
            grad_second = b_send[chunk].astype(F32) + b_recv[chunk].astype(F32)
            unit, scale = kept_norm(unit2, scale2)
            vec2[2:3, :width] += column_sum(grad_second * unit)
            vec2[3:4, :width] += column_sum(grad_second)
            grad_middle = grad_keep[lax.rem(chunk, 2)] + norm_pull(
                grad_second, gain2[layer : layer + 1, :], unit, scale
            )
            dmid_out[...] = grad_middle
            vec2[4:5, :width] += column_sum(grad_middle)
            low = grad_middle.astype(BF16)
            last_keep[...] = low
            out_sum[...] += tn(last_keep[:, pair], mixed_ref[...])
            dmix_out[...] = nt(low, wo[...]).astype(BF16)

        if not top:

            @pl.when(step < chunks)
            def _():
                entry_products()
                meet()
                exchange(0, step).start()

        @pl.when((step >= ahead) & (step < chunks + ahead))
        def _():
            if not top:
                exchange(0, step - ahead).wait_recv()
            if not bottom:

                @pl.when(step == ahead)
                def _():
                    load(0).wait()

            feed_forward(lambda: pl.when(step == ahead)(lambda: load(1).wait()))
            if not bottom:
                if top:
                    meet()
                exchange(1, step - ahead).start()

        if not bottom:

            @pl.when(step == ahead + 1)
            def _():
                load(2).wait()

            @pl.when(step >= ahead + 1)
            def _():
                exchange(1, step - ahead - 1).wait_recv()
                close()

        if bottom:

            def x_copy(index):
                source, target = ((dx_send, dx_recv), (vec1, vec_recv))[index]
                return remote(
                    source, target, x_send_sem.at[index], x_recv_sem.at[index], beside, core
                )

            @pl.when(step == chunks + 1)
            def _():
                dx_send[...] = dx_keep[at(beside * place_rows, place_rows), :].astype(BF16)
                x_copy(0).start()
                x_copy(1).start()
                dx_out[...] = dx_keep[at(me * place_rows, place_rows), :]
                x_copy(0).wait_recv()
                x_copy(1).wait_recv()
                dx_other[...] = dx_recv[...].astype(F32)
                vec_other[...] = vec_recv[...]
                x_copy(0).wait_send()
                x_copy(1).wait_send()

        @pl.when(step == pl.num_programs(0) - 1)
        def _():
            for kind in ([] if top else [0]) + ([] if bottom else [1]):
                for chunk in range(chunks):
                    exchange(kind, chunk).wait_send()
            finish_swap()

    def rows(columns, behind):
        return pl.BlockSpec(
            (span, columns), lambda s: (jnp.clip(s - behind, 0, chunks - 1), 0)
        )

    vec = jax.ShapeDtypeStruct((8, VEC), F32)
    operands, in_specs, out_shape, out_specs, scratch = [], [], [], [], []
    if top:
        operands += list(entry)
        in_specs += [halves_spec(entry[0].shape, chunks, 0, span)]
    else:
        operands += list(entry)
        in_specs += [rows(features, 0)] * 3
        in_specs += [rows(width, ahead), rows(PAIR, ahead), rows(width, ahead)]
        in_specs += [
            pl.BlockSpec(
                (1, *entry[6].shape[1:]),
                lambda s: (above, 0, 0, 0),
                pipeline_mode=pl.Buffered(1),
            ),
            whole(entry[7]),
        ]
        narrow = jax.ShapeDtypeStruct((8, features), F32)
        out_shape += [narrow]
        out_specs += [whole_out((8, features))]
        scratch += [pltpu.VMEM((chunks, span, width), BF16)] * 2
    if not bottom:
        operands += list(upper[1:])
        in_specs += [rows(hidden_units, ahead)] * 2
        in_specs += [rows(width, ahead + 1), rows(PAIR, ahead + 1), rows(PAIR, ahead)]
        in_specs += [rows(mixed_features, ahead + 1)] + [ANYWHERE] * 3 + [whole(upper[10])]
        sums = [mixed_features, hidden_units, hidden_units]
        out_shape += [
            jax.ShapeDtypeStruct((total, width), F32),
            jax.ShapeDtypeStruct((total, mixed_features), BF16),
        ]
        out_shape += [jax.ShapeDtypeStruct((PAIR, size), F32) for size in sums] + [vec]
        out_specs += [rows(width, ahead + 1), rows(mixed_features, ahead + 1)]
        out_specs += [whole_out((PAIR, size)) for size in sums] + [whole_out((8, VEC))]
        scratch += [pltpu.VMEM((chunks, span, width), BF16)] * 2
        scratch += [
            pltpu.VMEM((2, span, width), F32),
            pltpu.VMEM((span, hidden_units), BF16),
            pltpu.VMEM((span, width), BF16),
            pltpu.VMEM((span, width), BF16),
            pltpu.VMEM(upper[7].shape[1:], BF16),
            pltpu.VMEM(upper[8].shape[1:], BF16),
            pltpu.VMEM(upper[9].shape[1:], BF16),
            pltpu.SemaphoreType.DMA((3,)),
        ]
    else:
        out_shape += [
            jax.ShapeDtypeStruct((place_rows, width), F32),
            jax.ShapeDtypeStruct((place_rows, width), F32),
            narrow,
        ]
        out_specs += [whole_out((place_rows, width))] * 2 + [whole_out((8, features))]
        scratch += [
            pltpu.VMEM((total, width), F32),
            pltpu.VMEM((place_rows, width), BF16),
            pltpu.VMEM((place_rows, width), BF16),
            pltpu.VMEM((8, features), F32),
            pltpu.SemaphoreType.DMA((2,)),
            pltpu.SemaphoreType.DMA((2,)),
        ]
    scratch += [pltpu.SemaphoreType.DMA((2, chunks))] * 2
    operands += swap.operands()
    in_specs += swap.in_specs()
    shapes, specs = swap.outputs()
    out_shape += shapes
    out_specs += specs
    scratch += swap.scratch()
    return pl.pallas_call(
        kernel,
        grid=(chunks + (1 if top else 2),),
        out_shape=out_shape,
        in_specs=in_specs,
        out_specs=out_specs,
        scratch_shapes=scratch,
        compiler_params=pltpu.CompilerParams(
            collective_id=identity, has_side_effects=True, vmem_limit_bytes=VMEM_BYTES
        ),
        name=f"rows_backward_{identity}",
    )(*operands)


def assemble(sums, vecs, lanes, n, features, hidden_units):
    place = lanes[1].shape[0]
    width = lanes[1].shape[1]
    half = PAIR // 2

    def kernel(*refs):
        refs = list(refs)

        def take(count):
            taken = refs[:count]
            del refs[:count]
            return taken

        qkvs, outs, ups, downs = take(LAYERS), take(LAYERS), take(LAYERS), take(LAYERS)
        vec_refs = [take(4) for _ in range(LAYERS)]
        out_lane, out_other, dx_own, dx_other = take(4)
        out_ref, dx_ref, gain1, shift1, g_qkv, b_qkv, g_out, b_out = take(8)
        gain2, shift2, g_up, b_up, g_down, b_down = take(6)
        out_own, sem = refs
        me = lax.axis_index("seq")
        x = lax.rem(me, 2)
        fetch = pltpu.make_async_copy(out_lane.at[at(me * place, place), :], out_own, sem)
        fetch.start()

        for layer in range(LAYERS):
            for part in range(3):
                g_qkv[layer, part] = qkvs[layer][:, part * features : (part + 1) * features]
            for ref, target in ((outs, g_out), (ups, g_up), (downs, g_down)):
                target[layer] = ref[layer][...]

        for layer, (entry_own, entry_other, upper_own, upper_other) in enumerate(vec_refs):
            line = slice(layer, layer + 1)
            for part in range(3):
                row = slice(part, part + 1)
                b_qkv[part, line, :] = entry_own[row, :] + entry_other[row, :]
            b_up[line, :] = upper_own[0:1, :hidden_units] + upper_other[0:1, :hidden_units]

            def owned(mine, other, row):
                wide = mine.shape[1]
                place = (me // 2) * PAIR
                pair = at(lax.rem(place, wide), PAIR)
                both = mine[row : row + 1, pair] + other[row : row + 1, pair]
                for later in range(1, width // wide):
                    line = slice(row + later, row + later + 1)
                    both = jnp.where(place // wide == later, mine[line, pair] + other[line, pair], both)
                return jnp.where(x == 0, both[:, :half], both[:, half:])

            gain1[line, :] = owned(entry_own, entry_other, 3)
            shift1[line, :] = owned(entry_own, entry_other, 5)
            b_down[line, :] = owned(upper_own, upper_other, 1)
            gain2[line, :] = owned(upper_own, upper_other, 2)
            shift2[line, :] = owned(upper_own, upper_other, 3)
            b_out[line, :] = owned(upper_own, upper_other, 4)

        def both_lanes(target, mine, other):
            target[:, 0, :] = jnp.where(x == 0, mine, other)
            target[:, 1, :] = jnp.where(x == 0, other, mine)

        both_lanes(dx_ref, dx_own[...], dx_other[...])
        fetch.wait()
        both_lanes(out_ref, out_own[...], out_other[...])

    def f32(*shape):
        return jax.ShapeDtypeStruct(shape, F32)

    in_vmem = pl.BlockSpec(memory_space=pltpu.VMEM)
    flat = []
    for kind in range(4):
        flat += [sums[layer][kind] for layer in range(LAYERS)]
    for layer in range(LAYERS):
        flat += list(vecs[layer])
    flat += list(lanes)
    small = f32(LAYERS, width // n)
    return pl.pallas_call(
        kernel,
        out_shape=(
            f32(place, 2, width),
            f32(place, 2, width),
            small,
            small,
            f32(LAYERS, 3, half, features),
            f32(3, LAYERS, features),
            f32(LAYERS, half, features),
            small,
            small,
            small,
            f32(LAYERS, half, hidden_units),
            f32(LAYERS, hidden_units),
            f32(LAYERS, half, hidden_units),
            small,
        ),
        in_specs=[in_vmem] * (len(flat) - 4) + [ANYWHERE] + [in_vmem] * 3,
        out_specs=(in_vmem,) * 14,
        scratch_shapes=[pltpu.VMEM((place, width), F32), pltpu.SemaphoreType.DMA],
        compiler_params=pltpu.CompilerParams(vmem_limit_bytes=VMEM_BYTES),
        name="assemble",
    )(*flat)


def per_chip(
    tokens,
    d_out,
    norm1_gain,
    norm1_shift,
    w_qkv,
    b_qkv,
    w_out,
    b_out,
    norm2_gain,
    norm2_shift,
    w_up,
    b_up,
    w_down,
    b_down,
    episode_frames,
    live,
):
    n = lax.axis_size("seq")
    rows = tokens.shape[0]
    features = w_qkv.shape[3]
    fixed, ahead = turn_constants(rows * n // FRAME)
    qkv, qkv_bias = w_qkv.transpose(0, 2, 1, 3), b_qkv.transpose(1, 0, 2)

    gathered, key_bias, frames, *projected = gather_and_project(
        tokens, live.T, episode_frames, norm1_gain, norm1_shift, qkv, qkv_bias, fixed, ahead, n
    )
    streams, kept, d_lane = [gathered], [], None
    for layer in range(LAYERS):
        following = None
        if layer + 1 < LAYERS:
            following = (qkv, norm1_gain, norm1_shift, qkv_bias, fixed, frames)
        results = layer_forward(
            layer,
            projected[0],
            key_bias,
            streams[layer],
            (w_out, w_up, w_down),
            (b_out, norm2_gain, norm2_shift, b_up, b_down),
            following,
            d_out if layer == 0 else None,
            n,
            1 + layer,
        )
        kept.append((*projected, *results[:8]))
        streams.append(results[8])
        if following is not None:
            projected = results[9:13]
        if layer == 0:
            d_lane = results[-1]

    sums = [[None] * 4 for _ in range(LAYERS)]
    vecs = [[None] * 4 for _ in range(LAYERS)]
    entry, later = (d_lane,), None
    for layer in reversed(range(LAYERS)):
        turned, first, unit1, scale1, probs, divisor, mixed = kept[layer][:7]
        unit2, scale2, second, act, slope = kept[layer][7:]
        upper = (
            layer,
            act,
            slope,
            unit2,
            scale2,
            second,
            mixed,
            w_out,
            w_up,
            w_down,
            norm2_gain,
        )
        identity = 1 + LAYERS + 2 * (LAYERS - 1 - layer)
        if later is None:
            results = rows_backward(entry, upper, identity, FRAME, Swap([], []))
        else:
            swap = Swap(later[:2], [(later[2], 0), (streams[LAYERS], rows)])
            vec1, *results = rows_backward(entry, upper, identity, FRAME, swap)
            results, swapped = results[:6], results[6:]
            sums[layer + 1][3], sums[layer + 1][0] = swapped[:2]
            vecs[layer + 1][3], out_other = swapped[2:]
            vecs[layer + 1][0] = vec1
        grad_middle, grad_mixed, out_sum, up_sum, down_sum, vec2 = results
        vecs[layer][2] = vec2
        last = layer == 0
        if last:
            swap = Swap([up_sum, down_sum], [(vec2, 0), (vecs[layer + 1][0], 0)])
        else:
            swap = Swap([out_sum, up_sum], [])
        results = attention_backward(
            probs,
            divisor,
            mixed,
            turned,
            grad_mixed,
            first,
            fixed,
            frames,
            swap,
            False,
            identity + 1,
        )
        grad_query, grad_key, grad_value, qkv_sum = results[:4]
        if last:
            sums[layer][2:] = results[4:6]
            vecs[layer][3], vecs[layer + 1][1] = results[6:8]
        else:
            sums[layer][1:3] = results[4:6]
            later = [down_sum, qkv_sum, vec2]
        entry = (
            layer,
            grad_query,
            grad_key,
            grad_value,
            unit1,
            scale1,
            grad_middle,
            qkv,
            norm1_gain,
        )
    vec1, dx_own, dx_other, vec_other, sums[0][0], sums[0][1] = rows_backward(
        entry, None, 1 + 3 * LAYERS, FRAME, Swap([qkv_sum, out_sum], [])
    )
    vecs[0][:2] = [vec1, vec_other]
    results = list(
        assemble(
            sums,
            vecs,
            (streams[LAYERS], out_other, dx_own, dx_other),
            n,
            features,
            w_up.shape[2],
        )
    )
    results[4] = results[4].transpose(0, 2, 1, 3)
    results[5] = results[5].transpose(1, 0, 2)
    results[6] = results[6].transpose(0, 2, 1)
    results[12] = results[12].transpose(0, 2, 1)
    return tuple(results)


def lane_fits(mesh, tokens):
    n = mesh.shape["seq"]
    positions, lanes, width = tokens.shape
    rows = positions // n
    return (
        lanes == 2
        and n % 4 == 0
        and positions <= 4 * FRAME
        and positions % FRAME == 0
        and FRAME % rows == 0
        and width // n * 2 == PAIR
        and mesh.shape["tp"] == 2
    )


def solution(mesh):
    placed = (
        P("seq", None, None),
        P("seq", None, None),
        P(),
        P(),
        P(None, None, None, "tp"),
        P(None, None, "tp"),
        P(None, "tp", None),
        P(),
        P(),
        P(),
        P(None, None, "tp"),
        P(None, "tp"),
        P(None, "tp", None),
        P(),
        P(),
        P("seq", None),
    )
    def mapped(body):
        return jax.shard_map(
            body,
            mesh=mesh,
            in_specs=placed,
            out_specs=(
                P("seq", None, None),
                P("seq", None, None),
                P(None, "seq"),
                P(None, "seq"),
                P(None, "seq", None, "tp"),
                P(None, None, "tp"),
                P(None, "tp", "seq"),
                P(None, "seq"),
                P(None, "seq"),
                P(None, "seq"),
                P(None, "seq", "tp"),
                P(None, "tp"),
                P(None, "tp", "seq"),
                P(None, "seq"),
            ),
            check_vma=False,
        )

    def run(tokens, *others):
        if lane_fits(mesh, tokens):
            return mapped(per_chip)(tokens, *others)
        return mapped(per_device)(tokens, *others)

    return run
```
